32 devices in a mesh: dp: 8 (over z, y), tensor: 4 (over x, core).
Axes of the slice: x: 2, y: 2, z: 4, core: 2. Of those that a mesh axis runs over, the one named last changes fastest.
Arguments:
- tokens: bfloat16 [8192, 768], P('dp'), may hold values from -6 to 6
- text: bfloat16 [32, 77, 768], P('dp'), may hold values from -6 to 6
- timesteps: int32 [32], P('dp'), may hold values from 0 to 999
- item_frames: int32 [32], P('dp'), may hold values from 0 to 1024, as said below
- cotangent: bfloat16 [8192, 768], P('dp'), may hold values from -6 to 6
- self_query: bfloat16 [2, 768, 768], P(None, None, 'tensor'), may hold values from -0.21875 to 0.21875
- self_query_bias: bfloat16 [2, 768], P(None, 'tensor'), may hold values from -3 to 3
- self_key: bfloat16 [2, 768, 768], P(None, None, 'tensor'), may hold values from -0.21875 to 0.21875
- self_value: bfloat16 [2, 768, 768], P(None, None, 'tensor'), may hold values from -0.21875 to 0.21875
- self_value_bias: bfloat16 [2, 768], P(None, 'tensor'), may hold values from -3 to 3
- self_output: bfloat16 [2, 768, 768], P(None, 'tensor'), may hold values from -0.875 to 0.875
- self_output_bias: bfloat16 [2, 768], replicated, may hold values from -2 to 2
- cross_query: bfloat16 [2, 768, 768], P(None, None, 'tensor'), may hold values from -0.21875 to 0.21875
- cross_query_bias: bfloat16 [2, 768], P(None, 'tensor'), may hold values from -3 to 3
- cross_key: bfloat16 [2, 768, 768], P(None, None, 'tensor'), may hold values from -0.21875 to 0.21875
- cross_value: bfloat16 [2, 768, 768], P(None, None, 'tensor'), may hold values from -0.21875 to 0.21875
- cross_value_bias: bfloat16 [2, 768], P(None, 'tensor'), may hold values from -3 to 3
- cross_output: bfloat16 [2, 768, 768], P(None, 'tensor'), may hold values from -0.21875 to 0.21875
- cross_output_bias: bfloat16 [2, 768], replicated, may hold values from -2 to 2
- hidden_up: bfloat16 [2, 768, 3072], P(None, None, 'tensor'), may hold values from -0.21875 to 0.21875
- hidden_up_bias: bfloat16 [2, 3072], P(None, 'tensor'), may hold values from -3 to 3
- hidden_down: bfloat16 [2, 3072, 768], P(None, 'tensor'), may hold values from -0.109375 to 0.109375
- hidden_down_bias: bfloat16 [2, 768], replicated, may hold values from -2 to 2
- modulation: bfloat16 [2, 768, 6912], P(None, None, 'tensor'), may hold values from -0.21875 to 0.21875
- modulation_bias: bfloat16 [2, 6912], P(None, 'tensor'), may hold values from -2 to 2
Outputs:
- output: bfloat16 [8192, 768], P('dp')
- input_grad: bfloat16 [8192, 768], P('dp')
- self_query_grad: float32 [2, 768, 768], P(None, 'dp', 'tensor')
- self_query_bias_grad: float32 [2, 768], P(None, 'tensor')
- self_key_grad: float32 [2, 768, 768], P(None, 'dp', 'tensor')
- self_value_grad: float32 [2, 768, 768], P(None, 'dp', 'tensor')
- self_value_bias_grad: float32 [2, 768], P(None, 'tensor')
- self_output_grad: float32 [2, 768, 768], P(None, 'tensor', 'dp')
- self_output_bias_grad: float32 [2, 768], P(None, 'dp')
- cross_query_grad: float32 [2, 768, 768], P(None, 'dp', 'tensor')
- cross_query_bias_grad: float32 [2, 768], P(None, 'tensor')
- cross_key_grad: float32 [2, 768, 768], P(None, 'dp', 'tensor')
- cross_value_grad: float32 [2, 768, 768], P(None, 'dp', 'tensor')
- cross_value_bias_grad: float32 [2, 768], P(None, 'tensor')
- cross_output_grad: float32 [2, 768, 768], P(None, 'tensor', 'dp')
- cross_output_bias_grad: float32 [2, 768], P(None, 'dp')
- hidden_up_grad: float32 [2, 768, 3072], P(None, 'dp', 'tensor')
- hidden_up_bias_grad: float32 [2, 3072], P(None, 'tensor')
- hidden_down_grad: float32 [2, 3072, 768], P(None, 'tensor', 'dp')
- hidden_down_bias_grad: float32 [2, 768], P(None, 'dp')
- modulation_grad: float32 [2, 768, 6912], P(None, 'dp', 'tensor')
- modulation_bias_grad: float32 [2, 6912], P(None, 'tensor')
The draws below stay inside these ranges and needn't reach their ends.
Inputs may be any that keep to these rules, and one draw needn't show every extreme that they name: `item_frames`: each aligned block of 1024 frames of a dp index is filled exactly by whole items; the block's 1024 // 256 slots give their lengths in order, items first and zeros after; a length is 256, 512 or 1024; some block holds a single item of 1024 frames.
All inputs are finite; a program needn't handle non-finite values.
Results may differ from the reference program's by a relative error of at most 0.029.
Values may be sent and summed in bfloat16 or wider, within the bound.
No kernel may reach another device: no remote copies, remote signals or barrier semaphores. Data moves between devices by JAX's collectives and lax.ppermute only.
A program may use at most 256 MiB of HBM per device.

```python
import math
import jax
import jax.numpy as jnp
from jax import lax

D = 768
HEADS = 12
HEAD_WIDTH = 64
FF = 3072
TXT = 77
UNIT = 256
LAYERS = 2
WINDOW = 1024
FRAMES = 8192
ITEMS = 32


def draw_item_frames(key, part):
    key = jax.random.fold_in(key, 11)
    table = jnp.array([[4, 0, 0, 0], [2, 2, 0, 0], [2, 1, 1, 0], [1, 2, 1, 0], [1, 1, 2, 0], [1, 1, 1, 1]], dtype=jnp.int32)
    count = FRAMES // WINDOW
    picked = jax.random.randint(jax.random.fold_in(key, 1), (count,), 0, 6)
    forced = jax.random.randint(jax.random.fold_in(key, 2), (), 0, count)
    picked = jnp.where(jnp.arange(count) == forced, 0, picked)
    return (table[picked] * UNIT).reshape(count * 4).astype(jnp.int32)


def set_ends(values, key, low, largest):
    longest = values.shape.index(max(values.shape))
    spots = []
    for shift in (0, 1):
        where = [jax.random.randint(jax.random.fold_in(key, axis), (), 0, length) for axis, length in enumerate(values.shape)]
        where[longest] = (where[longest] + shift) % values.shape[longest]
        spots.append(tuple(where))
    return values.at[spots[0]].set(low).at[spots[1]].set(largest)


def levels(key, extent, split, smallest, largest):
    loudness = 1.0
    for axis_at, shards_of in split:
        draws = jax.random.uniform(jax.random.fold_in(jax.random.fold_in(key, 6), axis_at), (shards_of,), jnp.float32, smallest / len(split), largest / len(split))
        loudness = loudness * jnp.repeat(jnp.exp(draws), extent[axis_at] // shards_of).reshape((-1,) + (1,) * (len(extent) - 1 - axis_at))
    return loudness


def bell_draw(stream_key, extent, deviation, bound, split=(), kind=jnp.bfloat16):
    values = deviation * jax.random.normal(stream_key, extent, jnp.float32)
    if split:
        values = values * levels(stream_key, extent, split, -0.22, 0.18)
    return jnp.clip(values, -bound, bound).astype(kind)


def setup_inputs(seed: int = 0) -> dict:
    splits = jax.random.split(jax.random.key(seed), 26)
    return {
        "tokens": bell_draw(splits[0], (FRAMES, D), 1.0, 6.0, ((0, 8),)),
        "text": bell_draw(splits[1], (ITEMS, TXT, D), 1.0, 6.0, ((0, 8),)),
        "timesteps": set_ends(jax.random.randint(splits[2], (ITEMS,), 0, 1000), jax.random.fold_in(splits[2], 1), 0, 999).astype(jnp.int32),
        "item_frames": draw_item_frames(jax.random.fold_in(splits[25], 71), 0),
        "cotangent": bell_draw(splits[4], (FRAMES, D), 1.0, 6.0, ((0, 8),)),
        "self_query": bell_draw(splits[5], (LAYERS, D, HEADS * HEAD_WIDTH), D ** -0.5, 0.21875, ((2, 4),)),
        "self_query_bias": bell_draw(splits[6], (LAYERS, HEADS * HEAD_WIDTH), 0.5, 3.0, ((1, 4),)),
        "self_key": bell_draw(splits[7], (LAYERS, D, HEADS * HEAD_WIDTH), D ** -0.5, 0.21875, ((2, 4),)),
        "self_value": bell_draw(splits[8], (LAYERS, D, HEADS * HEAD_WIDTH), D ** -0.5, 0.21875, ((2, 4),)),
        "self_value_bias": bell_draw(splits[9], (LAYERS, HEADS * HEAD_WIDTH), 0.5, 3.0, ((1, 4),)),
        "self_output": bell_draw(splits[10], (LAYERS, HEADS * HEAD_WIDTH, D), (max(D // 16, 1)) ** -0.5, 0.875, ((1, 4),)),
        "self_output_bias": bell_draw(splits[11], (LAYERS, D), 0.3, 2.0),
        "cross_query": bell_draw(splits[12], (LAYERS, D, HEADS * HEAD_WIDTH), D ** -0.5, 0.21875, ((2, 4),)),
        "cross_query_bias": bell_draw(splits[13], (LAYERS, HEADS * HEAD_WIDTH), 0.5, 3.0, ((1, 4),)),
        "cross_key": bell_draw(splits[14], (LAYERS, D, HEADS * HEAD_WIDTH), D ** -0.5, 0.21875, ((2, 4),)),
        "cross_value": bell_draw(splits[15], (LAYERS, D, HEADS * HEAD_WIDTH), D ** -0.5, 0.21875, ((2, 4),)),
        "cross_value_bias": bell_draw(splits[16], (LAYERS, HEADS * HEAD_WIDTH), 0.5, 3.0, ((1, 4),)),
        "cross_output": bell_draw(splits[17], (LAYERS, HEADS * HEAD_WIDTH, D), D ** -0.5, 0.21875, ((1, 4),)),
        "cross_output_bias": bell_draw(splits[18], (LAYERS, D), 0.3, 2.0),
        "hidden_up": bell_draw(splits[19], (LAYERS, D, FF), D ** -0.5, 0.21875, ((2, 4),)),
        "hidden_up_bias": bell_draw(splits[20], (LAYERS, FF), 0.5, 3.0, ((1, 4),)),
        "hidden_down": bell_draw(splits[21], (LAYERS, FF, D), FF ** -0.5, 0.109375, ((1, 4),)),
        "hidden_down_bias": bell_draw(splits[22], (LAYERS, D), 0.3, 2.0),
        "modulation": bell_draw(splits[23], (LAYERS, D, 9 * D), D ** -0.5, 0.21875, ((2, 4),)),
        "modulation_bias": bell_draw(splits[24], (LAYERS, 9 * D), 0.3, 2.0, ((1, 4),)),
    }


@jax.custom_vjp
def low(v):
    return lax.optimization_barrier(v.astype(jnp.bfloat16)).astype(jnp.float32)

@jax.custom_vjp
def low_back(v):
    return v

def low_keep(v):
    return (low(v), None)

def low_pass(kept, grad):
    return (grad,)

def back_keep(v):
    return (v, None)

def back_low(kept, grad):
    return (low(grad),)
low.defvjp(low_keep, low_pass)
low_back.defvjp(back_keep, back_low)
EPSILON = 1e-06

def matmul(left, right):
    return jnp.dot(left, right, precision=lax.Precision.HIGHEST, preferred_element_type=jnp.float32)

def time_features(moments):
    half = D // 2
    rates = jnp.exp(-math.log(10000.0) * jnp.arange(half, dtype=jnp.float32) / half)
    angles = moments.astype(jnp.float32)[:, None] * rates[None, :]
    return jnp.concatenate([jnp.cos(angles), jnp.sin(angles)], axis=1)

def normalize(values):
    mean = lax.optimization_barrier(jnp.mean(values, axis=-1, keepdims=True))
    center = values - mean
    spread = lax.optimization_barrier(jnp.mean(center * center, axis=-1, keepdims=True))
    return center * lax.rsqrt(spread + EPSILON)

def attend(query, keys, values, allowed):
    count = query.shape[0]
    query_heads = query.reshape(count, HEADS, HEAD_WIDTH)
    key_heads = keys.reshape(keys.shape[0], HEADS, HEAD_WIDTH)
    value_heads = values.reshape(values.shape[0], HEADS, HEAD_WIDTH)
    logit_scores = jnp.einsum('agp,lgp->gal', query_heads, key_heads, precision=lax.Precision.HIGHEST) * HEAD_WIDTH ** (-0.5)
    logit_scores = low_back(logit_scores)
    logit_scores = jnp.where(allowed[None], logit_scores, -1e+30)
    attention_weights = low(jax.nn.softmax(logit_scores, axis=-1))
    attended_values = jnp.einsum('tzr,rtf->ztf', attention_weights, value_heads, precision=lax.Precision.HIGHEST)
    return low(low_back(attended_values.reshape(count, HEADS * HEAD_WIDTH)))

def layer(values, params, condition, slot, same_item, own_text, text_rows):
    s_query, s_query_bias, s_key, s_value, s_value_bias, s_output, s_output_bias, c_query, c_query_bias, c_key, c_value, c_value_bias, c_output, c_output_bias, up_weight, up_bias, down_weight, down_bias, mod_weight, mod_bias = params
    modes = matmul(low(jax.nn.silu(condition)), mod_weight) + mod_bias
    per_row = jnp.take(modes, slot, axis=0)

    def piece(index):
        return per_row[:, index * D:(index + 1) * D]
    entry = low(normalize(values) * (1.0 + piece(1)) + piece(0))
    query = low(low_back(matmul(entry, s_query) + s_query_bias))
    keys = low(low_back(matmul(entry, s_key)))
    vals = low(low_back(matmul(entry, s_value) + s_value_bias))
    branch = low_back(matmul(attend(query, keys, vals, same_item), s_output) + s_output_bias)
    values = values + piece(2) * branch
    entry = low(normalize(values) * (1.0 + piece(4)) + piece(3))
    query = low(low_back(matmul(entry, c_query) + c_query_bias))
    keys = low(low_back(matmul(text_rows, c_key)))
    vals = low(low_back(matmul(text_rows, c_value) + c_value_bias))
    branch = low_back(matmul(attend(query, keys, vals, own_text), c_output) + c_output_bias)
    values = values + piece(5) * branch
    entry = low(normalize(values) * (1.0 + piece(7)) + piece(6))
    active = low(jax.nn.gelu(low_back(matmul(entry, up_weight) + up_bias), approximate=True))
    branch = low_back(matmul(active, down_weight) + down_bias)
    return values + piece(8) * branch

def add_trees(first, second):
    return first + second

def reference(tokens, text, timesteps, item_frames, cotangent, self_query, self_query_bias, self_key, self_value, self_value_bias, self_output, self_output_bias, cross_query, cross_query_bias, cross_key, cross_value, cross_value_bias, cross_output, cross_output_bias, hidden_up, hidden_up_bias, hidden_down, hidden_down_bias, modulation, modulation_bias):
    params = tuple((weight.astype(jnp.float32) for weight in (self_query, self_query_bias, self_key, self_value, self_value_bias, self_output, self_output_bias, cross_query, cross_query_bias, cross_key, cross_value, cross_value_bias, cross_output, cross_output_bias, hidden_up, hidden_up_bias, hidden_down, hidden_down_bias, modulation, modulation_bias)))
    count = tokens.shape[0] // WINDOW
    per_window = WINDOW // UNIT
    ends = jnp.cumsum(item_frames.reshape(count, per_window), axis=1).astype(jnp.int32)
    position = jnp.arange(WINDOW, dtype=jnp.int32)
    slots = lax.optimization_barrier(jnp.sum((position[None, :, None] >= ends[:, None, :]).astype(jnp.int32), axis=2)).astype(jnp.int32)
    owners = (jnp.arange(per_window * TXT, dtype=jnp.int32) // TXT).astype(jnp.int32)

    def step(totals, inputs):
        rows_in, words_in, moments, slot, cot_rows = inputs
        condition = time_features(moments)
        same_item = slot[:, None] == slot[None, :]
        own_text = slot[:, None] == owners[None, :]
        text_rows = words_in.astype(jnp.float32).reshape(per_window * TXT, D)

        def forward(attention_weights, start):
            current = start
            for index in range(LAYERS):
                current = layer(current, tuple((weight[index] for weight in attention_weights)), condition, slot, same_item, own_text, text_rows)
            return current
        result, pull = jax.vjp(forward, params, rows_in.astype(jnp.float32))
        grads, back = pull(cot_rows.astype(jnp.float32))
        totals = jax.tree.map(add_trees, totals, grads)
        return (totals, (result.astype(jnp.bfloat16), back.astype(jnp.bfloat16)))
    zeros = tuple((jnp.zeros_like(weight) for weight in params))
    totals, (outputs, backs) = lax.scan(step, zeros, (tokens.reshape(count, WINDOW, D), text.reshape(count, per_window, TXT, D), timesteps.reshape(count, per_window), slots, cotangent.reshape(count, WINDOW, D)))
    return (outputs.reshape(count * WINDOW, D), backs.reshape(count * WINDOW, D), totals[0], totals[1], totals[2], totals[3], totals[4], totals[5], totals[6], totals[7], totals[8], totals[9], totals[10], totals[11], totals[12], totals[13], totals[14], totals[15], totals[16], totals[17], totals[18], totals[19])
```

```python
from functools import partial
import math

import jax
import jax.numpy as jnp
from jax import lax
from jax.experimental import pallas as pl
from jax.experimental.pallas import tpu as pltpu
from jax.sharding import PartitionSpec as P

HEAD_WIDTH = 64
UNIT = 256
LAYERS = 2
WINDOW = 1024
EPSILON = 1e-06
LANES = 128
CHUNK = 64
TILE = 512
SLOTS = WINDOW // UNIT
FAR = -1e30
VMEM_BYTES = 56 * 1024 * 1024
BF = jnp.bfloat16
F32 = jnp.float32
ROOT = math.sqrt(2.0 / math.pi)
CUBIC = 0.044715


def dot_nn(left, right):
    return jnp.dot(left, right, preferred_element_type=F32)


def dot_nt(left, right):
    return lax.dot_general(left, right, (((1,), (1,)), ((), ())), preferred_element_type=F32)


def dot_tn(left, right):
    return lax.dot_general(left, right, (((0,), (0,)), ((), ())), preferred_element_type=F32)


SMALL = pl.BlockSpec(memory_space=pltpu.SMEM)
NEAR = pl.BlockSpec(memory_space=pltpu.VMEM)
ANY = pl.BlockSpec(memory_space=pl.ANY)


def run(body, name, ins, outs, scratch, flops):
    moved = sum(math.prod(a.shape) * a.dtype.itemsize for _, a in ins)
    moved += sum(math.prod(o.shape) * o.dtype.itemsize for o in outs)
    return pl.pallas_call(
        body,
        out_shape=outs,
        in_specs=[spec for spec, _ in ins],
        out_specs=[NEAR] * len(outs),
        scratch_shapes=scratch,
        compiler_params=pltpu.CompilerParams(vmem_limit_bytes=VMEM_BYTES),
        cost_estimate=pl.CostEstimate(flops=int(flops), bytes_accessed=int(moved), transcendentals=0),
        name=name,
    )(*[a for _, a in ins])


def shape(*dims, dtype=F32):
    return jax.ShapeDtypeStruct(dims, dtype)


def start_rows(refs, place, plan, sems):
    own, sib, xa, ya, xb, yb = refs
    half = own.shape[0] // 2
    for rank in range(4):
        for parity in range(2):

            @pl.when(place == rank * 2 + parity)
            def _(rank=rank, parity=parity):
                for index, (shard, row, rows, dst) in enumerate(plan):
                    step = shard ^ rank
                    if step < 2:
                        src = (own, sib)[step].at[pl.ds(row, rows)]
                    else:
                        first, second = ((xa, ya), (xb, yb))[step - 2]
                        part = row // half
                        src = (first if part == parity else second).at[pl.ds(row - part * half, rows)]
                    pltpu.make_async_copy(src, dst, sems.at[index]).start()


def wait_rows(refs, plan, sems, which):
    for index in which:
        _, row, rows, dst = plan[index]
        pltpu.make_async_copy(refs[0].at[pl.ds(0, rows)], dst, sems.at[index]).wait()


def plan_of(buffers, first, rows):
    return [
        (shard, (first + which) * rows, rows, dst.at[pl.ds(shard * rows, rows)])
        for which, dst in enumerate(buffers)
        for shard in range(4)
    ]


def norm_rows(values):
    mean = jnp.mean(values, axis=-1, keepdims=True)
    center = values - mean
    factor = lax.rsqrt(jnp.mean(center * center, axis=-1, keepdims=True) + EPSILON)
    return center * factor, factor


def piece(mod, slot, index):
    width = mod.shape[1] // 9
    return mod[pl.ds(slot, 1), index * width : (index + 1) * width]


def entry_rows(x, mod, info, index, out):
    for block in range(x.shape[0] // UNIT):
        slot = info[1 + block]
        shift = piece(mod, slot, index)
        scale = 1.0 + piece(mod, slot, index + 1)

        def step(turn, carry):
            rows = pl.ds(pl.multiple_of(block * UNIT + turn * CHUNK, CHUNK), CHUNK)
            normed, _ = norm_rows(x[rows, :])
            out[rows, :] = (normed * scale + shift).astype(BF)
            return carry

        lax.fori_loop(0, UNIT // CHUNK, step, 0)


def residual_rows(x, mod, info, index, branch, branch_out, out):
    for block in range(x.shape[0] // UNIT):
        gate = piece(mod, info[1 + block], index)

        def step(turn, carry):
            rows = pl.ds(pl.multiple_of(block * UNIT + turn * CHUNK, CHUNK), CHUNK)
            values = branch[rows, :]
            branch_out[rows, :] = values.astype(BF)
            out[rows, :] = x[rows, :] + gate * values
            return carry

        lax.fori_loop(0, UNIT // CHUNK, step, 0)


def fold(values):
    return jnp.sum(values.reshape(values.shape[0] // 8, 8, values.shape[1]), axis=0)


def total(values):
    return jnp.sum(values, axis=0, keepdims=True)


def gate_back(g, mod, info, index, branch, gb, stats):
    width = g.shape[1]
    sums = jnp.zeros((8, width), F32)
    for block in range(g.shape[0] // UNIT):
        slot = info[1 + block]
        gate = piece(mod, slot, index)

        def step(turn, carry):
            rows = pl.ds(pl.multiple_of(block * UNIT + turn * CHUNK, CHUNK), CHUNK)
            grad = g[rows, :].astype(F32)
            low = (gate * grad).astype(BF)
            gb[rows, :] = low
            return (
                carry[0] + fold(low.astype(F32)),
                carry[1] + fold(grad * branch[rows, :].astype(F32)),
            )

        sums, rows_sum = lax.fori_loop(
            0, UNIT // CHUNK, step, (sums, jnp.zeros((8, width), F32))
        )
        stats[pl.ds(8 + slot, 1), :] += total(rows_sum)
    stats[12:13, :] = total(sums)


def norm_back_rows(x, g, de, mod, info, index, out, stats):
    width = x.shape[1]
    for block in range(x.shape[0] // UNIT):
        slot = info[1 + block]
        scale = 1.0 + piece(mod, slot, index + 1)

        def step(turn, carry):
            rows = pl.ds(pl.multiple_of(block * UNIT + turn * CHUNK, CHUNK), CHUNK)
            normed, factor = norm_rows(x[rows, :])
            grad = de[rows, :]
            inner = grad * normed
            dn = grad * scale
            mean = jnp.mean(dn, axis=-1, keepdims=True)
            along = jnp.mean(dn * normed, axis=-1, keepdims=True)
            out[rows, :] = g[rows, :].astype(F32) + factor * (dn - mean - normed * along)
            return (carry[0] + fold(grad), carry[1] + fold(inner))

        zero = jnp.zeros((8, width), F32)
        shift_sum, scale_sum = lax.fori_loop(0, UNIT // CHUNK, step, (zero, zero))
        stats[pl.ds(slot, 1), :] += total(shift_sum)
        stats[pl.ds(4 + slot, 1), :] += total(scale_sum)


def lane_ids(rows):
    return lax.broadcasted_iota(jnp.int32, (rows, LANES), 1)


def head_half(values, half):
    ids = lane_ids(values.shape[0])
    keep = ids < HEAD_WIDTH if half == 0 else ids >= HEAD_WIDTH
    return jnp.where(keep, values.astype(F32), 0.0)


def query_marks(slot):
    return jnp.where(lane_ids(UNIT) == slot, 1.0, 0.0).astype(BF)


def key_marks(slots):
    ids = lane_ids(UNIT)
    parts = [jnp.where((ids < SLOTS) & (ids != slot), FAR, 0.0).astype(BF) for slot in slots]
    return jnp.concatenate(parts, axis=0)


def pair_lanes(pair):
    return pl.ds(pl.multiple_of(pair * LANES, LANES), LANES)


def pack_kernel(info, *refs, transposed):
    count = len(transposed)
    sources, (out, first) = refs[:count], refs[count:]
    row = 0
    half = out.shape[0] // 2
    for source, flip in zip(sources, transposed):
        if flip:
            width = source.shape[1]
            ids = lax.broadcasted_iota(jnp.int32, (width, width), 0)
            others = lax.broadcasted_iota(jnp.int32, (width, width), 1)
            unit = jnp.where(ids == others, 1.0, 0.0).astype(BF)
            values = dot_nt(unit, source[...]).astype(BF)
        else:
            values = source[...]
        out[pl.ds(row, values.shape[0]), :] = values
        row += values.shape[0]
    for parity in range(2):

        @pl.when(info[0] % 2 == parity)
        def _(parity=parity):
            first[...] = out[pl.ds(parity * half, half), :]


def qkv_kernel(info, x, mod, q_bias, v_bias, *refs):
    weights, (entry, q, kv), (wq, wk, wv, sems) = refs[:6], refs[6:9], refs[9:]
    rows = weights[0].shape[0] // 4
    plan = plan_of((wq, wk, wv), 0, rows)
    start_rows(weights, info[0], plan, sems)
    entry_rows(x, mod, info, 0, entry)
    wait_rows(weights, plan, sems, range(0, 4))
    q[...] = (dot_nt(entry[...], wq[...]) + q_bias[...]).astype(BF)
    wait_rows(weights, plan, sems, range(4, 8))
    kv[0] = dot_nt(entry[...], wk[...]).astype(BF)
    wait_rows(weights, plan, sems, range(8, 12))
    kv[1] = (dot_nt(entry[...], wv[...]) + v_bias[...]).astype(BF)


def self_kernel(info, x, mod, bias, q, kv_own, kv_sib, *refs):
    weights, (x1, mixed, lse, branch), (wo, logs, work, sems) = refs[:6], refs[6:10], refs[10:]
    rows = weights[0].shape[0] // 4
    plan = [(s, 3 * rows, rows, wo.at[pl.ds(s * rows, rows)]) for s in range(4)]
    start_rows(weights, info[0], plan, sems)
    blocks = x.shape[0] // UNIT
    own_marks = key_marks([info[1 + b] for b in range(blocks)])
    sib_marks = key_marks([info[1 + blocks + b] for b in range(blocks)])
    ones = jnp.ones((x.shape[0], LANES), BF)

    def step(pair, carry):
        lanes = pair_lanes(pair)
        k_own = jnp.concatenate([kv_own[0, :, lanes], own_marks], axis=1)
        k_sib = jnp.concatenate([kv_sib[0, :, lanes], sib_marks], axis=1)
        v_own = jnp.concatenate([kv_own[1, :, lanes], ones], axis=1)
        v_sib = jnp.concatenate([kv_sib[1, :, lanes], ones], axis=1)
        for block in range(blocks):
            span = pl.ds(block * UNIT, UNIT)
            q_pair = q[span, lanes]
            marks = query_marks(info[1 + block])
            results = []
            for half in range(2):
                left = jnp.concatenate(
                    [(head_half(q_pair, half) * HEAD_WIDTH**-0.5).astype(BF), marks], axis=1
                )
                s_own = dot_nt(left, k_own)
                s_sib = dot_nt(left, k_sib)
                peak = jnp.maximum(
                    jnp.max(s_own, axis=-1, keepdims=True), jnp.max(s_sib, axis=-1, keepdims=True)
                )
                p_own = jnp.exp(s_own - peak).astype(BF)
                p_sib = jnp.exp(s_sib - peak).astype(BF)
                both = dot_nn(p_own, v_own) + dot_nn(p_sib, v_sib)
                sums = both[:, LANES:]
                results.append(both[:, :LANES] / sums)
                logs[span, :] = jnp.where(
                    lane_ids(UNIT) == 2 * pair + half, peak + jnp.log(sums), logs[span, :]
                )
            mixed[span, lanes] = jnp.where(
                lane_ids(UNIT) < HEAD_WIDTH, results[0], results[1]
            ).astype(BF)
        return carry

    logs[...] = jnp.zeros(logs.shape, F32)
    lax.fori_loop(0, x.shape[1] // LANES, step, 0)
    lse[...] = logs[...].T[: lse.shape[0], :]
    wait_rows(weights, plan, sems, range(4))
    work[...] = dot_nn(mixed[...], wo[...]) + bias[...]
    residual_rows(x, mod, info, 2, work, branch, x1)


def cross_kernel(info, x, mod, q_bias, v_bias, bias, text, *refs, words):
    weights, outs, scratch = refs[:6], refs[6:14], refs[14:]
    x2, entry, q, kv, mixed, lse, branch = outs[:7]
    wq, wk, wv, wo, logs, work, sems = (outs[7:] + scratch)
    rows = weights[0].shape[0] // 4
    plan = plan_of((wk, wv, wq, wo), 0, rows)
    order = (1, 2, 0, 3)
    plan = [
        (shard, order[i // 4] * rows, count, dst)
        for i, (shard, _, count, dst) in enumerate(plan)
    ]
    start_rows(weights, info[0], plan, sems)
    entry_rows(x, mod, info, 3, entry)
    wait_rows(weights, plan, sems, range(0, 4))
    kv[0] = dot_nt(text[...], wk[...]).astype(BF)
    wait_rows(weights, plan, sems, range(4, 8))
    kv[1] = (dot_nt(text[...], wv[...]) + v_bias[...]).astype(BF)
    wait_rows(weights, plan, sems, range(8, 12))
    q[...] = (dot_nt(entry[...], wq[...]) + q_bias[...]).astype(BF)
    ones = jnp.ones((LANES, LANES), BF)
    logs[...] = jnp.zeros(logs.shape, F32)

    def step(pair, carry):
        lanes = pair_lanes(pair)
        for block in range(x.shape[0] // UNIT):
            span = pl.ds(block * UNIT, UNIT)
            own = pl.ds(pl.multiple_of(info[1 + block] * LANES, LANES), LANES)
            q_pair = q[span, lanes]
            keys = kv[0, own, lanes]
            values = jnp.concatenate([kv[1, own, lanes], ones], axis=1)
            results = []
            for half in range(2):
                left = (head_half(q_pair, half) * HEAD_WIDTH**-0.5).astype(BF)
                scores = jnp.where(lane_ids(UNIT) < words, dot_nt(left, keys), FAR)
                peak = jnp.max(scores, axis=-1, keepdims=True)
                both = dot_nn(jnp.exp(scores - peak).astype(BF), values)
                sums = both[:, LANES:]
                results.append(both[:, :LANES] / sums)
                logs[span, :] = jnp.where(
                    lane_ids(UNIT) == 2 * pair + half, peak + jnp.log(sums), logs[span, :]
                )
            mixed[span, lanes] = jnp.where(
                lane_ids(UNIT) < HEAD_WIDTH, results[0], results[1]
            ).astype(BF)
        return carry

    lax.fori_loop(0, x.shape[1] // LANES, step, 0)
    lse[...] = logs[...].T[: lse.shape[0], :]
    wait_rows(weights, plan, sems, range(12, 16))
    work[...] = dot_nn(mixed[...], wo[...]) + bias[...]
    residual_rows(x, mod, info, 5, work, branch, x2)


def tile_at(index):
    return pl.ds(pl.multiple_of(index * TILE, TILE), TILE)


def hidden_kernel(info, x, mod, up_bias, bias, *refs):
    weights, outs, scratch = refs[:6], refs[6:11], refs[11:]
    x3, entry, active, slope, branch = outs
    up, down, before, work, sems = scratch
    rows = weights[0].shape[0] // 2
    plan = plan_of((up, down), 0, rows)
    start_rows(weights, info[0], plan, sems)
    entry_rows(x, mod, info, 6, entry)
    wait_rows(weights, plan, sems, range(0, 8))
    count = up.shape[0] // TILE

    def rise(index):
        return dot_nt(entry[...], up[tile_at(index), :]) + up_bias[:, tile_at(index)]

    before[0] = rise(0)
    work[...] = jnp.zeros(work.shape, F32) + bias[...]

    def step(index, carry):
        values = before[index % 2]
        before[(index + 1) % 2] = rise(lax.rem(index + 1, count))
        square = values * values
        bend = jnp.tanh(ROOT * values * (1.0 + CUBIC * square))
        half = 0.5 + 0.5 * bend
        act = (values * half).astype(BF)
        active[:, tile_at(index)] = act
        slope[:, tile_at(index)] = (
            half
            + 0.5 * values * (1.0 - bend * bend) * (ROOT * (1.0 + 3.0 * CUBIC * square))
        ).astype(BF)
        work[...] += dot_nn(act, down[tile_at(index), :])
        return carry

    lax.fori_loop(0, count, step, 0)
    residual_rows(x, mod, info, 8, work, branch, x3)


def hidden_back_kernel(info, x, g, mod, branch, slope, *refs):
    weights, (out, gb, d_before, stats), scratch = refs[:6], refs[6:10], refs[10:]
    up, down, rise, de, up_sum, sems = scratch
    rows = weights[0].shape[0] // 2
    plan = plan_of((down, up), 0, rows)
    plan = [
        (shard, (rows, 0)[i // 4], count, dst) for i, (shard, _, count, dst) in enumerate(plan)
    ]
    start_rows(weights, info[0], plan, sems)
    stats[...] = jnp.zeros(stats.shape, F32)
    gate_back(g, mod, info, 8, branch, gb, stats)
    wait_rows(weights, plan, sems, range(0, 8))
    count = up.shape[0] // TILE
    rise[0] = dot_nt(gb[...], down[tile_at(0), :])
    de[...] = jnp.zeros(de.shape, F32)

    def step(index, carry):
        values = rise[index % 2]
        rise[(index + 1) % 2] = dot_nt(gb[...], down[tile_at(lax.rem(index + 1, count)), :])
        low = (values * slope[:, tile_at(index)].astype(F32)).astype(BF)
        d_before[:, tile_at(index)] = low
        up_sum[:, tile_at(index)] = total(fold(low.astype(F32)))
        de[...] += dot_nn(low, up[tile_at(index), :])
        return carry

    lax.fori_loop(0, count, step, 0)
    width = x.shape[1]
    for shard in range(4):
        stats[13 + shard : 14 + shard, :] = up_sum[:, shard * width : (shard + 1) * width]
    norm_back_rows(x, g, de, mod, info, 6, out, stats)


def cross_back_kernel(info, x, g, mod, branch, q, kv, lse, *refs, words):
    weights, (out, gb, dq, dkv, stats), scratch = refs[:6], refs[6:11], refs[11:]
    wq, wo, d_mixed, de, dkv_sum, sems = scratch
    rows = weights[0].shape[0] // 4
    plan = plan_of((wo, wq), 0, rows)
    plan = [
        (shard, (3 * rows, 0)[i // 4], count, dst)
        for i, (shard, _, count, dst) in enumerate(plan)
    ]
    start_rows(weights, info[0], plan, sems)
    stats[...] = jnp.zeros(stats.shape, F32)
    gate_back(g, mod, info, 5, branch, gb, stats)
    wait_rows(weights, plan, sems, range(0, 4))
    d_mixed[...] = dot_nt(gb[...], wo[...]).astype(BF)
    dkv_sum[...] = jnp.zeros(dkv_sum.shape, F32)
    real = lax.broadcasted_iota(jnp.int32, (LANES, UNIT), 0) < words

    def step(pair, carry):
        lanes = pair_lanes(pair)
        for block in range(x.shape[0] // UNIT):
            span = pl.ds(block * UNIT, UNIT)
            own = pl.ds(pl.multiple_of(info[1 + block] * LANES, LANES), LANES)
            q_pair = q[span, lanes]
            d_pair = d_mixed[span, lanes]
            keys = kv[0, own, lanes]
            values = kv[1, own, lanes]
            grad_q = jnp.zeros((LANES, UNIT), F32)
            grad_k = jnp.zeros((LANES, LANES), F32)
            grad_v = jnp.zeros((LANES, LANES), F32)
            for half in range(2):
                left = (head_half(q_pair, half) * HEAD_WIDTH**-0.5).astype(BF)
                grad = head_half(d_pair, half).astype(BF)
                k_turned = head_half(keys, half).T.astype(BF)
                logs = lse[pl.ds(2 * pair + half, 1), span]
                probs = jnp.where(real, jnp.exp(dot_nt(keys, left) - logs), 0.0)
                d_probs = dot_nt(values, grad)
                inner = jnp.sum(probs * d_probs, axis=0, keepdims=True)
                d_scores = (probs * (d_probs - inner)).astype(BF)
                grad_v += dot_nn(probs.astype(BF), grad)
                grad_k += dot_nn(d_scores, left)
                grad_q += dot_nn(k_turned, d_scores)
            dq[span, lanes] = (grad_q.T * HEAD_WIDTH**-0.5).astype(BF)
            dkv_sum[0, own, lanes] += grad_k
            dkv_sum[1, own, lanes] += grad_v
        return carry

    lax.fori_loop(0, x.shape[1] // LANES, step, 0)
    dkv[...] = dkv_sum[...].astype(BF)
    stats[13:14, :] = total(fold(dq[...].astype(F32)))
    stats[14:15, :] = total(fold(dkv[1].astype(F32)))
    wait_rows(weights, plan, sems, range(4, 8))
    de[...] = dot_nn(dq[...], wq[...])
    norm_back_rows(x, g, de, mod, info, 3, out, stats)


def self_back_kernel(info, g, mod, branch, q, kv_own, kv_sib, lse, *refs):
    weights, (gb, dq, dkv_own, dkv_sib, stats), scratch = refs[:6], refs[6:11], refs[11:]
    wo, d_mixed, sems = scratch
    rows = weights[0].shape[0] // 4
    plan = [(s, 3 * rows, rows, wo.at[pl.ds(s * rows, rows)]) for s in range(4)]
    start_rows(weights, info[0], plan, sems)
    stats[...] = jnp.zeros(stats.shape, F32)
    gate_back(g, mod, info, 2, branch, gb, stats)
    blocks = g.shape[0] // UNIT
    marks = (
        key_marks([info[1 + b] for b in range(blocks)]),
        key_marks([info[1 + blocks + b] for b in range(blocks)]),
    )
    wait_rows(weights, plan, sems, range(4))
    d_mixed[...] = dot_nt(gb[...], wo[...]).astype(BF)
    sides = ((kv_own, dkv_own), (kv_sib, dkv_sib))

    def step(pair, carry):
        lanes = pair_lanes(pair)
        keys = [kv[0, :, lanes] for kv, _ in sides]
        values = [kv[1, :, lanes] for kv, _ in sides]
        marked = [jnp.concatenate([k, m], axis=1) for k, m in zip(keys, marks)]
        turned = [[head_half(k, half).T.astype(BF) for k in keys] for half in range(2)]
        grad_k = [jnp.zeros((blocks * UNIT, LANES), F32) for _ in sides]
        grad_v = [jnp.zeros((blocks * UNIT, LANES), F32) for _ in sides]
        for block in range(blocks):
            span = pl.ds(block * UNIT, UNIT)
            q_pair = q[span, lanes]
            d_pair = d_mixed[span, lanes]
            ends = query_marks(info[1 + block])
            grad_q = jnp.zeros((LANES, UNIT), F32)
            for half in range(2):
                left = (head_half(q_pair, half) * HEAD_WIDTH**-0.5).astype(BF)
                grad = head_half(d_pair, half).astype(BF)
                logs = lse[pl.ds(2 * pair + half, 1), span]
                query = jnp.concatenate([left, ends], axis=1)
                probs = [jnp.exp(dot_nt(k, query) - logs) for k in marked]
                d_probs = [dot_nt(v, grad) for v in values]
                inner = sum(
                    jnp.sum(p * d, axis=0, keepdims=True) for p, d in zip(probs, d_probs)
                )
                for side in range(2):
                    d_scores = (probs[side] * (d_probs[side] - inner)).astype(BF)
                    grad_v[side] += dot_nn(probs[side].astype(BF), grad)
                    grad_k[side] += dot_nn(d_scores, left)
                    grad_q += dot_nn(turned[half][side], d_scores)
            dq[span, lanes] = (grad_q.T * HEAD_WIDTH**-0.5).astype(BF)
        for side in range(2):
            sides[side][1][0, :, lanes] = grad_k[side].astype(BF)
            sides[side][1][1, :, lanes] = grad_v[side].astype(BF)
        return carry

    lax.fori_loop(0, g.shape[1] // LANES, step, 0)


def qkv_back_kernel(info, x, g, mod, dq, dkv_own, dkv_sib, early, *refs):
    weights, (out, dkv, stats), scratch = refs[:6], refs[6:9], refs[9:]
    wq, wk, wv, de, sems = scratch
    rows = weights[0].shape[0] // 4
    plan = plan_of((wq, wk, wv), 0, rows)
    start_rows(weights, info[0], plan, sems)
    stats[...] = early[...]
    for which in range(2):
        dkv[which] = (dkv_own[which].astype(F32) + dkv_sib[which].astype(F32)).astype(BF)
    stats[13:14, :] = total(fold(dq[...].astype(F32)))
    stats[14:15, :] = total(fold(dkv[1].astype(F32)))
    wait_rows(weights, plan, sems, range(0, 4))
    de[...] = dot_nn(dq[...], wq[...])
    wait_rows(weights, plan, sems, range(4, 8))
    de[...] += dot_nn(dkv[0], wk[...])
    wait_rows(weights, plan, sems, range(8, 12))
    de[...] += dot_nn(dkv[1], wv[...])
    norm_back_rows(x, g, de, mod, info, 0, out, stats)


def wide_grad_kernel(info, entry, gb, db_sib, db_own, act_sib, act_own, send, keep):
    width = entry.shape[1]
    for out, db, act in ((send, db_sib, act_sib), (keep, db_own, act_own)):
        out[:, :width] = dot_tn(entry[...], db[...]).astype(BF)
        out[:, width:] = dot_tn(gb[...], act[...]).astype(BF)


def narrow_grad_kernel(info, *refs):
    lefts, rights, (send, keep) = refs[:4], refs[4:8], refs[8:]
    rows = lefts[0].shape[1]
    low = lane_ids(rows) < HEAD_WIDTH
    step = 3 * LANES
    for at in range(2):
        products = [dot_tn(lefts[2 * at + i][...], rights[2 * at + i][...]) for i in range(2)]
        (a0, a1, a2), (b0, b1, b2) = [
            [p[:, i * LANES : (i + 1) * LANES] for i in range(3)] for p in products
        ]
        even = (a0, b0, jnp.where(low, a1, pltpu.roll(b1, HEAD_WIDTH, 1)))
        a1, b1 = pltpu.roll(a1, HEAD_WIDTH, 1), pltpu.roll(b1, HEAD_WIDTH, 1)
        a2r, b2r = pltpu.roll(a2, HEAD_WIDTH, 1), pltpu.roll(b2, HEAD_WIDTH, 1)
        odd = (jnp.where(low, a1, a2r), jnp.where(low, b1, b2r), jnp.where(low, a2r, b2))
        for core in range(2):

            @pl.when(info[5] % 2 == core)
            def _(core=core):
                for out, parts in ((send, (odd, even)[core]), (keep, (even, odd)[core])):
                    for i, part in enumerate(parts):
                        out[:, at * step + i * LANES : at * step + (i + 1) * LANES] = part.astype(
                            BF
                        )


def tensor_hop(values, step):
    return lax.ppermute(values, "tensor", [(i, i ^ step) for i in range(4)])


def dp_hop(values, step):
    size = lax.axis_size("dp")
    return lax.ppermute(values, "dp", [(i, i ^ step) for i in range(size)])


def gather_dp(values):
    me = lax.axis_index("dp")
    step = 1
    while step < lax.axis_size("dp"):
        other = dp_hop(values, step)
        upper = (me & step) > 0
        values = jnp.concatenate(
            [jnp.where(upper, other, values), jnp.where(upper, values, other)], axis=0
        )
        step *= 2
    return values


def scatter_dp(values):
    size = lax.axis_size("dp")
    me = lax.axis_index("dp")
    rows, columns = values.shape
    unit = rows // size
    step = 1
    while step < size:
        blocks = values.shape[0] // unit
        split = values.reshape(blocks // 2, 2, unit, columns)
        bit = (me & step) // step
        give = lax.dynamic_index_in_dim(split, 1 - bit, 1, keepdims=False)
        hold = lax.dynamic_index_in_dim(split, bit, 1, keepdims=False)
        give = give.reshape(blocks // 2 * unit, columns)
        hold = hold.reshape(blocks // 2 * unit, columns).astype(F32)
        values = hold + dp_hop(give, step).astype(F32)
        step *= 2
        if step < size:
            values = values.astype(BF)
    return values.astype(F32)


def unpack(values):
    wide, rest = 2 * LANES, LANES + HEAD_WIDTH
    return (
        jnp.concatenate([values[:, :LANES], values[:, wide : wide + HEAD_WIDTH]], axis=1),
        jnp.concatenate([values[:, LANES:wide], values[:, wide + HEAD_WIDTH :]], axis=1),
    )


def time_features(moments, width):
    half = width // 2
    rates = jnp.exp(-math.log(10000.0) * jnp.arange(half, dtype=F32) / half)
    angles = moments.astype(F32)[:, None] * rates[None, :]
    return jnp.concatenate([jnp.cos(angles), jnp.sin(angles)], axis=1)


def shards(
    tokens,
    text,
    timesteps,
    item_frames,
    cotangent,
    self_query,
    self_query_bias,
    self_key,
    self_value,
    self_value_bias,
    self_output,
    self_output_bias,
    cross_query,
    cross_query_bias,
    cross_key,
    cross_value,
    cross_value_bias,
    cross_output,
    cross_output_bias,
    hidden_up,
    hidden_up_bias,
    hidden_down,
    hidden_down_bias,
    modulation,
    modulation_bias,
):
    frames, width = tokens.shape
    words = text.shape[1]
    mod_width = modulation.shape[2]
    narrow = self_query.shape[2]
    units = hidden_up.shape[2]
    rank = lax.axis_index("tensor")
    me = lax.axis_index("dp")
    core = rank % 2
    share = frames // 2
    blocks = share // UNIT
    ends = jnp.cumsum(item_frames)
    starts = jnp.arange(frames // UNIT, dtype=jnp.int32) * UNIT
    slots = jnp.sum((starts[:, None] >= ends[None, :]).astype(jnp.int32), axis=1)
    own_slots = lax.dynamic_slice_in_dim(slots, core * blocks, blocks)
    sib_slots = lax.dynamic_slice_in_dim(slots, (1 - core) * blocks, blocks)
    info = jnp.concatenate(
        [
            (rank * 2 + me % 2)[None].astype(jnp.int32),
            own_slots,
            sib_slots,
            rank[None].astype(jnp.int32),
            (rank // 2)[None].astype(jnp.int32),
            (rank ^ 1)[None].astype(jnp.int32),
        ]
    )

    condition = jax.nn.silu(time_features(timesteps, width)).astype(BF)
    local_mod = jnp.einsum(
        "sd,ldc->lsc", condition, modulation, preferred_element_type=F32
    ) + modulation_bias[:, None, :].astype(F32)
    vectors = jnp.concatenate(
        [self_query_bias, self_value_bias, cross_query_bias, cross_value_bias, hidden_up_bias],
        axis=1,
    ).astype(F32)
    mine = jnp.concatenate([local_mod.reshape(LAYERS, SLOTS * mod_width), vectors], axis=1)
    pair = jnp.stack([mine, tensor_hop(mine, 1)])
    quad = jnp.concatenate([pair, tensor_hop(pair, 2)], axis=0)
    quad = jnp.take(quad, rank ^ jnp.arange(4, dtype=jnp.int32), axis=0)
    mods = quad[:, :, : SLOTS * mod_width].reshape(4, LAYERS, SLOTS, mod_width)
    mods = mods.transpose(1, 2, 0, 3).reshape(LAYERS, SLOTS, 4 * mod_width)
    rest = quad[:, :, SLOTS * mod_width :].transpose(1, 0, 2)
    biases = [
        rest[:, :, i * narrow : (i + 1) * narrow].reshape(LAYERS, 1, 4 * narrow) for i in range(4)
    ]
    up_biases = rest[:, :, 4 * narrow :].reshape(LAYERS, 1, 4 * units)
    all_times = gather_dp(timesteps)

    def pack(layer, members):
        rows = sum(a.shape[2] if flip else a.shape[1] for a, flip in members)
        specs = [
            pl.BlockSpec((None,) + a.shape[1:], lambda i, layer=layer: (layer, 0, 0))
            for a, _ in members
        ]
        own, first = pl.pallas_call(
            partial(pack_kernel, transposed=tuple(flip for _, flip in members)),
            grid=(1,),
            out_shape=[shape(rows, width, dtype=BF), shape(rows // 2, width, dtype=BF)],
            in_specs=[SMALL] + specs,
            out_specs=[
                pl.BlockSpec((rows, width), lambda i: (0, 0)),
                pl.BlockSpec((rows // 2, width), lambda i: (0, 0)),
            ],
            compiler_params=pltpu.CompilerParams(vmem_limit_bytes=VMEM_BYTES),
            cost_estimate=pl.CostEstimate(
                flops=2 * rows * width * 192, bytes_accessed=5 * rows * width, transcendentals=0
            ),
            name="pack_weights",
        )(info, *[a for a, _ in members])
        sib = tensor_hop(own, 1)
        xa = tensor_hop(first, 2)
        ya = dp_hop(xa, 1)
        return (own, sib, xa, ya, tensor_hop(xa, 1), tensor_hop(ya, 1))

    groups = []
    for layer in range(LAYERS):
        groups.append(
            (
                pack(
                    layer,
                    [(self_query, 1), (self_key, 1), (self_value, 1), (self_output, 0)],
                ),
                pack(
                    layer,
                    [(cross_query, 1), (cross_key, 1), (cross_value, 1), (cross_output, 0)],
                ),
                pack(layer, [(hidden_up, 1), (hidden_down, 0)]),
            )
        )

    text_rows = jnp.pad(text, ((0, 0), (0, LANES - words), (0, 0))).reshape(-1, width)
    square = 2 * share * width * width
    near = lambda *arrays: [(NEAR, a) for a in arrays]
    weights_in = lambda group: [(ANY, a) for a in group]
    whole = pltpu.VMEM((width, width), BF)
    wide = pltpu.VMEM((4 * units, width), BF)
    floats = pltpu.VMEM((share, width), F32)
    sems = lambda n: pltpu.SemaphoreType.DMA((n,))
    frame_low = shape(share, width, dtype=BF)
    frame_high = shape(share, width)
    two_low = shape(2, share, width, dtype=BF)
    logs = shape(16, share)
    log_work = pltpu.VMEM((share, LANES), F32)

    x = lax.dynamic_slice_in_dim(tokens, core * share, share).astype(F32)
    kept = []
    for layer in range(LAYERS):
        mod = mods[layer]
        s_group, c_group, f_group = groups[layer]
        entry1, q, kv = run(
            qkv_kernel,
            "self_qkv",
            [(SMALL, info)] + near(x, mod, biases[0][layer], biases[1][layer]) + weights_in(s_group),
            [frame_low, frame_low, two_low],
            [whole, whole, whole, sems(12)],
            3 * square,
        )
        kv_sib = tensor_hop(kv, 1)
        out_bias = self_output_bias[layer][None].astype(F32)
        x1, mixed1, lse1, branch1 = run(
            self_kernel,
            "self_attention",
            [(SMALL, info)] + near(x, mod, out_bias, q, kv, kv_sib) + weights_in(s_group),
            [frame_high, frame_low, logs, frame_low],
            [whole, log_work, floats, sems(4)],
            8 * square,
        )
        out_bias = cross_output_bias[layer][None].astype(F32)
        x2, entry2, cq, ckv, mixed2, lse2, branch2 = run(
            partial(cross_kernel, words=words),
            "cross_attention",
            [(SMALL, info)]
            + near(x1, mod, biases[2][layer], biases[3][layer], out_bias, text_rows)
            + weights_in(c_group),
            [
                frame_high,
                frame_low,
                frame_low,
                shape(2, SLOTS * LANES, width, dtype=BF),
                frame_low,
                logs,
                frame_low,
            ],
            [whole, whole, whole, whole, log_work, floats, sems(16)],
            5 * square,
        )
        out_bias = hidden_down_bias[layer][None].astype(F32)
        x3, entry3, active, slope, branch3 = run(
            hidden_kernel,
            "feed_forward",
            [(SMALL, info)] + near(x2, mod, up_biases[layer], out_bias) + weights_in(f_group),
            [
                frame_high,
                frame_low,
                shape(share, 4 * units, dtype=BF),
                shape(share, 4 * units, dtype=BF),
                frame_low,
            ],
            [wide, wide, pltpu.VMEM((2, share, TILE), F32), floats, sems(8)],
            8 * square,
        )
        kept.append(
            (
                x,
                entry1,
                q,
                kv,
                kv_sib,
                mixed1,
                lse1,
                branch1,
                x1,
                entry2,
                cq,
                ckv,
                mixed2,
                lse2,
                branch2,
                x2,
                entry3,
                active,
                slope,
                branch3,
            )
        )
        x = x3

    def join(rows):
        rows = rows.astype(BF)
        other = tensor_hop(rows, 1)
        return jnp.concatenate(
            [jnp.where(core == 0, rows, other), jnp.where(core == 0, other, rows)], axis=0
        )

    output = join(x)

    def reduce_grads(send, keep):
        summed = keep.astype(F32) + tensor_hop(send, 1).astype(F32)
        return scatter_dp(summed.astype(BF))

    def narrow_grads(lefts, rights):
        half = pl.BlockSpec((share, 2 * narrow), lambda i, info: (0, info[6]))
        full = pl.BlockSpec((share, width), lambda i, info: (0, 0))
        result = pl.BlockSpec((width, 4 * narrow), lambda i, info: (0, 0))
        send, keep = pl.pallas_call(
            narrow_grad_kernel,
            grid_spec=pltpu.PrefetchScalarGridSpec(
                num_scalar_prefetch=1,
                grid=(1,),
                in_specs=[full] * 4 + [half] * 4,
                out_specs=[result] * 2,
            ),
            out_shape=[shape(width, 4 * narrow, dtype=BF)] * 2,
            compiler_params=pltpu.CompilerParams(vmem_limit_bytes=VMEM_BYTES),
            cost_estimate=pl.CostEstimate(
                flops=2 * square, bytes_accessed=14 * share * width, transcendentals=0
            ),
            name="narrow_grads",
        )(info, *lefts, *rights)
        return reduce_grads(send, keep)

    def wide_grads(entry, gb, d_before, active):
        full = pl.BlockSpec((share, width), lambda i, info: (0, 0))
        sib = pl.BlockSpec((share, units), lambda i, info: (0, info[7]))
        own = pl.BlockSpec((share, units), lambda i, info: (0, info[5]))
        result = pl.BlockSpec((width, 2 * units), lambda i, info: (0, 0))
        send, keep = pl.pallas_call(
            wide_grad_kernel,
            grid_spec=pltpu.PrefetchScalarGridSpec(
                num_scalar_prefetch=1,
                grid=(1,),
                in_specs=[full, full, sib, own, sib, own],
                out_specs=[result] * 2,
            ),
            out_shape=[shape(width, 2 * units, dtype=BF)] * 2,
            compiler_params=pltpu.CompilerParams(vmem_limit_bytes=VMEM_BYTES),
            cost_estimate=pl.CostEstimate(
                flops=4 * square, bytes_accessed=24 * share * width, transcendentals=0
            ),
            name="wide_grads",
        )(info, entry, gb, d_before, d_before, active, active)
        return reduce_grads(send, keep)

    stat_shape = shape(24, width)
    g = lax.dynamic_slice_in_dim(cotangent, core * share, share)
    grads, sums = [None] * LAYERS, [None] * LAYERS
    for layer in reversed(range(LAYERS)):
        mod = mods[layer]
        s_group, c_group, f_group = groups[layer]
        (
            x,
            entry1,
            q,
            kv,
            kv_sib,
            mixed1,
            lse1,
            branch1,
            x1,
            entry2,
            cq,
            ckv,
            mixed2,
            lse2,
            branch2,
            x2,
            entry3,
            active,
            slope,
            branch3,
        ) = kept[layer]
        g, gb3, d_before, stats3 = run(
            hidden_back_kernel,
            "feed_forward_back",
            [(SMALL, info)] + near(x2, g, mod, branch3, slope) + weights_in(f_group),
            [frame_high, frame_low, shape(share, 4 * units, dtype=BF), stat_shape],
            [
                wide,
                wide,
                pltpu.VMEM((2, share, TILE), F32),
                floats,
                pltpu.VMEM((1, 4 * units), F32),
                sems(8),
            ],
            8 * square,
        )
        f_grads = wide_grads(entry3, gb3, d_before, active)
        g, gb2, dcq, dckv, stats2 = run(
            partial(cross_back_kernel, words=words),
            "cross_attention_back",
            [(SMALL, info)] + near(x1, g, mod, branch2, cq, ckv, lse2) + weights_in(c_group),
            [
                frame_high,
                frame_low,
                frame_low,
                shape(2, SLOTS * LANES, width, dtype=BF),
                stat_shape,
            ],
            [
                whole,
                whole,
                pltpu.VMEM((share, width), BF),
                floats,
                pltpu.VMEM((2, SLOTS * LANES, width), F32),
                sems(8),
            ],
            5 * square,
        )
        c_grads = narrow_grads(
            (entry2, text_rows, text_rows, gb2), (dcq, dckv[0], dckv[1], mixed2)
        )
        gb1, dq, dkv_own, dkv_give, early = run(
            self_back_kernel,
            "self_attention_back",
            [(SMALL, info)] + near(g, mod, branch1, q, kv, kv_sib, lse1) + weights_in(s_group),
            [frame_low, frame_low, two_low, two_low, stat_shape],
            [whole, pltpu.VMEM((share, width), BF), sems(4)],
            16 * square,
        )
        dkv_sib = tensor_hop(dkv_give, 1)
        g, dkv, stats1 = run(
            qkv_back_kernel,
            "self_qkv_back",
            [(SMALL, info)] + near(x, g, mod, dq, dkv_own, dkv_sib, early) + weights_in(s_group),
            [frame_high, two_low, stat_shape],
            [whole, whole, whole, floats, sems(12)],
            3 * square,
        )
        s_grads = narrow_grads((entry1, entry1, entry1, gb1), (dq, dkv[0], dkv[1], mixed1))
        grads[layer] = (s_grads, c_grads, f_grads)
        stats = jnp.stack([stats1, stats2, stats3])
        sums[layer] = stats + tensor_hop(stats, 1)
    input_grad = join(g)

    vector_parts = []
    for layer in range(LAYERS):
        stats = sums[layer]
        rows = stats[:, :12].reshape(9, SLOTS, width).transpose(1, 0, 2).reshape(SLOTS, 9 * width)
        rows = lax.dynamic_slice_in_dim(rows, rank * mod_width, mod_width, 1)
        four = stats[:2, 13:15].reshape(4, width)
        four = lax.dynamic_slice_in_dim(four, rank * narrow, narrow, 1)
        ups = lax.dynamic_index_in_dim(stats[2, 13:17], rank, 0, keepdims=False)
        vector_parts.append(
            jnp.concatenate(
                [rows.reshape(-1), four.reshape(-1), ups, stats[:, 12].reshape(-1)]
            )
        )
    gathered = gather_dp(jnp.stack(vector_parts)[None])
    count = gathered.shape[0]
    mod_rows = gathered[:, :, : SLOTS * mod_width].reshape(count, LAYERS, SLOTS, mod_width)
    summed = jnp.sum(gathered[:, :, SLOTS * mod_width :], axis=0)
    conditions = jax.nn.silu(time_features(all_times, width)).astype(BF).astype(F32)
    part = width // count
    conditions = lax.dynamic_slice_in_dim(conditions, me * part, part, 1)
    modulation_grad = jnp.einsum(
        "nsd,nlsc->ldc",
        conditions.reshape(count, SLOTS, part),
        mod_rows,
        precision=lax.Precision.HIGHEST,
        preferred_element_type=F32,
    )
    modulation_bias_grad = jnp.sum(mod_rows, axis=(0, 2))
    q_sum, v_sum, cq_sum, cv_sum = [summed[:, i * narrow : (i + 1) * narrow] for i in range(4)]
    at = 4 * narrow
    up_sum = summed[:, at : at + units]
    at += units
    out_sums = [
        lax.dynamic_slice_in_dim(summed[:, at + i * width : at + (i + 1) * width], me * part, part, 1)
        for i in range(3)
    ]

    def both(pick):
        return jnp.stack([pick(*grads[layer]) for layer in range(LAYERS)])

    step = 2 * narrow
    s_pairs = [(unpack(s[:, :step]), unpack(s[:, step:])) for s, _, _ in grads]
    c_pairs = [(unpack(c[:, :step]), unpack(c[:, step:])) for _, c, _ in grads]
    stack = lambda pairs, i, j: jnp.stack([p[i][j] for p in pairs])
    turn = lambda values: jnp.swapaxes(values, 1, 2)
    return (
        output,
        input_grad,
        stack(s_pairs, 0, 0),
        q_sum,
        stack(s_pairs, 0, 1),
        stack(s_pairs, 1, 0),
        v_sum,
        turn(stack(s_pairs, 1, 1)),
        out_sums[0],
        stack(c_pairs, 0, 0),
        cq_sum,
        stack(c_pairs, 0, 1),
        stack(c_pairs, 1, 0),
        cv_sum,
        turn(stack(c_pairs, 1, 1)),
        out_sums[1],
        both(lambda s, c, f: f[:, :units]),
        up_sum,
        turn(both(lambda s, c, f: f[:, units:])),
        out_sums[2],
        modulation_grad,
        modulation_bias_grad,
    )


def solution(mesh):
    dp, tensor = "dp", "tensor"
    columns, vector = P(None, None, tensor), P(None, tensor)
    matrix, turned, spread = P(None, dp, tensor), P(None, tensor, dp), P(None, dp)
    placed = (
        P(dp, None),
        P(dp, None, None),
        P(dp),
        P(dp),
        P(dp, None),
        columns,
        vector,
        columns,
        columns,
        vector,
        P(None, tensor, None),
        P(),
        columns,
        vector,
        columns,
        columns,
        vector,
        P(None, tensor, None),
        P(),
        columns,
        vector,
        P(None, tensor, None),
        P(),
        columns,
        vector,
    )
    results = (
        P(dp, None),
        P(dp, None),
        matrix,
        vector,
        matrix,
        matrix,
        vector,
        turned,
        spread,
        matrix,
        vector,
        matrix,
        matrix,
        vector,
        turned,
        spread,
        matrix,
        vector,
        turned,
        spread,
        matrix,
        vector,
    )
    return jax.shard_map(
        shards, mesh=mesh, in_specs=placed, out_specs=results, check_vma=False
    )
```

```python
from functools import partial
import math

import jax
import jax.numpy as jnp
from jax import lax
from jax.experimental import pallas as pl
from jax.experimental.pallas import tpu as pltpu
from jax.sharding import PartitionSpec as P

HEAD_WIDTH = 64
UNIT = 256
LAYERS = 2
WINDOW = 1024
EPSILON = 1e-06
LANES = 128
CHUNK = 64
TILE = 512
SLOTS = WINDOW // UNIT
FAR = -1e30
VMEM_BYTES = 56 * 1024 * 1024
BF = jnp.bfloat16
F32 = jnp.float32
ROOT = math.sqrt(2.0 / math.pi)
CUBIC = 0.044715


def dot_nn(left, right):
    return jnp.dot(left, right, preferred_element_type=F32)


def dot_nt(left, right):
    return lax.dot_general(left, right, (((1,), (1,)), ((), ())), preferred_element_type=F32)


def dot_tn(left, right):
    return lax.dot_general(left, right, (((0,), (0,)), ((), ())), preferred_element_type=F32)


SMALL = pl.BlockSpec(memory_space=pltpu.SMEM)
NEAR = pl.BlockSpec(memory_space=pltpu.VMEM)
ANY = pl.BlockSpec(memory_space=pl.ANY)


class Work:
    def __init__(self, ins, outs, scratch, in_sems, out_sems):
        self.ins, self.outs, self.scratch, self.out_sems = ins, outs, scratch, out_sems
        self.copies, self.waited, self.flushed = {}, set(), []
        for index, (name, (ref, buffer)) in enumerate(ins.items()):
            self.copies[name] = pltpu.make_async_copy(ref, buffer, in_sems.at[index])
            self.copies[name].start()

    def __getattr__(self, name):
        if name in self.__dict__["ins"]:
            return self.ins[name][1]
        if name in self.__dict__["outs"]:
            return self.outs[name][1]
        return self.__dict__["scratch"][name]

    def need(self, *names):
        for name in names:
            if name not in self.waited:
                self.waited.add(name)
                self.copies[name].wait()

    def flush(self, name, *at):
        ref, buffer = self.outs[name]
        if at:
            ref, buffer = ref.at[at], buffer.at[at]
        copy = pltpu.make_async_copy(buffer, ref, self.out_sems.at[len(self.flushed)])
        copy.start()
        self.flushed.append(copy)

    def finish(self):
        self.need(*self.ins)
        for copy in self.flushed:
            copy.wait()


def run(body, name, info, ins, small, weights, outs, small_outs, scratch, after=(), cost=1.0):
    in_names, out_names, names = list(ins), list(outs), list(scratch)
    small_names, small_out_names = list(small), list(small_outs)
    counts = [1, len(in_names), len(small), len(weights), len(after), len(outs), len(small_outs)]

    def kernel(*refs):
        refs = list(refs)
        parts = []
        for count in counts:
            parts.append(refs[:count])
            refs = refs[count:]
        (info_ref,), in_refs, small_refs, weight_refs, _, out_refs, small_out_refs = parts
        in_bufs, refs = refs[: len(in_names)], refs[len(in_names) :]
        out_bufs, refs = refs[: len(out_names)], refs[len(out_names) :]
        rest, (in_sems, out_sems) = refs[: len(names)], refs[len(names) :]
        extra = dict(zip(names, rest))
        extra.update(zip(small_names, small_refs))
        extra.update(zip(small_out_names, small_out_refs))
        work = Work(
            dict(zip(in_names, zip(in_refs, in_bufs))),
            dict(zip(out_names, zip(out_refs, out_bufs))),
            extra,
            in_sems,
            out_sems,
        )
        body(info_ref, work, weight_refs)
        work.finish()

    buffer = lambda a: pltpu.VMEM(a.shape, a.dtype)
    results = pl.pallas_call(
        kernel,
        out_shape=[outs[n] for n in out_names] + [small_outs[n] for n in small_out_names],
        in_specs=[SMALL]
        + [ANY] * len(ins)
        + [NEAR] * len(small)
        + [ANY] * (len(weights) + len(after)),
        out_specs=[ANY] * len(outs) + [NEAR] * len(small_outs),
        scratch_shapes=[buffer(ins[n]) for n in in_names]
        + [buffer(outs[n]) for n in out_names]
        + [scratch[n] for n in names]
        + [pltpu.SemaphoreType.DMA((max(len(ins), 1),)), pltpu.SemaphoreType.DMA((32,))],
        compiler_params=pltpu.CompilerParams(vmem_limit_bytes=VMEM_BYTES),
        cost_estimate=lasting(cost),
        name=name,
    )(info, *ins.values(), *small.values(), *weights, *after)
    return results


def lasting(units):
    return pl.CostEstimate(flops=int(units * 0.4e9), bytes_accessed=1000, transcendentals=0)


def shape(*dims, dtype=F32):
    return jax.ShapeDtypeStruct(dims, dtype)


def start_rows(refs, place, plan, sems):
    own, sib, xa, ya, xb, yb = refs
    half = own.shape[0] // 2
    for rank in range(4):
        for parity in range(2):

            @pl.when(place == rank * 2 + parity)
            def _(rank=rank, parity=parity):
                for index, (shard, row, rows, dst) in enumerate(plan):
                    step = shard ^ rank
                    if step < 2:
                        src = (own, sib)[step].at[pl.ds(row, rows)]
                    else:
                        first, second = ((xa, ya), (xb, yb))[step - 2]
                        part = row // half
                        src = (first if part == parity else second).at[pl.ds(row - part * half, rows)]
                    pltpu.make_async_copy(src, dst, sems.at[index]).start()


def wait_rows(refs, plan, sems, which):
    for index in which:
        _, row, rows, dst = plan[index]
        pltpu.make_async_copy(refs[0].at[pl.ds(0, rows)], dst, sems.at[index]).wait()


def plan_of(buffers, first, rows):
    return [
        (shard, (first + which) * rows, rows, dst.at[pl.ds(shard * rows, rows)])
        for which, dst in enumerate(buffers)
        for shard in range(4)
    ]


def norm_rows(values):
    mean = jnp.mean(values, axis=-1, keepdims=True)
    center = values - mean
    factor = lax.rsqrt(jnp.mean(center * center, axis=-1, keepdims=True) + EPSILON)
    return center * factor, factor


def piece(mod, slot, index):
    width = mod.shape[1] // 9
    return mod[pl.ds(slot, 1), index * width : (index + 1) * width]


def entry_rows(x, mod, info, index, out):
    for block in range(x.shape[0] // UNIT):
        slot = info[1 + block]
        shift = piece(mod, slot, index)
        scale = 1.0 + piece(mod, slot, index + 1)

        def step(turn, carry):
            rows = pl.ds(pl.multiple_of(block * UNIT + turn * CHUNK, CHUNK), CHUNK)
            normed, _ = norm_rows(x[rows, :])
            out[rows, :] = (normed * scale + shift).astype(BF)
            return carry

        lax.fori_loop(0, UNIT // CHUNK, step, 0, unroll=True)


def residual_rows(x, mod, info, index, branch, branch_out, out):
    for block in range(x.shape[0] // UNIT):
        gate = piece(mod, info[1 + block], index)

        def step(turn, carry):
            rows = pl.ds(pl.multiple_of(block * UNIT + turn * CHUNK, CHUNK), CHUNK)
            values = branch[rows, :]
            branch_out[rows, :] = values.astype(BF)
            out[rows, :] = x[rows, :] + gate * values
            return carry

        lax.fori_loop(0, UNIT // CHUNK, step, 0, unroll=True)


def fold(values):
    return jnp.sum(values.reshape(values.shape[0] // 8, 8, values.shape[1]), axis=0)


def total(values):
    return jnp.sum(values, axis=0, keepdims=True)


def gate_back(g, mod, info, index, branch, gb, stats):
    width = g.shape[1]
    sums = jnp.zeros((8, width), F32)
    for block in range(g.shape[0] // UNIT):
        slot = info[1 + block]
        gate = piece(mod, slot, index)

        def step(turn, carry):
            rows = pl.ds(pl.multiple_of(block * UNIT + turn * CHUNK, CHUNK), CHUNK)
            grad = g[rows, :].astype(F32)
            low = (gate * grad).astype(BF)
            gb[rows, :] = low
            return (
                carry[0] + fold(low.astype(F32)),
                carry[1] + fold(grad * branch[rows, :].astype(F32)),
            )

        sums, rows_sum = lax.fori_loop(
            0, UNIT // CHUNK, step, (sums, jnp.zeros((8, width), F32)), unroll=True
        )
        stats[pl.ds(8 + slot, 1), :] += total(rows_sum)
    stats[12:13, :] = total(sums)


def norm_back_rows(x, g, de, mod, info, index, out, stats):
    width = x.shape[1]
    for block in range(x.shape[0] // UNIT):
        slot = info[1 + block]
        scale = 1.0 + piece(mod, slot, index + 1)

        def step(turn, carry):
            rows = pl.ds(pl.multiple_of(block * UNIT + turn * CHUNK, CHUNK), CHUNK)
            normed, factor = norm_rows(x[rows, :])
            grad = de[rows, :]
            inner = grad * normed
            dn = grad * scale
            mean = jnp.mean(dn, axis=-1, keepdims=True)
            along = jnp.mean(dn * normed, axis=-1, keepdims=True)
            out[rows, :] = g[rows, :].astype(F32) + factor * (dn - mean - normed * along)
            return (carry[0] + fold(grad), carry[1] + fold(inner))

        zero = jnp.zeros((8, width), F32)
        shift_sum, scale_sum = lax.fori_loop(0, UNIT // CHUNK, step, (zero, zero), unroll=True)
        stats[pl.ds(slot, 1), :] += total(shift_sum)
        stats[pl.ds(4 + slot, 1), :] += total(scale_sum)


def lane_ids(rows):
    return lax.broadcasted_iota(jnp.int32, (rows, LANES), 1)


def head_half(values, half):
    ids = lane_ids(values.shape[0])
    keep = ids < HEAD_WIDTH if half == 0 else ids >= HEAD_WIDTH
    return jnp.where(keep, values.astype(F32), 0.0)


def query_marks(slot):
    return jnp.where(lane_ids(UNIT) == slot, 1.0, 0.0).astype(BF)


def key_marks(slots):
    ids = lane_ids(UNIT)
    parts = [jnp.where((ids < SLOTS) & (ids != slot), FAR, 0.0).astype(BF) for slot in slots]
    return jnp.concatenate(parts, axis=0)


def pair_lanes(pair):
    return pl.ds(pl.multiple_of(pair * LANES, LANES), LANES)


def qkv_kernel(info, work, weights):
    rows = weights[0].shape[0] // 4
    sems = work.sems
    plan = plan_of((work.wq, work.wk, work.wv), 0, rows)
    start_rows(weights, info[0], plan, sems)
    work.need("x")
    entry_rows(work.x, work.mod, info, 0, work.entry)
    work.flush("entry")
    entry = work.entry[...]
    wait_rows(weights, plan, sems, range(4, 8))
    work.kv[0] = dot_nt(entry, work.wk[...]).astype(BF)
    work.flush("kv", 0)
    wait_rows(weights, plan, sems, range(8, 12))
    work.kv[1] = (dot_nt(entry, work.wv[...]) + work.v_bias[...]).astype(BF)
    work.flush("kv", 1)
    wait_rows(weights, plan, sems, range(0, 4))
    work.q[...] = (dot_nt(entry, work.wq[...]) + work.q_bias[...]).astype(BF)
    work.flush("q")


def soft_pair(work, q_pair, keys, values, marks, logs, pair, span, words=None):
    ids = lane_ids(UNIT)
    results = []
    kept = logs[span, :]
    for half in range(2):
        left = (head_half(q_pair, half) * HEAD_WIDTH**-0.5).astype(BF)
        if marks is not None:
            left = jnp.concatenate([left, marks], axis=1)
        scores = dot_nt(left, keys)
        if words is not None:
            scores = jnp.where(ids < words, scores, FAR)
        peak = jnp.max(scores, axis=-1, keepdims=True)
        both = dot_nn(jnp.exp(scores - peak).astype(BF), values)
        sums = both[:, LANES:]
        results.append(both[:, :LANES] / sums)
        kept = jnp.where(ids == 2 * pair + half, peak + jnp.log(sums), kept)
    logs[span, :] = kept
    return jnp.where(ids < HEAD_WIDTH, results[0], results[1]).astype(BF)


def self_kernel(info, work, weights):
    rows = weights[0].shape[0] // 4
    sems = work.sems
    plan = [(s, 3 * rows, rows, work.wo.at[pl.ds(s * rows, rows)]) for s in range(4)]
    start_rows(weights, info[0], plan, sems)
    share = work.x.shape[0]
    blocks = share // UNIT
    marks = key_marks([info[1 + b] for b in range(2 * blocks)])
    ones = jnp.ones((2 * share, LANES), BF)
    logs, mixed = work.logs, work.mixed
    logs[...] = jnp.zeros(logs.shape, F32)
    work.need("q", "kv_own", "kv_sib")

    def both(which, lanes):
        return jnp.concatenate([work.kv_own[which, :, lanes], work.kv_sib[which, :, lanes]], axis=0)

    def step(pair, carry):
        lanes = pair_lanes(pair)
        keys = jnp.concatenate([both(0, lanes), marks], axis=1)
        values = jnp.concatenate([both(1, lanes), ones], axis=1)
        for block in range(blocks):
            span = pl.ds(block * UNIT, UNIT)
            mixed[span, lanes] = soft_pair(
                work,
                work.q[span, lanes],
                keys,
                values,
                query_marks(info[1 + block]),
                logs,
                pair,
                span,
            )
        return carry

    lax.fori_loop(0, mixed.shape[1] // LANES, step, 0)
    work.flush("mixed")
    work.lse[...] = logs[...].T[: work.lse.shape[0], :]
    work.flush("lse")
    wait_rows(weights, plan, sems, range(4))
    work.sum[...] = dot_nn(mixed[...], work.wo[...]) + work.bias[...]
    work.need("x")
    residual_rows(work.x, work.mod, info, 2, work.sum, work.branch, work.out)
    work.flush("branch")
    work.flush("out")


def cross_kernel(info, work, weights, words):
    rows = weights[0].shape[0] // 4
    sems = work.sems
    order = (1, 2, 0, 3)
    plan = [
        (shard, order[i // 4] * rows, count, dst)
        for i, (shard, _, count, dst) in enumerate(
            plan_of((work.wk, work.wv, work.wq, work.wo), 0, rows)
        )
    ]
    start_rows(weights, info[0], plan, sems)
    work.need("x")
    entry_rows(work.x, work.mod, info, 3, work.entry)
    work.flush("entry")
    work.need("text")
    wait_rows(weights, plan, sems, range(0, 4))
    work.kv[0] = dot_nt(work.text[...], work.wk[...]).astype(BF)
    wait_rows(weights, plan, sems, range(4, 8))
    work.kv[1] = (dot_nt(work.text[...], work.wv[...]) + work.v_bias[...]).astype(BF)
    work.flush("kv")
    wait_rows(weights, plan, sems, range(8, 12))
    work.q[...] = (dot_nt(work.entry[...], work.wq[...]) + work.q_bias[...]).astype(BF)
    work.flush("q")
    ones = jnp.ones((LANES, LANES), BF)
    logs, mixed = work.logs, work.mixed
    logs[...] = jnp.zeros(logs.shape, F32)

    def step(pair, carry):
        lanes = pair_lanes(pair)
        for block in range(mixed.shape[0] // UNIT):
            span = pl.ds(block * UNIT, UNIT)
            own = pl.ds(pl.multiple_of(info[1 + block] * LANES, LANES), LANES)
            mixed[span, lanes] = soft_pair(
                work,
                work.q[span, lanes],
                work.kv[0, own, lanes],
                jnp.concatenate([work.kv[1, own, lanes], ones], axis=1),
                None,
                logs,
                pair,
                span,
                words,
            )
        return carry

    lax.fori_loop(0, mixed.shape[1] // LANES, step, 0, unroll=2)
    work.flush("mixed")
    work.lse[...] = logs[...].T[: work.lse.shape[0], :]
    work.flush("lse")
    wait_rows(weights, plan, sems, range(12, 16))
    work.sum[...] = dot_nn(mixed[...], work.wo[...]) + work.bias[...]
    residual_rows(work.x, work.mod, info, 5, work.sum, work.branch, work.out)
    work.flush("branch")
    work.flush("out")


def halves_of(buffer):
    half = buffer.shape[1] // 2
    return [
        (shard, part * half, half, buffer.at[shard, pl.ds(part * half, half)])
        for shard in range(4)
        for part in range(2)
    ]


def hidden_kernel(info, work, ups, downs):
    sems = work.sems
    width = work.x.shape[1]
    up_plan = halves_of(work.up)
    down_plan = halves_of(work.down)
    start_rows(ups, info[0], up_plan, sems)
    start_rows(downs, info[0], down_plan, work.down_sems)
    work.need("x")
    entry_rows(work.x, work.mod, info, 6, work.entry)
    work.flush("entry")
    before = (work.before0, work.before1)

    def columns(shard):
        return pl.ds(shard * width, width)

    def rise(shard):
        wait_rows(ups, up_plan, sems, [2 * shard, 2 * shard + 1])
        before[shard % 2][...] = dot_nn(work.entry[...], work.up[shard])

    def bend(shard):
        bias = work.up_bias[:, columns(shard)]
        for row in range(0, work.x.shape[0], CHUNK):
            span = pl.ds(row, CHUNK)
            values = before[shard % 2][span, :] + bias
            square = values * values
            turn = jnp.tanh(values * (ROOT + (ROOT * CUBIC) * square))
            half = 0.5 + 0.5 * turn
            work.active[span, columns(shard)] = (values * half).astype(BF)
            work.slope[span, columns(shard)] = (
                half
                + (values * (0.5 - 0.5 * (turn * turn))) * (ROOT + (3.0 * ROOT * CUBIC) * square)
            ).astype(BF)
        work.flush("active", slice(None), columns(shard))
        work.flush("slope", slice(None), columns(shard))

    def fall(shard):
        wait_rows(downs, down_plan, work.down_sems, [2 * shard, 2 * shard + 1])
        part = dot_nn(work.active[:, columns(shard)], work.down[shard])
        work.sum[...] = part + (work.bias[...] if shard == 0 else work.sum[...])

    rise(0)
    for shard in range(4):
        if shard < 3:
            rise(shard + 1)
        bend(shard)
        fall(shard)
    residual_rows(work.x, work.mod, info, 8, work.sum, work.branch, work.out)
    work.flush("branch")
    work.flush("out")


def hidden_back_kernel(info, work, ups, downs):
    sems = work.sems
    width = work.x.shape[1]
    up_plan = halves_of(work.up)
    down_plan = halves_of(work.down)
    start_rows(downs, info[0], down_plan, work.down_sems)
    start_rows(ups, info[0], up_plan, sems)
    stats = work.stats
    stats[...] = jnp.zeros(stats.shape, F32)
    work.need("g", "branch")
    gate_back(work.g, work.mod, info, 8, work.branch, work.gb, stats)
    work.flush("gb")
    before = (work.before0, work.before1)
    work.need("slope")

    def columns(shard):
        return pl.ds(shard * width, width)

    def rise(shard):
        wait_rows(downs, down_plan, work.down_sems, [2 * shard, 2 * shard + 1])
        before[shard % 2][...] = dot_nt(work.gb[...], work.down[shard])

    def bend(shard):
        sums = jnp.zeros((8, width), F32)
        for row in range(0, work.x.shape[0], CHUNK):
            span = pl.ds(row, CHUNK)
            low = (before[shard % 2][span, :] * work.slope[span, columns(shard)].astype(F32)).astype(BF)
            work.d_before[span, columns(shard)] = low
            sums += fold(low.astype(F32))
        stats[13 + shard : 14 + shard, :] = total(sums)
        work.flush("d_before", slice(None), columns(shard))

    def fall(shard):
        wait_rows(ups, up_plan, sems, [2 * shard, 2 * shard + 1])
        part = dot_nt(work.d_before[:, columns(shard)], work.up[shard])
        work.de[...] = part if shard == 0 else work.de[...] + part

    rise(0)
    for shard in range(4):
        if shard < 3:
            rise(shard + 1)
        bend(shard)
        fall(shard)
    work.need("x")
    norm_back_rows(work.x, work.g, work.de, work.mod, info, 6, work.out, stats)
    work.flush("out")


def cross_back_kernel(info, work, weights, words):
    rows = weights[0].shape[0] // 4
    sems = work.sems
    plan = [
        (shard, (3 * rows, 0)[i // 4], count, dst)
        for i, (shard, _, count, dst) in enumerate(plan_of((work.wo, work.wq), 0, rows))
    ]
    start_rows(weights, info[0], plan, sems)
    stats = work.stats
    stats[...] = jnp.zeros(stats.shape, F32)
    work.need("g", "branch")
    gate_back(work.g, work.mod, info, 5, work.branch, work.gb, stats)
    work.flush("gb")
    wait_rows(weights, plan, sems, range(0, 4))
    work.d_mixed[...] = dot_nt(work.gb[...], work.wo[...]).astype(BF)
    work.dkv_sum[...] = jnp.zeros(work.dkv_sum.shape, F32)
    real = lax.broadcasted_iota(jnp.int32, (LANES, UNIT), 0) < words
    work.need("q", "kv", "lse")

    def step(pair, carry):
        lanes = pair_lanes(pair)
        for block in range(work.q.shape[0] // UNIT):
            span = pl.ds(block * UNIT, UNIT)
            own = pl.ds(pl.multiple_of(info[1 + block] * LANES, LANES), LANES)
            q_pair = work.q[span, lanes]
            d_pair = work.d_mixed[span, lanes]
            keys = work.kv[0, own, lanes]
            values = work.kv[1, own, lanes]
            lefts, grads, turned, probs_low, scores_low = [], [], [], [], []
            for half in range(2):
                left = (head_half(q_pair, half) * HEAD_WIDTH**-0.5).astype(BF)
                grad = head_half(d_pair, half).astype(BF)
                logs = work.lse[pl.ds(2 * pair + half, 1), span]
                probs = jnp.where(real, jnp.exp(dot_nt(keys, left) - logs), 0.0)
                d_probs = dot_nt(values, grad)
                inner = jnp.sum(probs * d_probs, axis=0, keepdims=True)
                lefts.append(left)
                grads.append(grad)
                turned.append(head_half(keys, half).T.astype(BF))
                probs_low.append(probs.astype(BF))
                scores_low.append((probs * (d_probs - inner)).astype(BF))
            wide_scores = jnp.concatenate(scores_low, axis=1)
            grad_v = dot_nn(jnp.concatenate(probs_low, axis=1), jnp.concatenate(grads, axis=0))
            grad_k = dot_nn(wide_scores, jnp.concatenate(lefts, axis=0))
            grad_q = dot_nn(
                jnp.concatenate(turned, axis=1), jnp.concatenate(scores_low, axis=0)
            )
            work.dq[span, lanes] = (grad_q.T * HEAD_WIDTH**-0.5).astype(BF)
            work.dkv_sum[0, own, lanes] += grad_k
            work.dkv_sum[1, own, lanes] += grad_v
        return carry

    lax.fori_loop(0, work.q.shape[1] // LANES, step, 0, unroll=2)
    work.flush("dq")
    work.dkv[...] = work.dkv_sum[...].astype(BF)
    work.flush("dkv")
    stats[13:14, :] = total(fold(work.dq[...].astype(F32)))
    stats[14:15, :] = total(fold(work.dkv[1].astype(F32)))
    wait_rows(weights, plan, sems, range(4, 8))
    work.de[...] = dot_nn(work.dq[...], work.wq[...])
    work.need("x")
    norm_back_rows(work.x, work.g, work.de, work.mod, info, 3, work.out, stats)
    work.flush("out")


def self_back_kernel(info, work, weights):
    rows = weights[0].shape[0] // 4
    sems = work.sems
    plan = [(s, 3 * rows, rows, work.wo.at[pl.ds(s * rows, rows)]) for s in range(4)]
    start_rows(weights, info[0], plan, sems)
    stats = work.stats
    stats[...] = jnp.zeros(stats.shape, F32)
    work.need("g", "branch")
    gate_back(work.g, work.mod, info, 2, work.branch, work.gb, stats)
    work.flush("gb")
    share = work.g.shape[0]
    blocks = share // UNIT
    marks = key_marks([info[1 + b] for b in range(2 * blocks)])
    wait_rows(weights, plan, sems, range(4))
    work.d_mixed[...] = dot_nt(work.gb[...], work.wo[...]).astype(BF)
    work.need("q", "kv_own", "kv_sib", "lse")

    def both(which, lanes):
        return jnp.concatenate([work.kv_own[which, :, lanes], work.kv_sib[which, :, lanes]], axis=0)

    def step(pair, carry):
        lanes = pair_lanes(pair)
        keys = both(0, lanes)
        values = both(1, lanes)
        marked = jnp.concatenate([keys, marks], axis=1)
        turned = jnp.concatenate([head_half(keys, half).T.astype(BF) for half in range(2)], axis=1)
        lefts, grads, probs_low, scores_low = [], [], [], []
        for block in range(blocks):
            span = pl.ds(block * UNIT, UNIT)
            q_pair = work.q[span, lanes]
            d_pair = work.d_mixed[span, lanes]
            ends = query_marks(info[1 + block])
            for half in range(2):
                left = (head_half(q_pair, half) * HEAD_WIDTH**-0.5).astype(BF)
                grad = head_half(d_pair, half).astype(BF)
                logs = work.lse[pl.ds(2 * pair + half, 1), span]
                probs = jnp.exp(dot_nt(marked, jnp.concatenate([left, ends], axis=1)) - logs)
                d_probs = dot_nt(values, grad)
                inner = jnp.sum(probs * d_probs, axis=0, keepdims=True)
                lefts.append(left)
                grads.append(grad)
                probs_low.append(probs.astype(BF))
                scores_low.append((probs * (d_probs - inner)).astype(BF))
            grad_q = dot_nn(turned, jnp.concatenate(scores_low[-2:], axis=0))
            work.dq[span, lanes] = (grad_q.T * HEAD_WIDTH**-0.5).astype(BF)
        grad_v = dot_nn(jnp.concatenate(probs_low, axis=1), jnp.concatenate(grads, axis=0))
        grad_k = dot_nn(jnp.concatenate(scores_low, axis=1), jnp.concatenate(lefts, axis=0))
        for which, grad in ((0, grad_k.astype(BF)), (1, grad_v.astype(BF))):
            work.dkv_own[which, :, lanes] = grad[:share]
            work.dkv_give[which, :, lanes] = grad[share:]
        return carry

    lax.fori_loop(0, work.q.shape[1] // LANES, step, 0)
    work.flush("dkv_give")
    work.flush("dkv_own")
    work.flush("dq")


def qkv_back_kernel(info, work, weights):
    rows = weights[0].shape[0] // 4
    sems = work.sems
    plan = plan_of((work.wq, work.wk, work.wv), 0, rows)
    start_rows(weights, info[0], plan, sems)
    stats = work.stats
    stats[...] = work.early[...]
    work.need("dq")
    stats[13:14, :] = total(fold(work.dq[...].astype(F32)))
    wait_rows(weights, plan, sems, range(0, 4))
    work.de[...] = dot_nn(work.dq[...], work.wq[...])
    work.need("dkv_own", "dkv_sib")
    for which, weight in ((0, work.wk), (1, work.wv)):
        low = (work.dkv_own[which].astype(F32) + work.dkv_sib[which].astype(F32)).astype(BF)
        work.dkv[which] = low
        wait_rows(weights, plan, sems, range(4 + 4 * which, 8 + 4 * which))
        work.de[...] += dot_nn(low, weight[...])
    work.flush("dkv")
    stats[14:15, :] = total(fold(work.dkv[1].astype(F32)))
    work.need("x", "g")
    norm_back_rows(work.x, work.g, work.de, work.mod, info, 0, work.out, stats)
    work.flush("out")


def wide_grad_kernel(info, entry, gb, db_sib, db_own, act_sib, act_own, *refs):
    send, keep = refs[-2:]
    width = entry.shape[1]
    left, right = entry[...].T, gb[...].T
    for out, db, act in ((send, db_sib, act_sib), (keep, db_own, act_own)):
        out[:, :width] = dot_nn(left, db[...]).astype(BF)
        out[:, width:] = dot_nn(right, act[...]).astype(BF)


def narrow_grad_kernel(info, *refs, lefts):
    count = max(lefts) + 1
    left_refs, rights, (send, keep) = refs[:count], refs[count : count + len(lefts)], refs[-2:]
    turned = [ref[...].T for ref in left_refs]
    low = lane_ids(turned[0].shape[0]) < HEAD_WIDTH
    step = 3 * LANES
    for at in range(len(lefts) // 2):
        products = [
            dot_nn(turned[lefts[2 * at + i]], rights[2 * at + i][...]) for i in range(2)
        ]
        (a0, a1, a2), (b0, b1, b2) = [
            [p[:, i * LANES : (i + 1) * LANES] for i in range(3)] for p in products
        ]
        even = (a0, b0, jnp.where(low, a1, pltpu.roll(b1, HEAD_WIDTH, 1)))
        a1, b1 = pltpu.roll(a1, HEAD_WIDTH, 1), pltpu.roll(b1, HEAD_WIDTH, 1)
        a2r, b2r = pltpu.roll(a2, HEAD_WIDTH, 1), pltpu.roll(b2, HEAD_WIDTH, 1)
        odd = (jnp.where(low, a1, a2r), jnp.where(low, b1, b2r), jnp.where(low, a2r, b2))
        for core in range(2):

            @pl.when(info[5] % 2 == core)
            def _(core=core):
                for out, parts in ((send, (odd, even)[core]), (keep, (even, odd)[core])):
                    for i, part in enumerate(parts):
                        out[:, at * step + i * LANES : at * step + (i + 1) * LANES] = part.astype(
                            BF
                        )


def merge_kernel(info, *refs, chains, after):
    ins, outs = refs[: 4 * chains], refs[4 * chains + after :]
    for chain in range(chains):
        for side in range(2):
            received, kept = ins[4 * chain + 2 * side], ins[4 * chain + 2 * side + 1]
            outs[2 * chain + side][...] = (
                received[...].astype(F32) + kept[...].astype(F32)
            ).astype(BF)


def gate(arrays, after):
    count = len(arrays)
    return pl.pallas_call(
        lambda *refs: None,
        out_shape=[shape(*a.shape, dtype=a.dtype) for a in arrays],
        in_specs=[ANY] * (count + len(after)),
        out_specs=[ANY] * count,
        input_output_aliases={i: i for i in range(count)},
        cost_estimate=lasting(0.5),
        name="gate",
    )(*arrays, *after)


def pack_kernel(info, *refs, groups, after):
    count = sum(len(members) for _, members in groups)
    sources, outs, sems = refs[:count], refs[count + after : -1], refs[-1]
    copies, halves = [], ([], [])
    at = 0
    for index, (layer, members) in enumerate(groups):
        out, first = outs[2 * index : 2 * index + 2]
        half = out.shape[0] // 2
        piece = out.shape[0] // 4
        for quarter in range(4):
            row = quarter * piece
            source = sources[at + row * len(members) // out.shape[0]]
            src = source.at[layer, pl.ds(row % source.shape[1], piece)]
            base = 6 * index
            copies.append(
                pltpu.make_async_copy(src, out.at[pl.ds(row, piece)], sems.at[base + quarter])
            )
            halves[quarter // 2].append(
                pltpu.make_async_copy(
                    src, first.at[pl.ds(row % half, piece)], sems.at[base + 4 + quarter % 2]
                )
            )
        at += len(members)
    for parity in range(2):

        @pl.when(info[0] % 2 == parity)
        def _(parity=parity):
            for copy in halves[parity]:
                copy.start()

    for copy in copies:
        copy.start()
    for parity in range(2):

        @pl.when(info[0] % 2 == parity)
        def _(parity=parity):
            for copy in halves[parity]:
                copy.wait()

    for copy in copies:
        copy.wait()


def tensor_hop(values, step):
    return lax.ppermute(values, "tensor", [(i, i ^ step) for i in range(4)])


def dp_hop(values, step):
    size = lax.axis_size("dp")
    return lax.ppermute(values, "dp", [(i, i ^ step) for i in range(size)])


def gather_dp(values):
    me = lax.axis_index("dp")
    step = 1
    while step < lax.axis_size("dp"):
        other = dp_hop(values, step)
        upper = (me & step) > 0
        values = jnp.concatenate(
            [jnp.where(upper, other, values), jnp.where(upper, values, other)], axis=0
        )
        step *= 2
    return values


def unpack(values):
    wide, rest = 2 * LANES, LANES + HEAD_WIDTH
    return (
        jnp.concatenate([values[:, :LANES], values[:, wide : wide + HEAD_WIDTH]], axis=1),
        jnp.concatenate([values[:, LANES:wide], values[:, wide + HEAD_WIDTH :]], axis=1),
    )


def time_features(moments, width):
    half = width // 2
    rates = jnp.exp(-math.log(10000.0) * jnp.arange(half, dtype=F32) / half)
    angles = moments.astype(F32)[:, None] * rates[None, :]
    return jnp.concatenate([jnp.cos(angles), jnp.sin(angles)], axis=1)


def shards(
    tokens,
    text,
    timesteps,
    item_frames,
    cotangent,
    self_query,
    self_query_bias,
    self_key,
    self_value,
    self_value_bias,
    self_output,
    self_output_bias,
    cross_query,
    cross_query_bias,
    cross_key,
    cross_value,
    cross_value_bias,
    cross_output,
    cross_output_bias,
    hidden_up,
    hidden_up_bias,
    hidden_down,
    hidden_down_bias,
    modulation,
    modulation_bias,
):
    frames, width = tokens.shape
    words = text.shape[1]
    mod_width = modulation.shape[2]
    narrow = self_query.shape[2]
    units = hidden_up.shape[2]
    rank = lax.axis_index("tensor")
    me = lax.axis_index("dp")
    size = lax.axis_size("dp")
    core = rank % 2
    share = frames // 2
    blocks = share // UNIT
    turn = lambda values: jnp.swapaxes(values, 1, 2)

    order = jnp.arange(SLOTS, dtype=jnp.int32)
    ends = jnp.sum(jnp.where(order[:, None] <= order[None, :], item_frames[:, None], 0), axis=0)
    turned = (jnp.arange(frames // UNIT, dtype=jnp.int32) + core * blocks) % (2 * blocks)
    slots = jnp.sum((turned[:, None] * UNIT >= ends[None, :]).astype(jnp.int32), axis=1)
    places = jnp.stack([rank, rank // 2, rank ^ 1, me]).astype(jnp.int32)
    info = jnp.concatenate([(rank * 2 + me % 2)[None].astype(jnp.int32), slots, places])

    condition = jax.nn.silu(time_features(timesteps, width)).astype(BF)
    local_mod = jnp.einsum(
        "sd,lcd->lsc", condition, turn(modulation), preferred_element_type=F32
    ) + modulation_bias[:, None, :].astype(F32)
    vectors = jnp.concatenate(
        [self_query_bias, self_value_bias, cross_query_bias, cross_value_bias, hidden_up_bias],
        axis=1,
    ).astype(F32)
    mine = jnp.concatenate([local_mod.reshape(LAYERS, SLOTS * mod_width), vectors], axis=1)
    pair = jnp.stack([mine, tensor_hop(mine, 1)])
    quad = jnp.concatenate([pair, tensor_hop(pair, 2)], axis=0)
    quad = jnp.take(quad, rank ^ jnp.arange(4, dtype=jnp.int32), axis=0)
    mods = quad[:, :, : SLOTS * mod_width].reshape(4, LAYERS, SLOTS, mod_width)
    mods = mods.transpose(1, 2, 0, 3).reshape(LAYERS, SLOTS, 4 * mod_width)
    rest = quad[:, :, SLOTS * mod_width :].transpose(1, 0, 2)
    biases = [
        rest[:, :, i * narrow : (i + 1) * narrow].reshape(LAYERS, 1, 4 * narrow) for i in range(4)
    ]
    up_biases = rest[:, :, 4 * narrow :].reshape(LAYERS, 1, 4 * units)
    out_biases = [
        b.reshape(LAYERS, 1, width) for b in (self_output_bias, cross_output_bias, hidden_down_bias)
    ]
    all_times = gather_dp(timesteps)

    def pack(members, after):
        rows = [sum(a.shape[1] for a in arrays) for _, arrays in members]
        outs = [shape(r // part, width, dtype=BF) for r in rows for part in (1, 2)]
        arrays = [a for _, some in members for a in some]
        return pl.pallas_call(
            partial(
                pack_kernel,
                groups=[(layer, [None] * len(some)) for layer, some in members],
                after=len(after),
            ),
            out_shape=outs,
            in_specs=[SMALL] + [ANY] * (len(arrays) + len(after)),
            out_specs=[ANY] * len(outs),
            scratch_shapes=[pltpu.SemaphoreType.DMA((6 * len(members),))],
            cost_estimate=lasting(1.0),
            name="pack_weights",
        )(info, *arrays, *after)

    kinds = (
        [turn(self_query), turn(self_key), turn(self_value), self_output],
        [turn(cross_query), turn(cross_key), turn(cross_value), cross_output],
        [hidden_up],
        [hidden_down],
    )
    all_groups = [(index // 4, kinds[index % 4]) for index in range(4 * LAYERS)]
    packed = [*pack(all_groups[:1], []), *pack(all_groups[1:], [mods])]
    firsts = [packed[2 * index + 1] for index in range(4 * LAYERS)]
    groups = [None] * (4 * LAYERS)
    along = [None] * (4 * LAYERS)

    def cross_x(index):
        along[index] = tensor_hop(firsts[index], 2)

    def spread(index):
        own, xa = packed[2 * index], along[index]
        ya = dp_hop(xa, 1)
        groups[index] = (own, tensor_hop(own, 1), xa, ya, tensor_hop(xa, 1), tensor_hop(ya, 1))

    opened = []

    def open_gate(after, arrived=(), leaving=()):
        nonlocal opened
        held_arrays = gate([along[i] for i in arrived] + [firsts[i] for i in leaving], after)
        for i, array in zip(arrived, held_arrays):
            along[i] = array
            spread(i)
        for i, array in zip(leaving, held_arrays[len(arrived) :]):
            firsts[i] = array
            cross_x(i)
        opened = list(held_arrays)

    for index in range(4):
        cross_x(index)
    spread(0)
    spread(1)
    opened = [along[1], *packed[2:]]

    text_rows = jnp.pad(text, ((0, 0), (0, LANES - words), (0, 0))).reshape(-1, width)
    whole = pltpu.VMEM((width, width), BF)
    four = pltpu.VMEM((4, width, units), BF)
    floats = pltpu.VMEM((share, width), F32)
    sems = lambda n: pltpu.SemaphoreType.DMA((n,))
    frame_low = shape(share, width, dtype=BF)
    frame_high = shape(share, width)
    frame_wide = shape(share, 4 * units, dtype=BF)
    two_low = shape(2, share, width, dtype=BF)
    two_text = shape(2, SLOTS * LANES, width, dtype=BF)
    logs = shape(16, share)
    log_work = pltpu.VMEM((share, LANES), F32)
    stat_shape = shape(24, width)

    x = lax.dynamic_slice_in_dim(tokens, core * share, share).astype(F32)
    kept = []
    for layer in range(LAYERS):
        small = lambda **named: dict(mod=mods[layer], **{k: v[layer] for k, v in named.items()})
        entry1, q, kv = run(
            qkv_kernel,
            "self_qkv",
            info,
            dict(x=x),
            small(q_bias=biases[0], v_bias=biases[1]),
            groups[4 * layer],
            dict(entry=frame_low, q=frame_low, kv=two_low),
            {},
            dict(wq=whole, wk=whole, wv=whole, sems=sems(12)),
            opened,
            3.0,
        )
        kv_sib = tensor_hop(kv, 1)
        opened = []
        if layer == 0:
            open_gate([entry1], [2], [4, 5])
        x1, mixed1, lse1, branch1 = run(
            self_kernel,
            "self_attention",
            info,
            dict(q=q, kv_own=kv, kv_sib=kv_sib, x=x),
            small(bias=out_biases[0]),
            groups[4 * layer],
            dict(out=frame_high, mixed=frame_low, lse=logs, branch=frame_low),
            {},
            dict(wo=whole, logs=log_work, sum=floats, sems=sems(4)),
            opened,
            8.0,
        )
        if layer == 0:
            open_gate([x1], [3], [6, 7])
        else:
            open_gate([x1], [6])
        x2, entry2, cq, ckv, mixed2, lse2, branch2 = run(
            partial(cross_kernel, words=words),
            "cross_attention",
            info,
            dict(x=x1, text=text_rows),
            small(q_bias=biases[2], v_bias=biases[3], bias=out_biases[1]),
            groups[4 * layer + 1],
            dict(
                out=frame_high,
                entry=frame_low,
                q=frame_low,
                kv=two_text,
                mixed=frame_low,
                lse=logs,
                branch=frame_low,
            ),
            {},
            dict(
                wq=whole, wk=whole, wv=whole, wo=whole, logs=log_work, sum=floats, sems=sems(16)
            ),
            opened,
            6.0,
        )
        open_gate([x2], [4] if layer == 0 else [7])
        x3, entry3, active, slope, branch3 = run(
            lambda info, work, w: hidden_kernel(info, work, w[:6], w[6:]),
            "feed_forward",
            info,
            dict(x=x2),
            small(up_bias=up_biases, bias=out_biases[2]),
            groups[4 * layer + 2] + groups[4 * layer + 3],
            dict(
                out=frame_high, entry=frame_low, active=frame_wide, slope=frame_wide, branch=frame_low
            ),
            {},
            dict(
                up=four,
                down=four,
                before0=floats,
                before1=floats,
                sum=floats,
                sems=sems(8),
                down_sems=sems(8),
            ),
            opened,
            7.0,
        )
        opened = []
        if layer == 0:
            open_gate([x3], [5])
        kept.append(
            dict(
                x=x,
                entry1=entry1,
                q=q,
                kv=kv,
                kv_sib=kv_sib,
                mixed1=mixed1,
                lse1=lse1,
                branch1=branch1,
                x1=x1,
                entry2=entry2,
                cq=cq,
                ckv=ckv,
                mixed2=mixed2,
                lse2=lse2,
                branch2=branch2,
                x2=x2,
                entry3=entry3,
                active=active,
                slope=slope,
                branch3=branch3,
            )
        )
        x = x3

    def join(rows):
        rows = rows.astype(BF)
        other = tensor_hop(rows, 1)
        return jnp.concatenate(
            [jnp.where(core == 0, rows, other), jnp.where(core == 0, other, rows)], axis=0
        )

    output = join(x)

    chains = {}

    def start(name, send, keep):
        view = (size, width // size, send.shape[1])
        chains[name] = (tensor_hop(send, 1).reshape(view), keep.reshape(view), 0)

    def held(*names):
        return [chains[name][1] for name in names]

    def advance(names, after=()):
        names = [n for n in names if 2 ** chains[n][2] < size]
        if not names:
            return
        ins, in_specs, outs, out_specs = [], [], [], []
        for name in names:
            received, kept_part, bit = chains[name]
            count, unit, columns = received.shape
            for side in range(2):

                def at(i, info, bit=bit, side=side):
                    return (0, ((info[8] >> bit) & 1) ^ side, 0, i)

                for part in (received, kept_part):
                    ins.append(part.reshape(count // 2, 2, unit, columns))
                    in_specs.append(pl.BlockSpec((count // 2, None, unit, columns // 2), at))
                outs.append(shape(count // 2, unit, columns, dtype=BF))
                out_specs.append(
                    pl.BlockSpec((count // 2, unit, columns // 2), lambda i, info: (0, 0, i))
                )
        results = pl.pallas_call(
            partial(merge_kernel, chains=len(names), after=len(after)),
            grid_spec=pltpu.PrefetchScalarGridSpec(
                num_scalar_prefetch=1,
                grid=(2,),
                in_specs=in_specs + [ANY] * len(after),
                out_specs=out_specs,
            ),
            out_shape=outs,
            compiler_params=pltpu.CompilerParams(vmem_limit_bytes=VMEM_BYTES),
            cost_estimate=lasting(1.5),
            name="merge_grads",
        )(info, *ins, *after)
        for index, name in enumerate(names):
            bit = chains[name][2]
            hold, give = results[2 * index : 2 * index + 2]
            chains[name] = (dp_hop(give, 2**bit), hold, bit + 1)

    def finish(name):
        received, kept_part, _ = chains[name]
        return (received.astype(F32) + kept_part.astype(F32)).reshape(width // size, -1)

    full = pl.BlockSpec((share, width), lambda i, info: (0, 0))

    def narrow_grads(members, after=()):
        lefts, which = [], []
        for left, _, _ in members:
            at = [i for i, seen in enumerate(lefts) if seen is left]
            if not at:
                lefts.append(left)
                at = [len(lefts) - 1]
            which.append(at[0])
        specs = []
        for _, right, first in members:
            if first is None:
                specs.append(pl.BlockSpec((share, 2 * narrow), lambda i, info: (0, info[6])))
            else:
                specs.append(
                    pl.BlockSpec(
                        (None, share, 2 * narrow), lambda i, info, first=first: (first, 0, info[6])
                    )
                )
        columns = len(members) * narrow
        result = pl.BlockSpec((width, columns), lambda i, info: (0, 0))
        return pl.pallas_call(
            partial(narrow_grad_kernel, lefts=tuple(which)),
            grid_spec=pltpu.PrefetchScalarGridSpec(
                num_scalar_prefetch=1,
                grid=(1,),
                in_specs=[full] * len(lefts) + specs + [ANY] * len(after),
                out_specs=[result] * 2,
            ),
            out_shape=[shape(width, columns, dtype=BF)] * 2,
            compiler_params=pltpu.CompilerParams(vmem_limit_bytes=VMEM_BYTES),
            cost_estimate=lasting(4.0),
            name="narrow_grads",
        )(info, *lefts, *[right for _, right, _ in members], *after)

    def wide_grads(entry, gb, d_before, active, after=()):
        sib = pl.BlockSpec((share, units), lambda i, info: (0, info[7]))
        own = pl.BlockSpec((share, units), lambda i, info: (0, info[5]))
        result = pl.BlockSpec((width, 2 * units), lambda i, info: (0, 0))
        return pl.pallas_call(
            wide_grad_kernel,
            grid_spec=pltpu.PrefetchScalarGridSpec(
                num_scalar_prefetch=1,
                grid=(1,),
                in_specs=[full, full, sib, own, sib, own] + [ANY] * len(after),
                out_specs=[result] * 2,
            ),
            out_shape=[shape(width, 2 * units, dtype=BF)] * 2,
            compiler_params=pltpu.CompilerParams(vmem_limit_bytes=VMEM_BYTES),
            cost_estimate=lasting(4.0),
            name="wide_grads",
        )(info, entry, gb, d_before, d_before, active, active, *after)

    g = lax.dynamic_slice_in_dim(cotangent, core * share, share)
    sums = [None] * LAYERS
    last = LAYERS - 1
    for layer in reversed(range(LAYERS)):
        s_group, c_group, u_group, d_group = groups[4 * layer : 4 * layer + 4]
        k = kept[layer]
        mod = dict(mod=mods[layer])
        older = [f"c{layer + 1}", f"s{layer + 1}"] if layer < last else []
        f_name, c_name, s_name = [f"{kind}{layer}" for kind in "fcs"]
        more = held(f"f{layer + 1}", *older) if older else [output]
        g, gb3, d_before, stats3 = run(
            lambda info, work, w: hidden_back_kernel(info, work, w[:6], w[6:]),
            "feed_forward_back",
            info,
            dict(g=g, branch=k["branch3"], slope=k["slope"], x=k["x2"]),
            mod,
            u_group + d_group,
            dict(out=frame_high, gb=frame_low, d_before=frame_wide),
            dict(stats=stat_shape),
            dict(
                up=four,
                down=four,
                before0=floats,
                before1=floats,
                de=floats,
                sems=sems(8),
                down_sems=sems(8),
            ),
            more,
            7.0,
        )
        start(f_name, *wide_grads(k["entry3"], gb3, d_before, k["active"]))
        if older:
            advance(older, held(f_name))
        g, gb2, dcq, dckv, stats2 = run(
            partial(cross_back_kernel, words=words),
            "cross_attention_back",
            info,
            dict(g=g, branch=k["branch2"], q=k["cq"], kv=k["ckv"], lse=k["lse2"], x=k["x1"]),
            mod,
            c_group,
            dict(out=frame_high, gb=frame_low, dq=frame_low, dkv=two_text),
            dict(stats=stat_shape),
            dict(
                wq=whole,
                wo=whole,
                d_mixed=pltpu.VMEM((share, width), BF),
                de=floats,
                dkv_sum=pltpu.VMEM(two_text.shape, F32),
                sems=sems(8),
            ),
            held(f_name, *older),
            7.0,
        )
        advance([f_name, *older], [g])
        cross_members = [
            (k["entry2"], dcq, None),
            (text_rows, dckv, 0),
            (text_rows, dckv, 1),
            (gb2, k["mixed2"], None),
        ]
        early_c = []
        if layer == 0:
            start(c_name, *narrow_grads(cross_members, held(f_name)))
            early_c = [c_name]
        gb1, dq, dkv_own, dkv_give, early = run(
            self_back_kernel,
            "self_attention_back",
            info,
            dict(
                g=g, branch=k["branch1"], q=k["q"], kv_own=k["kv"], kv_sib=k["kv_sib"], lse=k["lse1"]
            ),
            mod,
            s_group,
            dict(gb=frame_low, dq=frame_low, dkv_own=two_low, dkv_give=two_low),
            dict(stats=stat_shape),
            dict(wo=whole, d_mixed=pltpu.VMEM((share, width), BF), sems=sems(4)),
            held(f_name, *older, *early_c),
            13.0,
        )
        dkv_sib = tensor_hop(dkv_give, 1)
        advance([f_name, *older[1:], *early_c], [dq])
        if layer > 0:
            start(c_name, *narrow_grads(cross_members, held(f_name)))
        g, dkv, stats1 = run(
            qkv_back_kernel,
            "self_qkv_back",
            info,
            dict(dq=dq, dkv_own=dkv_own, dkv_sib=dkv_sib, x=k["x"], g=g),
            dict(mod, early=early),
            s_group,
            dict(out=frame_high, dkv=two_low),
            dict(stats=stat_shape),
            dict(wq=whole, wk=whole, wv=whole, de=floats, sems=sems(12)),
            held(f_name, *older, c_name),
            4.0,
        )
        self_members = [
            (k["entry1"], dq, None),
            (k["entry1"], dkv, 0),
            (k["entry1"], dkv, 1),
            (gb1, k["mixed1"], None),
        ]
        start(s_name, *narrow_grads(self_members))
        advance([f_name, c_name], held(s_name))
        stats = jnp.stack([stats1, stats2, stats3])
        sums[layer] = stats + tensor_hop(stats, 1)
    input_grad = join(g)
    previous = held("f0", "c0")
    while any(2 ** chain[2] < size for chain in chains.values()):
        advance(list(chains), previous)
        previous = held(*chains)

    vector_parts = []
    for layer in range(LAYERS):
        stats = sums[layer]
        rows = stats[:, :12].reshape(9, SLOTS, width).transpose(1, 0, 2).reshape(SLOTS, 9 * width)
        rows = lax.dynamic_slice_in_dim(rows, rank * mod_width, mod_width, 1)
        ways = stats[:2, 13:15].reshape(4, width)
        ways = lax.dynamic_slice_in_dim(ways, rank * narrow, narrow, 1)
        ups = lax.dynamic_index_in_dim(stats[2, 13:17], rank, 0, keepdims=False)
        vector_parts.append(
            jnp.concatenate([rows.reshape(-1), ways.reshape(-1), ups, stats[:, 12].reshape(-1)])
        )
    gathered = gather_dp(jnp.stack(vector_parts)[None])
    count = gathered.shape[0]
    mod_rows = gathered[:, :, : SLOTS * mod_width].reshape(count, LAYERS, SLOTS, mod_width)
    summed = jnp.sum(gathered[:, :, SLOTS * mod_width :], axis=0)
    conditions = jax.nn.silu(time_features(all_times, width)).astype(BF).astype(F32)
    part = width // count
    conditions = lax.dynamic_slice_in_dim(conditions, me * part, part, 1)
    modulation_grad = jnp.einsum(
        "nsd,nlsc->ldc",
        conditions.reshape(count, SLOTS, part),
        mod_rows,
        precision=lax.Precision.HIGHEST,
        preferred_element_type=F32,
    )
    modulation_bias_grad = jnp.sum(mod_rows, axis=(0, 2))
    q_sum, v_sum, cq_sum, cv_sum = [summed[:, i * narrow : (i + 1) * narrow] for i in range(4)]
    at = 4 * narrow
    up_sum = summed[:, at : at + units]
    at += units
    out_sums = [
        lax.dynamic_slice_in_dim(summed[:, at + i * width : at + (i + 1) * width], me * part, part, 1)
        for i in range(3)
    ]

    step = 2 * narrow
    done = {name: finish(name) for name in chains}
    pairs = {"s": [], "c": []}
    for layer in range(LAYERS):
        s_part = done[f"s{layer}"]
        c_part = done[f"c{layer}"]
        for name, values in (("s", s_part), ("c", c_part)):
            pairs[name].append((unpack(values[:, :step]), unpack(values[:, step : 2 * step])))
    stack = lambda name, i, j: jnp.stack([p[i][j] for p in pairs[name]])
    f_parts = jnp.stack([done[f"f{layer}"] for layer in range(LAYERS)])
    return (
        output,
        input_grad,
        stack("s", 0, 0),
        q_sum,
        stack("s", 0, 1),
        stack("s", 1, 0),
        v_sum,
        turn(stack("s", 1, 1)),
        out_sums[0],
        stack("c", 0, 0),
        cq_sum,
        stack("c", 0, 1),
        stack("c", 1, 0),
        cv_sum,
        turn(stack("c", 1, 1)),
        out_sums[1],
        f_parts[:, :, :units],
        up_sum,
        turn(f_parts[:, :, units:]),
        out_sums[2],
        modulation_grad,
        modulation_bias_grad,
    )


def solution(mesh):
    dp, tensor = "dp", "tensor"
    columns, vector = P(None, None, tensor), P(None, tensor)
    matrix, turned, spread = P(None, dp, tensor), P(None, tensor, dp), P(None, dp)
    placed = (
        P(dp, None),
        P(dp, None, None),
        P(dp),
        P(dp),
        P(dp, None),
        columns,
        vector,
        columns,
        columns,
        vector,
        P(None, tensor, None),
        P(),
        columns,
        vector,
        columns,
        columns,
        vector,
        P(None, tensor, None),
        P(),
        columns,
        vector,
        P(None, tensor, None),
        P(),
        columns,
        vector,
    )
    results = (
        P(dp, None),
        P(dp, None),
        matrix,
        vector,
        matrix,
        matrix,
        vector,
        turned,
        spread,
        matrix,
        vector,
        matrix,
        matrix,
        vector,
        turned,
        spread,
        matrix,
        vector,
        turned,
        spread,
        matrix,
        vector,
    )
    return jax.shard_map(
        shards, mesh=mesh, in_specs=placed, out_specs=results, check_vma=False
    )
```

```python
from functools import partial
import math

import jax
import jax.numpy as jnp
from jax import lax
from jax.experimental import pallas as pl
from jax.experimental.pallas import tpu as pltpu
from jax.sharding import PartitionSpec as P

HEAD_WIDTH = 64
UNIT = 256
LAYERS = 2
WINDOW = 1024
EPSILON = 1e-06
LANES = 128
SLOTS = WINDOW // UNIT
FAR = -1e30
VMEM_BYTES = 56 * 1024 * 1024
BF = jnp.bfloat16
F32 = jnp.float32
ROOT = math.sqrt(2.0 / math.pi)
CUBIC = 0.044715


def dot_nn(left, right):
    return jnp.dot(left, right, preferred_element_type=F32)


def dot_nt(left, right):
    return lax.dot_general(left, right, (((1,), (1,)), ((), ())), preferred_element_type=F32)


def dot_tn(left, right):
    return lax.dot_general(left, right, (((0,), (0,)), ((), ())), preferred_element_type=F32)


SMALL = pl.BlockSpec(memory_space=pltpu.SMEM)
NEAR = pl.BlockSpec(memory_space=pltpu.VMEM)
ANY = pl.BlockSpec(memory_space=pl.ANY)


class Work:
    def __init__(self, ins, outs, scratch, in_sems, out_sems):
        self.ins, self.outs, self.scratch, self.out_sems = ins, outs, scratch, out_sems
        self.copies, self.waited, self.flushed = {}, set(), []
        for index, (name, (ref, buffer)) in enumerate(ins.items()):
            self.copies[name] = pltpu.make_async_copy(ref, buffer, in_sems.at[index])
            self.copies[name].start()

    def __getattr__(self, name):
        if name in self.__dict__["ins"]:
            return self.ins[name][1]
        if name in self.__dict__["outs"]:
            return self.outs[name][1]
        return self.__dict__["scratch"][name]

    def has(self, name):
        return name in self.outs

    def need(self, *names):
        for name in names:
            if name not in self.waited:
                self.waited.add(name)
                self.copies[name].wait()

    def flush(self, name, *at):
        ref, buffer = self.outs[name]
        if at:
            ref, buffer = ref.at[at], buffer.at[at]
        copy = pltpu.make_async_copy(buffer, ref, self.out_sems.at[len(self.flushed)])
        copy.start()
        self.flushed.append(copy)

    def finish(self):
        self.need(*self.ins)
        for copy in self.flushed:
            copy.wait()


def run(body, name, info, ins, small, weights, outs, small_outs, scratch, after=(), cost=1.0):
    in_names, out_names, names = list(ins), list(outs), list(scratch)
    small_names, small_out_names = list(small), list(small_outs)
    counts = [1, len(in_names), len(small), len(weights), len(after), len(outs), len(small_outs)]

    def kernel(*refs):
        refs = list(refs)
        parts = []
        for count in counts:
            parts.append(refs[:count])
            refs = refs[count:]
        (info_ref,), in_refs, small_refs, weight_refs, _, out_refs, small_out_refs = parts
        in_bufs, refs = refs[: len(in_names)], refs[len(in_names) :]
        out_bufs, refs = refs[: len(out_names)], refs[len(out_names) :]
        rest, (in_sems, out_sems) = refs[:-2], refs[-2:]
        extra = {}
        rest = list(rest)
        for key in names:
            many = isinstance(scratch[key], list)
            size = len(scratch[key]) if many else 1
            extra[key] = rest[:size] if many else rest[0]
            rest = rest[size:]
        for key, ref in zip(small_names, small_refs):
            index = small[key][1]
            extra[key] = ref.at[index] if index else ref
        extra.update(zip(small_out_names, small_out_refs))
        work = Work(
            dict(zip(in_names, zip(in_refs, in_bufs))),
            dict(zip(out_names, zip(out_refs, out_bufs))),
            extra,
            in_sems,
            out_sems,
        )
        body(info_ref, work, weight_refs)
        work.finish()

    buffer = lambda a: pltpu.VMEM(a.shape, a.dtype)
    flat = []
    for value in scratch.values():
        flat += value if isinstance(value, list) else [value]
    results = pl.pallas_call(
        kernel,
        out_shape=[outs[n] for n in out_names] + [small_outs[n] for n in small_out_names],
        in_specs=[SMALL]
        + [ANY] * len(ins)
        + [NEAR] * len(small)
        + [ANY] * (len(weights) + len(after)),
        out_specs=[ANY] * len(outs) + [NEAR] * len(small_outs),
        scratch_shapes=[buffer(ins[n]) for n in in_names]
        + [buffer(outs[n]) for n in out_names]
        + flat
        + [pltpu.SemaphoreType.DMA((max(len(ins), 1),)), pltpu.SemaphoreType.DMA((32,))],
        compiler_params=pltpu.CompilerParams(vmem_limit_bytes=VMEM_BYTES),
        cost_estimate=lasting(cost),
        name=name,
    )(info, *ins.values(), *[array for array, _ in small.values()], *weights, *after)
    return results


def plain(body, name, info, ins, outs, scratch=()):
    results = pl.pallas_call(
        body,
        out_shape=outs,
        in_specs=([] if info is None else [SMALL]) + [NEAR] * len(ins),
        out_specs=[NEAR] * len(outs),
        scratch_shapes=list(scratch),
        compiler_params=pltpu.CompilerParams(vmem_limit_bytes=VMEM_BYTES),
        cost_estimate=lasting(1.0),
        name=name,
    )(*([] if info is None else [info]), *ins)
    return results if len(outs) > 1 else results[0]


def lasting(units):
    return pl.CostEstimate(flops=int(units * 0.4e9), bytes_accessed=1000, transcendentals=0)


def shape(*dims, dtype=F32):
    return jax.ShapeDtypeStruct(dims, dtype)


def start_rows(refs, place, plan, sems):
    own, sib, xa, ya, xb, yb = refs
    half = own.shape[0] // 2
    for rank in range(4):
        for parity in range(2):

            @pl.when(place == rank * 2 + parity)
            def _(rank=rank, parity=parity):
                for index, (shard, row, rows, dst) in enumerate(plan):
                    step = shard ^ rank
                    if step < 2:
                        src = (own, sib)[step].at[pl.ds(row, rows)]
                    else:
                        first, second = ((xa, ya), (xb, yb))[step - 2]
                        part = row // half
                        src = (first if part == parity else second).at[pl.ds(row - part * half, rows)]
                    pltpu.make_async_copy(src, dst, sems.at[index]).start()


def wait_rows(refs, plan, sems, which):
    for index in which:
        _, row, rows, dst = plan[index]
        pltpu.make_async_copy(refs[0].at[pl.ds(0, rows)], dst, sems.at[index]).wait()


def plan_of(buffers, first, rows):
    return [
        (shard, (first + which) * rows, rows, dst.at[pl.ds(shard * rows, rows)])
        for which, dst in enumerate(buffers)
        for shard in range(4)
    ]


def norm_rows(values):
    mean = jnp.mean(values, axis=-1, keepdims=True)
    center = values - mean
    factor = lax.rsqrt(jnp.mean(center * center, axis=-1, keepdims=True) + EPSILON)
    return center * factor, factor


def piece(mod, slot, index):
    width = mod.shape[1] // 9
    return mod[pl.ds(slot, 1), index * width : (index + 1) * width]


def each_rows(first, count, rows, step, carry=0, group=4):
    def turn(index, carry):
        for part in range(group):
            at = first + index * (rows * group) + part * rows
            carry = step(pl.ds(pl.multiple_of(at, rows), rows), carry)
        return carry

    return lax.fori_loop(0, count // (rows * group), turn, carry)


def entry_rows(x, mod, info, index, out):
    for block in range(x.shape[0] // UNIT):
        slot = info[1 + block]
        shift = piece(mod, slot, index)
        scale = 1.0 + piece(mod, slot, index + 1)

        def step(span, carry):
            normed, _ = norm_rows(x[span, :])
            out[span, :] = (normed * scale + shift).astype(BF)
            return carry

        each_rows(block * UNIT, UNIT, 16, step)


def residual_rows(x, mod, info, index, branch, bias, branch_out, out, low=None):
    for block in range(x.shape[0] // UNIT):
        gate = piece(mod, info[1 + block], index)

        def step(span, carry):
            values = branch[span, :] + bias
            branch_out[span, :] = values.astype(BF)
            result = x[span, :] + gate * values
            out[span, :] = result
            if low is not None:
                low[span, :] = result.astype(BF)
            return carry

        each_rows(block * UNIT, UNIT, 16, step)


def fold(values):
    return jnp.sum(values.reshape(values.shape[0] // 8, 8, values.shape[1]), axis=0)


def total(values):
    return jnp.sum(values, axis=0, keepdims=True)


def column_sum(ref):
    width = ref.shape[1]

    def step(span, carry):
        return carry + fold(ref[span, :].astype(F32))

    return total(each_rows(0, ref.shape[0], 16, step, jnp.zeros((8, width), F32)))


def gate_back(g, mod, info, index, branch, gb, stats):
    width = g.shape[1]
    zero = jnp.zeros((8, width), F32)
    sums = zero
    for block in range(g.shape[0] // UNIT):
        slot = info[1 + block]
        gate = piece(mod, slot, index)

        def step(span, carry):
            grad = g[span, :]
            low = (gate * grad).astype(BF)
            gb[span, :] = low
            return (
                carry[0] + fold(low.astype(F32)),
                carry[1] + fold(grad * branch[span, :].astype(F32)),
            )

        sums, rows_sum = each_rows(block * UNIT, UNIT, 16, step, (sums, zero), 2)
        stats[pl.ds(8 + slot, 1), :] += total(rows_sum)
    stats[12:13, :] = total(sums)


def norm_back_rows(x, g, de, mod, info, index, out, stats, low=None):
    width = x.shape[1]
    zero = jnp.zeros((8, width), F32)
    for block in range(x.shape[0] // UNIT):
        slot = info[1 + block]
        scale = 1.0 + piece(mod, slot, index + 1)

        def step(span, carry):
            normed, factor = norm_rows(x[span, :])
            grad = de[span, :]
            inner = grad * normed
            dn = grad * scale
            mean = jnp.mean(dn, axis=-1, keepdims=True)
            along = jnp.mean(dn * normed, axis=-1, keepdims=True)
            out[span, :] = g[span, :] + factor * (dn - mean - normed * along)
            return (carry[0] + fold(grad), carry[1] + fold(inner))

        shift_sum, scale_sum = each_rows(block * UNIT, UNIT, 8, step, (zero, zero), 8)
        stats[pl.ds(slot, 1), :] += total(shift_sum)
        stats[pl.ds(4 + slot, 1), :] += total(scale_sum)
    if low is not None:

        def lower(span, carry):
            low[span, :] = out[span, :].astype(BF)
            return carry

        each_rows(0, x.shape[0], 16, lower)


def lane_ids(rows):
    return lax.broadcasted_iota(jnp.int32, (rows, LANES), 1)


def head_half(values, half):
    ids = lane_ids(values.shape[0])
    keep = ids < HEAD_WIDTH if half == 0 else ids >= HEAD_WIDTH
    return jnp.where(keep, values.astype(F32), 0.0)


def query_marks(slot):
    return jnp.where(lane_ids(UNIT) == slot, 1.0, 0.0).astype(BF)


def key_marks(slots):
    ids = lane_ids(UNIT)
    parts = [jnp.where((ids < SLOTS) & (ids != slot), FAR, 0.0).astype(BF) for slot in slots]
    return jnp.concatenate(parts, axis=0)


def pair_lanes(pair):
    return pl.ds(pl.multiple_of(pair * LANES, LANES), LANES)


def with_bias(out, values, bias):
    for row in range(0, values.shape[0], 16):
        span = pl.ds(row, 16)
        out[span, :] = (values[span, :] + bias).astype(BF)


def qkv_kernel(info, work, weights):
    rows = weights[0].shape[0] // 4
    sems = work.sems
    plan = plan_of((work.wq, work.wk, work.wv), 0, rows)
    start_rows(weights, info[0], plan, sems)
    work.need("x")
    entry_rows(work.x, work.mod, info, 0, work.entry)
    work.flush("entry")
    wait_rows(weights, plan, sems, range(12))
    work.sum0[...] = dot_nt(work.entry[...], work.wq[...])
    work.sum1[...] = dot_nt(work.entry[...], work.wv[...])
    with_bias(work.q, work.sum0, work.q_bias[...])
    work.sum2[...] = dot_nt(work.entry[...], work.wk[...])
    with_bias(work.kv.at[1], work.sum1, work.v_bias[...])
    with_bias(work.kv.at[0], work.sum2, 0.0)
    work.flush("kv")
    work.flush("q")


def soft_pair(work, chains, keys, values, pair, words=None):
    ids = lane_ids(UNIT)
    count = 2 * len(chains)
    rows = 16 if words is None else 64

    def scores(index):
        span, marks, q_pair = chains[index // 2]
        left = (head_half(q_pair, index % 2) * HEAD_WIDTH**-0.5).astype(BF)
        if marks is not None:
            left = jnp.concatenate([left, marks], axis=1)
        work.scores[index % 2][...] = dot_nt(left, keys[index // 2])

    def soften(index):
        raw, low, peaks = work.scores[index % 2], work.probs[index % 2], work.peaks[index]
        for row in range(0, UNIT, rows):
            span = pl.ds(row, rows)
            part = raw[span, :]
            if words is not None:
                part = jnp.where(lane_ids(rows) < words, part, FAR)
            peak = jnp.max(part, axis=-1, keepdims=True)
            low[span, :] = jnp.exp(part - peak).astype(BF)
            peaks[span, :] = jnp.broadcast_to(peak, (rows, LANES))

    def mix(index):
        work.sums[index][...] = dot_nn(work.probs[index % 2][...], values[index // 2])

    def finish(block, lanes):
        first = chains[block][0]
        for row in range(0, UNIT, 32):
            span, at = pl.ds(row, 32), pl.ds(first + row, 32)
            kept = work.logs[at, :]
            parts = []
            for half in range(2):
                index = 2 * block + half
                sums = work.sums[index][span, LANES:]
                parts.append(work.sums[index][span, :LANES] / sums)
                kept = jnp.where(
                    lane_ids(32) == 2 * pair + half,
                    work.peaks[index][span, :] + jnp.log(sums),
                    kept,
                )
            work.logs[at, :] = kept
            work.mixed[at, lanes] = jnp.where(lane_ids(32) < HEAD_WIDTH, parts[0], parts[1]).astype(
                BF
            )

    lanes = pair_lanes(pair)
    scores(0)
    for index in range(count):
        if index + 1 < count:
            scores(index + 1)
        soften(index)
        mix(index)
        if index % 2:
            finish(index // 2, lanes)


def self_kernel(info, work, weights):
    rows = weights[0].shape[0] // 4
    sems = work.sems
    plan = [(s, 3 * rows, rows, work.wo.at[pl.ds(s * rows, rows)]) for s in range(4)]
    start_rows(weights, info[0], plan, sems)
    share = work.x.shape[0]
    blocks = share // UNIT
    work.marks[...] = key_marks([info[1 + b] for b in range(2 * blocks)])
    work.logs[...] = jnp.zeros(work.logs.shape, F32)
    work.need("q", "kv_own", "kv_sib")

    def both(which, lanes):
        return jnp.concatenate([work.kv_own[which, :, lanes], work.kv_sib[which, :, lanes]], axis=0)

    def step(pair, carry):
        lanes = pair_lanes(pair)
        keys = jnp.concatenate([both(0, lanes), work.marks[...]], axis=1)
        values = jnp.concatenate([both(1, lanes), jnp.ones((2 * share, LANES), BF)], axis=1)
        chains = [
            (b * UNIT, query_marks(info[1 + b]), work.q[pl.ds(b * UNIT, UNIT), lanes])
            for b in range(blocks)
        ]
        soft_pair(work, chains, [keys] * blocks, [values] * blocks, pair)
        return carry

    lax.fori_loop(0, work.mixed.shape[1] // LANES, step, 0)
    work.flush("mixed")
    work.lse[...] = work.logs[...].T[: work.lse.shape[0], :]
    work.flush("lse")
    wait_rows(weights, plan, sems, range(4))
    work.sum0[...] = dot_nn(work.mixed[...], work.wo[...])
    work.need("x")
    bias = work.bias[...].astype(F32)
    residual_rows(work.x, work.mod, info, 2, work.sum0, bias, work.branch, work.out)
    work.flush("branch")
    work.flush("out")


def cross_kernel(info, work, weights, words):
    rows = weights[0].shape[0] // 4
    sems = work.sems
    order = (1, 2, 0, 3)
    plan = [
        (shard, order[i // 4] * rows, count, dst)
        for i, (shard, _, count, dst) in enumerate(
            plan_of((work.wk, work.wv, work.wq, work.wo), 0, rows)
        )
    ]
    start_rows(weights, info[0], plan, sems)
    work.need("x")
    entry_rows(work.x, work.mod, info, 3, work.entry)
    work.flush("entry")
    work.need("text")
    wait_rows(weights, plan, sems, range(12))
    work.sum0[...] = dot_nt(work.text[...], work.wv[...])
    work.sum1[...] = dot_nt(work.entry[...], work.wq[...])
    with_bias(work.kv.at[1], work.sum0, work.v_bias[...])
    work.sum2[...] = dot_nt(work.text[...], work.wk[...])
    with_bias(work.q, work.sum1, work.q_bias[...])
    with_bias(work.kv.at[0], work.sum2, 0.0)
    work.flush("kv")
    work.flush("q")
    work.logs[...] = jnp.zeros(work.logs.shape, F32)
    blocks = work.x.shape[0] // UNIT

    def step(pair, carry):
        lanes = pair_lanes(pair)
        chains, keys, values = [], [], []
        for block in range(blocks):
            own = pl.ds(pl.multiple_of(info[1 + block] * LANES, LANES), LANES)
            chains.append((block * UNIT, None, work.q[pl.ds(block * UNIT, UNIT), lanes]))
            keys.append(work.kv[0, own, lanes])
            values.append(
                jnp.concatenate([work.kv[1, own, lanes], jnp.ones((LANES, LANES), BF)], axis=1)
            )
        soft_pair(work, chains, keys, values, pair, words)
        return carry

    lax.fori_loop(0, work.mixed.shape[1] // LANES, step, 0)
    work.flush("mixed")
    work.lse[...] = work.logs[...].T[: work.lse.shape[0], :]
    work.flush("lse")
    wait_rows(weights, plan, sems, range(12, 16))
    work.sum0[...] = dot_nn(work.mixed[...], work.wo[...])
    bias = work.bias[...].astype(F32)
    residual_rows(work.x, work.mod, info, 5, work.sum0, bias, work.branch, work.out)
    work.flush("branch")
    work.flush("out")


def halves_of(buffer):
    half = buffer.shape[1] // 2
    return [
        (shard, part * half, half, buffer.at[shard, pl.ds(part * half, half)])
        for shard in range(4)
        for part in range(2)
    ]


def hidden_kernel(info, work, ups, downs):
    sems = work.sems
    width = work.x.shape[1]
    up_plan = halves_of(work.up)
    down_plan = halves_of(work.down)
    start_rows(ups, info[0], up_plan, sems)
    start_rows(downs, info[0], down_plan, work.down_sems)
    work.need("x")
    entry_rows(work.x, work.mod, info, 6, work.entry)
    work.flush("entry")
    before = (work.before0, work.before1)

    def columns(shard):
        return pl.ds(shard * width, width)

    def rise(shard):
        wait_rows(ups, up_plan, sems, [2 * shard, 2 * shard + 1])
        before[shard % 2][...] = dot_nn(work.entry[...], work.up[shard])

    def bend(shard):
        half_width = width // 2
        for column in range(0, width, half_width):
            lanes = pl.ds(shard * width + column, half_width)
            bias = work.up_bias[:, lanes]
            for row in range(0, work.x.shape[0], 16):
                span = pl.ds(row, 16)
                values = before[shard % 2][span, pl.ds(column, half_width)] + bias
                square = values * values
                half = 1.0 / (1.0 + jnp.exp(values * (-2.0 * ROOT - (2.0 * ROOT * CUBIC) * square)))
                act = values * half
                work.active[span, lanes] = act.astype(BF)
                work.slope[span, lanes] = (
                    half + act * (1.0 - half) * (2.0 * ROOT + (6.0 * ROOT * CUBIC) * square)
                ).astype(BF)
        work.flush("active", slice(None), columns(shard))
        work.flush("slope", slice(None), columns(shard))

    def fall(shard):
        wait_rows(downs, down_plan, work.down_sems, [2 * shard, 2 * shard + 1])
        part = dot_nn(work.active[:, columns(shard)], work.down[shard])
        work.sum0[...] = part if shard == 0 else work.sum0[...] + part

    rise(0)
    for shard in range(4):
        if shard < 3:
            rise(shard + 1)
        bend(shard)
        fall(shard)
    bias = work.bias[...].astype(F32)
    low = work.low if work.has("low") else None
    residual_rows(work.x, work.mod, info, 8, work.sum0, bias, work.branch, work.out, low)
    work.flush("branch")
    work.flush("out")
    if low is not None:
        work.flush("low")


def hidden_back_kernel(info, work, ups, downs):
    sems = work.sems
    width = work.x.shape[1]
    up_plan = halves_of(work.up)
    down_plan = halves_of(work.down)
    start_rows(downs, info[0], down_plan, work.down_sems)
    start_rows(ups, info[0], up_plan, sems)
    work.stats[...] = jnp.zeros(work.stats.shape, F32)
    stats = work.stats.at[pl.ds(48, 24)]
    work.need("g", "branch")
    gate_back(work.g, work.mod, info, 8, work.branch, work.gb, stats)
    work.flush("gb")
    before = (work.before0, work.before1)
    work.need("slope")

    def columns(shard):
        return pl.ds(shard * width, width)

    def rise(shard):
        wait_rows(downs, down_plan, work.down_sems, [2 * shard, 2 * shard + 1])
        before[shard % 2][...] = dot_nt(work.gb[...], work.down[shard])

    def bend(shard):
        sums = jnp.zeros((8, width), F32)
        for row in range(0, work.x.shape[0], 16):
            span = pl.ds(row, 16)
            low = before[shard % 2][span, :] * work.slope[span, columns(shard)].astype(F32)
            low = low.astype(BF)
            work.d_before[span, columns(shard)] = low
            sums += fold(low.astype(F32))
        stats[13 + shard : 14 + shard, :] = total(sums)
        work.flush("d_before", slice(None), columns(shard))

    def fall(shard):
        wait_rows(ups, up_plan, sems, [2 * shard, 2 * shard + 1])
        part = dot_nt(work.d_before[:, columns(shard)], work.up[shard])
        work.de[...] = part if shard == 0 else work.de[...] + part

    rise(0)
    for shard in range(4):
        if shard < 3:
            rise(shard + 1)
        bend(shard)
        fall(shard)
    work.need("x")
    norm_back_rows(work.x, work.g, work.de, work.mod, info, 6, work.out, stats)
    work.flush("out")


def cross_back_kernel(info, work, weights, words):
    rows = weights[0].shape[0] // 4
    sems = work.sems
    plan = [
        (shard, (3 * rows, 0)[i // 4], count, dst)
        for i, (shard, _, count, dst) in enumerate(plan_of((work.wo, work.wq), 0, rows))
    ]
    start_rows(weights, info[0], plan, sems)
    work.stats[...] = work.early[...]
    stats = work.stats.at[pl.ds(24, 24)]
    work.need("g", "branch")
    gate_back(work.g, work.mod, info, 5, work.branch, work.gb, stats)
    work.flush("gb")
    wait_rows(weights, plan, sems, range(0, 4))
    work.de[...] = dot_nt(work.gb[...], work.wo[...])
    with_bias(work.d_mixed, work.de, 0.0)
    work.dkv_sum[...] = jnp.zeros(work.dkv_sum.shape, F32)
    work.need("q", "kv", "lse")

    def step(pair, carry):
        lanes = pair_lanes(pair)
        real = lax.broadcasted_iota(jnp.int32, (LANES, UNIT), 0) < words
        for block in range(work.q.shape[0] // UNIT):
            span = pl.ds(block * UNIT, UNIT)
            own = pl.ds(pl.multiple_of(info[1 + block] * LANES, LANES), LANES)
            q_pair = work.q[span, lanes]
            d_pair = work.d_mixed[span, lanes]
            keys = work.kv[0, own, lanes]
            values = work.kv[1, own, lanes]
            lefts, grads, turned, probs_low, scores_low = [], [], [], [], []
            for half in range(2):
                left = (head_half(q_pair, half) * HEAD_WIDTH**-0.5).astype(BF)
                grad = head_half(d_pair, half).astype(BF)
                logs = work.lse[pl.ds(2 * pair + half, 1), span]
                probs = jnp.where(real, jnp.exp(dot_nt(keys, left) - logs), 0.0)
                d_probs = dot_nt(values, grad)
                inner = jnp.sum(probs * d_probs, axis=0, keepdims=True)
                lefts.append(left)
                grads.append(grad)
                turned.append(head_half(keys, half).T.astype(BF))
                probs_low.append(probs.astype(BF))
                scores_low.append((probs * (d_probs - inner)).astype(BF))
            wide_scores = jnp.concatenate(scores_low, axis=1)
            grad_v = dot_nn(jnp.concatenate(probs_low, axis=1), jnp.concatenate(grads, axis=0))
            grad_k = dot_nn(wide_scores, jnp.concatenate(lefts, axis=0))
            grad_q = dot_nn(
                jnp.concatenate(turned, axis=1), jnp.concatenate(scores_low, axis=0)
            )
            work.dq[span, lanes] = (grad_q.T * HEAD_WIDTH**-0.5).astype(BF)
            work.dkv_sum[0, own, lanes] += grad_k
            work.dkv_sum[1, own, lanes] += grad_v
        return carry

    lax.fori_loop(0, work.q.shape[1] // LANES, step, 0, unroll=2)
    work.flush("dq")
    with_bias(work.dkv.at[0], work.dkv_sum.at[0], 0.0)
    with_bias(work.dkv.at[1], work.dkv_sum.at[1], 0.0)
    work.flush("dkv")
    wait_rows(weights, plan, sems, range(4, 8))
    work.de[...] = dot_nn(work.dq[...], work.wq[...])
    stats[13:14, :] = column_sum(work.dq)
    stats[14:15, :] = column_sum(work.dkv.at[1])
    work.need("x")
    norm_back_rows(work.x, work.g, work.de, work.mod, info, 3, work.out, stats)
    work.flush("out")


def self_back_kernel(info, work, weights):
    rows = weights[0].shape[0] // 4
    sems = work.sems
    plan = [(s, 3 * rows, rows, work.wo.at[pl.ds(s * rows, rows)]) for s in range(4)]
    start_rows(weights, info[0], plan, sems)
    work.stats[...] = work.early[...]
    stats = work.stats.at[pl.ds(0, 24)]
    work.need("g", "branch")
    gate_back(work.g, work.mod, info, 2, work.branch, work.gb, stats)
    work.flush("gb")
    share = work.g.shape[0]
    blocks = share // UNIT
    work.marks[...] = key_marks([info[1 + b] for b in range(2 * blocks)])
    wait_rows(weights, plan, sems, range(4))
    work.sum0[...] = dot_nt(work.gb[...], work.wo[...])
    with_bias(work.d_mixed, work.sum0, 0.0)
    work.need("q", "kv_own", "kv_sib", "lse")
    count = 2 * blocks

    def both(which, lanes):
        return jnp.concatenate([work.kv_own[which, :, lanes], work.kv_sib[which, :, lanes]], axis=0)

    def step(pair, carry):
        lanes = pair_lanes(pair)
        keys = both(0, lanes)
        values = both(1, lanes)
        marked = jnp.concatenate([keys, work.marks[...]], axis=1)
        turned = [head_half(keys, half).T.astype(BF) for half in range(2)]

        def raise_scores(index):
            block, half = index // 2, index % 2
            span, own = pl.ds(block * UNIT, UNIT), pl.ds(index * UNIT, UNIT)
            left = (head_half(work.q[span, lanes], half) * HEAD_WIDTH**-0.5).astype(BF)
            grad = head_half(work.d_mixed[span, lanes], half).astype(BF)
            work.lefts[own, :] = left
            work.grads[own, :] = grad
            query = jnp.concatenate([left, query_marks(info[1 + block])], axis=1)
            work.scores[index % 2][...] = dot_nt(marked, query)
            work.rises[index % 2][...] = dot_nt(values, grad)

        def soften(index):
            block, half = index // 2, index % 2
            own = pl.ds(index * UNIT, UNIT)
            logs = work.lse[pl.ds(2 * pair + half, 1), pl.ds(block * UNIT, UNIT)]
            scores, rises = work.scores[index % 2], work.rises[index % 2]
            inner = jnp.zeros((8, UNIT), F32)
            for row in range(0, 2 * share, 32):
                span = pl.ds(row, 32)
                probs = jnp.exp(scores[span, :] - logs)
                inner += fold(probs * rises[span, :])
                work.probs[span, own] = probs.astype(BF)
            inner = total(inner)
            for row in range(0, 2 * share, 32):
                span = pl.ds(row, 32)
                work.d_scores[span, own] = (
                    work.probs[span, own].astype(F32) * (rises[span, :] - inner)
                ).astype(BF)

        raise_scores(0)
        for index in range(count):
            if index + 1 < count:
                raise_scores(index + 1)
            soften(index)
            if index % 2:
                block = index // 2
                grad_q = sum(
                    dot_nn(turned[half], work.d_scores[:, pl.ds((2 * block + half) * UNIT, UNIT)])
                    for half in range(2)
                )
                work.dq[pl.ds(block * UNIT, UNIT), lanes] = (
                    grad_q.T * HEAD_WIDTH**-0.5
                ).astype(BF)
        for which, left, right in ((0, work.d_scores, work.lefts), (1, work.probs, work.grads)):
            grad = dot_nn(left[...], right[...]).astype(BF)
            work.dkv_own[which, :, lanes] = grad[:share]
            work.dkv_give[which, :, lanes] = grad[share:]
        return carry

    lax.fori_loop(0, work.q.shape[1] // LANES, step, 0)
    work.flush("dkv_give")
    work.flush("dkv_own")
    work.flush("dq")


def qkv_back_kernel(info, work, weights):
    rows = weights[0].shape[0] // 4
    sems = work.sems
    plan = plan_of((work.wq, work.wk, work.wv), 0, rows)
    start_rows(weights, info[0], plan, sems)
    work.stats[...] = work.early[...]
    stats = work.stats.at[pl.ds(0, 24)]
    work.need("dkv_own", "dkv_sib", "dq")
    for which in range(2):
        for row in range(0, work.x.shape[0], 16):
            span = pl.ds(row, 16)
            work.dkv[which, span, :] = (
                work.dkv_own[which, span, :].astype(F32) + work.dkv_sib[which, span, :].astype(F32)
            ).astype(BF)
    work.flush("dkv")
    wait_rows(weights, plan, sems, range(0, 12))
    work.de[...] = (
        dot_nn(work.dq[...], work.wq[...])
        + dot_nn(work.dkv[0], work.wk[...])
        + dot_nn(work.dkv[1], work.wv[...])
    )
    stats[13:14, :] = column_sum(work.dq)
    stats[14:15, :] = column_sum(work.dkv.at[1])
    work.need("x", "g")
    low = work.low if work.has("low") else None
    norm_back_rows(work.x, work.g, work.de, work.mod, info, 0, work.out, stats, low)
    work.flush("out")
    if low is not None:
        work.flush("low")


def wide_grad_kernel(info, entry, gb, db_sib, db_own, act_sib, act_own, *refs):
    send, keep = refs[-2:]
    width = entry.shape[1]
    left, right = entry[...].T, gb[...].T
    for out, db, act in ((send, db_sib, act_sib), (keep, db_own, act_own)):
        for column in range(0, width, 256):
            lanes = pl.ds(column, 256)
            out[:, lanes] = dot_nn(left, db[:, lanes]).astype(BF)
            out[:, pl.ds(width + column, 256)] = dot_nn(right, act[:, lanes]).astype(BF)


def narrow_grad_kernel(info, *refs, lefts):
    count = max(lefts) + 1
    left_refs, rights = refs[:count], refs[count : count + len(lefts)]
    send, keep, products = refs[-3:]
    turned = [ref[...].T for ref in left_refs]
    step = 3 * LANES
    for at in range(len(lefts)):
        products[at] = dot_nn(turned[lefts[at]], rights[at][...])
    low = lane_ids(16) < HEAD_WIDTH
    for at in range(len(lefts) // 2):
        for core in range(2):

            @pl.when(info[5] % 2 == core)
            def _(core=core, at=at):
                outs = (keep, send) if core == 0 else (send, keep)

                def spread(span, carry):
                    (a0, a1, a2), (b0, b1, b2) = [
                        [products[2 * at + i, span, pl.ds(j * LANES, LANES)] for j in range(3)]
                        for i in range(2)
                    ]
                    a1r, b1r = pltpu.roll(a1, HEAD_WIDTH, 1), pltpu.roll(b1, HEAD_WIDTH, 1)
                    a2r, b2r = pltpu.roll(a2, HEAD_WIDTH, 1), pltpu.roll(b2, HEAD_WIDTH, 1)
                    even = (a0, b0, jnp.where(low, a1, b1r))
                    odd = (jnp.where(low, a1r, a2r), jnp.where(low, b1r, b2r), jnp.where(low, a2r, b2))
                    for out, parts in zip(outs, (even, odd)):
                        for i, part in enumerate(parts):
                            out[span, pl.ds(at * step + i * LANES, LANES)] = part.astype(BF)
                    return carry

                each_rows(0, products.shape[1], 16, spread)


def merge_kernel(info, *refs, chains, after):
    ins, outs = refs[: 4 * chains], refs[4 * chains + after :]
    for chain in range(chains):
        for side in range(2):
            received, kept = ins[4 * chain + 2 * side], ins[4 * chain + 2 * side + 1]
            out = outs[2 * chain + side]
            count, unit, _ = out.shape
            rows = 16 if unit % 16 == 0 else unit
            for index in range(count):
                for row in range(0, unit, rows):
                    span = pl.ds(row, rows)
                    out[index, span, :] = (
                        received[index, span, :].astype(F32) + kept[index, span, :].astype(F32)
                    ).astype(BF)


def gate(arrays, after):
    count = len(arrays)
    return pl.pallas_call(
        lambda *refs: None,
        out_shape=[shape(*a.shape, dtype=a.dtype) for a in arrays],
        in_specs=[ANY] * (count + len(after)),
        out_specs=[ANY] * count,
        input_output_aliases={i: i for i in range(count)},
        cost_estimate=lasting(0.5),
        name="gate",
    )(*arrays, *after)


def pack_kernel(info, *refs, groups, after):
    count = sum(len(members) for _, members in groups)
    sources, rest = refs[:count], refs[count + after :]
    outs, (held, in_sems, out_sems) = rest[:-3], rest[-3:]
    spots = []
    at = 0
    for index, (layer, members) in enumerate(groups):
        rows = held.shape[1]
        piece_rows = rows // 4
        for quarter in range(4):
            row = quarter * piece_rows
            source = sources[at + quarter * len(members) // 4]
            src = source.at[layer, pl.ds(row % source.shape[1], piece_rows)]
            spots.append((index, quarter, held.at[index, pl.ds(row, piece_rows)], src))
        at += len(members)

    def arriving(place):
        _, _, spot, src = spots[place]
        return pltpu.make_async_copy(src, spot, in_sems.at[place])

    def leaving(index, which):
        out = outs[2 * index + (0 if which == 2 else 1)]
        rows = out.shape[0]
        src = held.at[index] if which == 2 else held.at[index, pl.ds(which * rows, rows)]
        return pltpu.make_async_copy(src, out, out_sems.at[2 * index + (0 if which == 2 else 1)])

    def by_parity(act):
        for parity in range(2):

            @pl.when(info[0] % 2 == parity)
            def _(parity=parity):
                act(parity)

    for place in range(len(spots)):
        arriving(place).start()
    for index in range(len(groups)):
        for quarter in range(4):
            arriving(4 * index + quarter).wait()
        by_parity(lambda parity: leaving(index, parity).start())
        leaving(index, 2).start()
    for index in range(len(groups)):
        by_parity(lambda parity: leaving(index, parity).wait())
        leaving(index, 2).wait()


def mod_kernel(condition, mod, mod_bias, q, v, cq, cv, up, out):
    narrow, units, columns = q.shape[1], up.shape[1], mod.shape[1]
    out[...] = jnp.zeros(out.shape, F32)
    for layer in range(LAYERS):
        row = pl.ds(layer, 1)
        out[layer, 0:SLOTS, 0:columns] = dot_nt(condition[...], mod[layer]) + mod_bias[
            row, :
        ].astype(F32)
        out[layer, 4:5, 0:units] = up[row, :].astype(F32)
        out[layer, 5:6, 0:narrow] = q[row, :].astype(F32)
        out[layer, 6:7, 0:narrow] = v[row, :].astype(F32)
        out[layer, 7:8, 0:narrow] = cq[row, :].astype(F32)
        out[layer, 4:5, 1024 : 1024 + narrow] = cv[row, :].astype(F32)


def assemble_kernel(info, *refs, narrow, units, columns):
    parts, (mods, narrows, ups) = refs[:4], refs[4:]
    for rank in range(4):

        @pl.when(info[5] == rank)
        def _(rank=rank):
            for shard in range(4):
                part = parts[shard ^ rank]
                for layer in range(LAYERS):
                    mods[layer, :, shard * columns : (shard + 1) * columns] = part[
                        layer, 0:SLOTS, 0:columns
                    ]
                    ups[layer, :, shard * units : (shard + 1) * units] = part[layer, 4:5, 0:units]
                    at = slice(shard * narrow, (shard + 1) * narrow)
                    for row in range(3):
                        narrows[layer, row : row + 1, at] = part[layer, 5 + row : 6 + row, 0:narrow]
                    narrows[layer, 3:4, at] = part[layer, 4:5, 1024 : 1024 + narrow]


def collect_kernel(info, *refs, narrow, units, columns):
    stats, condition, out = refs[: 2 * LAYERS], refs[2 * LAYERS], refs[2 * LAYERS + 1]
    sums = refs[2 * LAYERS + 2]
    width = stats[0].shape[1]
    out[...] = jnp.zeros(out.shape, F32)
    for layer in range(LAYERS):
        sums[...] = stats[2 * layer][...] + stats[2 * layer + 1][...]
        base = 8 * layer
        out[base + 4 : base + 5, width : 2 * width] = sums[60:61, :]
        out[base + 5 : base + 6, 0:width] = sums[12:13, :]
        out[base + 5 : base + 6, width : 2 * width] = sums[36:37, :]
        for index in range(2):
            out[base + 6 + index : base + 7 + index, 512 : 512 + width] = condition[
                2 * layer + index : 2 * layer + index + 1, :
            ].astype(F32)
        for rank in range(4):

            @pl.when(info[5] == rank)
            def _(rank=rank, base=base):
                first = rank * columns
                for index in range(9):
                    low = max(first, index * width)
                    high = min(first + columns, (index + 1) * width)
                    if low < high:
                        row = (index // 3) * 24 + (index % 3) * 4
                        out[base : base + 4, low - first : high - first] = sums[
                            row : row + 4, low - index * width : high - index * width
                        ]
                out[base + 4 : base + 5, 0:units] = sums[61 + rank : 62 + rank, :]
                own = slice(rank * narrow, (rank + 1) * narrow)
                out[base + 6 : base + 7, 0:narrow] = sums[13:14, own]
                out[base + 6 : base + 7, 256 : 256 + narrow] = sums[14:15, own]
                out[base + 7 : base + 8, 0:narrow] = sums[37:38, own]
                out[base + 7 : base + 8, 256 : 256 + narrow] = sums[38:39, own]


def spread_kernel(info, gathered, grad, bias_grad, q, v, cq, cv, up, o1, o2, o3, rows, conditions):
    count = gathered.shape[0]
    columns, part = grad.shape[2], grad.shape[1]
    width, narrow, units = conditions.shape[1], q.shape[1], up.shape[1]
    shift = lax.rem(width - info[8] * part, width)
    for index in range(count):
        for slot in range(SLOTS):
            row = 8 * (slot // 2) + 6 + slot % 2
            conditions[SLOTS * index + slot : SLOTS * index + slot + 1, :] = gathered[
                index, row : row + 1, 512 : 512 + width
            ]
    turned = pltpu.roll(conditions[...], shift, 1)[:, :part].T
    for layer in range(LAYERS):
        base = 8 * layer
        sums = jnp.zeros((8, gathered.shape[2]), F32)
        for index in range(count):
            values = gathered[index, base : base + 8, :]
            sums += values
            rows[SLOTS * index : SLOTS * (index + 1), :] = values[0:SLOTS, 0:columns]
        grad[layer] = jnp.dot(
            turned, rows[...], precision=lax.Precision.HIGHEST, preferred_element_type=F32
        )
        at = slice(layer, layer + 1)
        bias_grad[at, :] = jnp.sum(sums[0:SLOTS, 0:columns], axis=0, keepdims=True)
        up[at, :] = sums[4:5, 0:units]
        q[at, :] = sums[6:7, 0:narrow]
        v[at, :] = sums[6:7, 256 : 256 + narrow]
        cq[at, :] = sums[7:8, 0:narrow]
        cv[at, :] = sums[7:8, 256 : 256 + narrow]
        for out, row, lane in ((o1, 5, 0), (o2, 5, width), (o3, 4, width)):
            own = jnp.broadcast_to(sums[row : row + 1, lane : lane + width], (8, width))
            out[at, :] = pltpu.roll(own, shift, 1)[0:1, :part]


def narrow_finish_kernel(*refs, spots):
    parts, outs = refs[: 2 * len(spots)], refs[2 * len(spots) :]
    step = 3 * LANES
    for chain, places in enumerate(spots):
        values = parts[2 * chain][0].astype(F32) + parts[2 * chain + 1][0].astype(F32)
        for at, (layer, pair) in enumerate(places):
            both = values[:, at * step : (at + 1) * step]
            first = jnp.concatenate(
                [both[:, :LANES], both[:, 2 * LANES : 2 * LANES + HEAD_WIDTH]], axis=1
            )
            second = jnp.concatenate(
                [both[:, LANES : 2 * LANES], both[:, 2 * LANES + HEAD_WIDTH :]], axis=1
            )
            for out, matrix in zip(outs[2 * pair : 2 * pair + 2], (first, second)):
                out[layer] = matrix if out.shape[1:] == matrix.shape else matrix.T


def wide_finish_kernel(*refs):
    parts, (up, down) = refs[: 2 * LAYERS], refs[2 * LAYERS :]
    width = up.shape[2]
    for layer in range(LAYERS):
        values = parts[2 * layer][0].astype(F32) + parts[2 * layer + 1][0].astype(F32)
        up[layer] = values[:, :width]
        down[layer] = values[:, width:]


def join_kernel(info, rows, other, out):
    share = rows.shape[0]
    for core in range(2):

        @pl.when(info[5] % 2 == core)
        def _(core=core):
            out[pl.ds(core * share, share), :] = rows[...]
            out[pl.ds((1 - core) * share, share), :] = other[...]


def tensor_hop(values, step):
    return lax.ppermute(values, "tensor", [(i, i ^ step) for i in range(4)])


def dp_hop(values, step):
    size = lax.axis_size("dp")
    return lax.ppermute(values, "dp", [(i, i ^ step) for i in range(size)])


def time_features(moments, width):
    half = width // 2
    rates = jnp.exp(-math.log(10000.0) * jnp.arange(half, dtype=F32) / half)
    angles = moments.astype(F32)[:, None] * rates[None, :]
    return jnp.concatenate([jnp.cos(angles), jnp.sin(angles)], axis=1)


def shards(
    tokens,
    text,
    timesteps,
    item_frames,
    cotangent,
    self_query,
    self_query_bias,
    self_key,
    self_value,
    self_value_bias,
    self_output,
    self_output_bias,
    cross_query,
    cross_query_bias,
    cross_key,
    cross_value,
    cross_value_bias,
    cross_output,
    cross_output_bias,
    hidden_up,
    hidden_up_bias,
    hidden_down,
    hidden_down_bias,
    modulation,
    modulation_bias,
):
    frames, width = tokens.shape
    words = text.shape[1]
    columns = modulation.shape[2]
    narrow = self_query.shape[2]
    units = hidden_up.shape[2]
    rank = lax.axis_index("tensor")
    me = lax.axis_index("dp")
    size = lax.axis_size("dp")
    core = rank % 2
    share = frames // 2
    blocks = share // UNIT
    unit = width // size
    turn = lambda values: jnp.swapaxes(values, 1, 2)

    order = jnp.arange(SLOTS, dtype=jnp.int32)
    ends = jnp.sum(jnp.where(order[:, None] <= order[None, :], item_frames[:, None], 0), axis=0)
    turned = (jnp.arange(frames // UNIT, dtype=jnp.int32) + core * blocks) % (2 * blocks)
    slots = jnp.sum((turned[:, None] * UNIT >= ends[None, :]).astype(jnp.int32), axis=1)
    places = jnp.stack([rank, rank // 2, rank ^ 1, me]).astype(jnp.int32)
    info = jnp.concatenate([(rank * 2 + me % 2)[None].astype(jnp.int32), slots, places])

    condition = jax.nn.silu(time_features(timesteps, width)).astype(BF)
    mine = plain(
        mod_kernel,
        "modulation_rows",
        None,
        [
            condition,
            turn(modulation),
            modulation_bias,
            self_query_bias,
            self_value_bias,
            cross_query_bias,
            cross_value_bias,
            hidden_up_bias,
        ],
        [shape(LAYERS, 8, -(-columns // LANES) * LANES)],
    )
    others = [tensor_hop(mine, 1), tensor_hop(mine, 2)]
    others.append(tensor_hop(others[0], 2))
    mods, narrow_biases, up_biases = plain(
        partial(assemble_kernel, narrow=narrow, units=units, columns=columns),
        "modulation_of_all",
        info,
        [mine, *others],
        [
            shape(LAYERS, SLOTS, 4 * columns),
            shape(LAYERS, 8, 4 * narrow),
            shape(LAYERS, 1, 4 * units),
        ],
    )
    out_biases = [
        b.reshape(LAYERS, 1, width) for b in (self_output_bias, cross_output_bias, hidden_down_bias)
    ]

    def pack(members, after):
        outs = [shape(width // part, width, dtype=BF) for _ in members for part in (1, 2)]
        arrays = [a for _, some in members for a in some]
        return pl.pallas_call(
            partial(
                pack_kernel,
                groups=[(layer, [None] * len(some)) for layer, some in members],
                after=len(after),
            ),
            out_shape=outs,
            in_specs=[SMALL] + [ANY] * (len(arrays) + len(after)),
            out_specs=[ANY] * len(outs),
            scratch_shapes=[
                pltpu.VMEM((len(members), width, width), BF),
                pltpu.SemaphoreType.DMA((4 * len(members),)),
                pltpu.SemaphoreType.DMA((2 * len(members),)),
            ],
            compiler_params=pltpu.CompilerParams(vmem_limit_bytes=VMEM_BYTES),
            cost_estimate=lasting(1.0),
            name="pack_weights",
        )(info, *arrays, *after)

    kinds = (
        [turn(self_query), turn(self_key), turn(self_value), self_output],
        [turn(cross_query), turn(cross_key), turn(cross_value), cross_output],
        [hidden_up],
        [hidden_down],
    )
    all_groups = [(index // 4, kinds[index % 4]) for index in range(4 * LAYERS)]
    packed = [*pack(all_groups[:1], []), *pack(all_groups[1:], [mods])]
    firsts = [packed[2 * index + 1] for index in range(4 * LAYERS)]
    owns = [packed[2 * index] for index in range(4 * LAYERS)]
    along_x, along_y, over_x, over_y, sibs = [[None] * (4 * LAYERS) for _ in range(5)]

    def leave(index):
        along_x[index] = tensor_hop(firsts[index], 2)
        sibs[index] = tensor_hop(owns[index], 1)

    def go_on(index):
        along_y[index] = dp_hop(along_x[index], 1)
        over_x[index] = tensor_hop(along_x[index], 1)

    def end(index):
        over_y[index] = tensor_hop(along_y[index], 1)

    def weights_of(index):
        return [
            owns[index],
            sibs[index],
            along_x[index],
            along_y[index],
            over_x[index],
            over_y[index],
        ]

    def open_gate(after, leaving=(), at_x=(), at_y=()):
        places = [(firsts, i) for i in leaving]
        places += [(along_x, i) for i in at_x] + [(along_y, i) for i in at_y]
        opened = gate([values[i] for values, i in places], after)
        for (values, i), array in zip(places, opened):
            values[i] = array
        for i in leaving:
            leave(i)
        for i in at_x:
            go_on(i)
        for i in at_y:
            end(i)
        return list(opened)

    for index in range(4):
        leave(index)
    for index in range(3):
        go_on(index)
    end(0)

    text_rows = jnp.pad(text, ((0, 0), (0, LANES - words), (0, 0))).reshape(-1, width)
    whole = pltpu.VMEM((width, width), BF)
    four = pltpu.VMEM((4, width, units), BF)
    floats = pltpu.VMEM((share, width), F32)
    lows = pltpu.VMEM((share, width), BF)
    sems = lambda n: pltpu.SemaphoreType.DMA((n,))
    frame_low = shape(share, width, dtype=BF)
    frame_high = shape(share, width)
    frame_wide = shape(share, 4 * units, dtype=BF)
    two_low = shape(2, share, width, dtype=BF)
    two_text = shape(2, SLOTS * LANES, width, dtype=BF)
    logs = shape(16, share)
    stat_shape = shape(72, width)

    def soft_scratch(keys):
        return dict(
            logs=pltpu.VMEM((share, LANES), F32),
            scores=[pltpu.VMEM((UNIT, keys), F32)] * 2,
            probs=[pltpu.VMEM((UNIT, keys), BF)] * 2,
            sums=[pltpu.VMEM((UNIT, 2 * LANES), F32)] * (2 * blocks),
            peaks=[pltpu.VMEM((UNIT, LANES), F32)] * (2 * blocks),
            sum0=floats,
        )

    x = lax.dynamic_slice_in_dim(tokens, core * share, share).astype(F32)
    kept = []
    for layer in range(LAYERS):
        first = 4 * layer
        mod = (mods, (layer,))
        bias_row = lambda row: (narrow_biases, (layer, pl.ds(row, 1)))
        entry1, q, kv = run(
            qkv_kernel,
            "self_qkv",
            info,
            dict(x=x),
            dict(mod=mod, q_bias=bias_row(0), v_bias=bias_row(1)),
            weights_of(first),
            dict(entry=frame_low, q=frame_low, kv=two_low),
            {},
            dict(
                wq=whole, wk=whole, wv=whole, sum0=floats, sum1=floats, sum2=floats, sems=sems(12)
            ),
            [*along_x[1:3], *owns[1:]] if layer == 0 else [],
            3.0,
        )
        kv_sib = tensor_hop(kv, 1)
        opened = open_gate([entry1], [4, 5], [], [1]) if layer == 0 else open_gate([entry1], [], [6])
        x1, mixed1, lse1, branch1 = run(
            self_kernel,
            "self_attention",
            info,
            dict(q=q, kv_own=kv, kv_sib=kv_sib, x=x),
            dict(mod=mod, bias=(out_biases[0], (layer,))),
            weights_of(first),
            dict(out=frame_high, mixed=frame_low, lse=logs, branch=frame_low),
            {},
            dict(
                wo=whole,
                marks=pltpu.VMEM((2 * share, LANES), BF),
                sems=sems(4),
                **soft_scratch(2 * share),
            ),
            opened,
            8.0,
        )
        opened = open_gate([x1], [6, 7], [3], [2]) if layer == 0 else open_gate([x1], [], [7], [5, 6])
        x2, entry2, cq, ckv, mixed2, lse2, branch2 = run(
            partial(cross_kernel, words=words),
            "cross_attention",
            info,
            dict(x=x1, text=text_rows),
            dict(
                mod=mod, q_bias=bias_row(2), v_bias=bias_row(3), bias=(out_biases[1], (layer,))
            ),
            weights_of(first + 1),
            dict(
                out=frame_high,
                entry=frame_low,
                q=frame_low,
                kv=two_text,
                mixed=frame_low,
                lse=logs,
                branch=frame_low,
            ),
            {},
            dict(
                wq=whole,
                wk=whole,
                wv=whole,
                wo=whole,
                sum1=floats,
                sum2=floats,
                sems=sems(16),
                **soft_scratch(LANES),
            ),
            opened,
            6.0,
        )
        opened = open_gate([x2], [], [4], [3]) if layer == 0 else open_gate([x2], [], [], [7])
        results = run(
            lambda info, work, w: hidden_kernel(info, work, w[:6], w[6:]),
            "feed_forward",
            info,
            dict(x=x2),
            dict(mod=mod, up_bias=(up_biases, (layer,)), bias=(out_biases[2], (layer,))),
            weights_of(first + 2) + weights_of(first + 3),
            dict(
                out=frame_high,
                entry=frame_low,
                active=frame_wide,
                slope=frame_wide,
                branch=frame_low,
                **(dict(low=frame_low) if layer == LAYERS - 1 else {}),
            ),
            {},
            dict(
                up=four,
                down=four,
                before0=floats,
                before1=floats,
                sum0=floats,
                sems=sems(8),
                down_sems=sems(8),
            ),
            opened,
            7.0,
        )
        x3, entry3, active, slope, branch3 = results[:5]
        if layer == 0:
            open_gate([x3], [], [5], [4])
        kept.append(
            dict(
                x=x,
                entry1=entry1,
                q=q,
                kv=kv,
                kv_sib=kv_sib,
                mixed1=mixed1,
                lse1=lse1,
                branch1=branch1,
                x1=x1,
                entry2=entry2,
                cq=cq,
                ckv=ckv,
                mixed2=mixed2,
                lse2=lse2,
                branch2=branch2,
                x2=x2,
                entry3=entry3,
                active=active,
                slope=slope,
                branch3=branch3,
            )
        )
        x = x3

    def join(rows):
        return plain(
            join_kernel,
            "join_rows",
            info,
            [rows, tensor_hop(rows, 1)],
            [shape(2 * share, width, dtype=BF)],
        )

    output = join(results[5])

    chains = {}

    def start(name, send, keep):
        view = (size, unit, send.shape[1])
        chains[name] = (tensor_hop(send, 1).reshape(view), keep.reshape(view), 0)

    def held(*names):
        return [chains[name][1] for name in names]

    def advance(names, after=()):
        names = [n for n in names if 2 ** chains[n][2] < size]
        if not names:
            return
        ins, in_specs, outs, out_specs = [], [], [], []
        cuts = 2 if all(chains[name][0].shape[2] % (4 * LANES) == 0 for name in names) else 1
        for name in names:
            received, kept_part, bit = chains[name]
            count, unit, columns = received.shape
            for side in range(2):

                def at(i, info, bit=bit, side=side):
                    return (0, ((info[8] >> bit) & 1) ^ side, 0, i)

                for part in (received, kept_part):
                    ins.append(part.reshape(count // 2, 2, unit, columns))
                    in_specs.append(pl.BlockSpec((count // 2, None, unit, columns // cuts), at))
                outs.append(shape(count // 2, unit, columns, dtype=BF))
                out_specs.append(
                    pl.BlockSpec((count // 2, unit, columns // cuts), lambda i, info: (0, 0, i))
                )
        results = pl.pallas_call(
            partial(merge_kernel, chains=len(names), after=len(after)),
            grid_spec=pltpu.PrefetchScalarGridSpec(
                num_scalar_prefetch=1,
                grid=(cuts,),
                in_specs=in_specs + [ANY] * len(after),
                out_specs=out_specs,
            ),
            out_shape=outs,
            compiler_params=pltpu.CompilerParams(vmem_limit_bytes=VMEM_BYTES),
            cost_estimate=lasting(1.5),
            name="merge_grads",
        )(info, *ins, *after)
        for index, name in enumerate(names):
            bit = chains[name][2]
            hold, give = results[2 * index : 2 * index + 2]
            chains[name] = (dp_hop(give, 2**bit), hold, bit + 1)

    full = pl.BlockSpec((share, width), lambda i, info: (0, 0))

    def narrow_grads(members, after=()):
        lefts, which = [], []
        for left, _, _ in members:
            at = [i for i, seen in enumerate(lefts) if seen is left]
            if not at:
                lefts.append(left)
                at = [len(lefts) - 1]
            which.append(at[0])
        specs = []
        for _, right, first in members:
            if first is None:
                specs.append(pl.BlockSpec((share, 2 * narrow), lambda i, info: (0, info[6])))
            else:
                specs.append(
                    pl.BlockSpec(
                        (None, share, 2 * narrow), lambda i, info, first=first: (first, 0, info[6])
                    )
                )
        result = pl.BlockSpec((width, len(members) * narrow), lambda i, info: (0, 0))
        return pl.pallas_call(
            partial(narrow_grad_kernel, lefts=tuple(which)),
            grid_spec=pltpu.PrefetchScalarGridSpec(
                num_scalar_prefetch=1,
                grid=(1,),
                in_specs=[full] * len(lefts) + specs + [ANY] * len(after),
                out_specs=[result] * 2,
                scratch_shapes=[pltpu.VMEM((len(members), width, 2 * narrow), F32)],
            ),
            out_shape=[shape(width, len(members) * narrow, dtype=BF)] * 2,
            compiler_params=pltpu.CompilerParams(vmem_limit_bytes=VMEM_BYTES),
            cost_estimate=lasting(15.0),
            name="narrow_grads",
        )(info, *lefts, *[right for _, right, _ in members], *after)

    def wide_grads(entry, gb, d_before, active, after=()):
        sib = pl.BlockSpec((share, units), lambda i, info: (0, info[7]))
        own = pl.BlockSpec((share, units), lambda i, info: (0, info[5]))
        result = pl.BlockSpec((width, 2 * units), lambda i, info: (0, 0))
        return pl.pallas_call(
            wide_grad_kernel,
            grid_spec=pltpu.PrefetchScalarGridSpec(
                num_scalar_prefetch=1,
                grid=(1,),
                in_specs=[full, full, sib, own, sib, own] + [ANY] * len(after),
                out_specs=[result] * 2,
            ),
            out_shape=[shape(width, 2 * units, dtype=BF)] * 2,
            compiler_params=pltpu.CompilerParams(vmem_limit_bytes=VMEM_BYTES),
            cost_estimate=lasting(15.0),
            name="wide_grads",
        )(info, entry, gb, d_before, d_before, active, active, *after)

    g = lax.dynamic_slice_in_dim(cotangent, core * share, share).astype(F32)
    sums = []
    last = LAYERS - 1
    for layer in reversed(range(LAYERS)):
        first = 4 * layer
        k = kept[layer]
        mod = (mods, (layer,))
        older = [f"c{layer + 1}", f"s{layer + 1}"] if layer < last else []
        f_name, c_name, s_name = [f"{kind}{layer}" for kind in "fcs"]
        more = held(f"f{layer + 1}", *older) if older else [output]
        g, gb3, d_before, stats = run(
            lambda info, work, w: hidden_back_kernel(info, work, w[:6], w[6:]),
            "feed_forward_back",
            info,
            dict(g=g, branch=k["branch3"], slope=k["slope"], x=k["x2"]),
            dict(mod=mod),
            weights_of(first + 2) + weights_of(first + 3),
            dict(out=frame_high, gb=frame_low, d_before=frame_wide),
            dict(stats=stat_shape),
            dict(
                up=four,
                down=four,
                before0=floats,
                before1=floats,
                de=floats,
                sems=sems(8),
                down_sems=sems(8),
            ),
            more,
            7.0,
        )
        if older:
            advance(older, [gb3])
        start(f_name, *wide_grads(k["entry3"], gb3, d_before, k["active"], held(*older)))
        g, gb2, dcq, dckv, stats = run(
            partial(cross_back_kernel, words=words),
            "cross_attention_back",
            info,
            dict(g=g, branch=k["branch2"], q=k["cq"], kv=k["ckv"], lse=k["lse2"], x=k["x1"]),
            dict(mod=mod, early=(stats, ())),
            weights_of(first + 1),
            dict(out=frame_high, gb=frame_low, dq=frame_low, dkv=two_text),
            dict(stats=stat_shape),
            dict(
                wq=whole,
                wo=whole,
                d_mixed=lows,
                de=floats,
                dkv_sum=pltpu.VMEM(two_text.shape, F32),
                sems=sems(8),
            ),
            held(f_name, *older),
            7.0,
        )
        advance([f_name, *older], [g])
        cross_members = [
            (k["entry2"], dcq, None),
            (text_rows, dckv, 0),
            (text_rows, dckv, 1),
            (gb2, k["mixed2"], None),
        ]
        early_c = []
        if layer == 0:
            start(c_name, *narrow_grads(cross_members, held(f_name)))
            early_c = [c_name]
        gb1, dq, dkv_own, dkv_give, stats = run(
            self_back_kernel,
            "self_attention_back",
            info,
            dict(
                g=g, branch=k["branch1"], q=k["q"], kv_own=k["kv"], kv_sib=k["kv_sib"], lse=k["lse1"]
            ),
            dict(mod=mod, early=(stats, ())),
            weights_of(first),
            dict(gb=frame_low, dq=frame_low, dkv_own=two_low, dkv_give=two_low),
            dict(stats=stat_shape),
            dict(
                wo=whole,
                d_mixed=lows,
                sum0=floats,
                marks=pltpu.VMEM((2 * share, LANES), BF),
                lefts=pltpu.VMEM((2 * share, LANES), BF),
                grads=pltpu.VMEM((2 * share, LANES), BF),
                scores=[pltpu.VMEM((2 * share, UNIT), F32)] * 2,
                rises=[pltpu.VMEM((2 * share, UNIT), F32)] * 2,
                probs=pltpu.VMEM((2 * share, 2 * share), BF),
                d_scores=pltpu.VMEM((2 * share, 2 * share), BF),
                sems=sems(4),
            ),
            held(f_name, *older, *early_c),
            13.0,
        )
        dkv_sib = tensor_hop(dkv_give, 1)
        advance([f_name, *older[1:], *early_c], [dq])
        self_members = [(k["entry1"], dq, None), (gb1, k["mixed1"], None)]
        if layer > 0:
            start(c_name, *narrow_grads(cross_members, held(f_name)))
        else:
            start("a0", *narrow_grads(self_members, held(f_name)))
            self_members = []
        results = run(
            qkv_back_kernel,
            "self_qkv_back",
            info,
            dict(dkv_own=dkv_own, dkv_sib=dkv_sib, dq=dq, x=k["x"], g=g),
            dict(mod=mod, early=(stats, ())),
            weights_of(first),
            dict(
                out=frame_high, dkv=two_low, **(dict(low=frame_low) if layer == 0 else {})
            ),
            dict(stats=stat_shape),
            dict(wq=whole, wk=whole, wv=whole, de=floats, sems=sems(12)),
            held(f_name, *older, c_name, *(["a0"] if layer == 0 else [])),
            4.0,
        )
        g, dkv, stats = results[0], results[1], results[-1]
        self_members += [(k["entry1"], dkv, 0), (k["entry1"], dkv, 1)]
        start(s_name, *narrow_grads(self_members))
        advance([f_name, c_name, *(["a0"] if layer == 0 else [])], held(s_name))
        sums = [stats, tensor_hop(stats, 1)] + sums
    input_grad = join(results[2])
    vectors = plain(
        partial(collect_kernel, narrow=narrow, units=units, columns=columns),
        "collect_sums",
        info,
        [*sums, condition],
        [shape(16, mine.shape[2])],
        [pltpu.VMEM(stat_shape.shape, F32)],
    )
    gathered = lax.all_gather(vectors, "dp", axis=0)
    previous = held("f0", "c0", "a0")
    while any(2 ** chain[2] < size for chain in chains.values()):
        advance(list(chains), previous)
        previous = held(*chains)

    def parts_of(*names):
        return [part.reshape(1, unit, -1) for name in names for part in chains[name][:2]]

    up_grad, down_grad = plain(
        wide_finish_kernel,
        "finish_wide",
        None,
        parts_of(*[f"f{layer}" for layer in range(LAYERS)]),
        [shape(LAYERS, unit, units)] * 2,
    )
    straight, across = shape(LAYERS, unit, narrow), shape(LAYERS, narrow, unit)
    c_grads = plain(
        partial(narrow_finish_kernel, spots=[[(l, 0), (l, 1)] for l in range(LAYERS)]),
        "finish_narrow",
        None,
        parts_of(*[f"c{layer}" for layer in range(LAYERS)]),
        [straight, straight, straight, across],
    )
    s_grads = plain(
        partial(
            narrow_finish_kernel,
            spots=[[(0, 0)], [(0, 1)]] + [[(l, 0), (l, 1)] for l in range(1, LAYERS)],
        ),
        "finish_narrow",
        None,
        parts_of("a0", *[f"s{layer}" for layer in range(LAYERS)]),
        [straight, across, straight, straight],
    )
    small = plain(
        spread_kernel,
        "spread_sums",
        info,
        [gathered],
        [shape(LAYERS, unit, columns), shape(LAYERS, columns)]
        + [shape(LAYERS, narrow)] * 4
        + [shape(LAYERS, units)]
        + [shape(LAYERS, unit)] * 3,
        [pltpu.VMEM((SLOTS * size, columns), F32), pltpu.VMEM((SLOTS * size, width), F32)],
    )
    mod_grad, mod_bias_grad, q_sum, v_sum, cq_sum, cv_sum, up_sum, o1, o2, o3 = small
    q_grad, o_grad, k_grad, v_grad = s_grads
    return (
        output,
        input_grad,
        q_grad,
        q_sum,
        k_grad,
        v_grad,
        v_sum,
        o_grad,
        o1,
        c_grads[0],
        cq_sum,
        c_grads[1],
        c_grads[2],
        cv_sum,
        c_grads[3],
        o2,
        up_grad,
        up_sum,
        turn(down_grad),
        o3,
        mod_grad,
        mod_bias_grad,
    )


def solution(mesh):
    dp, tensor = "dp", "tensor"
    columns, vector = P(None, None, tensor), P(None, tensor)
    matrix, turned, spread = P(None, dp, tensor), P(None, tensor, dp), P(None, dp)
    placed = (
        P(dp, None),
        P(dp, None, None),
        P(dp),
        P(dp),
        P(dp, None),
        columns,
        vector,
        columns,
        columns,
        vector,
        P(None, tensor, None),
        P(),
        columns,
        vector,
        columns,
        columns,
        vector,
        P(None, tensor, None),
        P(),
        columns,
        vector,
        P(None, tensor, None),
        P(),
        columns,
        vector,
    )
    results = (
        P(dp, None),
        P(dp, None),
        matrix,
        vector,
        matrix,
        matrix,
        vector,
        turned,
        spread,
        matrix,
        vector,
        matrix,
        matrix,
        vector,
        turned,
        spread,
        matrix,
        vector,
        turned,
        spread,
        matrix,
        vector,
    )
    return jax.shard_map(
        shards, mesh=mesh, in_specs=placed, out_specs=results, check_vma=False
    )
```

```python
from functools import partial
import math

import jax
import jax.numpy as jnp
from jax import lax
from jax.experimental import pallas as pl
from jax.experimental.pallas import tpu as pltpu
from jax.sharding import PartitionSpec as P

HEAD_WIDTH = 64
UNIT = 256
LAYERS = 2
WINDOW = 1024
EPSILON = 1e-06
LANES = 128
TILE = 256
SLOTS = WINDOW // UNIT
FAR = -1e30
VMEM_BYTES = 56 * 1024 * 1024
BF = jnp.bfloat16
F32 = jnp.float32
ROOT = math.sqrt(2.0 / math.pi)
CUBIC = 0.044715


def dot_nn(left, right):
    return jnp.dot(left, right, preferred_element_type=F32)


def dot_nt(left, right):
    return lax.dot_general(left, right, (((1,), (1,)), ((), ())), preferred_element_type=F32)


def dot_tn(left, right):
    return lax.dot_general(left, right, (((0,), (0,)), ((), ())), preferred_element_type=F32)


SMALL = pl.BlockSpec(memory_space=pltpu.SMEM)
NEAR = pl.BlockSpec(memory_space=pltpu.VMEM)
ANY = pl.BlockSpec(memory_space=pl.ANY)


class Work:
    def __init__(self, ins, outs, scratch, in_sems, out_sems):
        self.ins, self.outs, self.scratch, self.out_sems = ins, outs, scratch, out_sems
        self.copies, self.waited, self.flushed = {}, set(), []
        for index, (name, (ref, buffer)) in enumerate(ins.items()):
            self.copies[name] = pltpu.make_async_copy(ref, buffer, in_sems.at[index])
            self.copies[name].start()

    def __getattr__(self, name):
        if name in self.__dict__["ins"]:
            return self.ins[name][1]
        if name in self.__dict__["outs"]:
            return self.outs[name][1]
        return self.__dict__["scratch"][name]

    def has(self, name):
        return name in self.outs

    def send(self, name, source, *at):
        ref = self.outs[name][0]
        copy = pltpu.make_async_copy(
            source, ref.at[at] if at else ref, self.out_sems.at[len(self.flushed)]
        )
        copy.start()
        self.flushed.append(copy)

    def need(self, *names):
        for name in names:
            if name not in self.waited:
                self.waited.add(name)
                self.copies[name].wait()

    def flush(self, name, *at):
        ref, buffer = self.outs[name]
        if at:
            ref, buffer = ref.at[at], buffer.at[at]
        copy = pltpu.make_async_copy(buffer, ref, self.out_sems.at[len(self.flushed)])
        copy.start()
        self.flushed.append(copy)

    def finish(self):
        self.need(*self.ins)
        for copy in self.flushed:
            copy.wait()


def run(body, name, info, ins, small, weights, outs, small_outs, scratch, after=(), cost=1.0):
    in_names, out_names, names = list(ins), list(outs), list(scratch)
    small_names, small_out_names = list(small), list(small_outs)
    counts = [1, len(in_names), len(small), len(weights), len(after), len(outs), len(small_outs)]

    def kernel(*refs):
        refs = list(refs)
        parts = []
        for count in counts:
            parts.append(refs[:count])
            refs = refs[count:]
        (info_ref,), in_refs, small_refs, weight_refs, _, out_refs, small_out_refs = parts
        in_bufs, refs = refs[: len(in_names)], refs[len(in_names) :]
        out_bufs, refs = refs[: len(out_names)], refs[len(out_names) :]
        rest, (in_sems, out_sems) = refs[:-2], refs[-2:]
        extra = {}
        rest = list(rest)
        for key in names:
            many = isinstance(scratch[key], list)
            size = len(scratch[key]) if many else 1
            extra[key] = rest[:size] if many else rest[0]
            rest = rest[size:]
        for key, ref in zip(small_names, small_refs):
            index = small[key][1]
            extra[key] = ref.at[index] if index else ref
        extra.update(zip(small_out_names, small_out_refs))
        work = Work(
            dict(zip(in_names, zip(in_refs, in_bufs))),
            dict(zip(out_names, zip(out_refs, out_bufs))),
            extra,
            in_sems,
            out_sems,
        )
        body(info_ref, work, weight_refs)
        work.finish()

    buffer = lambda a: pltpu.VMEM(a.shape, a.dtype)
    flat = []
    for value in scratch.values():
        flat += value if isinstance(value, list) else [value]
    results = pl.pallas_call(
        kernel,
        out_shape=[outs[n] for n in out_names] + [small_outs[n] for n in small_out_names],
        in_specs=[SMALL]
        + [ANY] * len(ins)
        + [NEAR] * len(small)
        + [ANY] * (len(weights) + len(after)),
        out_specs=[ANY] * len(outs) + [NEAR] * len(small_outs),
        scratch_shapes=[buffer(ins[n]) for n in in_names]
        + [buffer(outs[n]) for n in out_names]
        + flat
        + [pltpu.SemaphoreType.DMA((max(len(ins), 1),)), pltpu.SemaphoreType.DMA((32,))],
        compiler_params=pltpu.CompilerParams(vmem_limit_bytes=VMEM_BYTES),
        cost_estimate=lasting(cost),
        name=name,
    )(info, *ins.values(), *[array for array, _ in small.values()], *weights, *after)
    return results


def plain(body, name, info, ins, outs, scratch=()):
    results = pl.pallas_call(
        body,
        out_shape=outs,
        in_specs=([] if info is None else [SMALL]) + [NEAR] * len(ins),
        out_specs=[NEAR] * len(outs),
        scratch_shapes=list(scratch),
        compiler_params=pltpu.CompilerParams(vmem_limit_bytes=VMEM_BYTES),
        cost_estimate=lasting(1.0),
        name=name,
    )(*([] if info is None else [info]), *ins)
    return results if len(outs) > 1 else results[0]


def lasting(units):
    return pl.CostEstimate(flops=int(units * 0.4e9), bytes_accessed=1000, transcendentals=0)


def shape(*dims, dtype=F32):
    return jax.ShapeDtypeStruct(dims, dtype)


def start_rows(refs, place, plan, sems):
    own, sib, xa, ya, xb, yb = refs
    half = own.shape[0] // 2
    for rank in range(4):
        for parity in range(2):

            @pl.when(place == rank * 2 + parity)
            def _(rank=rank, parity=parity):
                for index, (shard, row, rows, dst) in enumerate(plan):
                    step = shard ^ rank
                    if step < 2:
                        src = (own, sib)[step].at[pl.ds(row, rows)]
                    else:
                        first, second = ((xa, ya), (xb, yb))[step - 2]
                        part = row // half
                        src = (first if part == parity else second).at[pl.ds(row - part * half, rows)]
                    pltpu.make_async_copy(src, dst, sems.at[index]).start()


def wait_rows(refs, plan, sems, which):
    for index in which:
        _, row, rows, dst = plan[index]
        pltpu.make_async_copy(refs[0].at[pl.ds(0, rows)], dst, sems.at[index]).wait()


def plan_of(buffers, first, rows):
    return [
        (shard, (first + which) * rows, rows, dst.at[pl.ds(shard * rows, rows)])
        for which, dst in enumerate(buffers)
        for shard in range(4)
    ]


def norm_rows(values):
    mean = jnp.mean(values, axis=-1, keepdims=True)
    center = values - mean
    factor = lax.rsqrt(jnp.mean(center * center, axis=-1, keepdims=True) + EPSILON)
    return center * factor, factor


def piece(mod, slot, index):
    width = mod.shape[1] // 9
    return mod[pl.ds(slot, 1), index * width : (index + 1) * width]


def each_rows(first, count, rows, step, carry=0, group=4):
    def turn(index, carry):
        for part in range(group):
            at = first + index * (rows * group) + part * rows
            carry = step(pl.ds(pl.multiple_of(at, rows), rows), carry)
        return carry

    return lax.fori_loop(0, count // (rows * group), turn, carry)


def div(index, count):
    return lax.div(index, jnp.int32(count))


def rem(index, count):
    return lax.rem(index, jnp.int32(count))


def loop(count, step):
    def turn(index, carry):
        step(index)
        return carry

    lax.fori_loop(0, count, turn, 0)


def tile(index):
    return pl.ds(pl.multiple_of(index * TILE, TILE), TILE)


def entry_rows(x, mod, info, index, out):
    def of_block(block):
        slot = info[1 + block]
        shift = piece(mod, slot, index)
        scale = 1.0 + piece(mod, slot, index + 1)

        def step(span, carry):
            normed, _ = norm_rows(x[span, :])
            out[span, :] = (normed * scale + shift).astype(BF)
            return carry

        each_rows(block * UNIT, UNIT, 16, step)

    loop(x.shape[0] // UNIT, of_block)


def residual_rows(x, mod, info, index, branch, bias, branch_out, out, low=None):
    def of_block(block):
        gate = piece(mod, info[1 + block], index)

        def step(span, carry):
            values = branch[span, :] + bias
            branch_out[span, :] = values.astype(BF)
            result = x[span, :] + gate * values
            out[span, :] = result
            if low is not None:
                low[span, :] = result.astype(BF)
            return carry

        each_rows(block * UNIT, UNIT, 16, step)

    loop(x.shape[0] // UNIT, of_block)


def fold(values):
    return jnp.sum(values.reshape(values.shape[0] // 8, 8, values.shape[1]), axis=0)


def total(values):
    return jnp.sum(values, axis=0, keepdims=True)


def column_sum(ref):
    width = ref.shape[1]

    def step(span, carry):
        return carry + fold(ref[span, :].astype(F32))

    return total(each_rows(0, ref.shape[0], 16, step, jnp.zeros((8, width), F32)))


def gate_back(g, mod, info, index, branch, gb, stats):
    width = g.shape[1]
    zero = jnp.zeros((8, width), F32)

    def of_block(block, sums):
        slot = info[1 + block]
        gate = piece(mod, slot, index)

        def step(span, carry):
            grad = g[span, :]
            low = (gate * grad).astype(BF)
            gb[span, :] = low
            return (
                carry[0] + fold(low.astype(F32)),
                carry[1] + fold(grad * branch[span, :].astype(F32)),
            )

        sums, rows_sum = each_rows(block * UNIT, UNIT, 16, step, (sums, zero), 2)
        stats[pl.ds(8 + slot, 1), :] += total(rows_sum)
        return sums

    stats[12:13, :] = total(lax.fori_loop(0, g.shape[0] // UNIT, of_block, zero))


def norm_back_rows(x, g, de, mod, info, index, out, stats, low=None):
    width = x.shape[1]
    zero = jnp.zeros((8, width), F32)

    def of_block(block):
        slot = info[1 + block]
        scale = 1.0 + piece(mod, slot, index + 1)

        def step(span, carry):
            normed, factor = norm_rows(x[span, :])
            grad = de[span, :]
            inner = grad * normed
            dn = grad * scale
            mean = jnp.mean(dn, axis=-1, keepdims=True)
            along = jnp.mean(dn * normed, axis=-1, keepdims=True)
            out[span, :] = g[span, :] + factor * (dn - mean - normed * along)
            return (carry[0] + fold(grad), carry[1] + fold(inner))

        shift_sum, scale_sum = each_rows(block * UNIT, UNIT, 8, step, (zero, zero), 4)
        stats[pl.ds(slot, 1), :] += total(shift_sum)
        stats[pl.ds(4 + slot, 1), :] += total(scale_sum)

    loop(x.shape[0] // UNIT, of_block)
    if low is not None:

        def lower(span, carry):
            low[span, :] = out[span, :].astype(BF)
            return carry

        each_rows(0, x.shape[0], 16, lower)


def lane_ids(rows):
    return lax.broadcasted_iota(jnp.int32, (rows, LANES), 1)


def head_half(values, half):
    ids = lane_ids(values.shape[0])
    keep = ids < HEAD_WIDTH if half == 0 else ids >= HEAD_WIDTH
    return jnp.where(keep, values.astype(F32), 0.0)


def query_marks(slot):
    return jnp.where(lane_ids(UNIT) == slot, 1.0, 0.0).astype(BF)


def key_marks(slots):
    ids = lane_ids(UNIT)
    parts = [jnp.where((ids < SLOTS) & (ids != slot), FAR, 0.0).astype(BF) for slot in slots]
    return jnp.concatenate(parts, axis=0)


def pair_lanes(pair):
    return pl.ds(pl.multiple_of(pair * LANES, LANES), LANES)


def kv_kernel(info, work, weights):
    rows = weights[0].shape[0] // 4
    plan = plan_of((work.w.at[0], work.w.at[1]), 1, rows)
    start_rows(weights, info[0], plan, work.sems)
    work.need("x")
    entry_rows(work.x, work.mod, info, 0, work.entry)
    work.flush("entry")
    wait_rows(weights, plan, work.sems, range(8))
    count = work.x.shape[1] // TILE

    def step(index):
        which, at = div(index, count), rem(index, count)
        product = dot_nt(work.entry[...], work.w[which, tile(at), :])
        work.kv[which, :, tile(at)] = (product + work.biases[pl.ds(1 + which, 1), tile(at)]).astype(
            BF
        )

    loop(2 * count, step)
    work.flush("kv")


def q_kernel(info, work, weights):
    rows = weights[0].shape[0] // 4
    plan = plan_of((work.w,), 0, rows)
    start_rows(weights, info[0], plan, work.sems)
    work.need("entry")
    wait_rows(weights, plan, work.sems, range(4))

    def step(at):
        product = dot_nt(work.entry[...], work.w[tile(at), :])
        work.q[:, tile(at)] = (product + work.biases[0:1, tile(at)]).astype(BF)

    loop(work.w.shape[0] // TILE, step)
    work.flush("q")


def soft_rows(raw, low, peaks, words=None):
    rows = 16 if words is None else 64

    def step(span, carry):
        part = raw[span, :]
        if words is not None:
            part = jnp.where(lane_ids(rows) < words, part, FAR)
        peak = jnp.max(part, axis=-1, keepdims=True)
        low[span, :] = jnp.exp(part - peak).astype(BF)
        peaks[span, :] = jnp.broadcast_to(peak, (rows, LANES))
        return carry

    each_rows(0, UNIT, rows, step)


def soft_block(work, pair, block, marks, keys, values, words=None):
    lanes = pair_lanes(pair)
    first = pl.multiple_of(block * UNIT, UNIT)
    q_pair = work.q[pl.ds(first, UNIT), lanes]
    for half in range(2):
        left = (head_half(q_pair, half) * HEAD_WIDTH**-0.5).astype(BF)
        if marks is not None:
            left = jnp.concatenate([left, marks], axis=1)
        work.scores[...] = dot_nt(left, keys)
        soft_rows(work.scores, work.probs, work.peaks.at[half], words)
        work.sums[half] = dot_nn(work.probs[...], values)

    def finish(span, carry):
        at = pl.ds(pl.multiple_of(first + span.start, 32), 32)
        kept = work.logs[at, :]
        parts = []
        for half in range(2):
            sums = work.sums[half, span, LANES:]
            parts.append(work.sums[half, span, :LANES] / sums)
            kept = jnp.where(
                lane_ids(32) == 2 * pair + half, work.peaks[half, span, :] + jnp.log(sums), kept
            )
        work.logs[at, :] = kept
        work.mixed[at, lanes] = jnp.where(lane_ids(32) < HEAD_WIDTH, parts[0], parts[1]).astype(BF)
        return carry

    each_rows(0, UNIT, 32, finish, group=2)


def output_rows(work, info, index):
    def step(at):
        work.sum0[:, tile(at)] = dot_nn(work.mixed[...], work.wo[:, tile(at)])

    loop(work.wo.shape[1] // TILE, step)
    bias = work.bias[...].astype(F32)
    residual_rows(work.x, work.mod, info, index, work.sum0, bias, work.branch, work.out)
    work.flush("branch")
    work.flush("out")


def self_kernel(info, work, weights):
    rows = weights[0].shape[0] // 4
    sems = work.sems
    plan = [(s, 3 * rows, rows, work.wo.at[pl.ds(s * rows, rows)]) for s in range(4)]
    start_rows(weights, info[0], plan, sems)
    share = work.x.shape[0]
    blocks = share // UNIT
    work.marks[...] = key_marks([info[1 + b] for b in range(2 * blocks)])
    work.logs[...] = jnp.zeros(work.logs.shape, F32)
    work.need("q", "kv_own", "kv_sib")

    def both(which, lanes):
        return jnp.concatenate([work.kv_own[which, :, lanes], work.kv_sib[which, :, lanes]], axis=0)

    def step(item):
        pair, block = div(item, blocks), rem(item, blocks)
        lanes = pair_lanes(pair)
        keys = jnp.concatenate([both(0, lanes), work.marks[...]], axis=1)
        values = jnp.concatenate([both(1, lanes), jnp.ones((2 * share, LANES), BF)], axis=1)
        soft_block(work, pair, block, query_marks(info[1 + block]), keys, values)

    loop(blocks * (work.mixed.shape[1] // LANES), step)
    work.flush("mixed")
    work.lse[...] = work.logs[...].T[: work.lse.shape[0], :]
    work.flush("lse")
    wait_rows(weights, plan, sems, range(4))
    work.need("x")
    output_rows(work, info, 2)


def cross_kernel(info, work, weights, words):
    rows = weights[0].shape[0] // 4
    sems = work.sems
    plan = plan_of((work.w.at[0], work.w.at[1], work.w.at[2], work.wo), 0, rows)
    start_rows(weights, info[0], plan, sems)
    work.need("x")
    entry_rows(work.x, work.mod, info, 3, work.entry)
    work.flush("entry")
    work.need("text")
    wait_rows(weights, plan, sems, range(12))
    count = work.x.shape[1] // TILE

    def of_text(index):
        which, at = div(index, count), rem(index, count)
        product = dot_nt(work.text[...], work.w[1 + which, tile(at), :])
        work.kv[which, :, tile(at)] = (product + work.biases[pl.ds(4 + which, 1), tile(at)]).astype(
            BF
        )

    loop(2 * count, of_text)
    work.flush("kv")

    def of_frames(at):
        product = dot_nt(work.entry[...], work.w[0, tile(at), :])
        work.q[:, tile(at)] = (product + work.biases[3:4, tile(at)]).astype(BF)

    loop(count, of_frames)
    work.flush("q")
    work.logs[...] = jnp.zeros(work.logs.shape, F32)
    blocks = work.x.shape[0] // UNIT

    def step(item):
        pair, block = div(item, blocks), rem(item, blocks)
        lanes = pair_lanes(pair)
        own = pl.ds(pl.multiple_of(info[1 + block] * LANES, LANES), LANES)
        keys = work.kv[0, own, lanes]
        values = jnp.concatenate([work.kv[1, own, lanes], jnp.ones((LANES, LANES), BF)], axis=1)
        soft_block(work, pair, block, None, keys, values, words)

    loop(blocks * (work.mixed.shape[1] // LANES), step)
    work.flush("mixed")
    work.lse[...] = work.logs[...].T[: work.lse.shape[0], :]
    work.flush("lse")
    wait_rows(weights, plan, sems, range(12, 16))
    output_rows(work, info, 5)


def halves_of(buffer):
    half = buffer.shape[1] // 2
    return [
        (shard, part * half, half, buffer.at[shard, pl.ds(part * half, half)])
        for shard in range(4)
        for part in range(2)
    ]


def hidden_kernel(info, work, ups, downs):
    sems = work.sems
    width = work.x.shape[1]
    up_plan = halves_of(work.up)
    down_plan = halves_of(work.down)
    start_rows(ups, info[0], up_plan, sems)
    start_rows(downs, info[0], down_plan, work.down_sems)
    work.need("x")
    entry_rows(work.x, work.mod, info, 6, work.entry)
    work.flush("entry")
    wait_rows(ups, up_plan, sems, range(8))
    count = width // TILE

    def rise(index):
        work.before[...] = dot_nn(work.entry[...], work.up[div(index, count), :, tile(rem(index, count))])
        lanes = tile(index)
        bias = work.up_bias[:, lanes]

        def bend(span, carry):
            values = work.before[span, :] + bias
            square = values * values
            half = 1.0 / (1.0 + jnp.exp(values * (-2.0 * ROOT - (2.0 * ROOT * CUBIC) * square)))
            act = values * half
            work.active[span, lanes] = act.astype(BF)
            work.slope[span, lanes] = (
                half + act * (1.0 - half) * (2.0 * ROOT + (6.0 * ROOT * CUBIC) * square)
            ).astype(BF)
            return carry

        each_rows(0, work.x.shape[0], 32, bend)

    loop(4 * count, rise)
    work.flush("active")
    work.flush("slope")
    wait_rows(downs, down_plan, work.down_sems, range(8))

    def fall(at):
        work.sum0[:, tile(at)] = sum(
            dot_nn(work.active[:, pl.ds(s * width, width)], work.down[s, :, tile(at)])
            for s in range(4)
        )

    loop(count, fall)
    bias = work.bias[...].astype(F32)
    low = work.low if work.has("low") else None
    residual_rows(work.x, work.mod, info, 8, work.sum0, bias, work.branch, work.out, low)
    work.flush("branch")
    work.flush("out")
    if low is not None:
        work.flush("low")


def hidden_back_kernel(info, work, ups, downs):
    sems = work.sems
    width = work.x.shape[1]
    up_plan = halves_of(work.up)
    down_plan = halves_of(work.down)
    start_rows(downs, info[0], down_plan, work.down_sems)
    start_rows(ups, info[0], up_plan, sems)
    work.stats[...] = jnp.zeros(work.stats.shape, F32)
    stats = work.stats.at[pl.ds(48, 24)]
    work.need("g", "branch")
    gate_back(work.g, work.mod, info, 8, work.branch, work.gb, stats)
    work.flush("gb")
    work.need("slope")
    wait_rows(downs, down_plan, work.down_sems, range(8))
    count = width // TILE

    def rise(index):
        lanes = tile(index)
        work.before[...] = dot_nt(work.gb[...], work.down[div(index, count), tile(rem(index, count)), :])

        def bend(span, carry):
            low = (work.before[span, :] * work.slope[span, lanes].astype(F32)).astype(BF)
            work.d_before[span, lanes] = low
            return carry + fold(low.astype(F32))

        zero = jnp.zeros((8, TILE), F32)
        sums = each_rows(0, work.x.shape[0], 32, bend, zero)
        stats[pl.ds(13 + div(index, count), 1), tile(rem(index, count))] = total(sums)

    loop(4 * count, rise)
    work.flush("d_before")
    wait_rows(ups, up_plan, sems, range(8))

    def fall(at):
        work.de[:, tile(at)] = sum(
            dot_nt(work.d_before[:, pl.ds(s * width, width)], work.up[s, tile(at), :])
            for s in range(4)
        )

    loop(count, fall)
    work.need("x")
    norm_back_rows(work.x, work.g, work.de, work.mod, info, 6, work.out, stats)
    work.flush("out")


def mixed_back(work):
    def step(at):
        work.d_mixed[:, tile(at)] = dot_nt(work.gb[...], work.wo[tile(at), :]).astype(BF)

    loop(work.wo.shape[0] // TILE, step)


def cross_back_kernel(info, work, weights, words):
    rows = weights[0].shape[0] // 4
    sems = work.sems
    plan = [
        (shard, (3 * rows, 0)[i // 4], count, dst)
        for i, (shard, _, count, dst) in enumerate(plan_of((work.wo, work.wq), 0, rows))
    ]
    start_rows(weights, info[0], plan, sems)
    work.stats[...] = work.early[...]
    stats = work.stats.at[pl.ds(24, 24)]
    work.need("g", "branch")
    gate_back(work.g, work.mod, info, 5, work.branch, work.gb, stats)
    work.flush("gb")
    wait_rows(weights, plan, sems, range(0, 4))
    mixed_back(work)
    work.dkv_sum[...] = jnp.zeros(work.dkv_sum.shape, F32)
    work.need("q", "kv", "lse")

    blocks = work.q.shape[0] // UNIT

    def step(item):
        pair, block = div(item, blocks), rem(item, blocks)
        lanes = pair_lanes(pair)
        real = lax.broadcasted_iota(jnp.int32, (LANES, UNIT), 0) < words
        span = pl.ds(pl.multiple_of(block * UNIT, UNIT), UNIT)
        own = pl.ds(pl.multiple_of(info[1 + block] * LANES, LANES), LANES)
        q_pair = work.q[span, lanes]
        d_pair = work.d_mixed[span, lanes]
        keys = work.kv[0, own, lanes]
        values = work.kv[1, own, lanes]
        lefts, grads, turned, probs_low, scores_low = [], [], [], [], []
        for half in range(2):
            left = (head_half(q_pair, half) * HEAD_WIDTH**-0.5).astype(BF)
            grad = head_half(d_pair, half).astype(BF)
            logs = work.lse[pl.ds(2 * pair + half, 1), span]
            probs = jnp.where(real, jnp.exp(dot_nt(keys, left) - logs), 0.0)
            d_probs = dot_nt(values, grad)
            inner = jnp.sum(probs * d_probs, axis=0, keepdims=True)
            lefts.append(left)
            grads.append(grad)
            turned.append(head_half(keys, half).T.astype(BF))
            probs_low.append(probs.astype(BF))
            scores_low.append((probs * (d_probs - inner)).astype(BF))
        wide_scores = jnp.concatenate(scores_low, axis=1)
        grad_v = dot_nn(jnp.concatenate(probs_low, axis=1), jnp.concatenate(grads, axis=0))
        grad_k = dot_nn(wide_scores, jnp.concatenate(lefts, axis=0))
        grad_q = dot_nn(
            jnp.concatenate(turned, axis=1), jnp.concatenate(scores_low, axis=0)
        )
        work.dq[span, lanes] = (grad_q.T * HEAD_WIDTH**-0.5).astype(BF)
        work.dkv_sum[0, own, lanes] += grad_k
        work.dkv_sum[1, own, lanes] += grad_v

    loop(blocks * (work.q.shape[1] // LANES), step)
    work.flush("dq")

    def lower(span, carry):
        for which in range(2):
            work.dkv[which, span, :] = work.dkv_sum[which, span, :].astype(BF)
        return carry

    each_rows(0, work.dkv.shape[1], 16, lower, group=2)
    work.flush("dkv")
    wait_rows(weights, plan, sems, range(4, 8))

    def fall(at):
        work.de[:, tile(at)] = dot_nn(work.dq[...], work.wq[:, tile(at)])

    loop(work.wq.shape[1] // TILE, fall)
    stats[13:14, :] = column_sum(work.dq)
    stats[14:15, :] = column_sum(work.dkv.at[1])
    work.need("x")
    norm_back_rows(work.x, work.g, work.de, work.mod, info, 3, work.out, stats)
    work.flush("out")


def self_back_kernel(info, work, weights):
    rows = weights[0].shape[0] // 4
    sems = work.sems
    plan = [(s, 3 * rows, rows, work.wo.at[pl.ds(s * rows, rows)]) for s in range(4)]
    start_rows(weights, info[0], plan, sems)
    work.stats[...] = work.early[...]
    stats = work.stats.at[pl.ds(0, 24)]
    work.need("g", "branch")
    gate_back(work.g, work.mod, info, 2, work.branch, work.gb, stats)
    work.flush("gb")
    share = work.g.shape[0]
    blocks = share // UNIT
    wait_rows(weights, plan, sems, range(4))
    mixed_back(work)
    work.need("q", "kv_own", "kv_sib", "lse")
    count = 2 * blocks

    def both(which, lanes):
        return jnp.concatenate([work.kv_own[which, :, lanes], work.kv_sib[which, :, lanes]], axis=0)

    def step(pair):
        lanes = pair_lanes(pair)
        keys = both(0, lanes)
        work.values[...] = both(1, lanes)
        work.marked[:, :LANES] = keys
        for half in range(2):
            work.turned[half] = head_half(keys, half).T.astype(BF)

        def chain(index):
            block, half = div(index, 2), rem(index, 2)
            span = pl.ds(pl.multiple_of(block * UNIT, UNIT), UNIT)
            own = tile(index)
            keep = (lane_ids(UNIT) < HEAD_WIDTH) == (half == 0)
            left = jnp.where(keep, work.q[span, lanes].astype(F32) * HEAD_WIDTH**-0.5, 0.0)
            left = left.astype(BF)
            grad = jnp.where(keep, work.d_mixed[span, lanes].astype(F32), 0.0).astype(BF)
            work.lefts[own, :] = left
            work.grads[own, :] = grad
            query = jnp.concatenate([left, query_marks(info[1 + block])], axis=1)
            work.scores[...] = dot_nt(work.marked[...], query)
            work.rises[...] = dot_nt(work.values[...], grad)
            logs = work.lse[pl.ds(2 * pair + half, 1), span]

            def soften(span, carry):
                probs = jnp.exp(work.scores[span, :] - logs)
                work.probs[span, own] = probs.astype(BF)
                return carry + fold(probs * work.rises[span, :])

            zero = jnp.zeros((8, UNIT), F32)
            inner = total(each_rows(0, 2 * share, 32, soften, zero))

            def sink(span, carry):
                work.d_scores[span, own] = (
                    work.probs[span, own].astype(F32) * (work.rises[span, :] - inner)
                ).astype(BF)
                return carry

            each_rows(0, 2 * share, 32, sink)
            part = dot_nn(work.turned[half], work.d_scores[:, own])
            work.dq_t[block] = jnp.where(half == 0, part, work.dq_t[block] + part)

        loop(count, chain)
        for block in range(blocks):
            work.dq[pl.ds(block * UNIT, UNIT), lanes] = (
                work.dq_t[block].T * HEAD_WIDTH**-0.5
            ).astype(BF)

        def gather(index):
            own = tile(index)
            for which, left, right in ((0, work.d_scores, work.lefts), (1, work.probs, work.grads)):
                work.dkv[which, own, lanes] = dot_nn(left[own, :], right[...]).astype(BF)

        loop(2 * share // TILE, gather)

    work.marked[:, LANES:] = key_marks([info[1 + b] for b in range(2 * blocks)])
    loop(work.q.shape[1] // LANES, step)
    for which in range(2):
        work.send("dkv_give", work.dkv.at[which, pl.ds(share, share)], which)
    for which in range(2):
        work.send("dkv_own", work.dkv.at[which, pl.ds(0, share)], which)
    work.flush("dq")


def qkv_back_kernel(info, work, weights):
    rows = weights[0].shape[0] // 4
    sems = work.sems
    plan = plan_of((work.w.at[0], work.w.at[1], work.w.at[2]), 0, rows)
    start_rows(weights, info[0], plan, sems)
    work.stats[...] = work.early[...]
    stats = work.stats.at[pl.ds(0, 24)]
    work.need("dkv_own", "dkv_sib", "dq")

    def join(span, carry):
        for which in range(2):
            work.dkv[which, span, :] = (
                work.dkv_own[which, span, :].astype(F32) + work.dkv_sib[which, span, :].astype(F32)
            ).astype(BF)
        return carry

    each_rows(0, work.x.shape[0], 16, join, group=2)
    work.flush("dkv")
    wait_rows(weights, plan, sems, range(0, 12))

    def fall(at):
        work.de[:, tile(at)] = (
            dot_nn(work.dq[...], work.w[0, :, tile(at)])
            + dot_nn(work.dkv[0], work.w[1, :, tile(at)])
            + dot_nn(work.dkv[1], work.w[2, :, tile(at)])
        )

    loop(work.x.shape[1] // TILE, fall)
    stats[13:14, :] = column_sum(work.dq)
    stats[14:15, :] = column_sum(work.dkv.at[1])
    work.need("x", "g")
    low = work.low if work.has("low") else None
    norm_back_rows(work.x, work.g, work.de, work.mod, info, 0, work.out, stats, low)
    work.flush("out")
    if low is not None:
        work.flush("low")


def wide_grad_kernel(info, entry, gb, db_sib, db_own, act_sib, act_own, *refs):
    send, keep, turned = refs[-3:]
    width = entry.shape[1]
    turned[0] = entry[...].T
    turned[1] = gb[...].T
    for out, pair in ((send, (db_sib, act_sib)), (keep, (db_own, act_own))):
        for index, right in enumerate(pair):

            def step(at, out=out, index=index, right=right):
                lanes = pl.ds(pl.multiple_of(index * width + at * TILE, TILE), TILE)
                out[:, lanes] = dot_nn(turned[index], right[:, tile(at)]).astype(BF)

            loop(width // TILE, step)


def narrow_grad_kernel(info, *refs, lefts):
    count = max(lefts) + 1
    left_refs, rights = refs[:count], refs[count : count + len(lefts)]
    send, keep, products, turned = refs[-4:]
    for at, ref in enumerate(left_refs):
        turned[at] = ref[...].T
    step = 3 * LANES
    rows = 2 * LANES
    for at in range(len(lefts)):

        def multiply(index, at=at):
            own = pl.ds(pl.multiple_of(index * rows, rows), rows)
            products[at, own, :] = dot_nn(turned[lefts[at], own, :], rights[at][...])

        loop(products.shape[1] // rows, multiply)
    low = lane_ids(16) < HEAD_WIDTH
    for core in range(2):

        @pl.when(info[5] % 2 == core)
        def _(core=core):
            outs = (keep, send) if core == 0 else (send, keep)

            def spread(span, carry):
                for at in range(len(lefts) // 2):
                    (a0, a1, a2), (b0, b1, b2) = [
                        [products[2 * at + i, span, pl.ds(j * LANES, LANES)] for j in range(3)]
                        for i in range(2)
                    ]
                    a1r, b1r = pltpu.roll(a1, HEAD_WIDTH, 1), pltpu.roll(b1, HEAD_WIDTH, 1)
                    a2r, b2r = pltpu.roll(a2, HEAD_WIDTH, 1), pltpu.roll(b2, HEAD_WIDTH, 1)
                    even = (a0, b0, jnp.where(low, a1, b1r))
                    odd = (
                        jnp.where(low, a1r, a2r),
                        jnp.where(low, b1r, b2r),
                        jnp.where(low, a2r, b2),
                    )
                    for out, parts in zip(outs, (even, odd)):
                        for i, part in enumerate(parts):
                            out[span, pl.ds(at * step + i * LANES, LANES)] = part.astype(BF)
                return carry

            each_rows(0, products.shape[1], 16, spread, group=2)


def merge_kernel(info, *refs, chains, after):
    ins, outs = refs[: 4 * chains], refs[4 * chains + after :]
    for chain in range(chains):
        count, unit, _ = outs[2 * chain].shape
        rows = 16 if unit % 16 == 0 else unit
        per = unit // rows

        def step(index, chain=chain, rows=rows, per=per):
            block = div(index, per)
            span = pl.ds(pl.multiple_of(rem(index, per) * rows, rows), rows) if per > 1 else slice(None)
            for side in range(2):
                received, kept = ins[4 * chain + 2 * side], ins[4 * chain + 2 * side + 1]
                outs[2 * chain + side][block, span, :] = (
                    received[block, span, :].astype(F32) + kept[block, span, :].astype(F32)
                ).astype(BF)

        loop(count * per, step)


def gate(arrays, after):
    count = len(arrays)
    return pl.pallas_call(
        lambda *refs: None,
        out_shape=[shape(*a.shape, dtype=a.dtype) for a in arrays],
        in_specs=[ANY] * (count + len(after)),
        out_specs=[ANY] * count,
        input_output_aliases={i: i for i in range(count)},
        cost_estimate=lasting(0.5),
        name="gate",
    )(*arrays, *after)


def pack_kernel(info, *refs, groups, after):
    count = sum(len(members) for _, members in groups)
    sources, rest = refs[:count], refs[count + after :]
    outs, (held, in_sems, out_sems) = rest[:-3], rest[-3:]
    spots = []
    at = 0
    for index, (layer, members) in enumerate(groups):
        rows = held.shape[1]
        piece_rows = rows // 4
        for quarter in range(4):
            row = quarter * piece_rows
            source = sources[at + quarter * len(members) // 4]
            src = source.at[layer, pl.ds(row % source.shape[1], piece_rows)]
            spots.append((index, quarter, held.at[index, pl.ds(row, piece_rows)], src))
        at += len(members)

    def arriving(place):
        _, _, spot, src = spots[place]
        return pltpu.make_async_copy(src, spot, in_sems.at[place])

    def leaving(index, which):
        out = outs[2 * index + (0 if which == 2 else 1)]
        rows = out.shape[0]
        src = held.at[index] if which == 2 else held.at[index, pl.ds(which * rows, rows)]
        return pltpu.make_async_copy(src, out, out_sems.at[2 * index + (0 if which == 2 else 1)])

    def by_parity(act):
        for parity in range(2):

            @pl.when(info[0] % 2 == parity)
            def _(parity=parity):
                act(parity)

    for place in range(len(spots)):
        arriving(place).start()
    for index in range(len(groups)):
        for quarter in range(4):
            arriving(4 * index + quarter).wait()
        by_parity(lambda parity: leaving(index, parity).start())
        leaving(index, 2).start()
    for index in range(len(groups)):
        by_parity(lambda parity: leaving(index, parity).wait())
        leaving(index, 2).wait()


def mod_kernel(condition, mod, mod_bias, q, v, cq, cv, up, out):
    narrow, units, columns = q.shape[1], up.shape[1], mod.shape[1]
    out[...] = jnp.zeros(out.shape, F32)
    for layer in range(LAYERS):
        row = pl.ds(layer, 1)
        out[layer, 0:SLOTS, 0:columns] = dot_nt(condition[...], mod[layer]) + mod_bias[
            row, :
        ].astype(F32)
        out[layer, 4:5, 0:units] = up[row, :].astype(F32)
        out[layer, 5:6, 0:narrow] = q[row, :].astype(F32)
        out[layer, 6:7, 0:narrow] = v[row, :].astype(F32)
        out[layer, 7:8, 0:narrow] = cq[row, :].astype(F32)
        out[layer, 4:5, 1024 : 1024 + narrow] = cv[row, :].astype(F32)


def assemble_kernel(info, *refs, narrow, units, columns):
    parts, (mods, narrows, ups) = refs[:4], refs[4:]
    narrows[...] = jnp.zeros(narrows.shape, F32)
    for rank in range(4):

        @pl.when(info[5] == rank)
        def _(rank=rank):
            for shard in range(4):
                part = parts[shard ^ rank]
                for layer in range(LAYERS):
                    mods[layer, :, shard * columns : (shard + 1) * columns] = part[
                        layer, 0:SLOTS, 0:columns
                    ]
                    ups[layer, :, shard * units : (shard + 1) * units] = part[layer, 4:5, 0:units]
                    at = slice(shard * narrow, (shard + 1) * narrow)
                    for row, source in ((0, 5), (2, 6), (3, 7)):
                        narrows[layer, row : row + 1, at] = part[
                            layer, source : source + 1, 0:narrow
                        ]
                    narrows[layer, 5:6, at] = part[layer, 4:5, 1024 : 1024 + narrow]


def collect_kernel(info, *refs, narrow, units, columns):
    stats, condition, out = refs[: 2 * LAYERS], refs[2 * LAYERS], refs[2 * LAYERS + 1]
    sums = refs[2 * LAYERS + 2]
    width = stats[0].shape[1]
    work = out
    out = refs[2 * LAYERS + 3]
    out[...] = jnp.zeros(out.shape, F32)
    for layer in range(LAYERS):
        sums[...] = stats[2 * layer][...] + stats[2 * layer + 1][...]
        base = 8 * layer
        out[base + 4 : base + 5, width : 2 * width] = sums[60:61, :]
        out[base + 5 : base + 6, 0:width] = sums[12:13, :]
        out[base + 5 : base + 6, width : 2 * width] = sums[36:37, :]
        for index in range(2):
            out[base + 6 + index : base + 7 + index, 512 : 512 + width] = condition[
                2 * layer + index : 2 * layer + index + 1, :
            ].astype(F32)
        for rank in range(4):

            @pl.when(info[5] == rank)
            def _(rank=rank, base=base):
                first = rank * columns
                for index in range(9):
                    low = max(first, index * width)
                    high = min(first + columns, (index + 1) * width)
                    if low < high:
                        row = (index // 3) * 24 + (index % 3) * 4
                        out[base : base + 4, low - first : high - first] = sums[
                            row : row + 4, low - index * width : high - index * width
                        ]
                out[base + 4 : base + 5, 0:units] = sums[61 + rank : 62 + rank, :]
                own = slice(rank * narrow, (rank + 1) * narrow)
                out[base + 6 : base + 7, 0:narrow] = sums[13:14, own]
                out[base + 6 : base + 7, 256 : 256 + narrow] = sums[14:15, own]
                out[base + 7 : base + 8, 0:narrow] = sums[37:38, own]
                out[base + 7 : base + 8, 256 : 256 + narrow] = sums[38:39, own]
    work[...] = out[...].astype(BF)


def spread_kernel(info, gathered, grad, bias_grad, q, v, cq, cv, up, o1, o2, o3, rows, conditions):
    count = gathered.shape[0]
    columns, part = grad.shape[2], grad.shape[1]
    width, narrow, units = conditions.shape[1], q.shape[1], up.shape[1]
    shift = lax.rem(width - info[8] * part, width)
    for index in range(count):
        for slot in range(SLOTS):
            row = 8 * (slot // 2) + 6 + slot % 2
            conditions[SLOTS * index + slot : SLOTS * index + slot + 1, :] = gathered[
                index ^ info[8], row : row + 1, 512 : 512 + width
            ].astype(F32)
    turned = pltpu.roll(conditions[...], shift, 1)[:, :part].T
    for layer in range(LAYERS):
        base = 8 * layer
        sums = jnp.zeros((8, gathered.shape[2]), F32)
        for index in range(count):
            values = gathered[index ^ info[8]].astype(F32)[base : base + 8]
            sums += values
            rows[SLOTS * index : SLOTS * (index + 1), :] = values[0:SLOTS, 0:columns]
        grad[layer] = jnp.dot(
            turned, rows[...], precision=lax.Precision.HIGHEST, preferred_element_type=F32
        )
        at = slice(layer, layer + 1)
        bias_grad[at, :] = jnp.sum(sums[0:SLOTS, 0:columns], axis=0, keepdims=True)
        up[at, :] = sums[4:5, 0:units]
        q[at, :] = sums[6:7, 0:narrow]
        v[at, :] = sums[6:7, 256 : 256 + narrow]
        cq[at, :] = sums[7:8, 0:narrow]
        cv[at, :] = sums[7:8, 256 : 256 + narrow]
        for out, row, lane in ((o1, 5, 0), (o2, 5, width), (o3, 4, width)):
            own = jnp.broadcast_to(sums[row : row + 1, lane : lane + width], (8, width))
            out[at, :] = pltpu.roll(own, shift, 1)[0:1, :part]


def narrow_finish_kernel(*refs, spots):
    parts, outs = refs[: 2 * len(spots)], refs[2 * len(spots) :]
    step = 3 * LANES
    for chain, places in enumerate(spots):
        values = parts[2 * chain][0].astype(F32) + parts[2 * chain + 1][0].astype(F32)
        for at, (layer, pair) in enumerate(places):
            both = values[:, at * step : (at + 1) * step]
            first = jnp.concatenate(
                [both[:, :LANES], both[:, 2 * LANES : 2 * LANES + HEAD_WIDTH]], axis=1
            )
            second = jnp.concatenate(
                [both[:, LANES : 2 * LANES], both[:, 2 * LANES + HEAD_WIDTH :]], axis=1
            )
            for out, matrix in zip(outs[2 * pair : 2 * pair + 2], (first, second)):
                out[layer] = matrix if out.shape[1:] == matrix.shape else matrix.T


def wide_finish_kernel(*refs):
    parts, (up, down) = refs[: 2 * LAYERS], refs[2 * LAYERS :]
    width = up.shape[2]
    for layer in range(LAYERS):
        values = parts[2 * layer][0].astype(F32) + parts[2 * layer + 1][0].astype(F32)
        up[layer] = values[:, :width]
        down[layer] = values[:, width:]


def join_kernel(info, rows, other, out):
    share = rows.shape[0]
    for core in range(2):

        @pl.when(info[5] % 2 == core)
        def _(core=core):
            out[pl.ds(core * share, share), :] = rows[...]
            out[pl.ds((1 - core) * share, share), :] = other[...]


def tensor_hop(values, step):
    return lax.ppermute(values, "tensor", [(i, i ^ step) for i in range(4)])


def dp_hop(values, step):
    size = lax.axis_size("dp")
    return lax.ppermute(values, "dp", [(i, i ^ step) for i in range(size)])


def time_features(moments, width):
    half = width // 2
    rates = jnp.exp(-math.log(10000.0) * jnp.arange(half, dtype=F32) / half)
    angles = moments.astype(F32)[:, None] * rates[None, :]
    return jnp.concatenate([jnp.cos(angles), jnp.sin(angles)], axis=1)


def shards(
    tokens,
    text,
    timesteps,
    item_frames,
    cotangent,
    self_query,
    self_query_bias,
    self_key,
    self_value,
    self_value_bias,
    self_output,
    self_output_bias,
    cross_query,
    cross_query_bias,
    cross_key,
    cross_value,
    cross_value_bias,
    cross_output,
    cross_output_bias,
    hidden_up,
    hidden_up_bias,
    hidden_down,
    hidden_down_bias,
    modulation,
    modulation_bias,
):
    frames, width = tokens.shape
    words = text.shape[1]
    columns = modulation.shape[2]
    narrow = self_query.shape[2]
    units = hidden_up.shape[2]
    rank = lax.axis_index("tensor")
    me = lax.axis_index("dp")
    size = lax.axis_size("dp")
    core = rank % 2
    share = frames // 2
    blocks = share // UNIT
    unit = width // size
    turn = lambda values: jnp.swapaxes(values, 1, 2)

    order = jnp.arange(SLOTS, dtype=jnp.int32)
    ends = jnp.sum(jnp.where(order[:, None] <= order[None, :], item_frames[:, None], 0), axis=0)
    turned = (jnp.arange(frames // UNIT, dtype=jnp.int32) + core * blocks) % (2 * blocks)
    slots = jnp.sum((turned[:, None] * UNIT >= ends[None, :]).astype(jnp.int32), axis=1)
    places = jnp.stack([rank, rank // 2, rank ^ 1, me]).astype(jnp.int32)
    info = jnp.concatenate([(rank * 2 + me % 2)[None].astype(jnp.int32), slots, places])

    condition = jax.nn.silu(time_features(timesteps, width)).astype(BF)
    mine = plain(
        mod_kernel,
        "modulation_rows",
        None,
        [
            condition,
            turn(modulation),
            modulation_bias,
            self_query_bias,
            self_value_bias,
            cross_query_bias,
            cross_value_bias,
            hidden_up_bias,
        ],
        [shape(LAYERS, 8, -(-columns // LANES) * LANES)],
    )
    others = [tensor_hop(mine, 1), tensor_hop(mine, 2)]
    others.append(tensor_hop(others[0], 2))
    mods, narrow_biases, up_biases = plain(
        partial(assemble_kernel, narrow=narrow, units=units, columns=columns),
        "modulation_of_all",
        info,
        [mine, *others],
        [
            shape(LAYERS, SLOTS, 4 * columns),
            shape(LAYERS, 8, 4 * narrow),
            shape(LAYERS, 1, 4 * units),
        ],
    )
    out_biases = [
        b.reshape(LAYERS, 1, width) for b in (self_output_bias, cross_output_bias, hidden_down_bias)
    ]

    def pack(members, after):
        outs = [shape(width // part, width, dtype=BF) for _ in members for part in (1, 2)]
        arrays = [a for _, some in members for a in some]
        return pl.pallas_call(
            partial(
                pack_kernel,
                groups=[(layer, [None] * len(some)) for layer, some in members],
                after=len(after),
            ),
            out_shape=outs,
            in_specs=[SMALL] + [ANY] * (len(arrays) + len(after)),
            out_specs=[ANY] * len(outs),
            scratch_shapes=[
                pltpu.VMEM((len(members), width, width), BF),
                pltpu.SemaphoreType.DMA((4 * len(members),)),
                pltpu.SemaphoreType.DMA((2 * len(members),)),
            ],
            compiler_params=pltpu.CompilerParams(vmem_limit_bytes=VMEM_BYTES),
            cost_estimate=lasting(1.0),
            name="pack_weights",
        )(info, *arrays, *after)

    kinds = (
        [turn(self_query), turn(self_key), turn(self_value), self_output],
        [turn(cross_query), turn(cross_key), turn(cross_value), cross_output],
        [hidden_up],
        [hidden_down],
    )
    all_groups = [(index // 4, kinds[index % 4]) for index in range(4 * LAYERS)]
    packed = [*pack(all_groups[:1], []), *pack(all_groups[1:], [mine])]
    firsts = [packed[2 * index + 1] for index in range(4 * LAYERS)]
    owns = [packed[2 * index] for index in range(4 * LAYERS)]
    along_x, along_y, over_x, over_y, sibs = [[None] * (4 * LAYERS) for _ in range(5)]

    def leave(index):
        along_x[index] = tensor_hop(firsts[index], 2)
        sibs[index] = tensor_hop(owns[index], 1)

    def go_on(index):
        along_y[index] = dp_hop(along_x[index], 1)
        over_x[index] = tensor_hop(along_x[index], 1)

    def end(index):
        over_y[index] = tensor_hop(along_y[index], 1)

    def weights_of(index):
        return [
            owns[index],
            sibs[index],
            along_x[index],
            along_y[index],
            over_x[index],
            over_y[index],
        ]

    def open_gate(after, leaving=(), at_x=(), at_y=()):
        places = [(firsts, i) for i in leaving]
        places += [(along_x, i) for i in at_x] + [(along_y, i) for i in at_y]
        opened = gate([values[i] for values, i in places], after)
        for (values, i), array in zip(places, opened):
            values[i] = array
        for i in leaving:
            leave(i)
        for i in at_x:
            go_on(i)
        for i in at_y:
            end(i)
        return list(opened)

    leave(0)
    open_gate([mine], [], [0])
    open_gate([mods], [1, 2, 3])
    go_on(1)
    end(0)

    text_rows = jnp.pad(text, ((0, 0), (0, LANES - words), (0, 0))).reshape(-1, width)
    whole = pltpu.VMEM((width, width), BF)
    four = pltpu.VMEM((4, width, units), BF)
    floats = pltpu.VMEM((share, width), F32)
    lows = pltpu.VMEM((share, width), BF)
    sems = lambda n: pltpu.SemaphoreType.DMA((n,))
    frame_low = shape(share, width, dtype=BF)
    frame_high = shape(share, width)
    frame_wide = shape(share, 4 * units, dtype=BF)
    two_low = shape(2, share, width, dtype=BF)
    two_text = shape(2, SLOTS * LANES, width, dtype=BF)
    logs = shape(16, share)
    stat_shape = shape(72, width)

    def soft_scratch(keys):
        return dict(
            logs=pltpu.VMEM((share, LANES), F32),
            scores=pltpu.VMEM((UNIT, keys), F32),
            probs=pltpu.VMEM((UNIT, keys), BF),
            sums=pltpu.VMEM((2, UNIT, 2 * LANES), F32),
            peaks=pltpu.VMEM((2, UNIT, LANES), F32),
            wo=whole,
            sum0=floats,
        )

    x = lax.dynamic_slice_in_dim(tokens, core * share, share).astype(F32)
    kept = []
    for layer in range(LAYERS):
        first = 4 * layer
        mod = (mods, (layer,))
        biases = (narrow_biases, (layer,))
        entry1, kv = run(
            kv_kernel,
            "self_keys_values",
            info,
            dict(x=x),
            dict(mod=mod, biases=biases),
            weights_of(first),
            dict(entry=frame_low, kv=two_low),
            {},
            dict(w=pltpu.VMEM((2, width, width), BF), sems=sems(8)),
            [along_x[1], *owns[1:]] if layer == 0 else [],
            3.0,
        )
        kv_sib = tensor_hop(kv, 1)
        opened = open_gate([entry1], [4, 5], [], [1]) if layer == 0 else open_gate([entry1], [], [6])
        (q,) = run(
            q_kernel,
            "self_query",
            info,
            dict(entry=entry1),
            dict(biases=biases),
            weights_of(first),
            dict(q=frame_low),
            {},
            dict(w=whole, sems=sems(4)),
            [],
            15.0,
        )
        x1, mixed1, lse1, branch1 = run(
            self_kernel,
            "self_attention",
            info,
            dict(q=q, kv_own=kv, kv_sib=kv_sib, x=x),
            dict(mod=mod, bias=(out_biases[0], (layer,))),
            weights_of(first),
            dict(out=frame_high, mixed=frame_low, lse=logs, branch=frame_low),
            {},
            dict(
                marks=pltpu.VMEM((2 * share, LANES), BF),
                sems=sems(4),
                **soft_scratch(2 * share),
            ),
            opened,
            8.0,
        )
        opened = open_gate([x1], [6, 7], [2]) if layer == 0 else open_gate([x1], [], [7], [5, 6])
        x2, entry2, cq, ckv, mixed2, lse2, branch2 = run(
            partial(cross_kernel, words=words),
            "cross_attention",
            info,
            dict(x=x1, text=text_rows),
            dict(mod=mod, biases=biases, bias=(out_biases[1], (layer,))),
            weights_of(first + 1),
            dict(
                out=frame_high,
                entry=frame_low,
                q=frame_low,
                kv=two_text,
                mixed=frame_low,
                lse=logs,
                branch=frame_low,
            ),
            {},
            dict(
                w=pltpu.VMEM((3, width, width), BF), sems=sems(16), **soft_scratch(LANES)
            ),
            opened,
            6.0,
        )
        opened = open_gate([x2], [], [3, 4], [2]) if layer == 0 else open_gate([x2], [], [], [7])
        if layer == 0:
            end(3)
        results = run(
            lambda info, work, w: hidden_kernel(info, work, w[:6], w[6:]),
            "feed_forward",
            info,
            dict(x=x2),
            dict(mod=mod, up_bias=(up_biases, (layer,)), bias=(out_biases[2], (layer,))),
            weights_of(first + 2) + weights_of(first + 3),
            dict(
                out=frame_high,
                entry=frame_low,
                active=frame_wide,
                slope=frame_wide,
                branch=frame_low,
                **(dict(low=frame_low) if layer == LAYERS - 1 else {}),
            ),
            {},
            dict(
                up=four,
                down=four,
                before=pltpu.VMEM((share, TILE), F32),
                sum0=floats,
                sems=sems(8),
                down_sems=sems(8),
            ),
            opened,
            7.0,
        )
        x3, entry3, active, slope, branch3 = results[:5]
        if layer == 0:
            open_gate([x3], [], [5], [4])
        kept.append(
            dict(
                x=x,
                entry1=entry1,
                q=q,
                kv=kv,
                kv_sib=kv_sib,
                mixed1=mixed1,
                lse1=lse1,
                branch1=branch1,
                x1=x1,
                entry2=entry2,
                cq=cq,
                ckv=ckv,
                mixed2=mixed2,
                lse2=lse2,
                branch2=branch2,
                x2=x2,
                entry3=entry3,
                active=active,
                slope=slope,
                branch3=branch3,
            )
        )
        x = x3

    def join(rows):
        return plain(
            join_kernel,
            "join_rows",
            info,
            [rows, tensor_hop(rows, 1)],
            [shape(2 * share, width, dtype=BF)],
        )

    output = join(results[5])

    chains = {}

    def start(name, send, keep):
        view = (size, unit, send.shape[1])
        chains[name] = (tensor_hop(send, 1).reshape(view), keep.reshape(view), 0)

    def held(*names):
        return [chains[name][1] for name in names]

    def advance(names, after=()):
        names = [n for n in names if 2 ** chains[n][2] < size]
        if not names:
            return
        ins, in_specs, outs, out_specs = [], [], [], []
        cuts = 2 if all(chains[name][0].shape[2] % (4 * LANES) == 0 for name in names) else 1
        for name in names:
            received, kept_part, bit = chains[name]
            count, unit, columns = received.shape
            for side in range(2):

                def at(i, info, bit=bit, side=side):
                    return (0, ((info[8] >> bit) & 1) ^ side, 0, i)

                for part in (received, kept_part):
                    ins.append(part.reshape(count // 2, 2, unit, columns))
                    in_specs.append(pl.BlockSpec((count // 2, None, unit, columns // cuts), at))
                outs.append(shape(count // 2, unit, columns, dtype=BF))
                out_specs.append(
                    pl.BlockSpec((count // 2, unit, columns // cuts), lambda i, info: (0, 0, i))
                )
        results = pl.pallas_call(
            partial(merge_kernel, chains=len(names), after=len(after)),
            grid_spec=pltpu.PrefetchScalarGridSpec(
                num_scalar_prefetch=1,
                grid=(cuts,),
                in_specs=in_specs + [ANY] * len(after),
                out_specs=out_specs,
            ),
            out_shape=outs,
            compiler_params=pltpu.CompilerParams(vmem_limit_bytes=VMEM_BYTES),
            cost_estimate=lasting(1.5),
            name="merge_grads",
        )(info, *ins, *after)
        for index, name in enumerate(names):
            bit = chains[name][2]
            hold, give = results[2 * index : 2 * index + 2]
            chains[name] = (dp_hop(give, 2**bit), hold, bit + 1)

    full = pl.BlockSpec((share, width), lambda i, info: (0, 0))

    def narrow_grads(members, after=()):
        lefts, which = [], []
        for left, _, _ in members:
            at = [i for i, seen in enumerate(lefts) if seen is left]
            if not at:
                lefts.append(left)
                at = [len(lefts) - 1]
            which.append(at[0])
        specs = []
        for _, right, first in members:
            if first is None:
                specs.append(pl.BlockSpec((share, 2 * narrow), lambda i, info: (0, info[6])))
            else:
                specs.append(
                    pl.BlockSpec(
                        (None, share, 2 * narrow), lambda i, info, first=first: (first, 0, info[6])
                    )
                )
        result = pl.BlockSpec((width, len(members) * narrow), lambda i, info: (0, 0))
        return pl.pallas_call(
            partial(narrow_grad_kernel, lefts=tuple(which)),
            grid_spec=pltpu.PrefetchScalarGridSpec(
                num_scalar_prefetch=1,
                grid=(1,),
                in_specs=[full] * len(lefts) + specs + [ANY] * len(after),
                out_specs=[result] * 2,
                scratch_shapes=[
                    pltpu.VMEM((len(members), width, 2 * narrow), F32),
                    pltpu.VMEM((len(lefts), width, share), BF),
                ],
            ),
            out_shape=[shape(width, len(members) * narrow, dtype=BF)] * 2,
            compiler_params=pltpu.CompilerParams(vmem_limit_bytes=VMEM_BYTES),
            cost_estimate=lasting(15.0),
            name="narrow_grads",
        )(info, *lefts, *[right for _, right, _ in members], *after)

    def wide_grads(entry, gb, d_before, active, after=()):
        sib = pl.BlockSpec((share, units), lambda i, info: (0, info[7]))
        own = pl.BlockSpec((share, units), lambda i, info: (0, info[5]))
        result = pl.BlockSpec((width, 2 * units), lambda i, info: (0, 0))
        return pl.pallas_call(
            wide_grad_kernel,
            grid_spec=pltpu.PrefetchScalarGridSpec(
                num_scalar_prefetch=1,
                grid=(1,),
                in_specs=[full, full, sib, own, sib, own] + [ANY] * len(after),
                out_specs=[result] * 2,
                scratch_shapes=[pltpu.VMEM((2, width, share), BF)],
            ),
            out_shape=[shape(width, 2 * units, dtype=BF)] * 2,
            compiler_params=pltpu.CompilerParams(vmem_limit_bytes=VMEM_BYTES),
            cost_estimate=lasting(15.0),
            name="wide_grads",
        )(info, entry, gb, d_before, d_before, active, active, *after)

    g = lax.dynamic_slice_in_dim(cotangent, core * share, share).astype(F32)
    sums = []
    last = LAYERS - 1
    for layer in reversed(range(LAYERS)):
        first = 4 * layer
        k = kept[layer]
        mod = (mods, (layer,))
        older = [f"c{layer + 1}", f"s{layer + 1}"] if layer < last else []
        f_name, c_name, s_name = [f"{kind}{layer}" for kind in "fcs"]
        more = held(f"f{layer + 1}", *older) if older else [output]
        g, gb3, d_before, stats = run(
            lambda info, work, w: hidden_back_kernel(info, work, w[:6], w[6:]),
            "feed_forward_back",
            info,
            dict(g=g, branch=k["branch3"], slope=k["slope"], x=k["x2"]),
            dict(mod=mod),
            weights_of(first + 2) + weights_of(first + 3),
            dict(out=frame_high, gb=frame_low, d_before=frame_wide),
            dict(stats=stat_shape),
            dict(
                up=four,
                down=four,
                before=pltpu.VMEM((share, TILE), F32),
                de=floats,
                sems=sems(8),
                down_sems=sems(8),
            ),
            more,
            7.0,
        )
        if older:
            advance(older, [gb3])
        start(f_name, *wide_grads(k["entry3"], gb3, d_before, k["active"], held(*older)))
        g, gb2, dcq, dckv, stats = run(
            partial(cross_back_kernel, words=words),
            "cross_attention_back",
            info,
            dict(g=g, branch=k["branch2"], q=k["cq"], kv=k["ckv"], lse=k["lse2"], x=k["x1"]),
            dict(mod=mod, early=(stats, ())),
            weights_of(first + 1),
            dict(out=frame_high, gb=frame_low, dq=frame_low, dkv=two_text),
            dict(stats=stat_shape),
            dict(
                wq=whole,
                wo=whole,
                d_mixed=lows,
                de=floats,
                dkv_sum=pltpu.VMEM(two_text.shape, F32),
                sems=sems(8),
            ),
            held(f_name, *older),
            7.0,
        )
        advance([f_name, *older], [g])
        cross_members = [
            (k["entry2"], dcq, None),
            (text_rows, dckv, 0),
            (text_rows, dckv, 1),
            (gb2, k["mixed2"], None),
        ]
        early_c = []
        if layer == 0:
            start(c_name, *narrow_grads(cross_members, held(f_name)))
            early_c = [c_name]
        gb1, dq, dkv_own, dkv_give, stats = run(
            self_back_kernel,
            "self_attention_back",
            info,
            dict(
                g=g, branch=k["branch1"], q=k["q"], kv_own=k["kv"], kv_sib=k["kv_sib"], lse=k["lse1"]
            ),
            dict(mod=mod, early=(stats, ())),
            weights_of(first),
            dict(gb=frame_low, dq=frame_low, dkv_own=two_low, dkv_give=two_low),
            dict(stats=stat_shape),
            dict(
                wo=whole,
                d_mixed=lows,
                values=pltpu.VMEM((2 * share, LANES), BF),
                marked=pltpu.VMEM((2 * share, 2 * LANES), BF),
                turned=pltpu.VMEM((2, LANES, 2 * share), BF),
                lefts=pltpu.VMEM((2 * share, LANES), BF),
                grads=pltpu.VMEM((2 * share, LANES), BF),
                scores=pltpu.VMEM((2 * share, UNIT), F32),
                rises=pltpu.VMEM((2 * share, UNIT), F32),
                probs=pltpu.VMEM((2 * share, 2 * share), BF),
                d_scores=pltpu.VMEM((2 * share, 2 * share), BF),
                dq_t=pltpu.VMEM((blocks, LANES, UNIT), F32),
                dkv=pltpu.VMEM((2, 2 * share, width), BF),
                sems=sems(4),
            ),
            held(f_name, *older, *early_c),
            13.0,
        )
        dkv_sib = tensor_hop(dkv_give, 1)
        advance([f_name, *older[1:], *early_c], [dq])
        self_members = [(k["entry1"], dq, None), (gb1, k["mixed1"], None)]
        if layer > 0:
            start(c_name, *narrow_grads(cross_members, held(f_name)))
        else:
            start("a0", *narrow_grads(self_members, held(f_name)))
            self_members = []
        results = run(
            qkv_back_kernel,
            "self_qkv_back",
            info,
            dict(dkv_own=dkv_own, dkv_sib=dkv_sib, dq=dq, x=k["x"], g=g),
            dict(mod=mod, early=(stats, ())),
            weights_of(first),
            dict(
                out=frame_high, dkv=two_low, **(dict(low=frame_low) if layer == 0 else {})
            ),
            dict(stats=stat_shape),
            dict(w=pltpu.VMEM((3, width, width), BF), de=floats, sems=sems(12)),
            held(f_name, *older, c_name, *(["a0"] if layer == 0 else [])),
            4.0,
        )
        g, dkv, stats = results[0], results[1], results[-1]
        self_members += [(k["entry1"], dkv, 0), (k["entry1"], dkv, 1)]
        start(s_name, *narrow_grads(self_members))
        advance([f_name, c_name, *(["a0"] if layer == 0 else [])], held(s_name))
        sums = [stats, tensor_hop(stats, 1)] + sums
    input_grad = join(results[2])
    vectors = plain(
        partial(collect_kernel, narrow=narrow, units=units, columns=columns),
        "collect_sums",
        info,
        [*sums, condition],
        [shape(16, mine.shape[2], dtype=BF)],
        [pltpu.VMEM(stat_shape.shape, F32), pltpu.VMEM((16, mine.shape[2]), F32)],
    )
    gathered = vectors[None]
    hop = size // 2
    while hop:
        both = jnp.stack([gathered, dp_hop(gathered, hop)], axis=1)
        gathered = both.reshape(-1, *vectors.shape)
        hop //= 2
    previous = held("f0", "c0", "a0")
    while any(2 ** chain[2] < size for chain in chains.values()):
        advance(list(chains), previous)
        previous = held(*chains)

    def parts_of(*names):
        return [part.reshape(1, unit, -1) for name in names for part in chains[name][:2]]

    up_grad, down_grad = plain(
        wide_finish_kernel,
        "finish_wide",
        None,
        parts_of(*[f"f{layer}" for layer in range(LAYERS)]),
        [shape(LAYERS, unit, units)] * 2,
    )
    straight, across = shape(LAYERS, unit, narrow), shape(LAYERS, narrow, unit)
    c_grads = plain(
        partial(narrow_finish_kernel, spots=[[(l, 0), (l, 1)] for l in range(LAYERS)]),
        "finish_narrow",
        None,
        parts_of(*[f"c{layer}" for layer in range(LAYERS)]),
        [straight, straight, straight, across],
    )
    s_grads = plain(
        partial(
            narrow_finish_kernel,
            spots=[[(0, 0)], [(0, 1)]] + [[(l, 0), (l, 1)] for l in range(1, LAYERS)],
        ),
        "finish_narrow",
        None,
        parts_of("a0", *[f"s{layer}" for layer in range(LAYERS)]),
        [straight, across, straight, straight],
    )
    small = plain(
        spread_kernel,
        "spread_sums",
        info,
        [gathered],
        [shape(LAYERS, unit, columns), shape(LAYERS, columns)]
        + [shape(LAYERS, narrow)] * 4
        + [shape(LAYERS, units)]
        + [shape(LAYERS, unit)] * 3,
        [pltpu.VMEM((SLOTS * size, columns), F32), pltpu.VMEM((SLOTS * size, width), F32)],
    )
    mod_grad, mod_bias_grad, q_sum, v_sum, cq_sum, cv_sum, up_sum, o1, o2, o3 = small
    q_grad, o_grad, k_grad, v_grad = s_grads
    return (
        output,
        input_grad,
        q_grad,
        q_sum,
        k_grad,
        v_grad,
        v_sum,
        o_grad,
        o1,
        c_grads[0],
        cq_sum,
        c_grads[1],
        c_grads[2],
        cv_sum,
        c_grads[3],
        o2,
        up_grad,
        up_sum,
        turn(down_grad),
        o3,
        mod_grad,
        mod_bias_grad,
    )


def solution(mesh):
    dp, tensor = "dp", "tensor"
    columns, vector = P(None, None, tensor), P(None, tensor)
    matrix, turned, spread = P(None, dp, tensor), P(None, tensor, dp), P(None, dp)
    placed = (
        P(dp, None),
        P(dp, None, None),
        P(dp),
        P(dp),
        P(dp, None),
        columns,
        vector,
        columns,
        columns,
        vector,
        P(None, tensor, None),
        P(),
        columns,
        vector,
        columns,
        columns,
        vector,
        P(None, tensor, None),
        P(),
        columns,
        vector,
        P(None, tensor, None),
        P(),
        columns,
        vector,
    )
    results = (
        P(dp, None),
        P(dp, None),
        matrix,
        vector,
        matrix,
        matrix,
        vector,
        turned,
        spread,
        matrix,
        vector,
        matrix,
        matrix,
        vector,
        turned,
        spread,
        matrix,
        vector,
        turned,
        spread,
        matrix,
        vector,
    )
    return jax.shard_map(
        shards, mesh=mesh, in_specs=placed, out_specs=results, check_vma=False
    )
```

```python
from functools import partial
import math

import jax
import jax.numpy as jnp
from jax import lax
from jax.experimental import pallas as pl
from jax.experimental.pallas import tpu as pltpu
from jax.sharding import PartitionSpec as P

HEAD_WIDTH = 64
UNIT = 256
LAYERS = 2
WINDOW = 1024
EPSILON = 1e-06
LANES = 128
CHUNK = 64
ROLLED = (True, False)
SLOTS = WINDOW // UNIT
FAR = -1e30
VMEM_BYTES = 62 * 1024 * 1024
BF = jnp.bfloat16
F32 = jnp.float32
ROOT = math.sqrt(2.0 / math.pi)
CUBIC = 0.044715


def dot_nn(left, right):
    return jnp.dot(left, right, preferred_element_type=F32)


def dot_nt(left, right):
    return lax.dot_general(left, right, (((1,), (1,)), ((), ())), preferred_element_type=F32)


def dot_tn(left, right):
    return lax.dot_general(left, right, (((0,), (0,)), ((), ())), preferred_element_type=F32)


SMALL = pl.BlockSpec(memory_space=pltpu.SMEM)
NEAR = pl.BlockSpec(memory_space=pltpu.VMEM)
ANY = pl.BlockSpec(memory_space=pl.ANY)


class Work:
    def __init__(self, ins, outs, scratch, in_sems, out_sems):
        self.ins, self.outs, self.scratch, self.out_sems = ins, outs, scratch, out_sems
        self.copies, self.waited, self.flushed = {}, set(), []
        for index, (name, (ref, buffer)) in enumerate(ins.items()):
            self.copies[name] = pltpu.make_async_copy(ref, buffer, in_sems.at[index])
            self.copies[name].start()

    def __getattr__(self, name):
        if name in self.__dict__["ins"]:
            return self.ins[name][1]
        if name in self.__dict__["outs"]:
            return self.outs[name][1]
        return self.__dict__["scratch"][name]

    def has(self, name):
        return name in self.outs

    def send(self, name, source, *at):
        ref = self.outs[name][0]
        copy = pltpu.make_async_copy(
            source, ref.at[at] if at else ref, self.out_sems.at[len(self.flushed)]
        )
        copy.start()
        self.flushed.append(copy)

    def need(self, *names):
        for name in names:
            if name not in self.waited:
                self.waited.add(name)
                self.copies[name].wait()

    def flush(self, name, *at):
        ref, buffer = self.outs[name]
        if at:
            ref, buffer = ref.at[at], buffer.at[at]
        copy = pltpu.make_async_copy(buffer, ref, self.out_sems.at[len(self.flushed)])
        copy.start()
        self.flushed.append(copy)

    def finish(self):
        self.need(*self.ins)
        for copy in self.flushed:
            copy.wait()


def run(body, name, info, ins, small, weights, outs, small_outs, scratch, after=(), cost=1.0):
    in_names, out_names, names = list(ins), list(outs), list(scratch)
    small_names, small_out_names = list(small), list(small_outs)
    counts = [1, len(in_names), len(small), len(weights), len(after), len(outs), len(small_outs)]

    def kernel(*refs):
        refs = list(refs)
        parts = []
        for count in counts:
            parts.append(refs[:count])
            refs = refs[count:]
        (info_ref,), in_refs, small_refs, weight_refs, _, out_refs, small_out_refs = parts
        in_bufs, refs = refs[: len(in_names)], refs[len(in_names) :]
        out_bufs, refs = refs[: len(out_names)], refs[len(out_names) :]
        rest, (in_sems, out_sems) = refs[:-2], refs[-2:]
        extra = {}
        rest = list(rest)
        for key in names:
            many = isinstance(scratch[key], list)
            size = len(scratch[key]) if many else 1
            extra[key] = rest[:size] if many else rest[0]
            rest = rest[size:]
        for key, ref in zip(small_names, small_refs):
            index = small[key][1]
            extra[key] = ref.at[index] if index else ref
        extra.update(zip(small_out_names, small_out_refs))
        work = Work(
            dict(zip(in_names, zip(in_refs, in_bufs))),
            dict(zip(out_names, zip(out_refs, out_bufs))),
            extra,
            in_sems,
            out_sems,
        )
        body(info_ref, work, weight_refs)
        work.finish()

    buffer = lambda a: pltpu.VMEM(a.shape, a.dtype)
    flat = []
    for value in scratch.values():
        flat += value if isinstance(value, list) else [value]
    results = pl.pallas_call(
        kernel,
        out_shape=[outs[n] for n in out_names] + [small_outs[n] for n in small_out_names],
        in_specs=[SMALL]
        + [ANY] * len(ins)
        + [NEAR] * len(small)
        + [ANY] * (len(weights) + len(after)),
        out_specs=[ANY] * len(outs) + [NEAR] * len(small_outs),
        scratch_shapes=[buffer(ins[n]) for n in in_names]
        + [buffer(outs[n]) for n in out_names]
        + flat
        + [pltpu.SemaphoreType.DMA((max(len(ins), 1),)), pltpu.SemaphoreType.DMA((32,))],
        compiler_params=pltpu.CompilerParams(vmem_limit_bytes=VMEM_BYTES),
        cost_estimate=lasting(cost),
        name=name,
    )(info, *ins.values(), *[array for array, _ in small.values()], *weights, *after)
    return results


def plain(body, name, info, ins, outs, scratch=()):
    results = pl.pallas_call(
        body,
        out_shape=outs,
        in_specs=([] if info is None else [SMALL]) + [NEAR] * len(ins),
        out_specs=[NEAR] * len(outs),
        scratch_shapes=list(scratch),
        compiler_params=pltpu.CompilerParams(vmem_limit_bytes=VMEM_BYTES),
        cost_estimate=lasting(1.0),
        name=name,
    )(*([] if info is None else [info]), *ins)
    return results if len(outs) > 1 else results[0]


def lasting(units):
    return pl.CostEstimate(flops=int(units * 0.4e9), bytes_accessed=1000, transcendentals=0)


def shape(*dims, dtype=F32):
    return jax.ShapeDtypeStruct(dims, dtype)


def start_rows(refs, place, plan, sems):
    own, sib, xa, ya, xb, yb = refs
    half = own.shape[0] // 2
    for rank in range(4):
        for parity in range(2):

            @pl.when(place == rank * 2 + parity)
            def _(rank=rank, parity=parity):
                for index, (shard, row, rows, dst) in enumerate(plan):
                    step = shard ^ rank
                    if step < 2:
                        src = (own, sib)[step].at[pl.ds(row, rows)]
                    else:
                        first, second = ((xa, ya), (xb, yb))[step - 2]
                        part = row // half
                        src = (first if part == parity else second).at[pl.ds(row - part * half, rows)]
                    pltpu.make_async_copy(src, dst, sems.at[index]).start()


def wait_rows(refs, plan, sems, which):
    for index in which:
        _, row, rows, dst = plan[index]
        pltpu.make_async_copy(refs[0].at[pl.ds(0, rows)], dst, sems.at[index]).wait()


def plan_of(buffers, first, rows):
    return [
        (shard, (first + which) * rows, rows, dst.at[pl.ds(shard * rows, rows)])
        for which, dst in enumerate(buffers)
        for shard in range(4)
    ]


def norm_rows(values):
    mean = jnp.mean(values, axis=-1, keepdims=True)
    center = values - mean
    factor = lax.rsqrt(jnp.mean(center * center, axis=-1, keepdims=True) + EPSILON)
    return center * factor, factor


def piece(mod, slot, index):
    width = mod.shape[1] // 9
    return mod[pl.ds(slot, 1), index * width : (index + 1) * width]


def entry_rows(x, mod, info, index, out):
    for block in range(x.shape[0] // UNIT):
        slot = info[1 + block]
        shift = piece(mod, slot, index)
        scale = 1.0 + piece(mod, slot, index + 1)

        def step(turn, carry):
            rows = pl.ds(pl.multiple_of(block * UNIT + turn * CHUNK, CHUNK), CHUNK)
            normed, _ = norm_rows(x[rows, :])
            out[rows, :] = (normed * scale + shift).astype(BF)
            return carry

        lax.fori_loop(0, UNIT // CHUNK, step, 0, unroll=True)


def residual_rows(x, mod, info, index, branch, branch_out, out, low=None):
    for block in range(x.shape[0] // UNIT):
        gate = piece(mod, info[1 + block], index)

        def step(turn, carry):
            rows = pl.ds(pl.multiple_of(block * UNIT + turn * CHUNK, CHUNK), CHUNK)
            values = branch[rows, :]
            branch_out[rows, :] = values.astype(BF)
            result = x[rows, :] + gate * values
            out[rows, :] = result
            if low is not None:
                low[rows, :] = result.astype(BF)
            return carry

        lax.fori_loop(0, UNIT // CHUNK, step, 0, unroll=True)


def fold(values):
    return jnp.sum(values.reshape(values.shape[0] // 8, 8, values.shape[1]), axis=0)


def total(values):
    return jnp.sum(values, axis=0, keepdims=True)


def gate_back(g, mod, info, index, branch, gb, stats):
    width = g.shape[1]
    sums = jnp.zeros((8, width), F32)
    for block in range(g.shape[0] // UNIT):
        slot = info[1 + block]
        gate = piece(mod, slot, index)

        def step(turn, carry):
            rows = pl.ds(pl.multiple_of(block * UNIT + turn * CHUNK, CHUNK), CHUNK)
            grad = g[rows, :]
            low = (gate * grad).astype(BF)
            gb[rows, :] = low
            return (
                carry[0] + fold(low.astype(F32)),
                carry[1] + fold(grad * branch[rows, :].astype(F32)),
            )

        sums, rows_sum = lax.fori_loop(
            0, UNIT // CHUNK, step, (sums, jnp.zeros((8, width), F32)), unroll=True
        )
        stats[pl.ds(8 + slot, 1), :] += total(rows_sum)
    stats[12:13, :] = total(sums)


def norm_back_rows(x, g, de, mod, info, index, out, stats, low=None):
    width = x.shape[1]
    for block in range(x.shape[0] // UNIT):
        slot = info[1 + block]
        scale = 1.0 + piece(mod, slot, index + 1)

        def step(turn, carry):
            rows = pl.ds(pl.multiple_of(block * UNIT + turn * CHUNK, CHUNK), CHUNK)
            normed, factor = norm_rows(x[rows, :])
            grad = de[rows, :]
            inner = grad * normed
            dn = grad * scale
            mean = jnp.mean(dn, axis=-1, keepdims=True)
            along = jnp.mean(dn * normed, axis=-1, keepdims=True)
            result = g[rows, :] + factor * (dn - mean - normed * along)
            out[rows, :] = result
            if low is not None:
                low[rows, :] = result.astype(BF)
            return (carry[0] + fold(grad), carry[1] + fold(inner))

        zero = jnp.zeros((8, width), F32)
        shift_sum, scale_sum = lax.fori_loop(0, UNIT // CHUNK, step, (zero, zero), unroll=True)
        stats[pl.ds(slot, 1), :] += total(shift_sum)
        stats[pl.ds(4 + slot, 1), :] += total(scale_sum)


def lane_ids(rows):
    return lax.broadcasted_iota(jnp.int32, (rows, LANES), 1)


def head_half(values, half):
    ids = lane_ids(values.shape[0])
    keep = ids < HEAD_WIDTH if half == 0 else ids >= HEAD_WIDTH
    return jnp.where(keep, values.astype(F32), 0.0)


def query_marks(slot):
    return jnp.where(lane_ids(UNIT) == slot, 1.0, 0.0).astype(BF)


def key_marks(slots):
    ids = lane_ids(UNIT)
    parts = [jnp.where((ids < SLOTS) & (ids != slot), FAR, 0.0).astype(BF) for slot in slots]
    return jnp.concatenate(parts, axis=0)


def pair_lanes(pair):
    return pl.ds(pl.multiple_of(pair * LANES, LANES), LANES)


def kv_kernel(info, work, weights):
    rows = weights[0].shape[0] // 4
    plan = plan_of((work.w.at[0], work.w.at[1]), 1, rows)
    start_rows(weights, info[0], plan, work.sems)
    work.need("x")
    entry_rows(work.x, work.mod, info, 0, work.entry)
    work.flush("entry")
    entry = work.entry[...]
    wait_rows(weights, plan, work.sems, range(4))
    work.kv[0] = dot_nt(entry, work.w[0]).astype(BF)
    work.flush("kv", 0)
    wait_rows(weights, plan, work.sems, range(4, 8))
    work.kv[1] = (dot_nt(entry, work.w[1]) + work.biases[2:3, :]).astype(BF)
    work.flush("kv", 1)


def q_kernel(info, work, weights):
    rows = weights[0].shape[0] // 4
    plan = plan_of((work.w,), 0, rows)
    start_rows(weights, info[0], plan, work.sems)
    work.need("entry")
    wait_rows(weights, plan, work.sems, range(4))
    work.q[...] = (dot_nt(work.entry[...], work.w[...]) + work.biases[0:1, :]).astype(BF)
    work.flush("q")


def soft_pair(work, q_pair, keys, values, marks, logs, pair, span, words=None):
    ids = lane_ids(UNIT)
    results = []
    kept = logs[span, :]
    for half in range(2):
        left = (head_half(q_pair, half) * HEAD_WIDTH**-0.5).astype(BF)
        if marks is not None:
            left = jnp.concatenate([left, marks], axis=1)
        scores = dot_nt(left, keys)
        if words is not None:
            scores = jnp.where(ids < words, scores, FAR)
        peak = jnp.max(scores, axis=-1, keepdims=True)
        both = dot_nn(jnp.exp(scores - peak).astype(BF), values)
        sums = both[:, LANES:]
        results.append(both[:, :LANES] / sums)
        kept = jnp.where(ids == 2 * pair + half, peak + jnp.log(sums), kept)
    logs[span, :] = kept
    return jnp.where(ids < HEAD_WIDTH, results[0], results[1]).astype(BF)


def self_kernel(info, work, weights):
    rows = weights[0].shape[0] // 4
    sems = work.sems
    plan = [(s, 3 * rows, rows, work.wo.at[pl.ds(s * rows, rows)]) for s in range(4)]
    start_rows(weights, info[0], plan, sems)
    share = work.x.shape[0]
    blocks = share // UNIT
    marks = key_marks([info[1 + b] for b in range(2 * blocks)])
    ones = jnp.ones((2 * share, LANES), BF)
    logs, mixed = work.logs, work.mixed
    logs[...] = jnp.zeros(logs.shape, F32)
    work.need("q", "kv_own", "kv_sib")

    def both(which, lanes):
        return jnp.concatenate([work.kv_own[which, :, lanes], work.kv_sib[which, :, lanes]], axis=0)

    def step(pair, carry):
        lanes = pair_lanes(pair)
        keys = jnp.concatenate([both(0, lanes), marks], axis=1)
        values = jnp.concatenate([both(1, lanes), ones], axis=1)
        for block in range(blocks):
            span = pl.ds(block * UNIT, UNIT)
            mixed[span, lanes] = soft_pair(
                work,
                work.q[span, lanes],
                keys,
                values,
                query_marks(info[1 + block]),
                logs,
                pair,
                span,
            )
        return carry

    lax.fori_loop(0, mixed.shape[1] // LANES, step, 0)
    work.flush("mixed")
    work.lse[...] = logs[...].T[: work.lse.shape[0], :]
    work.flush("lse")
    wait_rows(weights, plan, sems, range(4))
    work.sum[...] = dot_nn(mixed[...], work.wo[...]) + work.bias[...].astype(F32)
    work.need("x")
    residual_rows(work.x, work.mod, info, 2, work.sum, work.branch, work.out)
    work.flush("branch")
    work.flush("out")


def cross_kernel(info, work, weights, words):
    rows = weights[0].shape[0] // 4
    sems = work.sems
    order = (1, 2, 0, 3)
    plan = [
        (shard, order[i // 4] * rows, count, dst)
        for i, (shard, _, count, dst) in enumerate(
            plan_of((work.wk, work.wv, work.wq, work.wo), 0, rows)
        )
    ]
    start_rows(weights, info[0], plan, sems)
    work.need("x")
    entry_rows(work.x, work.mod, info, 3, work.entry)
    work.flush("entry")
    work.need("text")
    wait_rows(weights, plan, sems, range(0, 4))
    work.kv[0] = dot_nt(work.text[...], work.wk[...]).astype(BF)
    wait_rows(weights, plan, sems, range(4, 8))
    work.kv[1] = (dot_nt(work.text[...], work.wv[...]) + work.biases[5:6, :]).astype(BF)
    work.flush("kv")
    wait_rows(weights, plan, sems, range(8, 12))
    work.q[...] = (dot_nt(work.entry[...], work.wq[...]) + work.biases[3:4, :]).astype(BF)
    work.flush("q")
    ones = jnp.ones((LANES, LANES), BF)
    logs, mixed = work.logs, work.mixed
    logs[...] = jnp.zeros(logs.shape, F32)

    def step(pair, carry):
        lanes = pair_lanes(pair)
        for block in range(mixed.shape[0] // UNIT):
            span = pl.ds(block * UNIT, UNIT)
            own = pl.ds(pl.multiple_of(info[1 + block] * LANES, LANES), LANES)
            mixed[span, lanes] = soft_pair(
                work,
                work.q[span, lanes],
                work.kv[0, own, lanes],
                jnp.concatenate([work.kv[1, own, lanes], ones], axis=1),
                None,
                logs,
                pair,
                span,
                words,
            )
        return carry

    lax.fori_loop(0, mixed.shape[1] // LANES, step, 0, unroll=2)
    work.flush("mixed")
    work.lse[...] = logs[...].T[: work.lse.shape[0], :]
    work.flush("lse")
    wait_rows(weights, plan, sems, range(12, 16))
    work.sum[...] = dot_nn(mixed[...], work.wo[...]) + work.bias[...].astype(F32)
    residual_rows(work.x, work.mod, info, 5, work.sum, work.branch, work.out)
    work.flush("branch")
    work.flush("out")


def halves_of(buffer):
    half = buffer.shape[1] // 2
    return [
        (shard, part * half, half, buffer.at[shard, pl.ds(part * half, half)])
        for shard in range(4)
        for part in range(2)
    ]


def bend_rows(before, bias, active, slope, lanes):
    for row in range(0, before.shape[0], CHUNK):
        span = pl.ds(row, CHUNK)
        values = before[span, :] + bias
        square = values * values
        half = 1.0 / (1.0 + jnp.exp(values * (-2.0 * ROOT - (2.0 * ROOT * CUBIC) * square)))
        act = values * half
        active[span, lanes] = act.astype(BF)
        slope[span, lanes] = (
            half + act * (1.0 - half) * (2.0 * ROOT + (6.0 * ROOT * CUBIC) * square)
        ).astype(BF)


def hidden_kernel(info, work, ups, downs, rolled):
    sems = work.sems
    width = work.x.shape[1]
    up_plan = halves_of(work.up)
    down_plan = halves_of(work.down)
    start_rows(ups, info[0], up_plan, sems)
    start_rows(downs, info[0], down_plan, work.down_sems)
    work.need("x")
    entry_rows(work.x, work.mod, info, 6, work.entry)
    work.flush("entry")

    def columns(shard):
        return pl.ds(pl.multiple_of(shard * width, width), width)

    if rolled:
        wait_rows(ups, up_plan, sems, range(8))
        wait_rows(downs, down_plan, work.down_sems, range(8))
        work.sum[...] = jnp.zeros(work.sum.shape, F32) + work.bias[...].astype(F32)

        def step(shard, carry):
            lanes = columns(shard)
            work.before0[...] = dot_nn(work.entry[...], work.up[shard])
            bend_rows(work.before0, work.up_bias[:, lanes], work.active, work.slope, lanes)
            work.sum[...] += dot_nn(work.active[:, lanes], work.down[shard])
            return carry

        lax.fori_loop(0, 4, step, 0)
        work.flush("active")
        work.flush("slope")
    else:
        before = (work.before0, work.before1)

        def rise(shard):
            wait_rows(ups, up_plan, sems, [2 * shard, 2 * shard + 1])
            before[shard % 2][...] = dot_nn(work.entry[...], work.up[shard])

        rise(0)
        for shard in range(4):
            lanes = pl.ds(shard * width, width)
            if shard < 3:
                rise(shard + 1)
            bend_rows(before[shard % 2], work.up_bias[:, lanes], work.active, work.slope, lanes)
            work.flush("active", slice(None), lanes)
            work.flush("slope", slice(None), lanes)
        wait_rows(downs, down_plan, work.down_sems, range(8))
        work.sum[...] = (
            sum(dot_nn(work.active[:, pl.ds(s * width, width)], work.down[s]) for s in range(4))
            + work.bias[...].astype(F32)
        )
    low = work.low if work.has("low") else None
    residual_rows(work.x, work.mod, info, 8, work.sum, work.branch, work.out, low)
    work.flush("branch")
    work.flush("out")
    if low is not None:
        work.flush("low")


def hidden_back_kernel(info, work, ups, downs, entry, active, rolled):
    sems = work.sems
    width = work.x.shape[1]
    up_plan = halves_of(work.up)
    down_plan = halves_of(work.down)
    start_rows(downs, info[0], down_plan, work.down_sems)
    start_rows(ups, info[0], up_plan, sems)
    actives = [
        pltpu.make_async_copy(
            active.at[:, pl.ds(pl.multiple_of(rank * width, width), width)],
            work.acts.at[i],
            work.act_sems.at[i],
        )
        for i, rank in enumerate((info[7], info[5]))
    ]
    for copy in actives:
        copy.start()
    work.stats[...] = jnp.zeros(work.stats.shape, F32)
    stats = work.stats.at[pl.ds(48, 24)]
    work.need("g", "branch")
    gate_back(work.g, work.mod, info, 8, work.branch, work.gb, stats)
    work.need("slope")

    def columns(shard):
        return pl.ds(pl.multiple_of(shard * width, width), width)

    def bend(before, shard, lanes):
        sums = jnp.zeros((8, width), F32)
        for row in range(0, work.x.shape[0], CHUNK):
            span = pl.ds(row, CHUNK)
            low = (before[span, :] * work.slope[span, lanes].astype(F32)).astype(BF)
            work.d_before[span, lanes] = low
            sums += fold(low.astype(F32))
        stats[pl.ds(13 + shard, 1), :] = total(sums)

    if rolled:
        wait_rows(downs, down_plan, work.down_sems, range(8))
        wait_rows(ups, up_plan, sems, range(8))
        work.de[...] = jnp.zeros(work.de.shape, F32)

        def step(shard, carry):
            lanes = columns(shard)
            work.before0[...] = dot_nt(work.gb[...], work.down[shard])
            bend(work.before0, shard, lanes)
            work.de[...] += dot_nt(work.d_before[:, lanes], work.up[shard])
            return carry

        lax.fori_loop(0, 4, step, 0)
    else:
        before = (work.before0, work.before1)

        def rise(shard):
            wait_rows(downs, down_plan, work.down_sems, [2 * shard, 2 * shard + 1])
            before[shard % 2][...] = dot_nt(work.gb[...], work.down[shard])

        rise(0)
        for shard in range(4):
            if shard < 3:
                rise(shard + 1)
            bend(before[shard % 2], shard, pl.ds(shard * width, width))
        wait_rows(ups, up_plan, sems, range(8))
        work.de[...] = sum(
            dot_nt(work.d_before[:, pl.ds(s * width, width)], work.up[s]) for s in range(4)
        )
    work.need("entry")
    left, right = work.entry[...].T, work.gb[...].T
    for name, index, rank in (("send", 0, info[7]), ("keep", 1, info[5])):
        out = work.outs[name][1]
        out[:, :width] = dot_nn(left, work.d_before[:, columns(rank)]).astype(BF)
        actives[index].wait()
        out[:, width:] = dot_nn(right, work.acts[index]).astype(BF)
        work.flush(name)
    work.need("x")
    norm_back_rows(work.x, work.g, work.de, work.mod, info, 6, work.out, stats)
    work.flush("out")


def pair_grads(info, work, members):
    rows = members[0][0].shape[0]
    low = lane_ids(rows) < HEAD_WIDTH
    step = 3 * LANES
    for at in range(len(members) // 2):
        products = [dot_nn(left, right) for left, right in members[2 * at : 2 * at + 2]]
        (a0, a1, a2), (b0, b1, b2) = [
            [p[:, i * LANES : (i + 1) * LANES] for i in range(3)] for p in products
        ]
        even = (a0, b0, jnp.where(low, a1, pltpu.roll(b1, HEAD_WIDTH, 1)))
        a1, b1 = pltpu.roll(a1, HEAD_WIDTH, 1), pltpu.roll(b1, HEAD_WIDTH, 1)
        a2r, b2r = pltpu.roll(a2, HEAD_WIDTH, 1), pltpu.roll(b2, HEAD_WIDTH, 1)
        odd = (jnp.where(low, a1, a2r), jnp.where(low, b1, b2r), jnp.where(low, a2r, b2))
        first = info[5] % 2 == 0
        for i, (mine, other) in enumerate(zip(even, odd)):
            lanes = pl.ds(at * step + i * LANES, LANES)
            work.outs["keep"][1][:, lanes] = jnp.where(first, mine, other).astype(BF)
            work.outs["send"][1][:, lanes] = jnp.where(first, other, mine).astype(BF)
    work.flush("send")
    work.flush("keep")


def chip_lanes(info, width):
    return pl.ds(pl.multiple_of(info[6] * (width // 2), width // 2), width // 2)


def query_output_kernel(info, work, weights):
    work.need("entry", "gb", "dq", "mixed")
    lanes = chip_lanes(info, work.dq.shape[1])
    pair_grads(
        info,
        work,
        [
            (work.entry[...].T, work.dq[:, lanes]),
            (work.gb[...].T, work.mixed[:, lanes]),
        ],
    )


def cross_back_kernel(info, work, weights, words):
    rows = weights[0].shape[0] // 4
    sems = work.sems
    plan = [
        (shard, (3 * rows, 0)[i // 4], count, dst)
        for i, (shard, _, count, dst) in enumerate(plan_of((work.wo, work.wq), 0, rows))
    ]
    start_rows(weights, info[0], plan, sems)
    work.stats[...] = work.early[...]
    stats = work.stats.at[pl.ds(24, 24)]
    work.need("g", "branch")
    gate_back(work.g, work.mod, info, 5, work.branch, work.gb, stats)
    wait_rows(weights, plan, sems, range(0, 4))
    work.d_mixed[...] = dot_nt(work.gb[...], work.wo[...]).astype(BF)
    work.dkv_sum[...] = jnp.zeros(work.dkv_sum.shape, F32)
    real = lax.broadcasted_iota(jnp.int32, (LANES, UNIT), 0) < words
    work.need("q", "kv", "lse")

    def step(pair, carry):
        lanes = pair_lanes(pair)
        for block in range(work.q.shape[0] // UNIT):
            span = pl.ds(block * UNIT, UNIT)
            own = pl.ds(pl.multiple_of(info[1 + block] * LANES, LANES), LANES)
            q_pair = work.q[span, lanes]
            d_pair = work.d_mixed[span, lanes]
            keys = work.kv[0, own, lanes]
            values = work.kv[1, own, lanes]
            lefts, grads, turned, probs_low, scores_low = [], [], [], [], []
            for half in range(2):
                left = (head_half(q_pair, half) * HEAD_WIDTH**-0.5).astype(BF)
                grad = head_half(d_pair, half).astype(BF)
                logs = work.lse[pl.ds(2 * pair + half, 1), span]
                probs = jnp.where(real, jnp.exp(dot_nt(keys, left) - logs), 0.0)
                d_probs = dot_nt(values, grad)
                inner = jnp.sum(probs * d_probs, axis=0, keepdims=True)
                lefts.append(left)
                grads.append(grad)
                turned.append(head_half(keys, half).T.astype(BF))
                probs_low.append(probs.astype(BF))
                scores_low.append((probs * (d_probs - inner)).astype(BF))
            wide_scores = jnp.concatenate(scores_low, axis=1)
            grad_v = dot_nn(jnp.concatenate(probs_low, axis=1), jnp.concatenate(grads, axis=0))
            grad_k = dot_nn(wide_scores, jnp.concatenate(lefts, axis=0))
            grad_q = dot_nn(
                jnp.concatenate(turned, axis=1), jnp.concatenate(scores_low, axis=0)
            )
            work.dq[span, lanes] = (grad_q.T * HEAD_WIDTH**-0.5).astype(BF)
            work.dkv_sum[0, own, lanes] += grad_k
            work.dkv_sum[1, own, lanes] += grad_v
        return carry

    lax.fori_loop(0, work.q.shape[1] // LANES, step, 0, unroll=2)
    work.dkv[...] = work.dkv_sum[...].astype(BF)
    work.need("entry", "text", "mixed")
    lanes = chip_lanes(info, work.dq.shape[1])
    text = work.text[...].T
    pair_grads(
        info,
        work,
        [
            (work.entry[...].T, work.dq[:, lanes]),
            (text, work.dkv[0, :, lanes]),
            (text, work.dkv[1, :, lanes]),
            (work.gb[...].T, work.mixed[:, lanes]),
        ],
    )
    stats[13:14, :] = total(fold(work.dq[...].astype(F32)))
    stats[14:15, :] = total(fold(work.dkv[1].astype(F32)))
    wait_rows(weights, plan, sems, range(4, 8))
    work.de[...] = dot_nn(work.dq[...], work.wq[...])
    work.need("x")
    norm_back_rows(work.x, work.g, work.de, work.mod, info, 3, work.out, stats)
    work.flush("out")


def self_back_kernel(info, work, weights):
    rows = weights[0].shape[0] // 4
    sems = work.sems
    plan = [(s, 3 * rows, rows, work.wo.at[pl.ds(s * rows, rows)]) for s in range(4)]
    start_rows(weights, info[0], plan, sems)
    work.stats[...] = work.early[...]
    stats = work.stats.at[pl.ds(0, 24)]
    work.need("g", "branch")
    gate_back(work.g, work.mod, info, 2, work.branch, work.gb, stats)
    work.flush("gb")
    share = work.g.shape[0]
    blocks = share // UNIT
    marks = key_marks([info[1 + b] for b in range(2 * blocks)])
    wait_rows(weights, plan, sems, range(4))
    work.d_mixed[...] = dot_nt(work.gb[...], work.wo[...]).astype(BF)
    work.need("q", "kv_own", "kv_sib", "lse")

    def both(which, lanes):
        return jnp.concatenate([work.kv_own[which, :, lanes], work.kv_sib[which, :, lanes]], axis=0)

    def step(pair, carry):
        lanes = pair_lanes(pair)
        keys = both(0, lanes)
        values = both(1, lanes)
        marked = jnp.concatenate([keys, marks], axis=1)
        turned = jnp.concatenate([head_half(keys, half).T.astype(BF) for half in range(2)], axis=1)
        lefts, grads, probs_low, scores_low = [], [], [], []
        for block in range(blocks):
            span = pl.ds(block * UNIT, UNIT)
            q_pair = work.q[span, lanes]
            d_pair = work.d_mixed[span, lanes]
            ends = query_marks(info[1 + block])
            for half in range(2):
                left = (head_half(q_pair, half) * HEAD_WIDTH**-0.5).astype(BF)
                grad = head_half(d_pair, half).astype(BF)
                logs = work.lse[pl.ds(2 * pair + half, 1), span]
                probs = jnp.exp(dot_nt(marked, jnp.concatenate([left, ends], axis=1)) - logs)
                d_probs = dot_nt(values, grad)
                inner = jnp.sum(probs * d_probs, axis=0, keepdims=True)
                lefts.append(left)
                grads.append(grad)
                probs_low.append(probs.astype(BF))
                scores_low.append((probs * (d_probs - inner)).astype(BF))
            grad_q = dot_nn(turned, jnp.concatenate(scores_low[-2:], axis=0))
            work.dq[span, lanes] = (grad_q.T * HEAD_WIDTH**-0.5).astype(BF)
        grad_v = dot_nn(jnp.concatenate(probs_low, axis=1), jnp.concatenate(grads, axis=0))
        grad_k = dot_nn(jnp.concatenate(scores_low, axis=1), jnp.concatenate(lefts, axis=0))
        for which, grad in ((0, grad_k.astype(BF)), (1, grad_v.astype(BF))):
            work.dkv_own[which, :, lanes] = grad[:share]
            work.dkv_give[which, :, lanes] = grad[share:]
        return carry

    lax.fori_loop(0, work.q.shape[1] // LANES, step, 0)
    work.flush("dkv_give")
    work.flush("dkv_own")
    work.flush("dq")


def qkv_back_kernel(info, work, weights):
    rows = weights[0].shape[0] // 4
    sems = work.sems
    plan = plan_of((work.wq, work.wk, work.wv), 0, rows)
    start_rows(weights, info[0], plan, sems)
    work.stats[...] = work.early[...]
    stats = work.stats.at[pl.ds(0, 24)]
    work.need("dq")
    stats[13:14, :] = total(fold(work.dq[...].astype(F32)))
    work.need("dkv_own", "dkv_sib")
    for which in range(2):
        work.dkv[which] = (
            work.dkv_own[which].astype(F32) + work.dkv_sib[which].astype(F32)
        ).astype(BF)
    stats[14:15, :] = total(fold(work.dkv[1].astype(F32)))
    work.need("entry")
    lanes = chip_lanes(info, work.dq.shape[1])
    entry = work.entry[...].T
    pair_grads(info, work, [(entry, work.dkv[0, :, lanes]), (entry, work.dkv[1, :, lanes])])
    wait_rows(weights, plan, sems, range(0, 12))
    work.de[...] = (
        dot_nn(work.dq[...], work.wq[...])
        + dot_nn(work.dkv[0], work.wk[...])
        + dot_nn(work.dkv[1], work.wv[...])
    )
    work.need("x", "g")
    low = work.low if work.has("low") else None
    norm_back_rows(work.x, work.g, work.de, work.mod, info, 0, work.out, stats, low)
    work.flush("out")
    if low is not None:
        work.flush("low")


def merge_kernel(info, *refs, spots, after):
    chains = len(spots)
    ins, outs = refs[: 4 * chains], refs[4 * chains + after :]
    for chain, (result, column) in enumerate(spots):
        for side in range(2):
            received, kept = ins[4 * chain + 2 * side], ins[4 * chain + 2 * side + 1]
            out = outs[2 * result + side]
            lanes = pl.ds(column, received.shape[2])
            out[:, :, lanes] = (received[...].astype(F32) + kept[...].astype(F32)).astype(BF)


def gate(arrays, after):
    count = len(arrays)
    return pl.pallas_call(
        lambda *refs: None,
        out_shape=[shape(*a.shape, dtype=a.dtype) for a in arrays],
        in_specs=[ANY] * (count + len(after)),
        out_specs=[ANY] * count,
        input_output_aliases={i: i for i in range(count)},
        cost_estimate=lasting(0.5),
        name="gate",
    )(*arrays, *after)


def pack_kernel(info, *refs, groups, after):
    count = sum(len(members) for _, members in groups)
    sources, rest = refs[:count], refs[count + after :]
    outs, (held, in_sems, out_sems) = rest[:-3], rest[-3:]
    spots = []
    at = 0
    for index, (layer, members) in enumerate(groups):
        rows = held.shape[1]
        piece_rows = rows // 4
        for quarter in range(4):
            row = quarter * piece_rows
            source = sources[at + quarter * len(members) // 4]
            src = source.at[layer, pl.ds(row % source.shape[1], piece_rows)]
            spots.append((index, quarter, held.at[index, pl.ds(row, piece_rows)], src))
        at += len(members)

    def arriving(place):
        _, _, spot, src = spots[place]
        return pltpu.make_async_copy(src, spot, in_sems.at[place])

    def leaving(index, which):
        out = outs[2 * index + (0 if which == 2 else 1)]
        rows = out.shape[0]
        src = held.at[index] if which == 2 else held.at[index, pl.ds(which * rows, rows)]
        return pltpu.make_async_copy(src, out, out_sems.at[2 * index + (0 if which == 2 else 1)])

    def by_parity(act):
        for parity in range(2):

            @pl.when(info[0] % 2 == parity)
            def _(parity=parity):
                act(parity)

    for place in range(len(spots)):
        arriving(place).start()
    for index in range(len(groups)):
        for quarter in range(4):
            arriving(4 * index + quarter).wait()
        by_parity(lambda parity: leaving(index, parity).start())
        leaving(index, 2).start()
    for index in range(len(groups)):
        by_parity(lambda parity: leaving(index, parity).wait())
        leaving(index, 2).wait()


def mod_kernel(condition, mod, mod_bias, q, v, cq, cv, up, out):
    narrow, units, columns = q.shape[1], up.shape[1], mod.shape[1]
    out[...] = jnp.zeros(out.shape, F32)
    for layer in range(LAYERS):
        row = pl.ds(layer, 1)
        out[layer, 0:SLOTS, 0:columns] = dot_nt(condition[...], mod[layer]) + mod_bias[
            row, :
        ].astype(F32)
        out[layer, 4:5, 0:units] = up[row, :].astype(F32)
        out[layer, 5:6, 0:narrow] = q[row, :].astype(F32)
        out[layer, 6:7, 0:narrow] = v[row, :].astype(F32)
        out[layer, 7:8, 0:narrow] = cq[row, :].astype(F32)
        out[layer, 4:5, 1024 : 1024 + narrow] = cv[row, :].astype(F32)


def assemble_kernel(info, *refs, narrow, units, columns):
    parts, (mods, narrows, ups) = refs[:4], refs[4:]
    narrows[...] = jnp.zeros(narrows.shape, F32)
    for rank in range(4):

        @pl.when(info[5] == rank)
        def _(rank=rank):
            for shard in range(4):
                part = parts[shard ^ rank]
                for layer in range(LAYERS):
                    mods[layer, :, shard * columns : (shard + 1) * columns] = part[
                        layer, 0:SLOTS, 0:columns
                    ]
                    ups[layer, :, shard * units : (shard + 1) * units] = part[layer, 4:5, 0:units]
                    at = slice(shard * narrow, (shard + 1) * narrow)
                    for row, source in ((0, 5), (2, 6), (3, 7)):
                        narrows[layer, row : row + 1, at] = part[
                            layer, source : source + 1, 0:narrow
                        ]
                    narrows[layer, 5:6, at] = part[layer, 4:5, 1024 : 1024 + narrow]


def collect_kernel(info, *refs, narrow, units, columns):
    stats, condition, out = refs[: 2 * LAYERS], refs[2 * LAYERS], refs[2 * LAYERS + 1]
    sums = refs[2 * LAYERS + 2]
    width = stats[0].shape[1]
    work = out
    out = refs[2 * LAYERS + 3]
    out[...] = jnp.zeros(out.shape, F32)
    for layer in range(LAYERS):
        sums[...] = stats[2 * layer][...] + stats[2 * layer + 1][...]
        base = 8 * layer
        out[base + 4 : base + 5, width : 2 * width] = sums[60:61, :]
        out[base + 5 : base + 6, 0:width] = sums[12:13, :]
        out[base + 5 : base + 6, width : 2 * width] = sums[36:37, :]
        for index in range(2):
            out[base + 6 + index : base + 7 + index, 512 : 512 + width] = condition[
                2 * layer + index : 2 * layer + index + 1, :
            ].astype(F32)
        for rank in range(4):

            @pl.when(info[5] == rank)
            def _(rank=rank, base=base):
                first = rank * columns
                for index in range(9):
                    low = max(first, index * width)
                    high = min(first + columns, (index + 1) * width)
                    if low < high:
                        row = (index // 3) * 24 + (index % 3) * 4
                        out[base : base + 4, low - first : high - first] = sums[
                            row : row + 4, low - index * width : high - index * width
                        ]
                out[base + 4 : base + 5, 0:units] = sums[61 + rank : 62 + rank, :]
                own = slice(rank * narrow, (rank + 1) * narrow)
                out[base + 6 : base + 7, 0:narrow] = sums[13:14, own]
                out[base + 6 : base + 7, 256 : 256 + narrow] = sums[14:15, own]
                out[base + 7 : base + 8, 0:narrow] = sums[37:38, own]
                out[base + 7 : base + 8, 256 : 256 + narrow] = sums[38:39, own]
    work[...] = out[...].astype(BF)


def spread_kernel(info, gathered, grad, bias_grad, q, v, cq, cv, up, o1, o2, o3, rows, conditions):
    count = gathered.shape[0]
    columns, part = grad.shape[2], grad.shape[1]
    width, narrow, units = conditions.shape[1], q.shape[1], up.shape[1]
    shift = lax.rem(width - info[8] * part, width)
    for index in range(count):
        for slot in range(SLOTS):
            row = 8 * (slot // 2) + 6 + slot % 2
            conditions[SLOTS * index + slot : SLOTS * index + slot + 1, :] = gathered[
                index ^ info[8], row : row + 1, 512 : 512 + width
            ].astype(F32)
    turned = pltpu.roll(conditions[...], shift, 1)[:, :part].T
    for layer in range(LAYERS):
        base = 8 * layer
        sums = jnp.zeros((8, gathered.shape[2]), F32)
        for index in range(count):
            values = gathered[index ^ info[8]].astype(F32)[base : base + 8]
            sums += values
            rows[SLOTS * index : SLOTS * (index + 1), :] = values[0:SLOTS, 0:columns]
        grad[layer] = jnp.dot(
            turned, rows[...], precision=lax.Precision.HIGHEST, preferred_element_type=F32
        )
        at = slice(layer, layer + 1)
        bias_grad[at, :] = jnp.sum(sums[0:SLOTS, 0:columns], axis=0, keepdims=True)
        up[at, :] = sums[4:5, 0:units]
        q[at, :] = sums[6:7, 0:narrow]
        v[at, :] = sums[6:7, 256 : 256 + narrow]
        cq[at, :] = sums[7:8, 0:narrow]
        cv[at, :] = sums[7:8, 256 : 256 + narrow]
        for out, row, lane in ((o1, 5, 0), (o2, 5, width), (o3, 4, width)):
            own = jnp.broadcast_to(sums[row : row + 1, lane : lane + width], (8, width))
            out[at, :] = pltpu.roll(own, shift, 1)[0:1, :part]


def finish_kernel(*refs, wide, spots):
    parts, outs = refs[: 2 * len(spots)], refs[2 * len(spots) :]
    step = 3 * LANES
    for chain, places in enumerate(spots):
        values = parts[2 * chain][0].astype(F32) + parts[2 * chain + 1][0].astype(F32)
        at = 0
        for layer, pair in places:
            if wide:
                width = outs[0].shape[2]
                for out in outs:
                    out[layer] = values[:, at : at + width]
                    at += width
                continue
            both = values[:, at : at + step]
            at += step
            first = jnp.concatenate(
                [both[:, :LANES], both[:, 2 * LANES : 2 * LANES + HEAD_WIDTH]], axis=1
            )
            second = jnp.concatenate(
                [both[:, LANES : 2 * LANES], both[:, 2 * LANES + HEAD_WIDTH :]], axis=1
            )
            for out, matrix in zip(outs[2 * pair : 2 * pair + 2], (first, second)):
                out[layer] = matrix if out.shape[1:] == matrix.shape else matrix.T


def join_kernel(info, rows, other, out):
    share = rows.shape[0]
    for core in range(2):

        @pl.when(info[5] % 2 == core)
        def _(core=core):
            out[pl.ds(core * share, share), :] = rows[...]
            out[pl.ds((1 - core) * share, share), :] = other[...]


def tensor_hop(values, step):
    return lax.ppermute(values, "tensor", [(i, i ^ step) for i in range(4)])


def dp_hop(values, step):
    size = lax.axis_size("dp")
    return lax.ppermute(values, "dp", [(i, i ^ step) for i in range(size)])


def time_features(moments, width):
    half = width // 2
    rates = jnp.exp(-math.log(10000.0) * jnp.arange(half, dtype=F32) / half)
    angles = moments.astype(F32)[:, None] * rates[None, :]
    return jnp.concatenate([jnp.cos(angles), jnp.sin(angles)], axis=1)


def shards(
    tokens,
    text,
    timesteps,
    item_frames,
    cotangent,
    self_query,
    self_query_bias,
    self_key,
    self_value,
    self_value_bias,
    self_output,
    self_output_bias,
    cross_query,
    cross_query_bias,
    cross_key,
    cross_value,
    cross_value_bias,
    cross_output,
    cross_output_bias,
    hidden_up,
    hidden_up_bias,
    hidden_down,
    hidden_down_bias,
    modulation,
    modulation_bias,
):
    frames, width = tokens.shape
    words = text.shape[1]
    columns = modulation.shape[2]
    narrow = self_query.shape[2]
    units = hidden_up.shape[2]
    rank = lax.axis_index("tensor")
    me = lax.axis_index("dp")
    size = lax.axis_size("dp")
    core = rank % 2
    share = frames // 2
    blocks = share // UNIT
    unit = width // size
    turn = lambda values: jnp.swapaxes(values, 1, 2)

    order = jnp.arange(SLOTS, dtype=jnp.int32)
    ends = jnp.sum(jnp.where(order[:, None] <= order[None, :], item_frames[:, None], 0), axis=0)
    turned = (jnp.arange(frames // UNIT, dtype=jnp.int32) + core * blocks) % (2 * blocks)
    slots = jnp.sum((turned[:, None] * UNIT >= ends[None, :]).astype(jnp.int32), axis=1)
    places = jnp.stack([rank, rank // 2, rank ^ 1, me]).astype(jnp.int32)
    info = jnp.concatenate([(rank * 2 + me % 2)[None].astype(jnp.int32), slots, places])

    condition = jax.nn.silu(time_features(timesteps, width)).astype(BF)
    mine = plain(
        mod_kernel,
        "modulation_rows",
        None,
        [
            condition,
            turn(modulation),
            modulation_bias,
            self_query_bias,
            self_value_bias,
            cross_query_bias,
            cross_value_bias,
            hidden_up_bias,
        ],
        [shape(LAYERS, 8, -(-columns // LANES) * LANES)],
    )
    others = [tensor_hop(mine, 1), tensor_hop(mine, 2)]
    others.append(tensor_hop(others[0], 2))
    mods, narrow_biases, up_biases = plain(
        partial(assemble_kernel, narrow=narrow, units=units, columns=columns),
        "modulation_of_all",
        info,
        [mine, *others],
        [
            shape(LAYERS, SLOTS, 4 * columns),
            shape(LAYERS, 8, 4 * narrow),
            shape(LAYERS, 1, 4 * units),
        ],
    )
    out_biases = [
        b.reshape(LAYERS, 1, width) for b in (self_output_bias, cross_output_bias, hidden_down_bias)
    ]

    def pack(members, after):
        outs = [shape(width // part, width, dtype=BF) for _ in members for part in (1, 2)]
        arrays = [a for _, some in members for a in some]
        return pl.pallas_call(
            partial(
                pack_kernel,
                groups=[(layer, [None] * len(some)) for layer, some in members],
                after=len(after),
            ),
            out_shape=outs,
            in_specs=[SMALL] + [ANY] * (len(arrays) + len(after)),
            out_specs=[ANY] * len(outs),
            scratch_shapes=[
                pltpu.VMEM((len(members), width, width), BF),
                pltpu.SemaphoreType.DMA((4 * len(members),)),
                pltpu.SemaphoreType.DMA((2 * len(members),)),
            ],
            compiler_params=pltpu.CompilerParams(vmem_limit_bytes=VMEM_BYTES),
            cost_estimate=lasting(1.0),
            name="pack_weights",
        )(info, *arrays, *after)

    kinds = (
        [turn(self_query), turn(self_key), turn(self_value), self_output],
        [turn(cross_query), turn(cross_key), turn(cross_value), cross_output],
        [hidden_up],
        [hidden_down],
    )
    all_groups = [(index // 4, kinds[index % 4]) for index in range(4 * LAYERS)]
    packed = [*pack(all_groups[:1], []), *pack(all_groups[1:], [mine])]
    firsts = [packed[2 * index + 1] for index in range(4 * LAYERS)]
    owns = [packed[2 * index] for index in range(4 * LAYERS)]
    along_x, along_y, over_x, over_y, sibs = [[None] * (4 * LAYERS) for _ in range(5)]

    def leave(index):
        along_x[index] = tensor_hop(firsts[index], 2)
        sibs[index] = tensor_hop(owns[index], 1)

    def go_on(index):
        along_y[index] = dp_hop(along_x[index], 1)
        over_x[index] = tensor_hop(along_x[index], 1)

    def end(index):
        over_y[index] = tensor_hop(along_y[index], 1)

    def weights_of(index):
        return [
            owns[index],
            sibs[index],
            along_x[index],
            along_y[index],
            over_x[index],
            over_y[index],
        ]

    def open_gate(after, leaving=(), at_x=(), at_y=()):
        places = [(firsts, i) for i in leaving]
        places += [(along_x, i) for i in at_x] + [(along_y, i) for i in at_y]
        opened = gate([values[i] for values, i in places], after)
        for (values, i), array in zip(places, opened):
            values[i] = array
        for i in leaving:
            leave(i)
        for i in at_x:
            go_on(i)
        for i in at_y:
            end(i)
        return list(opened)

    leave(0)
    open_gate([mine], [], [0])
    open_gate([others[1]], [1, 2, 3])
    go_on(1)
    open_gate([mods], [], [], [0])

    text_rows = jnp.pad(text, ((0, 0), (0, LANES - words), (0, 0))).reshape(-1, width)
    whole = pltpu.VMEM((width, width), BF)
    four = pltpu.VMEM((4, width, units), BF)
    floats = pltpu.VMEM((share, width), F32)
    lows = pltpu.VMEM((share, width), BF)
    sems = lambda n: pltpu.SemaphoreType.DMA((n,))
    frame_low = shape(share, width, dtype=BF)
    frame_high = shape(share, width)
    frame_wide = shape(share, 4 * units, dtype=BF)
    two_low = shape(2, share, width, dtype=BF)
    two_text = shape(2, SLOTS * LANES, width, dtype=BF)
    logs = shape(16, share)
    log_work = pltpu.VMEM((share, LANES), F32)
    stat_shape = shape(72, width)

    x = lax.dynamic_slice_in_dim(tokens, core * share, share).astype(F32)
    kept = []
    for layer in range(LAYERS):
        first = 4 * layer
        mod = (mods, (layer,))
        biases = (narrow_biases, (layer,))
        entry1, kv = run(
            kv_kernel,
            "self_keys_values",
            info,
            dict(x=x),
            dict(mod=mod, biases=biases),
            weights_of(first),
            dict(entry=frame_low, kv=two_low),
            {},
            dict(w=pltpu.VMEM((2, width, width), BF), sems=sems(8)),
            [along_x[1], *owns[1:]] if layer == 0 else [],
            3.0,
        )
        kv_sib = tensor_hop(kv, 1)
        opened = open_gate([entry1], [4, 5], [], [1]) if layer == 0 else []
        (q,) = run(
            q_kernel,
            "self_query",
            info,
            dict(entry=entry1),
            dict(biases=biases),
            weights_of(first),
            dict(q=frame_low),
            {},
            dict(w=whole, sems=sems(4)),
            [],
            15.0,
        )
        x1, mixed1, lse1, branch1 = run(
            self_kernel,
            "self_attention",
            info,
            dict(q=q, kv_own=kv, kv_sib=kv_sib, x=x),
            dict(mod=mod, bias=(out_biases[0], (layer,))),
            weights_of(first),
            dict(out=frame_high, mixed=frame_low, lse=logs, branch=frame_low),
            {},
            dict(wo=whole, logs=log_work, sum=floats, sems=sems(4)),
            opened,
            8.0,
        )
        opened = open_gate([x1], [6, 7], [2]) if layer == 0 else open_gate([x1], [], [7], [5, 6])
        x2, entry2, cq, ckv, mixed2, lse2, branch2 = run(
            partial(cross_kernel, words=words),
            "cross_attention",
            info,
            dict(x=x1, text=text_rows),
            dict(mod=mod, biases=biases, bias=(out_biases[1], (layer,))),
            weights_of(first + 1),
            dict(
                out=frame_high,
                entry=frame_low,
                q=frame_low,
                kv=two_text,
                mixed=frame_low,
                lse=logs,
                branch=frame_low,
            ),
            {},
            dict(
                wq=whole, wk=whole, wv=whole, wo=whole, logs=log_work, sum=floats, sems=sems(16)
            ),
            opened,
            6.0,
        )
        opened = open_gate([x2], [], [3, 4], [2]) if layer == 0 else open_gate([x2], [], [], [7])
        if layer == 0:
            end(3)
        results = run(
            lambda info, work, w: hidden_kernel(info, work, w[:6], w[6:], ROLLED[layer]),
            "feed_forward",
            info,
            dict(x=x2),
            dict(mod=mod, up_bias=(up_biases, (layer,)), bias=(out_biases[2], (layer,))),
            weights_of(first + 2) + weights_of(first + 3),
            dict(
                out=frame_high,
                entry=frame_low,
                active=frame_wide,
                slope=frame_wide,
                branch=frame_low,
                **(dict(low=frame_low) if layer == LAYERS - 1 else {}),
            ),
            {},
            dict(
                up=four,
                down=four,
                before0=floats,
                before1=floats,
                sum=floats,
                sems=sems(8),
                down_sems=sems(8),
            ),
            opened,
            7.0,
        )
        x3, entry3, active, slope, branch3 = results[:5]
        if layer == 0:
            open_gate([x3], [], [5, 6], [4])
        kept.append(
            dict(
                x=x,
                entry1=entry1,
                q=q,
                kv=kv,
                kv_sib=kv_sib,
                mixed1=mixed1,
                lse1=lse1,
                branch1=branch1,
                x1=x1,
                entry2=entry2,
                cq=cq,
                ckv=ckv,
                mixed2=mixed2,
                lse2=lse2,
                branch2=branch2,
                x2=x2,
                entry3=entry3,
                active=active,
                slope=slope,
                branch3=branch3,
            )
        )
        x = x3

    def join(rows):
        return plain(
            join_kernel,
            "join_rows",
            info,
            [rows, tensor_hop(rows, 1)],
            [shape(2 * share, width, dtype=BF)],
        )

    output = join(results[5])

    chains = {}

    def start(name, send, keep):
        view = (size, unit, send.shape[1])
        chains[name] = (tensor_hop(send, 1).reshape(view), keep.reshape(view), 0)

    def held(*names):
        return [chains[name][1] for name in names]

    def advance(names, after=(), joined=None):
        names = [n for n in names if 2 ** chains[n][2] < size]
        if not names:
            return
        ins, in_specs, outs, out_specs, spots = [], [], [], [], []
        wide = all(chains[name][0].shape[2] % (4 * LANES) == 0 for name in names)
        cuts = 2 if wide and not joined else 1
        total_columns = sum(chains[name][0].shape[2] for name in names)
        for name in names:
            received, kept_part, bit = chains[name]
            count, unit, columns = received.shape
            spots.append(
                (0, sum(chains[n][0].shape[2] for n in names[: len(spots)]))
                if joined
                else (len(spots), 0)
            )
            for side in range(2):

                def at(i, info, bit=bit, side=side):
                    return (0, ((info[8] >> bit) & 1) ^ side, 0, i)

                for part in (received, kept_part):
                    ins.append(part.reshape(count // 2, 2, unit, columns))
                    in_specs.append(pl.BlockSpec((count // 2, None, unit, columns // cuts), at))
            if joined and len(spots) > 1:
                continue
            columns = total_columns if joined else columns
            for side in range(2):
                outs.append(shape(count // 2, unit, columns, dtype=BF))
                out_specs.append(
                    pl.BlockSpec((count // 2, unit, columns // cuts), lambda i, info: (0, 0, i))
                )
        results = pl.pallas_call(
            partial(merge_kernel, spots=spots, after=len(after)),
            grid_spec=pltpu.PrefetchScalarGridSpec(
                num_scalar_prefetch=1,
                grid=(cuts,),
                in_specs=in_specs + [ANY] * len(after),
                out_specs=out_specs,
            ),
            out_shape=outs,
            compiler_params=pltpu.CompilerParams(vmem_limit_bytes=VMEM_BYTES),
            cost_estimate=lasting(1.5),
            name="merge_grads",
        )(info, *ins, *after)
        bit = chains[names[0]][2]
        for index, name in enumerate([joined] if joined else names):
            bit = chains[names[index]][2]
            hold, give = results[2 * index : 2 * index + 2]
            chains[name] = (dp_hop(give, 2**bit), hold, bit + 1)
        if joined:
            for name in names:
                del chains[name]

    g = lax.dynamic_slice_in_dim(cotangent, core * share, share).astype(F32)
    sums = []
    last = LAYERS - 1
    for layer in reversed(range(LAYERS)):
        first = 4 * layer
        k = kept[layer]
        mod = (mods, (layer,))
        above = layer + 1
        f_name, c_name, a_name, s_name = [f"{kind}{layer}" for kind in "fcas"]
        n_name = f"n{above}"

        def grads_out(members):
            return {name: shape(width, members * narrow, dtype=BF) for name in ("send", "keep")}

        more = [output]
        if layer < last:
            more = held(f"f{above}", f"s{above}") + [chains[f"{kind}{above}"][0] for kind in "ca"]
        results = run(
            lambda info, work, w: hidden_back_kernel(
                info, work, w[:6], w[6:12], None, w[12], ROLLED[layer]
            ),
            "feed_forward_back",
            info,
            dict(g=g, branch=k["branch3"], slope=k["slope"], entry=k["entry3"], x=k["x2"]),
            dict(mod=mod),
            weights_of(first + 2) + weights_of(first + 3) + [k["active"]],
            {name: shape(width, 2 * units, dtype=BF) for name in ("send", "keep")}
            | dict(out=frame_high),
            dict(stats=stat_shape),
            dict(
                up=four,
                down=four,
                gb=lows,
                d_before=pltpu.VMEM((share, 4 * units), BF),
                acts=pltpu.VMEM((2, share, units), BF),
                act_sems=sems(2),
                before0=floats,
                before1=floats,
                de=floats,
                sems=sems(8),
                down_sems=sems(8),
            ),
            more,
            10.0,
        )
        send, keep, g, stats = results
        start(f_name, send, keep)
        if layer < last:
            advance([f"c{above}", f"a{above}", f"s{above}"], held(f_name), n_name)
        send, keep, g, stats = run(
            partial(cross_back_kernel, words=words),
            "cross_attention_back",
            info,
            dict(
                g=g,
                branch=k["branch2"],
                q=k["cq"],
                kv=k["ckv"],
                lse=k["lse2"],
                entry=k["entry2"],
                text=text_rows,
                mixed=k["mixed2"],
                x=k["x1"],
            ),
            dict(mod=mod, early=(stats, ())),
            weights_of(first + 1),
            grads_out(4) | dict(out=frame_high),
            dict(stats=stat_shape),
            dict(
                wq=whole,
                wo=whole,
                gb=lows,
                dq=lows,
                dkv=pltpu.VMEM(two_text.shape, BF),
                d_mixed=lows,
                de=floats,
                dkv_sum=pltpu.VMEM(two_text.shape, F32),
                sems=sems(8),
            ),
            held(f_name, *([n_name] if layer < last else [])),
            10.0,
        )
        start(c_name, send, keep)
        advance([f_name], [g])
        gb1, dq, dkv_own, dkv_give, stats = run(
            self_back_kernel,
            "self_attention_back",
            info,
            dict(
                g=g, branch=k["branch1"], q=k["q"], kv_own=k["kv"], kv_sib=k["kv_sib"], lse=k["lse1"]
            ),
            dict(mod=mod, early=(stats, ())),
            weights_of(first),
            dict(gb=frame_low, dq=frame_low, dkv_own=two_low, dkv_give=two_low),
            dict(stats=stat_shape),
            dict(wo=whole, d_mixed=lows, sems=sems(4)),
            held(f_name, c_name),
            13.0,
        )
        dkv_sib = tensor_hop(dkv_give, 1)
        advance([f_name, *([c_name, n_name] if layer < last else [])], [dq])
        send, keep = run(
            query_output_kernel,
            "query_output_grads",
            info,
            dict(entry=k["entry1"], gb=gb1, dq=dq, mixed=k["mixed1"]),
            {},
            [],
            grads_out(2),
            {},
            {},
            held(f_name),
            15.0,
        )
        start(a_name, send, keep)
        results = run(
            qkv_back_kernel,
            "self_qkv_back",
            info,
            dict(
                dq=dq, dkv_own=dkv_own, dkv_sib=dkv_sib, entry=k["entry1"], x=k["x"], g=g
            ),
            dict(mod=mod, early=(stats, ())),
            weights_of(first),
            grads_out(2)
            | dict(out=frame_high)
            | (dict(low=frame_low) if layer == 0 else {}),
            dict(stats=stat_shape),
            dict(
                wq=whole,
                wk=whole,
                wv=whole,
                de=floats,
                dkv=pltpu.VMEM(two_low.shape, BF),
                sems=sems(12),
            ),
            held(a_name),
            6.0,
        )
        send, keep, g, stats = results[0], results[1], results[2], results[-1]
        start(s_name, send, keep)
        if layer == last:
            advance([f_name], held(s_name))
        else:
            advance([f_name, c_name, a_name, n_name], held(s_name))
        sums = [stats, tensor_hop(stats, 1)] + sums
    input_grad = join(results[3])
    vectors = plain(
        partial(collect_kernel, narrow=narrow, units=units, columns=columns),
        "collect_sums",
        info,
        [*sums, condition],
        [shape(16, mine.shape[2], dtype=BF)],
        [pltpu.VMEM(stat_shape.shape, F32), pltpu.VMEM((16, mine.shape[2]), F32)],
    )
    gathered = vectors[None]
    hop = size // 2
    while hop:
        both = jnp.stack([gathered, dp_hop(gathered, hop)], axis=1)
        gathered = both.reshape(-1, *vectors.shape)
        hop //= 2
    previous = held("f0", "c0", "a0")
    while any(2 ** chain[2] < size for chain in chains.values()):
        advance(list(chains), previous)
        previous = held(*chains)

    def parts_of(*names):
        return [part.reshape(1, unit, -1) for name in names for part in chains[name][:2]]

    up_grad, down_grad = plain(
        partial(finish_kernel, wide=True, spots=[[(layer, 0)] for layer in range(LAYERS)]),
        "finish_wide",
        None,
        parts_of(*[f"f{layer}" for layer in range(LAYERS)]),
        [shape(LAYERS, unit, units)] * 2,
    )
    straight, across = shape(LAYERS, unit, narrow), shape(LAYERS, narrow, unit)
    lasts = [[(layer, pair) for pair in range(4)] for layer in range(1, LAYERS)]
    cq_grad, ck_grad, cv_grad, co_grad, q_grad, o_grad, k_grad, v_grad = plain(
        partial(finish_kernel, wide=False, spots=lasts + [[(0, 0), (0, 1)], [(0, 2)], [(0, 3)]]),
        "finish_narrow",
        None,
        parts_of(*[f"n{layer}" for layer in range(1, LAYERS)], "c0", "a0", "s0"),
        [straight, straight, straight, across, straight, across, straight, straight],
    )
    small = plain(
        spread_kernel,
        "spread_sums",
        info,
        [gathered],
        [shape(LAYERS, unit, columns), shape(LAYERS, columns)]
        + [shape(LAYERS, narrow)] * 4
        + [shape(LAYERS, units)]
        + [shape(LAYERS, unit)] * 3,
        [pltpu.VMEM((SLOTS * size, columns), F32), pltpu.VMEM((SLOTS * size, width), F32)],
    )
    mod_grad, mod_bias_grad, q_sum, v_sum, cq_sum, cv_sum, up_sum, o1, o2, o3 = small
    return (
        output,
        input_grad,
        q_grad,
        q_sum,
        k_grad,
        v_grad,
        v_sum,
        o_grad,
        o1,
        cq_grad,
        cq_sum,
        ck_grad,
        cv_grad,
        cv_sum,
        co_grad,
        o2,
        up_grad,
        up_sum,
        turn(down_grad),
        o3,
        mod_grad,
        mod_bias_grad,
    )


def solution(mesh):
    dp, tensor = "dp", "tensor"
    columns, vector = P(None, None, tensor), P(None, tensor)
    matrix, turned, spread = P(None, dp, tensor), P(None, tensor, dp), P(None, dp)
    placed = (
        P(dp, None),
        P(dp, None, None),
        P(dp),
        P(dp),
        P(dp, None),
        columns,
        vector,
        columns,
        columns,
        vector,
        P(None, tensor, None),
        P(),
        columns,
        vector,
        columns,
        columns,
        vector,
        P(None, tensor, None),
        P(),
        columns,
        vector,
        P(None, tensor, None),
        P(),
        columns,
        vector,
    )
    results = (
        P(dp, None),
        P(dp, None),
        matrix,
        vector,
        matrix,
        matrix,
        vector,
        turned,
        spread,
        matrix,
        vector,
        matrix,
        matrix,
        vector,
        turned,
        spread,
        matrix,
        vector,
        turned,
        spread,
        matrix,
        vector,
    )
    return jax.shard_map(
        shards, mesh=mesh, in_specs=placed, out_specs=results, check_vma=False
    )
```

```python
from functools import partial
import math

import jax
import jax.numpy as jnp
from jax import lax
from jax.experimental import pallas as pl
from jax.experimental.pallas import tpu as pltpu
from jax.sharding import PartitionSpec as P

HEAD_WIDTH = 64
UNIT = 256
LAYERS = 2
WINDOW = 1024
EPSILON = 1e-06
LANES = 128
CHUNK = 64
SLOTS = WINDOW // UNIT
FAR = -1e30
VMEM_BYTES = 62 * 1024 * 1024
BF = jnp.bfloat16
F32 = jnp.float32
ROOT = math.sqrt(2.0 / math.pi)
CUBIC = 0.044715


def dot_nn(left, right):
    return jnp.dot(left, right, preferred_element_type=F32)


def dot_nt(left, right):
    return lax.dot_general(left, right, (((1,), (1,)), ((), ())), preferred_element_type=F32)


def dot_tn(left, right):
    return lax.dot_general(left, right, (((0,), (0,)), ((), ())), preferred_element_type=F32)


SMALL = pl.BlockSpec(memory_space=pltpu.SMEM)
NEAR = pl.BlockSpec(memory_space=pltpu.VMEM)
ANY = pl.BlockSpec(memory_space=pl.ANY)


class Work:
    def __init__(self, ins, outs, scratch, in_sems, out_sems):
        self.ins, self.outs, self.scratch, self.out_sems = ins, outs, scratch, out_sems
        self.copies, self.waited, self.flushed = {}, set(), []
        for index, (name, (ref, buffer)) in enumerate(ins.items()):
            self.copies[name] = pltpu.make_async_copy(ref, buffer, in_sems.at[index])
            self.copies[name].start()

    def __getattr__(self, name):
        if name in self.__dict__["ins"]:
            return self.ins[name][1]
        if name in self.__dict__["outs"]:
            return self.outs[name][1]
        return self.__dict__["scratch"][name]

    def has(self, name):
        return name in self.outs

    def send(self, name, source, *at):
        ref = self.outs[name][0]
        copy = pltpu.make_async_copy(
            source, ref.at[at] if at else ref, self.out_sems.at[len(self.flushed)]
        )
        copy.start()
        self.flushed.append(copy)

    def need(self, *names):
        for name in names:
            if name not in self.waited:
                self.waited.add(name)
                self.copies[name].wait()

    def flush(self, name, *at):
        ref, buffer = self.outs[name]
        if at:
            ref, buffer = ref.at[at], buffer.at[at]
        copy = pltpu.make_async_copy(buffer, ref, self.out_sems.at[len(self.flushed)])
        copy.start()
        self.flushed.append(copy)

    def finish(self):
        self.need(*self.ins)
        for copy in self.flushed:
            copy.wait()


def run(body, name, info, ins, small, weights, outs, small_outs, scratch, after=(), cost=1.0):
    in_names, out_names, names = list(ins), list(outs), list(scratch)
    small_names, small_out_names = list(small), list(small_outs)
    counts = [1, len(in_names), len(small), len(weights), len(after), len(outs), len(small_outs)]

    def kernel(*refs):
        refs = list(refs)
        parts = []
        for count in counts:
            parts.append(refs[:count])
            refs = refs[count:]
        (info_ref,), in_refs, small_refs, weight_refs, _, out_refs, small_out_refs = parts
        in_bufs, refs = refs[: len(in_names)], refs[len(in_names) :]
        out_bufs, refs = refs[: len(out_names)], refs[len(out_names) :]
        rest, (in_sems, out_sems) = refs[:-2], refs[-2:]
        extra = {}
        rest = list(rest)
        for key in names:
            many = isinstance(scratch[key], list)
            size = len(scratch[key]) if many else 1
            extra[key] = rest[:size] if many else rest[0]
            rest = rest[size:]
        for key, ref in zip(small_names, small_refs):
            index = small[key][1]
            extra[key] = ref.at[index] if index else ref
        extra.update(zip(small_out_names, small_out_refs))
        work = Work(
            dict(zip(in_names, zip(in_refs, in_bufs))),
            dict(zip(out_names, zip(out_refs, out_bufs))),
            extra,
            in_sems,
            out_sems,
        )
        body(info_ref, work, weight_refs)
        work.finish()

    buffer = lambda a: pltpu.VMEM(a.shape, a.dtype)
    flat = []
    for value in scratch.values():
        flat += value if isinstance(value, list) else [value]
    results = pl.pallas_call(
        kernel,
        out_shape=[outs[n] for n in out_names] + [small_outs[n] for n in small_out_names],
        in_specs=[SMALL]
        + [ANY] * len(ins)
        + [NEAR] * len(small)
        + [ANY] * (len(weights) + len(after)),
        out_specs=[ANY] * len(outs) + [NEAR] * len(small_outs),
        scratch_shapes=[buffer(ins[n]) for n in in_names]
        + [buffer(outs[n]) for n in out_names]
        + flat
        + [pltpu.SemaphoreType.DMA((max(len(ins), 1),)), pltpu.SemaphoreType.DMA((32,))],
        compiler_params=pltpu.CompilerParams(vmem_limit_bytes=VMEM_BYTES),
        cost_estimate=lasting(cost),
        name=name,
    )(info, *ins.values(), *[array for array, _ in small.values()], *weights, *after)
    return results


def plain(body, name, info, ins, outs, scratch=(), after=()):
    first = len(ins) + (0 if info is None else 1)
    results = pl.pallas_call(
        lambda *refs: body(*refs[:first], *refs[first + len(after) :]),
        out_shape=outs,
        in_specs=([] if info is None else [SMALL]) + [NEAR] * len(ins) + [ANY] * len(after),
        out_specs=[NEAR] * len(outs),
        scratch_shapes=list(scratch),
        compiler_params=pltpu.CompilerParams(vmem_limit_bytes=VMEM_BYTES),
        cost_estimate=lasting(1.0),
        name=name,
    )(*([] if info is None else [info]), *ins, *after)
    return results if len(outs) > 1 else results[0]


def lasting(units):
    return pl.CostEstimate(flops=int(units * 0.4e9), bytes_accessed=1000, transcendentals=0)


def shape(*dims, dtype=F32):
    return jax.ShapeDtypeStruct(dims, dtype)


def start_rows(refs, place, plan, sems):
    own, sib, xa, ya, xb, yb = refs
    half = own.shape[0] // 2
    for rank in range(4):
        for parity in range(2):

            @pl.when(place == rank * 2 + parity)
            def _(rank=rank, parity=parity):
                for index, (shard, row, rows, dst) in enumerate(plan):
                    step = shard ^ rank
                    if step < 2:
                        src = (own, sib)[step].at[pl.ds(row, rows)]
                    else:
                        first, second = ((xa, ya), (xb, yb))[step - 2]
                        part = row // half
                        src = (first if part == parity else second).at[pl.ds(row - part * half, rows)]
                    pltpu.make_async_copy(src, dst, sems.at[index]).start()


def wait_rows(refs, plan, sems, which):
    for index in which:
        _, row, rows, dst = plan[index]
        pltpu.make_async_copy(refs[0].at[pl.ds(0, rows)], dst, sems.at[index]).wait()


def plan_of(buffers, first, rows):
    return [
        (shard, (first + which) * rows, rows, dst.at[pl.ds(shard * rows, rows)])
        for which, dst in enumerate(buffers)
        for shard in range(4)
    ]


def norm_rows(values):
    mean = jnp.mean(values, axis=-1, keepdims=True)
    center = values - mean
    factor = lax.rsqrt(jnp.mean(center * center, axis=-1, keepdims=True) + EPSILON)
    return center * factor, factor


def piece(mod, slot, index):
    width = mod.shape[1] // 9
    return mod[pl.ds(slot, 1), index * width : (index + 1) * width]


def entry_rows(x, mod, info, index, out):
    for block in range(x.shape[0] // UNIT):
        slot = info[1 + block]
        shift = piece(mod, slot, index)
        scale = 1.0 + piece(mod, slot, index + 1)

        def step(turn, carry):
            rows = pl.ds(pl.multiple_of(block * UNIT + turn * CHUNK, CHUNK), CHUNK)
            normed, _ = norm_rows(x[rows, :])
            out[rows, :] = (normed * scale + shift).astype(BF)
            return carry

        lax.fori_loop(0, UNIT // CHUNK, step, 0, unroll=True)


def residual_rows(x, mod, info, index, branch, branch_out, out, low=None):
    for block in range(x.shape[0] // UNIT):
        gate = piece(mod, info[1 + block], index)

        def step(turn, carry):
            rows = pl.ds(pl.multiple_of(block * UNIT + turn * CHUNK, CHUNK), CHUNK)
            values = branch[rows, :]
            branch_out[rows, :] = values.astype(BF)
            result = x[rows, :] + gate * values
            out[rows, :] = result
            if low is not None:
                low[rows, :] = result.astype(BF)
            return carry

        lax.fori_loop(0, UNIT // CHUNK, step, 0, unroll=True)


def fold(values):
    return jnp.sum(values.reshape(values.shape[0] // 8, 8, values.shape[1]), axis=0)


def total(values):
    return jnp.sum(values, axis=0, keepdims=True)


def gate_back(g, mod, info, index, branch, gb, stats):
    width = g.shape[1]
    sums = jnp.zeros((8, width), F32)
    for block in range(g.shape[0] // UNIT):
        slot = info[1 + block]
        gate = piece(mod, slot, index)

        def step(turn, carry):
            rows = pl.ds(pl.multiple_of(block * UNIT + turn * CHUNK, CHUNK), CHUNK)
            grad = g[rows, :]
            low = (gate * grad).astype(BF)
            gb[rows, :] = low
            return (
                carry[0] + fold(low.astype(F32)),
                carry[1] + fold(grad * branch[rows, :].astype(F32)),
            )

        sums, rows_sum = lax.fori_loop(
            0, UNIT // CHUNK, step, (sums, jnp.zeros((8, width), F32)), unroll=True
        )
        stats[pl.ds(8 + slot, 1), :] += total(rows_sum)
    stats[12:13, :] = total(sums)


def norm_back_rows(x, g, de, mod, info, index, out, stats, low=None):
    width = x.shape[1]
    for block in range(x.shape[0] // UNIT):
        slot = info[1 + block]
        scale = 1.0 + piece(mod, slot, index + 1)

        def step(turn, carry):
            rows = pl.ds(pl.multiple_of(block * UNIT + turn * CHUNK, CHUNK), CHUNK)
            normed, factor = norm_rows(x[rows, :])
            grad = de[rows, :]
            inner = grad * normed
            dn = grad * scale
            mean = jnp.mean(dn, axis=-1, keepdims=True)
            along = jnp.mean(dn * normed, axis=-1, keepdims=True)
            result = g[rows, :] + factor * (dn - mean - normed * along)
            out[rows, :] = result
            if low is not None:
                low[rows, :] = result.astype(BF)
            return (carry[0] + fold(grad), carry[1] + fold(inner))

        zero = jnp.zeros((8, width), F32)
        shift_sum, scale_sum = lax.fori_loop(0, UNIT // CHUNK, step, (zero, zero), unroll=True)
        stats[pl.ds(slot, 1), :] += total(shift_sum)
        stats[pl.ds(4 + slot, 1), :] += total(scale_sum)


def lane_ids(rows):
    return lax.broadcasted_iota(jnp.int32, (rows, LANES), 1)


def head_half(values, half):
    ids = lane_ids(values.shape[0])
    keep = ids < HEAD_WIDTH if half == 0 else ids >= HEAD_WIDTH
    return jnp.where(keep, values.astype(F32), 0.0)


def query_marks(slot):
    return jnp.where(lane_ids(UNIT) == slot, 1.0, 0.0).astype(BF)


def key_marks(slots):
    ids = lane_ids(UNIT)
    parts = [jnp.where((ids < SLOTS) & (ids != slot), FAR, 0.0).astype(BF) for slot in slots]
    return jnp.concatenate(parts, axis=0)


def pair_lanes(pair):
    return pl.ds(pl.multiple_of(pair * LANES, LANES), LANES)


def kv_kernel(info, work, weights):
    rows = weights[0].shape[0] // 4
    plan = plan_of((work.w.at[0], work.w.at[1]), 1, rows)
    start_rows(weights, info[0], plan, work.sems)
    work.need("x")
    entry_rows(work.x, work.mod, info, 0, work.entry)
    work.flush("entry")
    entry = work.entry[...]
    wait_rows(weights, plan, work.sems, range(4))
    work.kv[0] = dot_nt(entry, work.w[0]).astype(BF)
    work.flush("kv", 0)
    wait_rows(weights, plan, work.sems, range(4, 8))
    work.kv[1] = (dot_nt(entry, work.w[1]) + work.biases[2:3, :]).astype(BF)
    work.flush("kv", 1)


def q_kernel(info, work, weights):
    rows = weights[0].shape[0] // 4
    plan = plan_of((work.w,), 0, rows)
    start_rows(weights, info[0], plan, work.sems)
    work.need("entry")
    wait_rows(weights, plan, work.sems, range(4))
    work.q[...] = (dot_nt(work.entry[...], work.w[...]) + work.biases[0:1, :]).astype(BF)
    work.flush("q")


def soft_pair(work, q_pair, keys, values, marks, logs, pair, span, words=None):
    ids = lane_ids(UNIT)
    results = []
    kept = logs[span, :]
    for half in range(2):
        left = (head_half(q_pair, half) * HEAD_WIDTH**-0.5).astype(BF)
        if marks is not None:
            left = jnp.concatenate([left, marks], axis=1)
        scores = dot_nt(left, keys)
        if words is not None:
            scores = jnp.where(ids < words, scores, FAR)
        peak = jnp.max(scores, axis=-1, keepdims=True)
        both = dot_nn(jnp.exp(scores - peak).astype(BF), values)
        sums = both[:, LANES:]
        results.append(both[:, :LANES] / sums)
        kept = jnp.where(ids == 2 * pair + half, peak + jnp.log(sums), kept)
    logs[span, :] = kept
    return jnp.where(ids < HEAD_WIDTH, results[0], results[1]).astype(BF)


def self_kernel(info, work, weights):
    rows = weights[0].shape[0] // 4
    sems = work.sems
    plan = [(s, 3 * rows, rows, work.wo.at[pl.ds(s * rows, rows)]) for s in range(4)]
    start_rows(weights, info[0], plan, sems)
    share = work.x.shape[0]
    blocks = share // UNIT
    marks = key_marks([info[1 + b] for b in range(2 * blocks)])
    ones = jnp.ones((2 * share, LANES), BF)
    logs, mixed = work.logs, work.mixed
    logs[...] = jnp.zeros(logs.shape, F32)
    work.need("q", "kv_own", "kv_sib")

    def both(which, lanes):
        return jnp.concatenate([work.kv_own[which, :, lanes], work.kv_sib[which, :, lanes]], axis=0)

    def step(pair, carry):
        lanes = pair_lanes(pair)
        keys = jnp.concatenate([both(0, lanes), marks], axis=1)
        values = jnp.concatenate([both(1, lanes), ones], axis=1)
        for block in range(blocks):
            span = pl.ds(block * UNIT, UNIT)
            mixed[span, lanes] = soft_pair(
                work,
                work.q[span, lanes],
                keys,
                values,
                query_marks(info[1 + block]),
                logs,
                pair,
                span,
            )
        return carry

    lax.fori_loop(0, mixed.shape[1] // LANES, step, 0)
    work.flush("mixed")
    work.lse[...] = logs[...].T[: work.lse.shape[0], :]
    work.flush("lse")
    wait_rows(weights, plan, sems, range(4))
    work.sum[...] = dot_nn(mixed[...], work.wo[...]) + work.bias[...].astype(F32)
    work.need("x")
    residual_rows(work.x, work.mod, info, 2, work.sum, work.branch, work.out)
    work.flush("branch")
    work.flush("out")


def cross_kernel(info, work, weights, words):
    rows = weights[0].shape[0] // 4
    sems = work.sems
    order = (1, 2, 0, 3)
    plan = [
        (shard, order[i // 4] * rows, count, dst)
        for i, (shard, _, count, dst) in enumerate(
            plan_of((work.wk, work.wv, work.wq, work.wo), 0, rows)
        )
    ]
    start_rows(weights, info[0], plan, sems)
    work.need("x")
    entry_rows(work.x, work.mod, info, 3, work.entry)
    work.flush("entry")
    work.need("text")
    wait_rows(weights, plan, sems, range(0, 4))
    work.kv[0] = dot_nt(work.text[...], work.wk[...]).astype(BF)
    wait_rows(weights, plan, sems, range(4, 8))
    work.kv[1] = (dot_nt(work.text[...], work.wv[...]) + work.biases[5:6, :]).astype(BF)
    work.flush("kv")
    wait_rows(weights, plan, sems, range(8, 12))
    work.q[...] = (dot_nt(work.entry[...], work.wq[...]) + work.biases[3:4, :]).astype(BF)
    work.flush("q")
    ones = jnp.ones((LANES, LANES), BF)
    logs, mixed = work.logs, work.mixed
    logs[...] = jnp.zeros(logs.shape, F32)

    def step(pair, carry):
        lanes = pair_lanes(pair)
        for block in range(mixed.shape[0] // UNIT):
            span = pl.ds(block * UNIT, UNIT)
            own = pl.ds(pl.multiple_of(info[1 + block] * LANES, LANES), LANES)
            mixed[span, lanes] = soft_pair(
                work,
                work.q[span, lanes],
                work.kv[0, own, lanes],
                jnp.concatenate([work.kv[1, own, lanes], ones], axis=1),
                None,
                logs,
                pair,
                span,
                words,
            )
        return carry

    lax.fori_loop(0, mixed.shape[1] // LANES, step, 0, unroll=2)
    work.flush("mixed")
    work.lse[...] = logs[...].T[: work.lse.shape[0], :]
    work.flush("lse")
    wait_rows(weights, plan, sems, range(12, 16))
    work.sum[...] = dot_nn(mixed[...], work.wo[...]) + work.bias[...].astype(F32)
    residual_rows(work.x, work.mod, info, 5, work.sum, work.branch, work.out)
    work.flush("branch")
    work.flush("out")


def hidden_plan(refs, buffer, which):
    rows, half = buffer.shape[1], refs[0].shape[0] // 2
    first = which * rows if half == rows else 0
    return [
        (shard, first + row, half, buffer.at[shard, pl.ds(row, half)])
        for shard in range(4)
        for row in range(0, rows, half)
    ]


def bend_rows(before, bias, active, slope, lanes):
    for row in range(0, before.shape[0], CHUNK):
        span = pl.ds(row, CHUNK)
        values = before[span, :] + bias
        square = values * values
        half = 1.0 / (1.0 + jnp.exp(values * (-2.0 * ROOT - (2.0 * ROOT * CUBIC) * square)))
        act = values * half
        active[span, lanes] = act.astype(BF)
        slope[span, lanes] = (
            half + act * (1.0 - half) * (2.0 * ROOT + (6.0 * ROOT * CUBIC) * square)
        ).astype(BF)


def hidden_kernel(info, work, ups, downs):
    sems = work.sems
    width = work.x.shape[1]
    up_plan = hidden_plan(ups, work.up, 0)
    down_plan = hidden_plan(downs, work.down, 1)
    start_rows(ups, info[0], up_plan, sems)
    start_rows(downs, info[0], down_plan, work.down_sems)
    work.need("x")
    entry_rows(work.x, work.mod, info, 6, work.entry)
    work.flush("entry")

    def columns(shard):
        return pl.ds(pl.multiple_of(shard * width, width), width)

    wait_rows(ups, up_plan, sems, range(len(up_plan)))
    wait_rows(downs, down_plan, work.down_sems, range(len(down_plan)))
    work.sum[...] = jnp.zeros(work.sum.shape, F32) + work.bias[...].astype(F32)

    def step(shard, carry):
        lanes = columns(shard)
        work.before0[...] = dot_nn(work.entry[...], work.up[shard])
        bend_rows(work.before0, work.up_bias[:, lanes], work.active, work.slope, lanes)
        work.sum[...] += dot_nn(work.active[:, lanes], work.down[shard])
        return carry

    lax.fori_loop(0, 4, step, 0)
    work.flush("active")
    work.flush("slope")
    low = work.low if work.has("low") else None
    residual_rows(work.x, work.mod, info, 8, work.sum, work.branch, work.out, low)
    work.flush("branch")
    work.flush("out")
    if low is not None:
        work.flush("low")


def hidden_back_kernel(info, work, ups, downs, active):
    sems = work.sems
    width = work.x.shape[1]
    up_plan = hidden_plan(ups, work.up, 0)
    down_plan = hidden_plan(downs, work.down, 1)
    start_rows(downs, info[0], down_plan, work.down_sems)
    start_rows(ups, info[0], up_plan, sems)
    actives = [
        pltpu.make_async_copy(
            active.at[:, pl.ds(pl.multiple_of(rank * width, width), width)],
            work.acts.at[i],
            work.act_sems.at[i],
        )
        for i, rank in enumerate((info[7], info[5]))
    ]
    for copy in actives:
        copy.start()
    work.stats[...] = jnp.zeros(work.stats.shape, F32)
    stats = work.stats.at[pl.ds(48, 24)]
    work.need("g", "branch")
    gate_back(work.g, work.mod, info, 8, work.branch, work.gb, stats)
    work.need("slope")

    def columns(shard):
        return pl.ds(pl.multiple_of(shard * width, width), width)

    def bend(before, shard, lanes):
        sums = jnp.zeros((8, width), F32)
        for row in range(0, work.x.shape[0], CHUNK):
            span = pl.ds(row, CHUNK)
            low = (before[span, :] * work.slope[span, lanes].astype(F32)).astype(BF)
            work.d_before[span, lanes] = low
            sums += fold(low.astype(F32))
        stats[pl.ds(13 + shard, 1), :] = total(sums)

    wait_rows(downs, down_plan, work.down_sems, range(len(down_plan)))
    wait_rows(ups, up_plan, sems, range(len(up_plan)))
    work.de[...] = jnp.zeros(work.de.shape, F32)

    def step(shard, carry):
        lanes = columns(shard)
        work.before0[...] = dot_nt(work.gb[...], work.down[shard])
        bend(work.before0, shard, lanes)
        work.de[...] += dot_nt(work.d_before[:, lanes], work.up[shard])
        return carry

    lax.fori_loop(0, 4, step, 0)
    work.need("entry")
    left, right = work.entry[...].T, work.gb[...].T
    for name, index, rank in (("send", 0, info[7]), ("keep", 1, info[5])):
        out = work.outs[name][1]
        out[:, :width] = dot_nn(left, work.d_before[:, columns(rank)]).astype(BF)
        actives[index].wait()
        out[:, width:] = dot_nn(right, work.acts[index]).astype(BF)
        work.flush(name)
    work.need("x")
    norm_back_rows(work.x, work.g, work.de, work.mod, info, 6, work.out, stats)
    work.flush("out")


def pair_grads(info, work, members):
    rows = members[0][0].shape[0]
    low = lane_ids(rows) < HEAD_WIDTH
    step = 3 * LANES
    for at in range(len(members) // 2):
        products = [dot_nn(left, right) for left, right in members[2 * at : 2 * at + 2]]
        (a0, a1, a2), (b0, b1, b2) = [
            [p[:, i * LANES : (i + 1) * LANES] for i in range(3)] for p in products
        ]
        even = (a0, b0, jnp.where(low, a1, pltpu.roll(b1, HEAD_WIDTH, 1)))
        a1, b1 = pltpu.roll(a1, HEAD_WIDTH, 1), pltpu.roll(b1, HEAD_WIDTH, 1)
        a2r, b2r = pltpu.roll(a2, HEAD_WIDTH, 1), pltpu.roll(b2, HEAD_WIDTH, 1)
        odd = (jnp.where(low, a1, a2r), jnp.where(low, b1, b2r), jnp.where(low, a2r, b2))
        first = info[5] % 2 == 0
        for i, (mine, other) in enumerate(zip(even, odd)):
            lanes = pl.ds(at * step + i * LANES, LANES)
            work.outs["keep"][1][:, lanes] = jnp.where(first, mine, other).astype(BF)
            work.outs["send"][1][:, lanes] = jnp.where(first, other, mine).astype(BF)
    work.flush("send")
    work.flush("keep")


def chip_lanes(info, width):
    return pl.ds(pl.multiple_of(info[6] * (width // 2), width // 2), width // 2)


def query_output_kernel(info, work, weights):
    work.need("entry", "gb", "dq", "mixed")
    lanes = chip_lanes(info, work.dq.shape[1])
    pair_grads(
        info,
        work,
        [
            (work.entry[...].T, work.dq[:, lanes]),
            (work.gb[...].T, work.mixed[:, lanes]),
        ],
    )


def cross_back_kernel(info, work, weights, words):
    rows = weights[0].shape[0] // 4
    sems = work.sems
    plan = [
        (shard, (3 * rows, 0)[i // 4], count, dst)
        for i, (shard, _, count, dst) in enumerate(plan_of((work.wo, work.wq), 0, rows))
    ]
    start_rows(weights, info[0], plan, sems)
    work.stats[...] = work.early[...]
    stats = work.stats.at[pl.ds(24, 24)]
    work.need("g", "branch")
    gate_back(work.g, work.mod, info, 5, work.branch, work.gb, stats)
    wait_rows(weights, plan, sems, range(0, 4))
    work.d_mixed[...] = dot_nt(work.gb[...], work.wo[...]).astype(BF)
    work.dkv_sum[...] = jnp.zeros(work.dkv_sum.shape, F32)
    real = lax.broadcasted_iota(jnp.int32, (LANES, UNIT), 0) < words
    work.need("q", "kv", "lse")

    def step(pair, carry):
        lanes = pair_lanes(pair)
        for block in range(work.q.shape[0] // UNIT):
            span = pl.ds(block * UNIT, UNIT)
            own = pl.ds(pl.multiple_of(info[1 + block] * LANES, LANES), LANES)
            q_pair = work.q[span, lanes]
            d_pair = work.d_mixed[span, lanes]
            keys = work.kv[0, own, lanes]
            values = work.kv[1, own, lanes]
            lefts, grads, turned, probs_low, scores_low = [], [], [], [], []
            for half in range(2):
                left = (head_half(q_pair, half) * HEAD_WIDTH**-0.5).astype(BF)
                grad = head_half(d_pair, half).astype(BF)
                logs = work.lse[pl.ds(2 * pair + half, 1), span]
                probs = jnp.where(real, jnp.exp(dot_nt(keys, left) - logs), 0.0)
                d_probs = dot_nt(values, grad)
                inner = jnp.sum(probs * d_probs, axis=0, keepdims=True)
                lefts.append(left)
                grads.append(grad)
                turned.append(head_half(keys, half).T.astype(BF))
                probs_low.append(probs.astype(BF))
                scores_low.append((probs * (d_probs - inner)).astype(BF))
            wide_scores = jnp.concatenate(scores_low, axis=1)
            grad_v = dot_nn(jnp.concatenate(probs_low, axis=1), jnp.concatenate(grads, axis=0))
            grad_k = dot_nn(wide_scores, jnp.concatenate(lefts, axis=0))
            grad_q = dot_nn(
                jnp.concatenate(turned, axis=1), jnp.concatenate(scores_low, axis=0)
            )
            work.dq[span, lanes] = (grad_q.T * HEAD_WIDTH**-0.5).astype(BF)
            work.dkv_sum[0, own, lanes] += grad_k
            work.dkv_sum[1, own, lanes] += grad_v
        return carry

    lax.fori_loop(0, work.q.shape[1] // LANES, step, 0, unroll=2)
    work.dkv[...] = work.dkv_sum[...].astype(BF)
    work.need("entry", "text", "mixed")
    lanes = chip_lanes(info, work.dq.shape[1])
    text = work.text[...].T
    pair_grads(
        info,
        work,
        [
            (work.entry[...].T, work.dq[:, lanes]),
            (text, work.dkv[0, :, lanes]),
            (text, work.dkv[1, :, lanes]),
            (work.gb[...].T, work.mixed[:, lanes]),
        ],
    )
    stats[13:14, :] = total(fold(work.dq[...].astype(F32)))
    stats[14:15, :] = total(fold(work.dkv[1].astype(F32)))
    wait_rows(weights, plan, sems, range(4, 8))
    work.de[...] = dot_nn(work.dq[...], work.wq[...])
    work.need("x")
    norm_back_rows(work.x, work.g, work.de, work.mod, info, 3, work.out, stats)
    work.flush("out")


def self_back_kernel(info, work, weights):
    rows = weights[0].shape[0] // 4
    sems = work.sems
    plan = [(s, 3 * rows, rows, work.wo.at[pl.ds(s * rows, rows)]) for s in range(4)]
    start_rows(weights, info[0], plan, sems)
    work.stats[...] = work.early[...]
    stats = work.stats.at[pl.ds(0, 24)]
    work.need("g", "branch")
    gate_back(work.g, work.mod, info, 2, work.branch, work.gb, stats)
    work.flush("gb")
    share = work.g.shape[0]
    blocks = share // UNIT
    marks = key_marks([info[1 + b] for b in range(2 * blocks)])
    wait_rows(weights, plan, sems, range(4))
    work.d_mixed[...] = dot_nt(work.gb[...], work.wo[...]).astype(BF)
    work.need("q", "kv_own", "kv_sib", "lse")

    def both(which, lanes):
        return jnp.concatenate([work.kv_own[which, :, lanes], work.kv_sib[which, :, lanes]], axis=0)

    def step(pair, carry):
        lanes = pair_lanes(pair)
        keys = both(0, lanes)
        values = both(1, lanes)
        marked = jnp.concatenate([keys, marks], axis=1)
        turned = jnp.concatenate([head_half(keys, half).T.astype(BF) for half in range(2)], axis=1)
        lefts, grads, probs_low, scores_low = [], [], [], []
        for block in range(blocks):
            span = pl.ds(block * UNIT, UNIT)
            q_pair = work.q[span, lanes]
            d_pair = work.d_mixed[span, lanes]
            ends = query_marks(info[1 + block])
            for half in range(2):
                left = (head_half(q_pair, half) * HEAD_WIDTH**-0.5).astype(BF)
                grad = head_half(d_pair, half).astype(BF)
                logs = work.lse[pl.ds(2 * pair + half, 1), span]
                probs = jnp.exp(dot_nt(marked, jnp.concatenate([left, ends], axis=1)) - logs)
                d_probs = dot_nt(values, grad)
                inner = jnp.sum(probs * d_probs, axis=0, keepdims=True)
                lefts.append(left)
                grads.append(grad)
                probs_low.append(probs.astype(BF))
                scores_low.append((probs * (d_probs - inner)).astype(BF))
            grad_q = dot_nn(turned, jnp.concatenate(scores_low[-2:], axis=0))
            work.dq[span, lanes] = (grad_q.T * HEAD_WIDTH**-0.5).astype(BF)
        grad_v = dot_nn(jnp.concatenate(probs_low, axis=1), jnp.concatenate(grads, axis=0))
        grad_k = dot_nn(jnp.concatenate(scores_low, axis=1), jnp.concatenate(lefts, axis=0))
        for which, grad in ((0, grad_k.astype(BF)), (1, grad_v.astype(BF))):
            work.dkv_own[which, :, lanes] = grad[:share]
            work.dkv_give[which, :, lanes] = grad[share:]
        return carry

    lax.fori_loop(0, work.q.shape[1] // LANES, step, 0)
    work.flush("dkv_give")
    work.flush("dkv_own")
    work.flush("dq")


def qkv_back_kernel(info, work, weights):
    rows = weights[0].shape[0] // 4
    sems = work.sems
    plan = plan_of((work.wq, work.wk, work.wv), 0, rows)
    start_rows(weights, info[0], plan, sems)
    work.stats[...] = work.early[...]
    stats = work.stats.at[pl.ds(0, 24)]
    work.need("dq")
    stats[13:14, :] = total(fold(work.dq[...].astype(F32)))
    work.need("dkv_own", "dkv_sib")
    for which in range(2):
        work.dkv[which] = (
            work.dkv_own[which].astype(F32) + work.dkv_sib[which].astype(F32)
        ).astype(BF)
    stats[14:15, :] = total(fold(work.dkv[1].astype(F32)))
    work.need("entry")
    lanes = chip_lanes(info, work.dq.shape[1])
    entry = work.entry[...].T
    pair_grads(info, work, [(entry, work.dkv[0, :, lanes]), (entry, work.dkv[1, :, lanes])])
    wait_rows(weights, plan, sems, range(0, 12))
    work.de[...] = (
        dot_nn(work.dq[...], work.wq[...])
        + dot_nn(work.dkv[0], work.wk[...])
        + dot_nn(work.dkv[1], work.wv[...])
    )
    work.need("x", "g")
    low = work.low if work.has("low") else None
    norm_back_rows(work.x, work.g, work.de, work.mod, info, 0, work.out, stats, low)
    work.flush("out")
    if low is not None:
        work.flush("low")


def merge_kernel(info, *refs, spots, after):
    chains = len(spots)
    ins, outs = refs[: 4 * chains], refs[4 * chains + after :]
    for chain, (result, column) in enumerate(spots):
        for side in range(2):
            received, kept = ins[4 * chain + 2 * side], ins[4 * chain + 2 * side + 1]
            out = outs[2 * result + side]
            lanes = pl.ds(column, received.shape[2])
            out[:, :, lanes] = (received[...].astype(F32) + kept[...].astype(F32)).astype(BF)


def gate(arrays, after):
    count = len(arrays)
    return pl.pallas_call(
        lambda *refs: None,
        out_shape=[shape(*a.shape, dtype=a.dtype) for a in arrays],
        in_specs=[ANY] * (count + len(after)),
        out_specs=[ANY] * count,
        input_output_aliases={i: i for i in range(count)},
        cost_estimate=lasting(0.5),
        name="gate",
    )(*arrays, *after)


def pack_kernel(info, *refs, groups, after):
    count = sum(len(members) for _, members in groups)
    sources, rest = refs[:count], refs[count + after :]
    (in_sems, out_sems), rest = rest[-2:], rest[:-2]
    outs, held = rest[: 2 * len(groups)], rest[2 * len(groups) :]
    spots = []
    at = 0
    for index, (layer, members) in enumerate(groups):
        rows = held[index].shape[0]
        piece_rows = rows // 4
        for quarter in range(4):
            row = quarter * piece_rows
            source = sources[at + quarter * len(members) // 4]
            src = source.at[layer, pl.ds(row % source.shape[1], piece_rows)]
            spots.append((index, quarter, held[index].at[pl.ds(row, piece_rows)], src))
        at += len(members)

    def arriving(place):
        _, _, spot, src = spots[place]
        return pltpu.make_async_copy(src, spot, in_sems.at[place])

    def leaving(index, which):
        out = outs[2 * index + (0 if which == 2 else 1)]
        rows = out.shape[0]
        src = held[index] if which == 2 else held[index].at[pl.ds(which * rows, rows)]
        return pltpu.make_async_copy(src, out, out_sems.at[2 * index + (0 if which == 2 else 1)])

    def by_parity(act):
        for parity in range(2):

            @pl.when(info[0] % 2 == parity)
            def _(parity=parity):
                act(parity)

    for place in range(len(spots)):
        arriving(place).start()
    for index in range(len(groups)):
        for quarter in range(4):
            arriving(4 * index + quarter).wait()
        by_parity(lambda parity: leaving(index, parity).start())
        leaving(index, 2).start()
    for index in range(len(groups)):
        by_parity(lambda parity: leaving(index, parity).wait())
        leaving(index, 2).wait()


def mod_kernel(condition, mod, mod_bias, q, v, cq, cv, up, out):
    narrow, units, columns = q.shape[1], up.shape[1], mod.shape[1]
    out[...] = jnp.zeros(out.shape, F32)
    for layer in range(LAYERS):
        row = pl.ds(layer, 1)
        out[layer, 0:SLOTS, 0:columns] = dot_nt(condition[...], mod[layer]) + mod_bias[
            row, :
        ].astype(F32)
        out[layer, 4:5, 0:units] = up[row, :].astype(F32)
        out[layer, 5:6, 0:narrow] = q[row, :].astype(F32)
        out[layer, 6:7, 0:narrow] = v[row, :].astype(F32)
        out[layer, 7:8, 0:narrow] = cq[row, :].astype(F32)
        out[layer, 4:5, 1024 : 1024 + narrow] = cv[row, :].astype(F32)


def assemble_kernel(info, *refs, narrow, units, columns):
    parts, (mods, narrows, ups) = refs[:4], refs[4:]
    narrows[...] = jnp.zeros(narrows.shape, F32)
    for rank in range(4):

        @pl.when(info[5] == rank)
        def _(rank=rank):
            for shard in range(4):
                part = parts[shard ^ rank]
                for layer in range(LAYERS):
                    mods[layer, :, shard * columns : (shard + 1) * columns] = part[
                        layer, 0:SLOTS, 0:columns
                    ]
                    ups[layer, :, shard * units : (shard + 1) * units] = part[layer, 4:5, 0:units]
                    at = slice(shard * narrow, (shard + 1) * narrow)
                    for row, source in ((0, 5), (2, 6), (3, 7)):
                        narrows[layer, row : row + 1, at] = part[
                            layer, source : source + 1, 0:narrow
                        ]
                    narrows[layer, 5:6, at] = part[layer, 4:5, 1024 : 1024 + narrow]


def collect_kernel(info, *refs, narrow, units, columns):
    stats, condition, out = refs[: 2 * LAYERS], refs[2 * LAYERS], refs[2 * LAYERS + 1]
    sums = refs[2 * LAYERS + 2]
    width = stats[0].shape[1]
    work = out
    out = refs[2 * LAYERS + 3]
    out[...] = jnp.zeros(out.shape, F32)
    for layer in range(LAYERS):
        sums[...] = stats[2 * layer][...] + stats[2 * layer + 1][...]
        base = 8 * layer
        out[base + 4 : base + 5, width : 2 * width] = sums[60:61, :]
        out[base + 5 : base + 6, 0:width] = sums[12:13, :]
        out[base + 5 : base + 6, width : 2 * width] = sums[36:37, :]
        for index in range(2):
            out[base + 6 + index : base + 7 + index, 512 : 512 + width] = condition[
                2 * layer + index : 2 * layer + index + 1, :
            ].astype(F32)
        for rank in range(4):

            @pl.when(info[5] == rank)
            def _(rank=rank, base=base):
                first = rank * columns
                for index in range(9):
                    low = max(first, index * width)
                    high = min(first + columns, (index + 1) * width)
                    if low < high:
                        row = (index // 3) * 24 + (index % 3) * 4
                        out[base : base + 4, low - first : high - first] = sums[
                            row : row + 4, low - index * width : high - index * width
                        ]
                out[base + 4 : base + 5, 0:units] = sums[61 + rank : 62 + rank, :]
                own = slice(rank * narrow, (rank + 1) * narrow)
                out[base + 6 : base + 7, 0:narrow] = sums[13:14, own]
                out[base + 6 : base + 7, 256 : 256 + narrow] = sums[14:15, own]
                out[base + 7 : base + 8, 0:narrow] = sums[37:38, own]
                out[base + 7 : base + 8, 256 : 256 + narrow] = sums[38:39, own]
    work[...] = out[...].astype(BF)


def spread_kernel(info, gathered, grad, bias_grad, q, v, cq, cv, up, o1, o2, o3, rows, conditions):
    count = gathered.shape[0]
    columns, part = grad.shape[2], grad.shape[1]
    width, narrow, units = conditions.shape[1], q.shape[1], up.shape[1]
    shift = lax.rem(width - info[8] * part, width)
    for index in range(count):
        for slot in range(SLOTS):
            row = 8 * (slot // 2) + 6 + slot % 2
            conditions[SLOTS * index + slot : SLOTS * index + slot + 1, :] = gathered[
                index ^ info[8], row : row + 1, 512 : 512 + width
            ].astype(F32)
    turned = pltpu.roll(conditions[...], shift, 1)[:, :part].T
    for layer in range(LAYERS):
        base = 8 * layer
        sums = jnp.zeros((8, gathered.shape[2]), F32)
        for index in range(count):
            values = gathered[index ^ info[8]].astype(F32)[base : base + 8]
            sums += values
            rows[SLOTS * index : SLOTS * (index + 1), :] = values[0:SLOTS, 0:columns]
        grad[layer] = jnp.dot(
            turned, rows[...], precision=lax.Precision.HIGHEST, preferred_element_type=F32
        )
        at = slice(layer, layer + 1)
        bias_grad[at, :] = jnp.sum(sums[0:SLOTS, 0:columns], axis=0, keepdims=True)
        up[at, :] = sums[4:5, 0:units]
        q[at, :] = sums[6:7, 0:narrow]
        v[at, :] = sums[6:7, 256 : 256 + narrow]
        cq[at, :] = sums[7:8, 0:narrow]
        cv[at, :] = sums[7:8, 256 : 256 + narrow]
        for out, row, lane in ((o1, 5, 0), (o2, 5, width), (o3, 4, width)):
            own = jnp.broadcast_to(sums[row : row + 1, lane : lane + width], (8, width))
            out[at, :] = pltpu.roll(own, shift, 1)[0:1, :part]


def finish_kernel(*refs, wide, spots):
    parts, outs = refs[: 2 * len(spots)], refs[2 * len(spots) :]
    step = 3 * LANES
    for chain, places in enumerate(spots):
        values = parts[2 * chain][0].astype(F32) + parts[2 * chain + 1][0].astype(F32)
        at = 0
        for layer, pair in places:
            if wide:
                width = outs[0].shape[2]
                for out in outs:
                    out[layer] = values[:, at : at + width]
                    at += width
                continue
            both = values[:, at : at + step]
            at += step
            first = jnp.concatenate(
                [both[:, :LANES], both[:, 2 * LANES : 2 * LANES + HEAD_WIDTH]], axis=1
            )
            second = jnp.concatenate(
                [both[:, LANES : 2 * LANES], both[:, 2 * LANES + HEAD_WIDTH :]], axis=1
            )
            for out, matrix in zip(outs[2 * pair : 2 * pair + 2], (first, second)):
                out[layer] = matrix if out.shape[1:] == matrix.shape else matrix.T


def join_kernel(info, rows, other, out):
    share = rows.shape[0]
    for core in range(2):

        @pl.when(info[5] % 2 == core)
        def _(core=core):
            out[pl.ds(core * share, share), :] = rows[...]
            out[pl.ds((1 - core) * share, share), :] = other[...]


def tensor_hop(values, step):
    return lax.ppermute(values, "tensor", [(i, i ^ step) for i in range(4)])


def dp_hop(values, step):
    size = lax.axis_size("dp")
    return lax.ppermute(values, "dp", [(i, i ^ step) for i in range(size)])


def time_features(moments, width):
    half = width // 2
    rates = jnp.exp(-math.log(10000.0) * jnp.arange(half, dtype=F32) / half)
    angles = moments.astype(F32)[:, None] * rates[None, :]
    return jnp.concatenate([jnp.cos(angles), jnp.sin(angles)], axis=1)


def shards(
    tokens,
    text,
    timesteps,
    item_frames,
    cotangent,
    self_query,
    self_query_bias,
    self_key,
    self_value,
    self_value_bias,
    self_output,
    self_output_bias,
    cross_query,
    cross_query_bias,
    cross_key,
    cross_value,
    cross_value_bias,
    cross_output,
    cross_output_bias,
    hidden_up,
    hidden_up_bias,
    hidden_down,
    hidden_down_bias,
    modulation,
    modulation_bias,
):
    frames, width = tokens.shape
    words = text.shape[1]
    columns = modulation.shape[2]
    narrow = self_query.shape[2]
    units = hidden_up.shape[2]
    rank = lax.axis_index("tensor")
    me = lax.axis_index("dp")
    size = lax.axis_size("dp")
    core = rank % 2
    share = frames // 2
    blocks = share // UNIT
    unit = width // size
    turn = lambda values: jnp.swapaxes(values, 1, 2)

    order = jnp.arange(SLOTS, dtype=jnp.int32)
    ends = jnp.sum(jnp.where(order[:, None] <= order[None, :], item_frames[:, None], 0), axis=0)
    turned = (jnp.arange(frames // UNIT, dtype=jnp.int32) + core * blocks) % (2 * blocks)
    slots = jnp.sum((turned[:, None] * UNIT >= ends[None, :]).astype(jnp.int32), axis=1)
    places = jnp.stack([rank, rank // 2, rank ^ 1, me]).astype(jnp.int32)
    info = jnp.concatenate([(rank * 2 + me % 2)[None].astype(jnp.int32), slots, places])

    def pack(members, after):
        rows = [sum(a.shape[1] for a in some) for _, some in members]
        outs = [shape(r // part, width, dtype=BF) for r in rows for part in (1, 2)]
        arrays = [a for _, some in members for a in some]
        return pl.pallas_call(
            partial(
                pack_kernel,
                groups=[(layer, [None] * len(some)) for layer, some in members],
                after=len(after),
            ),
            out_shape=outs,
            in_specs=[SMALL] + [ANY] * (len(arrays) + len(after)),
            out_specs=[ANY] * len(outs),
            scratch_shapes=[
                *[pltpu.VMEM((r, width), BF) for r in rows],
                pltpu.SemaphoreType.DMA((4 * len(members),)),
                pltpu.SemaphoreType.DMA((2 * len(members),)),
            ],
            compiler_params=pltpu.CompilerParams(vmem_limit_bytes=VMEM_BYTES),
            cost_estimate=lasting(1.0),
            name="pack_weights",
        )(info, *arrays, *after)

    kinds = (
        [turn(self_query), turn(self_key), turn(self_value), self_output],
        [turn(cross_query), turn(cross_key), turn(cross_value), cross_output],
        [hidden_up, hidden_down],
        [hidden_up],
        [hidden_down],
    )
    all_groups = [(0, kinds[0]), (0, kinds[1]), (0, kinds[2])]
    all_groups += [(1, kinds[index]) for index in (0, 1, 3, 4)]
    packed = [*pack(all_groups[:1], []), *pack(all_groups[1:], [])]

    condition = jax.nn.silu(time_features(timesteps, width)).astype(BF)
    mine = plain(
        mod_kernel,
        "modulation_rows",
        None,
        [
            condition,
            turn(modulation),
            modulation_bias,
            self_query_bias,
            self_value_bias,
            cross_query_bias,
            cross_value_bias,
            hidden_up_bias,
        ],
        [shape(LAYERS, 8, -(-columns // LANES) * LANES)],
        after=[packed[2]],
    )
    others = [tensor_hop(mine, 1), tensor_hop(mine, 2)]
    others.append(tensor_hop(others[0], 2))
    mods, narrow_biases, up_biases = plain(
        partial(assemble_kernel, narrow=narrow, units=units, columns=columns),
        "modulation_of_all",
        info,
        [mine, *others],
        [
            shape(LAYERS, SLOTS, 4 * columns),
            shape(LAYERS, 8, 4 * narrow),
            shape(LAYERS, 1, 4 * units),
        ],
    )
    out_biases = [
        b.reshape(LAYERS, 1, width) for b in (self_output_bias, cross_output_bias, hidden_down_bias)
    ]

    firsts = [packed[2 * index + 1] for index in range(len(all_groups))]
    owns = [packed[2 * index] for index in range(len(all_groups))]
    along_x, along_y, over_x, over_y, sibs = [[None] * len(all_groups) for _ in range(5)]

    def leave(index):
        along_x[index] = tensor_hop(firsts[index], 2)
        sibs[index] = tensor_hop(owns[index], 1)

    def go_on(index):
        along_y[index] = dp_hop(along_x[index], 1)
        over_x[index] = tensor_hop(along_x[index], 1)

    def end(index):
        over_y[index] = tensor_hop(along_y[index], 1)

    def weights_of(index):
        return [
            owns[index],
            sibs[index],
            along_x[index],
            along_y[index],
            over_x[index],
            over_y[index],
        ]

    def open_gate(after, leaving=(), at_x=(), at_y=()):
        places = [(firsts, i) for i in leaving]
        places += [(along_x, i) for i in at_x] + [(along_y, i) for i in at_y]
        opened = gate([values[i] for values, i in places], after)
        for (values, i), array in zip(places, opened):
            values[i] = array
        for i in leaving:
            leave(i)
        for i in at_x:
            go_on(i)
        for i in at_y:
            end(i)
        return list(opened)

    leave(0)
    open_gate([mine], [], [0])
    open_gate([others[1]], [1, 2])
    go_on(1)
    open_gate([mods], [], [], [0])

    text_rows = jnp.pad(text, ((0, 0), (0, LANES - words), (0, 0))).reshape(-1, width)
    whole = pltpu.VMEM((width, width), BF)
    four = pltpu.VMEM((4, width, units), BF)
    floats = pltpu.VMEM((share, width), F32)
    lows = pltpu.VMEM((share, width), BF)
    sems = lambda n: pltpu.SemaphoreType.DMA((n,))
    frame_low = shape(share, width, dtype=BF)
    frame_high = shape(share, width)
    frame_wide = shape(share, 4 * units, dtype=BF)
    two_low = shape(2, share, width, dtype=BF)
    two_text = shape(2, SLOTS * LANES, width, dtype=BF)
    logs = shape(16, share)
    log_work = pltpu.VMEM((share, LANES), F32)
    stat_shape = shape(72, width)

    x = lax.dynamic_slice_in_dim(tokens, core * share, share).astype(F32)
    kept = []
    for layer in range(LAYERS):
        first = 3 * layer
        mod = (mods, (layer,))
        biases = (narrow_biases, (layer,))
        entry1, kv = run(
            kv_kernel,
            "self_keys_values",
            info,
            dict(x=x),
            dict(mod=mod, biases=biases),
            weights_of(first),
            dict(entry=frame_low, kv=two_low),
            {},
            dict(w=pltpu.VMEM((2, width, width), BF), sems=sems(8)),
            [along_x[1], *owns[1:]] if layer == 0 else [],
            3.0,
        )
        kv_sib = tensor_hop(kv, 1)
        opened = open_gate([entry1], [3, 4]) if layer == 0 else []
        (q,) = run(
            q_kernel,
            "self_query",
            info,
            dict(entry=entry1),
            dict(biases=biases),
            weights_of(first),
            dict(q=frame_low),
            {},
            dict(w=whole, sems=sems(4)),
            [],
            15.0,
        )
        x1, mixed1, lse1, branch1 = run(
            self_kernel,
            "self_attention",
            info,
            dict(q=q, kv_own=kv, kv_sib=kv_sib, x=x),
            dict(mod=mod, bias=(out_biases[0], (layer,))),
            weights_of(first),
            dict(out=frame_high, mixed=frame_low, lse=logs, branch=frame_low),
            {},
            dict(wo=whole, logs=log_work, sum=floats, sems=sems(4)),
            opened,
            8.0,
        )
        opened = open_gate([x1], [5, 6], [2], [1]) if layer == 0 else open_gate([x1], [], [6], [4, 5])
        x2, entry2, cq, ckv, mixed2, lse2, branch2 = run(
            partial(cross_kernel, words=words),
            "cross_attention",
            info,
            dict(x=x1, text=text_rows),
            dict(mod=mod, biases=biases, bias=(out_biases[1], (layer,))),
            weights_of(first + 1),
            dict(
                out=frame_high,
                entry=frame_low,
                q=frame_low,
                kv=two_text,
                mixed=frame_low,
                lse=logs,
                branch=frame_low,
            ),
            {},
            dict(
                wq=whole, wk=whole, wv=whole, wo=whole, logs=log_work, sum=floats, sems=sems(16)
            ),
            opened,
            6.0,
        )
        opened = open_gate([x2], [], [3, 4]) if layer == 0 else open_gate([x2], [], [], [6])
        if layer == 0:
            end(2)
        results = run(
            lambda info, work, w: hidden_kernel(info, work, w[:6], w[6:]),
            "feed_forward",
            info,
            dict(x=x2),
            dict(mod=mod, up_bias=(up_biases, (layer,)), bias=(out_biases[2], (layer,))),
            weights_of(first + 2) + (weights_of(first + 3) if layer else weights_of(first + 2)),
            dict(
                out=frame_high,
                entry=frame_low,
                active=frame_wide,
                slope=frame_wide,
                branch=frame_low,
                **(dict(low=frame_low) if layer == LAYERS - 1 else {}),
            ),
            {},
            dict(
                up=four,
                down=four,
                before0=floats,
                sum=floats,
                sems=sems(8),
                down_sems=sems(8),
            ),
            opened,
            7.0,
        )
        x3, entry3, active, slope, branch3 = results[:5]
        if layer == 0:
            open_gate([x3], [], [5], [3])
        kept.append(
            dict(
                x=x,
                entry1=entry1,
                q=q,
                kv=kv,
                kv_sib=kv_sib,
                mixed1=mixed1,
                lse1=lse1,
                branch1=branch1,
                x1=x1,
                entry2=entry2,
                cq=cq,
                ckv=ckv,
                mixed2=mixed2,
                lse2=lse2,
                branch2=branch2,
                x2=x2,
                entry3=entry3,
                active=active,
                slope=slope,
                branch3=branch3,
            )
        )
        x = x3

    def join(rows):
        return plain(
            join_kernel,
            "join_rows",
            info,
            [rows, tensor_hop(rows, 1)],
            [shape(2 * share, width, dtype=BF)],
        )

    output = join(results[5])

    chains = {}

    def start(name, send, keep):
        view = (size, unit, send.shape[1])
        chains[name] = (tensor_hop(send, 1).reshape(view), keep.reshape(view), 0)

    def held(*names):
        return [chains[name][1] for name in names]

    def advance(names, after=(), joined=None):
        names = [n for n in names if 2 ** chains[n][2] < size]
        if not names:
            return
        ins, in_specs, outs, out_specs, spots = [], [], [], [], []
        wide = all(chains[name][0].shape[2] % (4 * LANES) == 0 for name in names)
        cuts = 2 if wide and not joined else 1
        total_columns = sum(chains[name][0].shape[2] for name in names)
        for name in names:
            received, kept_part, bit = chains[name]
            count, unit, columns = received.shape
            spots.append(
                (0, sum(chains[n][0].shape[2] for n in names[: len(spots)]))
                if joined
                else (len(spots), 0)
            )
            for side in range(2):

                def at(i, info, bit=bit, side=side):
                    return (0, ((info[8] >> bit) & 1) ^ side, 0, i)

                for part in (received, kept_part):
                    ins.append(part.reshape(count // 2, 2, unit, columns))
                    in_specs.append(pl.BlockSpec((count // 2, None, unit, columns // cuts), at))
            if joined and len(spots) > 1:
                continue
            columns = total_columns if joined else columns
            for side in range(2):
                outs.append(shape(count // 2, unit, columns, dtype=BF))
                out_specs.append(
                    pl.BlockSpec((count // 2, unit, columns // cuts), lambda i, info: (0, 0, i))
                )
        results = pl.pallas_call(
            partial(merge_kernel, spots=spots, after=len(after)),
            grid_spec=pltpu.PrefetchScalarGridSpec(
                num_scalar_prefetch=1,
                grid=(cuts,),
                in_specs=in_specs + [ANY] * len(after),
                out_specs=out_specs,
            ),
            out_shape=outs,
            compiler_params=pltpu.CompilerParams(vmem_limit_bytes=VMEM_BYTES),
            cost_estimate=lasting(1.5),
            name="merge_grads",
        )(info, *ins, *after)
        bit = chains[names[0]][2]
        for index, name in enumerate([joined] if joined else names):
            bit = chains[names[index]][2]
            hold, give = results[2 * index : 2 * index + 2]
            chains[name] = (dp_hop(give, 2**bit), hold, bit + 1)
        if joined:
            for name in names:
                del chains[name]

    g = lax.dynamic_slice_in_dim(cotangent, core * share, share).astype(F32)
    sums = []
    last = LAYERS - 1
    for layer in reversed(range(LAYERS)):
        first = 3 * layer
        k = kept[layer]
        mod = (mods, (layer,))
        above = layer + 1
        f_name, c_name, a_name, s_name = [f"{kind}{layer}" for kind in "fcas"]
        n_name = f"n{above}"

        def grads_out(members):
            return {name: shape(width, members * narrow, dtype=BF) for name in ("send", "keep")}

        more, older = [output], []
        if layer < last:
            more = held(f"f{above}", f"c{above}", f"s{above}") + [chains[f"a{above}"][0]]
            older = [n_name, f"c{above}"]
        results = run(
            lambda info, work, w: hidden_back_kernel(
                info, work, w[:6], w[6:12], w[12]
            ),
            "feed_forward_back",
            info,
            dict(g=g, branch=k["branch3"], slope=k["slope"], entry=k["entry3"], x=k["x2"]),
            dict(mod=mod),
            weights_of(first + 2)
            + (weights_of(first + 3) if layer else weights_of(first + 2))
            + [k["active"]],
            {name: shape(width, 2 * units, dtype=BF) for name in ("send", "keep")}
            | dict(out=frame_high),
            dict(stats=stat_shape),
            dict(
                up=four,
                down=four,
                gb=lows,
                d_before=pltpu.VMEM((share, 4 * units), BF),
                acts=pltpu.VMEM((2, share, units), BF),
                act_sems=sems(2),
                before0=floats,
                de=floats,
                sems=sems(8),
                down_sems=sems(8),
            ),
            more,
            10.0,
        )
        send, keep, g, stats = results
        start(f_name, send, keep)
        if layer < last:
            advance([f"a{above}", f"s{above}"], held(f_name), n_name)
            advance([f"c{above}"], held(n_name))
        send, keep, g, stats = run(
            partial(cross_back_kernel, words=words),
            "cross_attention_back",
            info,
            dict(
                g=g,
                branch=k["branch2"],
                q=k["cq"],
                kv=k["ckv"],
                lse=k["lse2"],
                entry=k["entry2"],
                text=text_rows,
                mixed=k["mixed2"],
                x=k["x1"],
            ),
            dict(mod=mod, early=(stats, ())),
            weights_of(first + 1),
            grads_out(4) | dict(out=frame_high),
            dict(stats=stat_shape),
            dict(
                wq=whole,
                wo=whole,
                gb=lows,
                dq=lows,
                dkv=pltpu.VMEM(two_text.shape, BF),
                d_mixed=lows,
                de=floats,
                dkv_sum=pltpu.VMEM(two_text.shape, F32),
                sems=sems(8),
            ),
            held(f_name, *older),
            10.0,
        )
        start(c_name, send, keep)
        advance([f_name, *older], [g])
        gb1, dq, dkv_own, dkv_give, stats = run(
            self_back_kernel,
            "self_attention_back",
            info,
            dict(
                g=g, branch=k["branch1"], q=k["q"], kv_own=k["kv"], kv_sib=k["kv_sib"], lse=k["lse1"]
            ),
            dict(mod=mod, early=(stats, ())),
            weights_of(first),
            dict(gb=frame_low, dq=frame_low, dkv_own=two_low, dkv_give=two_low),
            dict(stats=stat_shape),
            dict(wo=whole, d_mixed=lows, sems=sems(4)),
            held(f_name, c_name, *older),
            13.0,
        )
        dkv_sib = tensor_hop(dkv_give, 1)
        advance([f_name, c_name, *older], [dq])
        send, keep = run(
            query_output_kernel,
            "query_output_grads",
            info,
            dict(entry=k["entry1"], gb=gb1, dq=dq, mixed=k["mixed1"]),
            {},
            [],
            grads_out(2),
            {},
            {},
            held(f_name, c_name),
            15.0,
        )
        start(a_name, send, keep)
        results = run(
            qkv_back_kernel,
            "self_qkv_back",
            info,
            dict(
                dq=dq, dkv_own=dkv_own, dkv_sib=dkv_sib, entry=k["entry1"], x=k["x"], g=g
            ),
            dict(mod=mod, early=(stats, ())),
            weights_of(first),
            grads_out(2)
            | dict(out=frame_high)
            | (dict(low=frame_low) if layer == 0 else {}),
            dict(stats=stat_shape),
            dict(
                wq=whole,
                wk=whole,
                wv=whole,
                de=floats,
                dkv=pltpu.VMEM(two_low.shape, BF),
                sems=sems(12),
            ),
            held(a_name, *([c_name] if layer == last else [])),
            6.0,
        )
        send, keep, g, stats = results[0], results[1], results[2], results[-1]
        start(s_name, send, keep)
        advance([f_name, c_name, *([a_name] if layer == 0 else [])], held(s_name))
        sums = [stats, tensor_hop(stats, 1)] + sums
    input_grad = join(results[3])
    vectors = plain(
        partial(collect_kernel, narrow=narrow, units=units, columns=columns),
        "collect_sums",
        info,
        [*sums, condition],
        [shape(16, mine.shape[2], dtype=BF)],
        [pltpu.VMEM(stat_shape.shape, F32), pltpu.VMEM((16, mine.shape[2]), F32)],
    )
    gathered = vectors[None]
    hop = size // 2
    while hop:
        both = jnp.stack([gathered, dp_hop(gathered, hop)], axis=1)
        gathered = both.reshape(-1, *vectors.shape)
        hop //= 2
    previous = held("f0", "c0", "a0")
    while any(2 ** chain[2] < size for chain in chains.values()):
        for names in (["s0"], [name for name in chains if name != "s0"]):
            if any(2 ** chains[name][2] < size for name in names):
                advance(names, previous)
                previous = held(*names)

    def parts_of(*names):
        return [part.reshape(1, unit, -1) for name in names for part in chains[name][:2]]

    up_grad, down_grad = plain(
        partial(finish_kernel, wide=True, spots=[[(layer, 0)] for layer in range(LAYERS)]),
        "finish_wide",
        None,
        parts_of(*[f"f{layer}" for layer in range(LAYERS)]),
        [shape(LAYERS, unit, units)] * 2,
        after=held("s0"),
    )
    straight, across = shape(LAYERS, unit, narrow), shape(LAYERS, narrow, unit)
    lasts = [[(1, 0), (1, 1)], [(1, 2), (1, 3)]]
    cq_grad, ck_grad, cv_grad, co_grad, q_grad, o_grad, k_grad, v_grad = plain(
        partial(finish_kernel, wide=False, spots=lasts + [[(0, 0), (0, 1)], [(0, 2)], [(0, 3)]]),
        "finish_narrow",
        None,
        parts_of("c1", "n1", "c0", "a0", "s0"),
        [straight, straight, straight, across, straight, across, straight, straight],
    )
    small = plain(
        spread_kernel,
        "spread_sums",
        info,
        [gathered],
        [shape(LAYERS, unit, columns), shape(LAYERS, columns)]
        + [shape(LAYERS, narrow)] * 4
        + [shape(LAYERS, units)]
        + [shape(LAYERS, unit)] * 3,
        [pltpu.VMEM((SLOTS * size, columns), F32), pltpu.VMEM((SLOTS * size, width), F32)],
    )
    mod_grad, mod_bias_grad, q_sum, v_sum, cq_sum, cv_sum, up_sum, o1, o2, o3 = small
    return (
        output,
        input_grad,
        q_grad,
        q_sum,
        k_grad,
        v_grad,
        v_sum,
        o_grad,
        o1,
        cq_grad,
        cq_sum,
        ck_grad,
        cv_grad,
        cv_sum,
        co_grad,
        o2,
        up_grad,
        up_sum,
        turn(down_grad),
        o3,
        mod_grad,
        mod_bias_grad,
    )


def solution(mesh):
    dp, tensor = "dp", "tensor"
    columns, vector = P(None, None, tensor), P(None, tensor)
    matrix, turned, spread = P(None, dp, tensor), P(None, tensor, dp), P(None, dp)
    placed = (
        P(dp, None),
        P(dp, None, None),
        P(dp),
        P(dp),
        P(dp, None),
        columns,
        vector,
        columns,
        columns,
        vector,
        P(None, tensor, None),
        P(),
        columns,
        vector,
        columns,
        columns,
        vector,
        P(None, tensor, None),
        P(),
        columns,
        vector,
        P(None, tensor, None),
        P(),
        columns,
        vector,
    )
    results = (
        P(dp, None),
        P(dp, None),
        matrix,
        vector,
        matrix,
        matrix,
        vector,
        turned,
        spread,
        matrix,
        vector,
        matrix,
        matrix,
        vector,
        turned,
        spread,
        matrix,
        vector,
        turned,
        spread,
        matrix,
        vector,
    )
    return jax.shard_map(
        shards, mesh=mesh, in_specs=placed, out_specs=results, check_vma=False
    )
```

```python
from functools import partial
import math

import jax
import jax.numpy as jnp
from jax import lax
from jax.experimental import pallas as pl
from jax.experimental.pallas import tpu as pltpu
from jax.sharding import PartitionSpec as P

HEAD_WIDTH = 64
UNIT = 256
LAYERS = 2
WINDOW = 1024
EPSILON = 1e-06
LANES = 128
CHUNK = 64
SLOTS = WINDOW // UNIT
FAR = -1e30
VMEM_BYTES = 62 * 1024 * 1024
BF = jnp.bfloat16
F32 = jnp.float32
ROOT = math.sqrt(2.0 / math.pi)
CUBIC = 0.044715


def dot_nn(left, right):
    return jnp.dot(left, right, preferred_element_type=F32)


def dot_nt(left, right):
    return lax.dot_general(left, right, (((1,), (1,)), ((), ())), preferred_element_type=F32)


def dot_tn(left, right):
    return lax.dot_general(left, right, (((0,), (0,)), ((), ())), preferred_element_type=F32)


SMALL = pl.BlockSpec(memory_space=pltpu.SMEM)
NEAR = pl.BlockSpec(memory_space=pltpu.VMEM)
ANY = pl.BlockSpec(memory_space=pl.ANY)


class Work:
    def __init__(self, ins, outs, scratch, in_sems, out_sems):
        self.ins, self.outs, self.scratch, self.out_sems = ins, outs, scratch, out_sems
        self.copies, self.waited, self.flushed = {}, set(), []
        for index, (name, (ref, buffer)) in enumerate(ins.items()):
            self.copies[name] = pltpu.make_async_copy(ref, buffer, in_sems.at[index])
            self.copies[name].start()

    def __getattr__(self, name):
        if name in self.__dict__["ins"]:
            return self.ins[name][1]
        if name in self.__dict__["outs"]:
            return self.outs[name][1]
        return self.__dict__["scratch"][name]

    def has(self, name):
        return name in self.outs

    def takes(self, name):
        return name in self.ins

    def send(self, name, source, *at):
        ref = self.outs[name][0]
        copy = pltpu.make_async_copy(
            source, ref.at[at] if at else ref, self.out_sems.at[len(self.flushed)]
        )
        copy.start()
        self.flushed.append(copy)

    def need(self, *names):
        for name in names:
            if name not in self.waited:
                self.waited.add(name)
                self.copies[name].wait()

    def flush(self, name, *at):
        ref, buffer = self.outs[name]
        if at:
            ref, buffer = ref.at[at], buffer.at[at]
        copy = pltpu.make_async_copy(buffer, ref, self.out_sems.at[len(self.flushed)])
        copy.start()
        self.flushed.append(copy)

    def finish(self):
        self.need(*self.ins)
        for copy in self.flushed:
            copy.wait()


def run(body, name, info, ins, small, weights, outs, small_outs, scratch, after=(), cost=1.0):
    in_names, out_names, names = list(ins), list(outs), list(scratch)
    small_names, small_out_names = list(small), list(small_outs)
    counts = [1, len(in_names), len(small), len(weights), len(after), len(outs), len(small_outs)]

    def kernel(*refs):
        refs = list(refs)
        parts = []
        for count in counts:
            parts.append(refs[:count])
            refs = refs[count:]
        (info_ref,), in_refs, small_refs, weight_refs, _, out_refs, small_out_refs = parts
        in_bufs, refs = refs[: len(in_names)], refs[len(in_names) :]
        out_bufs, refs = refs[: len(out_names)], refs[len(out_names) :]
        rest, (in_sems, out_sems) = refs[:-2], refs[-2:]
        extra = {}
        rest = list(rest)
        for key in names:
            many = isinstance(scratch[key], list)
            size = len(scratch[key]) if many else 1
            extra[key] = rest[:size] if many else rest[0]
            rest = rest[size:]
        for key, ref in zip(small_names, small_refs):
            index = small[key][1]
            extra[key] = ref.at[index] if index else ref
        extra.update(zip(small_out_names, small_out_refs))
        work = Work(
            dict(zip(in_names, zip(in_refs, in_bufs))),
            dict(zip(out_names, zip(out_refs, out_bufs))),
            extra,
            in_sems,
            out_sems,
        )
        body(info_ref, work, weight_refs)
        work.finish()

    buffer = lambda a: pltpu.VMEM(a.shape, a.dtype)
    flat = []
    for value in scratch.values():
        flat += value if isinstance(value, list) else [value]
    results = pl.pallas_call(
        kernel,
        out_shape=[outs[n] for n in out_names] + [small_outs[n] for n in small_out_names],
        in_specs=[SMALL]
        + [ANY] * len(ins)
        + [NEAR] * len(small)
        + [ANY] * (len(weights) + len(after)),
        out_specs=[ANY] * len(outs) + [NEAR] * len(small_outs),
        scratch_shapes=[buffer(ins[n]) for n in in_names]
        + [buffer(outs[n]) for n in out_names]
        + flat
        + [pltpu.SemaphoreType.DMA((max(len(ins), 1),)), pltpu.SemaphoreType.DMA((32,))],
        compiler_params=pltpu.CompilerParams(vmem_limit_bytes=VMEM_BYTES),
        cost_estimate=lasting(cost),
        name=name,
    )(info, *ins.values(), *[array for array, _ in small.values()], *weights, *after)
    return results


def plain(body, name, info, ins, outs, scratch=(), after=()):
    first = len(ins) + (0 if info is None else 1)
    results = pl.pallas_call(
        lambda *refs: body(*refs[:first], *refs[first + len(after) :]),
        out_shape=outs,
        in_specs=([] if info is None else [SMALL]) + [NEAR] * len(ins) + [ANY] * len(after),
        out_specs=[NEAR] * len(outs),
        scratch_shapes=list(scratch),
        compiler_params=pltpu.CompilerParams(vmem_limit_bytes=VMEM_BYTES),
        cost_estimate=lasting(1.0),
        name=name,
    )(*([] if info is None else [info]), *ins, *after)
    return results if len(outs) > 1 else results[0]


def lasting(units):
    return pl.CostEstimate(flops=int(units * 0.4e9), bytes_accessed=1000, transcendentals=0)


def shape(*dims, dtype=F32):
    return jax.ShapeDtypeStruct(dims, dtype)


def start_rows(refs, place, plan, sems):
    own, sib, xa, ya, xb, yb = refs
    half = own.shape[0] // 2
    for rank in range(4):
        for parity in range(2):

            @pl.when(place == rank * 2 + parity)
            def _(rank=rank, parity=parity):
                for index, (shard, row, rows, dst) in enumerate(plan):
                    step = shard ^ rank
                    if step < 2:
                        src = (own, sib)[step].at[pl.ds(row, rows)]
                    else:
                        first, second = ((xa, ya), (xb, yb))[step - 2]
                        part = row // half
                        src = (first if part == parity else second).at[pl.ds(row - part * half, rows)]
                    pltpu.make_async_copy(src, dst, sems.at[index]).start()


def wait_rows(refs, plan, sems, which):
    for index in which:
        _, row, rows, dst = plan[index]
        pltpu.make_async_copy(refs[0].at[pl.ds(0, rows)], dst, sems.at[index]).wait()


def plan_of(buffers, first, rows):
    return [
        (shard, (first + which) * rows, rows, dst.at[pl.ds(shard * rows, rows)])
        for which, dst in enumerate(buffers)
        for shard in range(4)
    ]


def norm_rows(values):
    mean = jnp.mean(values, axis=-1, keepdims=True)
    center = values - mean
    factor = lax.rsqrt(jnp.mean(center * center, axis=-1, keepdims=True) + EPSILON)
    return center * factor, factor


def piece(mod, slot, index):
    width = mod.shape[1] // 9
    return mod[pl.ds(slot, 1), index * width : (index + 1) * width]


def entry_rows(x, mod, info, index, out):
    for block in range(x.shape[0] // UNIT):
        slot = info[1 + block]
        shift = piece(mod, slot, index)
        scale = 1.0 + piece(mod, slot, index + 1)

        def step(turn, carry):
            rows = pl.ds(pl.multiple_of(block * UNIT + turn * CHUNK, CHUNK), CHUNK)
            normed, _ = norm_rows(x[rows, :])
            out[rows, :] = (normed * scale + shift).astype(BF)
            return carry

        lax.fori_loop(0, UNIT // CHUNK, step, 0, unroll=True)


def residual_rows(x, mod, info, index, branch, branch_out, out, low=None):
    for block in range(x.shape[0] // UNIT):
        gate = piece(mod, info[1 + block], index)

        def step(turn, carry):
            rows = pl.ds(pl.multiple_of(block * UNIT + turn * CHUNK, CHUNK), CHUNK)
            values = branch[rows, :]
            branch_out[rows, :] = values.astype(BF)
            result = x[rows, :] + gate * values
            out[rows, :] = result
            if low is not None:
                low[rows, :] = result.astype(BF)
            return carry

        lax.fori_loop(0, UNIT // CHUNK, step, 0, unroll=True)


def fold(values):
    return jnp.sum(values.reshape(values.shape[0] // 8, 8, values.shape[1]), axis=0)


def total(values):
    return jnp.sum(values, axis=0, keepdims=True)


def gate_back(g, mod, info, index, branch, gb, stats):
    width = g.shape[1]
    sums = jnp.zeros((8, width), F32)
    for block in range(g.shape[0] // UNIT):
        slot = info[1 + block]
        gate = piece(mod, slot, index)

        def step(turn, carry):
            rows = pl.ds(pl.multiple_of(block * UNIT + turn * CHUNK, CHUNK), CHUNK)
            grad = g[rows, :]
            low = (gate * grad).astype(BF)
            gb[rows, :] = low
            return (
                carry[0] + fold(low.astype(F32)),
                carry[1] + fold(grad * branch[rows, :].astype(F32)),
            )

        sums, rows_sum = lax.fori_loop(
            0, UNIT // CHUNK, step, (sums, jnp.zeros((8, width), F32)), unroll=True
        )
        stats[pl.ds(8 + slot, 1), :] += total(rows_sum)
    stats[12:13, :] = total(sums)


def norm_back_rows(x, g, de, mod, info, index, out, stats, low=None):
    width = x.shape[1]
    for block in range(x.shape[0] // UNIT):
        slot = info[1 + block]
        scale = 1.0 + piece(mod, slot, index + 1)

        def step(turn, carry):
            rows = pl.ds(pl.multiple_of(block * UNIT + turn * CHUNK, CHUNK), CHUNK)
            normed, factor = norm_rows(x[rows, :])
            grad = de[rows, :]
            inner = grad * normed
            dn = grad * scale
            mean = jnp.mean(dn, axis=-1, keepdims=True)
            along = jnp.mean(dn * normed, axis=-1, keepdims=True)
            result = g[rows, :] + factor * (dn - mean - normed * along)
            out[rows, :] = result
            if low is not None:
                low[rows, :] = result.astype(BF)
            return (carry[0] + fold(grad), carry[1] + fold(inner))

        zero = jnp.zeros((8, width), F32)
        shift_sum, scale_sum = lax.fori_loop(0, UNIT // CHUNK, step, (zero, zero), unroll=True)
        stats[pl.ds(slot, 1), :] += total(shift_sum)
        stats[pl.ds(4 + slot, 1), :] += total(scale_sum)


def lane_ids(rows):
    return lax.broadcasted_iota(jnp.int32, (rows, LANES), 1)


def head_half(values, half):
    ids = lane_ids(values.shape[0])
    keep = ids < HEAD_WIDTH if half == 0 else ids >= HEAD_WIDTH
    return jnp.where(keep, values.astype(F32), 0.0)


def turned_halves(keys):
    turned = keys.T
    low = lax.broadcasted_iota(jnp.int32, turned.shape, 0) < HEAD_WIDTH
    zero = jnp.zeros(turned.shape, turned.dtype)
    return jnp.concatenate([jnp.where(low, turned, zero), jnp.where(low, zero, turned)], axis=1)


def query_marks(slot):
    return jnp.where(lane_ids(UNIT) == slot, 1.0, 0.0).astype(BF)


def key_marks(slots):
    ids = lane_ids(UNIT)
    parts = [jnp.where((ids < SLOTS) & (ids != slot), FAR, 0.0).astype(BF) for slot in slots]
    return jnp.concatenate(parts, axis=0)


def pair_lanes(pair):
    return pl.ds(pl.multiple_of(pair * LANES, LANES), LANES)


def kv_kernel(info, work, weights):
    rows = weights[0].shape[0] // 4
    plan = plan_of((work.w.at[0], work.w.at[1]), 1, rows)
    start_rows(weights, info[0], plan, work.sems)
    if work.has("branch"):
        work.need("part", "other", "below")
        bias = work.bias[...].astype(F32)
        for row in range(0, work.sum.shape[0], CHUNK):
            span = pl.ds(row, CHUNK)
            work.sum[span, :] = (
                work.part[span, :].astype(F32) + work.other[span, :].astype(F32) + bias
            )
        residual_rows(work.below, work.mod_below, info, 8, work.sum, work.branch, work.x)
        work.flush("branch")
        work.flush("x")
    else:
        work.need("x")
    entry_rows(work.x, work.mod, info, 0, work.entry)
    work.flush("entry")
    entry = work.entry[...]
    wait_rows(weights, plan, work.sems, range(4))
    work.kv[0] = dot_nt(entry, work.w[0]).astype(BF)
    work.flush("kv", 0)
    wait_rows(weights, plan, work.sems, range(4, 8))
    work.kv[1] = (dot_nt(entry, work.w[1]) + work.biases[2:3, :]).astype(BF)
    work.flush("kv", 1)


def q_kernel(info, work, weights):
    rows = weights[0].shape[0] // 4
    plan = plan_of((work.w,), 0, rows)
    start_rows(weights, info[0], plan, work.sems)
    work.need("entry")
    wait_rows(weights, plan, work.sems, range(4))
    work.q[...] = (dot_nt(work.entry[...], work.w[...]) + work.biases[0:1, :]).astype(BF)
    work.flush("q")


def soft_pair(work, q_pair, keys, values, marks, logs, pair, span, words=None):
    ids = lane_ids(UNIT)
    results = []
    kept = logs[span, :]
    for half in range(2):
        left = (head_half(q_pair, half) * HEAD_WIDTH**-0.5).astype(BF)
        if marks is not None:
            left = jnp.concatenate([left, marks], axis=1)
        scores = dot_nt(left, keys)
        if words is not None:
            scores = jnp.where(ids < words, scores, FAR)
        peak = jnp.max(scores, axis=-1, keepdims=True)
        both = dot_nn(jnp.exp(scores - peak).astype(BF), values)
        sums = both[:, LANES:]
        results.append(both[:, :LANES] / sums)
        kept = jnp.where(ids == 2 * pair + half, peak + jnp.log(sums), kept)
    logs[span, :] = kept
    return jnp.where(ids < HEAD_WIDTH, results[0], results[1]).astype(BF)


def self_kernel(info, work, weights):
    rows = weights[0].shape[0] // 4
    sems = work.sems
    plan = [(s, 3 * rows, rows, work.wo.at[pl.ds(s * rows, rows)]) for s in range(4)]
    start_rows(weights, info[0], plan, sems)
    share = work.x.shape[0]
    blocks = share // UNIT
    marks = key_marks([info[1 + b] for b in range(2 * blocks)])
    ones = jnp.ones((2 * share, LANES), BF)
    logs, mixed = work.logs, work.mixed
    logs[...] = jnp.zeros(logs.shape, F32)
    work.need("q", "kv_own", "kv_sib")

    def both(which, lanes):
        return jnp.concatenate([work.kv_own[which, :, lanes], work.kv_sib[which, :, lanes]], axis=0)

    def step(pair, carry):
        lanes = pair_lanes(pair)
        keys = jnp.concatenate([both(0, lanes), marks], axis=1)
        values = jnp.concatenate([both(1, lanes), ones], axis=1)
        for block in range(blocks):
            span = pl.ds(block * UNIT, UNIT)
            mixed[span, lanes] = soft_pair(
                work,
                work.q[span, lanes],
                keys,
                values,
                query_marks(info[1 + block]),
                logs,
                pair,
                span,
            )
        return carry

    lax.fori_loop(0, mixed.shape[1] // LANES, step, 0)
    work.flush("mixed")
    work.lse[...] = logs[...].T[: work.lse.shape[0], :]
    work.flush("lse")
    wait_rows(weights, plan, sems, range(4))
    work.sum[...] = dot_nn(mixed[...], work.wo[...]) + work.bias[...].astype(F32)
    work.need("x")
    residual_rows(work.x, work.mod, info, 2, work.sum, work.branch, work.out)
    work.flush("branch")
    work.flush("out")


def cross_kernel(info, work, weights, words):
    rows = weights[0].shape[0] // 4
    sems = work.sems
    order = (1, 2, 0, 3)
    plan = [
        (shard, order[i // 4] * rows, count, dst)
        for i, (shard, _, count, dst) in enumerate(
            plan_of((work.wk, work.wv, work.wq, work.wo), 0, rows)
        )
    ]
    start_rows(weights, info[0], plan, sems)
    work.need("x")
    entry_rows(work.x, work.mod, info, 3, work.entry)
    work.flush("entry")
    work.need("text")
    wait_rows(weights, plan, sems, range(0, 4))
    work.kv[0] = dot_nt(work.text[...], work.wk[...]).astype(BF)
    wait_rows(weights, plan, sems, range(4, 8))
    work.kv[1] = (dot_nt(work.text[...], work.wv[...]) + work.biases[5:6, :]).astype(BF)
    work.flush("kv")
    wait_rows(weights, plan, sems, range(8, 12))
    work.q[...] = (dot_nt(work.entry[...], work.wq[...]) + work.biases[3:4, :]).astype(BF)
    work.flush("q")
    ones = jnp.ones((LANES, LANES), BF)
    logs, mixed = work.logs, work.mixed
    logs[...] = jnp.zeros(logs.shape, F32)

    def step(pair, carry):
        lanes = pair_lanes(pair)
        for block in range(mixed.shape[0] // UNIT):
            span = pl.ds(block * UNIT, UNIT)
            own = pl.ds(pl.multiple_of(info[1 + block] * LANES, LANES), LANES)
            mixed[span, lanes] = soft_pair(
                work,
                work.q[span, lanes],
                work.kv[0, own, lanes],
                jnp.concatenate([work.kv[1, own, lanes], ones], axis=1),
                None,
                logs,
                pair,
                span,
                words,
            )
        return carry

    lax.fori_loop(0, mixed.shape[1] // LANES, step, 0, unroll=2)
    work.flush("mixed")
    work.lse[...] = logs[...].T[: work.lse.shape[0], :]
    work.flush("lse")
    wait_rows(weights, plan, sems, range(12, 16))
    work.sum[...] = dot_nn(mixed[...], work.wo[...]) + work.bias[...].astype(F32)
    residual_rows(work.x, work.mod, info, 5, work.sum, work.branch, work.out)
    work.flush("branch")
    work.flush("out")


def hidden_plan(refs, buffer):
    rows = buffer.shape[1]
    half = rows // 2
    return [
        (shard, row, half, buffer.at[shard, pl.ds(row, half)])
        for shard in range(4)
        for row in range(0, rows, half)
    ]


def start_chip(info, refs, layer, buffer, sems):
    copies = [
        pltpu.make_async_copy(ref.at[layer], buffer.at[(info[5] + i) % 2], sems.at[i])
        for i, ref in enumerate(refs)
    ]
    for copy in copies:
        copy.start()
    return copies


def bend_rows(before, bias, active, slope, lanes):
    for row in range(0, before.shape[0], CHUNK):
        span = pl.ds(row, CHUNK)
        values = before[span, :] + bias
        square = values * values
        half = 1.0 / (1.0 + jnp.exp(values * (-2.0 * ROOT - (2.0 * ROOT * CUBIC) * square)))
        act = values * half
        active[span, lanes] = act.astype(BF)
        slope[span, lanes] = (
            half + act * (1.0 - half) * (2.0 * ROOT + (6.0 * ROOT * CUBIC) * square)
        ).astype(BF)


def columns_of(shard, width):
    return pl.ds(pl.multiple_of(shard * width, width), width)


def start_hidden(info, work, weights, layer):
    if len(weights) == 4:
        ups = start_chip(info, weights[:2], layer, work.up, work.sems)
        downs = start_chip(info, weights[2:], layer, work.down, work.down_sems)
        return [lambda some=some: [copy.wait() for copy in some] for some in (ups, downs)]
    waits = []
    for refs, buffer, sems in (
        (weights[:6], work.up, work.sems),
        (weights[6:12], work.down, work.down_sems),
    ):
        refs = [ref.at[layer] for ref in refs[:2]] + list(refs[2:])
        plan = hidden_plan(refs, buffer)
        start_rows(refs, info[0], plan, sems)
        waits.append(
            lambda refs=refs, plan=plan, sems=sems: wait_rows(refs, plan, sems, range(len(plan)))
        )
    return waits


def hidden_kernel(info, work, weights, layer):
    waits = start_hidden(info, work, weights, layer)
    width = work.x.shape[1]
    shards = work.up.shape[0]
    first = info[6] * 2 if shards == 2 else 0
    work.need("x")
    entry_rows(work.x, work.mod, info, 6, work.entry)
    work.flush("entry")
    for wait in waits:
        wait()
    start = 0.0 if shards == 2 else work.bias[...].astype(F32)
    work.sum[...] = jnp.zeros(work.sum.shape, F32) + start

    def step(shard, carry):
        lanes = columns_of(shard, width)
        bias = work.up_bias[:, columns_of(first + shard, width)]
        work.before[...] = dot_nn(work.entry[...], work.up[shard])
        bend_rows(work.before, bias, work.active, work.slope, lanes)
        work.sum[...] += dot_nn(work.active[:, lanes], work.down[shard])
        return carry

    lax.fori_loop(0, shards, step, 0)
    work.flush("active")
    work.flush("slope")
    if shards == 2:
        work.part[...] = work.sum[...].astype(BF)
        work.flush("part")
        return
    low = work.low if work.has("low") else None
    residual_rows(work.x, work.mod, info, 8, work.sum, work.branch, work.out, low)
    work.flush("branch")
    work.flush("out")
    if low is not None:
        work.flush("low")


def hidden_back_kernel(info, work, weights, layer):
    waits = start_hidden(info, work, weights, layer)
    width = work.g.shape[1]
    shards = work.up.shape[0]
    if shards == 4:
        actives = [
            pltpu.make_async_copy(
                weights[12].at[:, columns_of(rank, width)], work.acts.at[i], work.act_sems.at[i]
            )
            for i, rank in enumerate((info[7], info[5]))
        ]
        for copy in actives:
            copy.start()
    work.stats[...] = jnp.zeros(work.stats.shape, F32)
    stats = work.stats.at[pl.ds(48, 24)]
    work.need("g", "branch")
    gate_back(work.g, work.mod, info, 8, work.branch, work.gb, stats)
    work.need("slope")
    for wait in waits:
        wait()
    work.de[...] = jnp.zeros(work.de.shape, F32)
    first = info[6] * 2 if shards == 2 else 0

    def step(shard, carry):
        lanes = columns_of(shard, width)
        work.before[...] = dot_nt(work.gb[...], work.down[shard])
        sums = jnp.zeros((8, width), F32)
        for row in range(0, work.g.shape[0], CHUNK):
            span = pl.ds(row, CHUNK)
            low = (work.before[span, :] * work.slope[span, lanes].astype(F32)).astype(BF)
            work.d_before[span, lanes] = low
            sums += fold(low.astype(F32))
        stats[pl.ds(13 + first + shard, 1), :] = total(sums)
        work.de[...] += dot_nt(work.d_before[:, lanes], work.up[shard])
        return carry

    lax.fori_loop(0, shards, step, 0)
    if shards == 2:
        work.part[...] = work.de[...].astype(BF)
        work.flush("part")
        work.flush("gb")
        work.flush("d_before")
        return
    work.need("entry")
    left, right = work.entry[...].T, work.gb[...].T
    for name, index, rank in (("send", 0, info[7]), ("keep", 1, info[5])):
        out = work.outs[name][1]
        out[:, :width] = dot_nn(left, work.d_before[:, columns_of(rank, width)]).astype(BF)
        actives[index].wait()
        out[:, width:] = dot_nn(right, work.acts[index]).astype(BF)
        work.flush(name)
    work.need("x")
    norm_back_rows(work.x, work.g, work.de, work.mod, info, 6, work.out, stats)
    work.flush("out")


def hidden_grads_kernel(info, work, weights):
    width = work.entry.shape[1]
    work.need("entry", "d_before", "gb", "active")
    left, right = work.entry[...].T, work.gb[...].T
    for name, shift in (("send", 1), ("keep", 0)):
        out = work.outs[name][1]
        lanes = columns_of((info[5] + shift) % 2, width)
        out[:, :width] = dot_nn(left, work.d_before[:, lanes]).astype(BF)
        out[:, width:] = dot_nn(right, work.active[:, lanes]).astype(BF)
        work.flush(name)


def pair_grads(info, work, members):
    rows = members[0][0].shape[0]
    low = lane_ids(rows) < HEAD_WIDTH
    step = 3 * LANES
    for at in range(len(members) // 2):
        products = [dot_nn(left, right) for left, right in members[2 * at : 2 * at + 2]]
        (a0, a1, a2), (b0, b1, b2) = [
            [p[:, i * LANES : (i + 1) * LANES] for i in range(3)] for p in products
        ]
        even = (a0, b0, jnp.where(low, a1, pltpu.roll(b1, HEAD_WIDTH, 1)))
        a1, b1 = pltpu.roll(a1, HEAD_WIDTH, 1), pltpu.roll(b1, HEAD_WIDTH, 1)
        a2r, b2r = pltpu.roll(a2, HEAD_WIDTH, 1), pltpu.roll(b2, HEAD_WIDTH, 1)
        odd = (jnp.where(low, a1, a2r), jnp.where(low, b1, b2r), jnp.where(low, a2r, b2))
        first = info[5] % 2 == 0
        for i, (mine, other) in enumerate(zip(even, odd)):
            lanes = pl.ds(at * step + i * LANES, LANES)
            work.outs["keep"][1][:, lanes] = jnp.where(first, mine, other).astype(BF)
            work.outs["send"][1][:, lanes] = jnp.where(first, other, mine).astype(BF)
    work.flush("send")
    work.flush("keep")


def chip_lanes(info, width):
    return pl.ds(pl.multiple_of(info[6] * (width // 2), width // 2), width // 2)


def query_output_kernel(info, work, weights):
    work.need("entry", "gb", "dq", "mixed")
    lanes = chip_lanes(info, work.dq.shape[1])
    pair_grads(
        info,
        work,
        [
            (work.entry[...].T, work.dq[:, lanes]),
            (work.gb[...].T, work.mixed[:, lanes]),
        ],
    )


def cross_back_kernel(info, work, weights, words):
    rows = weights[0].shape[0] // 4
    sems = work.sems
    plan = [
        (shard, (3 * rows, 0)[i // 4], count, dst)
        for i, (shard, _, count, dst) in enumerate(plan_of((work.wo, work.wq), 0, rows))
    ]
    start_rows(weights, info[0], plan, sems)
    work.stats[...] = work.early[...]
    stats = work.stats.at[pl.ds(24, 24)]
    g = work.g
    work.need("g")
    if work.takes("part"):
        work.need("part", "other", "above")
        for row in range(0, g.shape[0], CHUNK):
            span = pl.ds(row, CHUNK)
            work.de[span, :] = work.part[span, :].astype(F32) + work.other[span, :].astype(F32)
        g = work.g_mid
        norm_back_rows(
            work.above, work.g, work.de, work.mod, info, 6, g, work.stats.at[pl.ds(48, 24)]
        )
    work.need("branch")
    gate_back(g, work.mod, info, 5, work.branch, work.gb, stats)
    wait_rows(weights, plan, sems, range(0, 4))
    work.d_mixed[...] = dot_nt(work.gb[...], work.wo[...]).astype(BF)
    work.dkv_sum[...] = jnp.zeros(work.dkv_sum.shape, F32)
    real = lax.broadcasted_iota(jnp.int32, (LANES, UNIT), 0) < words
    work.need("q", "kv", "lse")

    def step(pair, carry):
        lanes = pair_lanes(pair)
        for block in range(work.q.shape[0] // UNIT):
            span = pl.ds(block * UNIT, UNIT)
            own = pl.ds(pl.multiple_of(info[1 + block] * LANES, LANES), LANES)
            q_pair = work.q[span, lanes]
            d_pair = work.d_mixed[span, lanes]
            keys = work.kv[0, own, lanes]
            values = work.kv[1, own, lanes]
            lefts, grads, probs_low, scores_low = [], [], [], []
            for half in range(2):
                left = (head_half(q_pair, half) * HEAD_WIDTH**-0.5).astype(BF)
                grad = head_half(d_pair, half).astype(BF)
                logs = work.lse[pl.ds(2 * pair + half, 1), span]
                probs = jnp.where(real, jnp.exp(dot_nt(keys, left) - logs), 0.0)
                d_probs = dot_nt(values, grad)
                inner = jnp.sum(probs * d_probs, axis=0, keepdims=True)
                lefts.append(left)
                grads.append(grad)
                probs_low.append(probs.astype(BF))
                scores_low.append((probs * (d_probs - inner)).astype(BF))
            wide_scores = jnp.concatenate(scores_low, axis=1)
            grad_v = dot_nn(jnp.concatenate(probs_low, axis=1), jnp.concatenate(grads, axis=0))
            grad_k = dot_nn(wide_scores, jnp.concatenate(lefts, axis=0))
            grad_q = dot_nn(turned_halves(keys), jnp.concatenate(scores_low, axis=0))
            work.dq[span, lanes] = (grad_q.T * HEAD_WIDTH**-0.5).astype(BF)
            work.dkv_sum[0, own, lanes] += grad_k
            work.dkv_sum[1, own, lanes] += grad_v
        return carry

    lax.fori_loop(0, work.q.shape[1] // LANES, step, 0, unroll=2)
    work.dkv[...] = work.dkv_sum[...].astype(BF)
    work.need("entry", "text", "mixed")
    lanes = chip_lanes(info, work.dq.shape[1])
    text = work.text[...].T
    pair_grads(
        info,
        work,
        [
            (work.entry[...].T, work.dq[:, lanes]),
            (text, work.dkv[0, :, lanes]),
            (text, work.dkv[1, :, lanes]),
            (work.gb[...].T, work.mixed[:, lanes]),
        ],
    )
    stats[13:14, :] = total(fold(work.dq[...].astype(F32)))
    stats[14:15, :] = total(fold(work.dkv[1].astype(F32)))
    wait_rows(weights, plan, sems, range(4, 8))
    work.de[...] = dot_nn(work.dq[...], work.wq[...])
    work.need("x")
    norm_back_rows(work.x, g, work.de, work.mod, info, 3, work.out, stats)
    work.flush("out")


def self_back_kernel(info, work, weights):
    rows = weights[0].shape[0] // 4
    sems = work.sems
    plan = [(s, 3 * rows, rows, work.wo.at[pl.ds(s * rows, rows)]) for s in range(4)]
    start_rows(weights, info[0], plan, sems)
    work.stats[...] = work.early[...]
    stats = work.stats.at[pl.ds(0, 24)]
    work.need("g", "branch")
    gate_back(work.g, work.mod, info, 2, work.branch, work.gb, stats)
    work.flush("gb")
    share = work.g.shape[0]
    blocks = share // UNIT
    marks = key_marks([info[1 + b] for b in range(2 * blocks)])
    wait_rows(weights, plan, sems, range(4))
    work.d_mixed[...] = dot_nt(work.gb[...], work.wo[...]).astype(BF)
    work.need("q", "kv_own", "kv_sib", "lse")

    def both(which, lanes):
        return jnp.concatenate([work.kv_own[which, :, lanes], work.kv_sib[which, :, lanes]], axis=0)

    def step(pair, carry):
        lanes = pair_lanes(pair)
        keys = both(0, lanes)
        values = both(1, lanes)
        marked = jnp.concatenate([keys, marks], axis=1)
        turned = turned_halves(keys)
        lefts, grads, probs_low, scores_low = [], [], [], []
        for block in range(blocks):
            span = pl.ds(block * UNIT, UNIT)
            q_pair = work.q[span, lanes]
            d_pair = work.d_mixed[span, lanes]
            ends = query_marks(info[1 + block])
            for half in range(2):
                left = (head_half(q_pair, half) * HEAD_WIDTH**-0.5).astype(BF)
                grad = head_half(d_pair, half).astype(BF)
                logs = work.lse[pl.ds(2 * pair + half, 1), span]
                probs = jnp.exp(dot_nt(marked, jnp.concatenate([left, ends], axis=1)) - logs)
                d_probs = dot_nt(values, grad)
                inner = jnp.sum(probs * d_probs, axis=0, keepdims=True)
                lefts.append(left)
                grads.append(grad)
                probs_low.append(probs.astype(BF))
                scores_low.append((probs * (d_probs - inner)).astype(BF))
            grad_q = dot_nn(turned, jnp.concatenate(scores_low[-2:], axis=0))
            work.dq[span, lanes] = (grad_q.T * HEAD_WIDTH**-0.5).astype(BF)
        grad_v = dot_nn(jnp.concatenate(probs_low, axis=1), jnp.concatenate(grads, axis=0))
        grad_k = dot_nn(jnp.concatenate(scores_low, axis=1), jnp.concatenate(lefts, axis=0))
        for which, grad in ((0, grad_k.astype(BF)), (1, grad_v.astype(BF))):
            work.dkv_own[which, :, lanes] = grad[:share]
            work.dkv_give[which, :, lanes] = grad[share:]
        return carry

    lax.fori_loop(0, work.q.shape[1] // LANES, step, 0)
    work.flush("dkv_give")
    work.flush("dkv_own")
    work.flush("dq")


def sum_keys_values(info, work, dkv):
    work.need("dkv_own", "dkv_sib")
    for which in range(2):
        dkv[which] = (
            work.dkv_own[which].astype(F32) + work.dkv_sib[which].astype(F32)
        ).astype(BF)
    work.need("entry")
    lanes = chip_lanes(info, dkv.shape[2])
    entry = work.entry[...].T
    pair_grads(info, work, [(entry, dkv[0, :, lanes]), (entry, dkv[1, :, lanes])])


def kv_grads_kernel(info, work, weights):
    sum_keys_values(info, work, work.dkv)
    work.flush("dkv")


def qkv_back_kernel(info, work, weights):
    rows = weights[0].shape[0] // 4
    sems = work.sems
    plan = plan_of((work.wq, work.wk, work.wv), 0, rows)
    start_rows(weights, info[0], plan, sems)
    work.stats[...] = work.early[...]
    stats = work.stats.at[pl.ds(0, 24)]
    if work.has("send"):
        sum_keys_values(info, work, work.dkv)
    else:
        work.need("dkv")
    work.need("dq")
    stats[13:14, :] = total(fold(work.dq[...].astype(F32)))
    stats[14:15, :] = total(fold(work.dkv[1].astype(F32)))
    wait_rows(weights, plan, sems, range(0, 12))
    work.de[...] = (
        dot_nn(work.dq[...], work.wq[...])
        + dot_nn(work.dkv[0], work.wk[...])
        + dot_nn(work.dkv[1], work.wv[...])
    )
    work.need("x", "g")
    low = work.low if work.has("low") else None
    norm_back_rows(work.x, work.g, work.de, work.mod, info, 0, work.out, stats, low)
    work.flush("out")
    if low is not None:
        work.flush("low")


def merge_kernel(info, *refs, spots, after):
    chains = len(spots)
    ins, outs = refs[: 4 * chains], refs[4 * chains + after :]
    for chain, (result, column) in enumerate(spots):
        for side in range(2):
            received, kept = ins[4 * chain + 2 * side], ins[4 * chain + 2 * side + 1]
            out = outs[2 * result + side]
            lanes = pl.ds(column, received.shape[2])
            out[:, :, lanes] = (received[...].astype(F32) + kept[...].astype(F32)).astype(BF)


def gate(arrays, after):
    count = len(arrays)
    return pl.pallas_call(
        lambda *refs: None,
        out_shape=[shape(*a.shape, dtype=a.dtype) for a in arrays],
        in_specs=[ANY] * (count + len(after)),
        out_specs=[ANY] * count,
        input_output_aliases={i: i for i in range(count)},
        cost_estimate=lasting(0.5),
        name="gate",
    )(*arrays, *after)


def pack_kernel(info, *refs, groups, whole, after):
    count = sum(len(members) for _, members in groups)
    sources, rest = refs[:count], refs[count + after :]
    (in_sems, out_sems), rest = rest[-2:], rest[:-2]
    count = len(groups) + sum(whole)
    outs, held = list(rest[:count]), rest[count:]
    owns = [outs.pop(0) if one else None for one in whole]
    spots = []
    at = 0
    for index, (layer, members) in enumerate(groups):
        rows = held[index].shape[0]
        piece_rows = rows // 4
        for quarter in range(4):
            row = quarter * piece_rows
            source = sources[at + quarter * len(members) // 4]
            src = source.at[layer, pl.ds(row % source.shape[1], piece_rows)]
            spots.append((index, quarter, held[index].at[pl.ds(row, piece_rows)], src))
        at += len(members)

    def arriving(place):
        _, _, spot, src = spots[place]
        return pltpu.make_async_copy(src, spot, in_sems.at[place])

    def leaving(index, which):
        if which == 2:
            return pltpu.make_async_copy(held[index], owns[index], out_sems.at[2 * index])
        rows = outs[index].shape[0]
        src = held[index].at[pl.ds(which * rows, rows)]
        return pltpu.make_async_copy(src, outs[index], out_sems.at[2 * index + 1])

    def by_parity(act):
        for parity in range(2):

            @pl.when(info[0] % 2 == parity)
            def _(parity=parity):
                act(parity)

    for place in range(len(spots)):
        arriving(place).start()
    for index in range(len(groups)):
        for quarter in range(4):
            arriving(4 * index + quarter).wait()
        by_parity(lambda parity: leaving(index, parity).start())
        if whole[index]:
            leaving(index, 2).start()
    for index in range(len(groups)):
        by_parity(lambda parity: leaving(index, parity).wait())
        if whole[index]:
            leaving(index, 2).wait()


def mod_kernel(condition, mod, mod_bias, q, v, cq, cv, up, out):
    narrow, units, columns = q.shape[1], up.shape[1], mod.shape[1]
    out[...] = jnp.zeros(out.shape, F32)
    for layer in range(LAYERS):
        row = pl.ds(layer, 1)
        out[layer, 0:SLOTS, 0:columns] = dot_nt(condition[...], mod[layer]) + mod_bias[
            row, :
        ].astype(F32)
        out[layer, 4:5, 0:units] = up[row, :].astype(F32)
        out[layer, 5:6, 0:narrow] = q[row, :].astype(F32)
        out[layer, 6:7, 0:narrow] = v[row, :].astype(F32)
        out[layer, 7:8, 0:narrow] = cq[row, :].astype(F32)
        out[layer, 4:5, 1024 : 1024 + narrow] = cv[row, :].astype(F32)


def assemble_kernel(info, *refs, narrow, units, columns):
    parts, (mods, narrows, ups) = refs[:4], refs[4:]
    narrows[...] = jnp.zeros(narrows.shape, F32)
    for rank in range(4):

        @pl.when(info[5] == rank)
        def _(rank=rank):
            for shard in range(4):
                part = parts[shard ^ rank]
                for layer in range(LAYERS):
                    mods[layer, :, shard * columns : (shard + 1) * columns] = part[
                        layer, 0:SLOTS, 0:columns
                    ]
                    ups[layer, :, shard * units : (shard + 1) * units] = part[layer, 4:5, 0:units]
                    at = slice(shard * narrow, (shard + 1) * narrow)
                    for row, source in ((0, 5), (2, 6), (3, 7)):
                        narrows[layer, row : row + 1, at] = part[
                            layer, source : source + 1, 0:narrow
                        ]
                    narrows[layer, 5:6, at] = part[layer, 4:5, 1024 : 1024 + narrow]


def collect_kernel(info, *refs, narrow, units, columns):
    stats, condition, out = refs[: 2 * LAYERS], refs[2 * LAYERS], refs[2 * LAYERS + 1]
    sums = refs[2 * LAYERS + 2]
    width = stats[0].shape[1]
    work = out
    out = refs[2 * LAYERS + 3]
    out[...] = jnp.zeros(out.shape, F32)
    for layer in range(LAYERS):
        sums[...] = stats[2 * layer][...] + stats[2 * layer + 1][...]
        base = 8 * layer
        out[base + 4 : base + 5, width : 2 * width] = sums[60:61, :]
        out[base + 5 : base + 6, 0:width] = sums[12:13, :]
        out[base + 5 : base + 6, width : 2 * width] = sums[36:37, :]
        for index in range(2):
            out[base + 6 + index : base + 7 + index, 512 : 512 + width] = condition[
                2 * layer + index : 2 * layer + index + 1, :
            ].astype(F32)
        for rank in range(4):

            @pl.when(info[5] == rank)
            def _(rank=rank, base=base):
                first = rank * columns
                for index in range(9):
                    low = max(first, index * width)
                    high = min(first + columns, (index + 1) * width)
                    if low < high:
                        row = (index // 3) * 24 + (index % 3) * 4
                        out[base : base + 4, low - first : high - first] = sums[
                            row : row + 4, low - index * width : high - index * width
                        ]
                out[base + 4 : base + 5, 0:units] = sums[61 + rank : 62 + rank, :]
                own = slice(rank * narrow, (rank + 1) * narrow)
                out[base + 6 : base + 7, 0:narrow] = sums[13:14, own]
                out[base + 6 : base + 7, 256 : 256 + narrow] = sums[14:15, own]
                out[base + 7 : base + 8, 0:narrow] = sums[37:38, own]
                out[base + 7 : base + 8, 256 : 256 + narrow] = sums[38:39, own]
    work[...] = out[...].astype(BF)


def spread_kernel(info, gathered, grad, bias_grad, q, v, cq, cv, up, o1, o2, o3, rows, conditions):
    count = gathered.shape[0]
    columns, part = grad.shape[2], grad.shape[1]
    width, narrow, units = conditions.shape[1], q.shape[1], up.shape[1]
    shift = lax.rem(width - info[8] * part, width)
    for index in range(count):
        for slot in range(SLOTS):
            row = 8 * (slot // 2) + 6 + slot % 2
            conditions[SLOTS * index + slot : SLOTS * index + slot + 1, :] = gathered[
                index ^ info[8], row : row + 1, 512 : 512 + width
            ].astype(F32)
    turned = pltpu.roll(conditions[...], shift, 1)[:, :part].T
    for layer in range(LAYERS):
        base = 8 * layer
        sums = jnp.zeros((8, gathered.shape[2]), F32)
        for index in range(count):
            values = gathered[index ^ info[8]].astype(F32)[base : base + 8]
            sums += values
            rows[SLOTS * index : SLOTS * (index + 1), :] = values[0:SLOTS, 0:columns]
        grad[layer] = jnp.dot(
            turned, rows[...], precision=lax.Precision.HIGHEST, preferred_element_type=F32
        )
        at = slice(layer, layer + 1)
        bias_grad[at, :] = jnp.sum(sums[0:SLOTS, 0:columns], axis=0, keepdims=True)
        up[at, :] = sums[4:5, 0:units]
        q[at, :] = sums[6:7, 0:narrow]
        v[at, :] = sums[6:7, 256 : 256 + narrow]
        cq[at, :] = sums[7:8, 0:narrow]
        cv[at, :] = sums[7:8, 256 : 256 + narrow]
        for out, row, lane in ((o1, 5, 0), (o2, 5, width), (o3, 4, width)):
            own = jnp.broadcast_to(sums[row : row + 1, lane : lane + width], (8, width))
            out[at, :] = pltpu.roll(own, shift, 1)[0:1, :part]


def finish_kernel(*refs, wide, spots):
    parts, outs = refs[: 2 * len(spots)], refs[2 * len(spots) :]
    step = 3 * LANES
    for chain, places in enumerate(spots):
        values = parts[2 * chain][0].astype(F32) + parts[2 * chain + 1][0].astype(F32)
        at = 0
        for layer, pair in places:
            if wide:
                width = outs[0].shape[2]
                for out in outs:
                    out[layer] = values[:, at : at + width]
                    at += width
                continue
            both = values[:, at : at + step]
            at += step
            first = jnp.concatenate(
                [both[:, :LANES], both[:, 2 * LANES : 2 * LANES + HEAD_WIDTH]], axis=1
            )
            second = jnp.concatenate(
                [both[:, LANES : 2 * LANES], both[:, 2 * LANES + HEAD_WIDTH :]], axis=1
            )
            for out, matrix in zip(outs[2 * pair : 2 * pair + 2], (first, second)):
                out[layer] = matrix if out.shape[1:] == matrix.shape else matrix.T


def join_kernel(info, rows, other, out):
    share = rows.shape[0]
    for core in range(2):

        @pl.when(info[5] % 2 == core)
        def _(core=core):
            out[pl.ds(core * share, share), :] = rows[...]
            out[pl.ds((1 - core) * share, share), :] = other[...]


def tensor_hop(values, step):
    return lax.ppermute(values, "tensor", [(i, i ^ step) for i in range(4)])


def dp_hop(values, step):
    size = lax.axis_size("dp")
    return lax.ppermute(values, "dp", [(i, i ^ step) for i in range(size)])


def time_features(moments, width):
    half = width // 2
    rates = jnp.exp(-math.log(10000.0) * jnp.arange(half, dtype=F32) / half)
    angles = moments.astype(F32)[:, None] * rates[None, :]
    return jnp.concatenate([jnp.cos(angles), jnp.sin(angles)], axis=1)


def shards(
    tokens,
    text,
    timesteps,
    item_frames,
    cotangent,
    self_query,
    self_query_bias,
    self_key,
    self_value,
    self_value_bias,
    self_output,
    self_output_bias,
    cross_query,
    cross_query_bias,
    cross_key,
    cross_value,
    cross_value_bias,
    cross_output,
    cross_output_bias,
    hidden_up,
    hidden_up_bias,
    hidden_down,
    hidden_down_bias,
    modulation,
    modulation_bias,
):
    frames, width = tokens.shape
    words = text.shape[1]
    columns = modulation.shape[2]
    narrow = self_query.shape[2]
    units = hidden_up.shape[2]
    rank = lax.axis_index("tensor")
    me = lax.axis_index("dp")
    size = lax.axis_size("dp")
    core = rank % 2
    share = frames // 2
    blocks = share // UNIT
    unit = width // size
    turn = lambda values: jnp.swapaxes(values, 1, 2)

    order = jnp.arange(SLOTS, dtype=jnp.int32)
    ends = jnp.sum(jnp.where(order[:, None] <= order[None, :], item_frames[:, None], 0), axis=0)
    turned = (jnp.arange(frames // UNIT, dtype=jnp.int32) + core * blocks) % (2 * blocks)
    slots = jnp.sum((turned[:, None] * UNIT >= ends[None, :]).astype(jnp.int32), axis=1)
    places = jnp.stack([rank, rank // 2, rank ^ 1, me]).astype(jnp.int32)
    info = jnp.concatenate([(rank * 2 + me % 2)[None].astype(jnp.int32), slots, places])

    def pack(members, whole):
        rows = [sum(a.shape[1] for a in some) for _, some in members]
        outs = [shape(r, width, dtype=BF) for r, one in zip(rows, whole) if one]
        outs += [shape(r // 2, width, dtype=BF) for r in rows]
        arrays = [a for _, some in members for a in some]
        results = pl.pallas_call(
            partial(
                pack_kernel,
                groups=[(layer, [None] * len(some)) for layer, some in members],
                whole=whole,
                after=0,
            ),
            out_shape=outs,
            in_specs=[SMALL] + [ANY] * len(arrays),
            out_specs=[ANY] * len(outs),
            scratch_shapes=[
                *[pltpu.VMEM((r, width), BF) for r in rows],
                pltpu.SemaphoreType.DMA((4 * len(members),)),
                pltpu.SemaphoreType.DMA((2 * len(members),)),
            ],
            compiler_params=pltpu.CompilerParams(vmem_limit_bytes=VMEM_BYTES),
            cost_estimate=lasting(1.0),
            name="pack_weights",
        )(info, *arrays)
        return list(results[: sum(whole)]), list(results[sum(whole) :])

    selfs = [turn(self_query), turn(self_key), turn(self_value), self_output]
    crosses = [turn(cross_query), turn(cross_key), turn(cross_value), cross_output]
    own0, first0 = pack([(0, selfs)], [True])
    own1, first1 = pack(
        [(0, crosses), (1, selfs), (1, crosses), (1, [hidden_up]), (1, [hidden_down])],
        [True, True, True, False, False],
    )
    firsts, owns = first0 + first1, own0 + own1

    condition = jax.nn.silu(time_features(timesteps, width)).astype(BF)
    mine = plain(
        mod_kernel,
        "modulation_rows",
        None,
        [
            condition,
            turn(modulation),
            modulation_bias,
            self_query_bias,
            self_value_bias,
            cross_query_bias,
            cross_value_bias,
            hidden_up_bias,
        ],
        [shape(LAYERS, 8, -(-columns // LANES) * LANES)],
        after=[owns[1]],
    )
    others = [tensor_hop(mine, 1), tensor_hop(mine, 2)]
    others.append(tensor_hop(others[0], 2))
    mods, narrow_biases, up_biases = plain(
        partial(assemble_kernel, narrow=narrow, units=units, columns=columns),
        "modulation_of_all",
        info,
        [mine, *others],
        [
            shape(LAYERS, SLOTS, 4 * columns),
            shape(LAYERS, 8, 4 * narrow),
            shape(LAYERS, 1, 4 * units),
        ],
    )
    out_biases = [
        b.reshape(LAYERS, 1, width) for b in (self_output_bias, cross_output_bias, hidden_down_bias)
    ]

    count = len(firsts)
    along_x, along_y, over_x, over_y, sibs = [[None] * count for _ in range(5)]

    def leave(index):
        along_x[index] = tensor_hop(firsts[index], 2)

    def swap(index):
        sibs[index] = tensor_hop(owns[index], 1)

    def go_on(index):
        along_y[index] = dp_hop(along_x[index], 1)
        over_x[index] = tensor_hop(along_x[index], 1)

    def end(index):
        over_y[index] = tensor_hop(along_y[index], 1)

    def weights_of(index):
        return [
            owns[index],
            sibs[index],
            along_x[index],
            along_y[index],
            over_x[index],
            over_y[index],
        ]

    def open_gate(after, leaving=(), at_x=(), at_y=(), settled=()):
        places = [(firsts, i) for i in leaving]
        places += [(along_x, i) for i in at_x] + [(along_y, i) for i in at_y] + list(settled)
        opened = gate([values[i] for values, i in places], after)
        for (values, i), array in zip(places, opened):
            values[i] = array
        for i in leaving:
            leave(i)
        for i in at_x:
            go_on(i)
        for i in at_y:
            end(i)
        return list(opened)

    leave(0)
    swap(0)
    open_gate([mine], [], [0])
    open_gate([others[1]], [1])
    swap(1)
    go_on(1)
    owns += [hidden_up, hidden_down]
    sibs[4:6] = tensor_hop(hidden_up, 1), tensor_hop(hidden_down, 1)
    open_gate([mods], [], [], [0])

    text_rows = jnp.pad(text, ((0, 0), (0, LANES - words), (0, 0))).reshape(-1, width)
    whole = pltpu.VMEM((width, width), BF)
    four = pltpu.VMEM((4, width, units), BF)
    two = pltpu.VMEM((2, width, units), BF)
    floats = pltpu.VMEM((share, width), F32)
    lows = pltpu.VMEM((share, width), BF)
    sems = lambda n: pltpu.SemaphoreType.DMA((n,))
    frame_low = shape(share, width, dtype=BF)
    frame_high = shape(share, width)
    frame_wide = shape(share, 4 * units, dtype=BF)
    frame_chip = shape(share, 2 * units, dtype=BF)
    two_low = shape(2, share, width, dtype=BF)
    two_text = shape(2, SLOTS * LANES, width, dtype=BF)
    logs = shape(16, share)
    log_work = pltpu.VMEM((share, LANES), F32)
    stat_shape = shape(72, width)

    x = lax.dynamic_slice_in_dim(tokens, core * share, share).astype(F32)
    kept = []
    for layer in range(LAYERS):
        first = 2 * layer
        mod = (mods, (layer,))
        biases = (narrow_biases, (layer,))
        common = dict(w=pltpu.VMEM((2, width, width), BF), sems=sems(8))
        if layer == 0:
            entry1, kv = run(
                kv_kernel,
                "self_keys_values",
                info,
                dict(x=x),
                dict(mod=mod, biases=biases),
                weights_of(first),
                dict(entry=frame_low, kv=two_low),
                {},
                common,
                [along_x[1], sibs[1], sibs[4], sibs[5]],
                3.0,
            )
        else:
            entry1, kv, x, branch3 = run(
                kv_kernel,
                "residual_keys_values",
                info,
                dict(part=part, other=tensor_hop(part, 2), below=kept[-1]["x2"]),
                dict(
                    mod=mod,
                    mod_below=(mods, (layer - 1,)),
                    bias=(out_biases[2], (layer - 1,)),
                    biases=biases,
                ),
                weights_of(first),
                dict(entry=frame_low, kv=two_low, x=frame_high, branch=frame_low),
                {},
                common | dict(sum=floats),
                opened,
                3.0,
            )
            kept[-1]["branch3"] = branch3
        kv_sib = tensor_hop(kv, 1)
        opened = (
            open_gate([entry1], [2, 3], [], [], [(over_x, 1)])
            if layer == 0
            else open_gate([entry1], [5], [], [], [(over_x, 4), (over_y, 3)])
        )
        (q,) = run(
            q_kernel,
            "self_query",
            info,
            dict(entry=entry1),
            dict(biases=biases),
            weights_of(first),
            dict(q=frame_low),
            {},
            dict(w=whole, sems=sems(4)),
            [],
            15.0,
        )
        x1, mixed1, lse1, branch1 = run(
            self_kernel,
            "self_attention",
            info,
            dict(q=q, kv_own=kv, kv_sib=kv_sib, x=x),
            dict(mod=mod, bias=(out_biases[0], (layer,))),
            weights_of(first),
            dict(out=frame_high, mixed=frame_low, lse=logs, branch=frame_low),
            {},
            dict(wo=whole, logs=log_work, sum=floats, sems=sems(4)),
            opened,
            8.0,
        )
        if layer == 0:
            opened = open_gate([x1], [4], [2], [1], [(along_x, 3)])
            swap(2)
        else:
            opened = open_gate([x1], [], [5], [4])
        x2, entry2, cq, ckv, mixed2, lse2, branch2 = run(
            partial(cross_kernel, words=words),
            "cross_attention",
            info,
            dict(x=x1, text=text_rows),
            dict(mod=mod, biases=biases, bias=(out_biases[1], (layer,))),
            weights_of(first + 1),
            dict(
                out=frame_high,
                entry=frame_low,
                q=frame_low,
                kv=two_text,
                mixed=frame_low,
                lse=logs,
                branch=frame_low,
            ),
            {},
            dict(
                wq=whole, wk=whole, wv=whole, wo=whole, logs=log_work, sum=floats, sems=sems(16)
            ),
            opened,
            6.0,
        )
        if layer == 0:
            opened = open_gate([x2], [], [3], [2], [(over_x, 2), (sibs, 2), (along_x, 4)])
            swap(3)
        else:
            opened = open_gate([x2], [], [], [5], [(over_x, 5), (over_y, 4)])
        if layer == 0:
            part, entry3, active, slope = run(
                lambda info, work, w: hidden_kernel(info, work, w, 0),
                "feed_forward_part",
                info,
                dict(x=x2),
                dict(mod=mod, up_bias=(up_biases, (layer,))),
                [hidden_up, sibs[4], hidden_down, sibs[5]],
                dict(part=frame_low, entry=frame_low, active=frame_chip, slope=frame_chip),
                {},
                dict(
                    up=two, down=two, before=floats, sum=floats, sems=sems(2), down_sems=sems(2)
                ),
                opened,
                5.0,
            )
            opened = open_gate([part], [], [4], [3], [(over_x, 3), (over_y, 2), (sibs, 3)])
            x3 = branch3 = None
        else:
            x3, entry3, active, slope, branch3, low = run(
                lambda info, work, w: hidden_kernel(info, work, w, 1),
                "feed_forward",
                info,
                dict(x=x2),
                dict(mod=mod, up_bias=(up_biases, (layer,)), bias=(out_biases[2], (layer,))),
                weights_of(4) + weights_of(5),
                dict(
                    out=frame_high,
                    entry=frame_low,
                    active=frame_wide,
                    slope=frame_wide,
                    branch=frame_low,
                    low=frame_low,
                ),
                {},
                dict(
                    up=four, down=four, before=floats, sum=floats, sems=sems(8), down_sems=sems(8)
                ),
                opened,
                7.0,
            )
        kept.append(
            dict(
                x=x,
                entry1=entry1,
                q=q,
                kv=kv,
                kv_sib=kv_sib,
                mixed1=mixed1,
                lse1=lse1,
                branch1=branch1,
                x1=x1,
                entry2=entry2,
                cq=cq,
                ckv=ckv,
                mixed2=mixed2,
                lse2=lse2,
                branch2=branch2,
                x2=x2,
                entry3=entry3,
                active=active,
                slope=slope,
                branch3=branch3,
            )
        )
        x = x3

    def join(rows):
        return plain(
            join_kernel,
            "join_rows",
            info,
            [rows, tensor_hop(rows, 1)],
            [shape(2 * share, width, dtype=BF)],
        )

    output = join(low)

    chains = {}

    def start(name, send, keep):
        view = (size, unit, send.shape[1])
        chains[name] = (tensor_hop(send, 1).reshape(view), keep.reshape(view), 0)

    def held(*names):
        return [chains[name][1] for name in names]

    def advance(names, after=(), cost=1.5):
        targets = [(n, [n]) if isinstance(n, str) else n for n in names]
        targets = [t for t in targets if 2 ** chains[t[1][0]][2] < size]
        if not targets:
            return
        ins, in_specs, outs, out_specs, spots = [], [], [], [], []
        for result, (_, parts) in enumerate(targets):
            column = 0
            for name in parts:
                received, kept_part, bit = chains[name]
                blocks_left, rows, wide = received.shape
                spots.append((result, column))
                column += wide
                for side in range(2):

                    def at(i, info, bit=bit, side=side):
                        return (0, ((info[8] >> bit) & 1) ^ side, 0, 0)

                    for part in (received, kept_part):
                        ins.append(part.reshape(blocks_left // 2, 2, rows, wide))
                        in_specs.append(pl.BlockSpec((blocks_left // 2, None, rows, wide), at))
            for side in range(2):
                outs.append(shape(blocks_left // 2, rows, column, dtype=BF))
                out_specs.append(
                    pl.BlockSpec((blocks_left // 2, rows, column), lambda i, info: (0, 0, 0))
                )
        results = pl.pallas_call(
            partial(merge_kernel, spots=spots, after=len(after)),
            grid_spec=pltpu.PrefetchScalarGridSpec(
                num_scalar_prefetch=1,
                grid=(1,),
                in_specs=in_specs + [ANY] * len(after),
                out_specs=out_specs,
            ),
            out_shape=outs,
            compiler_params=pltpu.CompilerParams(vmem_limit_bytes=VMEM_BYTES),
            cost_estimate=lasting(cost),
            name="merge_grads",
        )(info, *ins, *after)
        for index, (name, parts) in enumerate(targets):
            bit = chains[parts[0]][2]
            hold, give = results[2 * index : 2 * index + 2]
            for part in parts:
                del chains[part]
            chains[name] = (dp_hop(give, 2**bit), hold, bit + 1)

    g = lax.dynamic_slice_in_dim(cotangent, core * share, share).astype(F32)
    sums = []
    last = LAYERS - 1
    for layer in reversed(range(LAYERS)):
        first = 2 * layer
        k = kept[layer]
        mod = (mods, (layer,))
        above = layer + 1
        f_name, c_name, a_name, s_name = [f"{kind}{layer}" for kind in "fcas"]
        n_name = f"n{above}"

        def grads_out(members):
            return {name: shape(width, members * narrow, dtype=BF) for name in ("send", "keep")}

        more, older = [output], []
        if layer < last:
            more = held(f"f{above}", f"c{above}", f"s{above}") + [chains[f"a{above}"][0]]
            older = [n_name, f"c{above}"]
        if layer == last:
            send, keep, g, stats = run(
                lambda info, work, w: hidden_back_kernel(info, work, w, 1),
                "feed_forward_back",
                info,
                dict(g=g, branch=k["branch3"], slope=k["slope"], entry=k["entry3"], x=k["x2"]),
                dict(mod=mod),
                weights_of(4) + weights_of(5) + [k["active"]],
                {name: shape(width, 2 * units, dtype=BF) for name in ("send", "keep")}
                | dict(out=frame_high),
                dict(stats=stat_shape),
                dict(
                    up=four,
                    down=four,
                    gb=lows,
                    d_before=pltpu.VMEM((share, 4 * units), BF),
                    acts=pltpu.VMEM((2, share, units), BF),
                    act_sems=sems(2),
                    before=floats,
                    de=floats,
                    sems=sems(8),
                    down_sems=sems(8),
                ),
                more,
                10.0,
            )
            start(f_name, send, keep)
            extra, scratch = {}, {}
        else:
            part, gb, d_before, stats = run(
                lambda info, work, w: hidden_back_kernel(info, work, w, 0),
                "feed_forward_back_part",
                info,
                dict(g=g, branch=k["branch3"], slope=k["slope"]),
                dict(mod=mod),
                [hidden_up, sibs[4], hidden_down, sibs[5]],
                dict(part=frame_low, gb=frame_low, d_before=frame_chip),
                dict(stats=stat_shape),
                dict(
                    up=two, down=two, before=floats, de=floats, sems=sems(2), down_sems=sems(2)
                ),
                more,
                5.0,
            )
            other = tensor_hop(part, 2)
            advance([(n_name, [f"a{above}", f"s{above}"]), f"c{above}"], [gb], 0.5)
            send, keep = run(
                hidden_grads_kernel,
                "feed_forward_grads",
                info,
                dict(entry=k["entry3"], d_before=d_before, gb=gb, active=k["active"]),
                {},
                [],
                {name: shape(width, 2 * units, dtype=BF) for name in ("send", "keep")},
                {},
                {},
                held(*older),
                1.0,
            )
            start(f_name, send, keep)
            extra = dict(part=part, other=other, above=k["x2"])
            scratch = dict(g_mid=floats)
        send, keep, g, stats = run(
            partial(cross_back_kernel, words=words),
            "cross_attention_back",
            info,
            dict(
                g=g,
                branch=k["branch2"],
                q=k["cq"],
                kv=k["ckv"],
                lse=k["lse2"],
                entry=k["entry2"],
                text=text_rows,
                mixed=k["mixed2"],
                x=k["x1"],
                **extra,
            ),
            dict(mod=mod, early=(stats, ())),
            weights_of(first + 1),
            grads_out(4) | dict(out=frame_high),
            dict(stats=stat_shape),
            dict(
                wq=whole,
                wo=whole,
                gb=lows,
                dq=lows,
                dkv=pltpu.VMEM(two_text.shape, BF),
                d_mixed=lows,
                de=floats,
                dkv_sum=pltpu.VMEM(two_text.shape, F32),
                sems=sems(8),
                **scratch,
            ),
            held(f_name, *older),
            60.0,
        )
        start(c_name, send, keep)
        advance([f_name, *older], [g])
        gb1, dq, dkv_own, dkv_give, stats = run(
            self_back_kernel,
            "self_attention_back",
            info,
            dict(
                g=g, branch=k["branch1"], q=k["q"], kv_own=k["kv"], kv_sib=k["kv_sib"], lse=k["lse1"]
            ),
            dict(mod=mod, early=(stats, ())),
            weights_of(first),
            dict(gb=frame_low, dq=frame_low, dkv_own=two_low, dkv_give=two_low),
            dict(stats=stat_shape),
            dict(wo=whole, d_mixed=lows, sems=sems(4)),
            held(f_name, c_name, *older),
            13.0,
        )
        dkv_sib = tensor_hop(dkv_give, 1)
        advance([f_name, c_name, *older], [dq])
        send, keep = run(
            query_output_kernel,
            "query_output_grads",
            info,
            dict(entry=k["entry1"], gb=gb1, dq=dq, mixed=k["mixed1"]),
            {},
            [],
            grads_out(2),
            {},
            {},
            held(f_name, c_name),
            15.0,
        )
        start(a_name, send, keep)
        arriving = dict(dkv_own=dkv_own, dkv_sib=dkv_sib, entry=k["entry1"])
        if layer == 0:
            send, keep, dkv = run(
                kv_grads_kernel,
                "keys_values_grads",
                info,
                arriving,
                {},
                [],
                grads_out(2) | dict(dkv=two_low),
                {},
                {},
                held(a_name),
                4.0,
            )
            start(s_name, send, keep)
            advance([a_name], held(s_name))
            arriving = dict(dkv=dkv)
        results = run(
            qkv_back_kernel,
            "self_qkv_back",
            info,
            arriving | dict(dq=dq, x=k["x"], g=g),
            dict(mod=mod, early=(stats, ())),
            weights_of(first),
            (dict(low=frame_low) if layer == 0 else grads_out(2)) | dict(out=frame_high),
            dict(stats=stat_shape),
            dict(wq=whole, wk=whole, wv=whole, de=floats, sems=sems(12))
            | (dict(dkv=pltpu.VMEM(two_low.shape, BF)) if layer else {}),
            held(a_name, c_name),
            6.0,
        )
        g, stats = results[-2:]
        if layer:
            start(s_name, *results[:2])
        advance([f_name, c_name, *([a_name, s_name] if layer == 0 else [])], [g])
        sums = [stats, tensor_hop(stats, 1)] + sums
    input_grad = join(results[0])
    vectors = plain(
        partial(collect_kernel, narrow=narrow, units=units, columns=columns),
        "collect_sums",
        info,
        [*sums, condition],
        [shape(16, mine.shape[2], dtype=BF)],
        [pltpu.VMEM(stat_shape.shape, F32), pltpu.VMEM((16, mine.shape[2]), F32)],
        held("s0"),
    )
    gathered = vectors[None]
    hop = size // 2
    while hop:
        both = jnp.stack([gathered, dp_hop(gathered, hop)], axis=1)
        gathered = both.reshape(-1, *vectors.shape)
        hop //= 2
    while any(2 ** chain[2] < size for chain in chains.values()):
        advance(list(chains), held("s0"))

    def parts_of(*names):
        return [part.reshape(1, unit, -1) for name in names for part in chains[name][:2]]

    up_grad, down_grad = plain(
        partial(finish_kernel, wide=True, spots=[[(layer, 0)] for layer in range(LAYERS)]),
        "finish_wide",
        None,
        parts_of(*[f"f{layer}" for layer in range(LAYERS)]),
        [shape(LAYERS, unit, units)] * 2,
        after=held("s0"),
    )
    straight, across = shape(LAYERS, unit, narrow), shape(LAYERS, narrow, unit)
    lasts = [[(1, 0), (1, 1)], [(1, 2), (1, 3)]]
    cq_grad, ck_grad, cv_grad, co_grad, q_grad, o_grad, k_grad, v_grad = plain(
        partial(finish_kernel, wide=False, spots=lasts + [[(0, 0), (0, 1)], [(0, 2)], [(0, 3)]]),
        "finish_narrow",
        None,
        parts_of("c1", "n1", "c0", "a0", "s0"),
        [straight, straight, straight, across, straight, across, straight, straight],
    )
    small = plain(
        spread_kernel,
        "spread_sums",
        info,
        [gathered],
        [shape(LAYERS, unit, columns), shape(LAYERS, columns)]
        + [shape(LAYERS, narrow)] * 4
        + [shape(LAYERS, units)]
        + [shape(LAYERS, unit)] * 3,
        [pltpu.VMEM((SLOTS * size, columns), F32), pltpu.VMEM((SLOTS * size, width), F32)],
    )
    mod_grad, mod_bias_grad, q_sum, v_sum, cq_sum, cv_sum, up_sum, o1, o2, o3 = small
    return (
        output,
        input_grad,
        q_grad,
        q_sum,
        k_grad,
        v_grad,
        v_sum,
        o_grad,
        o1,
        cq_grad,
        cq_sum,
        ck_grad,
        cv_grad,
        cv_sum,
        co_grad,
        o2,
        up_grad,
        up_sum,
        turn(down_grad),
        o3,
        mod_grad,
        mod_bias_grad,
    )


def solution(mesh):
    dp, tensor = "dp", "tensor"
    columns, vector = P(None, None, tensor), P(None, tensor)
    matrix, turned, spread = P(None, dp, tensor), P(None, tensor, dp), P(None, dp)
    placed = (
        P(dp, None),
        P(dp, None, None),
        P(dp),
        P(dp),
        P(dp, None),
        columns,
        vector,
        columns,
        columns,
        vector,
        P(None, tensor, None),
        P(),
        columns,
        vector,
        columns,
        columns,
        vector,
        P(None, tensor, None),
        P(),
        columns,
        vector,
        P(None, tensor, None),
        P(),
        columns,
        vector,
    )
    results = (
        P(dp, None),
        P(dp, None),
        matrix,
        vector,
        matrix,
        matrix,
        vector,
        turned,
        spread,
        matrix,
        vector,
        matrix,
        matrix,
        vector,
        turned,
        spread,
        matrix,
        vector,
        turned,
        spread,
        matrix,
        vector,
    )
    return jax.shard_map(
        shards, mesh=mesh, in_specs=placed, out_specs=results, check_vma=False
    )
```

```python
from functools import partial
import math

import jax
import jax.numpy as jnp
from jax import lax
from jax.experimental import pallas as pl
from jax.experimental.pallas import tpu as pltpu
from jax.sharding import PartitionSpec as P

HEAD_WIDTH = 64
UNIT = 256
LAYERS = 2
WINDOW = 1024
EPSILON = 1e-06
LANES = 128
CHUNK = 64
SLOTS = WINDOW // UNIT
FAR = -1e30
VMEM_BYTES = 62 * 1024 * 1024
BF = jnp.bfloat16
F32 = jnp.float32
ROOT = math.sqrt(2.0 / math.pi)
CUBIC = 0.044715


def dot_nn(left, right):
    return jnp.dot(left, right, preferred_element_type=F32)


def dot_nt(left, right):
    return lax.dot_general(left, right, (((1,), (1,)), ((), ())), preferred_element_type=F32)


def dot_tn(left, right):
    return lax.dot_general(left, right, (((0,), (0,)), ((), ())), preferred_element_type=F32)


SMALL = pl.BlockSpec(memory_space=pltpu.SMEM)
NEAR = pl.BlockSpec(memory_space=pltpu.VMEM)
ANY = pl.BlockSpec(memory_space=pl.ANY)


class Work:
    def __init__(self, ins, outs, scratch, in_sems, out_sems):
        self.ins, self.outs, self.scratch, self.out_sems = ins, outs, scratch, out_sems
        self.copies, self.waited, self.flushed = {}, set(), []
        for index, (name, (ref, buffer)) in enumerate(ins.items()):
            self.copies[name] = pltpu.make_async_copy(ref, buffer, in_sems.at[index])
            self.copies[name].start()

    def __getattr__(self, name):
        if name in self.__dict__["ins"]:
            return self.ins[name][1]
        if name in self.__dict__["outs"]:
            return self.outs[name][1]
        return self.__dict__["scratch"][name]

    def has(self, name):
        return name in self.outs

    def takes(self, name):
        return name in self.ins

    def send(self, name, source, *at):
        ref = self.outs[name][0]
        copy = pltpu.make_async_copy(
            source, ref.at[at] if at else ref, self.out_sems.at[len(self.flushed)]
        )
        copy.start()
        self.flushed.append(copy)

    def need(self, *names):
        for name in names:
            if name not in self.waited:
                self.waited.add(name)
                self.copies[name].wait()

    def flush(self, name, *at):
        ref, buffer = self.outs[name]
        if at:
            ref, buffer = ref.at[at], buffer.at[at]
        copy = pltpu.make_async_copy(buffer, ref, self.out_sems.at[len(self.flushed)])
        copy.start()
        self.flushed.append(copy)

    def finish(self):
        self.need(*self.ins)
        for copy in self.flushed:
            copy.wait()


def run(body, name, info, ins, small, weights, outs, small_outs, scratch, after=(), cost=1.0):
    in_names, out_names, names = list(ins), list(outs), list(scratch)
    small_names, small_out_names = list(small), list(small_outs)
    counts = [1, len(in_names), len(small), len(weights), len(after), len(outs), len(small_outs)]

    def kernel(*refs):
        refs = list(refs)
        parts = []
        for count in counts:
            parts.append(refs[:count])
            refs = refs[count:]
        (info_ref,), in_refs, small_refs, weight_refs, _, out_refs, small_out_refs = parts
        in_bufs, refs = refs[: len(in_names)], refs[len(in_names) :]
        out_bufs, refs = refs[: len(out_names)], refs[len(out_names) :]
        rest, (in_sems, out_sems) = refs[:-2], refs[-2:]
        extra = {}
        rest = list(rest)
        for key in names:
            many = isinstance(scratch[key], list)
            size = len(scratch[key]) if many else 1
            extra[key] = rest[:size] if many else rest[0]
            rest = rest[size:]
        for key, ref in zip(small_names, small_refs):
            index = small[key][1]
            extra[key] = ref.at[index] if index else ref
        extra.update(zip(small_out_names, small_out_refs))
        work = Work(
            dict(zip(in_names, zip(in_refs, in_bufs))),
            dict(zip(out_names, zip(out_refs, out_bufs))),
            extra,
            in_sems,
            out_sems,
        )
        body(info_ref, work, weight_refs)
        work.finish()

    buffer = lambda a: pltpu.VMEM(a.shape, a.dtype)
    flat = []
    for value in scratch.values():
        flat += value if isinstance(value, list) else [value]
    results = pl.pallas_call(
        kernel,
        out_shape=[outs[n] for n in out_names] + [small_outs[n] for n in small_out_names],
        in_specs=[SMALL]
        + [ANY] * len(ins)
        + [NEAR] * len(small)
        + [ANY] * (len(weights) + len(after)),
        out_specs=[ANY] * len(outs) + [NEAR] * len(small_outs),
        scratch_shapes=[buffer(ins[n]) for n in in_names]
        + [buffer(outs[n]) for n in out_names]
        + flat
        + [pltpu.SemaphoreType.DMA((max(len(ins), 1),)), pltpu.SemaphoreType.DMA((32,))],
        compiler_params=pltpu.CompilerParams(vmem_limit_bytes=VMEM_BYTES),
        cost_estimate=lasting(cost),
        name=name,
    )(info, *ins.values(), *[array for array, _ in small.values()], *weights, *after)
    return results


def plain(body, name, info, ins, outs, scratch=(), after=()):
    first = len(ins) + (0 if info is None else 1)
    results = pl.pallas_call(
        lambda *refs: body(*refs[:first], *refs[first + len(after) :]),
        out_shape=outs,
        in_specs=([] if info is None else [SMALL]) + [NEAR] * len(ins) + [ANY] * len(after),
        out_specs=[NEAR] * len(outs),
        scratch_shapes=list(scratch),
        compiler_params=pltpu.CompilerParams(vmem_limit_bytes=VMEM_BYTES),
        cost_estimate=lasting(1.0),
        name=name,
    )(*([] if info is None else [info]), *ins, *after)
    return results if len(outs) > 1 else results[0]


def lasting(units):
    return pl.CostEstimate(flops=int(units * 0.4e9), bytes_accessed=1000, transcendentals=0)


def shape(*dims, dtype=F32):
    return jax.ShapeDtypeStruct(dims, dtype)


def start_rows(refs, place, plan, sems):
    own, sib, xa, ya, xb, yb = refs
    half = own.shape[0] // 2
    for rank in range(4):
        for parity in range(2):

            @pl.when(place == rank * 2 + parity)
            def _(rank=rank, parity=parity):
                for index, (shard, row, rows, dst) in enumerate(plan):
                    step = shard ^ rank
                    if step < 2:
                        src = (own, sib)[step].at[pl.ds(row, rows)]
                    else:
                        first, second = ((xa, ya), (xb, yb))[step - 2]
                        part = row // half
                        src = (first if part == parity else second).at[pl.ds(row - part * half, rows)]
                    pltpu.make_async_copy(src, dst, sems.at[index]).start()


def wait_rows(refs, plan, sems, which):
    for index in which:
        _, row, rows, dst = plan[index]
        pltpu.make_async_copy(refs[0].at[pl.ds(0, rows)], dst, sems.at[index]).wait()


def plan_of(buffers, first, rows):
    return [
        (shard, (first + which) * rows, rows, dst.at[pl.ds(shard * rows, rows)])
        for which, dst in enumerate(buffers)
        for shard in range(4)
    ]


def norm_rows(values):
    mean = jnp.mean(values, axis=-1, keepdims=True)
    center = values - mean
    factor = lax.rsqrt(jnp.mean(center * center, axis=-1, keepdims=True) + EPSILON)
    return center * factor, factor


def piece(mod, slot, index):
    width = mod.shape[1] // 9
    return mod[pl.ds(slot, 1), index * width : (index + 1) * width]


def entry_rows(x, mod, info, index, out):
    for block in range(x.shape[0] // UNIT):
        slot = info[1 + block]
        shift = piece(mod, slot, index)
        scale = 1.0 + piece(mod, slot, index + 1)

        def step(turn, carry):
            rows = pl.ds(pl.multiple_of(block * UNIT + turn * CHUNK, CHUNK), CHUNK)
            normed, _ = norm_rows(x[rows, :])
            out[rows, :] = (normed * scale + shift).astype(BF)
            return carry

        lax.fori_loop(0, UNIT // CHUNK, step, 0, unroll=True)


def residual_rows(x, mod, info, index, branch, branch_out, out, low=None):
    for block in range(x.shape[0] // UNIT):
        gate = piece(mod, info[1 + block], index)

        def step(turn, carry):
            rows = pl.ds(pl.multiple_of(block * UNIT + turn * CHUNK, CHUNK), CHUNK)
            values = branch[rows, :]
            branch_out[rows, :] = values.astype(BF)
            result = x[rows, :] + gate * values
            out[rows, :] = result
            if low is not None:
                low[rows, :] = result.astype(BF)
            return carry

        lax.fori_loop(0, UNIT // CHUNK, step, 0, unroll=True)


def fold(values):
    return jnp.sum(values.reshape(values.shape[0] // 8, 8, values.shape[1]), axis=0)


def total(values):
    return jnp.sum(values, axis=0, keepdims=True)


def gate_back(g, mod, info, index, branch, gb, stats):
    width = g.shape[1]
    sums = jnp.zeros((8, width), F32)
    for block in range(g.shape[0] // UNIT):
        slot = info[1 + block]
        gate = piece(mod, slot, index)

        def step(turn, carry):
            rows = pl.ds(pl.multiple_of(block * UNIT + turn * CHUNK, CHUNK), CHUNK)
            grad = g[rows, :]
            low = (gate * grad).astype(BF)
            gb[rows, :] = low
            return (
                carry[0] + fold(low.astype(F32)),
                carry[1] + fold(grad * branch[rows, :].astype(F32)),
            )

        sums, rows_sum = lax.fori_loop(
            0, UNIT // CHUNK, step, (sums, jnp.zeros((8, width), F32)), unroll=True
        )
        stats[pl.ds(8 + slot, 1), :] += total(rows_sum)
    stats[12:13, :] = total(sums)


def norm_back_rows(x, g, de, mod, info, index, out, stats, low=None):
    width = x.shape[1]
    for block in range(x.shape[0] // UNIT):
        slot = info[1 + block]
        scale = 1.0 + piece(mod, slot, index + 1)

        def step(turn, carry):
            rows = pl.ds(pl.multiple_of(block * UNIT + turn * CHUNK, CHUNK), CHUNK)
            normed, factor = norm_rows(x[rows, :])
            grad = de[rows, :]
            inner = grad * normed
            dn = grad * scale
            mean = jnp.mean(dn, axis=-1, keepdims=True)
            along = jnp.mean(dn * normed, axis=-1, keepdims=True)
            result = g[rows, :] + factor * (dn - mean - normed * along)
            out[rows, :] = result
            if low is not None:
                low[rows, :] = result.astype(BF)
            return (carry[0] + fold(grad), carry[1] + fold(inner))

        zero = jnp.zeros((8, width), F32)
        shift_sum, scale_sum = lax.fori_loop(0, UNIT // CHUNK, step, (zero, zero), unroll=True)
        stats[pl.ds(slot, 1), :] += total(shift_sum)
        stats[pl.ds(4 + slot, 1), :] += total(scale_sum)


def lane_ids(rows):
    return lax.broadcasted_iota(jnp.int32, (rows, LANES), 1)


def head_half(values, half):
    ids = lane_ids(values.shape[0])
    keep = ids < HEAD_WIDTH if half == 0 else ids >= HEAD_WIDTH
    return jnp.where(keep, values.astype(F32), 0.0)


def turned_halves(keys):
    turned = keys.T
    low = lax.broadcasted_iota(jnp.int32, turned.shape, 0) < HEAD_WIDTH
    zero = jnp.zeros(turned.shape, turned.dtype)
    return jnp.concatenate([jnp.where(low, turned, zero), jnp.where(low, zero, turned)], axis=1)


def query_marks(slot):
    return jnp.where(lane_ids(UNIT) == slot, 1.0, 0.0).astype(BF)


def key_marks(slots):
    ids = lane_ids(UNIT)
    parts = [jnp.where((ids < SLOTS) & (ids != slot), FAR, 0.0).astype(BF) for slot in slots]
    return jnp.concatenate(parts, axis=0)


def pair_lanes(pair):
    return pl.ds(pl.multiple_of(pair * LANES, LANES), LANES)


def kv_kernel(info, work, weights):
    rows = weights[0].shape[0] // 4
    plan = plan_of((work.w.at[0], work.w.at[1]), 1, rows)
    start_rows(weights, info[0], plan, work.sems)
    if work.has("branch"):
        work.need("part", "other", "below")
        bias = work.bias[...].astype(F32)
        for row in range(0, work.sum.shape[0], CHUNK):
            span = pl.ds(row, CHUNK)
            work.sum[span, :] = (
                work.part[span, :].astype(F32) + work.other[span, :].astype(F32) + bias
            )
        residual_rows(work.below, work.mod_below, info, 8, work.sum, work.branch, work.x)
        work.flush("branch")
        work.flush("x")
    else:
        work.need("x")
    entry_rows(work.x, work.mod, info, 0, work.entry)
    work.flush("entry")
    entry = work.entry[...]
    wait_rows(weights, plan, work.sems, range(4))
    work.kv[0] = dot_nt(entry, work.w[0]).astype(BF)
    work.flush("kv", 0)
    wait_rows(weights, plan, work.sems, range(4, 8))
    work.kv[1] = (dot_nt(entry, work.w[1]) + work.biases[2:3, :]).astype(BF)
    work.flush("kv", 1)


def q_kernel(info, work, weights):
    rows = weights[0].shape[0] // 4
    plan = plan_of((work.w,), 0, rows)
    start_rows(weights, info[0], plan, work.sems)
    work.need("entry")
    wait_rows(weights, plan, work.sems, range(4))
    work.q[...] = (dot_nt(work.entry[...], work.w[...]) + work.biases[0:1, :]).astype(BF)
    work.flush("q")


def soft_pair(work, q_pair, keys, values, marks, logs, pair, span, words=None):
    ids = lane_ids(UNIT)
    results = []
    kept = logs[span, :]
    for half in range(2):
        left = (head_half(q_pair, half) * HEAD_WIDTH**-0.5).astype(BF)
        if marks is not None:
            left = jnp.concatenate([left, marks], axis=1)
        scores = dot_nt(left, keys)
        if words is not None:
            scores = jnp.where(ids < words, scores, FAR)
        peak = jnp.max(scores, axis=-1, keepdims=True)
        both = dot_nn(jnp.exp(scores - peak).astype(BF), values)
        sums = both[:, LANES:]
        results.append(both[:, :LANES] / sums)
        kept = jnp.where(ids == 2 * pair + half, peak + jnp.log(sums), kept)
    logs[span, :] = kept
    return jnp.where(ids < HEAD_WIDTH, results[0], results[1]).astype(BF)


def self_kernel(info, work, weights):
    rows = weights[0].shape[0] // 4
    sems = work.sems
    plan = [(s, 3 * rows, rows, work.wo.at[pl.ds(s * rows, rows)]) for s in range(4)]
    start_rows(weights, info[0], plan, sems)
    share = work.x.shape[0]
    blocks = share // UNIT
    marks = key_marks([info[1 + b] for b in range(2 * blocks)])
    ones = jnp.ones((2 * share, LANES), BF)
    logs, mixed = work.logs, work.mixed
    logs[...] = jnp.zeros(logs.shape, F32)
    work.need("q", "kv_own", "kv_sib")

    def both(which, lanes):
        return jnp.concatenate([work.kv_own[which, :, lanes], work.kv_sib[which, :, lanes]], axis=0)

    def step(pair, carry):
        lanes = pair_lanes(pair)
        keys = jnp.concatenate([both(0, lanes), marks], axis=1)
        values = jnp.concatenate([both(1, lanes), ones], axis=1)
        for block in range(blocks):
            span = pl.ds(block * UNIT, UNIT)
            mixed[span, lanes] = soft_pair(
                work,
                work.q[span, lanes],
                keys,
                values,
                query_marks(info[1 + block]),
                logs,
                pair,
                span,
            )
        return carry

    lax.fori_loop(0, mixed.shape[1] // LANES, step, 0)
    work.flush("mixed")
    work.lse[...] = logs[...].T[: work.lse.shape[0], :]
    work.flush("lse")
    wait_rows(weights, plan, sems, range(4))
    work.sum[...] = dot_nn(mixed[...], work.wo[...]) + work.bias[...].astype(F32)
    work.need("x")
    residual_rows(work.x, work.mod, info, 2, work.sum, work.branch, work.out)
    work.flush("branch")
    work.flush("out")


def cross_kernel(info, work, weights, words):
    rows = weights[0].shape[0] // 4
    sems = work.sems
    order = (1, 2, 0, 3)
    plan = [
        (shard, order[i // 4] * rows, count, dst)
        for i, (shard, _, count, dst) in enumerate(
            plan_of((work.wk, work.wv, work.wq, work.wo), 0, rows)
        )
    ]
    start_rows(weights, info[0], plan, sems)
    work.need("x")
    entry_rows(work.x, work.mod, info, 3, work.entry)
    work.flush("entry")
    work.need("text")
    wait_rows(weights, plan, sems, range(0, 4))
    work.kv[0] = dot_nt(work.text[...], work.wk[...]).astype(BF)
    wait_rows(weights, plan, sems, range(4, 8))
    work.kv[1] = (dot_nt(work.text[...], work.wv[...]) + work.biases[5:6, :]).astype(BF)
    work.flush("kv")
    wait_rows(weights, plan, sems, range(8, 12))
    work.q[...] = (dot_nt(work.entry[...], work.wq[...]) + work.biases[3:4, :]).astype(BF)
    work.flush("q")
    ones = jnp.ones((LANES, LANES), BF)
    logs, mixed = work.logs, work.mixed
    logs[...] = jnp.zeros(logs.shape, F32)

    def step(pair, carry):
        lanes = pair_lanes(pair)
        for block in range(mixed.shape[0] // UNIT):
            span = pl.ds(block * UNIT, UNIT)
            own = pl.ds(pl.multiple_of(info[1 + block] * LANES, LANES), LANES)
            mixed[span, lanes] = soft_pair(
                work,
                work.q[span, lanes],
                work.kv[0, own, lanes],
                jnp.concatenate([work.kv[1, own, lanes], ones], axis=1),
                None,
                logs,
                pair,
                span,
                words,
            )
        return carry

    lax.fori_loop(0, mixed.shape[1] // LANES, step, 0, unroll=2)
    work.flush("mixed")
    work.lse[...] = logs[...].T[: work.lse.shape[0], :]
    work.flush("lse")
    wait_rows(weights, plan, sems, range(12, 16))
    work.sum[...] = dot_nn(mixed[...], work.wo[...]) + work.bias[...].astype(F32)
    residual_rows(work.x, work.mod, info, 5, work.sum, work.branch, work.out)
    work.flush("branch")
    work.flush("out")


def hidden_plan(refs, buffer):
    rows = buffer.shape[1]
    half = rows // 2
    return [
        (shard, row, half, buffer.at[shard, pl.ds(row, half)])
        for shard in range(4)
        for row in range(0, rows, half)
    ]


def start_chip(info, refs, layer, buffer, sems):
    copies = [
        pltpu.make_async_copy(ref.at[layer], buffer.at[(info[5] + i) % 2], sems.at[i])
        for i, ref in enumerate(refs)
    ]
    for copy in copies:
        copy.start()
    return copies


def bend_rows(before, bias, active, slope, lanes):
    for row in range(0, before.shape[0], CHUNK):
        span = pl.ds(row, CHUNK)
        values = before[span, :] + bias
        square = values * values
        half = 1.0 / (1.0 + jnp.exp(values * (-2.0 * ROOT - (2.0 * ROOT * CUBIC) * square)))
        act = values * half
        active[span, lanes] = act.astype(BF)
        slope[span, lanes] = (
            half + act * (1.0 - half) * (2.0 * ROOT + (6.0 * ROOT * CUBIC) * square)
        ).astype(BF)


def columns_of(shard, width):
    return pl.ds(pl.multiple_of(shard * width, width), width)


def start_hidden(info, work, weights, layer):
    if len(weights) == 4:
        ups = start_chip(info, weights[:2], layer, work.up, work.sems)
        downs = start_chip(info, weights[2:], layer, work.down, work.down_sems)
        return [lambda some=some: [copy.wait() for copy in some] for some in (ups, downs)]
    waits = []
    for refs, buffer, sems in (
        (weights[:6], work.up, work.sems),
        (weights[6:12], work.down, work.down_sems),
    ):
        refs = [ref.at[layer] for ref in refs[:2]] + list(refs[2:])
        plan = hidden_plan(refs, buffer)
        start_rows(refs, info[0], plan, sems)
        waits.append(
            lambda refs=refs, plan=plan, sems=sems: wait_rows(refs, plan, sems, range(len(plan)))
        )
    return waits


def hidden_kernel(info, work, weights, layer):
    waits = start_hidden(info, work, weights, layer)
    width = work.x.shape[1]
    shards = work.up.shape[0]
    first = info[6] * 2 if shards == 2 else 0
    work.need("x")
    entry_rows(work.x, work.mod, info, 6, work.entry)
    work.flush("entry")
    for wait in waits:
        wait()
    start = 0.0 if shards == 2 else work.bias[...].astype(F32)
    work.sum[...] = jnp.zeros(work.sum.shape, F32) + start

    def step(shard, carry):
        lanes = columns_of(shard, width)
        bias = work.up_bias[:, columns_of(first + shard, width)]
        work.before[...] = dot_nn(work.entry[...], work.up[shard])
        bend_rows(work.before, bias, work.active, work.slope, lanes)
        work.sum[...] += dot_nn(work.active[:, lanes], work.down[shard])
        return carry

    lax.fori_loop(0, shards, step, 0)
    work.flush("active")
    work.flush("slope")
    if shards == 2:
        work.part[...] = work.sum[...].astype(BF)
        work.flush("part")
        return
    low = work.low if work.has("low") else None
    residual_rows(work.x, work.mod, info, 8, work.sum, work.branch, work.out, low)
    work.flush("branch")
    work.flush("out")
    if low is not None:
        work.flush("low")


def hidden_back_kernel(info, work, weights, layer):
    waits = start_hidden(info, work, weights, layer)
    width = work.g.shape[1]
    shards = work.up.shape[0]
    if shards == 4:
        actives = [
            pltpu.make_async_copy(
                weights[12].at[:, columns_of(rank, width)], work.acts.at[i], work.act_sems.at[i]
            )
            for i, rank in enumerate((info[7], info[5]))
        ]
        for copy in actives:
            copy.start()
    work.stats[...] = jnp.zeros(work.stats.shape, F32)
    stats = work.stats.at[pl.ds(48, 24)]
    work.need("g", "branch")
    gate_back(work.g, work.mod, info, 8, work.branch, work.gb, stats)
    work.need("slope")
    for wait in waits:
        wait()
    work.de[...] = jnp.zeros(work.de.shape, F32)
    first = info[6] * 2 if shards == 2 else 0

    def step(shard, carry):
        lanes = columns_of(shard, width)
        work.before[...] = dot_nt(work.gb[...], work.down[shard])
        sums = jnp.zeros((8, width), F32)
        for row in range(0, work.g.shape[0], CHUNK):
            span = pl.ds(row, CHUNK)
            low = (work.before[span, :] * work.slope[span, lanes].astype(F32)).astype(BF)
            work.d_before[span, lanes] = low
            sums += fold(low.astype(F32))
        stats[pl.ds(13 + first + shard, 1), :] = total(sums)
        work.de[...] += dot_nt(work.d_before[:, lanes], work.up[shard])
        return carry

    lax.fori_loop(0, shards, step, 0)
    if shards == 2:
        work.part[...] = work.de[...].astype(BF)
        work.flush("part")
        work.flush("gb")
        work.flush("d_before")
        return
    work.need("entry")
    left, right = work.entry[...].T, work.gb[...].T
    for name, index, rank in (("send", 0, info[7]), ("keep", 1, info[5])):
        out = work.outs[name][1]
        out[:, :width] = dot_nn(left, work.d_before[:, columns_of(rank, width)]).astype(BF)
        actives[index].wait()
        out[:, width:] = dot_nn(right, work.acts[index]).astype(BF)
        work.flush(name)
    work.need("x")
    norm_back_rows(work.x, work.g, work.de, work.mod, info, 6, work.out, stats)
    work.flush("out")


def hidden_grads_kernel(info, work, weights):
    width = work.entry.shape[1]
    work.need("entry", "d_before", "gb", "active")
    left, right = work.entry[...].T, work.gb[...].T
    for name, shift in (("send", 1), ("keep", 0)):
        out = work.outs[name][1]
        lanes = columns_of((info[5] + shift) % 2, width)
        out[:, :width] = dot_nn(left, work.d_before[:, lanes]).astype(BF)
        out[:, width:] = dot_nn(right, work.active[:, lanes]).astype(BF)
        work.flush(name)


def pair_grads(info, work, members):
    rows = members[0][0].shape[0]
    low = lane_ids(rows) < HEAD_WIDTH
    step = 3 * LANES
    for at in range(len(members) // 2):
        products = [dot_nn(left, right) for left, right in members[2 * at : 2 * at + 2]]
        (a0, a1, a2), (b0, b1, b2) = [
            [p[:, i * LANES : (i + 1) * LANES] for i in range(3)] for p in products
        ]
        even = (a0, b0, jnp.where(low, a1, pltpu.roll(b1, HEAD_WIDTH, 1)))
        a1, b1 = pltpu.roll(a1, HEAD_WIDTH, 1), pltpu.roll(b1, HEAD_WIDTH, 1)
        a2r, b2r = pltpu.roll(a2, HEAD_WIDTH, 1), pltpu.roll(b2, HEAD_WIDTH, 1)
        odd = (jnp.where(low, a1, a2r), jnp.where(low, b1, b2r), jnp.where(low, a2r, b2))
        first = info[5] % 2 == 0
        for i, (mine, other) in enumerate(zip(even, odd)):
            lanes = pl.ds(at * step + i * LANES, LANES)
            work.outs["keep"][1][:, lanes] = jnp.where(first, mine, other).astype(BF)
            work.outs["send"][1][:, lanes] = jnp.where(first, other, mine).astype(BF)
    work.flush("send")
    work.flush("keep")


def chip_lanes(info, width):
    return pl.ds(pl.multiple_of(info[6] * (width // 2), width // 2), width // 2)


def query_output_kernel(info, work, weights):
    work.need("entry", "gb", "dq", "mixed")
    lanes = chip_lanes(info, work.dq.shape[1])
    pair_grads(
        info,
        work,
        [
            (work.entry[...].T, work.dq[:, lanes]),
            (work.gb[...].T, work.mixed[:, lanes]),
        ],
    )


def cross_back_kernel(info, work, weights, words):
    rows = weights[0].shape[0] // 4
    sems = work.sems
    plan = [
        (shard, (3 * rows, 0)[i // 4], count, dst)
        for i, (shard, _, count, dst) in enumerate(plan_of((work.wo, work.wq), 0, rows))
    ]
    start_rows(weights, info[0], plan, sems)
    work.stats[...] = work.early[...]
    stats = work.stats.at[pl.ds(24, 24)]
    g = work.g
    work.need("g")
    if work.takes("part"):
        work.need("part", "other", "above")
        for row in range(0, g.shape[0], CHUNK):
            span = pl.ds(row, CHUNK)
            work.de[span, :] = work.part[span, :].astype(F32) + work.other[span, :].astype(F32)
        g = work.g_mid
        norm_back_rows(
            work.above, work.g, work.de, work.mod, info, 6, g, work.stats.at[pl.ds(48, 24)]
        )
    work.need("branch")
    gate_back(g, work.mod, info, 5, work.branch, work.gb, stats)
    wait_rows(weights, plan, sems, range(0, 4))
    work.d_mixed[...] = dot_nt(work.gb[...], work.wo[...]).astype(BF)
    work.dkv_sum[...] = jnp.zeros(work.dkv_sum.shape, F32)
    real = lax.broadcasted_iota(jnp.int32, (LANES, UNIT), 0) < words
    work.need("q", "kv", "lse")

    def step(pair, carry):
        lanes = pair_lanes(pair)
        for block in range(work.q.shape[0] // UNIT):
            span = pl.ds(block * UNIT, UNIT)
            own = pl.ds(pl.multiple_of(info[1 + block] * LANES, LANES), LANES)
            q_pair = work.q[span, lanes]
            d_pair = work.d_mixed[span, lanes]
            keys = work.kv[0, own, lanes]
            values = work.kv[1, own, lanes]
            lefts, grads, probs_low, scores_low = [], [], [], []
            for half in range(2):
                left = (head_half(q_pair, half) * HEAD_WIDTH**-0.5).astype(BF)
                grad = head_half(d_pair, half).astype(BF)
                logs = work.lse[pl.ds(2 * pair + half, 1), span]
                probs = jnp.where(real, jnp.exp(dot_nt(keys, left) - logs), 0.0)
                d_probs = dot_nt(values, grad)
                inner = jnp.sum(probs * d_probs, axis=0, keepdims=True)
                lefts.append(left)
                grads.append(grad)
                probs_low.append(probs.astype(BF))
                scores_low.append((probs * (d_probs - inner)).astype(BF))
            wide_scores = jnp.concatenate(scores_low, axis=1)
            grad_v = dot_nn(jnp.concatenate(probs_low, axis=1), jnp.concatenate(grads, axis=0))
            grad_k = dot_nn(wide_scores, jnp.concatenate(lefts, axis=0))
            grad_q = dot_nn(turned_halves(keys), jnp.concatenate(scores_low, axis=0))
            work.dq[span, lanes] = (grad_q.T * HEAD_WIDTH**-0.5).astype(BF)
            work.dkv_sum[0, own, lanes] += grad_k
            work.dkv_sum[1, own, lanes] += grad_v
        return carry

    lax.fori_loop(0, work.q.shape[1] // LANES, step, 0, unroll=2)
    work.dkv[...] = work.dkv_sum[...].astype(BF)
    work.need("entry", "text", "mixed")
    lanes = chip_lanes(info, work.dq.shape[1])
    text = work.text[...].T
    pair_grads(
        info,
        work,
        [
            (work.entry[...].T, work.dq[:, lanes]),
            (text, work.dkv[0, :, lanes]),
            (text, work.dkv[1, :, lanes]),
            (work.gb[...].T, work.mixed[:, lanes]),
        ],
    )
    stats[13:14, :] = total(fold(work.dq[...].astype(F32)))
    stats[14:15, :] = total(fold(work.dkv[1].astype(F32)))
    wait_rows(weights, plan, sems, range(4, 8))
    work.de[...] = dot_nn(work.dq[...], work.wq[...])
    work.need("x")
    norm_back_rows(work.x, g, work.de, work.mod, info, 3, work.out, stats)
    work.flush("out")


def self_back_kernel(info, work, weights):
    rows = weights[0].shape[0] // 4
    sems = work.sems
    plan = [(s, 3 * rows, rows, work.wo.at[pl.ds(s * rows, rows)]) for s in range(4)]
    start_rows(weights, info[0], plan, sems)
    work.stats[...] = work.early[...]
    stats = work.stats.at[pl.ds(0, 24)]
    work.need("g", "branch")
    gate_back(work.g, work.mod, info, 2, work.branch, work.gb, stats)
    work.flush("gb")
    share = work.g.shape[0]
    blocks = share // UNIT
    marks = key_marks([info[1 + b] for b in range(2 * blocks)])
    wait_rows(weights, plan, sems, range(4))
    work.d_mixed[...] = dot_nt(work.gb[...], work.wo[...]).astype(BF)
    work.need("q", "kv_own", "kv_sib", "lse")

    def both(which, lanes):
        return jnp.concatenate([work.kv_own[which, :, lanes], work.kv_sib[which, :, lanes]], axis=0)

    def step(pair, carry):
        lanes = pair_lanes(pair)
        keys = both(0, lanes)
        values = both(1, lanes)
        marked = jnp.concatenate([keys, marks], axis=1)
        turned = turned_halves(keys)
        lefts, grads, probs_low, scores_low = [], [], [], []
        for block in range(blocks):
            span = pl.ds(block * UNIT, UNIT)
            q_pair = work.q[span, lanes]
            d_pair = work.d_mixed[span, lanes]
            ends = query_marks(info[1 + block])
            for half in range(2):
                left = (head_half(q_pair, half) * HEAD_WIDTH**-0.5).astype(BF)
                grad = head_half(d_pair, half).astype(BF)
                logs = work.lse[pl.ds(2 * pair + half, 1), span]
                probs = jnp.exp(dot_nt(marked, jnp.concatenate([left, ends], axis=1)) - logs)
                d_probs = dot_nt(values, grad)
                inner = jnp.sum(probs * d_probs, axis=0, keepdims=True)
                lefts.append(left)
                grads.append(grad)
                probs_low.append(probs.astype(BF))
                scores_low.append((probs * (d_probs - inner)).astype(BF))
            grad_q = dot_nn(turned, jnp.concatenate(scores_low[-2:], axis=0))
            work.dq[span, lanes] = (grad_q.T * HEAD_WIDTH**-0.5).astype(BF)
        grad_v = dot_nn(jnp.concatenate(probs_low, axis=1), jnp.concatenate(grads, axis=0))
        grad_k = dot_nn(jnp.concatenate(scores_low, axis=1), jnp.concatenate(lefts, axis=0))
        for which, grad in ((0, grad_k.astype(BF)), (1, grad_v.astype(BF))):
            work.dkv_own[which, :, lanes] = grad[:share]
            work.dkv_give[which, :, lanes] = grad[share:]
        return carry

    lax.fori_loop(0, work.q.shape[1] // LANES, step, 0)
    work.flush("dkv_give")
    work.flush("dkv_own")
    work.flush("dq")


def sum_keys_values(info, work, dkv):
    work.need("dkv_own", "dkv_sib")
    for which in range(2):
        dkv[which] = (
            work.dkv_own[which].astype(F32) + work.dkv_sib[which].astype(F32)
        ).astype(BF)
    work.need("entry")
    lanes = chip_lanes(info, dkv.shape[2])
    entry = work.entry[...].T
    pair_grads(info, work, [(entry, dkv[0, :, lanes]), (entry, dkv[1, :, lanes])])


def kv_grads_kernel(info, work, weights):
    sum_keys_values(info, work, work.dkv)
    work.flush("dkv")


def qkv_back_kernel(info, work, weights):
    rows = weights[0].shape[0] // 4
    sems = work.sems
    plan = plan_of((work.wq, work.wk, work.wv), 0, rows)
    start_rows(weights, info[0], plan, sems)
    work.stats[...] = work.early[...]
    stats = work.stats.at[pl.ds(0, 24)]
    if work.has("send"):
        sum_keys_values(info, work, work.dkv)
    else:
        work.need("dkv")
    work.need("dq")
    stats[13:14, :] = total(fold(work.dq[...].astype(F32)))
    stats[14:15, :] = total(fold(work.dkv[1].astype(F32)))
    wait_rows(weights, plan, sems, range(0, 12))
    work.de[...] = (
        dot_nn(work.dq[...], work.wq[...])
        + dot_nn(work.dkv[0], work.wk[...])
        + dot_nn(work.dkv[1], work.wv[...])
    )
    work.need("x", "g")
    low = work.low if work.has("low") else None
    norm_back_rows(work.x, work.g, work.de, work.mod, info, 0, work.out, stats, low)
    work.flush("out")
    if low is not None:
        work.flush("low")


def merge_kernel(info, *refs, spots, after):
    chains = len(spots)
    ins, outs = refs[: 4 * chains], refs[4 * chains + after :]
    for chain, (result, column) in enumerate(spots):
        for side in range(2):
            received, kept = ins[4 * chain + 2 * side], ins[4 * chain + 2 * side + 1]
            out = outs[2 * result + side]
            lanes = pl.ds(column, received.shape[2])
            out[:, :, lanes] = (received[...].astype(F32) + kept[...].astype(F32)).astype(BF)


def gate(arrays, after):
    count = len(arrays)
    return pl.pallas_call(
        lambda *refs: None,
        out_shape=[shape(*a.shape, dtype=a.dtype) for a in arrays],
        in_specs=[ANY] * (count + len(after)),
        out_specs=[ANY] * count,
        input_output_aliases={i: i for i in range(count)},
        cost_estimate=lasting(0.5),
        name="gate",
    )(*arrays, *after)


def pack_kernel(info, *refs, groups, whole, after):
    count = sum(len(members) for _, members in groups)
    sources, rest = refs[:count], refs[count + after :]
    (in_sems, out_sems), rest = rest[-2:], rest[:-2]
    count = len(groups) + sum(whole)
    outs, held = list(rest[:count]), rest[count:]
    owns = [outs.pop(0) if one else None for one in whole]
    spots = []
    at = 0
    for index, (layer, members) in enumerate(groups):
        rows = held[index].shape[0]
        piece_rows = rows // 4
        for quarter in range(4):
            row = quarter * piece_rows
            source = sources[at + quarter * len(members) // 4]
            src = source.at[layer, pl.ds(row % source.shape[1], piece_rows)]
            spots.append((index, quarter, held[index].at[pl.ds(row, piece_rows)], src))
        at += len(members)

    def arriving(place):
        _, _, spot, src = spots[place]
        return pltpu.make_async_copy(src, spot, in_sems.at[place])

    def leaving(index, which):
        if which == 2:
            return pltpu.make_async_copy(held[index], owns[index], out_sems.at[2 * index])
        rows = outs[index].shape[0]
        src = held[index].at[pl.ds(which * rows, rows)]
        return pltpu.make_async_copy(src, outs[index], out_sems.at[2 * index + 1])

    def by_parity(act):
        for parity in range(2):

            @pl.when(info[0] % 2 == parity)
            def _(parity=parity):
                act(parity)

    for place in range(len(spots)):
        arriving(place).start()
    for index in range(len(groups)):
        for quarter in range(4):
            arriving(4 * index + quarter).wait()
        by_parity(lambda parity: leaving(index, parity).start())
        if whole[index]:
            leaving(index, 2).start()
    for index in range(len(groups)):
        by_parity(lambda parity: leaving(index, parity).wait())
        if whole[index]:
            leaving(index, 2).wait()


def mod_kernel(condition, mod, mod_bias, q, v, cq, cv, up, out):
    narrow, units, columns = q.shape[1], up.shape[1], mod.shape[1]
    out[...] = jnp.zeros(out.shape, F32)
    for layer in range(LAYERS):
        row = pl.ds(layer, 1)
        out[layer, 0:SLOTS, 0:columns] = dot_nt(condition[...], mod[layer]) + mod_bias[
            row, :
        ].astype(F32)
        out[layer, 4:5, 0:units] = up[row, :].astype(F32)
        out[layer, 5:6, 0:narrow] = q[row, :].astype(F32)
        out[layer, 6:7, 0:narrow] = v[row, :].astype(F32)
        out[layer, 7:8, 0:narrow] = cq[row, :].astype(F32)
        out[layer, 4:5, 1024 : 1024 + narrow] = cv[row, :].astype(F32)


def assemble_kernel(info, *refs, narrow, units, columns):
    parts, (mods, narrows, ups) = refs[:4], refs[4:]
    narrows[...] = jnp.zeros(narrows.shape, F32)
    for rank in range(4):

        @pl.when(info[5] == rank)
        def _(rank=rank):
            for shard in range(4):
                part = parts[shard ^ rank]
                for layer in range(LAYERS):
                    mods[layer, :, shard * columns : (shard + 1) * columns] = part[
                        layer, 0:SLOTS, 0:columns
                    ]
                    ups[layer, :, shard * units : (shard + 1) * units] = part[layer, 4:5, 0:units]
                    at = slice(shard * narrow, (shard + 1) * narrow)
                    for row, source in ((0, 5), (2, 6), (3, 7)):
                        narrows[layer, row : row + 1, at] = part[
                            layer, source : source + 1, 0:narrow
                        ]
                    narrows[layer, 5:6, at] = part[layer, 4:5, 1024 : 1024 + narrow]


def collect_kernel(info, *refs, narrow, units, columns):
    stats, condition, out = refs[: 2 * LAYERS], refs[2 * LAYERS], refs[2 * LAYERS + 1]
    sums = refs[2 * LAYERS + 2]
    width = stats[0].shape[1]
    work = out
    out = refs[2 * LAYERS + 3]
    out[...] = jnp.zeros(out.shape, F32)
    for layer in range(LAYERS):
        sums[...] = stats[2 * layer][...] + stats[2 * layer + 1][...]
        base = 8 * layer
        out[base + 4 : base + 5, width : 2 * width] = sums[60:61, :]
        out[base + 5 : base + 6, 0:width] = sums[12:13, :]
        out[base + 5 : base + 6, width : 2 * width] = sums[36:37, :]
        for index in range(2):
            out[base + 6 + index : base + 7 + index, 512 : 512 + width] = condition[
                2 * layer + index : 2 * layer + index + 1, :
            ].astype(F32)
        for rank in range(4):

            @pl.when(info[5] == rank)
            def _(rank=rank, base=base):
                first = rank * columns
                for index in range(9):
                    low = max(first, index * width)
                    high = min(first + columns, (index + 1) * width)
                    if low < high:
                        row = (index // 3) * 24 + (index % 3) * 4
                        out[base : base + 4, low - first : high - first] = sums[
                            row : row + 4, low - index * width : high - index * width
                        ]
                out[base + 4 : base + 5, 0:units] = sums[61 + rank : 62 + rank, :]
                own = slice(rank * narrow, (rank + 1) * narrow)
                out[base + 6 : base + 7, 0:narrow] = sums[13:14, own]
                out[base + 6 : base + 7, 256 : 256 + narrow] = sums[14:15, own]
                out[base + 7 : base + 8, 0:narrow] = sums[37:38, own]
                out[base + 7 : base + 8, 256 : 256 + narrow] = sums[38:39, own]
    work[...] = out[...].astype(BF)


def spread_kernel(info, gathered, grad, bias_grad, q, v, cq, cv, up, o1, o2, o3, rows, conditions):
    count = gathered.shape[0]
    columns, part = grad.shape[2], grad.shape[1]
    width, narrow, units = conditions.shape[1], q.shape[1], up.shape[1]
    shift = lax.rem(width - info[8] * part, width)
    for index in range(count):
        for slot in range(SLOTS):
            row = 8 * (slot // 2) + 6 + slot % 2
            conditions[SLOTS * index + slot : SLOTS * index + slot + 1, :] = gathered[
                index ^ info[8], row : row + 1, 512 : 512 + width
            ].astype(F32)
    turned = pltpu.roll(conditions[...], shift, 1)[:, :part].T
    for layer in range(LAYERS):
        base = 8 * layer
        sums = jnp.zeros((8, gathered.shape[2]), F32)
        for index in range(count):
            values = gathered[index ^ info[8]].astype(F32)[base : base + 8]
            sums += values
            rows[SLOTS * index : SLOTS * (index + 1), :] = values[0:SLOTS, 0:columns]
        grad[layer] = jnp.dot(
            turned, rows[...], precision=lax.Precision.HIGHEST, preferred_element_type=F32
        )
        at = slice(layer, layer + 1)
        bias_grad[at, :] = jnp.sum(sums[0:SLOTS, 0:columns], axis=0, keepdims=True)
        up[at, :] = sums[4:5, 0:units]
        q[at, :] = sums[6:7, 0:narrow]
        v[at, :] = sums[6:7, 256 : 256 + narrow]
        cq[at, :] = sums[7:8, 0:narrow]
        cv[at, :] = sums[7:8, 256 : 256 + narrow]
        for out, row, lane in ((o1, 5, 0), (o2, 5, width), (o3, 4, width)):
            own = jnp.broadcast_to(sums[row : row + 1, lane : lane + width], (8, width))
            out[at, :] = pltpu.roll(own, shift, 1)[0:1, :part]


def finish_kernel(*refs, wide, spots):
    parts, outs = refs[: 2 * len(spots)], refs[2 * len(spots) :]
    step = 3 * LANES
    for chain, places in enumerate(spots):
        values = parts[2 * chain][0].astype(F32) + parts[2 * chain + 1][0].astype(F32)
        at = 0
        for layer, pair in places:
            if wide:
                width = outs[0].shape[2]
                for out in outs:
                    out[layer] = values[:, at : at + width]
                    at += width
                continue
            both = values[:, at : at + step]
            at += step
            first = jnp.concatenate(
                [both[:, :LANES], both[:, 2 * LANES : 2 * LANES + HEAD_WIDTH]], axis=1
            )
            second = jnp.concatenate(
                [both[:, LANES : 2 * LANES], both[:, 2 * LANES + HEAD_WIDTH :]], axis=1
            )
            for out, matrix in zip(outs[2 * pair : 2 * pair + 2], (first, second)):
                out[layer] = matrix if out.shape[1:] == matrix.shape else matrix.T


def join_kernel(info, rows, other, out):
    share = rows.shape[0]
    for core in range(2):

        @pl.when(info[5] % 2 == core)
        def _(core=core):
            out[pl.ds(core * share, share), :] = rows[...]
            out[pl.ds((1 - core) * share, share), :] = other[...]


def tensor_hop(values, step):
    return lax.ppermute(values, "tensor", [(i, i ^ step) for i in range(4)])


def dp_hop(values, step):
    size = lax.axis_size("dp")
    return lax.ppermute(values, "dp", [(i, i ^ step) for i in range(size)])


def time_features(moments, width):
    half = width // 2
    rates = jnp.exp(-math.log(10000.0) * jnp.arange(half, dtype=F32) / half)
    angles = moments.astype(F32)[:, None] * rates[None, :]
    return jnp.concatenate([jnp.cos(angles), jnp.sin(angles)], axis=1)


def shards(
    tokens,
    text,
    timesteps,
    item_frames,
    cotangent,
    self_query,
    self_query_bias,
    self_key,
    self_value,
    self_value_bias,
    self_output,
    self_output_bias,
    cross_query,
    cross_query_bias,
    cross_key,
    cross_value,
    cross_value_bias,
    cross_output,
    cross_output_bias,
    hidden_up,
    hidden_up_bias,
    hidden_down,
    hidden_down_bias,
    modulation,
    modulation_bias,
):
    frames, width = tokens.shape
    words = text.shape[1]
    columns = modulation.shape[2]
    narrow = self_query.shape[2]
    units = hidden_up.shape[2]
    rank = lax.axis_index("tensor")
    me = lax.axis_index("dp")
    size = lax.axis_size("dp")
    core = rank % 2
    share = frames // 2
    blocks = share // UNIT
    unit = width // size
    turn = lambda values: jnp.swapaxes(values, 1, 2)

    order = jnp.arange(SLOTS, dtype=jnp.int32)
    ends = jnp.sum(jnp.where(order[:, None] <= order[None, :], item_frames[:, None], 0), axis=0)
    turned = (jnp.arange(frames // UNIT, dtype=jnp.int32) + core * blocks) % (2 * blocks)
    slots = jnp.sum((turned[:, None] * UNIT >= ends[None, :]).astype(jnp.int32), axis=1)
    places = jnp.stack([rank, rank // 2, rank ^ 1, me]).astype(jnp.int32)
    info = jnp.concatenate([(rank * 2 + me % 2)[None].astype(jnp.int32), slots, places])

    def pack(members, whole, after=()):
        rows = [sum(a.shape[1] for a in some) for _, some in members]
        outs = [shape(r, width, dtype=BF) for r, one in zip(rows, whole) if one]
        outs += [shape(r // 2, width, dtype=BF) for r in rows]
        arrays = [a for _, some in members for a in some]
        results = pl.pallas_call(
            partial(
                pack_kernel,
                groups=[(layer, [None] * len(some)) for layer, some in members],
                whole=whole,
                after=len(after),
            ),
            out_shape=outs,
            in_specs=[SMALL] + [ANY] * (len(arrays) + len(after)),
            out_specs=[ANY] * len(outs),
            scratch_shapes=[
                *[pltpu.VMEM((r, width), BF) for r in rows],
                pltpu.SemaphoreType.DMA((4 * len(members),)),
                pltpu.SemaphoreType.DMA((2 * len(members),)),
            ],
            compiler_params=pltpu.CompilerParams(vmem_limit_bytes=VMEM_BYTES),
            cost_estimate=lasting(1.0),
            name="pack_weights",
        )(info, *arrays, *after)
        return list(results[: sum(whole)]), list(results[sum(whole) :])

    selfs = [turn(self_query), turn(self_key), turn(self_value), self_output]
    crosses = [turn(cross_query), turn(cross_key), turn(cross_value), cross_output]
    own0, first0 = pack([(0, selfs)], [True])

    condition = jax.nn.silu(time_features(timesteps, width)).astype(BF)
    mine = plain(
        mod_kernel,
        "modulation_rows",
        None,
        [
            condition,
            turn(modulation),
            modulation_bias,
            self_query_bias,
            self_value_bias,
            cross_query_bias,
            cross_value_bias,
            hidden_up_bias,
        ],
        [shape(LAYERS, 8, -(-columns // LANES) * LANES)],
    )
    own1, first1 = pack(
        [(0, crosses), (1, selfs), (1, crosses), (1, [hidden_up]), (1, [hidden_down])],
        [True, True, True, False, False],
        [mine],
    )
    firsts, owns = first0 + first1, own0 + own1
    others = [tensor_hop(mine, 1), tensor_hop(mine, 2)]
    others.append(tensor_hop(others[0], 2))
    mods, narrow_biases, up_biases = plain(
        partial(assemble_kernel, narrow=narrow, units=units, columns=columns),
        "modulation_of_all",
        info,
        [mine, *others],
        [
            shape(LAYERS, SLOTS, 4 * columns),
            shape(LAYERS, 8, 4 * narrow),
            shape(LAYERS, 1, 4 * units),
        ],
    )
    out_biases = [
        b.reshape(LAYERS, 1, width) for b in (self_output_bias, cross_output_bias, hidden_down_bias)
    ]

    count = len(firsts)
    along_x, along_y, over_x, over_y, sibs = [[None] * count for _ in range(5)]

    def leave(index):
        along_x[index] = tensor_hop(firsts[index], 2)

    def swap(index):
        sibs[index] = tensor_hop(owns[index], 1)

    def go_on(index):
        along_y[index] = dp_hop(along_x[index], 1)
        over_x[index] = tensor_hop(along_x[index], 1)

    def end(index):
        over_y[index] = tensor_hop(along_y[index], 1)

    def weights_of(index):
        return [
            owns[index],
            sibs[index],
            along_x[index],
            along_y[index],
            over_x[index],
            over_y[index],
        ]

    def open_gate(after, leaving=(), at_x=(), at_y=(), settled=()):
        places = [(firsts, i) for i in leaving]
        places += [(along_x, i) for i in at_x] + [(along_y, i) for i in at_y] + list(settled)
        opened = gate([values[i] for values, i in places], after)
        for (values, i), array in zip(places, opened):
            values[i] = array
        for i in leaving:
            leave(i)
        for i in at_x:
            go_on(i)
        for i in at_y:
            end(i)
        return list(opened)

    leave(0)
    swap(0)
    open_gate([mine], [], [0])
    open_gate(others[:2], [1])
    swap(1)
    go_on(1)
    owns += [hidden_up, hidden_down]
    sibs[4:6] = tensor_hop(hidden_up, 1), tensor_hop(hidden_down, 1)
    open_gate([mods], [], [], [0])

    text_rows = jnp.pad(text, ((0, 0), (0, LANES - words), (0, 0))).reshape(-1, width)
    whole = pltpu.VMEM((width, width), BF)
    four = pltpu.VMEM((4, width, units), BF)
    two = pltpu.VMEM((2, width, units), BF)
    floats = pltpu.VMEM((share, width), F32)
    lows = pltpu.VMEM((share, width), BF)
    sems = lambda n: pltpu.SemaphoreType.DMA((n,))
    frame_low = shape(share, width, dtype=BF)
    frame_high = shape(share, width)
    frame_wide = shape(share, 4 * units, dtype=BF)
    frame_chip = shape(share, 2 * units, dtype=BF)
    two_low = shape(2, share, width, dtype=BF)
    two_text = shape(2, SLOTS * LANES, width, dtype=BF)
    logs = shape(16, share)
    log_work = pltpu.VMEM((share, LANES), F32)
    stat_shape = shape(72, width)

    x = lax.dynamic_slice_in_dim(tokens, core * share, share).astype(F32)
    kept = []
    for layer in range(LAYERS):
        first = 2 * layer
        mod = (mods, (layer,))
        biases = (narrow_biases, (layer,))
        common = dict(w=pltpu.VMEM((2, width, width), BF), sems=sems(8))
        if layer == 0:
            entry1, kv = run(
                kv_kernel,
                "self_keys_values",
                info,
                dict(x=x),
                dict(mod=mod, biases=biases),
                weights_of(first),
                dict(entry=frame_low, kv=two_low),
                {},
                common,
                [along_x[1], sibs[1], sibs[4], sibs[5]],
                3.0,
            )
        else:
            entry1, kv, x, branch3 = run(
                kv_kernel,
                "residual_keys_values",
                info,
                dict(part=part, other=tensor_hop(part, 2), below=kept[-1]["x2"]),
                dict(
                    mod=mod,
                    mod_below=(mods, (layer - 1,)),
                    bias=(out_biases[2], (layer - 1,)),
                    biases=biases,
                ),
                weights_of(first),
                dict(entry=frame_low, kv=two_low, x=frame_high, branch=frame_low),
                {},
                common | dict(sum=floats),
                opened,
                3.0,
            )
            kept[-1]["branch3"] = branch3
        kv_sib = tensor_hop(kv, 1)
        opened = (
            open_gate([entry1], [2, 3], [], [], [(over_x, 1)])
            if layer == 0
            else open_gate([entry1], [5], [], [], [(over_x, 4), (over_y, 3)])
        )
        (q,) = run(
            q_kernel,
            "self_query",
            info,
            dict(entry=entry1),
            dict(biases=biases),
            weights_of(first),
            dict(q=frame_low),
            {},
            dict(w=whole, sems=sems(4)),
            [],
            15.0,
        )
        x1, mixed1, lse1, branch1 = run(
            self_kernel,
            "self_attention",
            info,
            dict(q=q, kv_own=kv, kv_sib=kv_sib, x=x),
            dict(mod=mod, bias=(out_biases[0], (layer,))),
            weights_of(first),
            dict(out=frame_high, mixed=frame_low, lse=logs, branch=frame_low),
            {},
            dict(wo=whole, logs=log_work, sum=floats, sems=sems(4)),
            opened,
            8.0,
        )
        if layer == 0:
            opened = open_gate([x1], [4], [2], [1], [(along_x, 3)])
            swap(2)
        else:
            opened = open_gate([x1], [], [5], [4])
        x2, entry2, cq, ckv, mixed2, lse2, branch2 = run(
            partial(cross_kernel, words=words),
            "cross_attention",
            info,
            dict(x=x1, text=text_rows),
            dict(mod=mod, biases=biases, bias=(out_biases[1], (layer,))),
            weights_of(first + 1),
            dict(
                out=frame_high,
                entry=frame_low,
                q=frame_low,
                kv=two_text,
                mixed=frame_low,
                lse=logs,
                branch=frame_low,
            ),
            {},
            dict(
                wq=whole, wk=whole, wv=whole, wo=whole, logs=log_work, sum=floats, sems=sems(16)
            ),
            opened,
            6.0,
        )
        if layer == 0:
            opened = open_gate([x2], [], [3], [2], [(over_x, 2), (sibs, 2), (along_x, 4)])
            swap(3)
        else:
            opened = open_gate([x2], [], [], [5], [(over_x, 5), (over_y, 4)])
        if layer == 0:
            part, entry3, active, slope = run(
                lambda info, work, w: hidden_kernel(info, work, w, 0),
                "feed_forward_part",
                info,
                dict(x=x2),
                dict(mod=mod, up_bias=(up_biases, (layer,))),
                [hidden_up, sibs[4], hidden_down, sibs[5]],
                dict(part=frame_low, entry=frame_low, active=frame_chip, slope=frame_chip),
                {},
                dict(
                    up=two, down=two, before=floats, sum=floats, sems=sems(2), down_sems=sems(2)
                ),
                opened,
                5.0,
            )
            opened = open_gate([part], [], [4], [3], [(over_x, 3), (over_y, 2), (sibs, 3)])
            x3 = branch3 = None
        else:
            x3, entry3, active, slope, branch3, low = run(
                lambda info, work, w: hidden_kernel(info, work, w, 1),
                "feed_forward",
                info,
                dict(x=x2),
                dict(mod=mod, up_bias=(up_biases, (layer,)), bias=(out_biases[2], (layer,))),
                weights_of(4) + weights_of(5),
                dict(
                    out=frame_high,
                    entry=frame_low,
                    active=frame_wide,
                    slope=frame_wide,
                    branch=frame_low,
                    low=frame_low,
                ),
                {},
                dict(
                    up=four, down=four, before=floats, sum=floats, sems=sems(8), down_sems=sems(8)
                ),
                opened,
                7.0,
            )
        kept.append(
            dict(
                x=x,
                entry1=entry1,
                q=q,
                kv=kv,
                kv_sib=kv_sib,
                mixed1=mixed1,
                lse1=lse1,
                branch1=branch1,
                x1=x1,
                entry2=entry2,
                cq=cq,
                ckv=ckv,
                mixed2=mixed2,
                lse2=lse2,
                branch2=branch2,
                x2=x2,
                entry3=entry3,
                active=active,
                slope=slope,
                branch3=branch3,
            )
        )
        x = x3

    def join(rows, *after):
        return plain(
            join_kernel,
            "join_rows",
            info,
            [rows, tensor_hop(rows, 1)],
            [shape(2 * share, width, dtype=BF)],
            after=after,
        )


    chains = {}

    def start(name, send, keep):
        view = (size, unit, send.shape[1])
        chains[name] = (tensor_hop(send, 1).reshape(view), keep.reshape(view), 0)

    def held(*names):
        return [chains[name][1] for name in names]

    def advance(names, after=(), cost=1.5):
        targets = [(n, [n]) if isinstance(n, str) else n for n in names]
        targets = [t for t in targets if 2 ** chains[t[1][0]][2] < size]
        if not targets:
            return
        ins, in_specs, outs, out_specs, spots = [], [], [], [], []
        for result, (_, parts) in enumerate(targets):
            column = 0
            for name in parts:
                received, kept_part, bit = chains[name]
                blocks_left, rows, wide = received.shape
                spots.append((result, column))
                column += wide
                for side in range(2):

                    def at(i, info, bit=bit, side=side):
                        return (0, ((info[8] >> bit) & 1) ^ side, 0, 0)

                    for part in (received, kept_part):
                        ins.append(part.reshape(blocks_left // 2, 2, rows, wide))
                        in_specs.append(pl.BlockSpec((blocks_left // 2, None, rows, wide), at))
            for side in range(2):
                outs.append(shape(blocks_left // 2, rows, column, dtype=BF))
                out_specs.append(
                    pl.BlockSpec((blocks_left // 2, rows, column), lambda i, info: (0, 0, 0))
                )
        results = pl.pallas_call(
            partial(merge_kernel, spots=spots, after=len(after)),
            grid_spec=pltpu.PrefetchScalarGridSpec(
                num_scalar_prefetch=1,
                grid=(1,),
                in_specs=in_specs + [ANY] * len(after),
                out_specs=out_specs,
            ),
            out_shape=outs,
            compiler_params=pltpu.CompilerParams(vmem_limit_bytes=VMEM_BYTES),
            cost_estimate=lasting(cost),
            name="merge_grads",
        )(info, *ins, *after)
        for index, (name, parts) in enumerate(targets):
            bit = chains[parts[0]][2]
            hold, give = results[2 * index : 2 * index + 2]
            for part in parts:
                del chains[part]
            chains[name] = (dp_hop(give, 2**bit), hold, bit + 1)

    g = lax.dynamic_slice_in_dim(cotangent, core * share, share).astype(F32)
    sums = []
    last = LAYERS - 1
    for layer in reversed(range(LAYERS)):
        first = 2 * layer
        k = kept[layer]
        mod = (mods, (layer,))
        above = layer + 1
        f_name, c_name, a_name, s_name = [f"{kind}{layer}" for kind in "fcas"]
        n_name = f"n{above}"

        def grads_out(members):
            return {name: shape(width, members * narrow, dtype=BF) for name in ("send", "keep")}

        more, older = [], []
        if layer < last:
            more = held(f"f{above}", f"c{above}", n_name)
            older = [n_name, f"c{above}"]
        if layer == last:
            send, keep, g, stats = run(
                lambda info, work, w: hidden_back_kernel(info, work, w, 1),
                "feed_forward_back",
                info,
                dict(g=g, branch=k["branch3"], slope=k["slope"], entry=k["entry3"], x=k["x2"]),
                dict(mod=mod),
                weights_of(4) + weights_of(5) + [k["active"]],
                {name: shape(width, 2 * units, dtype=BF) for name in ("send", "keep")}
                | dict(out=frame_high),
                dict(stats=stat_shape),
                dict(
                    up=four,
                    down=four,
                    gb=lows,
                    d_before=pltpu.VMEM((share, 4 * units), BF),
                    acts=pltpu.VMEM((2, share, units), BF),
                    act_sems=sems(2),
                    before=floats,
                    de=floats,
                    sems=sems(8),
                    down_sems=sems(8),
                ),
                more,
                10.0,
            )
            start(f_name, send, keep)
            extra, scratch = {}, {}
        else:
            part, gb, d_before, stats = run(
                lambda info, work, w: hidden_back_kernel(info, work, w, 0),
                "feed_forward_back_part",
                info,
                dict(g=g, branch=k["branch3"], slope=k["slope"]),
                dict(mod=mod),
                [hidden_up, sibs[4], hidden_down, sibs[5]],
                dict(part=frame_low, gb=frame_low, d_before=frame_chip),
                dict(stats=stat_shape),
                dict(
                    up=two, down=two, before=floats, de=floats, sems=sems(2), down_sems=sems(2)
                ),
                more,
                5.0,
            )
            other = tensor_hop(part, 2)
            send, keep = run(
                hidden_grads_kernel,
                "feed_forward_grads",
                info,
                dict(entry=k["entry3"], d_before=d_before, gb=gb, active=k["active"]),
                {},
                [],
                {name: shape(width, 2 * units, dtype=BF) for name in ("send", "keep")},
                {},
                {},
                [gb],
                1.0,
            )
            start(f_name, send, keep)
            output = join(low, gb)
            extra = dict(part=part, other=other, above=k["x2"])
            scratch = dict(g_mid=floats)
        send, keep, g, stats = run(
            partial(cross_back_kernel, words=words),
            "cross_attention_back",
            info,
            dict(
                g=g,
                branch=k["branch2"],
                q=k["cq"],
                kv=k["ckv"],
                lse=k["lse2"],
                entry=k["entry2"],
                text=text_rows,
                mixed=k["mixed2"],
                x=k["x1"],
                **extra,
            ),
            dict(mod=mod, early=(stats, ())),
            weights_of(first + 1),
            grads_out(4) | dict(out=frame_high),
            dict(stats=stat_shape),
            dict(
                wq=whole,
                wo=whole,
                gb=lows,
                dq=lows,
                dkv=pltpu.VMEM(two_text.shape, BF),
                d_mixed=lows,
                de=floats,
                dkv_sum=pltpu.VMEM(two_text.shape, F32),
                sems=sems(8),
                **scratch,
            ),
            held(f_name, *older) + ([output] if layer < last else []),
            60.0,
        )
        start(c_name, send, keep)
        advance([f_name, *older], [g, *([chains[f"f{above}"][0]] if layer < last else [])])
        gb1, dq, dkv_own, dkv_give, stats = run(
            self_back_kernel,
            "self_attention_back",
            info,
            dict(
                g=g, branch=k["branch1"], q=k["q"], kv_own=k["kv"], kv_sib=k["kv_sib"], lse=k["lse1"]
            ),
            dict(mod=mod, early=(stats, ())),
            weights_of(first),
            dict(gb=frame_low, dq=frame_low, dkv_own=two_low, dkv_give=two_low),
            dict(stats=stat_shape),
            dict(wo=whole, d_mixed=lows, sems=sems(4)),
            held(f_name, c_name, *older),
            13.0,
        )
        dkv_sib = tensor_hop(dkv_give, 1)
        advance([f_name, c_name, *older], [dq, *([chains[f"c{above}"][0]] if layer < last else [])])
        send, keep = run(
            query_output_kernel,
            "query_output_grads",
            info,
            dict(entry=k["entry1"], gb=gb1, dq=dq, mixed=k["mixed1"]),
            {},
            [],
            grads_out(2),
            {},
            {},
            held(f_name, c_name),
            15.0,
        )
        start(a_name, send, keep)
        arriving = dict(dkv_own=dkv_own, dkv_sib=dkv_sib, entry=k["entry1"])
        if layer == 0:
            send, keep, dkv = run(
                kv_grads_kernel,
                "keys_values_grads",
                info,
                arriving,
                {},
                [],
                grads_out(2) | dict(dkv=two_low),
                {},
                {},
                held(a_name),
                4.0,
            )
            start(s_name, send, keep)
            advance([a_name], held(s_name) + [chains[n_name][0]])
            arriving = dict(dkv=dkv)
        results = run(
            qkv_back_kernel,
            "self_qkv_back",
            info,
            arriving | dict(dq=dq, x=k["x"], g=g),
            dict(mod=mod, early=(stats, ())),
            weights_of(first),
            (dict(low=frame_low) if layer == 0 else grads_out(2)) | dict(out=frame_high),
            dict(stats=stat_shape),
            dict(wq=whole, wk=whole, wv=whole, de=floats, sems=sems(12))
            | (dict(dkv=pltpu.VMEM(two_low.shape, BF)) if layer else {}),
            held(a_name, c_name),
            6.0,
        )
        g, stats = results[-2:]
        if layer:
            start(s_name, *results[:2])
        rest = [a_name, s_name] if layer == 0 else [(f"n{layer}", [a_name, s_name])]
        advance([f_name, c_name, *rest], [g])
        sums = [stats, tensor_hop(stats, 1)] + sums
    input_grad = join(results[0])
    second = held("s0")
    while any(2 ** chain[2] < size for chain in chains.values()):
        last_hops = [chains["f0"][0]] if second[0] is chains["s0"][1] else []
        advance(list(chains), held("s0") + last_hops)
        if last_hops:
            third = held("s0")

    vectors = plain(
        partial(collect_kernel, narrow=narrow, units=units, columns=columns),
        "collect_sums",
        info,
        [*sums, condition],
        [shape(16, mine.shape[2], dtype=BF)],
        [pltpu.VMEM(stat_shape.shape, F32), pltpu.VMEM((16, mine.shape[2]), F32)],
        second,
    )
    gathered = vectors[None]
    hop = size // 2
    while hop:
        other = dp_hop(gathered, hop)
        if hop == size // 2:
            (other,) = gate([other], third)
        both = jnp.stack([gathered, other], axis=1)
        gathered = both.reshape(-1, *vectors.shape)
        hop //= 2

    def parts_of(*names):
        return [part.reshape(1, unit, -1) for name in names for part in chains[name][:2]]

    up_grad, down_grad = plain(
        partial(finish_kernel, wide=True, spots=[[(layer, 0)] for layer in range(LAYERS)]),
        "finish_wide",
        None,
        parts_of(*[f"f{layer}" for layer in range(LAYERS)]),
        [shape(LAYERS, unit, units)] * 2,
        after=held("s0"),
    )
    straight, across = shape(LAYERS, unit, narrow), shape(LAYERS, narrow, unit)
    lasts = [[(1, 0), (1, 1)], [(1, 2), (1, 3)]]
    cq_grad, ck_grad, cv_grad, co_grad, q_grad, o_grad, k_grad, v_grad = plain(
        partial(finish_kernel, wide=False, spots=lasts + [[(0, 0), (0, 1)], [(0, 2)], [(0, 3)]]),
        "finish_narrow",
        None,
        parts_of("c1", "n1", "c0", "a0", "s0"),
        [straight, straight, straight, across, straight, across, straight, straight],
    )
    small = plain(
        spread_kernel,
        "spread_sums",
        info,
        [gathered],
        [shape(LAYERS, unit, columns), shape(LAYERS, columns)]
        + [shape(LAYERS, narrow)] * 4
        + [shape(LAYERS, units)]
        + [shape(LAYERS, unit)] * 3,
        [pltpu.VMEM((SLOTS * size, columns), F32), pltpu.VMEM((SLOTS * size, width), F32)],
    )
    mod_grad, mod_bias_grad, q_sum, v_sum, cq_sum, cv_sum, up_sum, o1, o2, o3 = small
    return (
        output,
        input_grad,
        q_grad,
        q_sum,
        k_grad,
        v_grad,
        v_sum,
        o_grad,
        o1,
        cq_grad,
        cq_sum,
        ck_grad,
        cv_grad,
        cv_sum,
        co_grad,
        o2,
        up_grad,
        up_sum,
        turn(down_grad),
        o3,
        mod_grad,
        mod_bias_grad,
    )


def solution(mesh):
    dp, tensor = "dp", "tensor"
    columns, vector = P(None, None, tensor), P(None, tensor)
    matrix, turned, spread = P(None, dp, tensor), P(None, tensor, dp), P(None, dp)
    placed = (
        P(dp, None),
        P(dp, None, None),
        P(dp),
        P(dp),
        P(dp, None),
        columns,
        vector,
        columns,
        columns,
        vector,
        P(None, tensor, None),
        P(),
        columns,
        vector,
        columns,
        columns,
        vector,
        P(None, tensor, None),
        P(),
        columns,
        vector,
        P(None, tensor, None),
        P(),
        columns,
        vector,
    )
    results = (
        P(dp, None),
        P(dp, None),
        matrix,
        vector,
        matrix,
        matrix,
        vector,
        turned,
        spread,
        matrix,
        vector,
        matrix,
        matrix,
        vector,
        turned,
        spread,
        matrix,
        vector,
        turned,
        spread,
        matrix,
        vector,
    )
    return jax.shard_map(
        shards, mesh=mesh, in_specs=placed, out_specs=results, check_vma=False
    )
```

```python
from functools import partial
import math

import jax
import jax.numpy as jnp
from jax import lax
from jax.experimental import pallas as pl
from jax.experimental.pallas import tpu as pltpu
from jax.sharding import PartitionSpec as P

HEAD_WIDTH = 64
UNIT = 256
LAYERS = 2
WINDOW = 1024
EPSILON = 1e-06
LANES = 128
CHUNK = 64
SLOTS = WINDOW // UNIT
FAR = -1e30
VMEM_BYTES = 62 * 1024 * 1024
BF = jnp.bfloat16
F32 = jnp.float32
ROOT = math.sqrt(2.0 / math.pi)
CUBIC = 0.044715


def dot_nn(left, right):
    return jnp.dot(left, right, preferred_element_type=F32)


def dot_nt(left, right):
    return lax.dot_general(left, right, (((1,), (1,)), ((), ())), preferred_element_type=F32)


def dot_tn(left, right):
    return lax.dot_general(left, right, (((0,), (0,)), ((), ())), preferred_element_type=F32)


SMALL = pl.BlockSpec(memory_space=pltpu.SMEM)
NEAR = pl.BlockSpec(memory_space=pltpu.VMEM)
ANY = pl.BlockSpec(memory_space=pl.ANY)


class Work:
    def __init__(self, ins, outs, scratch, in_sems, out_sems):
        self.ins, self.outs, self.scratch, self.out_sems = ins, outs, scratch, out_sems
        self.copies, self.waited, self.flushed = {}, set(), []
        for index, (name, (ref, buffer)) in enumerate(ins.items()):
            self.copies[name] = pltpu.make_async_copy(ref, buffer, in_sems.at[index])
            self.copies[name].start()

    def __getattr__(self, name):
        if name in self.__dict__["ins"]:
            return self.ins[name][1]
        if name in self.__dict__["outs"]:
            return self.outs[name][1]
        return self.__dict__["scratch"][name]

    def has(self, name):
        return name in self.outs

    def takes(self, name):
        return name in self.ins

    def send(self, name, source, *at):
        ref = self.outs[name][0]
        copy = pltpu.make_async_copy(
            source, ref.at[at] if at else ref, self.out_sems.at[len(self.flushed)]
        )
        copy.start()
        self.flushed.append(copy)

    def need(self, *names):
        for name in names:
            if name not in self.waited:
                self.waited.add(name)
                self.copies[name].wait()

    def flush(self, name, *at):
        ref, buffer = self.outs[name]
        if at:
            ref, buffer = ref.at[at], buffer.at[at]
        copy = pltpu.make_async_copy(buffer, ref, self.out_sems.at[len(self.flushed)])
        copy.start()
        self.flushed.append(copy)

    def finish(self):
        self.need(*self.ins)
        for copy in self.flushed:
            copy.wait()


def run(body, name, info, ins, small, weights, outs, small_outs, scratch, after=(), cost=1.0):
    in_names, out_names, names = list(ins), list(outs), list(scratch)
    small_names, small_out_names = list(small), list(small_outs)
    counts = [1, len(in_names), len(small), len(weights), len(after), len(outs), len(small_outs)]

    def kernel(*refs):
        refs = list(refs)
        parts = []
        for count in counts:
            parts.append(refs[:count])
            refs = refs[count:]
        (info_ref,), in_refs, small_refs, weight_refs, _, out_refs, small_out_refs = parts
        in_bufs, refs = refs[: len(in_names)], refs[len(in_names) :]
        out_bufs, refs = refs[: len(out_names)], refs[len(out_names) :]
        rest, (in_sems, out_sems) = refs[:-2], refs[-2:]
        extra = {}
        rest = list(rest)
        for key in names:
            many = isinstance(scratch[key], list)
            size = len(scratch[key]) if many else 1
            extra[key] = rest[:size] if many else rest[0]
            rest = rest[size:]
        for key, ref in zip(small_names, small_refs):
            index = small[key][1]
            extra[key] = ref.at[index] if index else ref
        extra.update(zip(small_out_names, small_out_refs))
        work = Work(
            dict(zip(in_names, zip(in_refs, in_bufs))),
            dict(zip(out_names, zip(out_refs, out_bufs))),
            extra,
            in_sems,
            out_sems,
        )
        body(info_ref, work, weight_refs)
        work.finish()

    buffer = lambda a: pltpu.VMEM(a.shape, a.dtype)
    flat = []
    for value in scratch.values():
        flat += value if isinstance(value, list) else [value]
    results = pl.pallas_call(
        kernel,
        out_shape=[outs[n] for n in out_names] + [small_outs[n] for n in small_out_names],
        in_specs=[SMALL]
        + [ANY] * len(ins)
        + [NEAR] * len(small)
        + [ANY] * (len(weights) + len(after)),
        out_specs=[ANY] * len(outs) + [NEAR] * len(small_outs),
        scratch_shapes=[buffer(ins[n]) for n in in_names]
        + [buffer(outs[n]) for n in out_names]
        + flat
        + [pltpu.SemaphoreType.DMA((max(len(ins), 1),)), pltpu.SemaphoreType.DMA((32,))],
        compiler_params=pltpu.CompilerParams(vmem_limit_bytes=VMEM_BYTES),
        cost_estimate=lasting(cost),
        name=name,
    )(info, *ins.values(), *[array for array, _ in small.values()], *weights, *after)
    return results


def plain(body, name, info, ins, outs, scratch=(), after=()):
    first = len(ins) + (0 if info is None else 1)
    results = pl.pallas_call(
        lambda *refs: body(*refs[:first], *refs[first + len(after) :]),
        out_shape=outs,
        in_specs=([] if info is None else [SMALL]) + [NEAR] * len(ins) + [ANY] * len(after),
        out_specs=[NEAR] * len(outs),
        scratch_shapes=list(scratch),
        compiler_params=pltpu.CompilerParams(vmem_limit_bytes=VMEM_BYTES),
        cost_estimate=lasting(1.0),
        name=name,
    )(*([] if info is None else [info]), *ins, *after)
    return results if len(outs) > 1 else results[0]


def lasting(units):
    return pl.CostEstimate(flops=int(units * 0.4e9), bytes_accessed=1000, transcendentals=0)


def shape(*dims, dtype=F32):
    return jax.ShapeDtypeStruct(dims, dtype)


def start_rows(refs, place, plan, sems):
    own, sib, xa, ya, xb, yb = refs
    half = own.shape[0] // 2
    for rank in range(4):
        for parity in range(2):

            @pl.when(place == rank * 2 + parity)
            def _(rank=rank, parity=parity):
                for index, (shard, row, rows, dst) in enumerate(plan):
                    step = shard ^ rank
                    if step < 2:
                        src = (own, sib)[step].at[pl.ds(row, rows)]
                    else:
                        first, second = ((xa, ya), (xb, yb))[step - 2]
                        part = row // half
                        src = (first if part == parity else second).at[pl.ds(row - part * half, rows)]
                    pltpu.make_async_copy(src, dst, sems.at[index]).start()


def wait_rows(refs, plan, sems, which):
    for index in which:
        _, row, rows, dst = plan[index]
        pltpu.make_async_copy(refs[0].at[pl.ds(0, rows)], dst, sems.at[index]).wait()


def plan_of(buffers, first, rows):
    return [
        (shard, (first + which) * rows, rows, dst.at[pl.ds(shard * rows, rows)])
        for which, dst in enumerate(buffers)
        for shard in range(4)
    ]


def norm_rows(values):
    mean = jnp.mean(values, axis=-1, keepdims=True)
    center = values - mean
    factor = lax.rsqrt(jnp.mean(center * center, axis=-1, keepdims=True) + EPSILON)
    return center * factor, factor


def piece(mod, slot, index):
    width = mod.shape[1] // 9
    return mod[pl.ds(slot, 1), index * width : (index + 1) * width]


def entry_rows(x, mod, info, index, out):
    for block in range(x.shape[0] // UNIT):
        slot = info[1 + block]
        shift = piece(mod, slot, index)
        scale = 1.0 + piece(mod, slot, index + 1)

        def step(turn, carry):
            rows = pl.ds(pl.multiple_of(block * UNIT + turn * CHUNK, CHUNK), CHUNK)
            normed, _ = norm_rows(x[rows, :])
            out[rows, :] = (normed * scale + shift).astype(BF)
            return carry

        lax.fori_loop(0, UNIT // CHUNK, step, 0, unroll=True)


def residual_rows(x, mod, info, index, branch, branch_out, out, low=None):
    for block in range(x.shape[0] // UNIT):
        gate = piece(mod, info[1 + block], index)

        def step(turn, carry):
            rows = pl.ds(pl.multiple_of(block * UNIT + turn * CHUNK, CHUNK), CHUNK)
            values = branch[rows, :]
            branch_out[rows, :] = values.astype(BF)
            result = x[rows, :] + gate * values
            out[rows, :] = result
            if low is not None:
                low[rows, :] = result.astype(BF)
            return carry

        lax.fori_loop(0, UNIT // CHUNK, step, 0, unroll=True)


def fold(values):
    return jnp.sum(values.reshape(values.shape[0] // 8, 8, values.shape[1]), axis=0)


def total(values):
    return jnp.sum(values, axis=0, keepdims=True)


def gate_back(g, mod, info, index, branch, gb, stats):
    width = g.shape[1]
    sums = jnp.zeros((8, width), F32)
    for block in range(g.shape[0] // UNIT):
        slot = info[1 + block]
        gate = piece(mod, slot, index)

        def step(turn, carry):
            rows = pl.ds(pl.multiple_of(block * UNIT + turn * CHUNK, CHUNK), CHUNK)
            grad = g[rows, :]
            low = (gate * grad).astype(BF)
            gb[rows, :] = low
            return (
                carry[0] + fold(low.astype(F32)),
                carry[1] + fold(grad * branch[rows, :].astype(F32)),
            )

        sums, rows_sum = lax.fori_loop(
            0, UNIT // CHUNK, step, (sums, jnp.zeros((8, width), F32)), unroll=True
        )
        stats[pl.ds(8 + slot, 1), :] += total(rows_sum)
    stats[12:13, :] = total(sums)


def norm_back_rows(x, g, de, mod, info, index, out, stats, low=None):
    width = x.shape[1]
    for block in range(x.shape[0] // UNIT):
        slot = info[1 + block]
        scale = 1.0 + piece(mod, slot, index + 1)

        def step(turn, carry):
            rows = pl.ds(pl.multiple_of(block * UNIT + turn * CHUNK, CHUNK), CHUNK)
            normed, factor = norm_rows(x[rows, :])
            grad = de[rows, :]
            inner = grad * normed
            dn = grad * scale
            mean = jnp.mean(dn, axis=-1, keepdims=True)
            along = jnp.mean(dn * normed, axis=-1, keepdims=True)
            result = g[rows, :] + factor * (dn - mean - normed * along)
            out[rows, :] = result
            if low is not None:
                low[rows, :] = result.astype(BF)
            return (carry[0] + fold(grad), carry[1] + fold(inner))

        zero = jnp.zeros((8, width), F32)
        shift_sum, scale_sum = lax.fori_loop(0, UNIT // CHUNK, step, (zero, zero), unroll=True)
        stats[pl.ds(slot, 1), :] += total(shift_sum)
        stats[pl.ds(4 + slot, 1), :] += total(scale_sum)


def lane_ids(rows):
    return lax.broadcasted_iota(jnp.int32, (rows, LANES), 1)


def head_half(values, half):
    ids = lane_ids(values.shape[0])
    keep = ids < HEAD_WIDTH if half == 0 else ids >= HEAD_WIDTH
    return jnp.where(keep, values.astype(F32), 0.0)


def turned_halves(keys):
    turned = keys.T
    low = lax.broadcasted_iota(jnp.int32, turned.shape, 0) < HEAD_WIDTH
    zero = jnp.zeros(turned.shape, turned.dtype)
    return jnp.concatenate([jnp.where(low, turned, zero), jnp.where(low, zero, turned)], axis=1)


def query_marks(slot):
    return jnp.where(lane_ids(UNIT) == slot, 1.0, 0.0).astype(BF)


def key_marks(slots):
    ids = lane_ids(UNIT)
    parts = [jnp.where((ids < SLOTS) & (ids != slot), FAR, 0.0).astype(BF) for slot in slots]
    return jnp.concatenate(parts, axis=0)


def pair_lanes(pair):
    return pl.ds(pl.multiple_of(pair * LANES, LANES), LANES)


def kv_kernel(info, work, weights):
    rows = weights[0].shape[0] // 4
    plan = plan_of((work.w.at[0], work.w.at[1]), 1, rows)
    start_rows(weights, info[0], plan, work.sems)
    if work.has("branch"):
        work.need("part", "other", "below")
        bias = work.bias[...].astype(F32)
        for row in range(0, work.sum.shape[0], CHUNK):
            span = pl.ds(row, CHUNK)
            work.sum[span, :] = (
                work.part[span, :].astype(F32) + work.other[span, :].astype(F32) + bias
            )
        residual_rows(work.below, work.mod_below, info, 8, work.sum, work.branch, work.x)
        work.flush("branch")
        work.flush("x")
    else:
        work.need("x")
    entry_rows(work.x, work.mod, info, 0, work.entry)
    work.flush("entry")
    entry = work.entry[...]
    wait_rows(weights, plan, work.sems, range(4))
    work.kv[0] = dot_nt(entry, work.w[0]).astype(BF)
    work.flush("kv", 0)
    wait_rows(weights, plan, work.sems, range(4, 8))
    work.kv[1] = (dot_nt(entry, work.w[1]) + work.biases[2:3, :]).astype(BF)
    work.flush("kv", 1)


def q_kernel(info, work, weights):
    rows = weights[0].shape[0] // 4
    plan = plan_of((work.w,), 0, rows)
    start_rows(weights, info[0], plan, work.sems)
    work.need("entry")
    wait_rows(weights, plan, work.sems, range(4))
    work.q[...] = (dot_nt(work.entry[...], work.w[...]) + work.biases[0:1, :]).astype(BF)
    work.flush("q")


def soft_pair(work, q_pair, keys, values, marks, logs, pair, span, words=None):
    ids = lane_ids(UNIT)
    results = []
    kept = logs[span, :]
    for half in range(2):
        left = (head_half(q_pair, half) * HEAD_WIDTH**-0.5).astype(BF)
        if marks is not None:
            left = jnp.concatenate([left, marks], axis=1)
        scores = dot_nt(left, keys)
        if words is not None:
            scores = jnp.where(ids < words, scores, FAR)
        peak = jnp.max(scores, axis=-1, keepdims=True)
        both = dot_nn(jnp.exp(scores - peak).astype(BF), values)
        sums = both[:, LANES:]
        results.append(both[:, :LANES] / sums)
        kept = jnp.where(ids == 2 * pair + half, peak + jnp.log(sums), kept)
    logs[span, :] = kept
    return jnp.where(ids < HEAD_WIDTH, results[0], results[1])


def self_kernel(info, work, weights):
    rows = weights[0].shape[0] // 4
    sems = work.sems
    plan = [(s, 3 * rows, rows, work.wo.at[pl.ds(s * rows, rows)]) for s in range(4)]
    start_rows(weights, info[0], plan, sems)
    share = work.x.shape[0]
    blocks = share // UNIT
    marks = key_marks([info[1 + b] for b in range(2 * blocks)])
    ones = jnp.ones((2 * share, LANES), BF)
    logs, mixed = work.logs, work.mixed
    logs[...] = jnp.zeros(logs.shape, F32)
    work.need("q", "kv_own", "kv_sib")

    def both(which, lanes):
        return jnp.concatenate([work.kv_own[which, :, lanes], work.kv_sib[which, :, lanes]], axis=0)

    def step(pair, carry):
        lanes = pair_lanes(pair)
        keys = jnp.concatenate([both(0, lanes), marks], axis=1)
        values = jnp.concatenate([both(1, lanes), ones], axis=1)
        for block in range(blocks):
            span = pl.ds(block * UNIT, UNIT)
            values_mixed = soft_pair(
                work,
                work.q[span, lanes],
                keys,
                values,
                query_marks(info[1 + block]),
                logs,
                pair,
                span,
            )
            low = values_mixed.astype(BF)
            mixed[span, lanes] = low
            work.rest[span, lanes] = (values_mixed - low.astype(F32)).astype(BF)
        return carry

    lax.fori_loop(0, mixed.shape[1] // LANES, step, 0)
    work.flush("mixed")
    work.flush("rest")
    work.lse[...] = logs[...].T[: work.lse.shape[0], :]
    work.flush("lse")
    wait_rows(weights, plan, sems, range(4))
    work.sum[...] = dot_nn(mixed[...], work.wo[...]) + work.bias[...].astype(F32)
    work.need("x")
    residual_rows(work.x, work.mod, info, 2, work.sum, work.branch, work.out)
    work.flush("branch")
    work.flush("out")


def cross_kernel(info, work, weights, words):
    rows = weights[0].shape[0] // 4
    sems = work.sems
    order = (1, 2, 0, 3)
    plan = [
        (shard, order[i // 4] * rows, count, dst)
        for i, (shard, _, count, dst) in enumerate(
            plan_of((work.wk, work.wv, work.wq, work.wo), 0, rows)
        )
    ]
    start_rows(weights, info[0], plan, sems)
    work.need("x")
    entry_rows(work.x, work.mod, info, 3, work.entry)
    work.flush("entry")
    work.need("text")
    wait_rows(weights, plan, sems, range(0, 4))
    work.kv[0] = dot_nt(work.text[...], work.wk[...]).astype(BF)
    wait_rows(weights, plan, sems, range(4, 8))
    work.kv[1] = (dot_nt(work.text[...], work.wv[...]) + work.biases[5:6, :]).astype(BF)
    work.flush("kv")
    wait_rows(weights, plan, sems, range(8, 12))
    work.q[...] = (dot_nt(work.entry[...], work.wq[...]) + work.biases[3:4, :]).astype(BF)
    work.flush("q")
    ones = jnp.ones((LANES, LANES), BF)
    logs, mixed = work.logs, work.mixed
    logs[...] = jnp.zeros(logs.shape, F32)

    def step(pair, carry):
        lanes = pair_lanes(pair)
        for block in range(mixed.shape[0] // UNIT):
            span = pl.ds(block * UNIT, UNIT)
            own = pl.ds(pl.multiple_of(info[1 + block] * LANES, LANES), LANES)
            mixed[span, lanes] = soft_pair(
                work,
                work.q[span, lanes],
                work.kv[0, own, lanes],
                jnp.concatenate([work.kv[1, own, lanes], ones], axis=1),
                None,
                logs,
                pair,
                span,
                words,
            ).astype(BF)
        return carry

    lax.fori_loop(0, mixed.shape[1] // LANES, step, 0, unroll=2)
    work.flush("mixed")
    work.lse[...] = logs[...].T[: work.lse.shape[0], :]
    work.flush("lse")
    wait_rows(weights, plan, sems, range(12, 16))
    work.sum[...] = dot_nn(mixed[...], work.wo[...]) + work.bias[...].astype(F32)
    residual_rows(work.x, work.mod, info, 5, work.sum, work.branch, work.out)
    work.flush("branch")
    work.flush("out")


def hidden_plan(refs, buffer):
    rows = buffer.shape[1]
    half = rows // 2
    return [
        (shard, row, half, buffer.at[shard, pl.ds(row, half)])
        for shard in range(4)
        for row in range(0, rows, half)
    ]


def start_chip(info, refs, layer, buffer, sems):
    copies = [
        pltpu.make_async_copy(ref.at[layer], buffer.at[(info[5] + i) % 2], sems.at[i])
        for i, ref in enumerate(refs)
    ]
    for copy in copies:
        copy.start()
    return copies


def bend_rows(before, bias, active, slope, lanes):
    for row in range(0, before.shape[0], CHUNK):
        span = pl.ds(row, CHUNK)
        values = before[span, :] + bias
        square = values * values
        half = 1.0 / (1.0 + jnp.exp(values * (-2.0 * ROOT - (2.0 * ROOT * CUBIC) * square)))
        act = values * half
        active[span, lanes] = act.astype(BF)
        slope[span, lanes] = (
            half + act * (1.0 - half) * (2.0 * ROOT + (6.0 * ROOT * CUBIC) * square)
        ).astype(BF)


def columns_of(shard, width):
    return pl.ds(pl.multiple_of(shard * width, width), width)


def start_hidden(info, work, weights, layer):
    if len(weights) == 4:
        ups = start_chip(info, weights[:2], layer, work.up, work.sems)
        downs = start_chip(info, weights[2:], layer, work.down, work.down_sems)
        return [lambda some=some: [copy.wait() for copy in some] for some in (ups, downs)]
    waits = []
    for refs, buffer, sems in (
        (weights[:6], work.up, work.sems),
        (weights[6:12], work.down, work.down_sems),
    ):
        refs = [ref.at[layer] for ref in refs[:2]] + list(refs[2:])
        plan = hidden_plan(refs, buffer)
        start_rows(refs, info[0], plan, sems)
        waits.append(
            lambda refs=refs, plan=plan, sems=sems: wait_rows(refs, plan, sems, range(len(plan)))
        )
    return waits


def hidden_kernel(info, work, weights, layer):
    waits = start_hidden(info, work, weights, layer)
    width = work.x.shape[1]
    shards = work.up.shape[0]
    first = info[6] * 2 if shards == 2 else 0
    work.need("x")
    entry_rows(work.x, work.mod, info, 6, work.entry)
    work.flush("entry")
    for wait in waits:
        wait()
    start = 0.0 if shards == 2 else work.bias[...].astype(F32)
    work.sum[...] = jnp.zeros(work.sum.shape, F32) + start

    def step(shard, carry):
        lanes = columns_of(shard, width)
        bias = work.up_bias[:, columns_of(first + shard, width)]
        work.before[...] = dot_nn(work.entry[...], work.up[shard])
        bend_rows(work.before, bias, work.active, work.slope, lanes)
        work.sum[...] += dot_nn(work.active[:, lanes], work.down[shard])
        return carry

    lax.fori_loop(0, shards, step, 0)
    work.flush("active")
    work.flush("slope")
    if shards == 2:
        work.part[...] = work.sum[...].astype(BF)
        work.flush("part")
        return
    low = work.low if work.has("low") else None
    residual_rows(work.x, work.mod, info, 8, work.sum, work.branch, work.out, low)
    work.flush("branch")
    work.flush("out")
    if low is not None:
        work.flush("low")


def hidden_back_kernel(info, work, weights, layer):
    waits = start_hidden(info, work, weights, layer)
    width = work.g.shape[1]
    shards = work.up.shape[0]
    if shards == 4:
        actives = [
            pltpu.make_async_copy(
                weights[12].at[:, columns_of(rank, width)], work.acts.at[i], work.act_sems.at[i]
            )
            for i, rank in enumerate((info[7], info[5]))
        ]
        for copy in actives:
            copy.start()
    work.stats[...] = jnp.zeros(work.stats.shape, F32)
    stats = work.stats.at[pl.ds(48, 24)]
    work.need("g", "branch")
    gate_back(work.g, work.mod, info, 8, work.branch, work.gb, stats)
    work.need("slope")
    for wait in waits:
        wait()
    work.de[...] = jnp.zeros(work.de.shape, F32)
    first = info[6] * 2 if shards == 2 else 0

    def step(shard, carry):
        lanes = columns_of(shard, width)
        work.before[...] = dot_nt(work.gb[...], work.down[shard])
        sums = jnp.zeros((8, width), F32)
        for row in range(0, work.g.shape[0], CHUNK):
            span = pl.ds(row, CHUNK)
            low = (work.before[span, :] * work.slope[span, lanes].astype(F32)).astype(BF)
            work.d_before[span, lanes] = low
            sums += fold(low.astype(F32))
        stats[pl.ds(13 + first + shard, 1), :] = total(sums)
        work.de[...] += dot_nt(work.d_before[:, lanes], work.up[shard])
        return carry

    lax.fori_loop(0, shards, step, 0)
    if shards == 2:
        work.part[...] = work.de[...].astype(BF)
        work.flush("part")
        work.flush("gb")
        work.flush("d_before")
        return
    work.need("entry")
    left, right = work.entry[...].T, work.gb[...].T
    for name, index, rank in (("send", 0, info[7]), ("keep", 1, info[5])):
        out = work.outs[name][1]
        out[:, :width] = dot_nn(left, work.d_before[:, columns_of(rank, width)]).astype(BF)
        actives[index].wait()
        out[:, width:] = dot_nn(right, work.acts[index]).astype(BF)
        work.flush(name)
    work.need("x")
    norm_back_rows(work.x, work.g, work.de, work.mod, info, 6, work.out, stats)
    work.flush("out")


def hidden_grads_kernel(info, work, weights):
    width = work.entry.shape[1]
    work.need("entry", "d_before", "gb", "active")
    left, right = work.entry[...].T, work.gb[...].T
    for name, shift in (("send", 1), ("keep", 0)):
        out = work.outs[name][1]
        lanes = columns_of((info[5] + shift) % 2, width)
        out[:, :width] = dot_nn(left, work.d_before[:, lanes]).astype(BF)
        out[:, width:] = dot_nn(right, work.active[:, lanes]).astype(BF)
        work.flush(name)


def pair_grads(info, work, members):
    rows = members[0][0].shape[0]
    low = lane_ids(rows) < HEAD_WIDTH
    step = 3 * LANES
    for at in range(len(members) // 2):
        products = [dot_nn(left, right) for left, right in members[2 * at : 2 * at + 2]]
        (a0, a1, a2), (b0, b1, b2) = [
            [p[:, i * LANES : (i + 1) * LANES] for i in range(3)] for p in products
        ]
        even = (a0, b0, jnp.where(low, a1, pltpu.roll(b1, HEAD_WIDTH, 1)))
        a1, b1 = pltpu.roll(a1, HEAD_WIDTH, 1), pltpu.roll(b1, HEAD_WIDTH, 1)
        a2r, b2r = pltpu.roll(a2, HEAD_WIDTH, 1), pltpu.roll(b2, HEAD_WIDTH, 1)
        odd = (jnp.where(low, a1, a2r), jnp.where(low, b1, b2r), jnp.where(low, a2r, b2))
        first = info[5] % 2 == 0
        for i, (mine, other) in enumerate(zip(even, odd)):
            lanes = pl.ds(at * step + i * LANES, LANES)
            work.outs["keep"][1][:, lanes] = jnp.where(first, mine, other).astype(BF)
            work.outs["send"][1][:, lanes] = jnp.where(first, other, mine).astype(BF)
    work.flush("send")
    work.flush("keep")


def chip_lanes(info, width):
    return pl.ds(pl.multiple_of(info[6] * (width // 2), width // 2), width // 2)


def query_output_kernel(info, work, weights):
    work.need("entry", "gb", "dq", "mixed")
    lanes = chip_lanes(info, work.dq.shape[1])
    pair_grads(
        info,
        work,
        [
            (work.entry[...].T, work.dq[:, lanes]),
            (work.gb[...].T, work.mixed[:, lanes]),
        ],
    )


def cross_back_kernel(info, work, weights, words):
    rows = weights[0].shape[0] // 4
    sems = work.sems
    plan = [
        (shard, (3 * rows, 0)[i // 4], count, dst)
        for i, (shard, _, count, dst) in enumerate(plan_of((work.wo, work.wq), 0, rows))
    ]
    start_rows(weights, info[0], plan, sems)
    work.stats[...] = work.early[...]
    stats = work.stats.at[pl.ds(24, 24)]
    g = work.g
    work.need("g")
    if work.takes("part"):
        work.need("part", "other", "above")
        for row in range(0, g.shape[0], CHUNK):
            span = pl.ds(row, CHUNK)
            work.de[span, :] = work.part[span, :].astype(F32) + work.other[span, :].astype(F32)
        g = work.g_mid
        norm_back_rows(
            work.above, work.g, work.de, work.mod, info, 6, g, work.stats.at[pl.ds(48, 24)]
        )
    work.need("branch")
    gate_back(g, work.mod, info, 5, work.branch, work.gb, stats)
    wait_rows(weights, plan, sems, range(0, 4))
    work.d_mixed[...] = dot_nt(work.gb[...], work.wo[...]).astype(BF)
    work.dkv_sum[...] = jnp.zeros(work.dkv_sum.shape, F32)
    real = lax.broadcasted_iota(jnp.int32, (LANES, UNIT), 0) < words
    work.need("q", "kv", "lse")

    def step(pair, carry):
        lanes = pair_lanes(pair)
        for block in range(work.q.shape[0] // UNIT):
            span = pl.ds(block * UNIT, UNIT)
            own = pl.ds(pl.multiple_of(info[1 + block] * LANES, LANES), LANES)
            q_pair = work.q[span, lanes]
            d_pair = work.d_mixed[span, lanes]
            keys = work.kv[0, own, lanes]
            values = work.kv[1, own, lanes]
            lefts, grads, probs_low, scores_low = [], [], [], []
            for half in range(2):
                left = (head_half(q_pair, half) * HEAD_WIDTH**-0.5).astype(BF)
                grad = head_half(d_pair, half).astype(BF)
                logs = work.lse[pl.ds(2 * pair + half, 1), span]
                probs = jnp.where(real, jnp.exp(dot_nt(keys, left) - logs), 0.0)
                d_probs = dot_nt(values, grad)
                inner = jnp.sum(probs * d_probs, axis=0, keepdims=True)
                lefts.append(left)
                grads.append(grad)
                probs_low.append(probs.astype(BF))
                scores_low.append((probs * (d_probs - inner)).astype(BF))
            wide_scores = jnp.concatenate(scores_low, axis=1)
            grad_v = dot_nn(jnp.concatenate(probs_low, axis=1), jnp.concatenate(grads, axis=0))
            grad_k = dot_nn(wide_scores, jnp.concatenate(lefts, axis=0))
            grad_q = dot_nn(turned_halves(keys), jnp.concatenate(scores_low, axis=0))
            work.dq[span, lanes] = (grad_q.T * HEAD_WIDTH**-0.5).astype(BF)
            work.dkv_sum[0, own, lanes] += grad_k
            work.dkv_sum[1, own, lanes] += grad_v
        return carry

    lax.fori_loop(0, work.q.shape[1] // LANES, step, 0, unroll=2)
    work.dkv[...] = work.dkv_sum[...].astype(BF)
    work.need("entry", "text", "mixed")
    lanes = chip_lanes(info, work.dq.shape[1])
    text = work.text[...].T
    pair_grads(
        info,
        work,
        [
            (work.entry[...].T, work.dq[:, lanes]),
            (text, work.dkv[0, :, lanes]),
            (text, work.dkv[1, :, lanes]),
            (work.gb[...].T, work.mixed[:, lanes]),
        ],
    )
    stats[13:14, :] = total(fold(work.dq[...].astype(F32)))
    stats[14:15, :] = total(fold(work.dkv[1].astype(F32)))
    wait_rows(weights, plan, sems, range(4, 8))
    work.de[...] = dot_nn(work.dq[...], work.wq[...])
    work.need("x")
    norm_back_rows(work.x, g, work.de, work.mod, info, 3, work.out, stats)
    work.flush("out")


def self_back_kernel(info, work, weights):
    rows = weights[0].shape[0] // 4
    sems = work.sems
    plan = [(s, 3 * rows, rows, work.wo.at[pl.ds(s * rows, rows)]) for s in range(4)]
    start_rows(weights, info[0], plan, sems)
    work.stats[...] = work.early[...]
    stats = work.stats.at[pl.ds(0, 24)]
    work.need("g", "branch")
    gate_back(work.g, work.mod, info, 2, work.branch, work.gb, stats)
    work.flush("gb")
    share = work.g.shape[0]
    blocks = share // UNIT
    marks = key_marks([info[1 + b] for b in range(2 * blocks)])
    wait_rows(weights, plan, sems, range(4))
    work.d_mixed[...] = dot_nt(work.gb[...], work.wo[...]).astype(BF)
    work.need("mixed", "rest", "q", "kv_own", "kv_sib", "lse")
    width = work.q.shape[1]
    head = lax.broadcasted_iota(jnp.int32, (16, width), 0)
    lane = lax.broadcasted_iota(jnp.int32, (16, width), 1)
    first = head * HEAD_WIDTH
    pick = jnp.where((lane >= first) & (lane < first + HEAD_WIDTH), 1.0, 0.0)
    for block in range(blocks):
        span = pl.ds(block * UNIT, UNIT)
        whole = work.mixed[span, :].astype(F32) + work.rest[span, :].astype(F32)
        work.inner[:, span] = lax.dot_general(
            pick,
            whole * work.d_mixed[span, :].astype(F32),
            (((1,), (1,)), ((), ())),
            precision=lax.Precision.HIGHEST,
            preferred_element_type=F32,
        )

    def both(which, lanes):
        return jnp.concatenate([work.kv_own[which, :, lanes], work.kv_sib[which, :, lanes]], axis=0)

    def step(pair, carry):
        lanes = pair_lanes(pair)
        keys = both(0, lanes)
        values = both(1, lanes)
        marked = jnp.concatenate([keys, marks], axis=1)
        turned = turned_halves(keys)
        lefts, grads, probs_low, scores_low = [], [], [], []
        for block in range(blocks):
            span = pl.ds(block * UNIT, UNIT)
            q_pair = work.q[span, lanes]
            d_pair = work.d_mixed[span, lanes]
            ends = query_marks(info[1 + block])
            for half in range(2):
                left = (head_half(q_pair, half) * HEAD_WIDTH**-0.5).astype(BF)
                grad = head_half(d_pair, half).astype(BF)
                logs = work.lse[pl.ds(2 * pair + half, 1), span]
                probs = jnp.exp(dot_nt(marked, jnp.concatenate([left, ends], axis=1)) - logs)
                d_probs = dot_nt(values, grad)
                inner = work.inner[pl.ds(2 * pair + half, 1), span]
                lefts.append(left)
                grads.append(grad)
                probs_low.append(probs.astype(BF))
                scores_low.append((probs * (d_probs - inner)).astype(BF))
            grad_q = dot_nn(turned, jnp.concatenate(scores_low[-2:], axis=0))
            work.dq[span, lanes] = (grad_q.T * HEAD_WIDTH**-0.5).astype(BF)
        grad_v = dot_nn(jnp.concatenate(probs_low, axis=1), jnp.concatenate(grads, axis=0))
        grad_k = dot_nn(jnp.concatenate(scores_low, axis=1), jnp.concatenate(lefts, axis=0))
        for which, grad in ((0, grad_k.astype(BF)), (1, grad_v.astype(BF))):
            work.dkv_own[which, :, lanes] = grad[:share]
            work.dkv_give[which, :, lanes] = grad[share:]
        return carry

    lax.fori_loop(0, work.q.shape[1] // LANES, step, 0)
    work.flush("dkv_give")
    work.flush("dkv_own")
    work.flush("dq")


def sum_keys_values(info, work, dkv):
    work.need("dkv_own", "dkv_sib")
    for which in range(2):
        dkv[which] = (
            work.dkv_own[which].astype(F32) + work.dkv_sib[which].astype(F32)
        ).astype(BF)
    work.need("entry")
    lanes = chip_lanes(info, dkv.shape[2])
    entry = work.entry[...].T
    pair_grads(info, work, [(entry, dkv[0, :, lanes]), (entry, dkv[1, :, lanes])])


def kv_grads_kernel(info, work, weights):
    sum_keys_values(info, work, work.dkv)
    work.flush("dkv")


def qkv_back_kernel(info, work, weights):
    rows = weights[0].shape[0] // 4
    sems = work.sems
    plan = plan_of((work.wq, work.wk, work.wv), 0, rows)
    start_rows(weights, info[0], plan, sems)
    work.stats[...] = work.early[...]
    stats = work.stats.at[pl.ds(0, 24)]
    if work.has("send"):
        sum_keys_values(info, work, work.dkv)
    else:
        work.need("dkv")
    work.need("dq")
    stats[13:14, :] = total(fold(work.dq[...].astype(F32)))
    stats[14:15, :] = total(fold(work.dkv[1].astype(F32)))
    wait_rows(weights, plan, sems, range(0, 12))
    work.de[...] = (
        dot_nn(work.dq[...], work.wq[...])
        + dot_nn(work.dkv[0], work.wk[...])
        + dot_nn(work.dkv[1], work.wv[...])
    )
    work.need("x", "g")
    low = work.low if work.has("low") else None
    norm_back_rows(work.x, work.g, work.de, work.mod, info, 0, work.out, stats, low)
    work.flush("out")
    if low is not None:
        work.flush("low")


def merge_kernel(info, *refs, spots, after):
    chains = len(spots)
    ins, outs = refs[: 4 * chains], refs[4 * chains + after :]
    for chain, (result, column) in enumerate(spots):
        for side in range(2):
            received, kept = ins[4 * chain + 2 * side], ins[4 * chain + 2 * side + 1]
            out = outs[2 * result + side]
            lanes = pl.ds(column, received.shape[2])
            out[:, :, lanes] = (received[...].astype(F32) + kept[...].astype(F32)).astype(BF)


def gate(arrays, after):
    count = len(arrays)
    return pl.pallas_call(
        lambda *refs: None,
        out_shape=[shape(*a.shape, dtype=a.dtype) for a in arrays],
        in_specs=[ANY] * (count + len(after)),
        out_specs=[ANY] * count,
        input_output_aliases={i: i for i in range(count)},
        cost_estimate=lasting(0.5),
        name="gate",
    )(*arrays, *after)


def pack_kernel(info, *refs, groups, whole, after):
    count = sum(len(members) for _, members in groups)
    sources, rest = refs[:count], refs[count + after :]
    (in_sems, out_sems), rest = rest[-2:], rest[:-2]
    count = len(groups) + sum(whole)
    outs, held = list(rest[:count]), rest[count:]
    owns = [outs.pop(0) if one else None for one in whole]
    spots = []
    at = 0
    for index, (layer, members) in enumerate(groups):
        rows = held[index].shape[0]
        piece_rows = rows // 4
        for quarter in range(4):
            row = quarter * piece_rows
            source = sources[at + quarter * len(members) // 4]
            src = source.at[layer, pl.ds(row % source.shape[1], piece_rows)]
            spots.append((index, quarter, held[index].at[pl.ds(row, piece_rows)], src))
        at += len(members)

    def arriving(place):
        _, _, spot, src = spots[place]
        return pltpu.make_async_copy(src, spot, in_sems.at[place])

    def leaving(index, which):
        if which == 2:
            return pltpu.make_async_copy(held[index], owns[index], out_sems.at[2 * index])
        rows = outs[index].shape[0]
        src = held[index].at[pl.ds(which * rows, rows)]
        return pltpu.make_async_copy(src, outs[index], out_sems.at[2 * index + 1])

    def by_parity(act):
        for parity in range(2):

            @pl.when(info[0] % 2 == parity)
            def _(parity=parity):
                act(parity)

    for place in range(len(spots)):
        arriving(place).start()
    for index in range(len(groups)):
        for quarter in range(4):
            arriving(4 * index + quarter).wait()
        by_parity(lambda parity: leaving(index, parity).start())
        if whole[index]:
            leaving(index, 2).start()
    for index in range(len(groups)):
        by_parity(lambda parity: leaving(index, parity).wait())
        if whole[index]:
            leaving(index, 2).wait()


def mod_kernel(condition, mod, mod_bias, q, v, cq, cv, up, out):
    narrow, units, columns = q.shape[1], up.shape[1], mod.shape[1]
    out[...] = jnp.zeros(out.shape, F32)
    for layer in range(LAYERS):
        row = pl.ds(layer, 1)
        out[layer, 0:SLOTS, 0:columns] = dot_nt(condition[...], mod[layer]) + mod_bias[
            row, :
        ].astype(F32)
        out[layer, 4:5, 0:units] = up[row, :].astype(F32)
        out[layer, 5:6, 0:narrow] = q[row, :].astype(F32)
        out[layer, 6:7, 0:narrow] = v[row, :].astype(F32)
        out[layer, 7:8, 0:narrow] = cq[row, :].astype(F32)
        out[layer, 4:5, 1024 : 1024 + narrow] = cv[row, :].astype(F32)


def assemble_kernel(info, *refs, narrow, units, columns):
    parts, (mods, narrows, ups) = refs[:4], refs[4:]
    narrows[...] = jnp.zeros(narrows.shape, F32)
    for rank in range(4):

        @pl.when(info[5] == rank)
        def _(rank=rank):
            for shard in range(4):
                part = parts[shard ^ rank]
                for layer in range(LAYERS):
                    mods[layer, :, shard * columns : (shard + 1) * columns] = part[
                        layer, 0:SLOTS, 0:columns
                    ]
                    ups[layer, :, shard * units : (shard + 1) * units] = part[layer, 4:5, 0:units]
                    at = slice(shard * narrow, (shard + 1) * narrow)
                    for row, source in ((0, 5), (2, 6), (3, 7)):
                        narrows[layer, row : row + 1, at] = part[
                            layer, source : source + 1, 0:narrow
                        ]
                    narrows[layer, 5:6, at] = part[layer, 4:5, 1024 : 1024 + narrow]


def collect_kernel(info, *refs, narrow, units, columns):
    stats, condition, out = refs[: 2 * LAYERS], refs[2 * LAYERS], refs[2 * LAYERS + 1]
    sums = refs[2 * LAYERS + 2]
    width = stats[0].shape[1]
    work = out
    out = refs[2 * LAYERS + 3]
    out[...] = jnp.zeros(out.shape, F32)
    for layer in range(LAYERS):
        sums[...] = stats[2 * layer][...] + stats[2 * layer + 1][...]
        base = 8 * layer
        out[base + 4 : base + 5, width : 2 * width] = sums[60:61, :]
        out[base + 5 : base + 6, 0:width] = sums[12:13, :]
        out[base + 5 : base + 6, width : 2 * width] = sums[36:37, :]
        for index in range(2):
            out[base + 6 + index : base + 7 + index, 512 : 512 + width] = condition[
                2 * layer + index : 2 * layer + index + 1, :
            ].astype(F32)
        for rank in range(4):

            @pl.when(info[5] == rank)
            def _(rank=rank, base=base):
                first = rank * columns
                for index in range(9):
                    low = max(first, index * width)
                    high = min(first + columns, (index + 1) * width)
                    if low < high:
                        row = (index // 3) * 24 + (index % 3) * 4
                        out[base : base + 4, low - first : high - first] = sums[
                            row : row + 4, low - index * width : high - index * width
                        ]
                out[base + 4 : base + 5, 0:units] = sums[61 + rank : 62 + rank, :]
                own = slice(rank * narrow, (rank + 1) * narrow)
                out[base + 6 : base + 7, 0:narrow] = sums[13:14, own]
                out[base + 6 : base + 7, 256 : 256 + narrow] = sums[14:15, own]
                out[base + 7 : base + 8, 0:narrow] = sums[37:38, own]
                out[base + 7 : base + 8, 256 : 256 + narrow] = sums[38:39, own]
    work[...] = out[...].astype(BF)


def spread_kernel(info, gathered, grad, bias_grad, q, v, cq, cv, up, o1, o2, o3, rows, conditions):
    count = gathered.shape[0]
    columns, part = grad.shape[2], grad.shape[1]
    width, narrow, units = conditions.shape[1], q.shape[1], up.shape[1]
    shift = lax.rem(width - info[8] * part, width)
    for index in range(count):
        for slot in range(SLOTS):
            row = 8 * (slot // 2) + 6 + slot % 2
            conditions[SLOTS * index + slot : SLOTS * index + slot + 1, :] = gathered[
                index ^ info[8], row : row + 1, 512 : 512 + width
            ].astype(F32)
    turned = pltpu.roll(conditions[...], shift, 1)[:, :part].T
    for layer in range(LAYERS):
        base = 8 * layer
        sums = jnp.zeros((8, gathered.shape[2]), F32)
        for index in range(count):
            values = gathered[index ^ info[8]].astype(F32)[base : base + 8]
            sums += values
            rows[SLOTS * index : SLOTS * (index + 1), :] = values[0:SLOTS, 0:columns]
        grad[layer] = jnp.dot(
            turned, rows[...], precision=lax.Precision.HIGHEST, preferred_element_type=F32
        )
        at = slice(layer, layer + 1)
        bias_grad[at, :] = jnp.sum(sums[0:SLOTS, 0:columns], axis=0, keepdims=True)
        up[at, :] = sums[4:5, 0:units]
        q[at, :] = sums[6:7, 0:narrow]
        v[at, :] = sums[6:7, 256 : 256 + narrow]
        cq[at, :] = sums[7:8, 0:narrow]
        cv[at, :] = sums[7:8, 256 : 256 + narrow]
        for out, row, lane in ((o1, 5, 0), (o2, 5, width), (o3, 4, width)):
            own = jnp.broadcast_to(sums[row : row + 1, lane : lane + width], (8, width))
            out[at, :] = pltpu.roll(own, shift, 1)[0:1, :part]


def finish_kernel(*refs, wide, spots):
    parts, outs = refs[: 2 * len(spots)], refs[2 * len(spots) :]
    step = 3 * LANES
    for chain, places in enumerate(spots):
        values = parts[2 * chain][0].astype(F32) + parts[2 * chain + 1][0].astype(F32)
        at = 0
        for layer, pair in places:
            if wide:
                width = outs[0].shape[2]
                for out in outs:
                    out[layer] = values[:, at : at + width]
                    at += width
                continue
            both = values[:, at : at + step]
            at += step
            first = jnp.concatenate(
                [both[:, :LANES], both[:, 2 * LANES : 2 * LANES + HEAD_WIDTH]], axis=1
            )
            second = jnp.concatenate(
                [both[:, LANES : 2 * LANES], both[:, 2 * LANES + HEAD_WIDTH :]], axis=1
            )
            for out, matrix in zip(outs[2 * pair : 2 * pair + 2], (first, second)):
                out[layer] = matrix if out.shape[1:] == matrix.shape else matrix.T


def join_kernel(info, rows, other, out):
    share = rows.shape[0]
    for core in range(2):

        @pl.when(info[5] % 2 == core)
        def _(core=core):
            out[pl.ds(core * share, share), :] = rows[...]
            out[pl.ds((1 - core) * share, share), :] = other[...]


def tensor_hop(values, step):
    return lax.ppermute(values, "tensor", [(i, i ^ step) for i in range(4)])


def dp_hop(values, step):
    size = lax.axis_size("dp")
    return lax.ppermute(values, "dp", [(i, i ^ step) for i in range(size)])


def time_features(moments, width):
    half = width // 2
    rates = jnp.exp(-math.log(10000.0) * jnp.arange(half, dtype=F32) / half)
    angles = moments.astype(F32)[:, None] * rates[None, :]
    return jnp.concatenate([jnp.cos(angles), jnp.sin(angles)], axis=1)


def shards(
    tokens,
    text,
    timesteps,
    item_frames,
    cotangent,
    self_query,
    self_query_bias,
    self_key,
    self_value,
    self_value_bias,
    self_output,
    self_output_bias,
    cross_query,
    cross_query_bias,
    cross_key,
    cross_value,
    cross_value_bias,
    cross_output,
    cross_output_bias,
    hidden_up,
    hidden_up_bias,
    hidden_down,
    hidden_down_bias,
    modulation,
    modulation_bias,
):
    frames, width = tokens.shape
    words = text.shape[1]
    columns = modulation.shape[2]
    narrow = self_query.shape[2]
    units = hidden_up.shape[2]
    rank = lax.axis_index("tensor")
    me = lax.axis_index("dp")
    size = lax.axis_size("dp")
    core = rank % 2
    share = frames // 2
    blocks = share // UNIT
    unit = width // size
    turn = lambda values: jnp.swapaxes(values, 1, 2)

    order = jnp.arange(SLOTS, dtype=jnp.int32)
    ends = jnp.sum(jnp.where(order[:, None] <= order[None, :], item_frames[:, None], 0), axis=0)
    turned = (jnp.arange(frames // UNIT, dtype=jnp.int32) + core * blocks) % (2 * blocks)
    slots = jnp.sum((turned[:, None] * UNIT >= ends[None, :]).astype(jnp.int32), axis=1)
    places = jnp.stack([rank, rank // 2, rank ^ 1, me]).astype(jnp.int32)
    info = jnp.concatenate([(rank * 2 + me % 2)[None].astype(jnp.int32), slots, places])

    def pack(members, whole, after=()):
        rows = [sum(a.shape[1] for a in some) for _, some in members]
        outs = [shape(r, width, dtype=BF) for r, one in zip(rows, whole) if one]
        outs += [shape(r // 2, width, dtype=BF) for r in rows]
        arrays = [a for _, some in members for a in some]
        results = pl.pallas_call(
            partial(
                pack_kernel,
                groups=[(layer, [None] * len(some)) for layer, some in members],
                whole=whole,
                after=len(after),
            ),
            out_shape=outs,
            in_specs=[SMALL] + [ANY] * (len(arrays) + len(after)),
            out_specs=[ANY] * len(outs),
            scratch_shapes=[
                *[pltpu.VMEM((r, width), BF) for r in rows],
                pltpu.SemaphoreType.DMA((4 * len(members),)),
                pltpu.SemaphoreType.DMA((2 * len(members),)),
            ],
            compiler_params=pltpu.CompilerParams(vmem_limit_bytes=VMEM_BYTES),
            cost_estimate=lasting(1.0),
            name="pack_weights",
        )(info, *arrays, *after)
        return list(results[: sum(whole)]), list(results[sum(whole) :])

    selfs = [turn(self_query), turn(self_key), turn(self_value), self_output]
    crosses = [turn(cross_query), turn(cross_key), turn(cross_value), cross_output]
    own0, first0 = pack([(0, selfs)], [True])

    condition = jax.nn.silu(time_features(timesteps, width)).astype(BF)
    mine = plain(
        mod_kernel,
        "modulation_rows",
        None,
        [
            condition,
            turn(modulation),
            modulation_bias,
            self_query_bias,
            self_value_bias,
            cross_query_bias,
            cross_value_bias,
            hidden_up_bias,
        ],
        [shape(LAYERS, 8, -(-columns // LANES) * LANES)],
    )
    own1, first1 = pack(
        [(0, crosses), (1, selfs), (1, crosses), (1, [hidden_up]), (1, [hidden_down])],
        [True, True, True, False, False],
        [mine],
    )
    firsts, owns = first0 + first1, own0 + own1
    others = [tensor_hop(mine, 1), tensor_hop(mine, 2)]
    others.append(tensor_hop(others[0], 2))
    out_biases = [
        b.reshape(LAYERS, 1, width) for b in (self_output_bias, cross_output_bias, hidden_down_bias)
    ]

    count = len(firsts)
    along_x, along_y, over_x, over_y, sibs = [[None] * count for _ in range(5)]

    def leave(index):
        along_x[index] = tensor_hop(firsts[index], 2)

    def swap(index):
        sibs[index] = tensor_hop(owns[index], 1)

    def go_on(index):
        along_y[index] = dp_hop(along_x[index], 1)
        over_x[index] = tensor_hop(along_x[index], 1)

    def end(index):
        over_y[index] = tensor_hop(along_y[index], 1)

    def weights_of(index):
        return [
            owns[index],
            sibs[index],
            along_x[index],
            along_y[index],
            over_x[index],
            over_y[index],
        ]

    def open_gate(after, leaving=(), at_x=(), at_y=(), settled=()):
        places = [(firsts, i) for i in leaving]
        places += [(along_x, i) for i in at_x] + [(along_y, i) for i in at_y] + list(settled)
        opened = gate([values[i] for values, i in places], after)
        for (values, i), array in zip(places, opened):
            values[i] = array
        for i in leaving:
            leave(i)
        for i in at_x:
            go_on(i)
        for i in at_y:
            end(i)
        return list(opened)

    leave(0)
    swap(0)
    open_gate([mine], [], [0])
    open_gate([*others, along_x[0]], [1])
    swap(1)
    go_on(1)
    owns += [hidden_up, hidden_down]
    sibs[4:6] = tensor_hop(hidden_up, 1), tensor_hop(hidden_down, 1)
    mods, narrow_biases, up_biases = plain(
        partial(assemble_kernel, narrow=narrow, units=units, columns=columns),
        "modulation_of_all",
        info,
        [mine, *others],
        [
            shape(LAYERS, SLOTS, 4 * columns),
            shape(LAYERS, 8, 4 * narrow),
            shape(LAYERS, 1, 4 * units),
        ],
        after=[along_x[1]],
    )
    open_gate([mods], [], [], [0])

    text_rows = jnp.pad(text, ((0, 0), (0, LANES - words), (0, 0))).reshape(-1, width)
    whole = pltpu.VMEM((width, width), BF)
    four = pltpu.VMEM((4, width, units), BF)
    two = pltpu.VMEM((2, width, units), BF)
    floats = pltpu.VMEM((share, width), F32)
    lows = pltpu.VMEM((share, width), BF)
    sems = lambda n: pltpu.SemaphoreType.DMA((n,))
    frame_low = shape(share, width, dtype=BF)
    frame_high = shape(share, width)
    frame_wide = shape(share, 4 * units, dtype=BF)
    frame_chip = shape(share, 2 * units, dtype=BF)
    two_low = shape(2, share, width, dtype=BF)
    two_text = shape(2, SLOTS * LANES, width, dtype=BF)
    logs = shape(16, share)
    log_work = pltpu.VMEM((share, LANES), F32)
    stat_shape = shape(72, width)

    x = lax.dynamic_slice_in_dim(tokens, core * share, share).astype(F32)
    kept = []
    for layer in range(LAYERS):
        first = 2 * layer
        mod = (mods, (layer,))
        biases = (narrow_biases, (layer,))
        common = dict(w=pltpu.VMEM((2, width, width), BF), sems=sems(8))
        if layer == 0:
            entry1, kv = run(
                kv_kernel,
                "self_keys_values",
                info,
                dict(x=x),
                dict(mod=mod, biases=biases),
                weights_of(first),
                dict(entry=frame_low, kv=two_low),
                {},
                common,
                [along_x[1], sibs[1], sibs[4], sibs[5]],
                3.0,
            )
        else:
            entry1, kv, x, branch3 = run(
                kv_kernel,
                "residual_keys_values",
                info,
                dict(part=part, other=tensor_hop(part, 2), below=kept[-1]["x2"]),
                dict(
                    mod=mod,
                    mod_below=(mods, (layer - 1,)),
                    bias=(out_biases[2], (layer - 1,)),
                    biases=biases,
                ),
                weights_of(first),
                dict(entry=frame_low, kv=two_low, x=frame_high, branch=frame_low),
                {},
                common | dict(sum=floats),
                opened,
                3.0,
            )
            kept[-1]["branch3"] = branch3
        kv_sib = tensor_hop(kv, 1)
        opened = (
            open_gate([entry1], [2, 3], [], [], [(over_x, 1)])
            if layer == 0
            else open_gate([entry1], [5], [], [], [(over_x, 4), (over_y, 3)])
        )
        (q,) = run(
            q_kernel,
            "self_query",
            info,
            dict(entry=entry1),
            dict(biases=biases),
            weights_of(first),
            dict(q=frame_low),
            {},
            dict(w=whole, sems=sems(4)),
            [],
            15.0,
        )
        x1, mixed1, rest1, lse1, branch1 = run(
            self_kernel,
            "self_attention",
            info,
            dict(q=q, kv_own=kv, kv_sib=kv_sib, x=x),
            dict(mod=mod, bias=(out_biases[0], (layer,))),
            weights_of(first),
            dict(out=frame_high, mixed=frame_low, rest=frame_low, lse=logs, branch=frame_low),
            {},
            dict(wo=whole, logs=log_work, sum=floats, sems=sems(4)),
            opened,
            8.0,
        )
        if layer == 0:
            opened = open_gate([x1], [4], [2], [1], [(along_x, 3)])
            swap(2)
        else:
            opened = open_gate([x1], [], [5], [4])
        x2, entry2, cq, ckv, mixed2, lse2, branch2 = run(
            partial(cross_kernel, words=words),
            "cross_attention",
            info,
            dict(x=x1, text=text_rows),
            dict(mod=mod, biases=biases, bias=(out_biases[1], (layer,))),
            weights_of(first + 1),
            dict(
                out=frame_high,
                entry=frame_low,
                q=frame_low,
                kv=two_text,
                mixed=frame_low,
                lse=logs,
                branch=frame_low,
            ),
            {},
            dict(
                wq=whole, wk=whole, wv=whole, wo=whole, logs=log_work, sum=floats, sems=sems(16)
            ),
            opened,
            6.0,
        )
        if layer == 0:
            opened = open_gate([x2], [], [3], [2], [(over_x, 2), (sibs, 2), (along_x, 4)])
            swap(3)
        else:
            opened = open_gate([x2], [], [], [5], [(over_x, 5), (over_y, 4)])
        if layer == 0:
            part, entry3, active, slope = run(
                lambda info, work, w: hidden_kernel(info, work, w, 0),
                "feed_forward_part",
                info,
                dict(x=x2),
                dict(mod=mod, up_bias=(up_biases, (layer,))),
                [hidden_up, sibs[4], hidden_down, sibs[5]],
                dict(part=frame_low, entry=frame_low, active=frame_chip, slope=frame_chip),
                {},
                dict(
                    up=two, down=two, before=floats, sum=floats, sems=sems(2), down_sems=sems(2)
                ),
                opened,
                5.0,
            )
            opened = open_gate([part], [], [4], [3], [(over_x, 3), (over_y, 2), (sibs, 3)])
            x3 = branch3 = None
        else:
            x3, entry3, active, slope, branch3, low = run(
                lambda info, work, w: hidden_kernel(info, work, w, 1),
                "feed_forward",
                info,
                dict(x=x2),
                dict(mod=mod, up_bias=(up_biases, (layer,)), bias=(out_biases[2], (layer,))),
                weights_of(4) + weights_of(5),
                dict(
                    out=frame_high,
                    entry=frame_low,
                    active=frame_wide,
                    slope=frame_wide,
                    branch=frame_low,
                    low=frame_low,
                ),
                {},
                dict(
                    up=four, down=four, before=floats, sum=floats, sems=sems(8), down_sems=sems(8)
                ),
                opened,
                7.0,
            )
        kept.append(
            dict(
                x=x,
                entry1=entry1,
                q=q,
                kv=kv,
                kv_sib=kv_sib,
                mixed1=mixed1,
                rest1=rest1,
                lse1=lse1,
                branch1=branch1,
                x1=x1,
                entry2=entry2,
                cq=cq,
                ckv=ckv,
                mixed2=mixed2,
                lse2=lse2,
                branch2=branch2,
                x2=x2,
                entry3=entry3,
                active=active,
                slope=slope,
                branch3=branch3,
            )
        )
        x = x3

    def join(rows, *after):
        return plain(
            join_kernel,
            "join_rows",
            info,
            [rows, tensor_hop(rows, 1)],
            [shape(2 * share, width, dtype=BF)],
            after=after,
        )


    chains = {}

    def start(name, send, keep):
        view = (size, unit, send.shape[1])
        chains[name] = (tensor_hop(send, 1).reshape(view), keep.reshape(view), 0)

    def held(*names):
        return [chains[name][1] for name in names]

    def advance(names, after=(), cost=1.5):
        targets = [(n, [n]) if isinstance(n, str) else n for n in names]
        targets = [t for t in targets if 2 ** chains[t[1][0]][2] < size]
        if not targets:
            return
        ins, in_specs, outs, out_specs, spots = [], [], [], [], []
        for result, (_, parts) in enumerate(targets):
            column = 0
            for name in parts:
                received, kept_part, bit = chains[name]
                blocks_left, rows, wide = received.shape
                spots.append((result, column))
                column += wide
                for side in range(2):

                    def at(i, info, bit=bit, side=side):
                        return (0, ((info[8] >> bit) & 1) ^ side, 0, 0)

                    for part in (received, kept_part):
                        ins.append(part.reshape(blocks_left // 2, 2, rows, wide))
                        in_specs.append(pl.BlockSpec((blocks_left // 2, None, rows, wide), at))
            for side in range(2):
                outs.append(shape(blocks_left // 2, rows, column, dtype=BF))
                out_specs.append(
                    pl.BlockSpec((blocks_left // 2, rows, column), lambda i, info: (0, 0, 0))
                )
        results = pl.pallas_call(
            partial(merge_kernel, spots=spots, after=len(after)),
            grid_spec=pltpu.PrefetchScalarGridSpec(
                num_scalar_prefetch=1,
                grid=(1,),
                in_specs=in_specs + [ANY] * len(after),
                out_specs=out_specs,
            ),
            out_shape=outs,
            compiler_params=pltpu.CompilerParams(vmem_limit_bytes=VMEM_BYTES),
            cost_estimate=lasting(cost),
            name="merge_grads",
        )(info, *ins, *after)
        for index, (name, parts) in enumerate(targets):
            bit = chains[parts[0]][2]
            hold, give = results[2 * index : 2 * index + 2]
            for part in parts:
                del chains[part]
            chains[name] = (dp_hop(give, 2**bit), hold, bit + 1)

    g = lax.dynamic_slice_in_dim(cotangent, core * share, share).astype(F32)
    sums = []
    last = LAYERS - 1
    for layer in reversed(range(LAYERS)):
        first = 2 * layer
        k = kept[layer]
        mod = (mods, (layer,))
        above = layer + 1
        f_name, c_name, a_name, s_name = [f"{kind}{layer}" for kind in "fcas"]
        n_name = f"n{above}"

        def grads_out(members):
            return {name: shape(width, members * narrow, dtype=BF) for name in ("send", "keep")}

        more, older = [], []
        if layer < last:
            more = held(f"f{above}", f"c{above}", n_name)
            older = [n_name, f"c{above}"]
        if layer == last:
            send, keep, g, stats = run(
                lambda info, work, w: hidden_back_kernel(info, work, w, 1),
                "feed_forward_back",
                info,
                dict(g=g, branch=k["branch3"], slope=k["slope"], entry=k["entry3"], x=k["x2"]),
                dict(mod=mod),
                weights_of(4) + weights_of(5) + [k["active"]],
                {name: shape(width, 2 * units, dtype=BF) for name in ("send", "keep")}
                | dict(out=frame_high),
                dict(stats=stat_shape),
                dict(
                    up=four,
                    down=four,
                    gb=lows,
                    d_before=pltpu.VMEM((share, 4 * units), BF),
                    acts=pltpu.VMEM((2, share, units), BF),
                    act_sems=sems(2),
                    before=floats,
                    de=floats,
                    sems=sems(8),
                    down_sems=sems(8),
                ),
                more,
                10.0,
            )
            start(f_name, send, keep)
            extra, scratch = {}, {}
        else:
            part, gb, d_before, stats = run(
                lambda info, work, w: hidden_back_kernel(info, work, w, 0),
                "feed_forward_back_part",
                info,
                dict(g=g, branch=k["branch3"], slope=k["slope"]),
                dict(mod=mod),
                [hidden_up, sibs[4], hidden_down, sibs[5]],
                dict(part=frame_low, gb=frame_low, d_before=frame_chip),
                dict(stats=stat_shape),
                dict(
                    up=two, down=two, before=floats, de=floats, sems=sems(2), down_sems=sems(2)
                ),
                more,
                5.0,
            )
            other = tensor_hop(part, 2)
            send, keep = run(
                hidden_grads_kernel,
                "feed_forward_grads",
                info,
                dict(entry=k["entry3"], d_before=d_before, gb=gb, active=k["active"]),
                {},
                [],
                {name: shape(width, 2 * units, dtype=BF) for name in ("send", "keep")},
                {},
                {},
                [gb],
                1.0,
            )
            start(f_name, send, keep)
            output = join(low, gb)
            extra = dict(part=part, other=other, above=k["x2"])
            scratch = dict(g_mid=floats)
        send, keep, g, stats = run(
            partial(cross_back_kernel, words=words),
            "cross_attention_back",
            info,
            dict(
                g=g,
                branch=k["branch2"],
                q=k["cq"],
                kv=k["ckv"],
                lse=k["lse2"],
                entry=k["entry2"],
                text=text_rows,
                mixed=k["mixed2"],
                x=k["x1"],
                **extra,
            ),
            dict(mod=mod, early=(stats, ())),
            weights_of(first + 1),
            grads_out(4) | dict(out=frame_high),
            dict(stats=stat_shape),
            dict(
                wq=whole,
                wo=whole,
                gb=lows,
                dq=lows,
                dkv=pltpu.VMEM(two_text.shape, BF),
                d_mixed=lows,
                de=floats,
                dkv_sum=pltpu.VMEM(two_text.shape, F32),
                sems=sems(8),
                **scratch,
            ),
            held(f_name, *older) + ([output] if layer < last else []),
            60.0,
        )
        start(c_name, send, keep)
        advance([f_name, *older], [g, *([chains[f"f{above}"][0]] if layer < last else [])])
        gb1, dq, dkv_own, dkv_give, stats = run(
            self_back_kernel,
            "self_attention_back",
            info,
            dict(
                g=g,
                branch=k["branch1"],
                mixed=k["mixed1"],
                rest=k["rest1"],
                q=k["q"],
                kv_own=k["kv"],
                kv_sib=k["kv_sib"],
                lse=k["lse1"],
            ),
            dict(mod=mod, early=(stats, ())),
            weights_of(first),
            dict(gb=frame_low, dq=frame_low, dkv_own=two_low, dkv_give=two_low),
            dict(stats=stat_shape),
            dict(wo=whole, d_mixed=lows, inner=pltpu.VMEM((16, share), F32), sems=sems(4)),
            held(f_name, c_name, *older),
            13.0,
        )
        dkv_sib = tensor_hop(dkv_give, 1)
        advance([f_name, c_name], [dq])
        send, keep = run(
            query_output_kernel,
            "query_output_grads",
            info,
            dict(entry=k["entry1"], gb=gb1, dq=dq, mixed=k["mixed1"]),
            {},
            [],
            grads_out(2),
            {},
            {},
            held(f_name, c_name),
            15.0,
        )
        start(a_name, send, keep)
        arriving = dict(dkv_own=dkv_own, dkv_sib=dkv_sib, entry=k["entry1"])
        if layer == 0:
            send, keep, dkv = run(
                kv_grads_kernel,
                "keys_values_grads",
                info,
                arriving,
                {},
                [],
                grads_out(2) | dict(dkv=two_low),
                {},
                {},
                held(a_name),
                4.0,
            )
            start(s_name, send, keep)
            advance([f_name, a_name, n_name], held(s_name) + [chains[f"c{above}"][0]])
            arriving = dict(dkv=dkv)
        results = run(
            qkv_back_kernel,
            "self_qkv_back",
            info,
            arriving | dict(dq=dq, x=k["x"], g=g),
            dict(mod=mod, early=(stats, ())),
            weights_of(first),
            (dict(low=frame_low) if layer == 0 else grads_out(2)) | dict(out=frame_high),
            dict(stats=stat_shape),
            dict(wq=whole, wk=whole, wv=whole, de=floats, sems=sems(12))
            | (dict(dkv=pltpu.VMEM(two_low.shape, BF)) if layer else {}),
            held(a_name, c_name, f_name),
            6.0,
        )
        g, stats = results[-2:]
        if layer:
            start(s_name, *results[:2])
        rest = [a_name, s_name] if layer == 0 else [f_name, (f"n{layer}", [a_name, s_name])]
        advance([c_name, *rest], [g] + ([chains["f0"][0], chains[n_name][0]] if layer < last else []))
        sums = [stats, tensor_hop(stats, 1)] + sums
    vectors = plain(
        partial(collect_kernel, narrow=narrow, units=units, columns=columns),
        "collect_sums",
        info,
        [*sums, condition],
        [shape(16, mine.shape[2], dtype=BF)],
        [pltpu.VMEM(stat_shape.shape, F32), pltpu.VMEM((16, mine.shape[2]), F32)],
        held("s0"),
    )
    gathered, hop = vectors[None], size // 2

    def gather_sums():
        nonlocal gathered, hop
        if hop:
            both = jnp.stack([gathered, dp_hop(gathered, hop)], axis=1)
            gathered = both.reshape(-1, *vectors.shape)
            hop //= 2

    low = results[0]
    while any(2 ** chain[2] < size for chain in chains.values()):
        gather_sums()
        advance(list(chains), held("s0") + [gathered])
        if low is results[0]:
            (low,) = gate([low], held("s0"))
    input_grad = join(low)
    while hop:
        gather_sums()

    def parts_of(*names):
        return [part.reshape(1, unit, -1) for name in names for part in chains[name][:2]]

    up_grad, down_grad = plain(
        partial(finish_kernel, wide=True, spots=[[(layer, 0)] for layer in range(LAYERS)]),
        "finish_wide",
        None,
        parts_of(*[f"f{layer}" for layer in range(LAYERS)]),
        [shape(LAYERS, unit, units)] * 2,
        after=held("s0"),
    )
    straight, across = shape(LAYERS, unit, narrow), shape(LAYERS, narrow, unit)
    lasts = [[(1, 0), (1, 1)], [(1, 2), (1, 3)]]
    cq_grad, ck_grad, cv_grad, co_grad, q_grad, o_grad, k_grad, v_grad = plain(
        partial(finish_kernel, wide=False, spots=lasts + [[(0, 0), (0, 1)], [(0, 2)], [(0, 3)]]),
        "finish_narrow",
        None,
        parts_of("c1", "n1", "c0", "a0", "s0"),
        [straight, straight, straight, across, straight, across, straight, straight],
    )
    small = plain(
        spread_kernel,
        "spread_sums",
        info,
        [gathered],
        [shape(LAYERS, unit, columns), shape(LAYERS, columns)]
        + [shape(LAYERS, narrow)] * 4
        + [shape(LAYERS, units)]
        + [shape(LAYERS, unit)] * 3,
        [pltpu.VMEM((SLOTS * size, columns), F32), pltpu.VMEM((SLOTS * size, width), F32)],
    )
    mod_grad, mod_bias_grad, q_sum, v_sum, cq_sum, cv_sum, up_sum, o1, o2, o3 = small
    return (
        output,
        input_grad,
        q_grad,
        q_sum,
        k_grad,
        v_grad,
        v_sum,
        o_grad,
        o1,
        cq_grad,
        cq_sum,
        ck_grad,
        cv_grad,
        cv_sum,
        co_grad,
        o2,
        up_grad,
        up_sum,
        turn(down_grad),
        o3,
        mod_grad,
        mod_bias_grad,
    )


def solution(mesh):
    dp, tensor = "dp", "tensor"
    columns, vector = P(None, None, tensor), P(None, tensor)
    matrix, turned, spread = P(None, dp, tensor), P(None, tensor, dp), P(None, dp)
    placed = (
        P(dp, None),
        P(dp, None, None),
        P(dp),
        P(dp),
        P(dp, None),
        columns,
        vector,
        columns,
        columns,
        vector,
        P(None, tensor, None),
        P(),
        columns,
        vector,
        columns,
        columns,
        vector,
        P(None, tensor, None),
        P(),
        columns,
        vector,
        P(None, tensor, None),
        P(),
        columns,
        vector,
    )
    results = (
        P(dp, None),
        P(dp, None),
        matrix,
        vector,
        matrix,
        matrix,
        vector,
        turned,
        spread,
        matrix,
        vector,
        matrix,
        matrix,
        vector,
        turned,
        spread,
        matrix,
        vector,
        turned,
        spread,
        matrix,
        vector,
    )
    return jax.shard_map(
        shards, mesh=mesh, in_specs=placed, out_specs=results, check_vma=False
    )
```

```python
from functools import partial
import math

import jax
import jax.numpy as jnp
from jax import lax
from jax.experimental import pallas as pl
from jax.experimental.pallas import tpu as pltpu
from jax.sharding import PartitionSpec as P

HEAD_WIDTH = 64
UNIT = 256
LAYERS = 2
WINDOW = 1024
EPSILON = 1e-06
LANES = 128
CHUNK = 64
SLOTS = WINDOW // UNIT
FAR = -1e30
VMEM_BYTES = 62 * 1024 * 1024
BF = jnp.bfloat16
F32 = jnp.float32
ROOT = math.sqrt(2.0 / math.pi)
CUBIC = 0.044715


def dot_nn(left, right):
    return jnp.dot(left, right, preferred_element_type=F32)


def dot_nt(left, right):
    return lax.dot_general(left, right, (((1,), (1,)), ((), ())), preferred_element_type=F32)


def dot_tn(left, right):
    return lax.dot_general(left, right, (((0,), (0,)), ((), ())), preferred_element_type=F32)


SMALL = pl.BlockSpec(memory_space=pltpu.SMEM)
NEAR = pl.BlockSpec(memory_space=pltpu.VMEM)
ANY = pl.BlockSpec(memory_space=pl.ANY)


class Work:
    def __init__(self, ins, outs, scratch, in_sems, out_sems):
        self.ins, self.outs, self.scratch, self.out_sems = ins, outs, scratch, out_sems
        self.copies, self.waited, self.flushed = {}, set(), []
        for index, (name, (ref, buffer)) in enumerate(ins.items()):
            self.copies[name] = pltpu.make_async_copy(ref, buffer, in_sems.at[index])
            self.copies[name].start()

    def __getattr__(self, name):
        if name in self.__dict__["ins"]:
            return self.ins[name][1]
        if name in self.__dict__["outs"]:
            return self.outs[name][1]
        return self.__dict__["scratch"][name]

    def has(self, name):
        return name in self.outs

    def takes(self, name):
        return name in self.ins

    def send(self, name, source, *at):
        ref = self.outs[name][0]
        copy = pltpu.make_async_copy(
            source, ref.at[at] if at else ref, self.out_sems.at[len(self.flushed)]
        )
        copy.start()
        self.flushed.append(copy)

    def need(self, *names):
        for name in names:
            if name not in self.waited:
                self.waited.add(name)
                self.copies[name].wait()

    def flush(self, name, *at):
        ref, buffer = self.outs[name]
        if at:
            ref, buffer = ref.at[at], buffer.at[at]
        copy = pltpu.make_async_copy(buffer, ref, self.out_sems.at[len(self.flushed)])
        copy.start()
        self.flushed.append(copy)

    def finish(self):
        self.need(*self.ins)
        for copy in self.flushed:
            copy.wait()


def run(body, name, info, ins, small, weights, outs, small_outs, scratch, after=(), cost=1.0):
    in_names, out_names, names = list(ins), list(outs), list(scratch)
    small_names, small_out_names = list(small), list(small_outs)
    counts = [1, len(in_names), len(small), len(weights), len(after), len(outs), len(small_outs)]

    def kernel(*refs):
        refs = list(refs)
        parts = []
        for count in counts:
            parts.append(refs[:count])
            refs = refs[count:]
        (info_ref,), in_refs, small_refs, weight_refs, _, out_refs, small_out_refs = parts
        in_bufs, refs = refs[: len(in_names)], refs[len(in_names) :]
        out_bufs, refs = refs[: len(out_names)], refs[len(out_names) :]
        rest, (in_sems, out_sems) = refs[:-2], refs[-2:]
        extra = {}
        rest = list(rest)
        for key in names:
            many = isinstance(scratch[key], list)
            size = len(scratch[key]) if many else 1
            extra[key] = rest[:size] if many else rest[0]
            rest = rest[size:]
        for key, ref in zip(small_names, small_refs):
            index = small[key][1]
            extra[key] = ref.at[index] if index else ref
        extra.update(zip(small_out_names, small_out_refs))
        work = Work(
            dict(zip(in_names, zip(in_refs, in_bufs))),
            dict(zip(out_names, zip(out_refs, out_bufs))),
            extra,
            in_sems,
            out_sems,
        )
        body(info_ref, work, weight_refs)
        work.finish()

    buffer = lambda a: pltpu.VMEM(a.shape, a.dtype)
    flat = []
    for value in scratch.values():
        flat += value if isinstance(value, list) else [value]
    results = pl.pallas_call(
        kernel,
        out_shape=[outs[n] for n in out_names] + [small_outs[n] for n in small_out_names],
        in_specs=[SMALL]
        + [ANY] * len(ins)
        + [NEAR] * len(small)
        + [ANY] * (len(weights) + len(after)),
        out_specs=[ANY] * len(outs) + [NEAR] * len(small_outs),
        scratch_shapes=[buffer(ins[n]) for n in in_names]
        + [buffer(outs[n]) for n in out_names]
        + flat
        + [pltpu.SemaphoreType.DMA((max(len(ins), 1),)), pltpu.SemaphoreType.DMA((32,))],
        compiler_params=pltpu.CompilerParams(vmem_limit_bytes=VMEM_BYTES),
        cost_estimate=lasting(cost),
        name=name,
    )(info, *ins.values(), *[array for array, _ in small.values()], *weights, *after)
    return results


def plain(body, name, info, ins, outs, scratch=(), after=()):
    first = len(ins) + (0 if info is None else 1)
    results = pl.pallas_call(
        lambda *refs: body(*refs[:first], *refs[first + len(after) :]),
        out_shape=outs,
        in_specs=([] if info is None else [SMALL]) + [NEAR] * len(ins) + [ANY] * len(after),
        out_specs=[NEAR] * len(outs),
        scratch_shapes=list(scratch),
        compiler_params=pltpu.CompilerParams(vmem_limit_bytes=VMEM_BYTES),
        cost_estimate=lasting(1.0),
        name=name,
    )(*([] if info is None else [info]), *ins, *after)
    return results if len(outs) > 1 else results[0]


def lasting(units):
    return pl.CostEstimate(flops=int(units * 0.4e9), bytes_accessed=1000, transcendentals=0)


def shape(*dims, dtype=F32):
    return jax.ShapeDtypeStruct(dims, dtype)


def start_rows(refs, place, plan, sems):
    own, sib, xa, ya, xb, yb = refs
    half = own.shape[0] // 2
    for rank in range(4):
        for parity in range(2):

            @pl.when(place == rank * 2 + parity)
            def _(rank=rank, parity=parity):
                for index, (shard, row, rows, dst) in enumerate(plan):
                    step = shard ^ rank
                    if step < 2:
                        src = (own, sib)[step].at[pl.ds(row, rows)]
                    else:
                        first, second = ((xa, ya), (xb, yb))[step - 2]
                        part = row // half
                        src = (first if part == parity else second).at[pl.ds(row - part * half, rows)]
                    pltpu.make_async_copy(src, dst, sems.at[index]).start()


def wait_rows(refs, plan, sems, which):
    for index in which:
        _, row, rows, dst = plan[index]
        pltpu.make_async_copy(refs[0].at[pl.ds(0, rows)], dst, sems.at[index]).wait()


def plan_of(buffers, first, rows):
    return [
        (shard, (first + which) * rows, rows, dst.at[pl.ds(shard * rows, rows)])
        for which, dst in enumerate(buffers)
        for shard in range(4)
    ]


def norm_rows(values):
    mean = jnp.mean(values, axis=-1, keepdims=True)
    center = values - mean
    factor = lax.rsqrt(jnp.mean(center * center, axis=-1, keepdims=True) + EPSILON)
    return center * factor, factor


def piece(mod, slot, index):
    width = mod.shape[1] // 9
    return mod[pl.ds(slot, 1), index * width : (index + 1) * width]


def entry_rows(x, mod, info, index, out):
    for block in range(x.shape[0] // UNIT):
        slot = info[1 + block]
        shift = piece(mod, slot, index)
        scale = 1.0 + piece(mod, slot, index + 1)

        def step(turn, carry):
            rows = pl.ds(pl.multiple_of(block * UNIT + turn * CHUNK, CHUNK), CHUNK)
            normed, _ = norm_rows(x[rows, :])
            out[rows, :] = (normed * scale + shift).astype(BF)
            return carry

        lax.fori_loop(0, UNIT // CHUNK, step, 0, unroll=True)


def residual_rows(x, mod, info, index, branch, branch_out, out, low=None):
    for block in range(x.shape[0] // UNIT):
        gate = piece(mod, info[1 + block], index)

        def step(turn, carry):
            rows = pl.ds(pl.multiple_of(block * UNIT + turn * CHUNK, CHUNK), CHUNK)
            values = branch[rows, :]
            branch_out[rows, :] = values.astype(BF)
            result = x[rows, :] + gate * values
            out[rows, :] = result
            if low is not None:
                low[rows, :] = result.astype(BF)
            return carry

        lax.fori_loop(0, UNIT // CHUNK, step, 0, unroll=True)


def fold(values):
    return jnp.sum(values.reshape(values.shape[0] // 8, 8, values.shape[1]), axis=0)


def total(values):
    return jnp.sum(values, axis=0, keepdims=True)


def gate_back(g, mod, info, index, branch, gb, stats):
    width = g.shape[1]
    sums = jnp.zeros((8, width), F32)
    for block in range(g.shape[0] // UNIT):
        slot = info[1 + block]
        gate = piece(mod, slot, index)

        def step(turn, carry):
            rows = pl.ds(pl.multiple_of(block * UNIT + turn * CHUNK, CHUNK), CHUNK)
            grad = g[rows, :]
            low = (gate * grad).astype(BF)
            gb[rows, :] = low
            return (
                carry[0] + fold(low.astype(F32)),
                carry[1] + fold(grad * branch[rows, :].astype(F32)),
            )

        sums, rows_sum = lax.fori_loop(
            0, UNIT // CHUNK, step, (sums, jnp.zeros((8, width), F32)), unroll=True
        )
        stats[pl.ds(8 + slot, 1), :] += total(rows_sum)
    stats[12:13, :] = total(sums)


def norm_back_rows(x, g, de, mod, info, index, out, stats, low=None):
    width = x.shape[1]
    for block in range(x.shape[0] // UNIT):
        slot = info[1 + block]
        scale = 1.0 + piece(mod, slot, index + 1)

        def step(turn, carry):
            rows = pl.ds(pl.multiple_of(block * UNIT + turn * CHUNK, CHUNK), CHUNK)
            normed, factor = norm_rows(x[rows, :])
            grad = de[rows, :]
            inner = grad * normed
            dn = grad * scale
            mean = jnp.mean(dn, axis=-1, keepdims=True)
            along = jnp.mean(dn * normed, axis=-1, keepdims=True)
            result = g[rows, :] + factor * (dn - mean - normed * along)
            out[rows, :] = result
            if low is not None:
                low[rows, :] = result.astype(BF)
            return (carry[0] + fold(grad), carry[1] + fold(inner))

        zero = jnp.zeros((8, width), F32)
        shift_sum, scale_sum = lax.fori_loop(0, UNIT // CHUNK, step, (zero, zero), unroll=True)
        stats[pl.ds(slot, 1), :] += total(shift_sum)
        stats[pl.ds(4 + slot, 1), :] += total(scale_sum)


def lane_ids(rows):
    return lax.broadcasted_iota(jnp.int32, (rows, LANES), 1)


def head_half(values, half):
    ids = lane_ids(values.shape[0])
    keep = ids < HEAD_WIDTH if half == 0 else ids >= HEAD_WIDTH
    return jnp.where(keep, values.astype(F32), 0.0)


def turned_halves(keys):
    turned = keys.T
    low = lax.broadcasted_iota(jnp.int32, turned.shape, 0) < HEAD_WIDTH
    zero = jnp.zeros(turned.shape, turned.dtype)
    return jnp.concatenate([jnp.where(low, turned, zero), jnp.where(low, zero, turned)], axis=1)


def query_marks(slot):
    return jnp.where(lane_ids(UNIT) == slot, 1.0, 0.0).astype(BF)


def key_marks(slots):
    ids = lane_ids(UNIT)
    parts = [jnp.where((ids < SLOTS) & (ids != slot), FAR, 0.0).astype(BF) for slot in slots]
    return jnp.concatenate(parts, axis=0)


def pair_lanes(pair):
    return pl.ds(pl.multiple_of(pair * LANES, LANES), LANES)


def kv_kernel(info, work, weights):
    rows = weights[0].shape[0] // 4
    plan = plan_of((work.w.at[0], work.w.at[1]), 1, rows)
    start_rows(weights, info[0], plan, work.sems)
    if work.has("branch"):
        work.need("part", "other", "below")
        bias = work.bias[...].astype(F32)
        for row in range(0, work.sum.shape[0], CHUNK):
            span = pl.ds(row, CHUNK)
            work.sum[span, :] = (
                work.part[span, :].astype(F32) + work.other[span, :].astype(F32) + bias
            )
        residual_rows(work.below, work.mod_below, info, 8, work.sum, work.branch, work.x)
        work.flush("branch")
        work.flush("x")
    else:
        work.need("x")
    entry_rows(work.x, work.mod, info, 0, work.entry)
    work.flush("entry")
    entry = work.entry[...]
    wait_rows(weights, plan, work.sems, range(4))
    work.kv[0] = dot_nt(entry, work.w[0]).astype(BF)
    work.flush("kv", 0)
    wait_rows(weights, plan, work.sems, range(4, 8))
    work.kv[1] = (dot_nt(entry, work.w[1]) + work.biases[2:3, :]).astype(BF)
    work.flush("kv", 1)


def q_kernel(info, work, weights):
    rows = weights[0].shape[0] // 4
    plan = plan_of((work.w,), 0, rows)
    start_rows(weights, info[0], plan, work.sems)
    work.need("entry")
    wait_rows(weights, plan, work.sems, range(4))
    work.q[...] = (dot_nt(work.entry[...], work.w[...]) + work.biases[0:1, :]).astype(BF)
    work.flush("q")


def soft_pair(work, q_pair, keys, values, marks, logs, pair, span, words=None):
    ids = lane_ids(UNIT)
    results = []
    kept = logs[span, :]
    for half in range(2):
        left = (head_half(q_pair, half) * HEAD_WIDTH**-0.5).astype(BF)
        if marks is not None:
            left = jnp.concatenate([left, marks], axis=1)
        scores = dot_nt(left, keys)
        if words is not None:
            scores = jnp.where(ids < words, scores, FAR)
        peak = jnp.max(scores, axis=-1, keepdims=True)
        both = dot_nn(jnp.exp(scores - peak).astype(BF), values)
        sums = both[:, LANES:]
        results.append(both[:, :LANES] / sums)
        kept = jnp.where(ids == 2 * pair + half, peak + jnp.log(sums), kept)
    logs[span, :] = kept
    return jnp.where(ids < HEAD_WIDTH, results[0], results[1])


def self_kernel(info, work, weights):
    rows = weights[0].shape[0] // 4
    sems = work.sems
    plan = [(s, 3 * rows, rows, work.wo.at[pl.ds(s * rows, rows)]) for s in range(4)]
    start_rows(weights, info[0], plan, sems)
    share = work.x.shape[0]
    blocks = share // UNIT
    marks = key_marks([info[1 + b] for b in range(2 * blocks)])
    ones = jnp.ones((2 * share, LANES), BF)
    logs, mixed = work.logs, work.mixed
    logs[...] = jnp.zeros(logs.shape, F32)
    work.need("q", "kv_own", "kv_sib")

    def both(which, lanes):
        return jnp.concatenate([work.kv_own[which, :, lanes], work.kv_sib[which, :, lanes]], axis=0)

    def step(pair, carry):
        lanes = pair_lanes(pair)
        keys = jnp.concatenate([both(0, lanes), marks], axis=1)
        values = jnp.concatenate([both(1, lanes), ones], axis=1)
        for block in range(blocks):
            span = pl.ds(block * UNIT, UNIT)
            values_mixed = soft_pair(
                work,
                work.q[span, lanes],
                keys,
                values,
                query_marks(info[1 + block]),
                logs,
                pair,
                span,
            )
            low = values_mixed.astype(BF)
            mixed[span, lanes] = low
            work.rest[span, lanes] = (values_mixed - low.astype(F32)).astype(BF)
        return carry

    lax.fori_loop(0, mixed.shape[1] // LANES, step, 0)
    work.flush("mixed")
    work.flush("rest")
    work.lse[...] = logs[...].T[: work.lse.shape[0], :]
    work.flush("lse")
    wait_rows(weights, plan, sems, range(4))
    work.sum[...] = dot_nn(mixed[...], work.wo[...]) + work.bias[...].astype(F32)
    work.need("x")
    residual_rows(work.x, work.mod, info, 2, work.sum, work.branch, work.out)
    work.flush("branch")
    work.flush("out")


def cross_kernel(info, work, weights, words):
    rows = weights[0].shape[0] // 4
    sems = work.sems
    order = (1, 2, 0, 3)
    plan = [
        (shard, order[i // 4] * rows, count, dst)
        for i, (shard, _, count, dst) in enumerate(
            plan_of((work.wk, work.wv, work.wq, work.wo), 0, rows)
        )
    ]
    start_rows(weights, info[0], plan, sems)
    work.need("x")
    entry_rows(work.x, work.mod, info, 3, work.entry)
    work.flush("entry")
    work.need("text")
    wait_rows(weights, plan, sems, range(0, 4))
    work.kv[0] = dot_nt(work.text[...], work.wk[...]).astype(BF)
    wait_rows(weights, plan, sems, range(4, 8))
    work.kv[1] = (dot_nt(work.text[...], work.wv[...]) + work.biases[5:6, :]).astype(BF)
    work.flush("kv")
    wait_rows(weights, plan, sems, range(8, 12))
    work.q[...] = (dot_nt(work.entry[...], work.wq[...]) + work.biases[3:4, :]).astype(BF)
    work.flush("q")
    ones = jnp.ones((LANES, LANES), BF)
    logs, mixed = work.logs, work.mixed
    logs[...] = jnp.zeros(logs.shape, F32)

    def step(pair, carry):
        lanes = pair_lanes(pair)
        for block in range(mixed.shape[0] // UNIT):
            span = pl.ds(block * UNIT, UNIT)
            own = pl.ds(pl.multiple_of(info[1 + block] * LANES, LANES), LANES)
            mixed[span, lanes] = soft_pair(
                work,
                work.q[span, lanes],
                work.kv[0, own, lanes],
                jnp.concatenate([work.kv[1, own, lanes], ones], axis=1),
                None,
                logs,
                pair,
                span,
                words,
            ).astype(BF)
        return carry

    lax.fori_loop(0, mixed.shape[1] // LANES, step, 0, unroll=2)
    work.flush("mixed")
    work.lse[...] = logs[...].T[: work.lse.shape[0], :]
    work.flush("lse")
    wait_rows(weights, plan, sems, range(12, 16))
    work.sum[...] = dot_nn(mixed[...], work.wo[...]) + work.bias[...].astype(F32)
    residual_rows(work.x, work.mod, info, 5, work.sum, work.branch, work.out)
    work.flush("branch")
    work.flush("out")


def hidden_plan(refs, buffer):
    rows = buffer.shape[1]
    half = rows // 2
    return [
        (shard, row, half, buffer.at[shard, pl.ds(row, half)])
        for shard in range(4)
        for row in range(0, rows, half)
    ]


def start_chip(info, refs, layer, buffer, sems):
    copies = [
        pltpu.make_async_copy(ref.at[layer], buffer.at[(info[5] + i) % 2], sems.at[i])
        for i, ref in enumerate(refs)
    ]
    for copy in copies:
        copy.start()
    return copies


def bend_rows(before, bias, active, slope, lanes):
    for row in range(0, before.shape[0], CHUNK):
        span = pl.ds(row, CHUNK)
        values = before[span, :] + bias
        square = values * values
        half = 1.0 / (1.0 + jnp.exp(values * (-2.0 * ROOT - (2.0 * ROOT * CUBIC) * square)))
        act = values * half
        active[span, lanes] = act.astype(BF)
        slope[span, lanes] = (
            half + act * (1.0 - half) * (2.0 * ROOT + (6.0 * ROOT * CUBIC) * square)
        ).astype(BF)


def columns_of(shard, width):
    return pl.ds(pl.multiple_of(shard * width, width), width)


def start_hidden(info, work, weights, layer):
    if len(weights) == 4:
        ups = start_chip(info, weights[:2], layer, work.up, work.sems)
        downs = start_chip(info, weights[2:], layer, work.down, work.down_sems)
        return [lambda some=some: [copy.wait() for copy in some] for some in (ups, downs)]
    waits = []
    for refs, buffer, sems in (
        (weights[:6], work.up, work.sems),
        (weights[6:12], work.down, work.down_sems),
    ):
        refs = [ref.at[layer] for ref in refs[:2]] + list(refs[2:])
        plan = hidden_plan(refs, buffer)
        start_rows(refs, info[0], plan, sems)
        waits.append(
            lambda refs=refs, plan=plan, sems=sems: wait_rows(refs, plan, sems, range(len(plan)))
        )
    return waits


def hidden_kernel(info, work, weights, layer):
    waits = start_hidden(info, work, weights, layer)
    width = work.x.shape[1]
    shards = work.up.shape[0]
    first = info[6] * 2 if shards == 2 else 0
    work.need("x")
    entry_rows(work.x, work.mod, info, 6, work.entry)
    work.flush("entry")
    for wait in waits:
        wait()
    start = 0.0 if shards == 2 else work.bias[...].astype(F32)
    work.sum[...] = jnp.zeros(work.sum.shape, F32) + start

    def step(shard, carry):
        lanes = columns_of(shard, width)
        bias = work.up_bias[:, columns_of(first + shard, width)]
        work.before[...] = dot_nn(work.entry[...], work.up[shard])
        bend_rows(work.before, bias, work.active, work.slope, lanes)
        work.sum[...] += dot_nn(work.active[:, lanes], work.down[shard])
        return carry

    lax.fori_loop(0, shards, step, 0)
    work.flush("active")
    work.flush("slope")
    if shards == 2:
        work.part[...] = work.sum[...].astype(BF)
        work.flush("part")
        return
    low = work.low if work.has("low") else None
    residual_rows(work.x, work.mod, info, 8, work.sum, work.branch, work.out, low)
    work.flush("branch")
    work.flush("out")
    if low is not None:
        work.flush("low")


def hidden_back_kernel(info, work, weights, layer):
    waits = start_hidden(info, work, weights, layer)
    width = work.g.shape[1]
    shards = work.up.shape[0]
    if shards == 4:
        actives = [
            pltpu.make_async_copy(
                weights[12].at[:, columns_of(rank, width)], work.acts.at[i], work.act_sems.at[i]
            )
            for i, rank in enumerate((info[7], info[5]))
        ]
        for copy in actives:
            copy.start()
    work.stats[...] = jnp.zeros(work.stats.shape, F32)
    stats = work.stats.at[pl.ds(48, 24)]
    work.need("g", "branch")
    gate_back(work.g, work.mod, info, 8, work.branch, work.gb, stats)
    work.need("slope")
    for wait in waits:
        wait()
    work.de[...] = jnp.zeros(work.de.shape, F32)
    first = info[6] * 2 if shards == 2 else 0

    def step(shard, carry):
        lanes = columns_of(shard, width)
        work.before[...] = dot_nt(work.gb[...], work.down[shard])
        sums = jnp.zeros((8, width), F32)
        for row in range(0, work.g.shape[0], CHUNK):
            span = pl.ds(row, CHUNK)
            low = (work.before[span, :] * work.slope[span, lanes].astype(F32)).astype(BF)
            work.d_before[span, lanes] = low
            sums += fold(low.astype(F32))
        stats[pl.ds(13 + first + shard, 1), :] = total(sums)
        work.de[...] += dot_nt(work.d_before[:, lanes], work.up[shard])
        return carry

    lax.fori_loop(0, shards, step, 0)
    if shards == 2:
        work.part[...] = work.de[...].astype(BF)
        work.flush("part")
        work.flush("gb")
        work.flush("d_before")
        return
    work.need("entry")
    left, right = work.entry[...].T, work.gb[...].T
    for name, index, rank in (("send", 0, info[7]), ("keep", 1, info[5])):
        out = work.outs[name][1]
        out[:, :width] = dot_nn(left, work.d_before[:, columns_of(rank, width)]).astype(BF)
        actives[index].wait()
        out[:, width:] = dot_nn(right, work.acts[index]).astype(BF)
        work.flush(name)
    work.need("x")
    norm_back_rows(work.x, work.g, work.de, work.mod, info, 6, work.out, stats)
    work.flush("out")


def hidden_grads_kernel(info, work, weights):
    width = work.entry.shape[1]
    work.need("entry", "d_before", "gb", "active")
    left, right = work.entry[...].T, work.gb[...].T
    for name, shift in (("send", 1), ("keep", 0)):
        out = work.outs[name][1]
        lanes = columns_of((info[5] + shift) % 2, width)
        out[:, :width] = dot_nn(left, work.d_before[:, lanes]).astype(BF)
        out[:, width:] = dot_nn(right, work.active[:, lanes]).astype(BF)
        work.flush(name)


def pair_grads(info, work, members):
    rows = members[0][0].shape[0]
    low = lane_ids(rows) < HEAD_WIDTH
    step = 3 * LANES
    for at in range(len(members) // 2):
        products = [dot_nn(left, right) for left, right in members[2 * at : 2 * at + 2]]
        (a0, a1, a2), (b0, b1, b2) = [
            [p[:, i * LANES : (i + 1) * LANES] for i in range(3)] for p in products
        ]
        even = (a0, b0, jnp.where(low, a1, pltpu.roll(b1, HEAD_WIDTH, 1)))
        a1, b1 = pltpu.roll(a1, HEAD_WIDTH, 1), pltpu.roll(b1, HEAD_WIDTH, 1)
        a2r, b2r = pltpu.roll(a2, HEAD_WIDTH, 1), pltpu.roll(b2, HEAD_WIDTH, 1)
        odd = (jnp.where(low, a1, a2r), jnp.where(low, b1, b2r), jnp.where(low, a2r, b2))
        first = info[5] % 2 == 0
        for i, (mine, other) in enumerate(zip(even, odd)):
            lanes = pl.ds(at * step + i * LANES, LANES)
            work.outs["keep"][1][:, lanes] = jnp.where(first, mine, other).astype(BF)
            work.outs["send"][1][:, lanes] = jnp.where(first, other, mine).astype(BF)
    work.flush("send")
    work.flush("keep")


def chip_lanes(info, width):
    return pl.ds(pl.multiple_of(info[6] * (width // 2), width // 2), width // 2)


def query_output_kernel(info, work, weights):
    work.need("entry", "gb", "dq", "mixed")
    lanes = chip_lanes(info, work.dq.shape[1])
    pair_grads(
        info,
        work,
        [
            (work.entry[...].T, work.dq[:, lanes]),
            (work.gb[...].T, work.mixed[:, lanes]),
        ],
    )


def cross_back_kernel(info, work, weights, words):
    rows = weights[0].shape[0] // 4
    sems = work.sems
    plan = [
        (shard, (3 * rows, 0)[i // 4], count, dst)
        for i, (shard, _, count, dst) in enumerate(plan_of((work.wo, work.wq), 0, rows))
    ]
    start_rows(weights, info[0], plan, sems)
    work.stats[...] = work.early[...]
    stats = work.stats.at[pl.ds(24, 24)]
    g = work.g
    work.need("g")
    if work.takes("part"):
        work.need("part", "other", "above")
        for row in range(0, g.shape[0], CHUNK):
            span = pl.ds(row, CHUNK)
            work.de[span, :] = work.part[span, :].astype(F32) + work.other[span, :].astype(F32)
        g = work.g_mid
        norm_back_rows(
            work.above, work.g, work.de, work.mod, info, 6, g, work.stats.at[pl.ds(48, 24)]
        )
    work.need("branch")
    gate_back(g, work.mod, info, 5, work.branch, work.gb, stats)
    wait_rows(weights, plan, sems, range(0, 4))
    work.d_mixed[...] = dot_nt(work.gb[...], work.wo[...]).astype(BF)
    work.dkv_sum[...] = jnp.zeros(work.dkv_sum.shape, F32)
    real = lax.broadcasted_iota(jnp.int32, (LANES, UNIT), 0) < words
    work.need("q", "kv", "lse")

    def step(pair, carry):
        lanes = pair_lanes(pair)
        for block in range(work.q.shape[0] // UNIT):
            span = pl.ds(block * UNIT, UNIT)
            own = pl.ds(pl.multiple_of(info[1 + block] * LANES, LANES), LANES)
            q_pair = work.q[span, lanes]
            d_pair = work.d_mixed[span, lanes]
            keys = work.kv[0, own, lanes]
            values = work.kv[1, own, lanes]
            lefts, grads, probs_low, scores_low = [], [], [], []
            for half in range(2):
                left = (head_half(q_pair, half) * HEAD_WIDTH**-0.5).astype(BF)
                grad = head_half(d_pair, half).astype(BF)
                logs = work.lse[pl.ds(2 * pair + half, 1), span]
                probs = jnp.where(real, jnp.exp(dot_nt(keys, left) - logs), 0.0)
                d_probs = dot_nt(values, grad)
                inner = jnp.sum(probs * d_probs, axis=0, keepdims=True)
                lefts.append(left)
                grads.append(grad)
                probs_low.append(probs.astype(BF))
                scores_low.append((probs * (d_probs - inner)).astype(BF))
            wide_scores = jnp.concatenate(scores_low, axis=1)
            grad_v = dot_nn(jnp.concatenate(probs_low, axis=1), jnp.concatenate(grads, axis=0))
            grad_k = dot_nn(wide_scores, jnp.concatenate(lefts, axis=0))
            grad_q = dot_nn(turned_halves(keys), jnp.concatenate(scores_low, axis=0))
            work.dq[span, lanes] = (grad_q.T * HEAD_WIDTH**-0.5).astype(BF)
            work.dkv_sum[0, own, lanes] += grad_k
            work.dkv_sum[1, own, lanes] += grad_v
        return carry

    lax.fori_loop(0, work.q.shape[1] // LANES, step, 0, unroll=2)
    work.dkv[...] = work.dkv_sum[...].astype(BF)
    work.need("entry", "text", "mixed")
    lanes = chip_lanes(info, work.dq.shape[1])
    text = work.text[...].T
    pair_grads(
        info,
        work,
        [
            (work.entry[...].T, work.dq[:, lanes]),
            (text, work.dkv[0, :, lanes]),
            (text, work.dkv[1, :, lanes]),
            (work.gb[...].T, work.mixed[:, lanes]),
        ],
    )
    stats[13:14, :] = total(fold(work.dq[...].astype(F32)))
    stats[14:15, :] = total(fold(work.dkv[1].astype(F32)))
    wait_rows(weights, plan, sems, range(4, 8))
    work.de[...] = dot_nn(work.dq[...], work.wq[...])
    work.need("x")
    norm_back_rows(work.x, g, work.de, work.mod, info, 3, work.out, stats)
    work.flush("out")


def self_back_kernel(info, work, weights):
    rows = weights[0].shape[0] // 4
    sems = work.sems
    plan = [(s, 3 * rows, rows, work.wo.at[pl.ds(s * rows, rows)]) for s in range(4)]
    start_rows(weights, info[0], plan, sems)
    work.stats[...] = work.early[...]
    stats = work.stats.at[pl.ds(0, 24)]
    work.need("g", "branch")
    gate_back(work.g, work.mod, info, 2, work.branch, work.gb, stats)
    work.flush("gb")
    share = work.g.shape[0]
    blocks = share // UNIT
    marks = key_marks([info[1 + b] for b in range(2 * blocks)])
    wait_rows(weights, plan, sems, range(4))
    work.d_mixed[...] = dot_nt(work.gb[...], work.wo[...]).astype(BF)
    work.need("mixed", "rest", "q", "kv_own", "kv_sib", "lse")
    width = work.q.shape[1]
    head = lax.broadcasted_iota(jnp.int32, (16, width), 0)
    lane = lax.broadcasted_iota(jnp.int32, (16, width), 1)
    first = head * HEAD_WIDTH
    pick = jnp.where((lane >= first) & (lane < first + HEAD_WIDTH), 1.0, 0.0)
    for block in range(blocks):
        span = pl.ds(block * UNIT, UNIT)
        whole = work.mixed[span, :].astype(F32) + work.rest[span, :].astype(F32)
        work.inner[:, span] = lax.dot_general(
            pick,
            whole * work.d_mixed[span, :].astype(F32),
            (((1,), (1,)), ((), ())),
            precision=lax.Precision.HIGHEST,
            preferred_element_type=F32,
        )

    def both(which, lanes):
        return jnp.concatenate([work.kv_own[which, :, lanes], work.kv_sib[which, :, lanes]], axis=0)

    def step(pair, carry):
        lanes = pair_lanes(pair)
        keys = both(0, lanes)
        values = both(1, lanes)
        marked = jnp.concatenate([keys, marks], axis=1)
        turned = turned_halves(keys)
        lefts, grads, probs_low, scores_low = [], [], [], []
        for block in range(blocks):
            span = pl.ds(block * UNIT, UNIT)
            q_pair = work.q[span, lanes]
            d_pair = work.d_mixed[span, lanes]
            ends = query_marks(info[1 + block])
            for half in range(2):
                left = (head_half(q_pair, half) * HEAD_WIDTH**-0.5).astype(BF)
                grad = head_half(d_pair, half).astype(BF)
                logs = work.lse[pl.ds(2 * pair + half, 1), span]
                probs = jnp.exp(dot_nt(marked, jnp.concatenate([left, ends], axis=1)) - logs)
                d_probs = dot_nt(values, grad)
                inner = work.inner[pl.ds(2 * pair + half, 1), span]
                lefts.append(left)
                grads.append(grad)
                probs_low.append(probs.astype(BF))
                scores_low.append((probs * (d_probs - inner)).astype(BF))
            grad_q = dot_nn(turned, jnp.concatenate(scores_low[-2:], axis=0))
            work.dq[span, lanes] = (grad_q.T * HEAD_WIDTH**-0.5).astype(BF)
        grad_v = dot_nn(jnp.concatenate(probs_low, axis=1), jnp.concatenate(grads, axis=0))
        grad_k = dot_nn(jnp.concatenate(scores_low, axis=1), jnp.concatenate(lefts, axis=0))
        for which, grad in ((0, grad_k.astype(BF)), (1, grad_v.astype(BF))):
            work.dkv_own[which, :, lanes] = grad[:share]
            work.dkv_give[which, :, lanes] = grad[share:]
        return carry

    lax.fori_loop(0, work.q.shape[1] // LANES, step, 0)
    work.flush("dkv_give")
    work.flush("dkv_own")
    work.flush("dq")


def sum_keys_values(info, work, dkv):
    work.need("dkv_own", "dkv_sib")
    for which in range(2):
        dkv[which] = (
            work.dkv_own[which].astype(F32) + work.dkv_sib[which].astype(F32)
        ).astype(BF)
    work.need("entry")
    lanes = chip_lanes(info, dkv.shape[2])
    entry = work.entry[...].T
    pair_grads(info, work, [(entry, dkv[0, :, lanes]), (entry, dkv[1, :, lanes])])


def kv_grads_kernel(info, work, weights):
    sum_keys_values(info, work, work.dkv)
    work.flush("dkv")


def qkv_back_kernel(info, work, weights):
    rows = weights[0].shape[0] // 4
    sems = work.sems
    plan = plan_of((work.wq, work.wk, work.wv), 0, rows)
    start_rows(weights, info[0], plan, sems)
    work.stats[...] = work.early[...]
    stats = work.stats.at[pl.ds(0, 24)]
    if work.has("send"):
        sum_keys_values(info, work, work.dkv)
    else:
        work.need("dkv")
    work.need("dq")
    stats[13:14, :] = total(fold(work.dq[...].astype(F32)))
    stats[14:15, :] = total(fold(work.dkv[1].astype(F32)))
    wait_rows(weights, plan, sems, range(0, 12))
    work.de[...] = (
        dot_nn(work.dq[...], work.wq[...])
        + dot_nn(work.dkv[0], work.wk[...])
        + dot_nn(work.dkv[1], work.wv[...])
    )
    work.need("x", "g")
    low = work.low if work.has("low") else None
    norm_back_rows(work.x, work.g, work.de, work.mod, info, 0, work.out, stats, low)
    work.flush("out")
    if low is not None:
        work.flush("low")


def merge_kernel(info, *refs, spots, after):
    chains = len(spots)
    ins, outs = refs[: 4 * chains], refs[4 * chains + after :]
    for chain, (result, column) in enumerate(spots):
        for side in range(2):
            received, kept = ins[4 * chain + 2 * side], ins[4 * chain + 2 * side + 1]
            out = outs[2 * result + side]
            lanes = pl.ds(column, received.shape[2])
            out[:, :, lanes] = (received[...].astype(F32) + kept[...].astype(F32)).astype(BF)


def gate(arrays, after):
    count = len(arrays)
    return pl.pallas_call(
        lambda *refs: None,
        out_shape=[shape(*a.shape, dtype=a.dtype) for a in arrays],
        in_specs=[ANY] * (count + len(after)),
        out_specs=[ANY] * count,
        input_output_aliases={i: i for i in range(count)},
        cost_estimate=lasting(0.5),
        name="gate",
    )(*arrays, *after)


def pack_kernel(info, *refs, groups, whole, after):
    count = sum(len(members) for _, members in groups)
    sources, rest = refs[:count], refs[count + after :]
    (in_sems, out_sems), rest = rest[-2:], rest[:-2]
    count = len(groups) + sum(whole)
    outs, held = list(rest[:count]), rest[count:]
    owns = [outs.pop(0) if one else None for one in whole]
    spots = []
    at = 0
    for index, (layer, members) in enumerate(groups):
        rows = held[index].shape[0]
        piece_rows = rows // 4
        for quarter in range(4):
            row = quarter * piece_rows
            source = sources[at + quarter * len(members) // 4]
            src = source.at[layer, pl.ds(row % source.shape[1], piece_rows)]
            spots.append((index, quarter, held[index].at[pl.ds(row, piece_rows)], src))
        at += len(members)

    def arriving(place):
        _, _, spot, src = spots[place]
        return pltpu.make_async_copy(src, spot, in_sems.at[place])

    def leaving(index, which):
        if which == 2:
            return pltpu.make_async_copy(held[index], owns[index], out_sems.at[2 * index])
        rows = outs[index].shape[0]
        src = held[index].at[pl.ds(which * rows, rows)]
        return pltpu.make_async_copy(src, outs[index], out_sems.at[2 * index + 1])

    def by_parity(act):
        for parity in range(2):

            @pl.when(info[0] % 2 == parity)
            def _(parity=parity):
                act(parity)

    for place in range(len(spots)):
        arriving(place).start()
    for index in range(len(groups)):
        for quarter in range(4):
            arriving(4 * index + quarter).wait()
        by_parity(lambda parity: leaving(index, parity).start())
        if whole[index]:
            leaving(index, 2).start()
    for index in range(len(groups)):
        by_parity(lambda parity: leaving(index, parity).wait())
        if whole[index]:
            leaving(index, 2).wait()


def mod_kernel(condition, mod, mod_bias, q, v, cq, cv, up, out):
    narrow, units, columns = q.shape[1], up.shape[1], mod.shape[1]
    out[...] = jnp.zeros(out.shape, F32)
    for layer in range(LAYERS):
        row = pl.ds(layer, 1)
        out[layer, 0:SLOTS, 0:columns] = dot_nt(condition[...], mod[layer]) + mod_bias[
            row, :
        ].astype(F32)
        out[layer, 4:5, 0:units] = up[row, :].astype(F32)
        out[layer, 5:6, 0:narrow] = q[row, :].astype(F32)
        out[layer, 6:7, 0:narrow] = v[row, :].astype(F32)
        out[layer, 7:8, 0:narrow] = cq[row, :].astype(F32)
        out[layer, 4:5, 1024 : 1024 + narrow] = cv[row, :].astype(F32)


def assemble_kernel(info, *refs, narrow, units, columns):
    parts, (mods, narrows, ups) = refs[:4], refs[4:]
    narrows[...] = jnp.zeros(narrows.shape, F32)
    for rank in range(4):

        @pl.when(info[5] == rank)
        def _(rank=rank):
            for shard in range(4):
                part = parts[shard ^ rank]
                for layer in range(LAYERS):
                    mods[layer, :, shard * columns : (shard + 1) * columns] = part[
                        layer, 0:SLOTS, 0:columns
                    ]
                    ups[layer, :, shard * units : (shard + 1) * units] = part[layer, 4:5, 0:units]
                    at = slice(shard * narrow, (shard + 1) * narrow)
                    for row, source in ((0, 5), (2, 6), (3, 7)):
                        narrows[layer, row : row + 1, at] = part[
                            layer, source : source + 1, 0:narrow
                        ]
                    narrows[layer, 5:6, at] = part[layer, 4:5, 1024 : 1024 + narrow]


def collect_kernel(info, *refs, narrow, units, columns):
    stats, condition, out = refs[: 2 * LAYERS], refs[2 * LAYERS], refs[2 * LAYERS + 1]
    sums = refs[2 * LAYERS + 2]
    width = stats[0].shape[1]
    work = out
    out = refs[2 * LAYERS + 3]
    out[...] = jnp.zeros(out.shape, F32)
    for layer in range(LAYERS):
        sums[...] = stats[2 * layer][...] + stats[2 * layer + 1][...]
        base = 8 * layer
        out[base + 4 : base + 5, width : 2 * width] = sums[60:61, :]
        out[base + 5 : base + 6, 0:width] = sums[12:13, :]
        out[base + 5 : base + 6, width : 2 * width] = sums[36:37, :]
        for index in range(2):
            out[base + 6 + index : base + 7 + index, 512 : 512 + width] = condition[
                2 * layer + index : 2 * layer + index + 1, :
            ].astype(F32)
        for rank in range(4):

            @pl.when(info[5] == rank)
            def _(rank=rank, base=base):
                first = rank * columns
                for index in range(9):
                    low = max(first, index * width)
                    high = min(first + columns, (index + 1) * width)
                    if low < high:
                        row = (index // 3) * 24 + (index % 3) * 4
                        out[base : base + 4, low - first : high - first] = sums[
                            row : row + 4, low - index * width : high - index * width
                        ]
                out[base + 4 : base + 5, 0:units] = sums[61 + rank : 62 + rank, :]
                own = slice(rank * narrow, (rank + 1) * narrow)
                out[base + 6 : base + 7, 0:narrow] = sums[13:14, own]
                out[base + 6 : base + 7, 256 : 256 + narrow] = sums[14:15, own]
                out[base + 7 : base + 8, 0:narrow] = sums[37:38, own]
                out[base + 7 : base + 8, 256 : 256 + narrow] = sums[38:39, own]
    work[...] = out[...].astype(BF)


def spread_kernel(info, gathered, grad, bias_grad, q, v, cq, cv, up, o1, o2, o3, rows, conditions):
    count = gathered.shape[0]
    columns, part = grad.shape[2], grad.shape[1]
    width, narrow, units = conditions.shape[1], q.shape[1], up.shape[1]
    shift = lax.rem(width - info[8] * part, width)
    for index in range(count):
        for slot in range(SLOTS):
            row = 8 * (slot // 2) + 6 + slot % 2
            conditions[SLOTS * index + slot : SLOTS * index + slot + 1, :] = gathered[
                index ^ info[8], row : row + 1, 512 : 512 + width
            ].astype(F32)
    turned = pltpu.roll(conditions[...], shift, 1)[:, :part].T
    for layer in range(LAYERS):
        base = 8 * layer
        sums = jnp.zeros((8, gathered.shape[2]), F32)
        for index in range(count):
            values = gathered[index ^ info[8]].astype(F32)[base : base + 8]
            sums += values
            rows[SLOTS * index : SLOTS * (index + 1), :] = values[0:SLOTS, 0:columns]
        grad[layer] = jnp.dot(
            turned, rows[...], precision=lax.Precision.HIGHEST, preferred_element_type=F32
        )
        at = slice(layer, layer + 1)
        bias_grad[at, :] = jnp.sum(sums[0:SLOTS, 0:columns], axis=0, keepdims=True)
        up[at, :] = sums[4:5, 0:units]
        q[at, :] = sums[6:7, 0:narrow]
        v[at, :] = sums[6:7, 256 : 256 + narrow]
        cq[at, :] = sums[7:8, 0:narrow]
        cv[at, :] = sums[7:8, 256 : 256 + narrow]
        for out, row, lane in ((o1, 5, 0), (o2, 5, width), (o3, 4, width)):
            own = jnp.broadcast_to(sums[row : row + 1, lane : lane + width], (8, width))
            out[at, :] = pltpu.roll(own, shift, 1)[0:1, :part]


def finish_kernel(*refs, wide, spots):
    parts, outs = refs[: 2 * len(spots)], refs[2 * len(spots) :]
    step = 3 * LANES
    for chain, places in enumerate(spots):
        values = parts[2 * chain][0].astype(F32) + parts[2 * chain + 1][0].astype(F32)
        at = 0
        for layer, pair in places:
            if wide:
                width = outs[0].shape[2]
                for out in outs:
                    out[layer] = values[:, at : at + width]
                    at += width
                continue
            both = values[:, at : at + step]
            at += step
            first = jnp.concatenate(
                [both[:, :LANES], both[:, 2 * LANES : 2 * LANES + HEAD_WIDTH]], axis=1
            )
            second = jnp.concatenate(
                [both[:, LANES : 2 * LANES], both[:, 2 * LANES + HEAD_WIDTH :]], axis=1
            )
            for out, matrix in zip(outs[2 * pair : 2 * pair + 2], (first, second)):
                out[layer] = matrix if out.shape[1:] == matrix.shape else matrix.T


def join_kernel(info, rows, other, out):
    share = rows.shape[0]
    for core in range(2):

        @pl.when(info[5] % 2 == core)
        def _(core=core):
            out[pl.ds(core * share, share), :] = rows[...]
            out[pl.ds((1 - core) * share, share), :] = other[...]


def tensor_hop(values, step):
    return lax.ppermute(values, "tensor", [(i, i ^ step) for i in range(4)])


def dp_hop(values, step):
    size = lax.axis_size("dp")
    return lax.ppermute(values, "dp", [(i, i ^ step) for i in range(size)])


def time_features(moments, width):
    half = width // 2
    rates = jnp.exp(-math.log(10000.0) * jnp.arange(half, dtype=F32) / half)
    angles = moments.astype(F32)[:, None] * rates[None, :]
    return jnp.concatenate([jnp.cos(angles), jnp.sin(angles)], axis=1)


def shards(
    tokens,
    text,
    timesteps,
    item_frames,
    cotangent,
    self_query,
    self_query_bias,
    self_key,
    self_value,
    self_value_bias,
    self_output,
    self_output_bias,
    cross_query,
    cross_query_bias,
    cross_key,
    cross_value,
    cross_value_bias,
    cross_output,
    cross_output_bias,
    hidden_up,
    hidden_up_bias,
    hidden_down,
    hidden_down_bias,
    modulation,
    modulation_bias,
):
    frames, width = tokens.shape
    words = text.shape[1]
    columns = modulation.shape[2]
    narrow = self_query.shape[2]
    units = hidden_up.shape[2]
    rank = lax.axis_index("tensor")
    me = lax.axis_index("dp")
    size = lax.axis_size("dp")
    core = rank % 2
    share = frames // 2
    blocks = share // UNIT
    unit = width // size
    turn = lambda values: jnp.swapaxes(values, 1, 2)

    order = jnp.arange(SLOTS, dtype=jnp.int32)
    ends = jnp.sum(jnp.where(order[:, None] <= order[None, :], item_frames[:, None], 0), axis=0)
    turned = (jnp.arange(frames // UNIT, dtype=jnp.int32) + core * blocks) % (2 * blocks)
    slots = jnp.sum((turned[:, None] * UNIT >= ends[None, :]).astype(jnp.int32), axis=1)
    places = jnp.stack([rank, rank // 2, rank ^ 1, me]).astype(jnp.int32)
    info = jnp.concatenate([(rank * 2 + me % 2)[None].astype(jnp.int32), slots, places])

    def pack(members, whole, after=()):
        rows = [sum(a.shape[1] for a in some) for _, some in members]
        outs = [shape(r, width, dtype=BF) for r, one in zip(rows, whole) if one]
        outs += [shape(r // 2, width, dtype=BF) for r in rows]
        arrays = [a for _, some in members for a in some]
        results = pl.pallas_call(
            partial(
                pack_kernel,
                groups=[(layer, [None] * len(some)) for layer, some in members],
                whole=whole,
                after=len(after),
            ),
            out_shape=outs,
            in_specs=[SMALL] + [ANY] * (len(arrays) + len(after)),
            out_specs=[ANY] * len(outs),
            scratch_shapes=[
                *[pltpu.VMEM((r, width), BF) for r in rows],
                pltpu.SemaphoreType.DMA((4 * len(members),)),
                pltpu.SemaphoreType.DMA((2 * len(members),)),
            ],
            compiler_params=pltpu.CompilerParams(vmem_limit_bytes=VMEM_BYTES),
            cost_estimate=lasting(1.0),
            name="pack_weights",
        )(info, *arrays, *after)
        return list(results[: sum(whole)]), list(results[sum(whole) :])

    selfs = [turn(self_query), turn(self_key), turn(self_value), self_output]
    crosses = [turn(cross_query), turn(cross_key), turn(cross_value), cross_output]
    own0, first0 = pack([(0, selfs)], [True])

    condition = jax.nn.silu(time_features(timesteps, width)).astype(BF)
    mine = plain(
        mod_kernel,
        "modulation_rows",
        None,
        [
            condition,
            turn(modulation),
            modulation_bias,
            self_query_bias,
            self_value_bias,
            cross_query_bias,
            cross_value_bias,
            hidden_up_bias,
        ],
        [shape(LAYERS, 8, -(-columns // LANES) * LANES)],
    )
    own1, first1 = pack(
        [(0, crosses), (1, selfs), (1, crosses), (1, [hidden_up]), (1, [hidden_down])],
        [True, True, True, False, False],
        [mine],
    )
    firsts, owns = first0 + first1, own0 + own1
    others = [tensor_hop(mine, 1), tensor_hop(mine, 2)]
    others.append(tensor_hop(others[0], 2))
    out_biases = [
        b.reshape(LAYERS, 1, width) for b in (self_output_bias, cross_output_bias, hidden_down_bias)
    ]

    count = len(firsts)
    along_x, along_y, over_x, over_y, sibs = [[None] * count for _ in range(5)]

    def leave(index):
        along_x[index] = tensor_hop(firsts[index], 2)

    def swap(index):
        sibs[index] = tensor_hop(owns[index], 1)

    def go_on(index):
        along_y[index] = dp_hop(along_x[index], 1)
        over_x[index] = tensor_hop(along_x[index], 1)

    def end(index):
        over_y[index] = tensor_hop(along_y[index], 1)

    def weights_of(index):
        return [
            owns[index],
            sibs[index],
            along_x[index],
            along_y[index],
            over_x[index],
            over_y[index],
        ]

    def open_gate(after, leaving=(), at_x=(), at_y=(), settled=()):
        places = [(firsts, i) for i in leaving]
        places += [(along_x, i) for i in at_x] + [(along_y, i) for i in at_y] + list(settled)
        opened = gate([values[i] for values, i in places], after)
        for (values, i), array in zip(places, opened):
            values[i] = array
        for i in leaving:
            leave(i)
        for i in at_x:
            go_on(i)
        for i in at_y:
            end(i)
        return list(opened)

    leave(0)
    swap(0)
    open_gate([mine], [], [0])
    open_gate([*others, along_x[0]], [1])
    swap(1)
    go_on(1)
    owns += [hidden_up, hidden_down]
    sibs[4:6] = tensor_hop(hidden_up, 1), tensor_hop(hidden_down, 1)
    mods, narrow_biases, up_biases = plain(
        partial(assemble_kernel, narrow=narrow, units=units, columns=columns),
        "modulation_of_all",
        info,
        [mine, *others],
        [
            shape(LAYERS, SLOTS, 4 * columns),
            shape(LAYERS, 8, 4 * narrow),
            shape(LAYERS, 1, 4 * units),
        ],
        after=[along_x[1]],
    )
    open_gate([mods], [], [], [0])

    text_rows = jnp.pad(text, ((0, 0), (0, LANES - words), (0, 0))).reshape(-1, width)
    whole = pltpu.VMEM((width, width), BF)
    four = pltpu.VMEM((4, width, units), BF)
    two = pltpu.VMEM((2, width, units), BF)
    floats = pltpu.VMEM((share, width), F32)
    lows = pltpu.VMEM((share, width), BF)
    sems = lambda n: pltpu.SemaphoreType.DMA((n,))
    frame_low = shape(share, width, dtype=BF)
    frame_high = shape(share, width)
    frame_wide = shape(share, 4 * units, dtype=BF)
    frame_chip = shape(share, 2 * units, dtype=BF)
    two_low = shape(2, share, width, dtype=BF)
    two_text = shape(2, SLOTS * LANES, width, dtype=BF)
    logs = shape(16, share)
    log_work = pltpu.VMEM((share, LANES), F32)
    stat_shape = shape(72, width)

    x = lax.dynamic_slice_in_dim(tokens, core * share, share).astype(F32)
    kept = []
    for layer in range(LAYERS):
        first = 2 * layer
        mod = (mods, (layer,))
        biases = (narrow_biases, (layer,))
        common = dict(w=pltpu.VMEM((2, width, width), BF), sems=sems(8))
        if layer == 0:
            entry1, kv = run(
                kv_kernel,
                "self_keys_values",
                info,
                dict(x=x),
                dict(mod=mod, biases=biases),
                weights_of(first),
                dict(entry=frame_low, kv=two_low),
                {},
                common,
                [along_x[1], sibs[1], sibs[4], sibs[5]],
                3.0,
            )
        else:
            entry1, kv, x, branch3 = run(
                kv_kernel,
                "residual_keys_values",
                info,
                dict(part=part, other=tensor_hop(part, 2), below=kept[-1]["x2"]),
                dict(
                    mod=mod,
                    mod_below=(mods, (layer - 1,)),
                    bias=(out_biases[2], (layer - 1,)),
                    biases=biases,
                ),
                weights_of(first),
                dict(entry=frame_low, kv=two_low, x=frame_high, branch=frame_low),
                {},
                common | dict(sum=floats),
                opened,
                3.0,
            )
            kept[-1]["branch3"] = branch3
        kv_sib = tensor_hop(kv, 1)
        opened = (
            open_gate([entry1], [2, 3], [], [], [(over_x, 1)])
            if layer == 0
            else open_gate([entry1], [5], [], [], [(over_x, 4), (over_y, 3)])
        )
        (q,) = run(
            q_kernel,
            "self_query",
            info,
            dict(entry=entry1),
            dict(biases=biases),
            weights_of(first),
            dict(q=frame_low),
            {},
            dict(w=whole, sems=sems(4)),
            [],
            15.0,
        )
        x1, mixed1, rest1, lse1, branch1 = run(
            self_kernel,
            "self_attention",
            info,
            dict(q=q, kv_own=kv, kv_sib=kv_sib, x=x),
            dict(mod=mod, bias=(out_biases[0], (layer,))),
            weights_of(first),
            dict(out=frame_high, mixed=frame_low, rest=frame_low, lse=logs, branch=frame_low),
            {},
            dict(wo=whole, logs=log_work, sum=floats, sems=sems(4)),
            opened,
            8.0,
        )
        if layer == 0:
            opened = open_gate([x1], [4], [2], [1], [(along_x, 3)])
            swap(2)
        else:
            opened = open_gate([x1], [], [5], [4])
        x2, entry2, cq, ckv, mixed2, lse2, branch2 = run(
            partial(cross_kernel, words=words),
            "cross_attention",
            info,
            dict(x=x1, text=text_rows),
            dict(mod=mod, biases=biases, bias=(out_biases[1], (layer,))),
            weights_of(first + 1),
            dict(
                out=frame_high,
                entry=frame_low,
                q=frame_low,
                kv=two_text,
                mixed=frame_low,
                lse=logs,
                branch=frame_low,
            ),
            {},
            dict(
                wq=whole, wk=whole, wv=whole, wo=whole, logs=log_work, sum=floats, sems=sems(16)
            ),
            opened,
            6.0,
        )
        if layer == 0:
            opened = open_gate([x2], [], [3], [2], [(over_x, 2), (sibs, 2), (along_x, 4)])
            swap(3)
        else:
            opened = open_gate([x2], [], [], [5], [(over_x, 5), (over_y, 4)])
        if layer == 0:
            part, entry3, active, slope = run(
                lambda info, work, w: hidden_kernel(info, work, w, 0),
                "feed_forward_part",
                info,
                dict(x=x2),
                dict(mod=mod, up_bias=(up_biases, (layer,))),
                [hidden_up, sibs[4], hidden_down, sibs[5]],
                dict(part=frame_low, entry=frame_low, active=frame_chip, slope=frame_chip),
                {},
                dict(
                    up=two, down=two, before=floats, sum=floats, sems=sems(2), down_sems=sems(2)
                ),
                opened,
                5.0,
            )
            opened = open_gate([part], [], [4], [3], [(over_x, 3), (over_y, 2), (sibs, 3)])
            x3 = branch3 = None
        else:
            x3, entry3, active, slope, branch3, low = run(
                lambda info, work, w: hidden_kernel(info, work, w, 1),
                "feed_forward",
                info,
                dict(x=x2),
                dict(mod=mod, up_bias=(up_biases, (layer,)), bias=(out_biases[2], (layer,))),
                weights_of(4) + weights_of(5),
                dict(
                    out=frame_high,
                    entry=frame_low,
                    active=frame_wide,
                    slope=frame_wide,
                    branch=frame_low,
                    low=frame_low,
                ),
                {},
                dict(
                    up=four, down=four, before=floats, sum=floats, sems=sems(8), down_sems=sems(8)
                ),
                opened,
                7.0,
            )
        kept.append(
            dict(
                x=x,
                entry1=entry1,
                q=q,
                kv=kv,
                kv_sib=kv_sib,
                mixed1=mixed1,
                rest1=rest1,
                lse1=lse1,
                branch1=branch1,
                x1=x1,
                entry2=entry2,
                cq=cq,
                ckv=ckv,
                mixed2=mixed2,
                lse2=lse2,
                branch2=branch2,
                x2=x2,
                entry3=entry3,
                active=active,
                slope=slope,
                branch3=branch3,
            )
        )
        x = x3

    def join(rows, *after):
        return plain(
            join_kernel,
            "join_rows",
            info,
            [rows, tensor_hop(rows, 1)],
            [shape(2 * share, width, dtype=BF)],
            after=after,
        )


    chains = {}

    def start(name, send, keep):
        view = (size, unit, send.shape[1])
        chains[name] = (tensor_hop(send, 1).reshape(view), keep.reshape(view), 0)

    def held(*names):
        return [chains[name][1] for name in names]

    def advance(names, after=(), cost=1.5):
        targets = [(n, [n]) if isinstance(n, str) else n for n in names]
        targets = [t for t in targets if 2 ** chains[t[1][0]][2] < size]
        if not targets:
            return
        ins, in_specs, outs, out_specs, spots = [], [], [], [], []
        for result, (_, parts) in enumerate(targets):
            column = 0
            for name in parts:
                received, kept_part, bit = chains[name]
                blocks_left, rows, wide = received.shape
                spots.append((result, column))
                column += wide
                for side in range(2):

                    def at(i, info, bit=bit, side=side):
                        return (0, ((info[8] >> bit) & 1) ^ side, 0, 0)

                    for part in (received, kept_part):
                        ins.append(part.reshape(blocks_left // 2, 2, rows, wide))
                        in_specs.append(pl.BlockSpec((blocks_left // 2, None, rows, wide), at))
            for side in range(2):
                outs.append(shape(blocks_left // 2, rows, column, dtype=BF))
                out_specs.append(
                    pl.BlockSpec((blocks_left // 2, rows, column), lambda i, info: (0, 0, 0))
                )
        results = pl.pallas_call(
            partial(merge_kernel, spots=spots, after=len(after)),
            grid_spec=pltpu.PrefetchScalarGridSpec(
                num_scalar_prefetch=1,
                grid=(1,),
                in_specs=in_specs + [ANY] * len(after),
                out_specs=out_specs,
            ),
            out_shape=outs,
            compiler_params=pltpu.CompilerParams(vmem_limit_bytes=VMEM_BYTES),
            cost_estimate=lasting(cost),
            name="merge_grads",
        )(info, *ins, *after)
        for index, (name, parts) in enumerate(targets):
            bit = chains[parts[0]][2]
            hold, give = results[2 * index : 2 * index + 2]
            for part in parts:
                del chains[part]
            chains[name] = (dp_hop(give, 2**bit), hold, bit + 1)

    g = lax.dynamic_slice_in_dim(cotangent, core * share, share).astype(F32)
    sums = []
    last = LAYERS - 1
    for layer in reversed(range(LAYERS)):
        first = 2 * layer
        k = kept[layer]
        mod = (mods, (layer,))
        above = layer + 1
        f_name, c_name, a_name, s_name = [f"{kind}{layer}" for kind in "fcas"]
        n_name = f"n{above}"

        def grads_out(members):
            return {name: shape(width, members * narrow, dtype=BF) for name in ("send", "keep")}

        more, older = [], []
        if layer < last:
            more = held(f"f{above}", f"c{above}", n_name)
            older = [n_name, f"c{above}"]
        if layer == last:
            send, keep, g, stats = run(
                lambda info, work, w: hidden_back_kernel(info, work, w, 1),
                "feed_forward_back",
                info,
                dict(g=g, branch=k["branch3"], slope=k["slope"], entry=k["entry3"], x=k["x2"]),
                dict(mod=mod),
                weights_of(4) + weights_of(5) + [k["active"]],
                {name: shape(width, 2 * units, dtype=BF) for name in ("send", "keep")}
                | dict(out=frame_high),
                dict(stats=stat_shape),
                dict(
                    up=four,
                    down=four,
                    gb=lows,
                    d_before=pltpu.VMEM((share, 4 * units), BF),
                    acts=pltpu.VMEM((2, share, units), BF),
                    act_sems=sems(2),
                    before=floats,
                    de=floats,
                    sems=sems(8),
                    down_sems=sems(8),
                ),
                more,
                10.0,
            )
            start(f_name, send, keep)
            extra, scratch = {}, {}
        else:
            part, gb, d_before, stats = run(
                lambda info, work, w: hidden_back_kernel(info, work, w, 0),
                "feed_forward_back_part",
                info,
                dict(g=g, branch=k["branch3"], slope=k["slope"]),
                dict(mod=mod),
                [hidden_up, sibs[4], hidden_down, sibs[5]],
                dict(part=frame_low, gb=frame_low, d_before=frame_chip),
                dict(stats=stat_shape),
                dict(
                    up=two, down=two, before=floats, de=floats, sems=sems(2), down_sems=sems(2)
                ),
                more,
                5.0,
            )
            other = tensor_hop(part, 2)
            send, keep = run(
                hidden_grads_kernel,
                "feed_forward_grads",
                info,
                dict(entry=k["entry3"], d_before=d_before, gb=gb, active=k["active"]),
                {},
                [],
                {name: shape(width, 2 * units, dtype=BF) for name in ("send", "keep")},
                {},
                {},
                [gb],
                1.0,
            )
            start(f_name, send, keep)
            output = join(low, gb)
            advance(older, held(f_name), 0.5)
            extra = dict(part=part, other=other, above=k["x2"])
            scratch = dict(g_mid=floats)
        send, keep, g, stats = run(
            partial(cross_back_kernel, words=words),
            "cross_attention_back",
            info,
            dict(
                g=g,
                branch=k["branch2"],
                q=k["cq"],
                kv=k["ckv"],
                lse=k["lse2"],
                entry=k["entry2"],
                text=text_rows,
                mixed=k["mixed2"],
                x=k["x1"],
                **extra,
            ),
            dict(mod=mod, early=(stats, ())),
            weights_of(first + 1),
            grads_out(4) | dict(out=frame_high),
            dict(stats=stat_shape),
            dict(
                wq=whole,
                wo=whole,
                gb=lows,
                dq=lows,
                dkv=pltpu.VMEM(two_text.shape, BF),
                d_mixed=lows,
                de=floats,
                dkv_sum=pltpu.VMEM(two_text.shape, F32),
                sems=sems(8),
                **scratch,
            ),
            held(f_name, *older) + ([output] if layer < last else []),
            60.0,
        )
        start(c_name, send, keep)
        if layer == last:
            advance([f_name], [g])
        else:
            ends = [chains[f"{kind}{above}"][0] for kind in "fc"]
            advance([f_name, n_name], [g, *ends])
        gb1, dq, dkv_own, dkv_give, stats = run(
            self_back_kernel,
            "self_attention_back",
            info,
            dict(
                g=g,
                branch=k["branch1"],
                mixed=k["mixed1"],
                rest=k["rest1"],
                q=k["q"],
                kv_own=k["kv"],
                kv_sib=k["kv_sib"],
                lse=k["lse1"],
            ),
            dict(mod=mod, early=(stats, ())),
            weights_of(first),
            dict(gb=frame_low, dq=frame_low, dkv_own=two_low, dkv_give=two_low),
            dict(stats=stat_shape),
            dict(wo=whole, d_mixed=lows, inner=pltpu.VMEM((16, share), F32), sems=sems(4)),
            held(f_name, c_name, *older),
            13.0,
        )
        dkv_sib = tensor_hop(dkv_give, 1)
        advance([f_name, c_name], [dq, *([chains[n_name][0]] if layer < last else [])])
        send, keep = run(
            query_output_kernel,
            "query_output_grads",
            info,
            dict(entry=k["entry1"], gb=gb1, dq=dq, mixed=k["mixed1"]),
            {},
            [],
            grads_out(2),
            {},
            {},
            held(f_name, c_name),
            15.0,
        )
        start(a_name, send, keep)
        arriving = dict(dkv_own=dkv_own, dkv_sib=dkv_sib, entry=k["entry1"])
        if layer == 0:
            send, keep, dkv = run(
                kv_grads_kernel,
                "keys_values_grads",
                info,
                arriving,
                {},
                [],
                grads_out(2) | dict(dkv=two_low),
                {},
                {},
                held(a_name),
                4.0,
            )
            start(s_name, send, keep)
            rest = f"t{layer}"
            advance([f_name, c_name, (rest, [a_name, s_name])], held(s_name))
            arriving = dict(dkv=dkv)
        results = run(
            qkv_back_kernel,
            "self_qkv_back",
            info,
            arriving | dict(dq=dq, x=k["x"], g=g),
            dict(mod=mod, early=(stats, ())),
            weights_of(first),
            (dict(low=frame_low) if layer == 0 else grads_out(2)) | dict(out=frame_high),
            dict(stats=stat_shape),
            dict(wq=whole, wk=whole, wv=whole, de=floats, sems=sems(12))
            | (dict(dkv=pltpu.VMEM(two_low.shape, BF)) if layer else {}),
            held(f_name, c_name, rest if layer == 0 else a_name),
            6.0,
        )
        g, stats = results[-2:]
        if layer:
            start(s_name, *results[:2])
        if layer:
            advance([f_name, c_name, (f"n{layer}", [a_name, s_name])], [g])
        else:
            advance([c_name, rest], [g, chains[f_name][0]])
        sums = [stats, tensor_hop(stats, 1)] + sums
    vectors = plain(
        partial(collect_kernel, narrow=narrow, units=units, columns=columns),
        "collect_sums",
        info,
        [*sums, condition],
        [shape(16, mine.shape[2], dtype=BF)],
        [pltpu.VMEM(stat_shape.shape, F32), pltpu.VMEM((16, mine.shape[2]), F32)],
        held("t0"),
    )
    gathered, hop = vectors[None], size // 2

    def gather_sums():
        nonlocal gathered, hop
        if hop:
            both = jnp.stack([gathered, dp_hop(gathered, hop)], axis=1)
            gathered = both.reshape(-1, *vectors.shape)
            hop //= 2

    low = results[0]
    while any(2 ** chain[2] < size for chain in chains.values()):
        gather_sums()
        advance(list(chains), held("t0") + [gathered, chains["c0"][0]])
        if low is results[0]:
            (low,) = gate([low], held("t0"))
    input_grad = join(low)
    while hop:
        gather_sums()

    def parts_of(*names):
        return [part.reshape(1, unit, -1) for name in names for part in chains[name][:2]]

    up_grad, down_grad = plain(
        partial(finish_kernel, wide=True, spots=[[(layer, 0)] for layer in range(LAYERS)]),
        "finish_wide",
        None,
        parts_of(*[f"f{layer}" for layer in range(LAYERS)]),
        [shape(LAYERS, unit, units)] * 2,
        after=held("t0"),
    )
    straight, across = shape(LAYERS, unit, narrow), shape(LAYERS, narrow, unit)
    lasts = [[(1, 0), (1, 1)], [(1, 2), (1, 3)]]
    cq_grad, ck_grad, cv_grad, co_grad, q_grad, o_grad, k_grad, v_grad = plain(
        partial(finish_kernel, wide=False, spots=lasts + [[(0, 0), (0, 1)], [(0, 2), (0, 3)]]),
        "finish_narrow",
        None,
        parts_of("c1", "n1", "c0", "t0"),
        [straight, straight, straight, across, straight, across, straight, straight],
    )
    small = plain(
        spread_kernel,
        "spread_sums",
        info,
        [gathered],
        [shape(LAYERS, unit, columns), shape(LAYERS, columns)]
        + [shape(LAYERS, narrow)] * 4
        + [shape(LAYERS, units)]
        + [shape(LAYERS, unit)] * 3,
        [pltpu.VMEM((SLOTS * size, columns), F32), pltpu.VMEM((SLOTS * size, width), F32)],
    )
    mod_grad, mod_bias_grad, q_sum, v_sum, cq_sum, cv_sum, up_sum, o1, o2, o3 = small
    return (
        output,
        input_grad,
        q_grad,
        q_sum,
        k_grad,
        v_grad,
        v_sum,
        o_grad,
        o1,
        cq_grad,
        cq_sum,
        ck_grad,
        cv_grad,
        cv_sum,
        co_grad,
        o2,
        up_grad,
        up_sum,
        turn(down_grad),
        o3,
        mod_grad,
        mod_bias_grad,
    )


def solution(mesh):
    dp, tensor = "dp", "tensor"
    columns, vector = P(None, None, tensor), P(None, tensor)
    matrix, turned, spread = P(None, dp, tensor), P(None, tensor, dp), P(None, dp)
    placed = (
        P(dp, None),
        P(dp, None, None),
        P(dp),
        P(dp),
        P(dp, None),
        columns,
        vector,
        columns,
        columns,
        vector,
        P(None, tensor, None),
        P(),
        columns,
        vector,
        columns,
        columns,
        vector,
        P(None, tensor, None),
        P(),
        columns,
        vector,
        P(None, tensor, None),
        P(),
        columns,
        vector,
    )
    results = (
        P(dp, None),
        P(dp, None),
        matrix,
        vector,
        matrix,
        matrix,
        vector,
        turned,
        spread,
        matrix,
        vector,
        matrix,
        matrix,
        vector,
        turned,
        spread,
        matrix,
        vector,
        turned,
        spread,
        matrix,
        vector,
    )
    return jax.shard_map(
        shards, mesh=mesh, in_specs=placed, out_specs=results, check_vma=False
    )
```

```python
from functools import partial
import math

import jax
import jax.numpy as jnp
from jax import lax
from jax.experimental import pallas as pl
from jax.experimental.pallas import tpu as pltpu
from jax.sharding import PartitionSpec as P

HEAD_WIDTH = 64
UNIT = 256
LAYERS = 2
WINDOW = 1024
EPSILON = 1e-06
LANES = 128
CHUNK = 64
SLOTS = WINDOW // UNIT
FAR = -1e30
VMEM_BYTES = 66_000_000
BF = jnp.bfloat16
F32 = jnp.float32
ROOT = math.sqrt(2.0 / math.pi)
CUBIC = 0.044715


def dot_nn(left, right):
    return jnp.dot(left, right, preferred_element_type=F32)


def dot_nt(left, right):
    return lax.dot_general(left, right, (((1,), (1,)), ((), ())), preferred_element_type=F32)


def dot_tn(left, right):
    return lax.dot_general(left, right, (((0,), (0,)), ((), ())), preferred_element_type=F32)


SMALL = pl.BlockSpec(memory_space=pltpu.SMEM)
NEAR = pl.BlockSpec(memory_space=pltpu.VMEM)
ANY = pl.BlockSpec(memory_space=pl.ANY)


class Work:
    def __init__(self, ins, outs, scratch, in_sems, out_sems):
        self.ins, self.outs, self.scratch, self.out_sems = ins, outs, scratch, out_sems
        self.copies, self.waited, self.flushed = {}, set(), []
        for index, (name, (ref, buffer)) in enumerate(ins.items()):
            self.copies[name] = pltpu.make_async_copy(ref, buffer, in_sems.at[index])
            self.copies[name].start()

    def __getattr__(self, name):
        if name in self.__dict__["ins"]:
            return self.ins[name][1]
        if name in self.__dict__["outs"]:
            return self.outs[name][1]
        return self.__dict__["scratch"][name]

    def has(self, name):
        return name in self.outs

    def takes(self, name):
        return name in self.ins

    def send(self, name, source, *at):
        ref = self.outs[name][0]
        copy = pltpu.make_async_copy(
            source, ref.at[at] if at else ref, self.out_sems.at[len(self.flushed)]
        )
        copy.start()
        self.flushed.append(copy)

    def need(self, *names):
        for name in names:
            if name not in self.waited:
                self.waited.add(name)
                self.copies[name].wait()

    def flush(self, name, *at):
        ref, buffer = self.outs[name]
        if at:
            ref, buffer = ref.at[at], buffer.at[at]
        copy = pltpu.make_async_copy(buffer, ref, self.out_sems.at[len(self.flushed)])
        copy.start()
        self.flushed.append(copy)

    def finish(self):
        self.need(*self.ins)
        for copy in self.flushed:
            copy.wait()


def run(body, name, info, ins, small, weights, outs, small_outs, scratch, after=(), cost=1.0):
    in_names, out_names, names = list(ins), list(outs), list(scratch)
    small_names, small_out_names = list(small), list(small_outs)
    counts = [1, len(in_names), len(small), len(weights), len(after), len(outs), len(small_outs)]

    def kernel(*refs):
        refs = list(refs)
        parts = []
        for count in counts:
            parts.append(refs[:count])
            refs = refs[count:]
        (info_ref,), in_refs, small_refs, weight_refs, _, out_refs, small_out_refs = parts
        in_bufs, refs = refs[: len(in_names)], refs[len(in_names) :]
        out_bufs, refs = refs[: len(out_names)], refs[len(out_names) :]
        rest, (in_sems, out_sems) = refs[:-2], refs[-2:]
        extra = {}
        rest = list(rest)
        for key in names:
            many = isinstance(scratch[key], list)
            size = len(scratch[key]) if many else 1
            extra[key] = rest[:size] if many else rest[0]
            rest = rest[size:]
        for key, ref in zip(small_names, small_refs):
            index = small[key][1]
            extra[key] = ref.at[index] if index else ref
        extra.update(zip(small_out_names, small_out_refs))
        work = Work(
            dict(zip(in_names, zip(in_refs, in_bufs))),
            dict(zip(out_names, zip(out_refs, out_bufs))),
            extra,
            in_sems,
            out_sems,
        )
        body(info_ref, work, weight_refs)
        work.finish()

    buffer = lambda a: pltpu.VMEM(a.shape, a.dtype)
    flat = []
    for value in scratch.values():
        flat += value if isinstance(value, list) else [value]
    results = pl.pallas_call(
        kernel,
        out_shape=[outs[n] for n in out_names] + [small_outs[n] for n in small_out_names],
        in_specs=[SMALL]
        + [ANY] * len(ins)
        + [NEAR] * len(small)
        + [ANY] * (len(weights) + len(after)),
        out_specs=[ANY] * len(outs) + [NEAR] * len(small_outs),
        scratch_shapes=[buffer(ins[n]) for n in in_names]
        + [buffer(outs[n]) for n in out_names]
        + flat
        + [pltpu.SemaphoreType.DMA((max(len(ins), 1),)), pltpu.SemaphoreType.DMA((32,))],
        compiler_params=pltpu.CompilerParams(vmem_limit_bytes=VMEM_BYTES),
        cost_estimate=lasting(cost),
        name=name,
    )(info, *ins.values(), *[array for array, _ in small.values()], *weights, *after)
    return results


def plain(body, name, info, ins, outs, scratch=(), after=()):
    first = len(ins) + (0 if info is None else 1)
    results = pl.pallas_call(
        lambda *refs: body(*refs[:first], *refs[first + len(after) :]),
        out_shape=outs,
        in_specs=([] if info is None else [SMALL]) + [NEAR] * len(ins) + [ANY] * len(after),
        out_specs=[NEAR] * len(outs),
        scratch_shapes=list(scratch),
        compiler_params=pltpu.CompilerParams(vmem_limit_bytes=VMEM_BYTES),
        cost_estimate=lasting(0.05),
        name=name,
    )(*([] if info is None else [info]), *ins, *after)
    return results if len(outs) > 1 else results[0]


def lasting(units):
    return pl.CostEstimate(flops=int(units * 0.4e9), bytes_accessed=1000, transcendentals=0)


def shape(*dims, dtype=F32):
    return jax.ShapeDtypeStruct(dims, dtype)


def start_rows(refs, place, plan, sems):
    own, sib, xa, ya, xb, yb = refs
    half = own.shape[0] // 2
    for rank in range(4):
        for parity in range(2):

            @pl.when(place == rank * 2 + parity)
            def _(rank=rank, parity=parity):
                for index, (shard, row, rows, dst) in enumerate(plan):
                    step = shard ^ rank
                    if step < 2:
                        src = (own, sib)[step].at[pl.ds(row, rows)]
                    else:
                        first, second = ((xa, ya), (xb, yb))[step - 2]
                        part = row // half
                        src = (first if part == parity else second).at[pl.ds(row - part * half, rows)]
                    pltpu.make_async_copy(src, dst, sems.at[index]).start()


def wait_rows(refs, plan, sems, which):
    for index in which:
        _, row, rows, dst = plan[index]
        pltpu.make_async_copy(refs[0].at[pl.ds(0, rows)], dst, sems.at[index]).wait()


def plan_of(buffers, first, rows):
    return [
        (shard, (first + which) * rows, rows, dst.at[pl.ds(shard * rows, rows)])
        for which, dst in enumerate(buffers)
        for shard in range(4)
    ]


def norm_rows(values):
    mean = jnp.mean(values, axis=-1, keepdims=True)
    center = values - mean
    factor = lax.rsqrt(jnp.mean(center * center, axis=-1, keepdims=True) + EPSILON)
    return center * factor, factor


def piece(mod, slot, index):
    width = mod.shape[1] // 9
    return mod[pl.ds(slot, 1), index * width : (index + 1) * width]


def entry_rows(x, mod, info, index, out):
    for block in range(x.shape[0] // UNIT):
        slot = info[1 + block]
        shift = piece(mod, slot, index)
        scale = 1.0 + piece(mod, slot, index + 1)

        def step(turn, carry):
            rows = pl.ds(pl.multiple_of(block * UNIT + turn * CHUNK, CHUNK), CHUNK)
            normed, _ = norm_rows(x[rows, :])
            out[rows, :] = (normed * scale + shift).astype(BF)
            return carry

        lax.fori_loop(0, UNIT // CHUNK, step, 0, unroll=True)


def residual_rows(x, mod, info, index, branch, branch_out, out, low=None):
    for block in range(x.shape[0] // UNIT):
        gate = piece(mod, info[1 + block], index)

        def step(turn, carry):
            rows = pl.ds(pl.multiple_of(block * UNIT + turn * CHUNK, CHUNK), CHUNK)
            values = branch[rows, :]
            branch_out[rows, :] = values.astype(BF)
            result = x[rows, :] + gate * values
            out[rows, :] = result
            if low is not None:
                low[rows, :] = result.astype(BF)
            return carry

        lax.fori_loop(0, UNIT // CHUNK, step, 0, unroll=True)


def fold(values):
    return jnp.sum(values.reshape(values.shape[0] // 8, 8, values.shape[1]), axis=0)


def total(values):
    return jnp.sum(values, axis=0, keepdims=True)


def gate_back(g, mod, info, index, branch, gb, stats):
    width = g.shape[1]
    sums = jnp.zeros((8, width), F32)
    for block in range(g.shape[0] // UNIT):
        slot = info[1 + block]
        gate = piece(mod, slot, index)

        def step(turn, carry):
            rows = pl.ds(pl.multiple_of(block * UNIT + turn * CHUNK, CHUNK), CHUNK)
            grad = g[rows, :]
            low = (gate * grad).astype(BF)
            gb[rows, :] = low
            return (
                carry[0] + fold(low.astype(F32)),
                carry[1] + fold(grad * branch[rows, :].astype(F32)),
            )

        sums, rows_sum = lax.fori_loop(
            0, UNIT // CHUNK, step, (sums, jnp.zeros((8, width), F32)), unroll=True
        )
        stats[pl.ds(8 + slot, 1), :] += total(rows_sum)
    stats[12:13, :] = total(sums)


def norm_back_rows(x, g, de, mod, info, index, out, stats, low=None):
    width = x.shape[1]
    for block in range(x.shape[0] // UNIT):
        slot = info[1 + block]
        scale = 1.0 + piece(mod, slot, index + 1)

        def step(turn, carry):
            rows = pl.ds(pl.multiple_of(block * UNIT + turn * CHUNK, CHUNK), CHUNK)
            normed, factor = norm_rows(x[rows, :])
            grad = de[rows, :]
            inner = grad * normed
            dn = grad * scale
            mean = jnp.mean(dn, axis=-1, keepdims=True)
            along = jnp.mean(dn * normed, axis=-1, keepdims=True)
            result = g[rows, :] + factor * (dn - mean - normed * along)
            out[rows, :] = result
            if low is not None:
                low[rows, :] = result.astype(BF)
            return (carry[0] + fold(grad), carry[1] + fold(inner))

        zero = jnp.zeros((8, width), F32)
        shift_sum, scale_sum = lax.fori_loop(0, UNIT // CHUNK, step, (zero, zero), unroll=True)
        stats[pl.ds(slot, 1), :] += total(shift_sum)
        stats[pl.ds(4 + slot, 1), :] += total(scale_sum)


def lane_ids(rows):
    return lax.broadcasted_iota(jnp.int32, (rows, LANES), 1)


def head_half(values, half):
    ids = lane_ids(values.shape[0])
    keep = ids < HEAD_WIDTH if half == 0 else ids >= HEAD_WIDTH
    return jnp.where(keep, values.astype(F32), 0.0)


def turned_halves(keys):
    turned = keys.T
    low = lax.broadcasted_iota(jnp.int32, turned.shape, 0) < HEAD_WIDTH
    zero = jnp.zeros(turned.shape, turned.dtype)
    return jnp.concatenate([jnp.where(low, turned, zero), jnp.where(low, zero, turned)], axis=1)


def query_marks(slot):
    return jnp.where(lane_ids(UNIT) == slot, 1.0, 0.0).astype(BF)


def key_marks(slots):
    ids = lane_ids(UNIT)
    parts = [jnp.where((ids < SLOTS) & (ids != slot), FAR, 0.0).astype(BF) for slot in slots]
    return jnp.concatenate(parts, axis=0)


def pair_lanes(pair):
    return pl.ds(pl.multiple_of(pair * LANES, LANES), LANES)


def start_own_rows(info, work, whole):
    share = work.rows.shape[0]
    first = pl.multiple_of((info[5] % 2) * share, share)
    copy = pltpu.make_async_copy(whole.at[pl.ds(first, share)], work.rows, work.row_sems.at[0])
    copy.start()
    return copy


def raise_rows(low, out):
    for row in range(0, low.shape[0], CHUNK):
        span = pl.ds(row, CHUNK)
        out[span, :] = low[span, :].astype(F32)


def kv_kernel(info, work, weights):
    rows = weights[0].shape[0] // 4
    plan = plan_of((work.w.at[0], work.w.at[1]), 1, rows)
    start_rows(weights[:6], info[0], plan, work.sems)
    if work.has("branch"):
        work.need("part", "other", "below")
        bias = work.bias[...].astype(F32)
        for row in range(0, work.sum.shape[0], CHUNK):
            span = pl.ds(row, CHUNK)
            work.sum[span, :] = (
                work.part[span, :].astype(F32) + work.other[span, :].astype(F32) + bias
            )
        residual_rows(work.below, work.mod_below, info, 8, work.sum, work.branch, work.x)
        work.flush("branch")
        work.flush("x")
    else:
        start_own_rows(info, work, weights[6]).wait()
        raise_rows(work.rows, work.x)
        work.flush("x")
    entry_rows(work.x, work.mod, info, 0, work.entry)
    work.flush("entry")
    entry = work.entry[...]
    wait_rows(weights, plan, work.sems, range(4))
    work.kv[0] = dot_nt(entry, work.w[0]).astype(BF)
    work.flush("kv", 0)
    wait_rows(weights, plan, work.sems, range(4, 8))
    work.kv[1] = (dot_nt(entry, work.w[1]) + work.biases[2:3, :]).astype(BF)
    work.flush("kv", 1)


def q_kernel(info, work, weights):
    rows = weights[0].shape[0] // 4
    plan = plan_of((work.w,), 0, rows)
    start_rows(weights, info[0], plan, work.sems)
    work.need("entry")
    wait_rows(weights, plan, work.sems, range(4))
    work.q[...] = (dot_nt(work.entry[...], work.w[...]) + work.biases[0:1, :]).astype(BF)
    work.flush("q")


def soft_pair(work, q_pair, keys, values, marks, logs, pair, span, words=None):
    ids = lane_ids(UNIT)
    results = []
    kept = logs[span, :]
    for half in range(2):
        left = (head_half(q_pair, half) * HEAD_WIDTH**-0.5).astype(BF)
        if marks is not None:
            left = jnp.concatenate([left, marks], axis=1)
        scores = dot_nt(left, keys)
        if words is not None:
            scores = jnp.where(ids < words, scores, FAR)
        peak = jnp.max(scores, axis=-1, keepdims=True)
        both = dot_nn(jnp.exp(scores - peak).astype(BF), values)
        sums = both[:, LANES:]
        results.append(both[:, :LANES] / sums)
        kept = jnp.where(ids == 2 * pair + half, peak + jnp.log(sums), kept)
    logs[span, :] = kept
    return jnp.where(ids < HEAD_WIDTH, results[0], results[1])


def self_kernel(info, work, weights):
    rows = weights[0].shape[0] // 4
    sems = work.sems
    plan = [(s, 3 * rows, rows, work.wo.at[pl.ds(s * rows, rows)]) for s in range(4)]
    start_rows(weights, info[0], plan, sems)
    share = work.x.shape[0]
    blocks = share // UNIT
    marks = key_marks([info[1 + b] for b in range(2 * blocks)])
    ones = jnp.ones((2 * share, LANES), BF)
    logs, mixed = work.logs, work.mixed
    logs[...] = jnp.zeros(logs.shape, F32)
    work.need("q", "kv_own", "kv_sib")

    def both(which, lanes):
        return jnp.concatenate([work.kv_own[which, :, lanes], work.kv_sib[which, :, lanes]], axis=0)

    def step(pair, carry):
        lanes = pair_lanes(pair)
        keys = jnp.concatenate([both(0, lanes), marks], axis=1)
        values = jnp.concatenate([both(1, lanes), ones], axis=1)
        for block in range(blocks):
            span = pl.ds(block * UNIT, UNIT)
            values_mixed = soft_pair(
                work,
                work.q[span, lanes],
                keys,
                values,
                query_marks(info[1 + block]),
                logs,
                pair,
                span,
            )
            low = values_mixed.astype(BF)
            mixed[span, lanes] = low
            work.rest[span, lanes] = (values_mixed - low.astype(F32)).astype(BF)
        return carry

    lax.fori_loop(0, mixed.shape[1] // LANES, step, 0)
    work.flush("mixed")
    work.flush("rest")
    work.lse[...] = logs[...].T[: work.lse.shape[0], :]
    work.flush("lse")
    wait_rows(weights, plan, sems, range(4))
    work.sum[...] = dot_nn(mixed[...], work.wo[...]) + work.bias[...].astype(F32)
    work.need("x")
    residual_rows(work.x, work.mod, info, 2, work.sum, work.branch, work.out)
    work.flush("branch")
    work.flush("out")


def cross_kernel(info, work, weights, words):
    rows = weights[0].shape[0] // 4
    sems = work.sems
    order = (1, 2, 0, 3)
    plan = [
        (shard, order[i // 4] * rows, count, dst)
        for i, (shard, _, count, dst) in enumerate(
            plan_of((work.wk, work.wv, work.wq, work.wo), 0, rows)
        )
    ]
    start_rows(weights, info[0], plan, sems)
    work.need("x")
    entry_rows(work.x, work.mod, info, 3, work.entry)
    work.flush("entry")
    work.need("text")
    wait_rows(weights, plan, sems, range(0, 4))
    work.kv[0] = dot_nt(work.text[...], work.wk[...]).astype(BF)
    wait_rows(weights, plan, sems, range(4, 8))
    work.kv[1] = (dot_nt(work.text[...], work.wv[...]) + work.biases[5:6, :]).astype(BF)
    work.flush("kv")
    wait_rows(weights, plan, sems, range(8, 12))
    work.q[...] = (dot_nt(work.entry[...], work.wq[...]) + work.biases[3:4, :]).astype(BF)
    work.flush("q")
    ones = jnp.ones((LANES, LANES), BF)
    logs, mixed = work.logs, work.mixed
    logs[...] = jnp.zeros(logs.shape, F32)

    def step(pair, carry):
        lanes = pair_lanes(pair)
        for block in range(mixed.shape[0] // UNIT):
            span = pl.ds(block * UNIT, UNIT)
            own = pl.ds(pl.multiple_of(info[1 + block] * LANES, LANES), LANES)
            mixed[span, lanes] = soft_pair(
                work,
                work.q[span, lanes],
                work.kv[0, own, lanes],
                jnp.concatenate([work.kv[1, own, lanes], ones], axis=1),
                None,
                logs,
                pair,
                span,
                words,
            ).astype(BF)
        return carry

    lax.fori_loop(0, mixed.shape[1] // LANES, step, 0, unroll=2)
    work.flush("mixed")
    work.lse[...] = logs[...].T[: work.lse.shape[0], :]
    work.flush("lse")
    wait_rows(weights, plan, sems, range(12, 16))
    work.sum[...] = dot_nn(mixed[...], work.wo[...]) + work.bias[...].astype(F32)
    residual_rows(work.x, work.mod, info, 5, work.sum, work.branch, work.out)
    work.flush("branch")
    work.flush("out")


def hidden_plan(refs, buffer):
    rows = buffer.shape[1]
    half = rows // 2
    return [
        (shard, row, half, buffer.at[shard, pl.ds(row, half)])
        for shard in range(4)
        for row in range(0, rows, half)
    ]


def start_chip(info, refs, layer, buffer, sems):
    copies = [
        pltpu.make_async_copy(ref.at[layer], buffer.at[(info[5] + i) % 2], sems.at[i])
        for i, ref in enumerate(refs)
    ]
    for copy in copies:
        copy.start()
    return copies


def bend_rows(before, bias, active, slope, lanes):
    for row in range(0, before.shape[0], CHUNK):
        span = pl.ds(row, CHUNK)
        values = before[span, :] + bias
        square = values * values
        half = 1.0 / (1.0 + jnp.exp(values * (-2.0 * ROOT - (2.0 * ROOT * CUBIC) * square)))
        act = values * half
        active[span, lanes] = act.astype(BF)
        slope[span, lanes] = (
            half + act * (1.0 - half) * (2.0 * ROOT + (6.0 * ROOT * CUBIC) * square)
        ).astype(BF)


def columns_of(shard, width):
    return pl.ds(pl.multiple_of(shard * width, width), width)


def start_hidden(info, work, weights, layer):
    if len(weights) == 4:
        ups = start_chip(info, weights[:2], layer, work.up, work.sems)
        downs = start_chip(info, weights[2:], layer, work.down, work.down_sems)
        return [lambda some=some: [copy.wait() for copy in some] for some in (ups, downs)]
    waits = []
    for refs, buffer, sems in (
        (weights[:6], work.up, work.sems),
        (weights[6:12], work.down, work.down_sems),
    ):
        refs = [ref.at[layer] for ref in refs[:2]] + list(refs[2:])
        plan = hidden_plan(refs, buffer)
        start_rows(refs, info[0], plan, sems)
        waits.append(
            lambda refs=refs, plan=plan, sems=sems: wait_rows(refs, plan, sems, range(len(plan)))
        )
    return waits


def hidden_kernel(info, work, weights, layer):
    waits = start_hidden(info, work, weights, layer)
    width = work.x.shape[1]
    shards = work.up.shape[0]
    first = info[6] * 2
    work.need("x")
    entry_rows(work.x, work.mod, info, 6, work.entry)
    work.flush("entry")
    for wait in waits:
        wait()
    work.sum[...] = jnp.zeros(work.sum.shape, F32)

    def step(shard, carry):
        lanes = columns_of(shard, width)
        bias = work.up_bias[:, columns_of(first + shard, width)]
        work.before[...] = dot_nn(work.entry[...], work.up[shard])
        bend_rows(work.before, bias, work.active, work.slope, lanes)
        work.sum[...] += dot_nn(work.active[:, lanes], work.down[shard])
        return carry

    lax.fori_loop(0, shards, step, 0)
    work.flush("active")
    work.flush("slope")
    work.part[...] = work.sum[...].astype(BF)
    work.flush("part")


def hidden_back_kernel(info, work, weights, layer):
    waits = start_hidden(info, work, weights, layer)
    work.stats[...] = jnp.zeros(work.stats.shape, F32)
    stats = work.stats.at[pl.ds(48, 24)]
    work.need("g", "branch")
    gate_back(work.g, work.mod, info, 8, work.branch, work.gb, stats)
    work.need("slope")
    for wait in waits:
        wait()
    hidden_back_rows(info, work, work.de, stats)
    work.part[...] = work.de[...].astype(BF)
    work.flush("part")
    work.flush("gb")
    work.flush("d_before")


def hidden_back_rows(info, work, de, stats):
    width = work.g.shape[1]
    shards = work.up.shape[0]
    first = info[6] * 2 if shards == 2 else 0
    de[...] = jnp.zeros(de.shape, F32)

    def step(shard, carry):
        lanes = columns_of(shard, width)
        work.before[...] = dot_nt(work.gb[...], work.down[shard])
        sums = jnp.zeros((8, width), F32)
        for row in range(0, work.g.shape[0], CHUNK):
            span = pl.ds(row, CHUNK)
            low = (work.before[span, :] * work.slope[span, lanes].astype(F32)).astype(BF)
            work.d_before[span, lanes] = low
            sums += fold(low.astype(F32))
        stats[pl.ds(13 + first + shard, 1), :] = total(sums)
        de[...] += dot_nt(work.d_before[:, lanes], work.up[shard])
        return carry

    lax.fori_loop(0, shards, step, 0)


def hidden_both_kernel(info, work, weights, layer):
    copy = start_own_rows(info, work, weights[12])
    waits = start_hidden(info, work, weights, layer)
    width = work.x.shape[1]
    work.need("x")
    entry_rows(work.x, work.mod, info, 6, work.entry)
    for wait in waits:
        wait()
    work.sum[...] = jnp.zeros(work.sum.shape, F32) + work.bias[...].astype(F32)

    def step(shard, carry):
        lanes = columns_of(shard, width)
        work.before[...] = dot_nn(work.entry[...], work.up[shard])
        bend_rows(work.before, work.up_bias[:, lanes], work.active, work.slope, lanes)
        work.sum[...] += dot_nn(work.active[:, lanes], work.down[shard])
        return carry

    lax.fori_loop(0, 4, step, 0)
    residual_rows(work.x, work.mod, info, 8, work.sum, work.branch, work.out, work.low)
    work.flush("low")
    work.stats[...] = jnp.zeros(work.stats.shape, F32)
    stats = work.stats.at[pl.ds(48, 24)]
    copy.wait()
    raise_rows(work.rows, work.g)
    gate_back(work.g, work.mod, info, 8, work.branch, work.gb, stats)
    hidden_back_rows(info, work, work.sum, stats)
    left, right = work.entry[...].T, work.gb[...].T
    for name, rank in (("send", info[7]), ("keep", info[5])):
        out = work.outs[name][1]
        lanes = columns_of(rank, width)
        out[:, :width] = dot_nn(left, work.d_before[:, lanes]).astype(BF)
        out[:, width:] = dot_nn(right, work.active[:, lanes]).astype(BF)
        work.flush(name)
    norm_back_rows(work.x, work.g, work.sum, work.mod, info, 6, work.out, stats)
    work.flush("out")


def hidden_grads_kernel(info, work, weights):
    width = work.entry.shape[1]
    work.need("entry", "d_before", "gb", "active")
    left, right = work.entry[...].T, work.gb[...].T
    for name, shift in (("send", 1), ("keep", 0)):
        out = work.outs[name][1]
        lanes = columns_of((info[5] + shift) % 2, width)
        out[:, :width] = dot_nn(left, work.d_before[:, lanes]).astype(BF)
        out[:, width:] = dot_nn(right, work.active[:, lanes]).astype(BF)
        work.flush(name)


def pair_grads(info, work, members):
    rows = members[0][0].shape[0]
    low = lane_ids(rows) < HEAD_WIDTH
    step = 3 * LANES
    for at in range(len(members) // 2):
        products = [dot_nn(left, right) for left, right in members[2 * at : 2 * at + 2]]
        (a0, a1, a2), (b0, b1, b2) = [
            [p[:, i * LANES : (i + 1) * LANES] for i in range(3)] for p in products
        ]
        even = (a0, b0, jnp.where(low, a1, pltpu.roll(b1, HEAD_WIDTH, 1)))
        a1, b1 = pltpu.roll(a1, HEAD_WIDTH, 1), pltpu.roll(b1, HEAD_WIDTH, 1)
        a2r, b2r = pltpu.roll(a2, HEAD_WIDTH, 1), pltpu.roll(b2, HEAD_WIDTH, 1)
        odd = (jnp.where(low, a1, a2r), jnp.where(low, b1, b2r), jnp.where(low, a2r, b2))
        first = info[5] % 2 == 0
        for i, (mine, other) in enumerate(zip(even, odd)):
            lanes = pl.ds(at * step + i * LANES, LANES)
            work.outs["keep"][1][:, lanes] = jnp.where(first, mine, other).astype(BF)
            work.outs["send"][1][:, lanes] = jnp.where(first, other, mine).astype(BF)
    work.flush("send")
    work.flush("keep")


def chip_lanes(info, width):
    return pl.ds(pl.multiple_of(info[6] * (width // 2), width // 2), width // 2)


def query_output_kernel(info, work, weights):
    work.need("entry", "gb", "dq", "mixed")
    lanes = chip_lanes(info, work.dq.shape[1])
    pair_grads(
        info,
        work,
        [
            (work.entry[...].T, work.dq[:, lanes]),
            (work.gb[...].T, work.mixed[:, lanes]),
        ],
    )


def cross_back_kernel(info, work, weights, words):
    rows = weights[0].shape[0] // 4
    sems = work.sems
    plan = [
        (shard, (3 * rows, 0)[i // 4], count, dst)
        for i, (shard, _, count, dst) in enumerate(plan_of((work.wo, work.wq), 0, rows))
    ]
    start_rows(weights, info[0], plan, sems)
    work.stats[...] = work.early[...]
    stats = work.stats.at[pl.ds(24, 24)]
    g = work.g
    work.need("g")
    if work.takes("part"):
        work.need("part", "other", "above")
        for row in range(0, g.shape[0], CHUNK):
            span = pl.ds(row, CHUNK)
            work.de[span, :] = work.part[span, :].astype(F32) + work.other[span, :].astype(F32)
        g = work.g_mid
        norm_back_rows(
            work.above, work.g, work.de, work.mod, info, 6, g, work.stats.at[pl.ds(48, 24)]
        )
    work.need("branch")
    gate_back(g, work.mod, info, 5, work.branch, work.gb, stats)
    wait_rows(weights, plan, sems, range(0, 4))
    work.d_mixed[...] = dot_nt(work.gb[...], work.wo[...]).astype(BF)
    work.dkv_sum[...] = jnp.zeros(work.dkv_sum.shape, F32)
    real = lax.broadcasted_iota(jnp.int32, (LANES, UNIT), 0) < words
    work.need("q", "kv", "lse")

    def step(pair, carry):
        lanes = pair_lanes(pair)
        for block in range(work.q.shape[0] // UNIT):
            span = pl.ds(block * UNIT, UNIT)
            own = pl.ds(pl.multiple_of(info[1 + block] * LANES, LANES), LANES)
            q_pair = work.q[span, lanes]
            d_pair = work.d_mixed[span, lanes]
            keys = work.kv[0, own, lanes]
            values = work.kv[1, own, lanes]
            lefts, grads, probs_low, scores_low = [], [], [], []
            for half in range(2):
                left = (head_half(q_pair, half) * HEAD_WIDTH**-0.5).astype(BF)
                grad = head_half(d_pair, half).astype(BF)
                logs = work.lse[pl.ds(2 * pair + half, 1), span]
                probs = jnp.where(real, jnp.exp(dot_nt(keys, left) - logs), 0.0)
                d_probs = dot_nt(values, grad)
                inner = jnp.sum(probs * d_probs, axis=0, keepdims=True)
                lefts.append(left)
                grads.append(grad)
                probs_low.append(probs.astype(BF))
                scores_low.append((probs * (d_probs - inner)).astype(BF))
            wide_scores = jnp.concatenate(scores_low, axis=1)
            grad_v = dot_nn(jnp.concatenate(probs_low, axis=1), jnp.concatenate(grads, axis=0))
            grad_k = dot_nn(wide_scores, jnp.concatenate(lefts, axis=0))
            grad_q = dot_nn(turned_halves(keys), jnp.concatenate(scores_low, axis=0))
            work.dq[span, lanes] = (grad_q.T * HEAD_WIDTH**-0.5).astype(BF)
            work.dkv_sum[0, own, lanes] += grad_k
            work.dkv_sum[1, own, lanes] += grad_v
        return carry

    lax.fori_loop(0, work.q.shape[1] // LANES, step, 0, unroll=2)
    work.dkv[...] = work.dkv_sum[...].astype(BF)
    work.need("entry", "text", "mixed")
    lanes = chip_lanes(info, work.dq.shape[1])
    text = work.text[...].T
    pair_grads(
        info,
        work,
        [
            (work.entry[...].T, work.dq[:, lanes]),
            (text, work.dkv[0, :, lanes]),
            (text, work.dkv[1, :, lanes]),
            (work.gb[...].T, work.mixed[:, lanes]),
        ],
    )
    stats[13:14, :] = total(fold(work.dq[...].astype(F32)))
    stats[14:15, :] = total(fold(work.dkv[1].astype(F32)))
    wait_rows(weights, plan, sems, range(4, 8))
    work.de[...] = dot_nn(work.dq[...], work.wq[...])
    work.need("x")
    norm_back_rows(work.x, g, work.de, work.mod, info, 3, work.out, stats)
    work.flush("out")


def self_back_kernel(info, work, weights):
    rows = weights[0].shape[0] // 4
    sems = work.sems
    plan = [(s, 3 * rows, rows, work.wo.at[pl.ds(s * rows, rows)]) for s in range(4)]
    start_rows(weights, info[0], plan, sems)
    work.stats[...] = work.early[...]
    stats = work.stats.at[pl.ds(0, 24)]
    work.need("g", "branch")
    gate_back(work.g, work.mod, info, 2, work.branch, work.gb, stats)
    work.flush("gb")
    share = work.g.shape[0]
    blocks = share // UNIT
    marks = key_marks([info[1 + b] for b in range(2 * blocks)])
    wait_rows(weights, plan, sems, range(4))
    work.d_mixed[...] = dot_nt(work.gb[...], work.wo[...]).astype(BF)
    work.need("mixed", "rest", "q", "kv_own", "kv_sib", "lse")
    width = work.q.shape[1]
    head = lax.broadcasted_iota(jnp.int32, (16, width), 0)
    lane = lax.broadcasted_iota(jnp.int32, (16, width), 1)
    first = head * HEAD_WIDTH
    pick = jnp.where((lane >= first) & (lane < first + HEAD_WIDTH), 1.0, 0.0)
    for block in range(blocks):
        span = pl.ds(block * UNIT, UNIT)
        whole = work.mixed[span, :].astype(F32) + work.rest[span, :].astype(F32)
        work.inner[:, span] = lax.dot_general(
            pick,
            whole * work.d_mixed[span, :].astype(F32),
            (((1,), (1,)), ((), ())),
            precision=lax.Precision.HIGHEST,
            preferred_element_type=F32,
        )

    def both(which, lanes):
        return jnp.concatenate([work.kv_own[which, :, lanes], work.kv_sib[which, :, lanes]], axis=0)

    def step(pair, carry):
        lanes = pair_lanes(pair)
        keys = both(0, lanes)
        values = both(1, lanes)
        marked = jnp.concatenate([keys, marks], axis=1)
        turned = turned_halves(keys)
        lefts, grads, probs_low, scores_low = [], [], [], []
        for block in range(blocks):
            span = pl.ds(block * UNIT, UNIT)
            q_pair = work.q[span, lanes]
            d_pair = work.d_mixed[span, lanes]
            ends = query_marks(info[1 + block])
            for half in range(2):
                left = (head_half(q_pair, half) * HEAD_WIDTH**-0.5).astype(BF)
                grad = head_half(d_pair, half).astype(BF)
                logs = work.lse[pl.ds(2 * pair + half, 1), span]
                probs = jnp.exp(dot_nt(marked, jnp.concatenate([left, ends], axis=1)) - logs)
                d_probs = dot_nt(values, grad)
                inner = work.inner[pl.ds(2 * pair + half, 1), span]
                lefts.append(left)
                grads.append(grad)
                probs_low.append(probs.astype(BF))
                scores_low.append((probs * (d_probs - inner)).astype(BF))
            grad_q = dot_nn(turned, jnp.concatenate(scores_low[-2:], axis=0))
            work.dq[span, lanes] = (grad_q.T * HEAD_WIDTH**-0.5).astype(BF)
        grad_v = dot_nn(jnp.concatenate(probs_low, axis=1), jnp.concatenate(grads, axis=0))
        grad_k = dot_nn(jnp.concatenate(scores_low, axis=1), jnp.concatenate(lefts, axis=0))
        for which, grad in ((0, grad_k.astype(BF)), (1, grad_v.astype(BF))):
            work.dkv_own[which, :, lanes] = grad[:share]
            work.dkv_give[which, :, lanes] = grad[share:]
        return carry

    lax.fori_loop(0, work.q.shape[1] // LANES, step, 0)
    work.flush("dkv_give")
    work.flush("dkv_own")
    work.flush("dq")


def sum_keys_values(info, work, dkv):
    work.need("dkv_own", "dkv_sib")
    for which in range(2):
        dkv[which] = (
            work.dkv_own[which].astype(F32) + work.dkv_sib[which].astype(F32)
        ).astype(BF)
    work.need("entry")
    lanes = chip_lanes(info, dkv.shape[2])
    entry = work.entry[...].T
    pair_grads(info, work, [(entry, dkv[0, :, lanes]), (entry, dkv[1, :, lanes])])


def kv_grads_kernel(info, work, weights):
    sum_keys_values(info, work, work.dkv)
    work.flush("dkv")


def qkv_back_kernel(info, work, weights):
    rows = weights[0].shape[0] // 4
    sems = work.sems
    plan = plan_of((work.wq, work.wk, work.wv), 0, rows)
    start_rows(weights, info[0], plan, sems)
    work.stats[...] = work.early[...]
    stats = work.stats.at[pl.ds(0, 24)]
    if work.has("send"):
        sum_keys_values(info, work, work.dkv)
    else:
        work.need("dkv")
    work.need("dq")
    stats[13:14, :] = total(fold(work.dq[...].astype(F32)))
    stats[14:15, :] = total(fold(work.dkv[1].astype(F32)))
    wait_rows(weights, plan, sems, range(0, 12))
    work.de[...] = (
        dot_nn(work.dq[...], work.wq[...])
        + dot_nn(work.dkv[0], work.wk[...])
        + dot_nn(work.dkv[1], work.wv[...])
    )
    work.need("x", "g")
    low = work.low if work.has("low") else None
    norm_back_rows(work.x, work.g, work.de, work.mod, info, 0, work.out, stats, low)
    work.flush("out")
    if low is not None:
        work.flush("low")


def merge_kernel(info, *refs, spots, after):
    chains = len(spots)
    ins, outs = refs[: 4 * chains], refs[4 * chains + after :]
    for chain, (result, column) in enumerate(spots):
        for side in range(2):
            received, kept = ins[4 * chain + 2 * side], ins[4 * chain + 2 * side + 1]
            out = outs[2 * result + side]
            lanes = pl.ds(column, received.shape[2])
            out[:, :, lanes] = (received[...].astype(F32) + kept[...].astype(F32)).astype(BF)


def gate(arrays, after):
    count = len(arrays)
    return pl.pallas_call(
        lambda *refs: None,
        out_shape=[shape(*a.shape, dtype=a.dtype) for a in arrays],
        in_specs=[ANY] * (count + len(after)),
        out_specs=[ANY] * count,
        input_output_aliases={i: i for i in range(count)},
        cost_estimate=lasting(0.5),
        name="gate",
    )(*arrays, *after)


def pack_kernel(info, *refs, groups, whole, after):
    count = sum(len(members) for _, members in groups)
    sources, rest = refs[:count], refs[count + after :]
    (in_sems, out_sems), rest = rest[-2:], rest[:-2]
    count = len(groups) + sum(whole)
    outs, held = list(rest[:count]), rest[count:]
    owns = [outs.pop(0) if one else None for one in whole]
    spots = []
    at = 0
    for index, (layer, members) in enumerate(groups):
        rows = held[index].shape[0]
        piece_rows = rows // 4
        for quarter in range(4):
            row = quarter * piece_rows
            source = sources[at + quarter * len(members) // 4]
            src = source.at[layer, pl.ds(row % source.shape[1], piece_rows)]
            spots.append((index, quarter, held[index].at[pl.ds(row, piece_rows)], src))
        at += len(members)

    def arriving(place):
        _, _, spot, src = spots[place]
        return pltpu.make_async_copy(src, spot, in_sems.at[place])

    def leaving(index, which):
        if which == 2:
            return pltpu.make_async_copy(held[index], owns[index], out_sems.at[2 * index])
        rows = outs[index].shape[0]
        src = held[index].at[pl.ds(which * rows, rows)]
        return pltpu.make_async_copy(src, outs[index], out_sems.at[2 * index + 1])

    def by_parity(act):
        for parity in range(2):

            @pl.when(info[0] % 2 == parity)
            def _(parity=parity):
                act(parity)

    for place in range(len(spots)):
        arriving(place).start()
    for index in range(len(groups)):
        for quarter in range(4):
            arriving(4 * index + quarter).wait()
        by_parity(lambda parity: leaving(index, parity).start())
        if whole[index]:
            leaving(index, 2).start()
    for index in range(len(groups)):
        by_parity(lambda parity: leaving(index, parity).wait())
        if whole[index]:
            leaving(index, 2).wait()


def mod_kernel(condition, mod, mod_bias, q, v, cq, cv, up, out):
    narrow, units, columns = q.shape[1], up.shape[1], mod.shape[1]
    out[...] = jnp.zeros(out.shape, F32)
    for layer in range(LAYERS):
        row = pl.ds(layer, 1)
        out[layer, 0:SLOTS, 0:columns] = dot_nt(condition[...], mod[layer]) + mod_bias[
            row, :
        ].astype(F32)
        out[layer, 4:5, 0:units] = up[row, :].astype(F32)
        out[layer, 5:6, 0:narrow] = q[row, :].astype(F32)
        out[layer, 6:7, 0:narrow] = v[row, :].astype(F32)
        out[layer, 7:8, 0:narrow] = cq[row, :].astype(F32)
        out[layer, 4:5, 1024 : 1024 + narrow] = cv[row, :].astype(F32)


def assemble_kernel(info, *refs, narrow, units, columns):
    parts, (mods, narrows, ups) = refs[:4], refs[4:]
    narrows[...] = jnp.zeros(narrows.shape, F32)
    for rank in range(4):

        @pl.when(info[5] == rank)
        def _(rank=rank):
            for shard in range(4):
                part = parts[shard ^ rank]
                for layer in range(LAYERS):
                    mods[layer, :, shard * columns : (shard + 1) * columns] = part[
                        layer, 0:SLOTS, 0:columns
                    ]
                    ups[layer, :, shard * units : (shard + 1) * units] = part[layer, 4:5, 0:units]
                    at = slice(shard * narrow, (shard + 1) * narrow)
                    for row, source in ((0, 5), (2, 6), (3, 7)):
                        narrows[layer, row : row + 1, at] = part[
                            layer, source : source + 1, 0:narrow
                        ]
                    narrows[layer, 5:6, at] = part[layer, 4:5, 1024 : 1024 + narrow]


def collect_kernel(info, *refs, narrow, units, columns):
    stats, condition, out = refs[: 2 * LAYERS], refs[2 * LAYERS], refs[2 * LAYERS + 1]
    sums = refs[2 * LAYERS + 2]
    width = stats[0].shape[1]
    work = out
    out = refs[2 * LAYERS + 3]
    out[...] = jnp.zeros(out.shape, F32)
    for layer in range(LAYERS):
        sums[...] = stats[2 * layer][...] + stats[2 * layer + 1][...]
        base = 8 * layer
        out[base + 4 : base + 5, width : 2 * width] = sums[60:61, :]
        out[base + 5 : base + 6, 0:width] = sums[12:13, :]
        out[base + 5 : base + 6, width : 2 * width] = sums[36:37, :]
        for index in range(2):
            out[base + 6 + index : base + 7 + index, 512 : 512 + width] = condition[
                2 * layer + index : 2 * layer + index + 1, :
            ].astype(F32)
        for rank in range(4):

            @pl.when(info[5] == rank)
            def _(rank=rank, base=base):
                first = rank * columns
                for index in range(9):
                    low = max(first, index * width)
                    high = min(first + columns, (index + 1) * width)
                    if low < high:
                        row = (index // 3) * 24 + (index % 3) * 4
                        out[base : base + 4, low - first : high - first] = sums[
                            row : row + 4, low - index * width : high - index * width
                        ]
                out[base + 4 : base + 5, 0:units] = sums[61 + rank : 62 + rank, :]
                own = slice(rank * narrow, (rank + 1) * narrow)
                out[base + 6 : base + 7, 0:narrow] = sums[13:14, own]
                out[base + 6 : base + 7, 256 : 256 + narrow] = sums[14:15, own]
                out[base + 7 : base + 8, 0:narrow] = sums[37:38, own]
                out[base + 7 : base + 8, 256 : 256 + narrow] = sums[38:39, own]
    work[...] = out[...].astype(BF)


def spread_kernel(info, gathered, grad, bias_grad, q, v, cq, cv, up, o1, o2, o3, rows, conditions):
    count = gathered.shape[0]
    columns, part = grad.shape[2], grad.shape[1]
    width, narrow, units = conditions.shape[1], q.shape[1], up.shape[1]
    shift = lax.rem(width - info[8] * part, width)
    for index in range(count):
        for slot in range(SLOTS):
            row = 8 * (slot // 2) + 6 + slot % 2
            conditions[SLOTS * index + slot : SLOTS * index + slot + 1, :] = gathered[
                index ^ info[8], row : row + 1, 512 : 512 + width
            ].astype(F32)
    turned = pltpu.roll(conditions[...], shift, 1)[:, :part].T
    for layer in range(LAYERS):
        base = 8 * layer
        sums = jnp.zeros((8, gathered.shape[2]), F32)
        for index in range(count):
            values = gathered[index ^ info[8]].astype(F32)[base : base + 8]
            sums += values
            rows[SLOTS * index : SLOTS * (index + 1), :] = values[0:SLOTS, 0:columns]
        grad[layer] = jnp.dot(
            turned, rows[...], precision=lax.Precision.HIGHEST, preferred_element_type=F32
        )
        at = slice(layer, layer + 1)
        bias_grad[at, :] = jnp.sum(sums[0:SLOTS, 0:columns], axis=0, keepdims=True)
        up[at, :] = sums[4:5, 0:units]
        q[at, :] = sums[6:7, 0:narrow]
        v[at, :] = sums[6:7, 256 : 256 + narrow]
        cq[at, :] = sums[7:8, 0:narrow]
        cv[at, :] = sums[7:8, 256 : 256 + narrow]
        for out, row, lane in ((o1, 5, 0), (o2, 5, width), (o3, 4, width)):
            own = jnp.broadcast_to(sums[row : row + 1, lane : lane + width], (8, width))
            out[at, :] = pltpu.roll(own, shift, 1)[0:1, :part]


def finish_kernel(*refs, wide, spots):
    parts, outs = refs[: 2 * len(spots)], refs[2 * len(spots) :]
    step = 3 * LANES
    for chain, places in enumerate(spots):
        values = parts[2 * chain][0].astype(F32) + parts[2 * chain + 1][0].astype(F32)
        at = 0
        for layer, pair in places:
            if wide:
                width = outs[0].shape[2]
                for out in outs:
                    out[layer] = values[:, at : at + width]
                    at += width
                continue
            both = values[:, at : at + step]
            at += step
            first = jnp.concatenate(
                [both[:, :LANES], both[:, 2 * LANES : 2 * LANES + HEAD_WIDTH]], axis=1
            )
            second = jnp.concatenate(
                [both[:, LANES : 2 * LANES], both[:, 2 * LANES + HEAD_WIDTH :]], axis=1
            )
            for out, matrix in zip(outs[2 * pair : 2 * pair + 2], (first, second)):
                out[layer] = matrix if out.shape[1:] == matrix.shape else matrix.T


def join_kernel(info, rows, other, out):
    share = rows.shape[0]
    for core in range(2):

        @pl.when(info[5] % 2 == core)
        def _(core=core):
            out[pl.ds(core * share, share), :] = rows[...]
            out[pl.ds((1 - core) * share, share), :] = other[...]


def tensor_hop(values, step):
    return lax.ppermute(values, "tensor", [(i, i ^ step) for i in range(4)])


def dp_hop(values, step):
    size = lax.axis_size("dp")
    return lax.ppermute(values, "dp", [(i, i ^ step) for i in range(size)])


def time_features(moments, width):
    half = width // 2
    rates = jnp.exp(-math.log(10000.0) * jnp.arange(half, dtype=F32) / half)
    angles = moments.astype(F32)[:, None] * rates[None, :]
    return jnp.concatenate([jnp.cos(angles), jnp.sin(angles)], axis=1)


def shards(
    tokens,
    text,
    timesteps,
    item_frames,
    cotangent,
    self_query,
    self_query_bias,
    self_key,
    self_value,
    self_value_bias,
    self_output,
    self_output_bias,
    cross_query,
    cross_query_bias,
    cross_key,
    cross_value,
    cross_value_bias,
    cross_output,
    cross_output_bias,
    hidden_up,
    hidden_up_bias,
    hidden_down,
    hidden_down_bias,
    modulation,
    modulation_bias,
):
    frames, width = tokens.shape
    words = text.shape[1]
    columns = modulation.shape[2]
    narrow = self_query.shape[2]
    units = hidden_up.shape[2]
    rank = lax.axis_index("tensor")
    me = lax.axis_index("dp")
    size = lax.axis_size("dp")
    core = rank % 2
    share = frames // 2
    blocks = share // UNIT
    unit = width // size
    turn = lambda values: jnp.swapaxes(values, 1, 2)

    order = jnp.arange(SLOTS, dtype=jnp.int32)
    ends = jnp.sum(jnp.where(order[:, None] <= order[None, :], item_frames[:, None], 0), axis=0)
    turned = (jnp.arange(frames // UNIT, dtype=jnp.int32) + core * blocks) % (2 * blocks)
    slots = jnp.sum((turned[:, None] * UNIT >= ends[None, :]).astype(jnp.int32), axis=1)
    places = jnp.stack([rank, rank // 2, rank ^ 1, me]).astype(jnp.int32)
    info = jnp.concatenate([(rank * 2 + me % 2)[None].astype(jnp.int32), slots, places])

    def pack(members, whole, after=()):
        rows = [sum(a.shape[1] for a in some) for _, some in members]
        outs = [shape(r, width, dtype=BF) for r, one in zip(rows, whole) if one]
        outs += [shape(r // 2, width, dtype=BF) for r in rows]
        arrays = [a for _, some in members for a in some]
        results = pl.pallas_call(
            partial(
                pack_kernel,
                groups=[(layer, [None] * len(some)) for layer, some in members],
                whole=whole,
                after=len(after),
            ),
            out_shape=outs,
            in_specs=[SMALL] + [ANY] * (len(arrays) + len(after)),
            out_specs=[ANY] * len(outs),
            scratch_shapes=[
                *[pltpu.VMEM((r, width), BF) for r in rows],
                pltpu.SemaphoreType.DMA((4 * len(members),)),
                pltpu.SemaphoreType.DMA((2 * len(members),)),
            ],
            compiler_params=pltpu.CompilerParams(vmem_limit_bytes=VMEM_BYTES),
            cost_estimate=lasting(1.0),
            name="pack_weights",
        )(info, *arrays, *after)
        return list(results[: sum(whole)]), list(results[sum(whole) :])

    selfs = [turn(self_query), turn(self_key), turn(self_value), self_output]
    crosses = [turn(cross_query), turn(cross_key), turn(cross_value), cross_output]
    own0, first0 = pack([(0, selfs)], [True])


    condition = jax.nn.silu(time_features(timesteps, width)).astype(BF)
    mine = plain(
        mod_kernel,
        "modulation_rows",
        None,
        [
            condition,
            turn(modulation),
            modulation_bias,
            self_query_bias,
            self_value_bias,
            cross_query_bias,
            cross_value_bias,
            hidden_up_bias,
        ],
        [shape(LAYERS, 8, -(-columns // LANES) * LANES)],
    )
    own1, first1 = pack(
        [(0, crosses), (1, selfs), (1, crosses), (1, [hidden_up]), (1, [hidden_down])],
        [True, True, True, False, False],
        [mine],
    )
    firsts, owns = first0 + first1, own0 + own1
    others = [tensor_hop(mine, 1), tensor_hop(mine, 2)]
    others.append(tensor_hop(others[0], 2))
    out_biases = [
        b.reshape(LAYERS, 1, width) for b in (self_output_bias, cross_output_bias, hidden_down_bias)
    ]

    count = len(firsts)
    along_x, along_y, over_x, over_y, sibs = [[None] * count for _ in range(5)]

    def leave(index):
        along_x[index] = tensor_hop(firsts[index], 2)

    def swap(index):
        sibs[index] = tensor_hop(owns[index], 1)

    def go_on(index):
        along_y[index] = dp_hop(along_x[index], 1)
        over_x[index] = tensor_hop(along_x[index], 1)

    def end(index):
        over_y[index] = tensor_hop(along_y[index], 1)

    def weights_of(index):
        return [
            owns[index],
            sibs[index],
            along_x[index],
            along_y[index],
            over_x[index],
            over_y[index],
        ]

    def open_gate(after, leaving=(), at_x=(), at_y=(), settled=()):
        places = [(firsts, i) for i in leaving]
        places += [(along_x, i) for i in at_x] + [(along_y, i) for i in at_y] + list(settled)
        opened = gate([values[i] for values, i in places], after)
        for (values, i), array in zip(places, opened):
            values[i] = array
        for i in leaving:
            leave(i)
        for i in at_x:
            go_on(i)
        for i in at_y:
            end(i)
        return list(opened)

    leave(0)
    swap(0)
    open_gate([mine], [], [0])
    open_gate([*others, along_x[0]], [1])
    swap(1)
    go_on(1)
    owns += [hidden_up, hidden_down]
    sibs[4:6] = tensor_hop(hidden_up, 1), tensor_hop(hidden_down, 1)
    mods, narrow_biases, up_biases = plain(
        partial(assemble_kernel, narrow=narrow, units=units, columns=columns),
        "modulation_of_all",
        info,
        [mine, *others],
        [
            shape(LAYERS, SLOTS, 4 * columns),
            shape(LAYERS, 8, 4 * narrow),
            shape(LAYERS, 1, 4 * units),
        ],
        after=[along_x[1]],
    )
    open_gate([mods], [], [], [0])

    text_rows = jnp.pad(text, ((0, 0), (0, LANES - words), (0, 0))).reshape(-1, width)
    whole = pltpu.VMEM((width, width), BF)
    four = pltpu.VMEM((4, width, units), BF)
    two = pltpu.VMEM((2, width, units), BF)
    floats = pltpu.VMEM((share, width), F32)
    lows = pltpu.VMEM((share, width), BF)
    sems = lambda n: pltpu.SemaphoreType.DMA((n,))
    frame_low = shape(share, width, dtype=BF)
    frame_high = shape(share, width)
    frame_wide = shape(share, 4 * units, dtype=BF)
    frame_chip = shape(share, 2 * units, dtype=BF)
    two_low = shape(2, share, width, dtype=BF)
    two_text = shape(2, SLOTS * LANES, width, dtype=BF)
    logs = shape(16, share)
    log_work = pltpu.VMEM((share, LANES), F32)
    stat_shape = shape(72, width)

    kept = []
    for layer in range(LAYERS):
        first = 2 * layer
        mod = (mods, (layer,))
        biases = (narrow_biases, (layer,))
        common = dict(w=pltpu.VMEM((2, width, width), BF), sems=sems(8))
        if layer == 0:
            entry1, kv, x = run(
                kv_kernel,
                "self_keys_values",
                info,
                {},
                dict(mod=mod, biases=biases),
                weights_of(first) + [tokens],
                dict(entry=frame_low, kv=two_low, x=frame_high),
                {},
                common | dict(rows=lows, row_sems=sems(1)),
                [along_x[1], sibs[1], sibs[4], sibs[5]],
                3.0,
            )
        else:
            entry1, kv, x, branch3 = run(
                kv_kernel,
                "residual_keys_values",
                info,
                dict(part=part, other=tensor_hop(part, 2), below=kept[-1]["x2"]),
                dict(
                    mod=mod,
                    mod_below=(mods, (layer - 1,)),
                    bias=(out_biases[2], (layer - 1,)),
                    biases=biases,
                ),
                weights_of(first),
                dict(entry=frame_low, kv=two_low, x=frame_high, branch=frame_low),
                {},
                common | dict(sum=floats),
                opened,
                3.0,
            )
            kept[-1]["branch3"] = branch3
        kv_sib = tensor_hop(kv, 1)
        opened = (
            open_gate([entry1], [2, 3], [], [], [(over_x, 1)])
            if layer == 0
            else open_gate([entry1], [5], [], [], [(over_x, 4), (over_y, 3)])
        )
        (q,) = run(
            q_kernel,
            "self_query",
            info,
            dict(entry=entry1),
            dict(biases=biases),
            weights_of(first),
            dict(q=frame_low),
            {},
            dict(w=whole, sems=sems(4)),
            [],
            15.0,
        )
        x1, mixed1, rest1, lse1, branch1 = run(
            self_kernel,
            "self_attention",
            info,
            dict(q=q, kv_own=kv, kv_sib=kv_sib, x=x),
            dict(mod=mod, bias=(out_biases[0], (layer,))),
            weights_of(first),
            dict(out=frame_high, mixed=frame_low, rest=frame_low, lse=logs, branch=frame_low),
            {},
            dict(wo=whole, logs=log_work, sum=floats, sems=sems(4)),
            opened,
            8.0,
        )
        if layer == 0:
            opened = open_gate([x1], [4], [2], [1], [(along_x, 3)])
            swap(2)
        else:
            opened = open_gate([x1], [], [5], [4])
        x2, entry2, cq, ckv, mixed2, lse2, branch2 = run(
            partial(cross_kernel, words=words),
            "cross_attention",
            info,
            dict(x=x1, text=text_rows),
            dict(mod=mod, biases=biases, bias=(out_biases[1], (layer,))),
            weights_of(first + 1),
            dict(
                out=frame_high,
                entry=frame_low,
                q=frame_low,
                kv=two_text,
                mixed=frame_low,
                lse=logs,
                branch=frame_low,
            ),
            {},
            dict(
                wq=whole, wk=whole, wv=whole, wo=whole, logs=log_work, sum=floats, sems=sems(16)
            ),
            opened,
            6.0,
        )
        if layer == 0:
            opened = open_gate([x2], [], [3], [2], [(over_x, 2), (sibs, 2), (along_x, 4)])
            swap(3)
        else:
            opened = open_gate([x2], [], [], [5], [(over_x, 5), (over_y, 4)])
        if layer == 0:
            part, entry3, active, slope = run(
                lambda info, work, w: hidden_kernel(info, work, w, 0),
                "feed_forward_part",
                info,
                dict(x=x2),
                dict(mod=mod, up_bias=(up_biases, (layer,))),
                [hidden_up, sibs[4], hidden_down, sibs[5]],
                dict(part=frame_low, entry=frame_low, active=frame_chip, slope=frame_chip),
                {},
                dict(
                    up=two, down=two, before=floats, sum=floats, sems=sems(2), down_sems=sems(2)
                ),
                opened,
                5.0,
            )
            opened = open_gate([part], [], [4], [3], [(over_x, 3), (over_y, 2), (sibs, 3)])
            x3 = branch3 = None
        else:
            x3 = branch3 = active = slope = entry3 = None
        kept.append(
            dict(
                x=x,
                entry1=entry1,
                q=q,
                kv=kv,
                kv_sib=kv_sib,
                mixed1=mixed1,
                rest1=rest1,
                lse1=lse1,
                branch1=branch1,
                x1=x1,
                entry2=entry2,
                cq=cq,
                ckv=ckv,
                mixed2=mixed2,
                lse2=lse2,
                branch2=branch2,
                x2=x2,
                entry3=entry3,
                active=active,
                slope=slope,
                branch3=branch3,
            )
        )
        x = x3
    last_gate = opened

    def join(rows, *after):
        return plain(
            join_kernel,
            "join_rows",
            info,
            [rows, tensor_hop(rows, 1)],
            [shape(2 * share, width, dtype=BF)],
            after=after,
        )


    chains = {}

    def start(name, send, keep):
        view = (size, unit, send.shape[1])
        chains[name] = (tensor_hop(send, 1).reshape(view), keep.reshape(view), 0)

    def held(*names):
        return [chains[name][1] for name in names]

    def advance(names, after=(), cost=1.5):
        targets = [(n, [n]) if isinstance(n, str) else n for n in names]
        targets = [t for t in targets if 2 ** chains[t[1][0]][2] < size]
        if not targets:
            return
        ins, in_specs, outs, out_specs, spots = [], [], [], [], []
        for result, (_, parts) in enumerate(targets):
            column = 0
            for name in parts:
                received, kept_part, bit = chains[name]
                blocks_left, rows, wide = received.shape
                spots.append((result, column))
                column += wide
                for side in range(2):

                    def at(i, info, bit=bit, side=side):
                        return (0, ((info[8] >> bit) & 1) ^ side, 0, 0)

                    for part in (received, kept_part):
                        ins.append(part.reshape(blocks_left // 2, 2, rows, wide))
                        in_specs.append(pl.BlockSpec((blocks_left // 2, None, rows, wide), at))
            for side in range(2):
                outs.append(shape(blocks_left // 2, rows, column, dtype=BF))
                out_specs.append(
                    pl.BlockSpec((blocks_left // 2, rows, column), lambda i, info: (0, 0, 0))
                )
        results = pl.pallas_call(
            partial(merge_kernel, spots=spots, after=len(after)),
            grid_spec=pltpu.PrefetchScalarGridSpec(
                num_scalar_prefetch=1,
                grid=(1,),
                in_specs=in_specs + [ANY] * len(after),
                out_specs=out_specs,
            ),
            out_shape=outs,
            compiler_params=pltpu.CompilerParams(vmem_limit_bytes=VMEM_BYTES),
            cost_estimate=lasting(cost),
            name="merge_grads",
        )(info, *ins, *after)
        for index, (name, parts) in enumerate(targets):
            bit = chains[parts[0]][2]
            hold, give = results[2 * index : 2 * index + 2]
            for part in parts:
                del chains[part]
            chains[name] = (dp_hop(give, 2**bit), hold, bit + 1)

    sums = []
    last = LAYERS - 1
    for layer in reversed(range(LAYERS)):
        first = 2 * layer
        k = kept[layer]
        mod = (mods, (layer,))
        above = layer + 1
        f_name, c_name, a_name, s_name = [f"{kind}{layer}" for kind in "fcas"]
        n_name = f"n{above}"

        def grads_out(members):
            return {name: shape(width, members * narrow, dtype=BF) for name in ("send", "keep")}

        older = []
        if layer < last:
            more = held(f"f{above}", f"c{above}", n_name)
            older = [n_name, f"c{above}"]
        if layer == last:
            send, keep, g, low, stats = run(
                lambda info, work, w: hidden_both_kernel(info, work, w, 1),
                "feed_forward_both",
                info,
                dict(x=k["x2"]),
                dict(mod=mod, up_bias=(up_biases, (layer,)), bias=(out_biases[2], (layer,))),
                weights_of(4) + weights_of(5) + [cotangent],
                {name: shape(width, 2 * units, dtype=BF) for name in ("send", "keep")}
                | dict(out=frame_high, low=frame_low),
                dict(stats=stat_shape),
                dict(
                    up=four,
                    down=four,
                    g=floats,
                    rows=lows,
                    row_sems=sems(1),
                    gb=lows,
                    entry=lows,
                    branch=lows,
                    active=pltpu.VMEM((share, 4 * units), BF),
                    slope=pltpu.VMEM((share, 4 * units), BF),
                    d_before=pltpu.VMEM((share, 4 * units), BF),
                    before=floats,
                    sum=floats,
                    sems=sems(8),
                    down_sems=sems(8),
                ),
                last_gate,
                10.0,
            )
            start(f_name, send, keep)
            extra, scratch = {}, {}
        else:
            part, gb, d_before, stats = run(
                lambda info, work, w: hidden_back_kernel(info, work, w, 0),
                "feed_forward_back_part",
                info,
                dict(g=g, branch=k["branch3"], slope=k["slope"]),
                dict(mod=mod),
                [hidden_up, sibs[4], hidden_down, sibs[5]],
                dict(part=frame_low, gb=frame_low, d_before=frame_chip),
                dict(stats=stat_shape),
                dict(
                    up=two, down=two, before=floats, de=floats, sems=sems(2), down_sems=sems(2)
                ),
                more,
                5.0,
            )
            other = tensor_hop(part, 2)
            send, keep = run(
                hidden_grads_kernel,
                "feed_forward_grads",
                info,
                dict(entry=k["entry3"], d_before=d_before, gb=gb, active=k["active"]),
                {},
                [],
                {name: shape(width, 2 * units, dtype=BF) for name in ("send", "keep")},
                {},
                {},
                [gb],
                1.0,
            )
            start(f_name, send, keep)
            output = join(low, gb)
            advance(older, held(f_name), 0.5)
            extra = dict(part=part, other=other, above=k["x2"])
            scratch = dict(g_mid=floats)
        send, keep, g, stats = run(
            partial(cross_back_kernel, words=words),
            "cross_attention_back",
            info,
            dict(
                g=g,
                branch=k["branch2"],
                q=k["cq"],
                kv=k["ckv"],
                lse=k["lse2"],
                entry=k["entry2"],
                text=text_rows,
                mixed=k["mixed2"],
                x=k["x1"],
                **extra,
            ),
            dict(mod=mod, early=(stats, ())),
            weights_of(first + 1),
            grads_out(4) | dict(out=frame_high),
            dict(stats=stat_shape),
            dict(
                wq=whole,
                wo=whole,
                gb=lows,
                dq=lows,
                dkv=pltpu.VMEM(two_text.shape, BF),
                d_mixed=lows,
                de=floats,
                dkv_sum=pltpu.VMEM(two_text.shape, F32),
                sems=sems(8),
                **scratch,
            ),
            held(f_name, *older) + ([output] if layer < last else []),
            60.0,
        )
        start(c_name, send, keep)
        if layer == last:
            advance([f_name], [g])
        else:
            ends = [chains[f"{kind}{above}"][0] for kind in "fc"]
            advance([f_name, n_name], [g, *ends])
        gb1, dq, dkv_own, dkv_give, stats = run(
            self_back_kernel,
            "self_attention_back",
            info,
            dict(
                g=g,
                branch=k["branch1"],
                mixed=k["mixed1"],
                rest=k["rest1"],
                q=k["q"],
                kv_own=k["kv"],
                kv_sib=k["kv_sib"],
                lse=k["lse1"],
            ),
            dict(mod=mod, early=(stats, ())),
            weights_of(first),
            dict(gb=frame_low, dq=frame_low, dkv_own=two_low, dkv_give=two_low),
            dict(stats=stat_shape),
            dict(wo=whole, d_mixed=lows, inner=pltpu.VMEM((16, share), F32), sems=sems(4)),
            held(f_name, c_name, *older),
            13.0,
        )
        dkv_sib = tensor_hop(dkv_give, 1)
        advance([f_name, c_name], [dq])
        send, keep = run(
            query_output_kernel,
            "query_output_grads",
            info,
            dict(entry=k["entry1"], gb=gb1, dq=dq, mixed=k["mixed1"]),
            {},
            [],
            grads_out(2),
            {},
            {},
            held(f_name, c_name),
            15.0,
        )
        start(a_name, send, keep)
        arriving = dict(dkv_own=dkv_own, dkv_sib=dkv_sib, entry=k["entry1"])
        if layer == 0:
            send, keep, dkv = run(
                kv_grads_kernel,
                "keys_values_grads",
                info,
                arriving,
                {},
                [],
                grads_out(2) | dict(dkv=two_low),
                {},
                {},
                held(a_name),
                4.0,
            )
            start(s_name, send, keep)
            rest = f"t{layer}"
            advance([f_name, c_name, (rest, [a_name, s_name])], held(s_name))
            arriving = dict(dkv=dkv)
        results = run(
            qkv_back_kernel,
            "self_qkv_back",
            info,
            arriving | dict(dq=dq, x=k["x"], g=g),
            dict(mod=mod, early=(stats, ())),
            weights_of(first),
            (dict(low=frame_low) if layer == 0 else grads_out(2)) | dict(out=frame_high),
            dict(stats=stat_shape),
            dict(wq=whole, wk=whole, wv=whole, de=floats, sems=sems(12))
            | (dict(dkv=pltpu.VMEM(two_low.shape, BF)) if layer else {}),
            held(f_name, c_name, rest if layer == 0 else a_name),
            6.0,
        )
        g, stats = results[-2:]
        if layer:
            start(s_name, *results[:2])
        if layer:
            advance([f_name, c_name, (f"n{layer}", [a_name, s_name])], [g])
        else:
            to_rest = [g, chains[f_name][0], chains[n_name][0]]
        sums = [stats, tensor_hop(stats, 1)] + sums
    vectors = plain(
        partial(collect_kernel, narrow=narrow, units=units, columns=columns),
        "collect_sums",
        info,
        [*sums, condition],
        [shape(16, mine.shape[2], dtype=BF)],
        [pltpu.VMEM(stat_shape.shape, F32), pltpu.VMEM((16, mine.shape[2]), F32)],
    )
    advance(["c0", "t0"], to_rest + [vectors])
    gathered, hop = vectors[None], size // 2

    def gather_sums():
        nonlocal gathered, hop
        if hop:
            both = jnp.stack([gathered, dp_hop(gathered, hop)], axis=1)
            gathered = both.reshape(-1, *vectors.shape)
            hop //= 2

    low = results[0]
    (low,) = gate([low], held("t0"))
    input_grad = join(low)

    def parts_of(*names):
        return [part.reshape(1, unit, -1) for name in names for part in chains[name][:2]]

    up_grad, down_grad = plain(
        partial(finish_kernel, wide=True, spots=[[(layer, 0)] for layer in range(LAYERS)]),
        "finish_wide",
        None,
        parts_of(*[f"f{layer}" for layer in range(LAYERS)]),
        [shape(LAYERS, unit, units)] * 2,
    )
    ready = [input_grad, up_grad, chains["c0"][0]]
    while any(2 ** chain[2] < size for chain in chains.values()):
        gather_sums()
        advance(list(chains), held("t0") + [gathered] + ready)
    while hop:
        gather_sums()
    straight, across = shape(LAYERS, unit, narrow), shape(LAYERS, narrow, unit)
    lasts = [[(1, 0), (1, 1)], [(1, 2), (1, 3)]]
    cq_grad, ck_grad, cv_grad, co_grad, q_grad, o_grad, k_grad, v_grad = plain(
        partial(finish_kernel, wide=False, spots=lasts + [[(0, 0), (0, 1)], [(0, 2), (0, 3)]]),
        "finish_narrow",
        None,
        parts_of("c1", "n1", "c0", "t0"),
        [straight, straight, straight, across, straight, across, straight, straight],
    )
    small = plain(
        spread_kernel,
        "spread_sums",
        info,
        [gathered],
        [shape(LAYERS, unit, columns), shape(LAYERS, columns)]
        + [shape(LAYERS, narrow)] * 4
        + [shape(LAYERS, units)]
        + [shape(LAYERS, unit)] * 3,
        [pltpu.VMEM((SLOTS * size, columns), F32), pltpu.VMEM((SLOTS * size, width), F32)],
    )
    mod_grad, mod_bias_grad, q_sum, v_sum, cq_sum, cv_sum, up_sum, o1, o2, o3 = small
    return (
        output,
        input_grad,
        q_grad,
        q_sum,
        k_grad,
        v_grad,
        v_sum,
        o_grad,
        o1,
        cq_grad,
        cq_sum,
        ck_grad,
        cv_grad,
        cv_sum,
        co_grad,
        o2,
        up_grad,
        up_sum,
        turn(down_grad),
        o3,
        mod_grad,
        mod_bias_grad,
    )


def solution(mesh):
    dp, tensor = "dp", "tensor"
    columns, vector = P(None, None, tensor), P(None, tensor)
    matrix, turned, spread = P(None, dp, tensor), P(None, tensor, dp), P(None, dp)
    placed = (
        P(dp, None),
        P(dp, None, None),
        P(dp),
        P(dp),
        P(dp, None),
        columns,
        vector,
        columns,
        columns,
        vector,
        P(None, tensor, None),
        P(),
        columns,
        vector,
        columns,
        columns,
        vector,
        P(None, tensor, None),
        P(),
        columns,
        vector,
        P(None, tensor, None),
        P(),
        columns,
        vector,
    )
    results = (
        P(dp, None),
        P(dp, None),
        matrix,
        vector,
        matrix,
        matrix,
        vector,
        turned,
        spread,
        matrix,
        vector,
        matrix,
        matrix,
        vector,
        turned,
        spread,
        matrix,
        vector,
        turned,
        spread,
        matrix,
        vector,
    )
    return jax.shard_map(
        shards, mesh=mesh, in_specs=placed, out_specs=results, check_vma=False
    )
```

```python
from functools import partial
import math

import jax
import jax.numpy as jnp
from jax import lax
from jax.experimental import pallas as pl
from jax.experimental.pallas import tpu as pltpu
from jax.sharding import PartitionSpec as P

HEAD_WIDTH = 64
UNIT = 256
LAYERS = 2
WINDOW = 1024
EPSILON = 1e-06
LANES = 128
CHUNK = 64
SLOTS = WINDOW // UNIT
FAR = -1e30
VMEM_BYTES = 66_000_000
BF = jnp.bfloat16
F32 = jnp.float32
ROOT = math.sqrt(2.0 / math.pi)
CUBIC = 0.044715


def dot_nn(left, right):
    return jnp.dot(left, right, preferred_element_type=F32)


def dot_nt(left, right):
    return lax.dot_general(left, right, (((1,), (1,)), ((), ())), preferred_element_type=F32)


def dot_tn(left, right):
    return lax.dot_general(left, right, (((0,), (0,)), ((), ())), preferred_element_type=F32)


SMALL = pl.BlockSpec(memory_space=pltpu.SMEM)
NEAR = pl.BlockSpec(memory_space=pltpu.VMEM)
ANY = pl.BlockSpec(memory_space=pl.ANY)


class Work:
    def __init__(self, ins, outs, scratch, in_sems, out_sems):
        self.ins, self.outs, self.scratch, self.out_sems = ins, outs, scratch, out_sems
        self.copies, self.waited, self.flushed = {}, set(), []
        for index, (name, (ref, buffer)) in enumerate(ins.items()):
            self.copies[name] = pltpu.make_async_copy(ref, buffer, in_sems.at[index])
            self.copies[name].start()

    def __getattr__(self, name):
        if name in self.__dict__["ins"]:
            return self.ins[name][1]
        if name in self.__dict__["outs"]:
            return self.outs[name][1]
        return self.__dict__["scratch"][name]

    def has(self, name):
        return name in self.outs

    def takes(self, name):
        return name in self.ins

    def send(self, name, source, *at):
        ref = self.outs[name][0]
        copy = pltpu.make_async_copy(
            source, ref.at[at] if at else ref, self.out_sems.at[len(self.flushed)]
        )
        copy.start()
        self.flushed.append(copy)

    def need(self, *names):
        for name in names:
            if name not in self.waited:
                self.waited.add(name)
                self.copies[name].wait()

    def flush(self, name, *at):
        ref, buffer = self.outs[name]
        if at:
            ref, buffer = ref.at[at], buffer.at[at]
        copy = pltpu.make_async_copy(buffer, ref, self.out_sems.at[len(self.flushed)])
        copy.start()
        self.flushed.append(copy)

    def finish(self):
        self.need(*self.ins)
        for copy in self.flushed:
            copy.wait()


class Names:
    def __init__(self, work, **names):
        self.work, self.names = work, names

    def to(self, name):
        return self.__dict__["names"].get(name, name)

    def __getattr__(self, name):
        return getattr(self.__dict__["work"], self.to(name))

    @property
    def outs(self):
        return {name: self.work.outs[self.to(name)] for name in ("send", "keep")}

    def has(self, name):
        return self.work.has(self.to(name))

    def takes(self, name):
        return self.work.takes(self.to(name))

    def need(self, *names):
        self.work.need(*[name for name in map(self.to, names) if self.work.takes(name)])

    def flush(self, name, *at):
        if self.has(name):
            self.work.flush(self.to(name), *at)


def run(body, name, info, ins, small, weights, outs, small_outs, scratch, after=(), cost=1.0):
    in_names, out_names, names = list(ins), list(outs), list(scratch)
    small_names, small_out_names = list(small), list(small_outs)
    counts = [1, len(in_names), len(small), len(weights), len(after), len(outs), len(small_outs)]

    def kernel(*refs):
        refs = list(refs)
        parts = []
        for count in counts:
            parts.append(refs[:count])
            refs = refs[count:]
        (info_ref,), in_refs, small_refs, weight_refs, _, out_refs, small_out_refs = parts
        in_bufs, refs = refs[: len(in_names)], refs[len(in_names) :]
        out_bufs, refs = refs[: len(out_names)], refs[len(out_names) :]
        rest, (in_sems, out_sems) = refs[:-2], refs[-2:]
        extra = {}
        rest = list(rest)
        for key in names:
            many = isinstance(scratch[key], list)
            size = len(scratch[key]) if many else 1
            extra[key] = rest[:size] if many else rest[0]
            rest = rest[size:]
        for key, ref in zip(small_names, small_refs):
            index = small[key][1]
            extra[key] = ref.at[index] if index else ref
        extra.update(zip(small_out_names, small_out_refs))
        work = Work(
            dict(zip(in_names, zip(in_refs, in_bufs))),
            dict(zip(out_names, zip(out_refs, out_bufs))),
            extra,
            in_sems,
            out_sems,
        )
        body(info_ref, work, weight_refs)
        work.finish()

    buffer = lambda a: pltpu.VMEM(a.shape, a.dtype)
    flat = []
    for value in scratch.values():
        flat += value if isinstance(value, list) else [value]
    results = pl.pallas_call(
        kernel,
        out_shape=[outs[n] for n in out_names] + [small_outs[n] for n in small_out_names],
        in_specs=[SMALL]
        + [ANY] * len(ins)
        + [NEAR] * len(small)
        + [ANY] * (len(weights) + len(after)),
        out_specs=[ANY] * len(outs) + [NEAR] * len(small_outs),
        scratch_shapes=[buffer(ins[n]) for n in in_names]
        + [buffer(outs[n]) for n in out_names]
        + flat
        + [pltpu.SemaphoreType.DMA((max(len(ins), 1),)), pltpu.SemaphoreType.DMA((32,))],
        compiler_params=pltpu.CompilerParams(vmem_limit_bytes=VMEM_BYTES),
        cost_estimate=lasting(cost),
        name=name,
    )(info, *ins.values(), *[array for array, _ in small.values()], *weights, *after)
    return results


def plain(body, name, info, ins, outs, scratch=(), after=()):
    first = len(ins) + (0 if info is None else 1)
    results = pl.pallas_call(
        lambda *refs: body(*refs[:first], *refs[first + len(after) :]),
        out_shape=outs,
        in_specs=([] if info is None else [SMALL]) + [NEAR] * len(ins) + [ANY] * len(after),
        out_specs=[NEAR] * len(outs),
        scratch_shapes=list(scratch),
        compiler_params=pltpu.CompilerParams(vmem_limit_bytes=VMEM_BYTES),
        cost_estimate=lasting(0.05),
        name=name,
    )(*([] if info is None else [info]), *ins, *after)
    return results if len(outs) > 1 else results[0]


def lasting(units):
    return pl.CostEstimate(flops=int(units * 0.4e9), bytes_accessed=1000, transcendentals=0)


def shape(*dims, dtype=F32):
    return jax.ShapeDtypeStruct(dims, dtype)


def start_rows(refs, place, plan, sems):
    own, sib, xa, ya, xb, yb = refs
    half = own.shape[0] // 2
    for rank in range(4):
        for parity in range(2):

            @pl.when(place == rank * 2 + parity)
            def _(rank=rank, parity=parity):
                for index, (shard, row, rows, dst) in enumerate(plan):
                    step = shard ^ rank
                    if step < 2:
                        src = (own, sib)[step].at[pl.ds(row, rows)]
                    else:
                        first, second = ((xa, ya), (xb, yb))[step - 2]
                        part = row // half
                        src = (first if part == parity else second).at[pl.ds(row - part * half, rows)]
                    pltpu.make_async_copy(src, dst, sems.at[index]).start()


def wait_rows(refs, plan, sems, which):
    for index in which:
        _, row, rows, dst = plan[index]
        pltpu.make_async_copy(refs[0].at[pl.ds(0, rows)], dst, sems.at[index]).wait()


def plan_of(buffers, first, rows):
    return [
        (shard, (first + which) * rows, rows, dst.at[pl.ds(shard * rows, rows)])
        for which, dst in enumerate(buffers)
        for shard in range(4)
    ]


def norm_rows(values):
    mean = jnp.mean(values, axis=-1, keepdims=True)
    center = values - mean
    factor = lax.rsqrt(jnp.mean(center * center, axis=-1, keepdims=True) + EPSILON)
    return center * factor, factor


def piece(mod, slot, index):
    width = mod.shape[1] // 9
    return mod[pl.ds(slot, 1), index * width : (index + 1) * width]


def entry_rows(x, mod, info, index, out):
    for block in range(x.shape[0] // UNIT):
        slot = info[1 + block]
        shift = piece(mod, slot, index)
        scale = 1.0 + piece(mod, slot, index + 1)

        def step(turn, carry):
            rows = pl.ds(pl.multiple_of(block * UNIT + turn * CHUNK, CHUNK), CHUNK)
            normed, _ = norm_rows(x[rows, :])
            out[rows, :] = (normed * scale + shift).astype(BF)
            return carry

        lax.fori_loop(0, UNIT // CHUNK, step, 0, unroll=True)


def residual_rows(x, mod, info, index, branch, branch_out, out, low=None):
    for block in range(x.shape[0] // UNIT):
        gate = piece(mod, info[1 + block], index)

        def step(turn, carry):
            rows = pl.ds(pl.multiple_of(block * UNIT + turn * CHUNK, CHUNK), CHUNK)
            values = branch[rows, :]
            branch_out[rows, :] = values.astype(BF)
            result = x[rows, :] + gate * values
            out[rows, :] = result
            if low is not None:
                low[rows, :] = result.astype(BF)
            return carry

        lax.fori_loop(0, UNIT // CHUNK, step, 0, unroll=True)


def fold(values):
    return jnp.sum(values.reshape(values.shape[0] // 8, 8, values.shape[1]), axis=0)


def total(values):
    return jnp.sum(values, axis=0, keepdims=True)


def gate_back(g, mod, info, index, branch, gb, stats):
    width = g.shape[1]
    sums = jnp.zeros((8, width), F32)
    for block in range(g.shape[0] // UNIT):
        slot = info[1 + block]
        gate = piece(mod, slot, index)

        def step(turn, carry):
            rows = pl.ds(pl.multiple_of(block * UNIT + turn * CHUNK, CHUNK), CHUNK)
            grad = g[rows, :]
            low = (gate * grad).astype(BF)
            gb[rows, :] = low
            return (
                carry[0] + fold(low.astype(F32)),
                carry[1] + fold(grad * branch[rows, :].astype(F32)),
            )

        sums, rows_sum = lax.fori_loop(
            0, UNIT // CHUNK, step, (sums, jnp.zeros((8, width), F32)), unroll=True
        )
        stats[pl.ds(8 + slot, 1), :] += total(rows_sum)
    stats[12:13, :] = total(sums)


def norm_back_rows(x, g, de, mod, info, index, out, stats, low=None):
    width = x.shape[1]
    for block in range(x.shape[0] // UNIT):
        slot = info[1 + block]
        scale = 1.0 + piece(mod, slot, index + 1)

        def step(turn, carry):
            rows = pl.ds(pl.multiple_of(block * UNIT + turn * CHUNK, CHUNK), CHUNK)
            normed, factor = norm_rows(x[rows, :])
            grad = de[rows, :]
            inner = grad * normed
            dn = grad * scale
            mean = jnp.mean(dn, axis=-1, keepdims=True)
            along = jnp.mean(dn * normed, axis=-1, keepdims=True)
            result = g[rows, :] + factor * (dn - mean - normed * along)
            out[rows, :] = result
            if low is not None:
                low[rows, :] = result.astype(BF)
            return (carry[0] + fold(grad), carry[1] + fold(inner))

        zero = jnp.zeros((8, width), F32)
        shift_sum, scale_sum = lax.fori_loop(0, UNIT // CHUNK, step, (zero, zero), unroll=True)
        stats[pl.ds(slot, 1), :] += total(shift_sum)
        stats[pl.ds(4 + slot, 1), :] += total(scale_sum)


def lane_ids(rows):
    return lax.broadcasted_iota(jnp.int32, (rows, LANES), 1)


def head_half(values, half):
    ids = lane_ids(values.shape[0])
    keep = ids < HEAD_WIDTH if half == 0 else ids >= HEAD_WIDTH
    return jnp.where(keep, values.astype(F32), 0.0)


def turned_halves(keys):
    turned = keys.T
    low = lax.broadcasted_iota(jnp.int32, turned.shape, 0) < HEAD_WIDTH
    zero = jnp.zeros(turned.shape, turned.dtype)
    return jnp.concatenate([jnp.where(low, turned, zero), jnp.where(low, zero, turned)], axis=1)


def query_marks(slot):
    return jnp.where(lane_ids(UNIT) == slot, 1.0, 0.0).astype(BF)


def key_marks(slots):
    ids = lane_ids(UNIT)
    parts = [jnp.where((ids < SLOTS) & (ids != slot), FAR, 0.0).astype(BF) for slot in slots]
    return jnp.concatenate(parts, axis=0)


def pair_lanes(pair):
    return pl.ds(pl.multiple_of(pair * LANES, LANES), LANES)


def start_own_rows(info, work, whole):
    share = work.rows.shape[0]
    first = pl.multiple_of((info[5] % 2) * share, share)
    copy = pltpu.make_async_copy(whole.at[pl.ds(first, share)], work.rows, work.row_sems.at[0])
    copy.start()
    return copy


def raise_rows(low, out):
    for row in range(0, low.shape[0], CHUNK):
        span = pl.ds(row, CHUNK)
        out[span, :] = low[span, :].astype(F32)


def kv_kernel(info, work, weights):
    rows = weights[0].shape[0] // 4
    plan = plan_of((work.w.at[0], work.w.at[1]), 1, rows)
    start_rows(weights[:6], info[0], plan, work.sems)
    if work.has("branch"):
        work.need("part", "other", "below")
        bias = work.bias[...].astype(F32)
        for row in range(0, work.sum.shape[0], CHUNK):
            span = pl.ds(row, CHUNK)
            work.sum[span, :] = (
                work.part[span, :].astype(F32) + work.other[span, :].astype(F32) + bias
            )
        residual_rows(work.below, work.mod_below, info, 8, work.sum, work.branch, work.x)
        work.flush("branch")
        work.flush("x")
    else:
        start_own_rows(info, work, weights[6]).wait()
        raise_rows(work.rows, work.x)
        work.flush("x")
    entry_rows(work.x, work.mod, info, 0, work.entry)
    work.flush("entry")
    entry = work.entry[...]
    wait_rows(weights, plan, work.sems, range(4))
    work.kv[0] = dot_nt(entry, work.w[0]).astype(BF)
    work.flush("kv", 0)
    wait_rows(weights, plan, work.sems, range(4, 8))
    work.kv[1] = (dot_nt(entry, work.w[1]) + work.biases[2:3, :]).astype(BF)
    work.flush("kv", 1)


def q_kernel(info, work, weights):
    rows = weights[0].shape[0] // 4
    plan = plan_of((work.w,), 0, rows)
    start_rows(weights, info[0], plan, work.sems)
    work.need("entry")
    wait_rows(weights, plan, work.sems, range(4))
    work.q[...] = (dot_nt(work.entry[...], work.w[...]) + work.biases[0:1, :]).astype(BF)
    work.flush("q")


def soft_pair(work, q_pair, keys, values, marks, logs, pair, span, words=None):
    ids = lane_ids(UNIT)
    results = []
    kept = logs[span, :]
    for half in range(2):
        left = (head_half(q_pair, half) * HEAD_WIDTH**-0.5).astype(BF)
        if marks is not None:
            left = jnp.concatenate([left, marks], axis=1)
        scores = dot_nt(left, keys)
        if words is not None:
            scores = jnp.where(ids < words, scores, FAR)
        peak = jnp.max(scores, axis=-1, keepdims=True)
        both = dot_nn(jnp.exp(scores - peak).astype(BF), values)
        sums = both[:, LANES:]
        results.append(both[:, :LANES] / sums)
        kept = jnp.where(ids == 2 * pair + half, peak + jnp.log(sums), kept)
    logs[span, :] = kept
    return jnp.where(ids < HEAD_WIDTH, results[0], results[1])


def self_kernel(info, work, weights):
    rows = weights[0].shape[0] // 4
    sems = work.sems
    plan = [(s, 3 * rows, rows, work.wo.at[pl.ds(s * rows, rows)]) for s in range(4)]
    start_rows(weights, info[0], plan, sems)
    share = work.x.shape[0]
    blocks = share // UNIT
    marks = key_marks([info[1 + b] for b in range(2 * blocks)])
    ones = jnp.ones((2 * share, LANES), BF)
    logs, mixed = work.logs, work.mixed
    logs[...] = jnp.zeros(logs.shape, F32)
    work.need("q", "kv_own", "kv_sib")

    def both(which, lanes):
        return jnp.concatenate([work.kv_own[which, :, lanes], work.kv_sib[which, :, lanes]], axis=0)

    def step(pair, carry):
        lanes = pair_lanes(pair)
        keys = jnp.concatenate([both(0, lanes), marks], axis=1)
        values = jnp.concatenate([both(1, lanes), ones], axis=1)
        for block in range(blocks):
            span = pl.ds(block * UNIT, UNIT)
            values_mixed = soft_pair(
                work,
                work.q[span, lanes],
                keys,
                values,
                query_marks(info[1 + block]),
                logs,
                pair,
                span,
            )
            low = values_mixed.astype(BF)
            mixed[span, lanes] = low
            work.rest[span, lanes] = (values_mixed - low.astype(F32)).astype(BF)
        return carry

    lax.fori_loop(0, mixed.shape[1] // LANES, step, 0)
    work.flush("mixed")
    work.flush("rest")
    work.lse[...] = logs[...].T[: work.lse.shape[0], :]
    work.flush("lse")
    wait_rows(weights, plan, sems, range(4))
    work.sum[...] = dot_nn(mixed[...], work.wo[...]) + work.bias[...].astype(F32)
    work.need("x")
    residual_rows(work.x, work.mod, info, 2, work.sum, work.branch, work.out)
    work.flush("branch")
    work.flush("out")


def cross_kernel(info, work, weights, words):
    rows = weights[0].shape[0] // 4
    sems = work.sems
    order = (1, 2, 0, 3)
    plan = [
        (shard, order[i // 4] * rows, count, dst)
        for i, (shard, _, count, dst) in enumerate(
            plan_of((work.wk, work.wv, work.wq, work.wo), 0, rows)
        )
    ]
    start_rows(weights, info[0], plan, sems)
    work.need("x")
    entry_rows(work.x, work.mod, info, 3, work.entry)
    work.flush("entry")
    work.need("text")
    wait_rows(weights, plan, sems, range(0, 4))
    work.kv[0] = dot_nt(work.text[...], work.wk[...]).astype(BF)
    wait_rows(weights, plan, sems, range(4, 8))
    work.kv[1] = (dot_nt(work.text[...], work.wv[...]) + work.biases[5:6, :]).astype(BF)
    work.flush("kv")
    wait_rows(weights, plan, sems, range(8, 12))
    work.q[...] = (dot_nt(work.entry[...], work.wq[...]) + work.biases[3:4, :]).astype(BF)
    work.flush("q")
    ones = jnp.ones((LANES, LANES), BF)
    logs, mixed = work.logs, work.mixed
    logs[...] = jnp.zeros(logs.shape, F32)

    def step(pair, carry):
        lanes = pair_lanes(pair)
        for block in range(mixed.shape[0] // UNIT):
            span = pl.ds(block * UNIT, UNIT)
            own = pl.ds(pl.multiple_of(info[1 + block] * LANES, LANES), LANES)
            mixed[span, lanes] = soft_pair(
                work,
                work.q[span, lanes],
                work.kv[0, own, lanes],
                jnp.concatenate([work.kv[1, own, lanes], ones], axis=1),
                None,
                logs,
                pair,
                span,
                words,
            ).astype(BF)
        return carry

    lax.fori_loop(0, mixed.shape[1] // LANES, step, 0, unroll=2)
    work.flush("mixed")
    work.lse[...] = logs[...].T[: work.lse.shape[0], :]
    work.flush("lse")
    wait_rows(weights, plan, sems, range(12, 16))
    work.sum[...] = dot_nn(mixed[...], work.wo[...]) + work.bias[...].astype(F32)
    residual_rows(work.x, work.mod, info, 5, work.sum, work.branch, work.out)
    work.flush("branch")
    work.flush("out")


def hidden_plan(refs, buffer):
    rows = buffer.shape[1]
    half = rows // 2
    return [
        (shard, row, half, buffer.at[shard, pl.ds(row, half)])
        for shard in range(4)
        for row in range(0, rows, half)
    ]


def start_chip(info, refs, layer, buffer, sems):
    copies = [
        pltpu.make_async_copy(ref.at[layer], buffer.at[(info[5] + i) % 2], sems.at[i])
        for i, ref in enumerate(refs)
    ]
    for copy in copies:
        copy.start()
    return copies


def bend_rows(before, bias, active, slope, lanes):
    for row in range(0, before.shape[0], CHUNK):
        span = pl.ds(row, CHUNK)
        values = before[span, :] + bias
        square = values * values
        half = 1.0 / (1.0 + jnp.exp(values * (-2.0 * ROOT - (2.0 * ROOT * CUBIC) * square)))
        act = values * half
        active[span, lanes] = act.astype(BF)
        slope[span, lanes] = (
            half + act * (1.0 - half) * (2.0 * ROOT + (6.0 * ROOT * CUBIC) * square)
        ).astype(BF)


def columns_of(shard, width):
    return pl.ds(pl.multiple_of(shard * width, width), width)


def start_hidden(info, work, weights, layer):
    if len(weights) == 4:
        ups = start_chip(info, weights[:2], layer, work.up, work.sems)
        downs = start_chip(info, weights[2:], layer, work.down, work.down_sems)
        return [lambda some=some: [copy.wait() for copy in some] for some in (ups, downs)]
    waits = []
    for refs, buffer, sems in (
        (weights[:6], work.up, work.sems),
        (weights[6:12], work.down, work.down_sems),
    ):
        refs = [ref.at[layer] for ref in refs[:2]] + list(refs[2:])
        plan = hidden_plan(refs, buffer)
        start_rows(refs, info[0], plan, sems)
        waits.append(
            lambda refs=refs, plan=plan, sems=sems: wait_rows(refs, plan, sems, range(len(plan)))
        )
    return waits


def hidden_kernel(info, work, weights, layer):
    waits = start_hidden(info, work, weights, layer)
    width = work.x.shape[1]
    shards = work.up.shape[0]
    first = info[6] * 2
    work.need("x")
    entry_rows(work.x, work.mod, info, 6, work.entry)
    work.flush("entry")
    for wait in waits:
        wait()
    work.sum[...] = jnp.zeros(work.sum.shape, F32)

    def step(shard, carry):
        lanes = columns_of(shard, width)
        bias = work.up_bias[:, columns_of(first + shard, width)]
        work.before[...] = dot_nn(work.entry[...], work.up[shard])
        bend_rows(work.before, bias, work.active, work.slope, lanes)
        work.sum[...] += dot_nn(work.active[:, lanes], work.down[shard])
        return carry

    lax.fori_loop(0, shards, step, 0)
    work.flush("active")
    work.flush("slope")
    work.part[...] = work.sum[...].astype(BF)
    work.flush("part")


def hidden_back_kernel(info, work, weights, layer):
    waits = start_hidden(info, work, weights, layer)
    work.stats[...] = jnp.zeros(work.stats.shape, F32)
    stats = work.stats.at[pl.ds(48, 24)]
    work.need("g", "branch")
    gate_back(work.g, work.mod, info, 8, work.branch, work.gb, stats)
    work.need("slope")
    for wait in waits:
        wait()
    hidden_back_rows(info, work, work.de, stats)
    work.part[...] = work.de[...].astype(BF)
    work.flush("part")
    work.flush("gb")
    work.flush("d_before")


def hidden_back_rows(info, work, de, stats):
    width = work.g.shape[1]
    shards = work.up.shape[0]
    first = info[6] * 2 if shards == 2 else 0
    de[...] = jnp.zeros(de.shape, F32)

    def step(shard, carry):
        lanes = columns_of(shard, width)
        work.before[...] = dot_nt(work.gb[...], work.down[shard])
        sums = jnp.zeros((8, width), F32)
        for row in range(0, work.g.shape[0], CHUNK):
            span = pl.ds(row, CHUNK)
            low = (work.before[span, :] * work.slope[span, lanes].astype(F32)).astype(BF)
            work.d_before[span, lanes] = low
            sums += fold(low.astype(F32))
        stats[pl.ds(13 + first + shard, 1), :] = total(sums)
        de[...] += dot_nt(work.d_before[:, lanes], work.up[shard])
        return carry

    lax.fori_loop(0, shards, step, 0)


def hidden_both_kernel(info, work, weights, layer):
    copy = start_own_rows(info, work, weights[12])
    waits = start_hidden(info, work, weights, layer)
    width = work.x.shape[1]
    work.need("x")
    entry_rows(work.x, work.mod, info, 6, work.entry)
    for wait in waits:
        wait()
    work.sum[...] = jnp.zeros(work.sum.shape, F32) + work.bias[...].astype(F32)

    def step(shard, carry):
        lanes = columns_of(shard, width)
        work.before[...] = dot_nn(work.entry[...], work.up[shard])
        bend_rows(work.before, work.up_bias[:, lanes], work.active, work.slope, lanes)
        work.sum[...] += dot_nn(work.active[:, lanes], work.down[shard])
        return carry

    lax.fori_loop(0, 4, step, 0)
    residual_rows(work.x, work.mod, info, 8, work.sum, work.branch, work.out, work.low)
    work.flush("low")
    work.stats[...] = jnp.zeros(work.stats.shape, F32)
    stats = work.stats.at[pl.ds(48, 24)]
    copy.wait()
    raise_rows(work.rows, work.g)
    gate_back(work.g, work.mod, info, 8, work.branch, work.gb, stats)
    hidden_back_rows(info, work, work.sum, stats)
    left, right = work.entry[...].T, work.gb[...].T
    for name, rank in (("send", info[7]), ("keep", info[5])):
        out = work.outs[name][1]
        lanes = columns_of(rank, width)
        out[:, :width] = dot_nn(left, work.d_before[:, lanes]).astype(BF)
        out[:, width:] = dot_nn(right, work.active[:, lanes]).astype(BF)
        work.flush(name)
    norm_back_rows(work.x, work.g, work.sum, work.mod, info, 6, work.out, stats)
    work.flush("out")


def hidden_cross_kernel(info, work, weights, words):
    hidden_both_kernel(
        info,
        Names(
            work,
            x="x2",
            entry="entry3",
            branch="branch3",
            out="g_mid",
            send="f_send",
            keep="f_keep",
        ),
        weights[:13],
        1,
    )
    cross_back_kernel(
        info,
        Names(
            work,
            early="stats",
            g="g_mid",
            branch="branch2",
            entry="entry2",
            x="x1",
            de="sum",
            dq="entry3",
            d_mixed="rows",
            sems="cross_sems",
            send="c_send",
            keep="c_keep",
        ),
        weights[13:],
        words,
    )


def attention_kernel(info, work, weights, words):
    self_kernel(
        info,
        Names(work, out="x1", mixed="mixed1", lse="lse1", branch="branch1", bias="self_bias"),
        weights[:6],
    )
    cross_kernel(
        info,
        Names(
            work,
            x="x1",
            q="cq",
            kv="ckv",
            mixed="mixed2",
            lse="lse2",
            branch="branch2",
            bias="cross_bias",
            wo="cross_wo",
            sems="cross_sems",
        ),
        weights[6:],
        words,
    )


def hidden_grads_kernel(info, work, weights):
    width = work.entry.shape[1]
    work.need("entry", "d_before", "gb", "active")
    left, right = work.entry[...].T, work.gb[...].T
    for name, shift in (("send", 1), ("keep", 0)):
        out = work.outs[name][1]
        lanes = columns_of((info[5] + shift) % 2, width)
        out[:, :width] = dot_nn(left, work.d_before[:, lanes]).astype(BF)
        out[:, width:] = dot_nn(right, work.active[:, lanes]).astype(BF)
        work.flush(name)


def pair_grads(info, work, members):
    rows = members[0][0].shape[0]
    low = lane_ids(rows) < HEAD_WIDTH
    step = 3 * LANES
    for at in range(len(members) // 2):
        products = [dot_nn(left, right) for left, right in members[2 * at : 2 * at + 2]]
        (a0, a1, a2), (b0, b1, b2) = [
            [p[:, i * LANES : (i + 1) * LANES] for i in range(3)] for p in products
        ]
        even = (a0, b0, jnp.where(low, a1, pltpu.roll(b1, HEAD_WIDTH, 1)))
        a1, b1 = pltpu.roll(a1, HEAD_WIDTH, 1), pltpu.roll(b1, HEAD_WIDTH, 1)
        a2r, b2r = pltpu.roll(a2, HEAD_WIDTH, 1), pltpu.roll(b2, HEAD_WIDTH, 1)
        odd = (jnp.where(low, a1, a2r), jnp.where(low, b1, b2r), jnp.where(low, a2r, b2))
        first = info[5] % 2 == 0
        for i, (mine, other) in enumerate(zip(even, odd)):
            lanes = pl.ds(at * step + i * LANES, LANES)
            work.outs["keep"][1][:, lanes] = jnp.where(first, mine, other).astype(BF)
            work.outs["send"][1][:, lanes] = jnp.where(first, other, mine).astype(BF)
    work.flush("send")
    work.flush("keep")


def chip_lanes(info, width):
    return pl.ds(pl.multiple_of(info[6] * (width // 2), width // 2), width // 2)


def query_output_kernel(info, work, weights):
    work.need("entry", "gb", "dq", "mixed")
    lanes = chip_lanes(info, work.dq.shape[1])
    pair_grads(
        info,
        work,
        [
            (work.entry[...].T, work.dq[:, lanes]),
            (work.gb[...].T, work.mixed[:, lanes]),
        ],
    )


def cross_back_kernel(info, work, weights, words):
    rows = weights[0].shape[0] // 4
    sems = work.sems
    plan = [
        (shard, (3 * rows, 0)[i // 4], count, dst)
        for i, (shard, _, count, dst) in enumerate(plan_of((work.wo, work.wq), 0, rows))
    ]
    start_rows(weights, info[0], plan, sems)
    work.stats[...] = work.early[...]
    stats = work.stats.at[pl.ds(24, 24)]
    g = work.g
    work.need("g")
    if work.takes("part"):
        work.need("part", "other", "above")
        for row in range(0, g.shape[0], CHUNK):
            span = pl.ds(row, CHUNK)
            work.de[span, :] = work.part[span, :].astype(F32) + work.other[span, :].astype(F32)
        g = work.g_mid
        norm_back_rows(
            work.above, work.g, work.de, work.mod, info, 6, g, work.stats.at[pl.ds(48, 24)]
        )
    work.need("branch")
    gate_back(g, work.mod, info, 5, work.branch, work.gb, stats)
    wait_rows(weights, plan, sems, range(0, 4))
    work.d_mixed[...] = dot_nt(work.gb[...], work.wo[...]).astype(BF)
    work.dkv_sum[...] = jnp.zeros(work.dkv_sum.shape, F32)
    real = lax.broadcasted_iota(jnp.int32, (LANES, UNIT), 0) < words
    work.need("q", "kv", "lse")

    def step(pair, carry):
        lanes = pair_lanes(pair)
        for block in range(work.q.shape[0] // UNIT):
            span = pl.ds(block * UNIT, UNIT)
            own = pl.ds(pl.multiple_of(info[1 + block] * LANES, LANES), LANES)
            q_pair = work.q[span, lanes]
            d_pair = work.d_mixed[span, lanes]
            keys = work.kv[0, own, lanes]
            values = work.kv[1, own, lanes]
            lefts, grads, probs_low, scores_low = [], [], [], []
            for half in range(2):
                left = (head_half(q_pair, half) * HEAD_WIDTH**-0.5).astype(BF)
                grad = head_half(d_pair, half).astype(BF)
                logs = work.lse[pl.ds(2 * pair + half, 1), span]
                probs = jnp.where(real, jnp.exp(dot_nt(keys, left) - logs), 0.0)
                d_probs = dot_nt(values, grad)
                inner = jnp.sum(probs * d_probs, axis=0, keepdims=True)
                lefts.append(left)
                grads.append(grad)
                probs_low.append(probs.astype(BF))
                scores_low.append((probs * (d_probs - inner)).astype(BF))
            wide_scores = jnp.concatenate(scores_low, axis=1)
            grad_v = dot_nn(jnp.concatenate(probs_low, axis=1), jnp.concatenate(grads, axis=0))
            grad_k = dot_nn(wide_scores, jnp.concatenate(lefts, axis=0))
            grad_q = dot_nn(turned_halves(keys), jnp.concatenate(scores_low, axis=0))
            work.dq[span, lanes] = (grad_q.T * HEAD_WIDTH**-0.5).astype(BF)
            work.dkv_sum[0, own, lanes] += grad_k
            work.dkv_sum[1, own, lanes] += grad_v
        return carry

    lax.fori_loop(0, work.q.shape[1] // LANES, step, 0, unroll=2)
    work.dkv[...] = work.dkv_sum[...].astype(BF)
    work.need("entry", "text", "mixed")
    lanes = chip_lanes(info, work.dq.shape[1])
    text = work.text[...].T
    pair_grads(
        info,
        work,
        [
            (work.entry[...].T, work.dq[:, lanes]),
            (text, work.dkv[0, :, lanes]),
            (text, work.dkv[1, :, lanes]),
            (work.gb[...].T, work.mixed[:, lanes]),
        ],
    )
    stats[13:14, :] = total(fold(work.dq[...].astype(F32)))
    stats[14:15, :] = total(fold(work.dkv[1].astype(F32)))
    wait_rows(weights, plan, sems, range(4, 8))
    work.de[...] = dot_nn(work.dq[...], work.wq[...])
    work.need("x")
    norm_back_rows(work.x, g, work.de, work.mod, info, 3, work.out, stats)
    work.flush("out")


def self_back_kernel(info, work, weights):
    rows = weights[0].shape[0] // 4
    sems = work.sems
    plan = [(s, 3 * rows, rows, work.wo.at[pl.ds(s * rows, rows)]) for s in range(4)]
    start_rows(weights, info[0], plan, sems)
    work.stats[...] = work.early[...]
    stats = work.stats.at[pl.ds(0, 24)]
    work.need("g", "branch")
    gate_back(work.g, work.mod, info, 2, work.branch, work.gb, stats)
    work.flush("gb")
    share = work.g.shape[0]
    blocks = share // UNIT
    marks = key_marks([info[1 + b] for b in range(2 * blocks)])
    wait_rows(weights, plan, sems, range(4))
    work.d_mixed[...] = dot_nt(work.gb[...], work.wo[...]).astype(BF)
    work.need("mixed", "rest", "q", "kv_own", "kv_sib", "lse")
    width = work.q.shape[1]
    head = lax.broadcasted_iota(jnp.int32, (16, width), 0)
    lane = lax.broadcasted_iota(jnp.int32, (16, width), 1)
    first = head * HEAD_WIDTH
    pick = jnp.where((lane >= first) & (lane < first + HEAD_WIDTH), 1.0, 0.0)
    for block in range(blocks):
        span = pl.ds(block * UNIT, UNIT)
        whole = work.mixed[span, :].astype(F32) + work.rest[span, :].astype(F32)
        work.inner[:, span] = lax.dot_general(
            pick,
            whole * work.d_mixed[span, :].astype(F32),
            (((1,), (1,)), ((), ())),
            precision=lax.Precision.HIGHEST,
            preferred_element_type=F32,
        )

    def both(which, lanes):
        return jnp.concatenate([work.kv_own[which, :, lanes], work.kv_sib[which, :, lanes]], axis=0)

    def step(pair, carry):
        lanes = pair_lanes(pair)
        keys = both(0, lanes)
        values = both(1, lanes)
        marked = jnp.concatenate([keys, marks], axis=1)
        turned = turned_halves(keys)
        lefts, grads, probs_low, scores_low = [], [], [], []
        for block in range(blocks):
            span = pl.ds(block * UNIT, UNIT)
            q_pair = work.q[span, lanes]
            d_pair = work.d_mixed[span, lanes]
            ends = query_marks(info[1 + block])
            for half in range(2):
                left = (head_half(q_pair, half) * HEAD_WIDTH**-0.5).astype(BF)
                grad = head_half(d_pair, half).astype(BF)
                logs = work.lse[pl.ds(2 * pair + half, 1), span]
                probs = jnp.exp(dot_nt(marked, jnp.concatenate([left, ends], axis=1)) - logs)
                d_probs = dot_nt(values, grad)
                inner = work.inner[pl.ds(2 * pair + half, 1), span]
                lefts.append(left)
                grads.append(grad)
                probs_low.append(probs.astype(BF))
                scores_low.append((probs * (d_probs - inner)).astype(BF))
            grad_q = dot_nn(turned, jnp.concatenate(scores_low[-2:], axis=0))
            work.dq[span, lanes] = (grad_q.T * HEAD_WIDTH**-0.5).astype(BF)
        grad_v = dot_nn(jnp.concatenate(probs_low, axis=1), jnp.concatenate(grads, axis=0))
        grad_k = dot_nn(jnp.concatenate(scores_low, axis=1), jnp.concatenate(lefts, axis=0))
        for which, grad in ((0, grad_k.astype(BF)), (1, grad_v.astype(BF))):
            work.dkv_own[which, :, lanes] = grad[:share]
            work.dkv_give[which, :, lanes] = grad[share:]
        return carry

    lax.fori_loop(0, work.q.shape[1] // LANES, step, 0)
    work.flush("dkv_give")
    work.flush("dkv_own")
    work.flush("dq")


def sum_keys_values(info, work, dkv):
    work.need("dkv_own", "dkv_sib")
    for which in range(2):
        dkv[which] = (
            work.dkv_own[which].astype(F32) + work.dkv_sib[which].astype(F32)
        ).astype(BF)
    work.need("entry")
    lanes = chip_lanes(info, dkv.shape[2])
    entry = work.entry[...].T
    pair_grads(info, work, [(entry, dkv[0, :, lanes]), (entry, dkv[1, :, lanes])])


def kv_grads_kernel(info, work, weights):
    sum_keys_values(info, work, work.dkv)
    work.flush("dkv")


def qkv_back_kernel(info, work, weights):
    rows = weights[0].shape[0] // 4
    sems = work.sems
    plan = plan_of((work.wq, work.wk, work.wv), 0, rows)
    start_rows(weights, info[0], plan, sems)
    work.stats[...] = work.early[...]
    stats = work.stats.at[pl.ds(0, 24)]
    if work.has("send"):
        sum_keys_values(info, work, work.dkv)
    else:
        work.need("dkv")
    work.need("dq")
    stats[13:14, :] = total(fold(work.dq[...].astype(F32)))
    stats[14:15, :] = total(fold(work.dkv[1].astype(F32)))
    wait_rows(weights, plan, sems, range(0, 12))
    work.de[...] = (
        dot_nn(work.dq[...], work.wq[...])
        + dot_nn(work.dkv[0], work.wk[...])
        + dot_nn(work.dkv[1], work.wv[...])
    )
    work.need("x", "g")
    low = work.low if work.has("low") else None
    norm_back_rows(work.x, work.g, work.de, work.mod, info, 0, work.out, stats, low)
    work.flush("out")
    if low is not None:
        work.flush("low")


def merge_kernel(info, *refs, spots, after):
    chains = len(spots)
    ins, outs = refs[: 4 * chains], refs[4 * chains + after :]
    for chain, (result, column) in enumerate(spots):
        for side in range(2):
            received, kept = ins[4 * chain + 2 * side], ins[4 * chain + 2 * side + 1]
            out = outs[2 * result + side]
            lanes = pl.ds(column, received.shape[2])
            out[:, :, lanes] = (received[...].astype(F32) + kept[...].astype(F32)).astype(BF)


def gate(arrays, after):
    count = len(arrays)
    return pl.pallas_call(
        lambda *refs: None,
        out_shape=[shape(*a.shape, dtype=a.dtype) for a in arrays],
        in_specs=[ANY] * (count + len(after)),
        out_specs=[ANY] * count,
        input_output_aliases={i: i for i in range(count)},
        cost_estimate=lasting(0.5),
        name="gate",
    )(*arrays, *after)


def pack_kernel(info, *refs, groups, whole, after):
    count = sum(len(members) for _, members in groups)
    sources, rest = refs[:count], refs[count + after :]
    (in_sems, out_sems), rest = rest[-2:], rest[:-2]
    count = len(groups) + sum(whole)
    outs, held = list(rest[:count]), rest[count:]
    owns = [outs.pop(0) if one else None for one in whole]
    spots = []
    at = 0
    for index, (layer, members) in enumerate(groups):
        rows = held[index].shape[0]
        piece_rows = rows // 4
        for quarter in range(4):
            row = quarter * piece_rows
            source = sources[at + quarter * len(members) // 4]
            src = source.at[layer, pl.ds(row % source.shape[1], piece_rows)]
            spots.append((index, quarter, held[index].at[pl.ds(row, piece_rows)], src))
        at += len(members)

    def arriving(place):
        _, _, spot, src = spots[place]
        return pltpu.make_async_copy(src, spot, in_sems.at[place])

    def leaving(index, which):
        if which == 2:
            return pltpu.make_async_copy(held[index], owns[index], out_sems.at[2 * index])
        rows = outs[index].shape[0]
        src = held[index].at[pl.ds(which * rows, rows)]
        return pltpu.make_async_copy(src, outs[index], out_sems.at[2 * index + 1])

    def by_parity(act):
        for parity in range(2):

            @pl.when(info[0] % 2 == parity)
            def _(parity=parity):
                act(parity)

    for place in range(len(spots)):
        arriving(place).start()
    for index in range(len(groups)):
        for quarter in range(4):
            arriving(4 * index + quarter).wait()
        by_parity(lambda parity: leaving(index, parity).start())
        if whole[index]:
            leaving(index, 2).start()
    for index in range(len(groups)):
        by_parity(lambda parity: leaving(index, parity).wait())
        if whole[index]:
            leaving(index, 2).wait()


def mod_kernel(condition, mod, mod_bias, q, v, cq, cv, up, out):
    narrow, units, columns = q.shape[1], up.shape[1], mod.shape[1]
    out[...] = jnp.zeros(out.shape, F32)
    for layer in range(LAYERS):
        row = pl.ds(layer, 1)
        out[layer, 0:SLOTS, 0:columns] = dot_nt(condition[...], mod[layer]) + mod_bias[
            row, :
        ].astype(F32)
        out[layer, 4:5, 0:units] = up[row, :].astype(F32)
        out[layer, 5:6, 0:narrow] = q[row, :].astype(F32)
        out[layer, 6:7, 0:narrow] = v[row, :].astype(F32)
        out[layer, 7:8, 0:narrow] = cq[row, :].astype(F32)
        out[layer, 4:5, 1024 : 1024 + narrow] = cv[row, :].astype(F32)


def assemble_kernel(info, *refs, narrow, units, columns):
    parts, (mods, narrows, ups) = refs[:4], refs[4:]
    narrows[...] = jnp.zeros(narrows.shape, F32)
    for rank in range(4):

        @pl.when(info[5] == rank)
        def _(rank=rank):
            for shard in range(4):
                part = parts[shard ^ rank]
                for layer in range(LAYERS):
                    mods[layer, :, shard * columns : (shard + 1) * columns] = part[
                        layer, 0:SLOTS, 0:columns
                    ]
                    ups[layer, :, shard * units : (shard + 1) * units] = part[layer, 4:5, 0:units]
                    at = slice(shard * narrow, (shard + 1) * narrow)
                    for row, source in ((0, 5), (2, 6), (3, 7)):
                        narrows[layer, row : row + 1, at] = part[
                            layer, source : source + 1, 0:narrow
                        ]
                    narrows[layer, 5:6, at] = part[layer, 4:5, 1024 : 1024 + narrow]


def collect_kernel(info, *refs, narrow, units, columns):
    stats, condition, out = refs[: 2 * LAYERS], refs[2 * LAYERS], refs[2 * LAYERS + 1]
    sums = refs[2 * LAYERS + 2]
    width = stats[0].shape[1]
    work = out
    out = refs[2 * LAYERS + 3]
    out[...] = jnp.zeros(out.shape, F32)
    for layer in range(LAYERS):
        sums[...] = stats[2 * layer][...] + stats[2 * layer + 1][...]
        base = 8 * layer
        out[base + 4 : base + 5, width : 2 * width] = sums[60:61, :]
        out[base + 5 : base + 6, 0:width] = sums[12:13, :]
        out[base + 5 : base + 6, width : 2 * width] = sums[36:37, :]
        for index in range(2):
            out[base + 6 + index : base + 7 + index, 512 : 512 + width] = condition[
                2 * layer + index : 2 * layer + index + 1, :
            ].astype(F32)
        for rank in range(4):

            @pl.when(info[5] == rank)
            def _(rank=rank, base=base):
                first = rank * columns
                for index in range(9):
                    low = max(first, index * width)
                    high = min(first + columns, (index + 1) * width)
                    if low < high:
                        row = (index // 3) * 24 + (index % 3) * 4
                        out[base : base + 4, low - first : high - first] = sums[
                            row : row + 4, low - index * width : high - index * width
                        ]
                out[base + 4 : base + 5, 0:units] = sums[61 + rank : 62 + rank, :]
                own = slice(rank * narrow, (rank + 1) * narrow)
                out[base + 6 : base + 7, 0:narrow] = sums[13:14, own]
                out[base + 6 : base + 7, 256 : 256 + narrow] = sums[14:15, own]
                out[base + 7 : base + 8, 0:narrow] = sums[37:38, own]
                out[base + 7 : base + 8, 256 : 256 + narrow] = sums[38:39, own]
    work[...] = out[...].astype(BF)


def spread_kernel(info, gathered, grad, bias_grad, q, v, cq, cv, up, o1, o2, o3, rows, conditions):
    count = gathered.shape[0]
    columns, part = grad.shape[2], grad.shape[1]
    width, narrow, units = conditions.shape[1], q.shape[1], up.shape[1]
    shift = lax.rem(width - info[8] * part, width)
    for index in range(count):
        for slot in range(SLOTS):
            row = 8 * (slot // 2) + 6 + slot % 2
            conditions[SLOTS * index + slot : SLOTS * index + slot + 1, :] = gathered[
                index ^ info[8], row : row + 1, 512 : 512 + width
            ].astype(F32)
    turned = pltpu.roll(conditions[...], shift, 1)[:, :part].T
    for layer in range(LAYERS):
        base = 8 * layer
        sums = jnp.zeros((8, gathered.shape[2]), F32)
        for index in range(count):
            values = gathered[index ^ info[8]].astype(F32)[base : base + 8]
            sums += values
            rows[SLOTS * index : SLOTS * (index + 1), :] = values[0:SLOTS, 0:columns]
        grad[layer] = jnp.dot(
            turned, rows[...], precision=lax.Precision.HIGHEST, preferred_element_type=F32
        )
        at = slice(layer, layer + 1)
        bias_grad[at, :] = jnp.sum(sums[0:SLOTS, 0:columns], axis=0, keepdims=True)
        up[at, :] = sums[4:5, 0:units]
        q[at, :] = sums[6:7, 0:narrow]
        v[at, :] = sums[6:7, 256 : 256 + narrow]
        cq[at, :] = sums[7:8, 0:narrow]
        cv[at, :] = sums[7:8, 256 : 256 + narrow]
        for out, row, lane in ((o1, 5, 0), (o2, 5, width), (o3, 4, width)):
            own = jnp.broadcast_to(sums[row : row + 1, lane : lane + width], (8, width))
            out[at, :] = pltpu.roll(own, shift, 1)[0:1, :part]


def finish_kernel(*refs, wide, spots):
    parts, outs = refs[: 2 * len(spots)], refs[2 * len(spots) :]
    step = 3 * LANES
    for chain, (at, places) in enumerate(spots):
        values = parts[2 * chain][0].astype(F32) + parts[2 * chain + 1][0].astype(F32)
        for layer, pair in places:
            if wide:
                width = outs[0].shape[2]
                for out in outs:
                    out[layer] = values[:, at : at + width]
                    at += width
                continue
            both = values[:, at : at + step]
            at += step
            first = jnp.concatenate(
                [both[:, :LANES], both[:, 2 * LANES : 2 * LANES + HEAD_WIDTH]], axis=1
            )
            second = jnp.concatenate(
                [both[:, LANES : 2 * LANES], both[:, 2 * LANES + HEAD_WIDTH :]], axis=1
            )
            for out, matrix in zip(outs[2 * pair : 2 * pair + 2], (first, second)):
                out[layer] = matrix if out.shape[1:] == matrix.shape else matrix.T


def join_kernel(info, rows, other, out):
    share = rows.shape[0]
    for core in range(2):

        @pl.when(info[5] % 2 == core)
        def _(core=core):
            out[pl.ds(core * share, share), :] = rows[...]
            out[pl.ds((1 - core) * share, share), :] = other[...]


def tensor_hop(values, step):
    return lax.ppermute(values, "tensor", [(i, i ^ step) for i in range(4)])


def dp_hop(values, step):
    size = lax.axis_size("dp")
    return lax.ppermute(values, "dp", [(i, i ^ step) for i in range(size)])


def time_features(moments, width):
    half = width // 2
    rates = jnp.exp(-math.log(10000.0) * jnp.arange(half, dtype=F32) / half)
    angles = moments.astype(F32)[:, None] * rates[None, :]
    return jnp.concatenate([jnp.cos(angles), jnp.sin(angles)], axis=1)


def shards(
    tokens,
    text,
    timesteps,
    item_frames,
    cotangent,
    self_query,
    self_query_bias,
    self_key,
    self_value,
    self_value_bias,
    self_output,
    self_output_bias,
    cross_query,
    cross_query_bias,
    cross_key,
    cross_value,
    cross_value_bias,
    cross_output,
    cross_output_bias,
    hidden_up,
    hidden_up_bias,
    hidden_down,
    hidden_down_bias,
    modulation,
    modulation_bias,
):
    frames, width = tokens.shape
    words = text.shape[1]
    columns = modulation.shape[2]
    narrow = self_query.shape[2]
    units = hidden_up.shape[2]
    rank = lax.axis_index("tensor")
    me = lax.axis_index("dp")
    size = lax.axis_size("dp")
    core = rank % 2
    share = frames // 2
    blocks = share // UNIT
    unit = width // size
    turn = lambda values: jnp.swapaxes(values, 1, 2)

    order = jnp.arange(SLOTS, dtype=jnp.int32)
    ends = jnp.sum(jnp.where(order[:, None] <= order[None, :], item_frames[:, None], 0), axis=0)
    turned = (jnp.arange(frames // UNIT, dtype=jnp.int32) + core * blocks) % (2 * blocks)
    slots = jnp.sum((turned[:, None] * UNIT >= ends[None, :]).astype(jnp.int32), axis=1)
    places = jnp.stack([rank, rank // 2, rank ^ 1, me]).astype(jnp.int32)
    info = jnp.concatenate([(rank * 2 + me % 2)[None].astype(jnp.int32), slots, places])

    def pack(members, whole, after=()):
        rows = [sum(a.shape[1] for a in some) for _, some in members]
        outs = [shape(r, width, dtype=BF) for r, one in zip(rows, whole) if one]
        outs += [shape(r // 2, width, dtype=BF) for r in rows]
        arrays = [a for _, some in members for a in some]
        results = pl.pallas_call(
            partial(
                pack_kernel,
                groups=[(layer, [None] * len(some)) for layer, some in members],
                whole=whole,
                after=len(after),
            ),
            out_shape=outs,
            in_specs=[SMALL] + [ANY] * (len(arrays) + len(after)),
            out_specs=[ANY] * len(outs),
            scratch_shapes=[
                *[pltpu.VMEM((r, width), BF) for r in rows],
                pltpu.SemaphoreType.DMA((4 * len(members),)),
                pltpu.SemaphoreType.DMA((2 * len(members),)),
            ],
            compiler_params=pltpu.CompilerParams(vmem_limit_bytes=VMEM_BYTES),
            cost_estimate=lasting(1.0),
            name="pack_weights",
        )(info, *arrays, *after)
        return list(results[: sum(whole)]), list(results[sum(whole) :])

    selfs = [turn(self_query), turn(self_key), turn(self_value), self_output]
    crosses = [turn(cross_query), turn(cross_key), turn(cross_value), cross_output]
    own0, first0 = pack([(0, selfs)], [True])


    condition = jax.nn.silu(time_features(timesteps, width)).astype(BF)
    mine = plain(
        mod_kernel,
        "modulation_rows",
        None,
        [
            condition,
            turn(modulation),
            modulation_bias,
            self_query_bias,
            self_value_bias,
            cross_query_bias,
            cross_value_bias,
            hidden_up_bias,
        ],
        [shape(LAYERS, 8, -(-columns // LANES) * LANES)],
    )
    own1, first1 = pack(
        [(0, crosses), (1, selfs), (1, crosses), (1, [hidden_up]), (1, [hidden_down])],
        [True, True, True, False, False],
        [mine],
    )
    firsts, owns = first0 + first1, own0 + own1
    others = [tensor_hop(mine, 1), tensor_hop(mine, 2)]
    others.append(tensor_hop(others[0], 2))
    out_biases = [
        b.reshape(LAYERS, 1, width) for b in (self_output_bias, cross_output_bias, hidden_down_bias)
    ]

    count = len(firsts)
    along_x, along_y, over_x, over_y, sibs = [[None] * count for _ in range(5)]

    def leave(index):
        along_x[index] = tensor_hop(firsts[index], 2)

    def swap(index):
        sibs[index] = tensor_hop(owns[index], 1)

    def go_on(index):
        along_y[index] = dp_hop(along_x[index], 1)
        over_x[index] = tensor_hop(along_x[index], 1)

    def end(index):
        over_y[index] = tensor_hop(along_y[index], 1)

    def weights_of(index):
        return [
            owns[index],
            sibs[index],
            along_x[index],
            along_y[index],
            over_x[index],
            over_y[index],
        ]

    def open_gate(after, leaving=(), at_x=(), at_y=(), settled=()):
        places = [(firsts, i) for i in leaving]
        places += [(along_x, i) for i in at_x] + [(along_y, i) for i in at_y] + list(settled)
        opened = gate([values[i] for values, i in places], after)
        for (values, i), array in zip(places, opened):
            values[i] = array
        for i in leaving:
            leave(i)
        for i in at_x:
            go_on(i)
        for i in at_y:
            end(i)
        return list(opened)

    leave(0)
    swap(0)
    open_gate([mine], [], [0])
    open_gate([*others, along_x[0]], [1])
    swap(1)
    go_on(1)
    owns += [hidden_up, hidden_down]
    sibs[4:6] = tensor_hop(hidden_up, 1), tensor_hop(hidden_down, 1)
    mods, narrow_biases, up_biases = plain(
        partial(assemble_kernel, narrow=narrow, units=units, columns=columns),
        "modulation_of_all",
        info,
        [mine, *others],
        [
            shape(LAYERS, SLOTS, 4 * columns),
            shape(LAYERS, 8, 4 * narrow),
            shape(LAYERS, 1, 4 * units),
        ],
        after=[along_x[1]],
    )
    open_gate([mods], [], [], [0])

    text_rows = jnp.pad(text, ((0, 0), (0, LANES - words), (0, 0))).reshape(-1, width)
    whole = pltpu.VMEM((width, width), BF)
    four = pltpu.VMEM((4, width, units), BF)
    two = pltpu.VMEM((2, width, units), BF)
    floats = pltpu.VMEM((share, width), F32)
    lows = pltpu.VMEM((share, width), BF)
    sems = lambda n: pltpu.SemaphoreType.DMA((n,))
    frame_low = shape(share, width, dtype=BF)
    frame_high = shape(share, width)
    frame_wide = shape(share, 4 * units, dtype=BF)
    frame_chip = shape(share, 2 * units, dtype=BF)
    two_low = shape(2, share, width, dtype=BF)
    two_text = shape(2, SLOTS * LANES, width, dtype=BF)
    logs = shape(16, share)
    log_work = pltpu.VMEM((share, LANES), F32)
    stat_shape = shape(72, width)

    kept = []
    for layer in range(LAYERS):
        first = 2 * layer
        mod = (mods, (layer,))
        biases = (narrow_biases, (layer,))
        common = dict(w=pltpu.VMEM((2, width, width), BF), sems=sems(8))
        if layer == 0:
            entry1, kv, x = run(
                kv_kernel,
                "self_keys_values",
                info,
                {},
                dict(mod=mod, biases=biases),
                weights_of(first) + [tokens],
                dict(entry=frame_low, kv=two_low, x=frame_high),
                {},
                common | dict(rows=lows, row_sems=sems(1)),
                [along_x[1], sibs[1], sibs[4], sibs[5]],
                3.0,
            )
        else:
            entry1, kv, x, branch3 = run(
                kv_kernel,
                "residual_keys_values",
                info,
                dict(part=part, other=tensor_hop(part, 2), below=kept[-1]["x2"]),
                dict(
                    mod=mod,
                    mod_below=(mods, (layer - 1,)),
                    bias=(out_biases[2], (layer - 1,)),
                    biases=biases,
                ),
                weights_of(first),
                dict(entry=frame_low, kv=two_low, x=frame_high, branch=frame_low),
                {},
                common | dict(sum=floats),
                opened,
                3.0,
            )
            kept[-1]["branch3"] = branch3
        kv_sib = tensor_hop(kv, 1)
        opened = (
            open_gate([entry1], [2, 3], [], [], [(over_x, 1)])
            if layer == 0
            else open_gate([entry1], [5], [], [], [(over_x, 4), (over_y, 3)])
        )
        (q,) = run(
            q_kernel,
            "self_query",
            info,
            dict(entry=entry1),
            dict(biases=biases),
            weights_of(first),
            dict(q=frame_low),
            {},
            dict(w=whole, sems=sems(4)),
            [],
            15.0,
        )
        x1, mixed1, rest1, lse1, branch1 = run(
            self_kernel,
            "self_attention",
            info,
            dict(q=q, kv_own=kv, kv_sib=kv_sib, x=x),
            dict(mod=mod, bias=(out_biases[0], (layer,))),
            weights_of(first),
            dict(out=frame_high, mixed=frame_low, rest=frame_low, lse=logs, branch=frame_low),
            {},
            dict(wo=whole, logs=log_work, sum=floats, sems=sems(4)),
            opened,
            8.0,
        )
        if layer == 0:
            opened = open_gate([x1], [4], [2], [1], [(along_x, 3)])
            swap(2)
        else:
            opened = open_gate([x1], [], [5], [4])
        x2, entry2, cq, ckv, mixed2, lse2, branch2 = run(
            partial(cross_kernel, words=words),
            "cross_attention",
            info,
            dict(x=x1, text=text_rows),
            dict(mod=mod, biases=biases, bias=(out_biases[1], (layer,))),
            weights_of(first + 1),
            dict(
                out=frame_high,
                entry=frame_low,
                q=frame_low,
                kv=two_text,
                mixed=frame_low,
                lse=logs,
                branch=frame_low,
            ),
            {},
            dict(
                wq=whole, wk=whole, wv=whole, wo=whole, logs=log_work, sum=floats, sems=sems(16)
            ),
            opened,
            6.0,
        )
        if layer == 0:
            opened = open_gate([x2], [], [3], [2], [(over_x, 2), (sibs, 2), (along_x, 4)])
            swap(3)
        else:
            opened = open_gate([x2], [], [], [5], [(over_x, 5), (over_y, 4)])
        if layer == 0:
            part, entry3, active, slope = run(
                lambda info, work, w: hidden_kernel(info, work, w, 0),
                "feed_forward_part",
                info,
                dict(x=x2),
                dict(mod=mod, up_bias=(up_biases, (layer,))),
                [hidden_up, sibs[4], hidden_down, sibs[5]],
                dict(part=frame_low, entry=frame_low, active=frame_chip, slope=frame_chip),
                {},
                dict(
                    up=two, down=two, before=floats, sum=floats, sems=sems(2), down_sems=sems(2)
                ),
                opened,
                5.0,
            )
            opened = open_gate([part], [], [4], [3], [(over_x, 3), (over_y, 2), (sibs, 3)])
            x3 = branch3 = None
        else:
            x3 = branch3 = active = slope = entry3 = None
        kept.append(
            dict(
                x=x,
                entry1=entry1,
                q=q,
                kv=kv,
                kv_sib=kv_sib,
                mixed1=mixed1,
                rest1=rest1,
                lse1=lse1,
                branch1=branch1,
                x1=x1,
                entry2=entry2,
                cq=cq,
                ckv=ckv,
                mixed2=mixed2,
                lse2=lse2,
                branch2=branch2,
                x2=x2,
                entry3=entry3,
                active=active,
                slope=slope,
                branch3=branch3,
            )
        )
        x = x3
    last_gate = opened

    def join(rows, *after):
        return plain(
            join_kernel,
            "join_rows",
            info,
            [rows, tensor_hop(rows, 1)],
            [shape(2 * share, width, dtype=BF)],
            after=after,
        )


    chains = {}

    def start(name, send, keep):
        view = (size, unit, send.shape[1])
        chains[name] = (tensor_hop(send, 1).reshape(view), keep.reshape(view), 0)

    def held(*names):
        return [chains[name][1] for name in names]

    def advance(names, after=(), cost=1.5):
        targets = [(n, [n]) if isinstance(n, str) else n for n in names]
        targets = [t for t in targets if 2 ** chains[t[1][0]][2] < size]
        if not targets:
            return
        ins, in_specs, outs, out_specs, spots = [], [], [], [], []
        for result, (_, parts) in enumerate(targets):
            column = 0
            for name in parts:
                received, kept_part, bit = chains[name]
                blocks_left, rows, wide = received.shape
                spots.append((result, column))
                column += wide
                for side in range(2):

                    def at(i, info, bit=bit, side=side):
                        return (0, ((info[8] >> bit) & 1) ^ side, 0, 0)

                    for part in (received, kept_part):
                        ins.append(part.reshape(blocks_left // 2, 2, rows, wide))
                        in_specs.append(pl.BlockSpec((blocks_left // 2, None, rows, wide), at))
            for side in range(2):
                outs.append(shape(blocks_left // 2, rows, column, dtype=BF))
                out_specs.append(
                    pl.BlockSpec((blocks_left // 2, rows, column), lambda i, info: (0, 0, 0))
                )
        results = pl.pallas_call(
            partial(merge_kernel, spots=spots, after=len(after)),
            grid_spec=pltpu.PrefetchScalarGridSpec(
                num_scalar_prefetch=1,
                grid=(1,),
                in_specs=in_specs + [ANY] * len(after),
                out_specs=out_specs,
            ),
            out_shape=outs,
            compiler_params=pltpu.CompilerParams(vmem_limit_bytes=VMEM_BYTES),
            cost_estimate=lasting(cost),
            name="merge_grads",
        )(info, *ins, *after)
        for index, (name, parts) in enumerate(targets):
            bit = chains[parts[0]][2]
            hold, give = results[2 * index : 2 * index + 2]
            for part in parts:
                del chains[part]
            chains[name] = (dp_hop(give, 2**bit), hold, bit + 1)

    sums = []
    last = LAYERS - 1
    for layer in reversed(range(LAYERS)):
        first = 2 * layer
        k = kept[layer]
        mod = (mods, (layer,))
        above = layer + 1
        f_name, c_name, a_name, s_name = [f"{kind}{layer}" for kind in "fcas"]
        n_name = f"n{above}"

        def grads_out(members):
            return {name: shape(width, members * narrow, dtype=BF) for name in ("send", "keep")}

        older = []
        if layer < last:
            older = [f"f{above}", n_name]
            more = held(*older)
        if layer == last:
            f_send, f_keep, low, c_send, c_keep, g, stats = run(
                lambda info, work, w: hidden_cross_kernel(info, work, w, words),
                "feed_forward_cross_back",
                info,
                dict(
                    x2=k["x2"],
                    branch2=k["branch2"],
                    q=k["cq"],
                    kv=k["ckv"],
                    lse=k["lse2"],
                    entry2=k["entry2"],
                    text=text_rows,
                    mixed=k["mixed2"],
                    x1=k["x1"],
                ),
                dict(mod=mod, up_bias=(up_biases, (layer,)), bias=(out_biases[2], (layer,))),
                weights_of(4) + weights_of(5) + [cotangent] + weights_of(first + 1),
                {f"f_{name}": shape(width, 2 * units, dtype=BF) for name in ("send", "keep")}
                | dict(low=frame_low)
                | {f"c_{name}": shape(width, 4 * narrow, dtype=BF) for name in ("send", "keep")}
                | dict(out=frame_high),
                dict(stats=stat_shape),
                dict(
                    up=four,
                    down=four,
                    g=floats,
                    g_mid=floats,
                    rows=lows,
                    row_sems=sems(1),
                    gb=lows,
                    entry3=lows,
                    branch3=lows,
                    active=pltpu.VMEM((share, 4 * units), BF),
                    slope=pltpu.VMEM((share, 4 * units), BF),
                    d_before=pltpu.VMEM((share, 4 * units), BF),
                    before=floats,
                    sum=floats,
                    sems=sems(8),
                    down_sems=sems(8),
                    wq=whole,
                    wo=whole,
                    dkv=pltpu.VMEM(two_text.shape, BF),
                    dkv_sum=pltpu.VMEM(two_text.shape, F32),
                    cross_sems=sems(8),
                ),
                last_gate,
                10.0,
            )
            start(f_name, f_send, f_keep)
            start(c_name, c_send, c_keep)
        else:
            part, gb, d_before, stats = run(
                lambda info, work, w: hidden_back_kernel(info, work, w, 0),
                "feed_forward_back_part",
                info,
                dict(g=g, branch=k["branch3"], slope=k["slope"]),
                dict(mod=mod),
                [hidden_up, sibs[4], hidden_down, sibs[5]],
                dict(part=frame_low, gb=frame_low, d_before=frame_chip),
                dict(stats=stat_shape),
                dict(
                    up=two, down=two, before=floats, de=floats, sems=sems(2), down_sems=sems(2)
                ),
                more,
                5.0,
            )
            other = tensor_hop(part, 2)
            send, keep = run(
                hidden_grads_kernel,
                "feed_forward_grads",
                info,
                dict(entry=k["entry3"], d_before=d_before, gb=gb, active=k["active"]),
                {},
                [],
                {name: shape(width, 2 * units, dtype=BF) for name in ("send", "keep")},
                {},
                {},
                [gb],
                1.0,
            )
            start(f_name, send, keep)
            output = join(low, gb)
            advance(older, held(f_name), 0.5)
            extra = dict(part=part, other=other, above=k["x2"])
            scratch = dict(g_mid=floats)
        if layer < last:
            send, keep, g, stats = run(
                partial(cross_back_kernel, words=words),
                "cross_attention_back",
                info,
                dict(
                    g=g,
                    branch=k["branch2"],
                    q=k["cq"],
                    kv=k["ckv"],
                    lse=k["lse2"],
                    entry=k["entry2"],
                    text=text_rows,
                    mixed=k["mixed2"],
                    x=k["x1"],
                    **extra,
                ),
                dict(mod=mod, early=(stats, ())),
                weights_of(first + 1),
                grads_out(4) | dict(out=frame_high),
                dict(stats=stat_shape),
                dict(
                    wq=whole,
                    wo=whole,
                    gb=lows,
                    dq=lows,
                    dkv=pltpu.VMEM(two_text.shape, BF),
                    d_mixed=lows,
                    de=floats,
                    dkv_sum=pltpu.VMEM(two_text.shape, F32),
                    sems=sems(8),
                    **scratch,
                ),
                held(f_name, *older) + [output],
                60.0,
            )
            start(c_name, send, keep)
            advance([f_name, n_name], [g, chains[f"f{above}"][0]])
        gb1, dq, dkv_own, dkv_give, stats = run(
            self_back_kernel,
            "self_attention_back",
            info,
            dict(
                g=g,
                branch=k["branch1"],
                mixed=k["mixed1"],
                rest=k["rest1"],
                q=k["q"],
                kv_own=k["kv"],
                kv_sib=k["kv_sib"],
                lse=k["lse1"],
            ),
            dict(mod=mod, early=(stats, ())),
            weights_of(first),
            dict(gb=frame_low, dq=frame_low, dkv_own=two_low, dkv_give=two_low),
            dict(stats=stat_shape),
            dict(wo=whole, d_mixed=lows, inner=pltpu.VMEM((16, share), F32), sems=sems(4)),
            held(f_name, c_name, *([n_name] if layer < last else [])),
            13.0,
        )
        dkv_sib = tensor_hop(dkv_give, 1)
        advance([f_name, *([c_name] if layer < last else [])], [dq])
        send, keep = run(
            query_output_kernel,
            "query_output_grads",
            info,
            dict(entry=k["entry1"], gb=gb1, dq=dq, mixed=k["mixed1"]),
            {},
            [],
            grads_out(2),
            {},
            {},
            held(f_name, c_name),
            15.0,
        )
        start(a_name, send, keep)
        arriving = dict(dkv_own=dkv_own, dkv_sib=dkv_sib, entry=k["entry1"])
        if layer == 0:
            send, keep, dkv = run(
                kv_grads_kernel,
                "keys_values_grads",
                info,
                arriving,
                {},
                [],
                grads_out(2) | dict(dkv=two_low),
                {},
                {},
                held(a_name),
                4.0,
            )
            start(s_name, send, keep)
            rest = f"t{layer}"
            advance([f_name, c_name, (rest, [a_name, s_name])], held(s_name))
            arriving = dict(dkv=dkv)
        results = run(
            qkv_back_kernel,
            "self_qkv_back",
            info,
            arriving | dict(dq=dq, x=k["x"], g=g),
            dict(mod=mod, early=(stats, ())),
            weights_of(first),
            (dict(low=frame_low) if layer == 0 else grads_out(2)) | dict(out=frame_high),
            dict(stats=stat_shape),
            dict(wq=whole, wk=whole, wv=whole, de=floats, sems=sems(12))
            | (dict(dkv=pltpu.VMEM(two_low.shape, BF)) if layer else {}),
            held(f_name, c_name, rest if layer == 0 else a_name),
            6.0,
        )
        g, stats = results[-2:]
        if layer:
            start(s_name, *results[:2])
        if layer:
            advance([f_name, (f"n{layer}", [c_name, a_name, s_name])], [g])
        else:
            to_rest = [g, chains[f_name][0], chains[n_name][0]]
        sums = [stats, tensor_hop(stats, 1)] + sums
    vectors = plain(
        partial(collect_kernel, narrow=narrow, units=units, columns=columns),
        "collect_sums",
        info,
        [*sums, condition],
        [shape(16, mine.shape[2], dtype=BF)],
        [pltpu.VMEM(stat_shape.shape, F32), pltpu.VMEM((16, mine.shape[2]), F32)],
    )
    advance(["c0", "t0"], to_rest + [vectors])
    gathered, hop = vectors[None], size // 2

    def gather_sums():
        nonlocal gathered, hop
        if hop:
            both = jnp.stack([gathered, dp_hop(gathered, hop)], axis=1)
            gathered = both.reshape(-1, *vectors.shape)
            hop //= 2

    low = results[0]
    (low,) = gate([low], held("t0"))
    input_grad = join(low)

    def parts_of(*names):
        return [part.reshape(1, unit, -1) for name in names for part in chains[name][:2]]

    up_grad, down_grad = plain(
        partial(finish_kernel, wide=True, spots=[(0, [(0, 0)]), (0, [(1, 0)])]),
        "finish_wide",
        None,
        parts_of("f0", "f1"),
        [shape(LAYERS, unit, units)] * 2,
    )
    ready = [input_grad, up_grad, chains["c0"][0]]
    while any(2 ** chain[2] < size for chain in chains.values()):
        gather_sums()
        advance(list(chains), held("t0") + [gathered] + ready)
    while hop:
        gather_sums()
    straight, across = shape(LAYERS, unit, narrow), shape(LAYERS, narrow, unit)
    spots = [(0, [(1, 0), (1, 1), (1, 2), (1, 3)])]
    spots += [(0, [(0, 0), (0, 1)]), (0, [(0, 2), (0, 3)])]
    cq_grad, ck_grad, cv_grad, co_grad, q_grad, o_grad, k_grad, v_grad = plain(
        partial(finish_kernel, wide=False, spots=spots),
        "finish_narrow",
        None,
        parts_of("n1", "c0", "t0"),
        [straight, straight, straight, across, straight, across, straight, straight],
    )
    small = plain(
        spread_kernel,
        "spread_sums",
        info,
        [gathered],
        [shape(LAYERS, unit, columns), shape(LAYERS, columns)]
        + [shape(LAYERS, narrow)] * 4
        + [shape(LAYERS, units)]
        + [shape(LAYERS, unit)] * 3,
        [pltpu.VMEM((SLOTS * size, columns), F32), pltpu.VMEM((SLOTS * size, width), F32)],
    )
    mod_grad, mod_bias_grad, q_sum, v_sum, cq_sum, cv_sum, up_sum, o1, o2, o3 = small
    return (
        output,
        input_grad,
        q_grad,
        q_sum,
        k_grad,
        v_grad,
        v_sum,
        o_grad,
        o1,
        cq_grad,
        cq_sum,
        ck_grad,
        cv_grad,
        cv_sum,
        co_grad,
        o2,
        up_grad,
        up_sum,
        turn(down_grad),
        o3,
        mod_grad,
        mod_bias_grad,
    )


def solution(mesh):
    dp, tensor = "dp", "tensor"
    columns, vector = P(None, None, tensor), P(None, tensor)
    matrix, turned, spread = P(None, dp, tensor), P(None, tensor, dp), P(None, dp)
    placed = (
        P(dp, None),
        P(dp, None, None),
        P(dp),
        P(dp),
        P(dp, None),
        columns,
        vector,
        columns,
        columns,
        vector,
        P(None, tensor, None),
        P(),
        columns,
        vector,
        columns,
        columns,
        vector,
        P(None, tensor, None),
        P(),
        columns,
        vector,
        P(None, tensor, None),
        P(),
        columns,
        vector,
    )
    results = (
        P(dp, None),
        P(dp, None),
        matrix,
        vector,
        matrix,
        matrix,
        vector,
        turned,
        spread,
        matrix,
        vector,
        matrix,
        matrix,
        vector,
        turned,
        spread,
        matrix,
        vector,
        turned,
        spread,
        matrix,
        vector,
    )
    return jax.shard_map(
        shards, mesh=mesh, in_specs=placed, out_specs=results, check_vma=False
    )
```

```python
from functools import partial
import math

import jax
import jax.numpy as jnp
from jax import lax
from jax.experimental import pallas as pl
from jax.experimental.pallas import tpu as pltpu
from jax.sharding import PartitionSpec as P

HEAD_WIDTH = 64
UNIT = 256
LAYERS = 2
WINDOW = 1024
EPSILON = 1e-06
LANES = 128
CHUNK = 64
SLOTS = WINDOW // UNIT
FAR = -1e30
SIDES = ("send", "keep")
VMEM_BYTES = 66_000_000
BF = jnp.bfloat16
F32 = jnp.float32
ROOT = math.sqrt(2.0 / math.pi)
CUBIC = 0.044715


def dot_nn(left, right):
    return jnp.dot(left, right, preferred_element_type=F32)


def dot_nt(left, right):
    return lax.dot_general(left, right, (((1,), (1,)), ((), ())), preferred_element_type=F32)


def dot_tn(left, right):
    return lax.dot_general(left, right, (((0,), (0,)), ((), ())), preferred_element_type=F32)


SMALL = pl.BlockSpec(memory_space=pltpu.SMEM)
NEAR = pl.BlockSpec(memory_space=pltpu.VMEM)
ANY = pl.BlockSpec(memory_space=pl.ANY)


class Work:
    def __init__(self, ins, outs, scratch, in_sems, out_sems):
        self.ins, self.outs, self.scratch, self.out_sems = ins, outs, scratch, out_sems
        self.copies, self.waited, self.flushed = {}, set(), []
        for index, (name, (ref, buffer)) in enumerate(ins.items()):
            self.copies[name] = pltpu.make_async_copy(ref, buffer, in_sems.at[index])
            self.copies[name].start()

    def __getattr__(self, name):
        if name in self.__dict__["ins"]:
            return self.ins[name][1]
        if name in self.__dict__["outs"]:
            return self.outs[name][1]
        return self.__dict__["scratch"][name]

    def has(self, name):
        return name in self.outs

    def takes(self, name):
        return name in self.ins

    def send(self, name, source, *at):
        ref = self.outs[name][0]
        copy = pltpu.make_async_copy(
            source, ref.at[at] if at else ref, self.out_sems.at[len(self.flushed)]
        )
        copy.start()
        self.flushed.append(copy)

    def need(self, *names):
        for name in names:
            if name not in self.waited:
                self.waited.add(name)
                self.copies[name].wait()

    def flush(self, name, *at):
        ref, buffer = self.outs[name]
        if at:
            ref, buffer = ref.at[at], buffer.at[at]
        copy = pltpu.make_async_copy(buffer, ref, self.out_sems.at[len(self.flushed)])
        copy.start()
        self.flushed.append(copy)

    def finish(self):
        self.need(*self.ins)
        for copy in self.flushed:
            copy.wait()


class Names:
    def __init__(self, work, **names):
        self.work, self.names = work, names

    def to(self, name):
        return self.__dict__["names"].get(name, name)

    def __getattr__(self, name):
        return getattr(self.__dict__["work"], self.to(name))

    @property
    def outs(self):
        return {name: self.work.outs[self.to(name)] for name in SIDES}

    def has(self, name):
        return self.work.has(self.to(name))

    def takes(self, name):
        return self.work.takes(self.to(name))

    def need(self, *names):
        self.work.need(*[name for name in map(self.to, names) if self.work.takes(name)])

    def flush(self, name, *at):
        if self.has(name):
            self.work.flush(self.to(name), *at)


def run(body, name, info, ins, small, weights, outs, small_outs, scratch, after=(), cost=1.0):
    in_names, out_names, names = list(ins), list(outs), list(scratch)
    small_names, small_out_names = list(small), list(small_outs)
    counts = [1, len(in_names), len(small), len(weights), len(after), len(outs), len(small_outs)]

    def kernel(*refs):
        refs = list(refs)
        parts = []
        for count in counts:
            parts.append(refs[:count])
            refs = refs[count:]
        (info_ref,), in_refs, small_refs, weight_refs, _, out_refs, small_out_refs = parts
        in_bufs, refs = refs[: len(in_names)], refs[len(in_names) :]
        out_bufs, refs = refs[: len(out_names)], refs[len(out_names) :]
        rest, (in_sems, out_sems) = refs[:-2], refs[-2:]
        extra = {}
        rest = list(rest)
        for key in names:
            many = isinstance(scratch[key], list)
            size = len(scratch[key]) if many else 1
            extra[key] = rest[:size] if many else rest[0]
            rest = rest[size:]
        for key, ref in zip(small_names, small_refs):
            index = small[key][1]
            extra[key] = ref.at[index] if index else ref
        extra.update(zip(small_out_names, small_out_refs))
        work = Work(
            dict(zip(in_names, zip(in_refs, in_bufs))),
            dict(zip(out_names, zip(out_refs, out_bufs))),
            extra,
            in_sems,
            out_sems,
        )
        body(info_ref, work, weight_refs)
        work.finish()

    buffer = lambda a: pltpu.VMEM(a.shape, a.dtype)
    flat = []
    for value in scratch.values():
        flat += value if isinstance(value, list) else [value]
    results = pl.pallas_call(
        kernel,
        out_shape=[outs[n] for n in out_names] + [small_outs[n] for n in small_out_names],
        in_specs=[SMALL]
        + [ANY] * len(ins)
        + [NEAR] * len(small)
        + [ANY] * (len(weights) + len(after)),
        out_specs=[ANY] * len(outs) + [NEAR] * len(small_outs),
        scratch_shapes=[buffer(ins[n]) for n in in_names]
        + [buffer(outs[n]) for n in out_names]
        + flat
        + [pltpu.SemaphoreType.DMA((max(len(ins), 1),)), pltpu.SemaphoreType.DMA((32,))],
        compiler_params=pltpu.CompilerParams(vmem_limit_bytes=VMEM_BYTES),
        cost_estimate=lasting(cost),
        name=name,
    )(info, *ins.values(), *[array for array, _ in small.values()], *weights, *after)
    return results


def plain(body, name, info, ins, outs, scratch=(), after=()):
    first = len(ins) + (0 if info is None else 1)
    results = pl.pallas_call(
        lambda *refs: body(*refs[:first], *refs[first + len(after) :]),
        out_shape=outs,
        in_specs=([] if info is None else [SMALL]) + [NEAR] * len(ins) + [ANY] * len(after),
        out_specs=[NEAR] * len(outs),
        scratch_shapes=list(scratch),
        compiler_params=pltpu.CompilerParams(vmem_limit_bytes=VMEM_BYTES),
        cost_estimate=lasting(0.05),
        name=name,
    )(*([] if info is None else [info]), *ins, *after)
    return results if len(outs) > 1 else results[0]


def lasting(units):
    return pl.CostEstimate(flops=int(units * 0.4e9), bytes_accessed=1000, transcendentals=0)


def shape(*dims, dtype=F32):
    return jax.ShapeDtypeStruct(dims, dtype)


def start_rows(refs, place, plan, sems):
    own, sib, xa, ya, xb, yb = refs
    half = own.shape[0] // 2
    for rank in range(4):
        for parity in range(2):

            @pl.when(place == rank * 2 + parity)
            def _(rank=rank, parity=parity):
                for index, (shard, row, rows, dst) in enumerate(plan):
                    step = shard ^ rank
                    if step < 2:
                        src = (own, sib)[step].at[pl.ds(row, rows)]
                    else:
                        first, second = ((xa, ya), (xb, yb))[step - 2]
                        part = row // half
                        src = (first if part == parity else second).at[pl.ds(row - part * half, rows)]
                    pltpu.make_async_copy(src, dst, sems.at[index]).start()


def wait_rows(refs, plan, sems, which):
    for index in which:
        _, row, rows, dst = plan[index]
        pltpu.make_async_copy(refs[0].at[pl.ds(0, rows)], dst, sems.at[index]).wait()


def plan_of(buffers, first, rows):
    return [
        (shard, (first + which) * rows, rows, dst.at[pl.ds(shard * rows, rows)])
        for which, dst in enumerate(buffers)
        for shard in range(4)
    ]


def norm_rows(values):
    mean = jnp.mean(values, axis=-1, keepdims=True)
    center = values - mean
    factor = lax.rsqrt(jnp.mean(center * center, axis=-1, keepdims=True) + EPSILON)
    return center * factor, factor


def piece(mod, slot, index):
    width = mod.shape[1] // 9
    return mod[pl.ds(slot, 1), index * width : (index + 1) * width]


def entry_rows(x, mod, info, index, out):
    for block in range(x.shape[0] // UNIT):
        slot = info[1 + block]
        shift = piece(mod, slot, index)
        scale = 1.0 + piece(mod, slot, index + 1)

        def step(turn, carry):
            rows = pl.ds(pl.multiple_of(block * UNIT + turn * CHUNK, CHUNK), CHUNK)
            normed, _ = norm_rows(x[rows, :])
            out[rows, :] = (normed * scale + shift).astype(BF)
            return carry

        lax.fori_loop(0, UNIT // CHUNK, step, 0, unroll=True)


def residual_rows(x, mod, info, index, branch, branch_out, out, low=None):
    for block in range(x.shape[0] // UNIT):
        gate = piece(mod, info[1 + block], index)

        def step(turn, carry):
            rows = pl.ds(pl.multiple_of(block * UNIT + turn * CHUNK, CHUNK), CHUNK)
            values = branch[rows, :]
            branch_out[rows, :] = values.astype(BF)
            result = x[rows, :] + gate * values
            out[rows, :] = result
            if low is not None:
                low[rows, :] = result.astype(BF)
            return carry

        lax.fori_loop(0, UNIT // CHUNK, step, 0, unroll=True)


def fold(values):
    return jnp.sum(values.reshape(values.shape[0] // 8, 8, values.shape[1]), axis=0)


def total(values):
    return jnp.sum(values, axis=0, keepdims=True)


def gate_back(g, mod, info, index, branch, gb, stats):
    width = g.shape[1]
    sums = jnp.zeros((8, width), F32)
    for block in range(g.shape[0] // UNIT):
        slot = info[1 + block]
        gate = piece(mod, slot, index)

        def step(turn, carry):
            rows = pl.ds(pl.multiple_of(block * UNIT + turn * CHUNK, CHUNK), CHUNK)
            grad = g[rows, :]
            low = (gate * grad).astype(BF)
            gb[rows, :] = low
            return (
                carry[0] + fold(low.astype(F32)),
                carry[1] + fold(grad * branch[rows, :].astype(F32)),
            )

        sums, rows_sum = lax.fori_loop(
            0, UNIT // CHUNK, step, (sums, jnp.zeros((8, width), F32)), unroll=True
        )
        stats[pl.ds(8 + slot, 1), :] += total(rows_sum)
    stats[12:13, :] = total(sums)


def norm_back_rows(x, g, de, mod, info, index, out, stats, low=None):
    width = x.shape[1]
    for block in range(x.shape[0] // UNIT):
        slot = info[1 + block]
        scale = 1.0 + piece(mod, slot, index + 1)

        def step(turn, carry):
            rows = pl.ds(pl.multiple_of(block * UNIT + turn * CHUNK, CHUNK), CHUNK)
            normed, factor = norm_rows(x[rows, :])
            grad = de[rows, :]
            inner = grad * normed
            dn = grad * scale
            mean = jnp.mean(dn, axis=-1, keepdims=True)
            along = jnp.mean(dn * normed, axis=-1, keepdims=True)
            result = g[rows, :] + factor * (dn - mean - normed * along)
            out[rows, :] = result
            if low is not None:
                low[rows, :] = result.astype(BF)
            return (carry[0] + fold(grad), carry[1] + fold(inner))

        zero = jnp.zeros((8, width), F32)
        shift_sum, scale_sum = lax.fori_loop(0, UNIT // CHUNK, step, (zero, zero), unroll=True)
        stats[pl.ds(slot, 1), :] += total(shift_sum)
        stats[pl.ds(4 + slot, 1), :] += total(scale_sum)


def lane_ids(rows):
    return lax.broadcasted_iota(jnp.int32, (rows, LANES), 1)


def head_half(values, half):
    ids = lane_ids(values.shape[0])
    keep = ids < HEAD_WIDTH if half == 0 else ids >= HEAD_WIDTH
    return jnp.where(keep, values.astype(F32), 0.0)


def turned_halves(keys):
    turned = keys.T
    low = lax.broadcasted_iota(jnp.int32, turned.shape, 0) < HEAD_WIDTH
    zero = jnp.zeros(turned.shape, turned.dtype)
    return jnp.concatenate([jnp.where(low, turned, zero), jnp.where(low, zero, turned)], axis=1)


def query_marks(slot):
    return jnp.where(lane_ids(UNIT) == slot, 1.0, 0.0).astype(BF)


def key_marks(slots):
    ids = lane_ids(UNIT)
    parts = [jnp.where((ids < SLOTS) & (ids != slot), FAR, 0.0).astype(BF) for slot in slots]
    return jnp.concatenate(parts, axis=0)


def pair_lanes(pair):
    return pl.ds(pl.multiple_of(pair * LANES, LANES), LANES)


def start_own_rows(info, work, whole):
    share = work.rows.shape[0]
    first = pl.multiple_of((info[5] % 2) * share, share)
    copy = pltpu.make_async_copy(whole.at[pl.ds(first, share)], work.rows, work.row_sems.at[0])
    copy.start()
    return copy


def raise_rows(low, out):
    for row in range(0, low.shape[0], CHUNK):
        span = pl.ds(row, CHUNK)
        out[span, :] = low[span, :].astype(F32)


def kv_kernel(info, work, weights):
    rows = weights[0].shape[0] // 4
    plan = plan_of((work.w.at[0], work.w.at[1]), 1, rows)
    start_rows(weights[:6], info[0], plan, work.sems)
    if work.has("branch"):
        work.need("part", "other", "below")
        bias = work.bias[...].astype(F32)
        for row in range(0, work.sum.shape[0], CHUNK):
            span = pl.ds(row, CHUNK)
            work.sum[span, :] = (
                work.part[span, :].astype(F32) + work.other[span, :].astype(F32) + bias
            )
        residual_rows(work.below, work.mod_below, info, 8, work.sum, work.branch, work.x)
        work.flush("branch")
        work.flush("x")
    else:
        start_own_rows(info, work, weights[6]).wait()
        raise_rows(work.rows, work.x)
        work.flush("x")
    entry_rows(work.x, work.mod, info, 0, work.entry)
    work.flush("entry")
    entry = work.entry[...]
    wait_rows(weights, plan, work.sems, range(4))
    work.kv[0] = dot_nt(entry, work.w[0]).astype(BF)
    work.flush("kv", 0)
    wait_rows(weights, plan, work.sems, range(4, 8))
    work.kv[1] = (dot_nt(entry, work.w[1]) + work.biases[2:3, :]).astype(BF)
    work.flush("kv", 1)


def q_kernel(info, work, weights):
    rows = weights[0].shape[0] // 4
    plan = plan_of((work.w,), 0, rows)
    start_rows(weights, info[0], plan, work.sems)
    work.need("entry")
    wait_rows(weights, plan, work.sems, range(4))
    work.q[...] = (dot_nt(work.entry[...], work.w[...]) + work.biases[0:1, :]).astype(BF)
    work.flush("q")


def soft_pair(work, q_pair, keys, values, marks, logs, pair, span, words=None):
    ids = lane_ids(UNIT)
    results = []
    kept = logs[span, :]
    for half in range(2):
        left = (head_half(q_pair, half) * HEAD_WIDTH**-0.5).astype(BF)
        if marks is not None:
            left = jnp.concatenate([left, marks], axis=1)
        scores = dot_nt(left, keys)
        if words is not None:
            scores = jnp.where(ids < words, scores, FAR)
        peak = jnp.max(scores, axis=-1, keepdims=True)
        both = dot_nn(jnp.exp(scores - peak).astype(BF), values)
        sums = both[:, LANES:]
        results.append(both[:, :LANES] / sums)
        kept = jnp.where(ids == 2 * pair + half, peak + jnp.log(sums), kept)
    logs[span, :] = kept
    return jnp.where(ids < HEAD_WIDTH, results[0], results[1])


def self_kernel(info, work, weights):
    rows = weights[0].shape[0] // 4
    sems = work.sems
    plan = [(s, 3 * rows, rows, work.wo.at[pl.ds(s * rows, rows)]) for s in range(4)]
    start_rows(weights, info[0], plan, sems)
    share = work.x.shape[0]
    blocks = share // UNIT
    marks = key_marks([info[1 + b] for b in range(2 * blocks)])
    ones = jnp.ones((2 * share, LANES), BF)
    logs, mixed = work.logs, work.mixed
    logs[...] = jnp.zeros(logs.shape, F32)
    work.need("q", "kv_own", "kv_sib")

    def both(which, lanes):
        return jnp.concatenate([work.kv_own[which, :, lanes], work.kv_sib[which, :, lanes]], axis=0)

    def step(pair, carry):
        lanes = pair_lanes(pair)
        keys = jnp.concatenate([both(0, lanes), marks], axis=1)
        values = jnp.concatenate([both(1, lanes), ones], axis=1)
        for block in range(blocks):
            span = pl.ds(block * UNIT, UNIT)
            values_mixed = soft_pair(
                work,
                work.q[span, lanes],
                keys,
                values,
                query_marks(info[1 + block]),
                logs,
                pair,
                span,
            )
            low = values_mixed.astype(BF)
            mixed[span, lanes] = low
            work.rest[span, lanes] = (values_mixed - low.astype(F32)).astype(BF)
        return carry

    lax.fori_loop(0, mixed.shape[1] // LANES, step, 0)
    work.flush("mixed")
    work.flush("rest")
    work.lse[...] = logs[...].T[: work.lse.shape[0], :]
    work.flush("lse")
    wait_rows(weights, plan, sems, range(4))
    work.sum[...] = dot_nn(mixed[...], work.wo[...]) + work.bias[...].astype(F32)
    work.need("x")
    residual_rows(work.x, work.mod, info, 2, work.sum, work.branch, work.out)
    work.flush("branch")
    work.flush("out")


def cross_kernel(info, work, weights, words):
    rows = weights[0].shape[0] // 4
    sems = work.sems
    order = (1, 2, 0, 3)
    plan = [
        (shard, order[i // 4] * rows, count, dst)
        for i, (shard, _, count, dst) in enumerate(
            plan_of((work.wk, work.wv, work.wq, work.wo), 0, rows)
        )
    ]
    start_rows(weights, info[0], plan, sems)
    work.need("x")
    entry_rows(work.x, work.mod, info, 3, work.entry)
    work.flush("entry")
    work.need("text")
    wait_rows(weights, plan, sems, range(0, 4))
    work.kv[0] = dot_nt(work.text[...], work.wk[...]).astype(BF)
    wait_rows(weights, plan, sems, range(4, 8))
    work.kv[1] = (dot_nt(work.text[...], work.wv[...]) + work.biases[5:6, :]).astype(BF)
    work.flush("kv")
    wait_rows(weights, plan, sems, range(8, 12))
    work.q[...] = (dot_nt(work.entry[...], work.wq[...]) + work.biases[3:4, :]).astype(BF)
    work.flush("q")
    ones = jnp.ones((LANES, LANES), BF)
    logs, mixed = work.logs, work.mixed
    logs[...] = jnp.zeros(logs.shape, F32)

    def step(pair, carry):
        lanes = pair_lanes(pair)
        for block in range(mixed.shape[0] // UNIT):
            span = pl.ds(block * UNIT, UNIT)
            own = pl.ds(pl.multiple_of(info[1 + block] * LANES, LANES), LANES)
            mixed[span, lanes] = soft_pair(
                work,
                work.q[span, lanes],
                work.kv[0, own, lanes],
                jnp.concatenate([work.kv[1, own, lanes], ones], axis=1),
                None,
                logs,
                pair,
                span,
                words,
            ).astype(BF)
        return carry

    lax.fori_loop(0, mixed.shape[1] // LANES, step, 0, unroll=2)
    work.flush("mixed")
    work.lse[...] = logs[...].T[: work.lse.shape[0], :]
    work.flush("lse")
    wait_rows(weights, plan, sems, range(12, 16))
    work.sum[...] = dot_nn(mixed[...], work.wo[...]) + work.bias[...].astype(F32)
    residual_rows(work.x, work.mod, info, 5, work.sum, work.branch, work.out)
    work.flush("branch")
    work.flush("out")


def hidden_plan(refs, buffer):
    rows = buffer.shape[1]
    half = rows // 2
    return [
        (shard, row, half, buffer.at[shard, pl.ds(row, half)])
        for shard in range(4)
        for row in range(0, rows, half)
    ]


def start_chip(info, refs, layer, buffer, sems):
    copies = [
        pltpu.make_async_copy(ref.at[layer], buffer.at[(info[5] + i) % 2], sems.at[i])
        for i, ref in enumerate(refs)
    ]
    for copy in copies:
        copy.start()
    return copies


def bend_rows(before, bias, active, slope, lanes):
    for row in range(0, before.shape[0], CHUNK):
        span = pl.ds(row, CHUNK)
        values = before[span, :] + bias
        square = values * values
        half = 1.0 / (1.0 + jnp.exp(values * (-2.0 * ROOT - (2.0 * ROOT * CUBIC) * square)))
        act = values * half
        active[span, lanes] = act.astype(BF)
        slope[span, lanes] = (
            half + act * (1.0 - half) * (2.0 * ROOT + (6.0 * ROOT * CUBIC) * square)
        ).astype(BF)


def columns_of(shard, width):
    return pl.ds(pl.multiple_of(shard * width, width), width)


def start_hidden(info, work, weights, layer):
    if len(weights) == 4:
        ups = start_chip(info, weights[:2], layer, work.up, work.sems)
        downs = start_chip(info, weights[2:], layer, work.down, work.down_sems)
        return [lambda some=some: [copy.wait() for copy in some] for some in (ups, downs)]
    waits = []
    for refs, buffer, sems in (
        (weights[:6], work.up, work.sems),
        (weights[6:12], work.down, work.down_sems),
    ):
        refs = [ref.at[layer] for ref in refs[:2]] + list(refs[2:])
        plan = hidden_plan(refs, buffer)
        start_rows(refs, info[0], plan, sems)
        waits.append(
            lambda refs=refs, plan=plan, sems=sems: wait_rows(refs, plan, sems, range(len(plan)))
        )
    return waits


def hidden_kernel(info, work, weights, layer):
    waits = start_hidden(info, work, weights, layer)
    width = work.x.shape[1]
    shards = work.up.shape[0]
    first = info[6] * 2
    work.need("x")
    entry_rows(work.x, work.mod, info, 6, work.entry)
    work.flush("entry")
    for wait in waits:
        wait()
    work.sum[...] = jnp.zeros(work.sum.shape, F32)

    def step(shard, carry):
        lanes = columns_of(shard, width)
        bias = work.up_bias[:, columns_of(first + shard, width)]
        work.before[...] = dot_nn(work.entry[...], work.up[shard])
        bend_rows(work.before, bias, work.active, work.slope, lanes)
        work.sum[...] += dot_nn(work.active[:, lanes], work.down[shard])
        return carry

    lax.fori_loop(0, shards, step, 0)
    work.flush("active")
    work.flush("slope")
    work.part[...] = work.sum[...].astype(BF)
    work.flush("part")


def hidden_back_kernel(info, work, weights, layer):
    waits = start_hidden(info, work, weights, layer)
    work.stats[...] = jnp.zeros(work.stats.shape, F32)
    stats = work.stats.at[pl.ds(48, 24)]
    work.need("g", "branch")
    gate_back(work.g, work.mod, info, 8, work.branch, work.gb, stats)
    work.need("slope")
    for wait in waits:
        wait()
    hidden_back_rows(info, work, work.de, stats)
    work.part[...] = work.de[...].astype(BF)
    work.flush("part")
    work.flush("gb")
    work.flush("d_before")


def hidden_back_rows(info, work, de, stats):
    width = work.g.shape[1]
    shards = work.up.shape[0]
    first = info[6] * 2 if shards == 2 else 0
    de[...] = jnp.zeros(de.shape, F32)

    def step(shard, carry):
        lanes = columns_of(shard, width)
        work.before[...] = dot_nt(work.gb[...], work.down[shard])
        sums = jnp.zeros((8, width), F32)
        for row in range(0, work.g.shape[0], CHUNK):
            span = pl.ds(row, CHUNK)
            low = (work.before[span, :] * work.slope[span, lanes].astype(F32)).astype(BF)
            work.d_before[span, lanes] = low
            sums += fold(low.astype(F32))
        stats[pl.ds(13 + first + shard, 1), :] = total(sums)
        de[...] += dot_nt(work.d_before[:, lanes], work.up[shard])
        return carry

    lax.fori_loop(0, shards, step, 0)


def hidden_both_kernel(info, work, weights, layer):
    copy = start_own_rows(info, work, weights[12])
    waits = start_hidden(info, work, weights, layer)
    width = work.x.shape[1]
    work.need("x")
    entry_rows(work.x, work.mod, info, 6, work.entry)
    for wait in waits:
        wait()
    work.sum[...] = jnp.zeros(work.sum.shape, F32) + work.bias[...].astype(F32)

    def step(shard, carry):
        lanes = columns_of(shard, width)
        work.before[...] = dot_nn(work.entry[...], work.up[shard])
        bend_rows(work.before, work.up_bias[:, lanes], work.active, work.slope, lanes)
        work.sum[...] += dot_nn(work.active[:, lanes], work.down[shard])
        return carry

    lax.fori_loop(0, 4, step, 0)
    residual_rows(work.x, work.mod, info, 8, work.sum, work.branch, work.out, work.low)
    work.flush("low")
    work.stats[...] = jnp.zeros(work.stats.shape, F32)
    stats = work.stats.at[pl.ds(48, 24)]
    copy.wait()
    raise_rows(work.rows, work.g)
    gate_back(work.g, work.mod, info, 8, work.branch, work.gb, stats)
    hidden_back_rows(info, work, work.sum, stats)
    left, right = work.entry[...].T, work.gb[...].T
    for name, rank in zip(SIDES, (info[7], info[5])):
        out = work.outs[name][1]
        lanes = columns_of(rank, width)
        out[:, :width] = dot_nn(left, work.d_before[:, lanes]).astype(BF)
        out[:, width:] = dot_nn(right, work.active[:, lanes]).astype(BF)
        work.flush(name)
    norm_back_rows(work.x, work.g, work.sum, work.mod, info, 6, work.out, stats)
    work.flush("out")


def hidden_cross_kernel(info, work, weights, words):
    hidden_both_kernel(
        info,
        Names(
            work,
            x="x2",
            entry="entry3",
            branch="branch3",
            out="g_mid",
            send="f_send",
            keep="f_keep",
        ),
        weights[:13],
        1,
    )
    cross_back_kernel(
        info,
        Names(
            work,
            early="stats",
            g="g_mid",
            branch="branch2",
            entry="entry2",
            x="x1",
            de="sum",
            dq="entry3",
            d_mixed="rows",
            sems="csems",
            send="c_send",
            keep="c_keep",
        ),
        weights[13:],
        words,
    )


def attention_kernel(info, work, weights, words):
    self_kernel(
        info,
        Names(work, out="x1", mixed="mixed1", lse="lse1", branch="branch1", bias="self_bias"),
        weights[:6],
    )
    cross_kernel(
        info,
        Names(
            work,
            x="x1",
            q="cq",
            kv="ckv",
            mixed="mixed2",
            lse="lse2",
            branch="branch2",
            bias="cross_bias",
            wo="cross_wo",
            sems="csems",
        ),
        weights[6:],
        words,
    )


def hidden_grads_kernel(info, work, weights):
    width = work.entry.shape[1]
    work.need("entry", "d_before", "gb", "active")
    left, right = work.entry[...].T, work.gb[...].T
    for name, shift in zip(SIDES, (1, 0)):
        out = work.outs[name][1]
        lanes = columns_of((info[5] + shift) % 2, width)
        out[:, :width] = dot_nn(left, work.d_before[:, lanes]).astype(BF)
        out[:, width:] = dot_nn(right, work.active[:, lanes]).astype(BF)
        work.flush(name)


def pair_grads(info, work, members):
    rows = members[0][0].shape[0]
    low = lane_ids(rows) < HEAD_WIDTH
    step = 3 * LANES
    for at in range(len(members) // 2):
        products = [dot_nn(left, right) for left, right in members[2 * at : 2 * at + 2]]
        (a0, a1, a2), (b0, b1, b2) = [
            [p[:, i * LANES : (i + 1) * LANES] for i in range(3)] for p in products
        ]
        even = (a0, b0, jnp.where(low, a1, pltpu.roll(b1, HEAD_WIDTH, 1)))
        a1, b1 = pltpu.roll(a1, HEAD_WIDTH, 1), pltpu.roll(b1, HEAD_WIDTH, 1)
        a2r, b2r = pltpu.roll(a2, HEAD_WIDTH, 1), pltpu.roll(b2, HEAD_WIDTH, 1)
        odd = (jnp.where(low, a1, a2r), jnp.where(low, b1, b2r), jnp.where(low, a2r, b2))
        first = info[5] % 2 == 0
        for i, (mine, other) in enumerate(zip(even, odd)):
            lanes = pl.ds(at * step + i * LANES, LANES)
            work.outs["keep"][1][:, lanes] = jnp.where(first, mine, other).astype(BF)
            work.outs["send"][1][:, lanes] = jnp.where(first, other, mine).astype(BF)
    work.flush("send")
    work.flush("keep")


def chip_lanes(info, width):
    return pl.ds(pl.multiple_of(info[6] * (width // 2), width // 2), width // 2)


def query_output_kernel(info, work, weights):
    work.need("entry", "gb", "dq", "mixed")
    lanes = chip_lanes(info, work.dq.shape[1])
    pair_grads(
        info,
        work,
        [
            (work.entry[...].T, work.dq[:, lanes]),
            (work.gb[...].T, work.mixed[:, lanes]),
        ],
    )


def cross_back_kernel(info, work, weights, words):
    rows = weights[0].shape[0] // 4
    sems = work.sems
    plan = [
        (shard, (3 * rows, 0)[i // 4], count, dst)
        for i, (shard, _, count, dst) in enumerate(plan_of((work.wo, work.wq), 0, rows))
    ]
    start_rows(weights, info[0], plan, sems)
    work.stats[...] = work.early[...]
    stats = work.stats.at[pl.ds(24, 24)]
    g = work.g
    work.need("g")
    if work.takes("part"):
        work.need("part", "other", "above")
        for row in range(0, g.shape[0], CHUNK):
            span = pl.ds(row, CHUNK)
            work.de[span, :] = work.part[span, :].astype(F32) + work.other[span, :].astype(F32)
        g = work.g_mid
        norm_back_rows(
            work.above, work.g, work.de, work.mod, info, 6, g, work.stats.at[pl.ds(48, 24)]
        )
    work.need("branch")
    gate_back(g, work.mod, info, 5, work.branch, work.gb, stats)
    wait_rows(weights, plan, sems, range(0, 4))
    work.d_mixed[...] = dot_nt(work.gb[...], work.wo[...]).astype(BF)
    work.dkv_sum[...] = jnp.zeros(work.dkv_sum.shape, F32)
    real = lax.broadcasted_iota(jnp.int32, (LANES, UNIT), 0) < words
    work.need("q", "kv", "lse")

    def step(pair, carry):
        lanes = pair_lanes(pair)
        for block in range(work.q.shape[0] // UNIT):
            span = pl.ds(block * UNIT, UNIT)
            own = pl.ds(pl.multiple_of(info[1 + block] * LANES, LANES), LANES)
            q_pair = work.q[span, lanes]
            d_pair = work.d_mixed[span, lanes]
            keys = work.kv[0, own, lanes]
            values = work.kv[1, own, lanes]
            lefts, grads, probs_low, scores_low = [], [], [], []
            for half in range(2):
                left = (head_half(q_pair, half) * HEAD_WIDTH**-0.5).astype(BF)
                grad = head_half(d_pair, half).astype(BF)
                logs = work.lse[pl.ds(2 * pair + half, 1), span]
                probs = jnp.where(real, jnp.exp(dot_nt(keys, left) - logs), 0.0)
                d_probs = dot_nt(values, grad)
                inner = jnp.sum(probs * d_probs, axis=0, keepdims=True)
                lefts.append(left)
                grads.append(grad)
                probs_low.append(probs.astype(BF))
                scores_low.append((probs * (d_probs - inner)).astype(BF))
            wide_scores = jnp.concatenate(scores_low, axis=1)
            grad_v = dot_nn(jnp.concatenate(probs_low, axis=1), jnp.concatenate(grads, axis=0))
            grad_k = dot_nn(wide_scores, jnp.concatenate(lefts, axis=0))
            grad_q = dot_nn(turned_halves(keys), jnp.concatenate(scores_low, axis=0))
            work.dq[span, lanes] = (grad_q.T * HEAD_WIDTH**-0.5).astype(BF)
            work.dkv_sum[0, own, lanes] += grad_k
            work.dkv_sum[1, own, lanes] += grad_v
        return carry

    lax.fori_loop(0, work.q.shape[1] // LANES, step, 0, unroll=2)
    work.dkv[...] = work.dkv_sum[...].astype(BF)
    work.need("entry", "text", "mixed")
    lanes = chip_lanes(info, work.dq.shape[1])
    text = work.text[...].T
    pair_grads(
        info,
        work,
        [
            (work.entry[...].T, work.dq[:, lanes]),
            (text, work.dkv[0, :, lanes]),
            (text, work.dkv[1, :, lanes]),
            (work.gb[...].T, work.mixed[:, lanes]),
        ],
    )
    stats[13:14, :] = total(fold(work.dq[...].astype(F32)))
    stats[14:15, :] = total(fold(work.dkv[1].astype(F32)))
    wait_rows(weights, plan, sems, range(4, 8))
    work.de[...] = dot_nn(work.dq[...], work.wq[...])
    work.need("x")
    norm_back_rows(work.x, g, work.de, work.mod, info, 3, work.out, stats)
    work.flush("out")


def self_back_kernel(info, work, weights):
    rows = weights[0].shape[0] // 4
    sems = work.sems
    plan = [(s, 3 * rows, rows, work.wo.at[pl.ds(s * rows, rows)]) for s in range(4)]
    start_rows(weights, info[0], plan, sems)
    work.stats[...] = work.early[...]
    stats = work.stats.at[pl.ds(0, 24)]
    work.need("g", "branch")
    gate_back(work.g, work.mod, info, 2, work.branch, work.gb, stats)
    work.flush("gb")
    share = work.g.shape[0]
    blocks = share // UNIT
    marks = key_marks([info[1 + b] for b in range(2 * blocks)])
    wait_rows(weights, plan, sems, range(4))
    work.d_mixed[...] = dot_nt(work.gb[...], work.wo[...]).astype(BF)
    work.need("mixed", "rest", "q", "kv_own", "kv_sib", "lse")
    width = work.q.shape[1]
    head = lax.broadcasted_iota(jnp.int32, (16, width), 0)
    lane = lax.broadcasted_iota(jnp.int32, (16, width), 1)
    first = head * HEAD_WIDTH
    pick = jnp.where((lane >= first) & (lane < first + HEAD_WIDTH), 1.0, 0.0)
    for block in range(blocks):
        span = pl.ds(block * UNIT, UNIT)
        whole = work.mixed[span, :].astype(F32) + work.rest[span, :].astype(F32)
        work.inner[:, span] = lax.dot_general(
            pick,
            whole * work.d_mixed[span, :].astype(F32),
            (((1,), (1,)), ((), ())),
            precision=lax.Precision.HIGHEST,
            preferred_element_type=F32,
        )

    def both(which, lanes):
        return jnp.concatenate([work.kv_own[which, :, lanes], work.kv_sib[which, :, lanes]], axis=0)

    def step(pair, carry):
        lanes = pair_lanes(pair)
        keys = both(0, lanes)
        values = both(1, lanes)
        marked = jnp.concatenate([keys, marks], axis=1)
        turned = turned_halves(keys)
        lefts, grads, probs_low, scores_low = [], [], [], []
        for block in range(blocks):
            span = pl.ds(block * UNIT, UNIT)
            q_pair = work.q[span, lanes]
            d_pair = work.d_mixed[span, lanes]
            ends = query_marks(info[1 + block])
            for half in range(2):
                left = (head_half(q_pair, half) * HEAD_WIDTH**-0.5).astype(BF)
                grad = head_half(d_pair, half).astype(BF)
                logs = work.lse[pl.ds(2 * pair + half, 1), span]
                probs = jnp.exp(dot_nt(marked, jnp.concatenate([left, ends], axis=1)) - logs)
                d_probs = dot_nt(values, grad)
                inner = work.inner[pl.ds(2 * pair + half, 1), span]
                lefts.append(left)
                grads.append(grad)
                probs_low.append(probs.astype(BF))
                scores_low.append((probs * (d_probs - inner)).astype(BF))
            grad_q = dot_nn(turned, jnp.concatenate(scores_low[-2:], axis=0))
            work.dq[span, lanes] = (grad_q.T * HEAD_WIDTH**-0.5).astype(BF)
        grad_v = dot_nn(jnp.concatenate(probs_low, axis=1), jnp.concatenate(grads, axis=0))
        grad_k = dot_nn(jnp.concatenate(scores_low, axis=1), jnp.concatenate(lefts, axis=0))
        for which, grad in ((0, grad_k.astype(BF)), (1, grad_v.astype(BF))):
            work.dkv_own[which, :, lanes] = grad[:share]
            work.dkv_give[which, :, lanes] = grad[share:]
        return carry

    lax.fori_loop(0, work.q.shape[1] // LANES, step, 0)
    work.flush("dkv_give")
    work.flush("dkv_own")
    work.flush("dq")


def sum_keys_values(info, work, dkv):
    work.need("dkv_own", "dkv_sib")
    for which in range(2):
        dkv[which] = (
            work.dkv_own[which].astype(F32) + work.dkv_sib[which].astype(F32)
        ).astype(BF)
    work.need("entry")
    lanes = chip_lanes(info, dkv.shape[2])
    entry = work.entry[...].T
    pair_grads(info, work, [(entry, dkv[0, :, lanes]), (entry, dkv[1, :, lanes])])


def kv_grads_kernel(info, work, weights):
    sum_keys_values(info, work, work.dkv)
    work.flush("dkv")


def qkv_back_kernel(info, work, weights):
    rows = weights[0].shape[0] // 4
    sems = work.sems
    plan = plan_of((work.wq, work.wk, work.wv), 0, rows)
    start_rows(weights, info[0], plan, sems)
    work.stats[...] = work.early[...]
    stats = work.stats.at[pl.ds(0, 24)]
    if work.has("send"):
        sum_keys_values(info, work, work.dkv)
    else:
        work.need("dkv")
    work.need("dq")
    stats[13:14, :] = total(fold(work.dq[...].astype(F32)))
    stats[14:15, :] = total(fold(work.dkv[1].astype(F32)))
    wait_rows(weights, plan, sems, range(0, 12))
    work.de[...] = (
        dot_nn(work.dq[...], work.wq[...])
        + dot_nn(work.dkv[0], work.wk[...])
        + dot_nn(work.dkv[1], work.wv[...])
    )
    work.need("x", "g")
    low = work.low if work.has("low") else None
    norm_back_rows(work.x, work.g, work.de, work.mod, info, 0, work.out, stats, low)
    work.flush("out")
    if low is not None:
        work.flush("low")


def merge_kernel(info, *refs, spots, after):
    chains = len(spots)
    ins, outs = refs[: 4 * chains], refs[4 * chains + after :]
    for chain, (result, column) in enumerate(spots):
        for side in range(2):
            received, kept = ins[4 * chain + 2 * side], ins[4 * chain + 2 * side + 1]
            out = outs[2 * result + side]
            lanes = pl.ds(column, received.shape[2])
            out[:, :, lanes] = (received[...].astype(F32) + kept[...].astype(F32)).astype(BF)


def gate(arrays, after):
    count = len(arrays)
    return pl.pallas_call(
        lambda *refs: None,
        out_shape=[shape(*a.shape, dtype=a.dtype) for a in arrays],
        in_specs=[ANY] * (count + len(after)),
        out_specs=[ANY] * count,
        input_output_aliases={i: i for i in range(count)},
        cost_estimate=lasting(0.5),
        name="gate",
    )(*arrays, *after)


def pack_kernel(info, *refs, groups, whole, after):
    count = sum(len(members) for _, members in groups)
    sources, rest = refs[:count], refs[count + after :]
    (in_sems, out_sems), rest = rest[-2:], rest[:-2]
    count = len(groups) + sum(whole)
    outs, held = list(rest[:count]), rest[count:]
    owns = [outs.pop(0) if one else None for one in whole]
    spots = []
    at = 0
    for index, (layer, members) in enumerate(groups):
        rows = held[index].shape[0]
        piece_rows = rows // 4
        for quarter in range(4):
            row = quarter * piece_rows
            source = sources[at + quarter * len(members) // 4]
            src = source.at[layer, pl.ds(row % source.shape[1], piece_rows)]
            spots.append((index, quarter, held[index].at[pl.ds(row, piece_rows)], src))
        at += len(members)

    def arriving(place):
        _, _, spot, src = spots[place]
        return pltpu.make_async_copy(src, spot, in_sems.at[place])

    def leaving(index, which):
        if which == 2:
            return pltpu.make_async_copy(held[index], owns[index], out_sems.at[2 * index])
        rows = outs[index].shape[0]
        src = held[index].at[pl.ds(which * rows, rows)]
        return pltpu.make_async_copy(src, outs[index], out_sems.at[2 * index + 1])

    def by_parity(act):
        for parity in range(2):

            @pl.when(info[0] % 2 == parity)
            def _(parity=parity):
                act(parity)

    for place in range(len(spots)):
        arriving(place).start()
    for index in range(len(groups)):
        for quarter in range(4):
            arriving(4 * index + quarter).wait()
        by_parity(lambda parity: leaving(index, parity).start())
        if whole[index]:
            leaving(index, 2).start()
    for index in range(len(groups)):
        by_parity(lambda parity: leaving(index, parity).wait())
        if whole[index]:
            leaving(index, 2).wait()


def mod_kernel(condition, mod, mod_bias, q, v, cq, cv, up, out):
    narrow, units, columns = q.shape[1], up.shape[1], mod.shape[1]
    out[...] = jnp.zeros(out.shape, F32)
    for layer in range(LAYERS):
        row = pl.ds(layer, 1)
        out[layer, 0:SLOTS, 0:columns] = dot_nt(condition[...], mod[layer]) + mod_bias[
            row, :
        ].astype(F32)
        out[layer, 4:5, 0:units] = up[row, :].astype(F32)
        out[layer, 5:6, 0:narrow] = q[row, :].astype(F32)
        out[layer, 6:7, 0:narrow] = v[row, :].astype(F32)
        out[layer, 7:8, 0:narrow] = cq[row, :].astype(F32)
        out[layer, 4:5, 1024 : 1024 + narrow] = cv[row, :].astype(F32)


def assemble_kernel(info, *refs, narrow, units, columns):
    parts, (mods, narrows, ups) = refs[:4], refs[4:]
    narrows[...] = jnp.zeros(narrows.shape, F32)
    for rank in range(4):

        @pl.when(info[5] == rank)
        def _(rank=rank):
            for shard in range(4):
                part = parts[shard ^ rank]
                for layer in range(LAYERS):
                    mods[layer, :, shard * columns : (shard + 1) * columns] = part[
                        layer, 0:SLOTS, 0:columns
                    ]
                    ups[layer, :, shard * units : (shard + 1) * units] = part[layer, 4:5, 0:units]
                    at = slice(shard * narrow, (shard + 1) * narrow)
                    for row, source in ((0, 5), (2, 6), (3, 7)):
                        narrows[layer, row : row + 1, at] = part[
                            layer, source : source + 1, 0:narrow
                        ]
                    narrows[layer, 5:6, at] = part[layer, 4:5, 1024 : 1024 + narrow]


def collect_kernel(info, *refs, narrow, units, columns):
    stats, condition, out = refs[: 2 * LAYERS], refs[2 * LAYERS], refs[2 * LAYERS + 1]
    sums = refs[2 * LAYERS + 2]
    width = stats[0].shape[1]
    work = out
    out = refs[2 * LAYERS + 3]
    out[...] = jnp.zeros(out.shape, F32)
    for layer in range(LAYERS):
        sums[...] = stats[2 * layer][...] + stats[2 * layer + 1][...]
        base = 8 * layer
        out[base + 4 : base + 5, width : 2 * width] = sums[60:61, :]
        out[base + 5 : base + 6, 0:width] = sums[12:13, :]
        out[base + 5 : base + 6, width : 2 * width] = sums[36:37, :]
        for index in range(2):
            out[base + 6 + index : base + 7 + index, 512 : 512 + width] = condition[
                2 * layer + index : 2 * layer + index + 1, :
            ].astype(F32)
        for rank in range(4):

            @pl.when(info[5] == rank)
            def _(rank=rank, base=base):
                first = rank * columns
                for index in range(9):
                    low = max(first, index * width)
                    high = min(first + columns, (index + 1) * width)
                    if low < high:
                        row = (index // 3) * 24 + (index % 3) * 4
                        out[base : base + 4, low - first : high - first] = sums[
                            row : row + 4, low - index * width : high - index * width
                        ]
                out[base + 4 : base + 5, 0:units] = sums[61 + rank : 62 + rank, :]
                own = slice(rank * narrow, (rank + 1) * narrow)
                out[base + 6 : base + 7, 0:narrow] = sums[13:14, own]
                out[base + 6 : base + 7, 256 : 256 + narrow] = sums[14:15, own]
                out[base + 7 : base + 8, 0:narrow] = sums[37:38, own]
                out[base + 7 : base + 8, 256 : 256 + narrow] = sums[38:39, own]
    work[...] = out[...].astype(BF)


def spread_kernel(info, gathered, grad, bias_grad, q, v, cq, cv, up, o1, o2, o3, rows, conditions):
    count = gathered.shape[0]
    columns, part = grad.shape[2], grad.shape[1]
    width, narrow, units = conditions.shape[1], q.shape[1], up.shape[1]
    shift = lax.rem(width - info[8] * part, width)
    for index in range(count):
        for slot in range(SLOTS):
            row = 8 * (slot // 2) + 6 + slot % 2
            conditions[SLOTS * index + slot : SLOTS * index + slot + 1, :] = gathered[
                index ^ info[8], row : row + 1, 512 : 512 + width
            ].astype(F32)
    turned = pltpu.roll(conditions[...], shift, 1)[:, :part].T
    for layer in range(LAYERS):
        base = 8 * layer
        sums = jnp.zeros((8, gathered.shape[2]), F32)
        for index in range(count):
            values = gathered[index ^ info[8]].astype(F32)[base : base + 8]
            sums += values
            rows[SLOTS * index : SLOTS * (index + 1), :] = values[0:SLOTS, 0:columns]
        grad[layer] = jnp.dot(
            turned, rows[...], precision=lax.Precision.HIGHEST, preferred_element_type=F32
        )
        at = slice(layer, layer + 1)
        bias_grad[at, :] = jnp.sum(sums[0:SLOTS, 0:columns], axis=0, keepdims=True)
        up[at, :] = sums[4:5, 0:units]
        q[at, :] = sums[6:7, 0:narrow]
        v[at, :] = sums[6:7, 256 : 256 + narrow]
        cq[at, :] = sums[7:8, 0:narrow]
        cv[at, :] = sums[7:8, 256 : 256 + narrow]
        for out, row, lane in ((o1, 5, 0), (o2, 5, width), (o3, 4, width)):
            own = jnp.broadcast_to(sums[row : row + 1, lane : lane + width], (8, width))
            out[at, :] = pltpu.roll(own, shift, 1)[0:1, :part]


def finish_kernel(*refs, wide, spots):
    parts, outs = refs[: 2 * len(spots)], refs[2 * len(spots) :]
    step = 3 * LANES
    for chain, (at, places) in enumerate(spots):
        values = parts[2 * chain][0].astype(F32) + parts[2 * chain + 1][0].astype(F32)
        for layer, pair in places:
            if wide:
                width = outs[0].shape[2]
                for out in outs:
                    out[layer] = values[:, at : at + width]
                    at += width
                continue
            both = values[:, at : at + step]
            at += step
            first = jnp.concatenate(
                [both[:, :LANES], both[:, 2 * LANES : 2 * LANES + HEAD_WIDTH]], axis=1
            )
            second = jnp.concatenate(
                [both[:, LANES : 2 * LANES], both[:, 2 * LANES + HEAD_WIDTH :]], axis=1
            )
            for out, matrix in zip(outs[2 * pair : 2 * pair + 2], (first, second)):
                out[layer] = matrix if out.shape[1:] == matrix.shape else matrix.T


def join_kernel(info, rows, other, out):
    share = rows.shape[0]
    for core in range(2):

        @pl.when(info[5] % 2 == core)
        def _(core=core):
            out[pl.ds(core * share, share), :] = rows[...]
            out[pl.ds((1 - core) * share, share), :] = other[...]


def tensor_hop(values, step):
    return lax.ppermute(values, "tensor", [(i, i ^ step) for i in range(4)])


def dp_hop(values, step):
    size = lax.axis_size("dp")
    return lax.ppermute(values, "dp", [(i, i ^ step) for i in range(size)])


def time_features(moments, width):
    half = width // 2
    rates = jnp.exp(-math.log(10000.0) * jnp.arange(half, dtype=F32) / half)
    angles = moments.astype(F32)[:, None] * rates[None, :]
    return jnp.concatenate([jnp.cos(angles), jnp.sin(angles)], axis=1)


def shards(
    tokens,
    text,
    timesteps,
    item_frames,
    cotangent,
    self_query,
    self_query_bias,
    self_key,
    self_value,
    self_value_bias,
    self_output,
    self_output_bias,
    cross_query,
    cross_query_bias,
    cross_key,
    cross_value,
    cross_value_bias,
    cross_output,
    cross_output_bias,
    hidden_up,
    hidden_up_bias,
    hidden_down,
    hidden_down_bias,
    modulation,
    modulation_bias,
):
    frames, width = tokens.shape
    words = text.shape[1]
    columns = modulation.shape[2]
    narrow = self_query.shape[2]
    units = hidden_up.shape[2]
    rank = lax.axis_index("tensor")
    me = lax.axis_index("dp")
    size = lax.axis_size("dp")
    core = rank % 2
    share = frames // 2
    blocks = share // UNIT
    unit = width // size
    turn = lambda values: jnp.swapaxes(values, 1, 2)

    order = jnp.arange(SLOTS, dtype=jnp.int32)
    ends = jnp.sum(jnp.where(order[:, None] <= order[None, :], item_frames[:, None], 0), axis=0)
    turned = (jnp.arange(frames // UNIT, dtype=jnp.int32) + core * blocks) % (2 * blocks)
    slots = jnp.sum((turned[:, None] * UNIT >= ends[None, :]).astype(jnp.int32), axis=1)
    places = jnp.stack([rank, rank // 2, rank ^ 1, me]).astype(jnp.int32)
    info = jnp.concatenate([(rank * 2 + me % 2)[None].astype(jnp.int32), slots, places])

    def pack(members, whole, after=()):
        rows = [sum(a.shape[1] for a in some) for _, some in members]
        outs = [shape(r, width, dtype=BF) for r, one in zip(rows, whole) if one]
        outs += [shape(r // 2, width, dtype=BF) for r in rows]
        arrays = [a for _, some in members for a in some]
        results = pl.pallas_call(
            partial(
                pack_kernel,
                groups=[(layer, [None] * len(some)) for layer, some in members],
                whole=whole,
                after=len(after),
            ),
            out_shape=outs,
            in_specs=[SMALL] + [ANY] * (len(arrays) + len(after)),
            out_specs=[ANY] * len(outs),
            scratch_shapes=[
                *[pltpu.VMEM((r, width), BF) for r in rows],
                pltpu.SemaphoreType.DMA((4 * len(members),)),
                pltpu.SemaphoreType.DMA((2 * len(members),)),
            ],
            compiler_params=pltpu.CompilerParams(vmem_limit_bytes=VMEM_BYTES),
            cost_estimate=lasting(1.0),
            name="pack_weights",
        )(info, *arrays, *after)
        return list(results[: sum(whole)]), list(results[sum(whole) :])

    selfs = [turn(self_query), turn(self_key), turn(self_value), self_output]
    crosses = [turn(cross_query), turn(cross_key), turn(cross_value), cross_output]
    own0, first0 = pack([(0, selfs)], [True])


    condition = jax.nn.silu(time_features(timesteps, width)).astype(BF)
    mine = plain(
        mod_kernel,
        "mod_rows",
        None,
        [
            condition,
            turn(modulation),
            modulation_bias,
            self_query_bias,
            self_value_bias,
            cross_query_bias,
            cross_value_bias,
            hidden_up_bias,
        ],
        [shape(LAYERS, 8, -(-columns // LANES) * LANES)],
    )
    own1, first1 = pack(
        [(0, crosses), (1, selfs), (1, crosses), (1, [hidden_up]), (1, [hidden_down])],
        [True, True, True, False, False],
        [mine],
    )
    firsts, owns = first0 + first1, own0 + own1
    others = [tensor_hop(mine, 1), tensor_hop(mine, 2)]
    others.append(tensor_hop(others[0], 2))
    out_biases = [
        b.reshape(LAYERS, 1, width) for b in (self_output_bias, cross_output_bias, hidden_down_bias)
    ]

    count = len(firsts)
    along_x, along_y, over_x, over_y, sibs = [[None] * count for _ in range(5)]

    def leave(index):
        along_x[index] = tensor_hop(firsts[index], 2)

    def swap(index):
        sibs[index] = tensor_hop(owns[index], 1)

    def go_on(index):
        along_y[index] = dp_hop(along_x[index], 1)
        over_x[index] = tensor_hop(along_x[index], 1)

    def end(index):
        over_y[index] = tensor_hop(along_y[index], 1)

    def weights_of(index):
        return [
            owns[index],
            sibs[index],
            along_x[index],
            along_y[index],
            over_x[index],
            over_y[index],
        ]

    def open_gate(after, leaving=(), at_x=(), at_y=(), settled=()):
        places = [(firsts, i) for i in leaving]
        places += [(along_x, i) for i in at_x] + [(along_y, i) for i in at_y] + list(settled)
        opened = gate([values[i] for values, i in places], after)
        for (values, i), array in zip(places, opened):
            values[i] = array
        for i in leaving:
            leave(i)
        for i in at_x:
            go_on(i)
        for i in at_y:
            end(i)
        return list(opened)

    leave(0)
    swap(0)
    open_gate([mine], [], [0])
    open_gate([*others, along_x[0]], [1])
    swap(1)
    go_on(1)
    owns += [hidden_up, hidden_down]
    sibs[4:6] = tensor_hop(hidden_up, 1), tensor_hop(hidden_down, 1)
    mods, narrow_biases, up_biases = plain(
        partial(assemble_kernel, narrow=narrow, units=units, columns=columns),
        "mod_all",
        info,
        [mine, *others],
        [
            shape(LAYERS, SLOTS, 4 * columns),
            shape(LAYERS, 8, 4 * narrow),
            shape(LAYERS, 1, 4 * units),
        ],
        after=[along_x[1]],
    )
    open_gate([mods], [], [], [0])

    text_rows = jnp.pad(text, ((0, 0), (0, LANES - words), (0, 0))).reshape(-1, width)
    whole = pltpu.VMEM((width, width), BF)
    four = pltpu.VMEM((4, width, units), BF)
    two = pltpu.VMEM((2, width, units), BF)
    floats = pltpu.VMEM((share, width), F32)
    lows = pltpu.VMEM((share, width), BF)
    sems = lambda n: pltpu.SemaphoreType.DMA((n,))
    frame_low = shape(share, width, dtype=BF)
    frame_high = shape(share, width)
    frame_wide = shape(share, 4 * units, dtype=BF)
    frame_chip = shape(share, 2 * units, dtype=BF)
    two_low = shape(2, share, width, dtype=BF)
    two_text = shape(2, SLOTS * LANES, width, dtype=BF)
    logs = shape(16, share)
    log_work = pltpu.VMEM((share, LANES), F32)
    stat_shape = shape(72, width)

    kept = []
    for layer in range(LAYERS):
        first = 2 * layer
        mod = (mods, (layer,))
        biases = (narrow_biases, (layer,))
        common = dict(w=pltpu.VMEM((2, width, width), BF), sems=sems(8))
        if layer == 0:
            entry1, kv, x = run(
                kv_kernel,
                "self_kv",
                info,
                {},
                dict(mod=mod, biases=biases),
                weights_of(first) + [tokens],
                dict(entry=frame_low, kv=two_low, x=frame_high),
                {},
                common | dict(rows=lows, row_sems=sems(1)),
                [along_x[1], sibs[1], sibs[4], sibs[5]],
                3.0,
            )
        else:
            entry1, kv, x, branch3 = run(
                kv_kernel,
                "residual_kv",
                info,
                dict(part=part, other=tensor_hop(part, 2), below=kept[-1]["x2"]),
                dict(
                    mod=mod,
                    mod_below=(mods, (layer - 1,)),
                    bias=(out_biases[2], (layer - 1,)),
                    biases=biases,
                ),
                weights_of(first),
                dict(entry=frame_low, kv=two_low, x=frame_high, branch=frame_low),
                {},
                common | dict(sum=floats),
                opened,
                3.0,
            )
            kept[-1]["branch3"] = branch3
        kv_sib = tensor_hop(kv, 1)
        opened = (
            open_gate([entry1], [2, 3], [], [], [(over_x, 1)])
            if layer == 0
            else open_gate([entry1], [5], [], [], [(over_x, 4), (over_y, 3)])
        )
        (q,) = run(
            q_kernel,
            "query",
            info,
            dict(entry=entry1),
            dict(biases=biases),
            weights_of(first),
            dict(q=frame_low),
            {},
            dict(w=whole, sems=sems(4)),
            [],
            15.0,
        )
        x1, mixed1, rest1, lse1, branch1 = run(
            self_kernel,
            "self",
            info,
            dict(q=q, kv_own=kv, kv_sib=kv_sib, x=x),
            dict(mod=mod, bias=(out_biases[0], (layer,))),
            weights_of(first),
            dict(out=frame_high, mixed=frame_low, rest=frame_low, lse=logs, branch=frame_low),
            {},
            dict(wo=whole, logs=log_work, sum=floats, sems=sems(4)),
            opened,
            8.0,
        )
        if layer == 0:
            opened = open_gate([x1], [4], [2], [1], [(along_x, 3)])
            swap(2)
        else:
            opened = open_gate([x1], [], [5], [4])
        x2, entry2, cq, ckv, mixed2, lse2, branch2 = run(
            partial(cross_kernel, words=words),
            "cross",
            info,
            dict(x=x1, text=text_rows),
            dict(mod=mod, biases=biases, bias=(out_biases[1], (layer,))),
            weights_of(first + 1),
            dict(
                out=frame_high,
                entry=frame_low,
                q=frame_low,
                kv=two_text,
                mixed=frame_low,
                lse=logs,
                branch=frame_low,
            ),
            {},
            dict(
                wq=whole, wk=whole, wv=whole, wo=whole, logs=log_work, sum=floats, sems=sems(16)
            ),
            opened,
            6.0,
        )
        if layer == 0:
            opened = open_gate([x2], [], [3], [2], [(over_x, 2), (sibs, 2), (along_x, 4)])
            swap(3)
        else:
            opened = open_gate([x2], [], [], [5], [(over_x, 5), (over_y, 4)])
        if layer == 0:
            part, entry3, active, slope = run(
                lambda info, work, w: hidden_kernel(info, work, w, 0),
                "ff_part",
                info,
                dict(x=x2),
                dict(mod=mod, up_bias=(up_biases, (layer,))),
                [hidden_up, sibs[4], hidden_down, sibs[5]],
                dict(part=frame_low, entry=frame_low, active=frame_chip, slope=frame_chip),
                {},
                dict(
                    up=two, down=two, before=floats, sum=floats, sems=sems(2), down_sems=sems(2)
                ),
                opened,
                5.0,
            )
            opened = open_gate([part], [], [4], [3], [(over_x, 3), (over_y, 2), (sibs, 3)])
            x3 = branch3 = None
        else:
            x3 = branch3 = active = slope = entry3 = None
        kept.append(
            dict(
                x=x,
                entry1=entry1,
                q=q,
                kv=kv,
                kv_sib=kv_sib,
                mixed1=mixed1,
                rest1=rest1,
                lse1=lse1,
                branch1=branch1,
                x1=x1,
                entry2=entry2,
                cq=cq,
                ckv=ckv,
                mixed2=mixed2,
                lse2=lse2,
                branch2=branch2,
                x2=x2,
                entry3=entry3,
                active=active,
                slope=slope,
                branch3=branch3,
            )
        )
        x = x3
    last_gate = opened

    def join(rows, *after):
        return plain(
            join_kernel,
            "join_rows",
            info,
            [rows, tensor_hop(rows, 1)],
            [shape(2 * share, width, dtype=BF)],
            after=after,
        )


    chains = {}

    def start(name, send, keep):
        view = (size, unit, send.shape[1])
        chains[name] = (tensor_hop(send, 1).reshape(view), keep.reshape(view), 0)

    def held(*names):
        return [chains[name][1] for name in names]

    def advance(names, after=(), cost=1.5):
        targets = [(n, [n]) if isinstance(n, str) else n for n in names]
        targets = [t for t in targets if 2 ** chains[t[1][0]][2] < size]
        if not targets:
            return
        ins, in_specs, outs, out_specs, spots = [], [], [], [], []
        for result, (_, parts) in enumerate(targets):
            column = 0
            for name in parts:
                received, kept_part, bit = chains[name]
                blocks_left, rows, wide = received.shape
                spots.append((result, column))
                column += wide
                for side in range(2):

                    def at(i, info, bit=bit, side=side):
                        return (0, ((info[8] >> bit) & 1) ^ side, 0, 0)

                    for part in (received, kept_part):
                        ins.append(part.reshape(blocks_left // 2, 2, rows, wide))
                        in_specs.append(pl.BlockSpec((blocks_left // 2, None, rows, wide), at))
            for side in range(2):
                outs.append(shape(blocks_left // 2, rows, column, dtype=BF))
                out_specs.append(
                    pl.BlockSpec((blocks_left // 2, rows, column), lambda i, info: (0, 0, 0))
                )
        results = pl.pallas_call(
            partial(merge_kernel, spots=spots, after=len(after)),
            grid_spec=pltpu.PrefetchScalarGridSpec(
                num_scalar_prefetch=1,
                grid=(1,),
                in_specs=in_specs + [ANY] * len(after),
                out_specs=out_specs,
            ),
            out_shape=outs,
            compiler_params=pltpu.CompilerParams(vmem_limit_bytes=VMEM_BYTES),
            cost_estimate=lasting(cost),
            name="merge_grads",
        )(info, *ins, *after)
        for index, (name, parts) in enumerate(targets):
            bit = chains[parts[0]][2]
            hold, give = results[2 * index : 2 * index + 2]
            for part in parts:
                del chains[part]
            chains[name] = (dp_hop(give, 2**bit), hold, bit + 1)

    sums = []
    last = LAYERS - 1
    for layer in reversed(range(LAYERS)):
        first = 2 * layer
        k = kept[layer]
        mod = (mods, (layer,))
        above = layer + 1
        f_name, c_name, a_name, s_name = [f"{kind}{layer}" for kind in "fcas"]
        n_name = f"n{above}"

        def grads_out(members):
            return dict.fromkeys(SIDES, shape(width, members * narrow, dtype=BF))

        older = []
        if layer < last:
            older = [f"f{above}", n_name]
            more = held(*older)
        if layer == last:
            f_send, f_keep, low, c_send, c_keep, g, stats = run(
                lambda info, work, w: hidden_cross_kernel(info, work, w, words),
                "ff_cross_back",
                info,
                dict(
                    x2=k["x2"],
                    branch2=k["branch2"],
                    q=k["cq"],
                    kv=k["ckv"],
                    lse=k["lse2"],
                    entry2=k["entry2"],
                    text=text_rows,
                    mixed=k["mixed2"],
                    x1=k["x1"],
                ),
                dict(mod=mod, up_bias=(up_biases, (layer,)), bias=(out_biases[2], (layer,))),
                weights_of(4) + weights_of(5) + [cotangent] + weights_of(first + 1),
                {f"f_{name}": shape(width, 2 * units, dtype=BF) for name in SIDES}
                | dict(low=frame_low)
                | {f"c_{name}": shape(width, 4 * narrow, dtype=BF) for name in SIDES}
                | dict(out=frame_high),
                dict(stats=stat_shape),
                dict(
                    up=four,
                    down=four,
                    g=floats,
                    g_mid=floats,
                    rows=lows,
                    row_sems=sems(1),
                    gb=lows,
                    entry3=lows,
                    branch3=lows,
                    active=pltpu.VMEM((share, 4 * units), BF),
                    slope=pltpu.VMEM((share, 4 * units), BF),
                    d_before=pltpu.VMEM((share, 4 * units), BF),
                    before=floats,
                    sum=floats,
                    sems=sems(8),
                    down_sems=sems(8),
                    wq=whole,
                    wo=whole,
                    dkv=pltpu.VMEM(two_text.shape, BF),
                    dkv_sum=pltpu.VMEM(two_text.shape, F32),
                    csems=sems(8),
                ),
                last_gate,
                10.0,
            )
            start(f_name, f_send, f_keep)
            start(c_name, c_send, c_keep)
        else:
            part, gb, d_before, stats = run(
                lambda info, work, w: hidden_back_kernel(info, work, w, 0),
                "ff_back",
                info,
                dict(g=g, branch=k["branch3"], slope=k["slope"]),
                dict(mod=mod),
                [hidden_up, sibs[4], hidden_down, sibs[5]],
                dict(part=frame_low, gb=frame_low, d_before=frame_chip),
                dict(stats=stat_shape),
                dict(
                    up=two, down=two, before=floats, de=floats, sems=sems(2), down_sems=sems(2)
                ),
                more,
                5.0,
            )
            other = tensor_hop(part, 2)
            send, keep = run(
                hidden_grads_kernel,
                "ff_grads",
                info,
                dict(entry=k["entry3"], d_before=d_before, gb=gb, active=k["active"]),
                {},
                [],
                dict.fromkeys(SIDES, shape(width, 2 * units, dtype=BF)),
                {},
                {},
                [gb],
                1.0,
            )
            start(f_name, send, keep)
            output = join(low, gb)
            advance(older, held(f_name), 0.5)
            extra = dict(part=part, other=other, above=k["x2"])
            scratch = dict(g_mid=floats)
        if layer < last:
            send, keep, g, stats = run(
                partial(cross_back_kernel, words=words),
                "cross_back",
                info,
                dict(
                    g=g,
                    branch=k["branch2"],
                    q=k["cq"],
                    kv=k["ckv"],
                    lse=k["lse2"],
                    entry=k["entry2"],
                    text=text_rows,
                    mixed=k["mixed2"],
                    x=k["x1"],
                    **extra,
                ),
                dict(mod=mod, early=(stats, ())),
                weights_of(first + 1),
                grads_out(4) | dict(out=frame_high),
                dict(stats=stat_shape),
                dict(
                    wq=whole,
                    wo=whole,
                    gb=lows,
                    dq=lows,
                    dkv=pltpu.VMEM(two_text.shape, BF),
                    d_mixed=lows,
                    de=floats,
                    dkv_sum=pltpu.VMEM(two_text.shape, F32),
                    sems=sems(8),
                    **scratch,
                ),
                held(f_name, *older) + [output],
                60.0,
            )
            start(c_name, send, keep)
            advance([f_name, n_name], [g, chains[f"f{above}"][0]])
        gb1, dq, dkv_own, dkv_give, stats = run(
            self_back_kernel,
            "self_back",
            info,
            dict(
                g=g,
                branch=k["branch1"],
                mixed=k["mixed1"],
                rest=k["rest1"],
                q=k["q"],
                kv_own=k["kv"],
                kv_sib=k["kv_sib"],
                lse=k["lse1"],
            ),
            dict(mod=mod, early=(stats, ())),
            weights_of(first),
            dict(gb=frame_low, dq=frame_low, dkv_own=two_low, dkv_give=two_low),
            dict(stats=stat_shape),
            dict(wo=whole, d_mixed=lows, inner=pltpu.VMEM((16, share), F32), sems=sems(4)),
            held(f_name, c_name, *([n_name] if layer < last else [])),
            13.0,
        )
        dkv_sib = tensor_hop(dkv_give, 1)
        if layer == last:
            advance([f_name], [dq])
        else:
            advance([f_name, c_name], [dq, chains[n_name][0]])
        send, keep = run(
            query_output_kernel,
            "qo_grads",
            info,
            dict(entry=k["entry1"], gb=gb1, dq=dq, mixed=k["mixed1"]),
            {},
            [],
            grads_out(2),
            {},
            {},
            held(f_name, c_name),
            60.0,
        )
        start(a_name, send, keep)
        arriving = dict(dkv_own=dkv_own, dkv_sib=dkv_sib, entry=k["entry1"])
        if layer == 0:
            send, keep, dkv = run(
                kv_grads_kernel,
                "kv_grads",
                info,
                arriving,
                {},
                [],
                grads_out(2) | dict(dkv=two_low),
                {},
                {},
                held(a_name),
                4.0,
            )
            start(s_name, send, keep)
            rest = f"t{layer}"
            advance([f_name, c_name, (rest, [a_name, s_name])], held(s_name))
            arriving = dict(dkv=dkv)
        results = run(
            qkv_back_kernel,
            "qkv_back",
            info,
            arriving | dict(dq=dq, x=k["x"], g=g),
            dict(mod=mod, early=(stats, ())),
            weights_of(first),
            (dict(low=frame_low) if layer == 0 else grads_out(2)) | dict(out=frame_high),
            dict(stats=stat_shape),
            dict(wq=whole, wk=whole, wv=whole, de=floats, sems=sems(12))
            | (dict(dkv=pltpu.VMEM(two_low.shape, BF)) if layer else {}),
            held(f_name, c_name, rest if layer == 0 else a_name),
            6.0,
        )
        g, stats = results[-2:]
        if layer:
            start(s_name, *results[:2])
        if layer:
            advance([f_name, (f"n{layer}", [c_name, a_name, s_name])], [g])
        else:
            to_rest = [g, chains[f_name][0]]
        sums = [stats, tensor_hop(stats, 1)] + sums
    vectors = plain(
        partial(collect_kernel, narrow=narrow, units=units, columns=columns),
        "collect",
        info,
        [*sums, condition],
        [shape(16, mine.shape[2], dtype=BF)],
        [pltpu.VMEM(stat_shape.shape, F32), pltpu.VMEM((16, mine.shape[2]), F32)],
    )
    advance(["c0", "t0"], to_rest + [vectors])
    gathered, hop = vectors[None], size // 2

    def gather_sums():
        nonlocal gathered, hop
        if hop:
            both = jnp.stack([gathered, dp_hop(gathered, hop)], axis=1)
            gathered = both.reshape(-1, *vectors.shape)
            hop //= 2

    low = results[0]
    (low,) = gate([low], held("t0"))
    input_grad = join(low)

    def parts_of(*names):
        return [part.reshape(1, unit, -1) for name in names for part in chains[name][:2]]

    up_grad, down_grad = plain(
        partial(finish_kernel, wide=True, spots=[(0, [(0, 0)]), (0, [(1, 0)])]),
        "wide",
        None,
        parts_of("f0", "f1"),
        [shape(LAYERS, unit, units)] * 2,
    )
    ready = [input_grad, up_grad, chains["c0"][0]]
    while any(2 ** chain[2] < size for chain in chains.values()):
        gather_sums()
        advance(list(chains), held("t0") + [gathered] + ready)
    while hop:
        gather_sums()
    straight, across = shape(LAYERS, unit, narrow), shape(LAYERS, narrow, unit)
    spots = [(0, [(1, 0), (1, 1), (1, 2), (1, 3)])]
    spots += [(0, [(0, 0), (0, 1)]), (0, [(0, 2), (0, 3)])]
    cq_grad, ck_grad, cv_grad, co_grad, q_grad, o_grad, k_grad, v_grad = plain(
        partial(finish_kernel, wide=False, spots=spots),
        "narrow",
        None,
        parts_of("n1", "c0", "t0"),
        [straight, straight, straight, across, straight, across, straight, straight],
    )
    small = plain(
        spread_kernel,
        "spread",
        info,
        [gathered],
        [shape(LAYERS, unit, columns), shape(LAYERS, columns)]
        + [shape(LAYERS, narrow)] * 4
        + [shape(LAYERS, units)]
        + [shape(LAYERS, unit)] * 3,
        [pltpu.VMEM((SLOTS * size, columns), F32), pltpu.VMEM((SLOTS * size, width), F32)],
    )
    mod_grad, mod_bias_grad, q_sum, v_sum, cq_sum, cv_sum, up_sum, o1, o2, o3 = small
    return (
        output,
        input_grad,
        q_grad,
        q_sum,
        k_grad,
        v_grad,
        v_sum,
        o_grad,
        o1,
        cq_grad,
        cq_sum,
        ck_grad,
        cv_grad,
        cv_sum,
        co_grad,
        o2,
        up_grad,
        up_sum,
        turn(down_grad),
        o3,
        mod_grad,
        mod_bias_grad,
    )


def solution(mesh):
    dp, tensor = "dp", "tensor"
    columns, vector = P(None, None, tensor), P(None, tensor)
    matrix, turned, spread = P(None, dp, tensor), P(None, tensor, dp), P(None, dp)
    placed = (
        P(dp, None),
        P(dp, None, None),
        P(dp),
        P(dp),
        P(dp, None),
        columns,
        vector,
        columns,
        columns,
        vector,
        P(None, tensor, None),
        P(),
        columns,
        vector,
        columns,
        columns,
        vector,
        P(None, tensor, None),
        P(),
        columns,
        vector,
        P(None, tensor, None),
        P(),
        columns,
        vector,
    )
    results = (
        P(dp, None),
        P(dp, None),
        matrix,
        vector,
        matrix,
        matrix,
        vector,
        turned,
        spread,
        matrix,
        vector,
        matrix,
        matrix,
        vector,
        turned,
        spread,
        matrix,
        vector,
        turned,
        spread,
        matrix,
        vector,
    )
    return jax.shard_map(
        shards, mesh=mesh, in_specs=placed, out_specs=results, check_vma=False
    )
```

```python
from functools import partial
import math

import jax
import jax.numpy as jnp
from jax import lax
from jax.experimental import pallas as pl
from jax.experimental.pallas import tpu as pltpu
from jax.sharding import PartitionSpec as P

HEAD_WIDTH = 64
UNIT = 256
LAYERS = 2
WINDOW = 1024
EPSILON = 1e-06
LANES = 128
CHUNK = 64
SLOTS = WINDOW // UNIT
FAR = -1e30
SIDES = ("send", "keep")
VMEM_BYTES = 66_600_000
BF = jnp.bfloat16
F32 = jnp.float32
ROOT = math.sqrt(2.0 / math.pi)
CUBIC = 0.044715


def dot_nn(left, right):
    return jnp.dot(left, right, preferred_element_type=F32)


def dot_nt(left, right):
    return lax.dot_general(left, right, (((1,), (1,)), ((), ())), preferred_element_type=F32)


def dot_tn(left, right):
    return lax.dot_general(left, right, (((0,), (0,)), ((), ())), preferred_element_type=F32)


SMALL = pl.BlockSpec(memory_space=pltpu.SMEM)
NEAR = pl.BlockSpec(memory_space=pltpu.VMEM)
ANY = pl.BlockSpec(memory_space=pl.ANY)


class Work:
    def __init__(self, ins, outs, scratch, in_sems, out_sems):
        self.ins, self.outs, self.scratch, self.out_sems = ins, outs, scratch, out_sems
        self.copies, self.waited, self.flushed = {}, set(), []
        for index, (name, (ref, buffer)) in enumerate(ins.items()):
            self.copies[name] = pltpu.make_async_copy(ref, buffer, in_sems.at[index])
            self.copies[name].start()

    def __getattr__(self, name):
        if name in self.__dict__["ins"]:
            return self.ins[name][1]
        if name in self.__dict__["outs"]:
            return self.outs[name][1]
        return self.__dict__["scratch"][name]

    def has(self, name):
        return name in self.outs

    def takes(self, name):
        return name in self.ins

    def send(self, name, source, *at):
        ref = self.outs[name][0]
        copy = pltpu.make_async_copy(
            source, ref.at[at] if at else ref, self.out_sems.at[len(self.flushed)]
        )
        copy.start()
        self.flushed.append(copy)

    def need(self, *names):
        for name in names:
            if name not in self.waited:
                self.waited.add(name)
                self.copies[name].wait()

    def flush(self, name, *at):
        ref, buffer = self.outs[name]
        if at:
            ref, buffer = ref.at[at], buffer.at[at]
        copy = pltpu.make_async_copy(buffer, ref, self.out_sems.at[len(self.flushed)])
        copy.start()
        self.flushed.append(copy)

    def finish(self):
        self.need(*self.ins)
        for copy in self.flushed:
            copy.wait()


class Names:
    def __init__(self, work, **names):
        self.work, self.names = work, names

    def to(self, name):
        return self.__dict__["names"].get(name, name)

    def __getattr__(self, name):
        return getattr(self.__dict__["work"], self.to(name))

    @property
    def outs(self):
        return {name: self.work.outs[self.to(name)] for name in SIDES}

    def has(self, name):
        return self.work.has(self.to(name))

    def takes(self, name):
        return self.work.takes(self.to(name))

    def need(self, *names):
        self.work.need(*[name for name in map(self.to, names) if self.work.takes(name)])

    def flush(self, name, *at):
        if self.has(name):
            self.work.flush(self.to(name), *at)


def run(body, name, info, ins, small, weights, outs, small_outs, scratch, after=(), cost=1.0):
    in_names, out_names, names = list(ins), list(outs), list(scratch)
    small_names, small_out_names = list(small), list(small_outs)
    counts = [1, len(in_names), len(small), len(weights), len(after), len(outs), len(small_outs)]

    def kernel(*refs):
        refs = list(refs)
        parts = []
        for count in counts:
            parts.append(refs[:count])
            refs = refs[count:]
        (info_ref,), in_refs, small_refs, weight_refs, _, out_refs, small_out_refs = parts
        in_bufs, refs = refs[: len(in_names)], refs[len(in_names) :]
        out_bufs, refs = refs[: len(out_names)], refs[len(out_names) :]
        rest, (in_sems, out_sems) = refs[:-2], refs[-2:]
        extra = {}
        rest = list(rest)
        for key in names:
            many = isinstance(scratch[key], list)
            size = len(scratch[key]) if many else 1
            extra[key] = rest[:size] if many else rest[0]
            rest = rest[size:]
        for key, ref in zip(small_names, small_refs):
            index = small[key][1]
            extra[key] = ref.at[index] if index else ref
        extra.update(zip(small_out_names, small_out_refs))
        work = Work(
            dict(zip(in_names, zip(in_refs, in_bufs))),
            dict(zip(out_names, zip(out_refs, out_bufs))),
            extra,
            in_sems,
            out_sems,
        )
        body(info_ref, work, weight_refs)
        work.finish()

    buffer = lambda a: pltpu.VMEM(a.shape, a.dtype)
    flat = []
    for value in scratch.values():
        flat += value if isinstance(value, list) else [value]
    results = pl.pallas_call(
        kernel,
        out_shape=[outs[n] for n in out_names] + [small_outs[n] for n in small_out_names],
        in_specs=[SMALL]
        + [ANY] * len(ins)
        + [NEAR] * len(small)
        + [ANY] * (len(weights) + len(after)),
        out_specs=[ANY] * len(outs) + [NEAR] * len(small_outs),
        scratch_shapes=[buffer(ins[n]) for n in in_names]
        + [buffer(outs[n]) for n in out_names]
        + flat
        + [pltpu.SemaphoreType.DMA((max(len(ins), 1),)), pltpu.SemaphoreType.DMA((32,))],
        compiler_params=pltpu.CompilerParams(vmem_limit_bytes=VMEM_BYTES),
        cost_estimate=lasting(cost),
        name=name,
    )(info, *ins.values(), *[array for array, _ in small.values()], *weights, *after)
    return results


def plain(body, name, info, ins, outs, scratch=(), after=()):
    first = len(ins) + (0 if info is None else 1)
    results = pl.pallas_call(
        lambda *refs: body(*refs[:first], *refs[first + len(after) :]),
        out_shape=outs,
        in_specs=([] if info is None else [SMALL]) + [NEAR] * len(ins) + [ANY] * len(after),
        out_specs=[NEAR] * len(outs),
        scratch_shapes=list(scratch),
        compiler_params=pltpu.CompilerParams(vmem_limit_bytes=VMEM_BYTES),
        cost_estimate=lasting(0.05),
        name=name,
    )(*([] if info is None else [info]), *ins, *after)
    return results if len(outs) > 1 else results[0]


def lasting(units):
    return pl.CostEstimate(flops=int(units * 0.4e9), bytes_accessed=1000, transcendentals=0)


def shape(*dims, dtype=F32):
    return jax.ShapeDtypeStruct(dims, dtype)


def start_rows(refs, place, plan, sems):
    own, sib, xa, ya, xb, yb = refs
    half = own.shape[0] // 2
    for rank in range(4):
        for parity in range(2):

            @pl.when(place == rank * 2 + parity)
            def _(rank=rank, parity=parity):
                for index, (shard, row, rows, dst) in enumerate(plan):
                    step = shard ^ rank
                    if step < 2:
                        src = (own, sib)[step].at[pl.ds(row, rows)]
                    else:
                        first, second = ((xa, ya), (xb, yb))[step - 2]
                        part = row // half
                        src = (first if part == parity else second).at[pl.ds(row - part * half, rows)]
                    pltpu.make_async_copy(src, dst, sems.at[index]).start()


def wait_rows(refs, plan, sems, which):
    for index in which:
        _, row, rows, dst = plan[index]
        pltpu.make_async_copy(refs[0].at[pl.ds(0, rows)], dst, sems.at[index]).wait()


def plan_of(buffers, first, rows):
    return [
        (shard, (first + which) * rows, rows, dst.at[pl.ds(shard * rows, rows)])
        for which, dst in enumerate(buffers)
        for shard in range(4)
    ]


def norm_rows(values):
    mean = jnp.mean(values, axis=-1, keepdims=True)
    center = values - mean
    factor = lax.rsqrt(jnp.mean(center * center, axis=-1, keepdims=True) + EPSILON)
    return center * factor, factor


def piece(mod, slot, index):
    width = mod.shape[1] // 9
    return mod[pl.ds(slot, 1), index * width : (index + 1) * width]


def entry_rows(x, mod, info, index, out):
    for block in range(x.shape[0] // UNIT):
        slot = info[1 + block]
        shift = piece(mod, slot, index)
        scale = 1.0 + piece(mod, slot, index + 1)

        def step(turn, carry):
            rows = pl.ds(pl.multiple_of(block * UNIT + turn * CHUNK, CHUNK), CHUNK)
            normed, _ = norm_rows(x[rows, :])
            out[rows, :] = (normed * scale + shift).astype(BF)
            return carry

        lax.fori_loop(0, UNIT // CHUNK, step, 0, unroll=True)


def residual_rows(x, mod, info, index, branch, branch_out, out, low=None):
    for block in range(x.shape[0] // UNIT):
        gate = piece(mod, info[1 + block], index)

        def step(turn, carry):
            rows = pl.ds(pl.multiple_of(block * UNIT + turn * CHUNK, CHUNK), CHUNK)
            values = branch[rows, :]
            branch_out[rows, :] = values.astype(BF)
            result = x[rows, :] + gate * values
            out[rows, :] = result
            if low is not None:
                low[rows, :] = result.astype(BF)
            return carry

        lax.fori_loop(0, UNIT // CHUNK, step, 0, unroll=True)


def fold(values):
    return jnp.sum(values.reshape(values.shape[0] // 8, 8, values.shape[1]), axis=0)


def total(values):
    return jnp.sum(values, axis=0, keepdims=True)


def gate_back(g, mod, info, index, branch, gb, stats):
    width = g.shape[1]
    sums = jnp.zeros((8, width), F32)
    for block in range(g.shape[0] // UNIT):
        slot = info[1 + block]
        gate = piece(mod, slot, index)

        def step(turn, carry):
            rows = pl.ds(pl.multiple_of(block * UNIT + turn * CHUNK, CHUNK), CHUNK)
            grad = g[rows, :]
            low = (gate * grad).astype(BF)
            gb[rows, :] = low
            return (
                carry[0] + fold(low.astype(F32)),
                carry[1] + fold(grad * branch[rows, :].astype(F32)),
            )

        sums, rows_sum = lax.fori_loop(
            0, UNIT // CHUNK, step, (sums, jnp.zeros((8, width), F32)), unroll=True
        )
        stats[pl.ds(8 + slot, 1), :] += total(rows_sum)
    stats[12:13, :] = total(sums)


def norm_back_rows(x, g, de, mod, info, index, out, stats, low=None):
    width = x.shape[1]
    for block in range(x.shape[0] // UNIT):
        slot = info[1 + block]
        scale = 1.0 + piece(mod, slot, index + 1)

        def step(turn, carry):
            rows = pl.ds(pl.multiple_of(block * UNIT + turn * CHUNK, CHUNK), CHUNK)
            normed, factor = norm_rows(x[rows, :])
            grad = de[rows, :]
            inner = grad * normed
            dn = grad * scale
            mean = jnp.mean(dn, axis=-1, keepdims=True)
            along = jnp.mean(dn * normed, axis=-1, keepdims=True)
            result = g[rows, :] + factor * (dn - mean - normed * along)
            out[rows, :] = result
            if low is not None:
                low[rows, :] = result.astype(BF)
            return (carry[0] + fold(grad), carry[1] + fold(inner))

        zero = jnp.zeros((8, width), F32)
        shift_sum, scale_sum = lax.fori_loop(0, UNIT // CHUNK, step, (zero, zero), unroll=True)
        stats[pl.ds(slot, 1), :] += total(shift_sum)
        stats[pl.ds(4 + slot, 1), :] += total(scale_sum)


def lane_ids(rows):
    return lax.broadcasted_iota(jnp.int32, (rows, LANES), 1)


def head_half(values, half):
    ids = lane_ids(values.shape[0])
    keep = ids < HEAD_WIDTH if half == 0 else ids >= HEAD_WIDTH
    return jnp.where(keep, values.astype(F32), 0.0)


def turned_halves(keys):
    turned = keys.T
    low = lax.broadcasted_iota(jnp.int32, turned.shape, 0) < HEAD_WIDTH
    zero = jnp.zeros(turned.shape, turned.dtype)
    return jnp.concatenate([jnp.where(low, turned, zero), jnp.where(low, zero, turned)], axis=1)


def query_marks(slot):
    return jnp.where(lane_ids(UNIT) == slot, 1.0, 0.0).astype(BF)


def key_marks(slots):
    ids = lane_ids(UNIT)
    parts = [jnp.where((ids < SLOTS) & (ids != slot), FAR, 0.0).astype(BF) for slot in slots]
    return jnp.concatenate(parts, axis=0)


def pair_lanes(pair):
    return pl.ds(pl.multiple_of(pair * LANES, LANES), LANES)


def start_own_rows(info, work, whole):
    share = work.rows.shape[0]
    first = pl.multiple_of((info[5] % 2) * share, share)
    copy = pltpu.make_async_copy(whole.at[pl.ds(first, share)], work.rows, work.row_sems.at[0])
    copy.start()
    return copy


def raise_rows(low, out):
    for row in range(0, low.shape[0], CHUNK):
        span = pl.ds(row, CHUNK)
        out[span, :] = low[span, :].astype(F32)


def kv_kernel(info, work, weights):
    rows = weights[0].shape[0] // 4
    plan = plan_of((work.w.at[0], work.w.at[1]), 1, rows)
    start_rows(weights[:6], info[0], plan, work.sems)
    if work.has("branch"):
        work.need("part", "other", "below")
        bias = work.bias[...].astype(F32)
        for row in range(0, work.sum.shape[0], CHUNK):
            span = pl.ds(row, CHUNK)
            work.sum[span, :] = (
                work.part[span, :].astype(F32) + work.other[span, :].astype(F32) + bias
            )
        residual_rows(work.below, work.mod_below, info, 8, work.sum, work.branch, work.x)
        work.flush("branch")
        work.flush("x")
    else:
        start_own_rows(info, work, weights[6]).wait()
        raise_rows(work.rows, work.x)
        work.flush("x")
    entry_rows(work.x, work.mod, info, 0, work.entry)
    work.flush("entry")
    entry = work.entry[...]
    wait_rows(weights, plan, work.sems, range(4))
    work.kv[0] = dot_nt(entry, work.w[0]).astype(BF)
    work.flush("kv", 0)
    wait_rows(weights, plan, work.sems, range(4, 8))
    work.kv[1] = (dot_nt(entry, work.w[1]) + work.biases[2:3, :]).astype(BF)
    work.flush("kv", 1)


def q_kernel(info, work, weights):
    rows = weights[0].shape[0] // 4
    plan = plan_of((work.w,), 0, rows)
    start_rows(weights, info[0], plan, work.sems)
    work.need("entry")
    wait_rows(weights, plan, work.sems, range(4))
    work.q[...] = (dot_nt(work.entry[...], work.w[...]) + work.biases[0:1, :]).astype(BF)
    work.flush("q")


def soft_pair(work, q_pair, keys, values, marks, logs, pair, span, words=None):
    ids = lane_ids(UNIT)
    results = []
    kept = logs[span, :]
    for half in range(2):
        left = (head_half(q_pair, half) * HEAD_WIDTH**-0.5).astype(BF)
        if marks is not None:
            left = jnp.concatenate([left, marks], axis=1)
        scores = dot_nt(left, keys)
        if words is not None:
            scores = jnp.where(ids < words, scores, FAR)
        peak = jnp.max(scores, axis=-1, keepdims=True)
        both = dot_nn(jnp.exp(scores - peak).astype(BF), values)
        sums = both[:, LANES:]
        results.append(both[:, :LANES] / sums)
        kept = jnp.where(ids == 2 * pair + half, peak + jnp.log(sums), kept)
    logs[span, :] = kept
    return jnp.where(ids < HEAD_WIDTH, results[0], results[1])


def self_kernel(info, work, weights):
    rows = weights[0].shape[0] // 4
    sems = work.sems
    plan = [(s, 3 * rows, rows, work.wo.at[pl.ds(s * rows, rows)]) for s in range(4)]
    start_rows(weights, info[0], plan, sems)
    share = work.x.shape[0]
    blocks = share // UNIT
    marks = key_marks([info[1 + b] for b in range(2 * blocks)])
    ones = jnp.ones((2 * share, LANES), BF)
    logs, mixed = work.logs, work.mixed
    logs[...] = jnp.zeros(logs.shape, F32)
    work.need("q", "kv_own", "kv_sib")

    def both(which, lanes):
        return jnp.concatenate([work.kv_own[which, :, lanes], work.kv_sib[which, :, lanes]], axis=0)

    def step(pair, carry):
        lanes = pair_lanes(pair)
        keys = jnp.concatenate([both(0, lanes), marks], axis=1)
        values = jnp.concatenate([both(1, lanes), ones], axis=1)
        for block in range(blocks):
            span = pl.ds(block * UNIT, UNIT)
            values_mixed = soft_pair(
                work,
                work.q[span, lanes],
                keys,
                values,
                query_marks(info[1 + block]),
                logs,
                pair,
                span,
            )
            low = values_mixed.astype(BF)
            mixed[span, lanes] = low
            work.rest[span, lanes] = (values_mixed - low.astype(F32)).astype(BF)
        return carry

    lax.fori_loop(0, mixed.shape[1] // LANES, step, 0)
    work.flush("mixed")
    work.flush("rest")
    work.lse[...] = logs[...].T[: work.lse.shape[0], :]
    work.flush("lse")
    wait_rows(weights, plan, sems, range(4))
    work.sum[...] = dot_nn(mixed[...], work.wo[...]) + work.bias[...].astype(F32)
    work.need("x")
    residual_rows(work.x, work.mod, info, 2, work.sum, work.branch, work.out)
    work.flush("branch")
    work.flush("out")


def cross_kernel(info, work, weights, words):
    rows = weights[0].shape[0] // 4
    sems = work.sems
    order = (1, 2, 0, 3)
    plan = [
        (shard, order[i // 4] * rows, count, dst)
        for i, (shard, _, count, dst) in enumerate(
            plan_of((work.wk, work.wv, work.wq, work.wo), 0, rows)
        )
    ]
    start_rows(weights, info[0], plan, sems)
    work.need("x")
    entry_rows(work.x, work.mod, info, 3, work.entry)
    work.flush("entry")
    work.need("text")
    wait_rows(weights, plan, sems, range(0, 4))
    work.kv[0] = dot_nt(work.text[...], work.wk[...]).astype(BF)
    wait_rows(weights, plan, sems, range(4, 8))
    work.kv[1] = (dot_nt(work.text[...], work.wv[...]) + work.biases[5:6, :]).astype(BF)
    work.flush("kv")
    wait_rows(weights, plan, sems, range(8, 12))
    work.q[...] = (dot_nt(work.entry[...], work.wq[...]) + work.biases[3:4, :]).astype(BF)
    work.flush("q")
    ones = jnp.ones((LANES, LANES), BF)
    logs, mixed = work.logs, work.mixed
    logs[...] = jnp.zeros(logs.shape, F32)

    def step(pair, carry):
        lanes = pair_lanes(pair)
        for block in range(mixed.shape[0] // UNIT):
            span = pl.ds(block * UNIT, UNIT)
            own = pl.ds(pl.multiple_of(info[1 + block] * LANES, LANES), LANES)
            mixed[span, lanes] = soft_pair(
                work,
                work.q[span, lanes],
                work.kv[0, own, lanes],
                jnp.concatenate([work.kv[1, own, lanes], ones], axis=1),
                None,
                logs,
                pair,
                span,
                words,
            ).astype(BF)
        return carry

    lax.fori_loop(0, mixed.shape[1] // LANES, step, 0, unroll=2)
    work.flush("mixed")
    work.lse[...] = logs[...].T[: work.lse.shape[0], :]
    work.flush("lse")
    wait_rows(weights, plan, sems, range(12, 16))
    work.sum[...] = dot_nn(mixed[...], work.wo[...]) + work.bias[...].astype(F32)
    residual_rows(work.x, work.mod, info, 5, work.sum, work.branch, work.out)
    work.flush("branch")
    work.flush("out")


def hidden_plan(refs, buffer):
    rows = buffer.shape[1]
    half = rows // 2
    return [
        (shard, row, half, buffer.at[shard, pl.ds(row, half)])
        for shard in range(4)
        for row in range(0, rows, half)
    ]


def start_chip(info, refs, layer, buffer, sems):
    copies = [
        pltpu.make_async_copy(ref.at[layer], buffer.at[(info[5] + i) % 2], sems.at[i])
        for i, ref in enumerate(refs)
    ]
    for copy in copies:
        copy.start()
    return copies


def bend_rows(before, bias, active, slope, lanes):
    for row in range(0, before.shape[0], CHUNK):
        span = pl.ds(row, CHUNK)
        values = before[span, :] + bias
        square = values * values
        half = 1.0 / (1.0 + jnp.exp(values * (-2.0 * ROOT - (2.0 * ROOT * CUBIC) * square)))
        act = values * half
        active[span, lanes] = act.astype(BF)
        slope[span, lanes] = (
            half + act * (1.0 - half) * (2.0 * ROOT + (6.0 * ROOT * CUBIC) * square)
        ).astype(BF)


def columns_of(shard, width):
    return pl.ds(pl.multiple_of(shard * width, width), width)


def start_hidden(info, work, weights, layer):
    if len(weights) == 4:
        ups = start_chip(info, weights[:2], layer, work.up, work.sems)
        downs = start_chip(info, weights[2:], layer, work.down, work.down_sems)
        return [lambda some=some: [copy.wait() for copy in some] for some in (ups, downs)]
    waits = []
    for refs, buffer, sems in (
        (weights[:6], work.up, work.sems),
        (weights[6:12], work.down, work.down_sems),
    ):
        refs = [ref.at[layer] for ref in refs[:2]] + list(refs[2:])
        plan = hidden_plan(refs, buffer)
        start_rows(refs, info[0], plan, sems)
        waits.append(
            lambda refs=refs, plan=plan, sems=sems: wait_rows(refs, plan, sems, range(len(plan)))
        )
    return waits


def hidden_kernel(info, work, weights, layer):
    waits = start_hidden(info, work, weights, layer)
    width = work.x.shape[1]
    shards = work.up.shape[0]
    first = info[6] * 2
    work.need("x")
    entry_rows(work.x, work.mod, info, 6, work.entry)
    work.flush("entry")
    for wait in waits:
        wait()
    work.sum[...] = jnp.zeros(work.sum.shape, F32)

    def step(shard, carry):
        lanes = columns_of(shard, width)
        bias = work.up_bias[:, columns_of(first + shard, width)]
        work.before[...] = dot_nn(work.entry[...], work.up[shard])
        bend_rows(work.before, bias, work.active, work.slope, lanes)
        work.sum[...] += dot_nn(work.active[:, lanes], work.down[shard])
        return carry

    lax.fori_loop(0, shards, step, 0)
    work.flush("active")
    work.flush("slope")
    work.part[...] = work.sum[...].astype(BF)
    work.flush("part")


def hidden_back_kernel(info, work, weights, layer):
    waits = start_hidden(info, work, weights, layer)
    work.stats[...] = jnp.zeros(work.stats.shape, F32)
    stats = work.stats.at[pl.ds(48, 24)]
    work.need("g", "branch")
    gate_back(work.g, work.mod, info, 8, work.branch, work.gb, stats)
    work.need("slope")
    for wait in waits:
        wait()
    hidden_back_rows(info, work, work.de, stats)
    work.part[...] = work.de[...].astype(BF)
    work.flush("part")
    work.flush("gb")
    work.flush("d_before")


def hidden_back_rows(info, work, de, stats):
    width = work.g.shape[1]
    shards = work.up.shape[0]
    first = info[6] * 2 if shards == 2 else 0
    de[...] = jnp.zeros(de.shape, F32)

    def step(shard, carry):
        lanes = columns_of(shard, width)
        work.before[...] = dot_nt(work.gb[...], work.down[shard])
        sums = jnp.zeros((8, width), F32)
        for row in range(0, work.g.shape[0], CHUNK):
            span = pl.ds(row, CHUNK)
            low = (work.before[span, :] * work.slope[span, lanes].astype(F32)).astype(BF)
            work.d_before[span, lanes] = low
            sums += fold(low.astype(F32))
        stats[pl.ds(13 + first + shard, 1), :] = total(sums)
        de[...] += dot_nt(work.d_before[:, lanes], work.up[shard])
        return carry

    lax.fori_loop(0, shards, step, 0)


def hidden_both_kernel(info, work, weights, layer):
    copy = start_own_rows(info, work, weights[12])
    waits = start_hidden(info, work, weights, layer)
    width = work.x.shape[1]
    work.need("x")
    entry_rows(work.x, work.mod, info, 6, work.entry)
    for wait in waits:
        wait()
    work.sum[...] = jnp.zeros(work.sum.shape, F32) + work.bias[...].astype(F32)

    def step(shard, carry):
        lanes = columns_of(shard, width)
        work.before[...] = dot_nn(work.entry[...], work.up[shard])
        bend_rows(work.before, work.up_bias[:, lanes], work.active, work.slope, lanes)
        work.sum[...] += dot_nn(work.active[:, lanes], work.down[shard])
        return carry

    lax.fori_loop(0, 4, step, 0)
    residual_rows(work.x, work.mod, info, 8, work.sum, work.branch, work.out, work.low)
    work.flush("low")
    work.stats[...] = jnp.zeros(work.stats.shape, F32)
    stats = work.stats.at[pl.ds(48, 24)]
    copy.wait()
    raise_rows(work.rows, work.g)
    gate_back(work.g, work.mod, info, 8, work.branch, work.gb, stats)
    hidden_back_rows(info, work, work.sum, stats)
    left, right = work.entry[...].T, work.gb[...].T
    for name, rank in zip(SIDES, (info[7], info[5])):
        out = work.outs[name][1]
        lanes = columns_of(rank, width)
        out[:, :width] = dot_nn(left, work.d_before[:, lanes]).astype(BF)
        out[:, width:] = dot_nn(right, work.active[:, lanes]).astype(BF)
        work.flush(name)
    norm_back_rows(work.x, work.g, work.sum, work.mod, info, 6, work.out, stats)
    work.flush("out")


def hidden_cross_kernel(info, work, weights, words):
    hidden_both_kernel(
        info,
        Names(
            work,
            x="x2",
            entry="entry3",
            branch="branch3",
            out="g_mid",
            send="f_send",
            keep="f_keep",
        ),
        weights[:13],
        1,
    )
    cross_back_kernel(
        info,
        Names(
            work,
            early="stats",
            g="g_mid",
            branch="branch2",
            entry="entry2",
            x="x1",
            de="sum",
            dq="entry3",
            d_mixed="rows",
            sems="csems",
            send="c_send",
            keep="c_keep",
        ),
        weights[13:],
        words,
    )


def attention_kernel(info, work, weights, words):
    self_kernel(
        info,
        Names(work, out="x1", mixed="mixed1", lse="lse1", branch="branch1", bias="self_bias"),
        weights[:6],
    )
    cross_kernel(
        info,
        Names(
            work,
            x="x1",
            q="cq",
            kv="ckv",
            mixed="mixed2",
            lse="lse2",
            branch="branch2",
            bias="cross_bias",
            wo="cross_wo",
            sems="csems",
        ),
        weights[6:],
        words,
    )


def hidden_grads_kernel(info, work, weights):
    width = work.entry.shape[1]
    work.need("entry", "d_before", "gb", "active")
    left, right = work.entry[...].T, work.gb[...].T
    for name, shift in zip(SIDES, (1, 0)):
        out = work.outs[name][1]
        lanes = columns_of((info[5] + shift) % 2, width)
        out[:, :width] = dot_nn(left, work.d_before[:, lanes]).astype(BF)
        out[:, width:] = dot_nn(right, work.active[:, lanes]).astype(BF)
        work.flush(name)


def pair_grads(info, work, members):
    rows = members[0][0].shape[0]
    low = lane_ids(rows) < HEAD_WIDTH
    step = 3 * LANES
    for at in range(len(members) // 2):
        products = [dot_nn(left, right) for left, right in members[2 * at : 2 * at + 2]]
        (a0, a1, a2), (b0, b1, b2) = [
            [p[:, i * LANES : (i + 1) * LANES] for i in range(3)] for p in products
        ]
        even = (a0, b0, jnp.where(low, a1, pltpu.roll(b1, HEAD_WIDTH, 1)))
        a1, b1 = pltpu.roll(a1, HEAD_WIDTH, 1), pltpu.roll(b1, HEAD_WIDTH, 1)
        a2r, b2r = pltpu.roll(a2, HEAD_WIDTH, 1), pltpu.roll(b2, HEAD_WIDTH, 1)
        odd = (jnp.where(low, a1, a2r), jnp.where(low, b1, b2r), jnp.where(low, a2r, b2))
        first = info[5] % 2 == 0
        for i, (mine, other) in enumerate(zip(even, odd)):
            lanes = pl.ds(at * step + i * LANES, LANES)
            work.outs["keep"][1][:, lanes] = jnp.where(first, mine, other).astype(BF)
            work.outs["send"][1][:, lanes] = jnp.where(first, other, mine).astype(BF)
    work.flush("send")
    work.flush("keep")


def chip_lanes(info, width):
    return pl.ds(pl.multiple_of(info[6] * (width // 2), width // 2), width // 2)


def query_output_kernel(info, work, weights):
    work.need("entry", "gb", "dq", "mixed")
    lanes = chip_lanes(info, work.dq.shape[1])
    pair_grads(
        info,
        work,
        [
            (work.entry[...].T, work.dq[:, lanes]),
            (work.gb[...].T, work.mixed[:, lanes]),
        ],
    )


def cross_back_kernel(info, work, weights, words):
    rows = weights[0].shape[0] // 4
    sems = work.sems
    plan = [
        (shard, (3 * rows, 0)[i // 4], count, dst)
        for i, (shard, _, count, dst) in enumerate(plan_of((work.wo, work.wq), 0, rows))
    ]
    start_rows(weights, info[0], plan, sems)
    work.stats[...] = work.early[...]
    stats = work.stats.at[pl.ds(24, 24)]
    g = work.g
    work.need("g")
    if work.takes("part"):
        work.need("part", "other", "above")
        for row in range(0, g.shape[0], CHUNK):
            span = pl.ds(row, CHUNK)
            work.de[span, :] = work.part[span, :].astype(F32) + work.other[span, :].astype(F32)
        g = work.g_mid
        norm_back_rows(
            work.above, work.g, work.de, work.mod, info, 6, g, work.stats.at[pl.ds(48, 24)]
        )
    work.need("branch")
    gate_back(g, work.mod, info, 5, work.branch, work.gb, stats)
    wait_rows(weights, plan, sems, range(0, 4))
    work.d_mixed[...] = dot_nt(work.gb[...], work.wo[...]).astype(BF)
    work.dkv_sum[...] = jnp.zeros(work.dkv_sum.shape, F32)
    real = lax.broadcasted_iota(jnp.int32, (LANES, UNIT), 0) < words
    work.need("q", "kv", "lse")

    def step(pair, carry):
        lanes = pair_lanes(pair)
        for block in range(work.q.shape[0] // UNIT):
            span = pl.ds(block * UNIT, UNIT)
            own = pl.ds(pl.multiple_of(info[1 + block] * LANES, LANES), LANES)
            q_pair = work.q[span, lanes]
            d_pair = work.d_mixed[span, lanes]
            keys = work.kv[0, own, lanes]
            values = work.kv[1, own, lanes]
            lefts, grads, probs_low, scores_low = [], [], [], []
            for half in range(2):
                left = (head_half(q_pair, half) * HEAD_WIDTH**-0.5).astype(BF)
                grad = head_half(d_pair, half).astype(BF)
                logs = work.lse[pl.ds(2 * pair + half, 1), span]
                probs = jnp.where(real, jnp.exp(dot_nt(keys, left) - logs), 0.0)
                d_probs = dot_nt(values, grad)
                inner = jnp.sum(probs * d_probs, axis=0, keepdims=True)
                lefts.append(left)
                grads.append(grad)
                probs_low.append(probs.astype(BF))
                scores_low.append((probs * (d_probs - inner)).astype(BF))
            wide_scores = jnp.concatenate(scores_low, axis=1)
            grad_v = dot_nn(jnp.concatenate(probs_low, axis=1), jnp.concatenate(grads, axis=0))
            grad_k = dot_nn(wide_scores, jnp.concatenate(lefts, axis=0))
            grad_q = dot_nn(turned_halves(keys), jnp.concatenate(scores_low, axis=0))
            work.dq[span, lanes] = (grad_q.T * HEAD_WIDTH**-0.5).astype(BF)
            work.dkv_sum[0, own, lanes] += grad_k
            work.dkv_sum[1, own, lanes] += grad_v
        return carry

    lax.fori_loop(0, work.q.shape[1] // LANES, step, 0, unroll=2)
    work.dkv[...] = work.dkv_sum[...].astype(BF)
    work.need("entry", "text", "mixed")
    lanes = chip_lanes(info, work.dq.shape[1])
    text = work.text[...].T
    pair_grads(
        info,
        work,
        [
            (work.entry[...].T, work.dq[:, lanes]),
            (text, work.dkv[0, :, lanes]),
            (text, work.dkv[1, :, lanes]),
            (work.gb[...].T, work.mixed[:, lanes]),
        ],
    )
    stats[13:14, :] = total(fold(work.dq[...].astype(F32)))
    stats[14:15, :] = total(fold(work.dkv[1].astype(F32)))
    wait_rows(weights, plan, sems, range(4, 8))
    work.de[...] = dot_nn(work.dq[...], work.wq[...])
    work.need("x")
    norm_back_rows(work.x, g, work.de, work.mod, info, 3, work.out, stats)
    work.flush("out")


def self_back_kernel(info, work, weights):
    rows = weights[0].shape[0] // 4
    sems = work.sems
    plan = [(s, 3 * rows, rows, work.wo.at[pl.ds(s * rows, rows)]) for s in range(4)]
    start_rows(weights, info[0], plan, sems)
    work.stats[...] = work.early[...]
    stats = work.stats.at[pl.ds(0, 24)]
    work.need("g", "branch")
    gate_back(work.g, work.mod, info, 2, work.branch, work.gb, stats)
    work.flush("gb")
    share = work.g.shape[0]
    blocks = share // UNIT
    marks = key_marks([info[1 + b] for b in range(2 * blocks)])
    wait_rows(weights, plan, sems, range(4))
    work.d_mixed[...] = dot_nt(work.gb[...], work.wo[...]).astype(BF)
    work.need("mixed", "rest", "q", "kv_own", "kv_sib", "lse")
    width = work.q.shape[1]
    head = lax.broadcasted_iota(jnp.int32, (16, width), 0)
    lane = lax.broadcasted_iota(jnp.int32, (16, width), 1)
    first = head * HEAD_WIDTH
    pick = jnp.where((lane >= first) & (lane < first + HEAD_WIDTH), 1.0, 0.0)
    for block in range(blocks):
        span = pl.ds(block * UNIT, UNIT)
        whole = work.mixed[span, :].astype(F32) + work.rest[span, :].astype(F32)
        work.inner[:, span] = lax.dot_general(
            pick,
            whole * work.d_mixed[span, :].astype(F32),
            (((1,), (1,)), ((), ())),
            precision=lax.Precision.HIGHEST,
            preferred_element_type=F32,
        )

    def both(which, lanes):
        return jnp.concatenate([work.kv_own[which, :, lanes], work.kv_sib[which, :, lanes]], axis=0)

    def step(pair, carry):
        lanes = pair_lanes(pair)
        keys = both(0, lanes)
        values = both(1, lanes)
        marked = jnp.concatenate([keys, marks], axis=1)
        turned = turned_halves(keys)
        lefts, grads, probs_low, scores_low = [], [], [], []
        for block in range(blocks):
            span = pl.ds(block * UNIT, UNIT)
            q_pair = work.q[span, lanes]
            d_pair = work.d_mixed[span, lanes]
            ends = query_marks(info[1 + block])
            for half in range(2):
                left = (head_half(q_pair, half) * HEAD_WIDTH**-0.5).astype(BF)
                grad = head_half(d_pair, half).astype(BF)
                logs = work.lse[pl.ds(2 * pair + half, 1), span]
                probs = jnp.exp(dot_nt(marked, jnp.concatenate([left, ends], axis=1)) - logs)
                d_probs = dot_nt(values, grad)
                inner = work.inner[pl.ds(2 * pair + half, 1), span]
                lefts.append(left)
                grads.append(grad)
                probs_low.append(probs.astype(BF))
                scores_low.append((probs * (d_probs - inner)).astype(BF))
            grad_q = dot_nn(turned, jnp.concatenate(scores_low[-2:], axis=0))
            work.dq[span, lanes] = (grad_q.T * HEAD_WIDTH**-0.5).astype(BF)
        grad_v = dot_nn(jnp.concatenate(probs_low, axis=1), jnp.concatenate(grads, axis=0))
        grad_k = dot_nn(jnp.concatenate(scores_low, axis=1), jnp.concatenate(lefts, axis=0))
        for which, grad in ((0, grad_k.astype(BF)), (1, grad_v.astype(BF))):
            work.dkv_own[which, :, lanes] = grad[:share]
            work.dkv_give[which, :, lanes] = grad[share:]
        return carry

    lax.fori_loop(0, work.q.shape[1] // LANES, step, 0)
    work.flush("dkv_give")
    work.flush("dkv_own")
    work.flush("dq")


def sum_keys_values(info, work, dkv):
    work.need("dkv_own", "dkv_sib")
    for which in range(2):
        dkv[which] = (
            work.dkv_own[which].astype(F32) + work.dkv_sib[which].astype(F32)
        ).astype(BF)
    work.need("entry")
    lanes = chip_lanes(info, dkv.shape[2])
    entry = work.entry[...].T
    pair_grads(info, work, [(entry, dkv[0, :, lanes]), (entry, dkv[1, :, lanes])])


def kv_grads_kernel(info, work, weights):
    sum_keys_values(info, work, work.dkv)
    work.flush("dkv")


def qkv_back_kernel(info, work, weights):
    rows = weights[0].shape[0] // 4
    sems = work.sems
    plan = plan_of((work.wq, work.wk, work.wv), 0, rows)
    start_rows(weights, info[0], plan, sems)
    work.stats[...] = work.early[...]
    stats = work.stats.at[pl.ds(0, 24)]
    if work.has("send"):
        sum_keys_values(info, work, work.dkv)
    else:
        work.need("dkv")
    work.need("dq")
    stats[13:14, :] = total(fold(work.dq[...].astype(F32)))
    stats[14:15, :] = total(fold(work.dkv[1].astype(F32)))
    wait_rows(weights, plan, sems, range(0, 12))
    work.de[...] = (
        dot_nn(work.dq[...], work.wq[...])
        + dot_nn(work.dkv[0], work.wk[...])
        + dot_nn(work.dkv[1], work.wv[...])
    )
    work.need("x", "g")
    low = work.low if work.has("low") else None
    norm_back_rows(work.x, work.g, work.de, work.mod, info, 0, work.out, stats, low)
    work.flush("out")
    if low is not None:
        work.flush("low")


def merge_kernel(info, *refs, spots, after):
    chains = len(spots)
    ins, outs = refs[: 4 * chains], refs[4 * chains + after :]
    for chain, (result, column) in enumerate(spots):
        for side in range(2):
            received, kept = ins[4 * chain + 2 * side], ins[4 * chain + 2 * side + 1]
            out = outs[2 * result + side]
            lanes = pl.ds(column, received.shape[2])
            out[:, :, lanes] = (received[...].astype(F32) + kept[...].astype(F32)).astype(BF)


def gate(arrays, after):
    count = len(arrays)
    return pl.pallas_call(
        lambda *refs: None,
        out_shape=[shape(*a.shape, dtype=a.dtype) for a in arrays],
        in_specs=[ANY] * (count + len(after)),
        out_specs=[ANY] * count,
        input_output_aliases={i: i for i in range(count)},
        cost_estimate=lasting(0.5),
        name="gate",
    )(*arrays, *after)


def pack_kernel(info, *refs, groups, whole, after):
    count = sum(len(members) for _, members in groups)
    sources, rest = refs[:count], refs[count + after :]
    (in_sems, out_sems), rest = rest[-2:], rest[:-2]
    count = len(groups) + sum(whole)
    outs, held = list(rest[:count]), rest[count:]
    owns = [outs.pop(0) if one else None for one in whole]
    spots = []
    at = 0
    for index, (layer, members) in enumerate(groups):
        rows = held[index].shape[0]
        piece_rows = rows // 4
        for quarter in range(4):
            row = quarter * piece_rows
            source = sources[at + quarter * len(members) // 4]
            src = source.at[layer, pl.ds(row % source.shape[1], piece_rows)]
            spots.append((index, quarter, held[index].at[pl.ds(row, piece_rows)], src))
        at += len(members)

    def arriving(place):
        _, _, spot, src = spots[place]
        return pltpu.make_async_copy(src, spot, in_sems.at[place])

    def leaving(index, which):
        if which == 2:
            return pltpu.make_async_copy(held[index], owns[index], out_sems.at[2 * index])
        rows = outs[index].shape[0]
        src = held[index].at[pl.ds(which * rows, rows)]
        return pltpu.make_async_copy(src, outs[index], out_sems.at[2 * index + 1])

    def by_parity(act):
        for parity in range(2):

            @pl.when(info[0] % 2 == parity)
            def _(parity=parity):
                act(parity)

    for place in range(len(spots)):
        arriving(place).start()
    for index in range(len(groups)):
        for quarter in range(4):
            arriving(4 * index + quarter).wait()
        by_parity(lambda parity: leaving(index, parity).start())
        if whole[index]:
            leaving(index, 2).start()
    for index in range(len(groups)):
        by_parity(lambda parity: leaving(index, parity).wait())
        if whole[index]:
            leaving(index, 2).wait()


def mod_kernel(condition, mod, mod_bias, q, v, cq, cv, up, out):
    narrow, units, columns = q.shape[1], up.shape[1], mod.shape[1]
    out[...] = jnp.zeros(out.shape, F32)
    for layer in range(LAYERS):
        row = pl.ds(layer, 1)
        out[layer, 0:SLOTS, 0:columns] = dot_nt(condition[...], mod[layer]) + mod_bias[
            row, :
        ].astype(F32)
        out[layer, 4:5, 0:units] = up[row, :].astype(F32)
        out[layer, 5:6, 0:narrow] = q[row, :].astype(F32)
        out[layer, 6:7, 0:narrow] = v[row, :].astype(F32)
        out[layer, 7:8, 0:narrow] = cq[row, :].astype(F32)
        out[layer, 4:5, 1024 : 1024 + narrow] = cv[row, :].astype(F32)


def assemble_kernel(info, *refs, narrow, units, columns):
    parts, (mods, narrows, ups) = refs[:4], refs[4:]
    narrows[...] = jnp.zeros(narrows.shape, F32)
    for rank in range(4):

        @pl.when(info[5] == rank)
        def _(rank=rank):
            for shard in range(4):
                part = parts[shard ^ rank]
                for layer in range(LAYERS):
                    mods[layer, :, shard * columns : (shard + 1) * columns] = part[
                        layer, 0:SLOTS, 0:columns
                    ]
                    ups[layer, :, shard * units : (shard + 1) * units] = part[layer, 4:5, 0:units]
                    at = slice(shard * narrow, (shard + 1) * narrow)
                    for row, source in ((0, 5), (2, 6), (3, 7)):
                        narrows[layer, row : row + 1, at] = part[
                            layer, source : source + 1, 0:narrow
                        ]
                    narrows[layer, 5:6, at] = part[layer, 4:5, 1024 : 1024 + narrow]


def collect_kernel(info, *refs, narrow, units, columns):
    stats, condition, out = refs[: 2 * LAYERS], refs[2 * LAYERS], refs[2 * LAYERS + 1]
    sums = refs[2 * LAYERS + 2]
    width = stats[0].shape[1]
    work = out
    out = refs[2 * LAYERS + 3]
    out[...] = jnp.zeros(out.shape, F32)
    for layer in range(LAYERS):
        sums[...] = stats[2 * layer][...] + stats[2 * layer + 1][...]
        base = 8 * layer
        out[base + 4 : base + 5, width : 2 * width] = sums[60:61, :]
        out[base + 5 : base + 6, 0:width] = sums[12:13, :]
        out[base + 5 : base + 6, width : 2 * width] = sums[36:37, :]
        for index in range(2):
            out[base + 6 + index : base + 7 + index, 512 : 512 + width] = condition[
                2 * layer + index : 2 * layer + index + 1, :
            ].astype(F32)
        for rank in range(4):

            @pl.when(info[5] == rank)
            def _(rank=rank, base=base):
                first = rank * columns
                for index in range(9):
                    low = max(first, index * width)
                    high = min(first + columns, (index + 1) * width)
                    if low < high:
                        row = (index // 3) * 24 + (index % 3) * 4
                        out[base : base + 4, low - first : high - first] = sums[
                            row : row + 4, low - index * width : high - index * width
                        ]
                out[base + 4 : base + 5, 0:units] = sums[61 + rank : 62 + rank, :]
                own = slice(rank * narrow, (rank + 1) * narrow)
                out[base + 6 : base + 7, 0:narrow] = sums[13:14, own]
                out[base + 6 : base + 7, 256 : 256 + narrow] = sums[14:15, own]
                out[base + 7 : base + 8, 0:narrow] = sums[37:38, own]
                out[base + 7 : base + 8, 256 : 256 + narrow] = sums[38:39, own]
    work[...] = out[...].astype(BF)


def spread_kernel(info, gathered, grad, bias_grad, q, v, cq, cv, up, o1, o2, o3, rows, conditions):
    count = gathered.shape[0]
    columns, part = grad.shape[2], grad.shape[1]
    width, narrow, units = conditions.shape[1], q.shape[1], up.shape[1]
    shift = lax.rem(width - info[8] * part, width)
    for index in range(count):
        for slot in range(SLOTS):
            row = 8 * (slot // 2) + 6 + slot % 2
            conditions[SLOTS * index + slot : SLOTS * index + slot + 1, :] = gathered[
                index ^ info[8], row : row + 1, 512 : 512 + width
            ].astype(F32)
    turned = pltpu.roll(conditions[...], shift, 1)[:, :part].T
    for layer in range(LAYERS):
        base = 8 * layer
        sums = jnp.zeros((8, gathered.shape[2]), F32)
        for index in range(count):
            values = gathered[index ^ info[8]].astype(F32)[base : base + 8]
            sums += values
            rows[SLOTS * index : SLOTS * (index + 1), :] = values[0:SLOTS, 0:columns]
        grad[layer] = jnp.dot(
            turned, rows[...], precision=lax.Precision.HIGHEST, preferred_element_type=F32
        )
        at = slice(layer, layer + 1)
        bias_grad[at, :] = jnp.sum(sums[0:SLOTS, 0:columns], axis=0, keepdims=True)
        up[at, :] = sums[4:5, 0:units]
        q[at, :] = sums[6:7, 0:narrow]
        v[at, :] = sums[6:7, 256 : 256 + narrow]
        cq[at, :] = sums[7:8, 0:narrow]
        cv[at, :] = sums[7:8, 256 : 256 + narrow]
        for out, row, lane in ((o1, 5, 0), (o2, 5, width), (o3, 4, width)):
            own = jnp.broadcast_to(sums[row : row + 1, lane : lane + width], (8, width))
            out[at, :] = pltpu.roll(own, shift, 1)[0:1, :part]


def finish_kernel(*refs, wide, spots):
    parts, outs = refs[: 2 * len(spots)], refs[2 * len(spots) :]
    step = 3 * LANES
    for chain, (at, places) in enumerate(spots):
        values = parts[2 * chain][0].astype(F32) + parts[2 * chain + 1][0].astype(F32)
        for layer, pair in places:
            if wide:
                width = outs[0].shape[2]
                for out in outs:
                    out[layer] = values[:, at : at + width]
                    at += width
                continue
            both = values[:, at : at + step]
            at += step
            first = jnp.concatenate(
                [both[:, :LANES], both[:, 2 * LANES : 2 * LANES + HEAD_WIDTH]], axis=1
            )
            second = jnp.concatenate(
                [both[:, LANES : 2 * LANES], both[:, 2 * LANES + HEAD_WIDTH :]], axis=1
            )
            for out, matrix in zip(outs[2 * pair : 2 * pair + 2], (first, second)):
                out[layer] = matrix if out.shape[1:] == matrix.shape else matrix.T


def join_kernel(info, rows, other, out):
    share = rows.shape[0]
    for core in range(2):

        @pl.when(info[5] % 2 == core)
        def _(core=core):
            out[pl.ds(core * share, share), :] = rows[...]
            out[pl.ds((1 - core) * share, share), :] = other[...]


def tensor_hop(values, step):
    return lax.ppermute(values, "tensor", [(i, i ^ step) for i in range(4)])


def dp_hop(values, step):
    size = lax.axis_size("dp")
    return lax.ppermute(values, "dp", [(i, i ^ step) for i in range(size)])


def time_features(moments, width):
    half = width // 2
    rates = jnp.exp(-math.log(10000.0) * jnp.arange(half, dtype=F32) / half)
    angles = moments.astype(F32)[:, None] * rates[None, :]
    return jnp.concatenate([jnp.cos(angles), jnp.sin(angles)], axis=1)


def shards(
    tokens,
    text,
    timesteps,
    item_frames,
    cotangent,
    self_query,
    self_query_bias,
    self_key,
    self_value,
    self_value_bias,
    self_output,
    self_output_bias,
    cross_query,
    cross_query_bias,
    cross_key,
    cross_value,
    cross_value_bias,
    cross_output,
    cross_output_bias,
    hidden_up,
    hidden_up_bias,
    hidden_down,
    hidden_down_bias,
    modulation,
    modulation_bias,
):
    frames, width = tokens.shape
    words = text.shape[1]
    columns = modulation.shape[2]
    narrow = self_query.shape[2]
    units = hidden_up.shape[2]
    rank = lax.axis_index("tensor")
    me = lax.axis_index("dp")
    size = lax.axis_size("dp")
    core = rank % 2
    share = frames // 2
    blocks = share // UNIT
    unit = width // size
    turn = lambda values: jnp.swapaxes(values, 1, 2)

    order = jnp.arange(SLOTS, dtype=jnp.int32)
    ends = jnp.sum(jnp.where(order[:, None] <= order[None, :], item_frames[:, None], 0), axis=0)
    turned = (jnp.arange(frames // UNIT, dtype=jnp.int32) + core * blocks) % (2 * blocks)
    slots = jnp.sum((turned[:, None] * UNIT >= ends[None, :]).astype(jnp.int32), axis=1)
    places = jnp.stack([rank, rank // 2, rank ^ 1, me]).astype(jnp.int32)
    info = jnp.concatenate([(rank * 2 + me % 2)[None].astype(jnp.int32), slots, places])

    def pack(members, whole, after=()):
        rows = [sum(a.shape[1] for a in some) for _, some in members]
        outs = [shape(r, width, dtype=BF) for r, one in zip(rows, whole) if one]
        outs += [shape(r // 2, width, dtype=BF) for r in rows]
        arrays = [a for _, some in members for a in some]
        results = pl.pallas_call(
            partial(
                pack_kernel,
                groups=[(layer, [None] * len(some)) for layer, some in members],
                whole=whole,
                after=len(after),
            ),
            out_shape=outs,
            in_specs=[SMALL] + [ANY] * (len(arrays) + len(after)),
            out_specs=[ANY] * len(outs),
            scratch_shapes=[
                *[pltpu.VMEM((r, width), BF) for r in rows],
                pltpu.SemaphoreType.DMA((4 * len(members),)),
                pltpu.SemaphoreType.DMA((2 * len(members),)),
            ],
            compiler_params=pltpu.CompilerParams(vmem_limit_bytes=VMEM_BYTES),
            cost_estimate=lasting(1.0),
            name="pack_weights",
        )(info, *arrays, *after)
        return list(results[: sum(whole)]), list(results[sum(whole) :])

    selfs = [turn(self_query), turn(self_key), turn(self_value), self_output]
    crosses = [turn(cross_query), turn(cross_key), turn(cross_value), cross_output]
    own0, first0 = pack([(0, selfs)], [True])


    condition = jax.nn.silu(time_features(timesteps, width)).astype(BF)
    mine = plain(
        mod_kernel,
        "mod_rows",
        None,
        [
            condition,
            turn(modulation),
            modulation_bias,
            self_query_bias,
            self_value_bias,
            cross_query_bias,
            cross_value_bias,
            hidden_up_bias,
        ],
        [shape(LAYERS, 8, -(-columns // LANES) * LANES)],
    )
    own1, first1 = pack(
        [(0, crosses), (1, selfs), (1, crosses), (1, [hidden_up]), (1, [hidden_down])],
        [True, True, True, False, False],
        [mine],
    )
    firsts, owns = first0 + first1, own0 + own1
    others = [tensor_hop(mine, 1), tensor_hop(mine, 2)]
    others.append(tensor_hop(others[0], 2))
    out_biases = [
        b.reshape(LAYERS, 1, width) for b in (self_output_bias, cross_output_bias, hidden_down_bias)
    ]

    count = len(firsts)
    along_x, along_y, over_x, over_y, sibs = [[None] * count for _ in range(5)]

    def leave(index):
        along_x[index] = tensor_hop(firsts[index], 2)

    def swap(index):
        sibs[index] = tensor_hop(owns[index], 1)

    def go_on(index):
        along_y[index] = dp_hop(along_x[index], 1)
        over_x[index] = tensor_hop(along_x[index], 1)

    def end(index):
        over_y[index] = tensor_hop(along_y[index], 1)

    def weights_of(index):
        return [
            owns[index],
            sibs[index],
            along_x[index],
            along_y[index],
            over_x[index],
            over_y[index],
        ]

    def open_gate(after, leaving=(), at_x=(), at_y=(), settled=()):
        places = [(firsts, i) for i in leaving]
        places += [(along_x, i) for i in at_x] + [(along_y, i) for i in at_y] + list(settled)
        opened = gate([values[i] for values, i in places], after)
        for (values, i), array in zip(places, opened):
            values[i] = array
        for i in leaving:
            leave(i)
        for i in at_x:
            go_on(i)
        for i in at_y:
            end(i)
        return list(opened)

    leave(0)
    swap(0)
    open_gate([mine], [], [0])
    open_gate([*others, along_x[0]], [1])
    swap(1)
    go_on(1)
    owns += [hidden_up, hidden_down]
    sibs[4:6] = tensor_hop(hidden_up, 1), tensor_hop(hidden_down, 1)
    mods, narrow_biases, up_biases = plain(
        partial(assemble_kernel, narrow=narrow, units=units, columns=columns),
        "mod_all",
        info,
        [mine, *others],
        [
            shape(LAYERS, SLOTS, 4 * columns),
            shape(LAYERS, 8, 4 * narrow),
            shape(LAYERS, 1, 4 * units),
        ],
        after=[along_x[1]],
    )
    open_gate([mods], [], [], [0])

    text_rows = jnp.pad(text, ((0, 0), (0, LANES - words), (0, 0))).reshape(-1, width)
    whole = pltpu.VMEM((width, width), BF)
    four = pltpu.VMEM((4, width, units), BF)
    two = pltpu.VMEM((2, width, units), BF)
    floats = pltpu.VMEM((share, width), F32)
    lows = pltpu.VMEM((share, width), BF)
    sems = lambda n: pltpu.SemaphoreType.DMA((n,))
    frame_low = shape(share, width, dtype=BF)
    frame_high = shape(share, width)
    frame_wide = shape(share, 4 * units, dtype=BF)
    frame_chip = shape(share, 2 * units, dtype=BF)
    two_low = shape(2, share, width, dtype=BF)
    two_text = shape(2, SLOTS * LANES, width, dtype=BF)
    logs = shape(16, share)
    log_work = pltpu.VMEM((share, LANES), F32)
    stat_shape = shape(72, width)

    kept = []
    for layer in range(LAYERS):
        first = 2 * layer
        mod = (mods, (layer,))
        biases = (narrow_biases, (layer,))
        common = dict(w=pltpu.VMEM((2, width, width), BF), sems=sems(8))
        if layer == 0:
            entry1, kv, x = run(
                kv_kernel,
                "self_kv",
                info,
                {},
                dict(mod=mod, biases=biases),
                weights_of(first) + [tokens],
                dict(entry=frame_low, kv=two_low, x=frame_high),
                {},
                common | dict(rows=lows, row_sems=sems(1)),
                [along_x[1], sibs[1], sibs[4], sibs[5]],
                3.0,
            )
        else:
            entry1, kv, x, branch3 = run(
                kv_kernel,
                "residual_kv",
                info,
                dict(part=part, other=tensor_hop(part, 2), below=kept[-1]["x2"]),
                dict(
                    mod=mod,
                    mod_below=(mods, (layer - 1,)),
                    bias=(out_biases[2], (layer - 1,)),
                    biases=biases,
                ),
                weights_of(first),
                dict(entry=frame_low, kv=two_low, x=frame_high, branch=frame_low),
                {},
                common | dict(sum=floats),
                opened,
                3.0,
            )
            kept[-1]["branch3"] = branch3
        kv_sib = tensor_hop(kv, 1)
        opened = (
            open_gate([entry1], [2, 3, 4], [], [], [(over_x, 1)])
            if layer == 0
            else open_gate([entry1], [5], [], [3], [(over_x, 3), (sibs, 3)])
        )
        if layer == 0:
            end(1)
        (q,) = run(
            q_kernel,
            "query",
            info,
            dict(entry=entry1),
            dict(biases=biases),
            weights_of(first),
            dict(q=frame_low),
            {},
            dict(w=whole, sems=sems(4)),
            [],
            15.0,
        )
        if layer == 0:
            x1, mixed1, rest1, lse1, branch1, x2, entry2, cq, ckv, mixed2, lse2, branch2 = run(
                lambda info, work, w: attention_kernel(info, work, w, words),
                "self_cross",
                info,
                dict(q=q, kv_own=kv, kv_sib=kv_sib, x=x, text=text_rows),
                dict(
                    mod=mod,
                    biases=biases,
                    self_bias=(out_biases[0], (layer,)),
                    cross_bias=(out_biases[1], (layer,)),
                ),
                weights_of(first) + weights_of(first + 1),
                dict(
                    x1=frame_high,
                    mixed1=frame_low,
                    rest=frame_low,
                    lse1=logs,
                    branch1=frame_low,
                    out=frame_high,
                    entry=frame_low,
                    cq=frame_low,
                    ckv=two_text,
                    mixed2=frame_low,
                    lse2=logs,
                    branch2=frame_low,
                ),
                {},
                dict(
                    wq=whole,
                    wk=whole,
                    wv=whole,
                    wo=whole,
                    cross_wo=whole,
                    logs=log_work,
                    sum=floats,
                    sems=sems(4),
                    csems=sems(16),
                ),
                opened,
                14.0,
            )
            opened = open_gate([x2], [], [2, 3], [], [(along_x, 4)])
            swap(2)
            swap(3)
        else:
            x1, mixed1, rest1, lse1, branch1 = run(
                self_kernel,
                "self",
                info,
                dict(q=q, kv_own=kv, kv_sib=kv_sib, x=x),
                dict(mod=mod, bias=(out_biases[0], (layer,))),
                weights_of(first),
                dict(out=frame_high, mixed=frame_low, rest=frame_low, lse=logs, branch=frame_low),
                {},
                dict(wo=whole, logs=log_work, sum=floats, sems=sems(4)),
                opened,
                8.0,
            )
            opened = open_gate([x1], [], [5], [4], [(over_x, 4), (over_y, 3)])
            x2, entry2, cq, ckv, mixed2, lse2, branch2 = run(
                partial(cross_kernel, words=words),
                "cross",
                info,
                dict(x=x1, text=text_rows),
                dict(mod=mod, biases=biases, bias=(out_biases[1], (layer,))),
                weights_of(first + 1),
                dict(
                    out=frame_high,
                    entry=frame_low,
                    q=frame_low,
                    kv=two_text,
                    mixed=frame_low,
                    lse=logs,
                    branch=frame_low,
                ),
                {},
                dict(
                    wq=whole, wk=whole, wv=whole, wo=whole, logs=log_work, sum=floats, sems=sems(16)
                ),
                opened,
                6.0,
            )
            opened = open_gate([x2], [], [], [5], [(over_x, 5), (over_y, 4)])
        if layer == 0:
            part, entry3, active, slope = run(
                lambda info, work, w: hidden_kernel(info, work, w, 0),
                "ff_part",
                info,
                dict(x=x2),
                dict(mod=mod, up_bias=(up_biases, (layer,))),
                [hidden_up, sibs[4], hidden_down, sibs[5]],
                dict(part=frame_low, entry=frame_low, active=frame_chip, slope=frame_chip),
                {},
                dict(
                    up=two, down=two, before=floats, sum=floats, sems=sems(2), down_sems=sems(2)
                ),
                opened,
                5.0,
            )
            opened = open_gate([part], [], [4], [2], [(over_x, 2), (sibs, 2)])
            x3 = branch3 = None
        else:
            x3 = branch3 = active = slope = entry3 = None
        kept.append(
            dict(
                x=x,
                entry1=entry1,
                q=q,
                kv=kv,
                kv_sib=kv_sib,
                mixed1=mixed1,
                rest1=rest1,
                lse1=lse1,
                branch1=branch1,
                x1=x1,
                entry2=entry2,
                cq=cq,
                ckv=ckv,
                mixed2=mixed2,
                lse2=lse2,
                branch2=branch2,
                x2=x2,
                entry3=entry3,
                active=active,
                slope=slope,
                branch3=branch3,
            )
        )
        x = x3
    last_gate = opened

    def join(rows, *after):
        return plain(
            join_kernel,
            "join_rows",
            info,
            [rows, tensor_hop(rows, 1)],
            [shape(2 * share, width, dtype=BF)],
            after=after,
        )


    chains = {}

    def start(name, send, keep):
        view = (size, unit, send.shape[1])
        chains[name] = (tensor_hop(send, 1).reshape(view), keep.reshape(view), 0)

    def held(*names):
        return [chains[name][1] for name in names]

    def advance(names, after=(), cost=1.5):
        targets = [(n, [n]) if isinstance(n, str) else n for n in names]
        targets = [t for t in targets if 2 ** chains[t[1][0]][2] < size]
        if not targets:
            return
        ins, in_specs, outs, out_specs, spots = [], [], [], [], []
        for result, (_, parts) in enumerate(targets):
            column = 0
            for name in parts:
                received, kept_part, bit = chains[name]
                blocks_left, rows, wide = received.shape
                spots.append((result, column))
                column += wide
                for side in range(2):

                    def at(i, info, bit=bit, side=side):
                        return (0, ((info[8] >> bit) & 1) ^ side, 0, 0)

                    for part in (received, kept_part):
                        ins.append(part.reshape(blocks_left // 2, 2, rows, wide))
                        in_specs.append(pl.BlockSpec((blocks_left // 2, None, rows, wide), at))
            for side in range(2):
                outs.append(shape(blocks_left // 2, rows, column, dtype=BF))
                out_specs.append(
                    pl.BlockSpec((blocks_left // 2, rows, column), lambda i, info: (0, 0, 0))
                )
        results = pl.pallas_call(
            partial(merge_kernel, spots=spots, after=len(after)),
            grid_spec=pltpu.PrefetchScalarGridSpec(
                num_scalar_prefetch=1,
                grid=(1,),
                in_specs=in_specs + [ANY] * len(after),
                out_specs=out_specs,
            ),
            out_shape=outs,
            compiler_params=pltpu.CompilerParams(vmem_limit_bytes=VMEM_BYTES),
            cost_estimate=lasting(cost),
            name="merge_grads",
        )(info, *ins, *after)
        for index, (name, parts) in enumerate(targets):
            bit = chains[parts[0]][2]
            hold, give = results[2 * index : 2 * index + 2]
            for part in parts:
                del chains[part]
            chains[name] = (dp_hop(give, 2**bit), hold, bit + 1)

    sums = []
    last = LAYERS - 1
    for layer in reversed(range(LAYERS)):
        first = 2 * layer
        k = kept[layer]
        mod = (mods, (layer,))
        above = layer + 1
        f_name, c_name, a_name, s_name = [f"{kind}{layer}" for kind in "fcas"]
        n_name = f"n{above}"

        def grads_out(members):
            return dict.fromkeys(SIDES, shape(width, members * narrow, dtype=BF))

        older = []
        if layer < last:
            older = [f"f{above}", n_name]
            more = held(*older)
        if layer == last:
            f_send, f_keep, low, c_send, c_keep, g, stats = run(
                lambda info, work, w: hidden_cross_kernel(info, work, w, words),
                "ff_cross_back",
                info,
                dict(
                    x2=k["x2"],
                    branch2=k["branch2"],
                    q=k["cq"],
                    kv=k["ckv"],
                    lse=k["lse2"],
                    entry2=k["entry2"],
                    text=text_rows,
                    mixed=k["mixed2"],
                    x1=k["x1"],
                ),
                dict(mod=mod, up_bias=(up_biases, (layer,)), bias=(out_biases[2], (layer,))),
                weights_of(4) + weights_of(5) + [cotangent] + weights_of(first + 1),
                {f"f_{name}": shape(width, 2 * units, dtype=BF) for name in SIDES}
                | dict(low=frame_low)
                | {f"c_{name}": shape(width, 4 * narrow, dtype=BF) for name in SIDES}
                | dict(out=frame_high),
                dict(stats=stat_shape),
                dict(
                    up=four,
                    down=four,
                    g=floats,
                    g_mid=floats,
                    rows=lows,
                    row_sems=sems(1),
                    gb=lows,
                    entry3=lows,
                    branch3=lows,
                    active=pltpu.VMEM((share, 4 * units), BF),
                    slope=pltpu.VMEM((share, 4 * units), BF),
                    d_before=pltpu.VMEM((share, 4 * units), BF),
                    before=floats,
                    sum=floats,
                    sems=sems(8),
                    down_sems=sems(8),
                    wq=whole,
                    wo=whole,
                    dkv=pltpu.VMEM(two_text.shape, BF),
                    dkv_sum=pltpu.VMEM(two_text.shape, F32),
                    csems=sems(8),
                ),
                last_gate,
                10.0,
            )
            start(f_name, f_send, f_keep)
            start(c_name, c_send, c_keep)
        else:
            part, gb, d_before, stats = run(
                lambda info, work, w: hidden_back_kernel(info, work, w, 0),
                "ff_back",
                info,
                dict(g=g, branch=k["branch3"], slope=k["slope"]),
                dict(mod=mod),
                [hidden_up, sibs[4], hidden_down, sibs[5]],
                dict(part=frame_low, gb=frame_low, d_before=frame_chip),
                dict(stats=stat_shape),
                dict(
                    up=two, down=two, before=floats, de=floats, sems=sems(2), down_sems=sems(2)
                ),
                more,
                5.0,
            )
            other = tensor_hop(part, 2)
            send, keep = run(
                hidden_grads_kernel,
                "ff_grads",
                info,
                dict(entry=k["entry3"], d_before=d_before, gb=gb, active=k["active"]),
                {},
                [],
                dict.fromkeys(SIDES, shape(width, 2 * units, dtype=BF)),
                {},
                {},
                [gb],
                1.0,
            )
            start(f_name, send, keep)
            output = join(low, gb)
            advance(older, held(f_name), 0.5)
            extra = dict(part=part, other=other, above=k["x2"])
            scratch = dict(g_mid=floats)
        if layer < last:
            send, keep, g, stats = run(
                partial(cross_back_kernel, words=words),
                "cross_back",
                info,
                dict(
                    g=g,
                    branch=k["branch2"],
                    q=k["cq"],
                    kv=k["ckv"],
                    lse=k["lse2"],
                    entry=k["entry2"],
                    text=text_rows,
                    mixed=k["mixed2"],
                    x=k["x1"],
                    **extra,
                ),
                dict(mod=mod, early=(stats, ())),
                weights_of(first + 1),
                grads_out(4) | dict(out=frame_high),
                dict(stats=stat_shape),
                dict(
                    wq=whole,
                    wo=whole,
                    gb=lows,
                    dq=lows,
                    dkv=pltpu.VMEM(two_text.shape, BF),
                    d_mixed=lows,
                    de=floats,
                    dkv_sum=pltpu.VMEM(two_text.shape, F32),
                    sems=sems(8),
                    **scratch,
                ),
                held(f_name, *older) + [output],
                60.0,
            )
            start(c_name, send, keep)
            advance([f_name, n_name], [g, chains[f"f{above}"][0]])
        gb1, dq, dkv_own, dkv_give, stats = run(
            self_back_kernel,
            "self_back",
            info,
            dict(
                g=g,
                branch=k["branch1"],
                mixed=k["mixed1"],
                rest=k["rest1"],
                q=k["q"],
                kv_own=k["kv"],
                kv_sib=k["kv_sib"],
                lse=k["lse1"],
            ),
            dict(mod=mod, early=(stats, ())),
            weights_of(first),
            dict(gb=frame_low, dq=frame_low, dkv_own=two_low, dkv_give=two_low),
            dict(stats=stat_shape),
            dict(wo=whole, d_mixed=lows, inner=pltpu.VMEM((16, share), F32), sems=sems(4)),
            held(f_name, c_name, *([n_name] if layer < last else [])),
            13.0,
        )
        dkv_sib = tensor_hop(dkv_give, 1)
        if layer == last:
            advance([f_name], [dq])
        else:
            advance([f_name, c_name], [dq, chains[n_name][0]])
        send, keep = run(
            query_output_kernel,
            "qo_grads",
            info,
            dict(entry=k["entry1"], gb=gb1, dq=dq, mixed=k["mixed1"]),
            {},
            [],
            grads_out(2),
            {},
            {},
            held(f_name, c_name),
            60.0,
        )
        start(a_name, send, keep)
        arriving = dict(dkv_own=dkv_own, dkv_sib=dkv_sib, entry=k["entry1"])
        if layer == 0:
            send, keep, dkv = run(
                kv_grads_kernel,
                "kv_grads",
                info,
                arriving,
                {},
                [],
                grads_out(2) | dict(dkv=two_low),
                {},
                {},
                held(a_name),
                4.0,
            )
            start(s_name, send, keep)
            rest = f"t{layer}"
            advance([f_name, c_name, (rest, [a_name, s_name])], held(s_name))
            arriving = dict(dkv=dkv)
        results = run(
            qkv_back_kernel,
            "qkv_back",
            info,
            arriving | dict(dq=dq, x=k["x"], g=g),
            dict(mod=mod, early=(stats, ())),
            weights_of(first),
            (dict(low=frame_low) if layer == 0 else grads_out(2)) | dict(out=frame_high),
            dict(stats=stat_shape),
            dict(wq=whole, wk=whole, wv=whole, de=floats, sems=sems(12))
            | (dict(dkv=pltpu.VMEM(two_low.shape, BF)) if layer else {}),
            held(f_name, c_name, rest if layer == 0 else a_name),
            6.0,
        )
        g, stats = results[-2:]
        if layer:
            start(s_name, *results[:2])
        if layer:
            advance([f_name, (f"n{layer}", [c_name, a_name, s_name])], [g])
        else:
            to_rest = [g, chains[f_name][0]]
        sums = [stats, tensor_hop(stats, 1)] + sums
    vectors = plain(
        partial(collect_kernel, narrow=narrow, units=units, columns=columns),
        "collect",
        info,
        [*sums, condition],
        [shape(16, mine.shape[2], dtype=BF)],
        [pltpu.VMEM(stat_shape.shape, F32), pltpu.VMEM((16, mine.shape[2]), F32)],
    )
    advance(["c0", "t0"], to_rest + [vectors])
    gathered, hop = vectors[None], size // 2

    def gather_sums():
        nonlocal gathered, hop
        if hop:
            both = jnp.stack([gathered, dp_hop(gathered, hop)], axis=1)
            gathered = both.reshape(-1, *vectors.shape)
            hop //= 2

    low = results[0]
    (low,) = gate([low], held("t0"))
    input_grad = join(low)

    def parts_of(*names):
        return [part.reshape(1, unit, -1) for name in names for part in chains[name][:2]]

    up_grad, down_grad = plain(
        partial(finish_kernel, wide=True, spots=[(0, [(0, 0)]), (0, [(1, 0)])]),
        "wide",
        None,
        parts_of("f0", "f1"),
        [shape(LAYERS, unit, units)] * 2,
    )
    ready = [input_grad, up_grad, chains["c0"][0]]
    while any(2 ** chain[2] < size for chain in chains.values()):
        gather_sums()
        advance(list(chains), held("t0") + [gathered] + ready)
    while hop:
        gather_sums()
    straight, across = shape(LAYERS, unit, narrow), shape(LAYERS, narrow, unit)
    spots = [(0, [(1, 0), (1, 1), (1, 2), (1, 3)])]
    spots += [(0, [(0, 0), (0, 1)]), (0, [(0, 2), (0, 3)])]
    cq_grad, ck_grad, cv_grad, co_grad, q_grad, o_grad, k_grad, v_grad = plain(
        partial(finish_kernel, wide=False, spots=spots),
        "narrow",
        None,
        parts_of("n1", "c0", "t0"),
        [straight, straight, straight, across, straight, across, straight, straight],
    )
    small = plain(
        spread_kernel,
        "spread",
        info,
        [gathered],
        [shape(LAYERS, unit, columns), shape(LAYERS, columns)]
        + [shape(LAYERS, narrow)] * 4
        + [shape(LAYERS, units)]
        + [shape(LAYERS, unit)] * 3,
        [pltpu.VMEM((SLOTS * size, columns), F32), pltpu.VMEM((SLOTS * size, width), F32)],
    )
    mod_grad, mod_bias_grad, q_sum, v_sum, cq_sum, cv_sum, up_sum, o1, o2, o3 = small
    return (
        output,
        input_grad,
        q_grad,
        q_sum,
        k_grad,
        v_grad,
        v_sum,
        o_grad,
        o1,
        cq_grad,
        cq_sum,
        ck_grad,
        cv_grad,
        cv_sum,
        co_grad,
        o2,
        up_grad,
        up_sum,
        turn(down_grad),
        o3,
        mod_grad,
        mod_bias_grad,
    )


def solution(mesh):
    dp, tensor = "dp", "tensor"
    columns, vector = P(None, None, tensor), P(None, tensor)
    matrix, turned, spread = P(None, dp, tensor), P(None, tensor, dp), P(None, dp)
    placed = (
        P(dp, None),
        P(dp, None, None),
        P(dp),
        P(dp),
        P(dp, None),
        columns,
        vector,
        columns,
        columns,
        vector,
        P(None, tensor, None),
        P(),
        columns,
        vector,
        columns,
        columns,
        vector,
        P(None, tensor, None),
        P(),
        columns,
        vector,
        P(None, tensor, None),
        P(),
        columns,
        vector,
    )
    results = (
        P(dp, None),
        P(dp, None),
        matrix,
        vector,
        matrix,
        matrix,
        vector,
        turned,
        spread,
        matrix,
        vector,
        matrix,
        matrix,
        vector,
        turned,
        spread,
        matrix,
        vector,
        turned,
        spread,
        matrix,
        vector,
    )
    return jax.shard_map(
        shards, mesh=mesh, in_specs=placed, out_specs=results, check_vma=False
    )
```

```python
from functools import partial
import math

import jax
import jax.numpy as jnp
from jax import lax
from jax.experimental import pallas as pl
from jax.experimental.pallas import tpu as pltpu
from jax.sharding import PartitionSpec as P

HEAD_WIDTH = 64
UNIT = 256
LAYERS = 2
WINDOW = 1024
EPSILON = 1e-06
LANES = 128
CHUNK = 64
SLOTS = WINDOW // UNIT
FAR = -1e30
SIDES = ("send", "keep")
VMEM_BYTES = 66_000_000
BF = jnp.bfloat16
F32 = jnp.float32
ROOT = math.sqrt(2.0 / math.pi)
CUBIC = 0.044715


def dot_nn(left, right):
    return jnp.dot(left, right, preferred_element_type=F32)


def dot_nt(left, right):
    return lax.dot_general(left, right, (((1,), (1,)), ((), ())), preferred_element_type=F32)


def dot_tn(left, right):
    return lax.dot_general(left, right, (((0,), (0,)), ((), ())), preferred_element_type=F32)


SMALL = pl.BlockSpec(memory_space=pltpu.SMEM)
NEAR = pl.BlockSpec(memory_space=pltpu.VMEM)
ANY = pl.BlockSpec(memory_space=pl.ANY)


class Work:
    def __init__(self, ins, outs, scratch, in_sems, out_sems):
        self.ins, self.outs, self.scratch, self.out_sems = ins, outs, scratch, out_sems
        self.copies, self.waited, self.flushed = {}, set(), []
        for index, (name, (ref, buffer)) in enumerate(ins.items()):
            self.copies[name] = pltpu.make_async_copy(ref, buffer, in_sems.at[index])
            self.copies[name].start()

    def __getattr__(self, name):
        if name in self.__dict__["ins"]:
            return self.ins[name][1]
        if name in self.__dict__["outs"]:
            return self.outs[name][1]
        return self.__dict__["scratch"][name]

    def has(self, name):
        return name in self.outs

    def takes(self, name):
        return name in self.ins

    def send(self, name, source, *at):
        ref = self.outs[name][0]
        copy = pltpu.make_async_copy(
            source, ref.at[at] if at else ref, self.out_sems.at[len(self.flushed)]
        )
        copy.start()
        self.flushed.append(copy)

    def need(self, *names):
        for name in names:
            if name not in self.waited:
                self.waited.add(name)
                self.copies[name].wait()

    def flush(self, name, *at):
        ref, buffer = self.outs[name]
        if at:
            ref, buffer = ref.at[at], buffer.at[at]
        copy = pltpu.make_async_copy(buffer, ref, self.out_sems.at[len(self.flushed)])
        copy.start()
        self.flushed.append(copy)

    def finish(self):
        self.need(*self.ins)
        for copy in self.flushed:
            copy.wait()


class Names:
    def __init__(self, work, **names):
        self.work, self.names = work, names

    def to(self, name):
        return self.__dict__["names"].get(name, name)

    def __getattr__(self, name):
        return getattr(self.__dict__["work"], self.to(name))

    @property
    def outs(self):
        return {name: self.work.outs[self.to(name)] for name in SIDES}

    def has(self, name):
        return self.work.has(self.to(name))

    def takes(self, name):
        return self.work.takes(self.to(name))

    def need(self, *names):
        self.work.need(*[name for name in map(self.to, names) if self.work.takes(name)])

    def flush(self, name, *at):
        if self.has(name):
            self.work.flush(self.to(name), *at)


def run(body, name, info, ins, small, weights, outs, small_outs, scratch, after=(), cost=1.0):
    in_names, out_names, names = list(ins), list(outs), list(scratch)
    small_names, small_out_names = list(small), list(small_outs)
    counts = [1, len(in_names), len(small), len(weights), len(after), len(outs), len(small_outs)]

    def kernel(*refs):
        refs = list(refs)
        parts = []
        for count in counts:
            parts.append(refs[:count])
            refs = refs[count:]
        (info_ref,), in_refs, small_refs, weight_refs, _, out_refs, small_out_refs = parts
        in_bufs, refs = refs[: len(in_names)], refs[len(in_names) :]
        out_bufs, refs = refs[: len(out_names)], refs[len(out_names) :]
        rest, (in_sems, out_sems) = refs[:-2], refs[-2:]
        extra = {}
        rest = list(rest)
        for key in names:
            many = isinstance(scratch[key], list)
            size = len(scratch[key]) if many else 1
            extra[key] = rest[:size] if many else rest[0]
            rest = rest[size:]
        for key, ref in zip(small_names, small_refs):
            index = small[key][1]
            extra[key] = ref.at[index] if index else ref
        extra.update(zip(small_out_names, small_out_refs))
        work = Work(
            dict(zip(in_names, zip(in_refs, in_bufs))),
            dict(zip(out_names, zip(out_refs, out_bufs))),
            extra,
            in_sems,
            out_sems,
        )
        body(info_ref, work, weight_refs)
        work.finish()

    buffer = lambda a: pltpu.VMEM(a.shape, a.dtype)
    flat = []
    for value in scratch.values():
        flat += value if isinstance(value, list) else [value]
    results = pl.pallas_call(
        kernel,
        out_shape=[outs[n] for n in out_names] + [small_outs[n] for n in small_out_names],
        in_specs=[SMALL]
        + [ANY] * len(ins)
        + [NEAR] * len(small)
        + [ANY] * (len(weights) + len(after)),
        out_specs=[ANY] * len(outs) + [NEAR] * len(small_outs),
        scratch_shapes=[buffer(ins[n]) for n in in_names]
        + [buffer(outs[n]) for n in out_names]
        + flat
        + [pltpu.SemaphoreType.DMA((max(len(ins), 1),)), pltpu.SemaphoreType.DMA((32,))],
        compiler_params=pltpu.CompilerParams(vmem_limit_bytes=VMEM_BYTES),
        cost_estimate=lasting(cost),
        name=name,
    )(info, *ins.values(), *[array for array, _ in small.values()], *weights, *after)
    return results


def plain(body, name, info, ins, outs, scratch=(), after=()):
    first = len(ins) + (0 if info is None else 1)
    results = pl.pallas_call(
        lambda *refs: body(*refs[:first], *refs[first + len(after) :]),
        out_shape=outs,
        in_specs=([] if info is None else [SMALL]) + [NEAR] * len(ins) + [ANY] * len(after),
        out_specs=[NEAR] * len(outs),
        scratch_shapes=list(scratch),
        compiler_params=pltpu.CompilerParams(vmem_limit_bytes=VMEM_BYTES),
        cost_estimate=lasting(0.05),
        name=name,
    )(*([] if info is None else [info]), *ins, *after)
    return results if len(outs) > 1 else results[0]


def lasting(units):
    return pl.CostEstimate(flops=int(units * 0.4e9), bytes_accessed=1000, transcendentals=0)


def shape(*dims, dtype=F32):
    return jax.ShapeDtypeStruct(dims, dtype)


def start_rows(refs, place, plan, sems):
    own, sib, xa, ya, xb, yb = refs
    half = own.shape[0] // 2
    for rank in range(4):
        for parity in range(2):

            @pl.when(place == rank * 2 + parity)
            def _(rank=rank, parity=parity):
                for index, (shard, row, rows, dst) in enumerate(plan):
                    step = shard ^ rank
                    if step < 2:
                        src = (own, sib)[step].at[pl.ds(row, rows)]
                    else:
                        first, second = ((xa, ya), (xb, yb))[step - 2]
                        part = row // half
                        src = (first if part == parity else second).at[pl.ds(row - part * half, rows)]
                    pltpu.make_async_copy(src, dst, sems.at[index]).start()


def wait_rows(refs, plan, sems, which):
    for index in which:
        _, row, rows, dst = plan[index]
        pltpu.make_async_copy(refs[0].at[pl.ds(0, rows)], dst, sems.at[index]).wait()


def plan_of(buffers, first, rows):
    return [
        (shard, (first + which) * rows, rows, dst.at[pl.ds(shard * rows, rows)])
        for which, dst in enumerate(buffers)
        for shard in range(4)
    ]


def norm_rows(values):
    mean = jnp.mean(values, axis=-1, keepdims=True)
    center = values - mean
    factor = lax.rsqrt(jnp.mean(center * center, axis=-1, keepdims=True) + EPSILON)
    return center * factor, factor


def piece(mod, slot, index):
    width = mod.shape[1] // 9
    return mod[pl.ds(slot, 1), index * width : (index + 1) * width]


def entry_rows(x, mod, info, index, out):
    for block in range(x.shape[0] // UNIT):
        slot = info[1 + block]
        shift = piece(mod, slot, index)
        scale = 1.0 + piece(mod, slot, index + 1)

        def step(turn, carry):
            rows = pl.ds(pl.multiple_of(block * UNIT + turn * CHUNK, CHUNK), CHUNK)
            normed, _ = norm_rows(x[rows, :])
            out[rows, :] = (normed * scale + shift).astype(BF)
            return carry

        lax.fori_loop(0, UNIT // CHUNK, step, 0, unroll=True)


def residual_rows(x, mod, info, index, branch, branch_out, out, low=None):
    for block in range(x.shape[0] // UNIT):
        gate = piece(mod, info[1 + block], index)

        def step(turn, carry):
            rows = pl.ds(pl.multiple_of(block * UNIT + turn * CHUNK, CHUNK), CHUNK)
            values = branch[rows, :]
            branch_out[rows, :] = values.astype(BF)
            result = x[rows, :] + gate * values
            out[rows, :] = result
            if low is not None:
                low[rows, :] = result.astype(BF)
            return carry

        lax.fori_loop(0, UNIT // CHUNK, step, 0, unroll=True)


def fold(values):
    return jnp.sum(values.reshape(values.shape[0] // 8, 8, values.shape[1]), axis=0)


def total(values):
    return jnp.sum(values, axis=0, keepdims=True)


def gate_back(g, mod, info, index, branch, gb, stats):
    width = g.shape[1]
    sums = jnp.zeros((8, width), F32)
    for block in range(g.shape[0] // UNIT):
        slot = info[1 + block]
        gate = piece(mod, slot, index)

        def step(turn, carry):
            rows = pl.ds(pl.multiple_of(block * UNIT + turn * CHUNK, CHUNK), CHUNK)
            grad = g[rows, :]
            low = (gate * grad).astype(BF)
            gb[rows, :] = low
            return (
                carry[0] + fold(low.astype(F32)),
                carry[1] + fold(grad * branch[rows, :].astype(F32)),
            )

        sums, rows_sum = lax.fori_loop(
            0, UNIT // CHUNK, step, (sums, jnp.zeros((8, width), F32)), unroll=True
        )
        stats[pl.ds(8 + slot, 1), :] += total(rows_sum)
    stats[12:13, :] = total(sums)


def norm_back_rows(x, g, de, mod, info, index, out, stats, low=None):
    width = x.shape[1]
    for block in range(x.shape[0] // UNIT):
        slot = info[1 + block]
        scale = 1.0 + piece(mod, slot, index + 1)

        def step(turn, carry):
            rows = pl.ds(pl.multiple_of(block * UNIT + turn * CHUNK, CHUNK), CHUNK)
            normed, factor = norm_rows(x[rows, :])
            grad = de[rows, :]
            inner = grad * normed
            dn = grad * scale
            mean = jnp.mean(dn, axis=-1, keepdims=True)
            along = jnp.mean(dn * normed, axis=-1, keepdims=True)
            result = g[rows, :] + factor * (dn - mean - normed * along)
            out[rows, :] = result
            if low is not None:
                low[rows, :] = result.astype(BF)
            return (carry[0] + fold(grad), carry[1] + fold(inner))

        zero = jnp.zeros((8, width), F32)
        shift_sum, scale_sum = lax.fori_loop(0, UNIT // CHUNK, step, (zero, zero), unroll=True)
        stats[pl.ds(slot, 1), :] += total(shift_sum)
        stats[pl.ds(4 + slot, 1), :] += total(scale_sum)


def lane_ids(rows):
    return lax.broadcasted_iota(jnp.int32, (rows, LANES), 1)


def head_half(values, half):
    ids = lane_ids(values.shape[0])
    keep = ids < HEAD_WIDTH if half == 0 else ids >= HEAD_WIDTH
    return jnp.where(keep, values.astype(F32), 0.0)


def turned_halves(keys):
    turned = keys.T
    low = lax.broadcasted_iota(jnp.int32, turned.shape, 0) < HEAD_WIDTH
    zero = jnp.zeros(turned.shape, turned.dtype)
    return jnp.concatenate([jnp.where(low, turned, zero), jnp.where(low, zero, turned)], axis=1)


def query_marks(slot):
    return jnp.where(lane_ids(UNIT) == slot, 1.0, 0.0).astype(BF)


def key_marks(slots):
    ids = lane_ids(UNIT)
    parts = [jnp.where((ids < SLOTS) & (ids != slot), FAR, 0.0).astype(BF) for slot in slots]
    return jnp.concatenate(parts, axis=0)


def pair_lanes(pair):
    return pl.ds(pl.multiple_of(pair * LANES, LANES), LANES)


def start_own_rows(info, work, whole):
    share = work.rows.shape[0]
    first = pl.multiple_of((info[5] % 2) * share, share)
    copy = pltpu.make_async_copy(whole.at[pl.ds(first, share)], work.rows, work.row_sems.at[0])
    copy.start()
    return copy


def raise_rows(low, out):
    for row in range(0, low.shape[0], CHUNK):
        span = pl.ds(row, CHUNK)
        out[span, :] = low[span, :].astype(F32)


def kv_kernel(info, work, weights):
    rows = weights[0].shape[0] // 4
    plan = plan_of((work.w.at[0], work.w.at[1]), 1, rows)
    start_rows(weights[:6], info[0], plan, work.sems)
    if work.has("branch"):
        work.need("part", "other", "below")
        bias = work.bias[...].astype(F32)
        for row in range(0, work.sum.shape[0], CHUNK):
            span = pl.ds(row, CHUNK)
            work.sum[span, :] = (
                work.part[span, :].astype(F32) + work.other[span, :].astype(F32) + bias
            )
        residual_rows(work.below, work.mod_below, info, 8, work.sum, work.branch, work.x)
        work.flush("branch")
        work.flush("x")
    else:
        start_own_rows(info, work, weights[6]).wait()
        raise_rows(work.rows, work.x)
        work.flush("x")
    entry_rows(work.x, work.mod, info, 0, work.entry)
    work.flush("entry")
    entry = work.entry[...]
    wait_rows(weights, plan, work.sems, range(4))
    work.kv[0] = dot_nt(entry, work.w[0]).astype(BF)
    work.flush("kv", 0)
    wait_rows(weights, plan, work.sems, range(4, 8))
    work.kv[1] = (dot_nt(entry, work.w[1]) + work.biases[2:3, :]).astype(BF)
    work.flush("kv", 1)


def q_kernel(info, work, weights):
    rows = weights[0].shape[0] // 4
    plan = plan_of((work.w,), 0, rows)
    start_rows(weights, info[0], plan, work.sems)
    work.need("entry")
    wait_rows(weights, plan, work.sems, range(4))
    work.q[...] = (dot_nt(work.entry[...], work.w[...]) + work.biases[0:1, :]).astype(BF)
    work.flush("q")


def soft_pair(work, q_pair, keys, values, marks, logs, pair, span, words=None):
    ids = lane_ids(UNIT)
    results = []
    kept = logs[span, :]
    for half in range(2):
        left = (head_half(q_pair, half) * HEAD_WIDTH**-0.5).astype(BF)
        if marks is not None:
            left = jnp.concatenate([left, marks], axis=1)
        scores = dot_nt(left, keys)
        if words is not None:
            scores = jnp.where(ids < words, scores, FAR)
        peak = jnp.max(scores, axis=-1, keepdims=True)
        both = dot_nn(jnp.exp(scores - peak).astype(BF), values)
        sums = both[:, LANES:]
        results.append(both[:, :LANES] / sums)
        kept = jnp.where(ids == 2 * pair + half, peak + jnp.log(sums), kept)
    logs[span, :] = kept
    return jnp.where(ids < HEAD_WIDTH, results[0], results[1])


def self_kernel(info, work, weights):
    rows = weights[0].shape[0] // 4
    sems = work.sems
    plan = [(s, 3 * rows, rows, work.wo.at[pl.ds(s * rows, rows)]) for s in range(4)]
    start_rows(weights, info[0], plan, sems)
    share = work.x.shape[0]
    blocks = share // UNIT
    marks = key_marks([info[1 + b] for b in range(2 * blocks)])
    ones = jnp.ones((2 * share, LANES), BF)
    logs, mixed = work.logs, work.mixed
    logs[...] = jnp.zeros(logs.shape, F32)
    work.need("q", "kv_own", "kv_sib")

    def both(which, lanes):
        return jnp.concatenate([work.kv_own[which, :, lanes], work.kv_sib[which, :, lanes]], axis=0)

    def step(pair, carry):
        lanes = pair_lanes(pair)
        keys = jnp.concatenate([both(0, lanes), marks], axis=1)
        values = jnp.concatenate([both(1, lanes), ones], axis=1)
        for block in range(blocks):
            span = pl.ds(block * UNIT, UNIT)
            values_mixed = soft_pair(
                work,
                work.q[span, lanes],
                keys,
                values,
                query_marks(info[1 + block]),
                logs,
                pair,
                span,
            )
            low = values_mixed.astype(BF)
            mixed[span, lanes] = low
            work.rest[span, lanes] = (values_mixed - low.astype(F32)).astype(BF)
        return carry

    lax.fori_loop(0, mixed.shape[1] // LANES, step, 0)
    work.flush("mixed")
    work.flush("rest")
    work.lse[...] = logs[...].T[: work.lse.shape[0], :]
    work.flush("lse")
    wait_rows(weights, plan, sems, range(4))
    work.sum[...] = dot_nn(mixed[...], work.wo[...]) + work.bias[...].astype(F32)
    work.need("x")
    residual_rows(work.x, work.mod, info, 2, work.sum, work.branch, work.out)
    work.flush("branch")
    work.flush("out")


def cross_kernel(info, work, weights, words):
    rows = weights[0].shape[0] // 4
    sems = work.sems
    order = (1, 2, 0, 3)
    plan = [
        (shard, order[i // 4] * rows, count, dst)
        for i, (shard, _, count, dst) in enumerate(
            plan_of((work.wk, work.wv, work.wq, work.wo), 0, rows)
        )
    ]
    start_rows(weights, info[0], plan, sems)
    work.need("x")
    entry_rows(work.x, work.mod, info, 3, work.entry)
    work.flush("entry")
    work.need("text")
    wait_rows(weights, plan, sems, range(0, 4))
    work.kv[0] = dot_nt(work.text[...], work.wk[...]).astype(BF)
    wait_rows(weights, plan, sems, range(4, 8))
    work.kv[1] = (dot_nt(work.text[...], work.wv[...]) + work.biases[5:6, :]).astype(BF)
    work.flush("kv")
    wait_rows(weights, plan, sems, range(8, 12))
    work.q[...] = (dot_nt(work.entry[...], work.wq[...]) + work.biases[3:4, :]).astype(BF)
    work.flush("q")
    ones = jnp.ones((LANES, LANES), BF)
    logs, mixed = work.logs, work.mixed
    logs[...] = jnp.zeros(logs.shape, F32)

    def step(pair, carry):
        lanes = pair_lanes(pair)
        for block in range(mixed.shape[0] // UNIT):
            span = pl.ds(block * UNIT, UNIT)
            own = pl.ds(pl.multiple_of(info[1 + block] * LANES, LANES), LANES)
            mixed[span, lanes] = soft_pair(
                work,
                work.q[span, lanes],
                work.kv[0, own, lanes],
                jnp.concatenate([work.kv[1, own, lanes], ones], axis=1),
                None,
                logs,
                pair,
                span,
                words,
            ).astype(BF)
        return carry

    lax.fori_loop(0, mixed.shape[1] // LANES, step, 0, unroll=2)
    work.flush("mixed")
    work.lse[...] = logs[...].T[: work.lse.shape[0], :]
    work.flush("lse")
    wait_rows(weights, plan, sems, range(12, 16))
    work.sum[...] = dot_nn(mixed[...], work.wo[...]) + work.bias[...].astype(F32)
    residual_rows(work.x, work.mod, info, 5, work.sum, work.branch, work.out)
    work.flush("branch")
    work.flush("out")


def hidden_plan(refs, buffer):
    rows = buffer.shape[1]
    half = rows // 2
    return [
        (shard, row, half, buffer.at[shard, pl.ds(row, half)])
        for shard in range(4)
        for row in range(0, rows, half)
    ]


def start_chip(info, refs, layer, buffer, sems):
    copies = [
        pltpu.make_async_copy(ref.at[layer], buffer.at[(info[5] + i) % 2], sems.at[i])
        for i, ref in enumerate(refs)
    ]
    for copy in copies:
        copy.start()
    return copies


def bend_rows(before, bias, active, slope, lanes):
    for row in range(0, before.shape[0], CHUNK):
        span = pl.ds(row, CHUNK)
        values = before[span, :] + bias
        square = values * values
        half = 1.0 / (1.0 + jnp.exp(values * (-2.0 * ROOT - (2.0 * ROOT * CUBIC) * square)))
        act = values * half
        active[span, lanes] = act.astype(BF)
        slope[span, lanes] = (
            half + act * (1.0 - half) * (2.0 * ROOT + (6.0 * ROOT * CUBIC) * square)
        ).astype(BF)


def columns_of(shard, width):
    return pl.ds(pl.multiple_of(shard * width, width), width)


def start_hidden(info, work, weights, layer):
    if len(weights) == 4:
        ups = start_chip(info, weights[:2], layer, work.up, work.sems)
        downs = start_chip(info, weights[2:], layer, work.down, work.down_sems)
        return [lambda some=some: [copy.wait() for copy in some] for some in (ups, downs)]
    waits = []
    for refs, buffer, sems in (
        (weights[:6], work.up, work.sems),
        (weights[6:12], work.down, work.down_sems),
    ):
        refs = [ref.at[layer] for ref in refs[:2]] + list(refs[2:])
        plan = hidden_plan(refs, buffer)
        start_rows(refs, info[0], plan, sems)
        waits.append(
            lambda refs=refs, plan=plan, sems=sems: wait_rows(refs, plan, sems, range(len(plan)))
        )
    return waits


def hidden_kernel(info, work, weights, layer):
    waits = start_hidden(info, work, weights, layer)
    width = work.x.shape[1]
    shards = work.up.shape[0]
    first = info[6] * 2
    work.need("x")
    entry_rows(work.x, work.mod, info, 6, work.entry)
    work.flush("entry")
    for wait in waits:
        wait()
    work.sum[...] = jnp.zeros(work.sum.shape, F32)

    def step(shard, carry):
        lanes = columns_of(shard, width)
        bias = work.up_bias[:, columns_of(first + shard, width)]
        work.before[...] = dot_nn(work.entry[...], work.up[shard])
        bend_rows(work.before, bias, work.active, work.slope, lanes)
        work.sum[...] += dot_nn(work.active[:, lanes], work.down[shard])
        return carry

    lax.fori_loop(0, shards, step, 0)
    work.flush("active")
    work.flush("slope")
    work.part[...] = work.sum[...].astype(BF)
    work.flush("part")


def hidden_back_kernel(info, work, weights, layer):
    waits = start_hidden(info, work, weights, layer)
    work.stats[...] = jnp.zeros(work.stats.shape, F32)
    stats = work.stats.at[pl.ds(48, 24)]
    work.need("g", "branch")
    gate_back(work.g, work.mod, info, 8, work.branch, work.gb, stats)
    work.need("slope")
    for wait in waits:
        wait()
    hidden_back_rows(info, work, work.de, stats)
    work.part[...] = work.de[...].astype(BF)
    work.flush("part")
    work.flush("gb")
    work.flush("d_before")


def hidden_back_rows(info, work, de, stats):
    width = work.g.shape[1]
    shards = work.up.shape[0]
    first = info[6] * 2 if shards == 2 else 0
    de[...] = jnp.zeros(de.shape, F32)

    def step(shard, carry):
        lanes = columns_of(shard, width)
        work.before[...] = dot_nt(work.gb[...], work.down[shard])
        sums = jnp.zeros((8, width), F32)
        for row in range(0, work.g.shape[0], CHUNK):
            span = pl.ds(row, CHUNK)
            low = (work.before[span, :] * work.slope[span, lanes].astype(F32)).astype(BF)
            work.d_before[span, lanes] = low
            sums += fold(low.astype(F32))
        stats[pl.ds(13 + first + shard, 1), :] = total(sums)
        de[...] += dot_nt(work.d_before[:, lanes], work.up[shard])
        return carry

    lax.fori_loop(0, shards, step, 0)


def hidden_both_kernel(info, work, weights, layer):
    copy = start_own_rows(info, work, weights[12])
    waits = start_hidden(info, work, weights, layer)
    width = work.x.shape[1]
    work.need("x")
    entry_rows(work.x, work.mod, info, 6, work.entry)
    for wait in waits:
        wait()
    work.sum[...] = jnp.zeros(work.sum.shape, F32) + work.bias[...].astype(F32)

    def step(shard, carry):
        lanes = columns_of(shard, width)
        work.before[...] = dot_nn(work.entry[...], work.up[shard])
        bend_rows(work.before, work.up_bias[:, lanes], work.active, work.slope, lanes)
        work.sum[...] += dot_nn(work.active[:, lanes], work.down[shard])
        return carry

    lax.fori_loop(0, 4, step, 0)
    residual_rows(work.x, work.mod, info, 8, work.sum, work.branch, work.out, work.low)
    work.flush("low")
    work.stats[...] = jnp.zeros(work.stats.shape, F32)
    stats = work.stats.at[pl.ds(48, 24)]
    copy.wait()
    raise_rows(work.rows, work.g)
    gate_back(work.g, work.mod, info, 8, work.branch, work.gb, stats)
    hidden_back_rows(info, work, work.sum, stats)
    left, right = work.entry[...].T, work.gb[...].T
    for name, rank in zip(SIDES, (info[7], info[5])):
        out = work.outs[name][1]
        lanes = columns_of(rank, width)
        out[:, :width] = dot_nn(left, work.d_before[:, lanes]).astype(BF)
        out[:, width:] = dot_nn(right, work.active[:, lanes]).astype(BF)
        work.flush(name)
    norm_back_rows(work.x, work.g, work.sum, work.mod, info, 6, work.out, stats)
    work.flush("out")


def hidden_cross_kernel(info, work, weights, words):
    hidden_both_kernel(
        info,
        Names(
            work,
            x="x2",
            entry="entry3",
            branch="branch3",
            out="g_mid",
            send="f_send",
            keep="f_keep",
        ),
        weights[:13],
        1,
    )
    cross_back_kernel(
        info,
        Names(
            work,
            early="stats",
            g="g_mid",
            branch="branch2",
            entry="entry2",
            x="x1",
            de="sum",
            dq="entry3",
            d_mixed="rows",
            sems="csems",
            send="c_send",
            keep="c_keep",
        ),
        weights[13:],
        words,
    )


def attention_kernel(info, work, weights, words):
    self_kernel(
        info,
        Names(work, out="x1", mixed="mixed1", lse="lse1", branch="branch1", bias="self_bias"),
        weights[:6],
    )
    cross_kernel(
        info,
        Names(
            work,
            x="x1",
            q="cq",
            kv="ckv",
            mixed="mixed2",
            lse="lse2",
            branch="branch2",
            bias="cross_bias",
            wo="cross_wo",
            sems="csems",
        ),
        weights[6:],
        words,
    )


def hidden_grads_kernel(info, work, weights):
    width = work.entry.shape[1]
    work.need("entry", "d_before", "gb", "active")
    left, right = work.entry[...].T, work.gb[...].T
    for name, shift in zip(SIDES, (1, 0)):
        out = work.outs[name][1]
        lanes = columns_of((info[5] + shift) % 2, width)
        out[:, :width] = dot_nn(left, work.d_before[:, lanes]).astype(BF)
        out[:, width:] = dot_nn(right, work.active[:, lanes]).astype(BF)
        work.flush(name)


def pair_grads(info, work, members):
    rows = members[0][0].shape[0]
    low = lane_ids(rows) < HEAD_WIDTH
    step = 3 * LANES
    for at in range(len(members) // 2):
        products = [dot_nn(left, right) for left, right in members[2 * at : 2 * at + 2]]
        (a0, a1, a2), (b0, b1, b2) = [
            [p[:, i * LANES : (i + 1) * LANES] for i in range(3)] for p in products
        ]
        even = (a0, b0, jnp.where(low, a1, pltpu.roll(b1, HEAD_WIDTH, 1)))
        a1, b1 = pltpu.roll(a1, HEAD_WIDTH, 1), pltpu.roll(b1, HEAD_WIDTH, 1)
        a2r, b2r = pltpu.roll(a2, HEAD_WIDTH, 1), pltpu.roll(b2, HEAD_WIDTH, 1)
        odd = (jnp.where(low, a1, a2r), jnp.where(low, b1, b2r), jnp.where(low, a2r, b2))
        first = info[5] % 2 == 0
        for i, (mine, other) in enumerate(zip(even, odd)):
            lanes = pl.ds(at * step + i * LANES, LANES)
            work.outs["keep"][1][:, lanes] = jnp.where(first, mine, other).astype(BF)
            work.outs["send"][1][:, lanes] = jnp.where(first, other, mine).astype(BF)
    work.flush("send")
    work.flush("keep")


def chip_lanes(info, width):
    return pl.ds(pl.multiple_of(info[6] * (width // 2), width // 2), width // 2)


def query_output_kernel(info, work, weights):
    work.need("entry", "gb", "dq", "mixed")
    lanes = chip_lanes(info, work.dq.shape[1])
    pair_grads(
        info,
        work,
        [
            (work.entry[...].T, work.dq[:, lanes]),
            (work.gb[...].T, work.mixed[:, lanes]),
        ],
    )


def cross_back_kernel(info, work, weights, words):
    rows = weights[0].shape[0] // 4
    sems = work.sems
    plan = [
        (shard, (3 * rows, 0)[i // 4], count, dst)
        for i, (shard, _, count, dst) in enumerate(plan_of((work.wo, work.wq), 0, rows))
    ]
    start_rows(weights, info[0], plan, sems)
    work.stats[...] = work.early[...]
    stats = work.stats.at[pl.ds(24, 24)]
    g = work.g
    work.need("g")
    if work.takes("part"):
        work.need("part", "other", "above")
        for row in range(0, g.shape[0], CHUNK):
            span = pl.ds(row, CHUNK)
            work.de[span, :] = work.part[span, :].astype(F32) + work.other[span, :].astype(F32)
        g = work.g_mid
        norm_back_rows(
            work.above, work.g, work.de, work.mod, info, 6, g, work.stats.at[pl.ds(48, 24)]
        )
    work.need("branch")
    gate_back(g, work.mod, info, 5, work.branch, work.gb, stats)
    wait_rows(weights, plan, sems, range(0, 4))
    work.d_mixed[...] = dot_nt(work.gb[...], work.wo[...]).astype(BF)
    work.dkv_sum[...] = jnp.zeros(work.dkv_sum.shape, F32)
    real = lax.broadcasted_iota(jnp.int32, (LANES, UNIT), 0) < words
    work.need("q", "kv", "lse")

    def step(pair, carry):
        lanes = pair_lanes(pair)
        for block in range(work.q.shape[0] // UNIT):
            span = pl.ds(block * UNIT, UNIT)
            own = pl.ds(pl.multiple_of(info[1 + block] * LANES, LANES), LANES)
            q_pair = work.q[span, lanes]
            d_pair = work.d_mixed[span, lanes]
            keys = work.kv[0, own, lanes]
            values = work.kv[1, own, lanes]
            lefts, grads, probs_low, scores_low = [], [], [], []
            for half in range(2):
                left = (head_half(q_pair, half) * HEAD_WIDTH**-0.5).astype(BF)
                grad = head_half(d_pair, half).astype(BF)
                logs = work.lse[pl.ds(2 * pair + half, 1), span]
                probs = jnp.where(real, jnp.exp(dot_nt(keys, left) - logs), 0.0)
                d_probs = dot_nt(values, grad)
                inner = jnp.sum(probs * d_probs, axis=0, keepdims=True)
                lefts.append(left)
                grads.append(grad)
                probs_low.append(probs.astype(BF))
                scores_low.append((probs * (d_probs - inner)).astype(BF))
            wide_scores = jnp.concatenate(scores_low, axis=1)
            grad_v = dot_nn(jnp.concatenate(probs_low, axis=1), jnp.concatenate(grads, axis=0))
            grad_k = dot_nn(wide_scores, jnp.concatenate(lefts, axis=0))
            grad_q = dot_nn(turned_halves(keys), jnp.concatenate(scores_low, axis=0))
            work.dq[span, lanes] = (grad_q.T * HEAD_WIDTH**-0.5).astype(BF)
            work.dkv_sum[0, own, lanes] += grad_k
            work.dkv_sum[1, own, lanes] += grad_v
        return carry

    lax.fori_loop(0, work.q.shape[1] // LANES, step, 0, unroll=2)
    work.dkv[...] = work.dkv_sum[...].astype(BF)
    work.need("entry", "text", "mixed")
    lanes = chip_lanes(info, work.dq.shape[1])
    text = work.text[...].T
    pair_grads(
        info,
        work,
        [
            (work.entry[...].T, work.dq[:, lanes]),
            (text, work.dkv[0, :, lanes]),
            (text, work.dkv[1, :, lanes]),
            (work.gb[...].T, work.mixed[:, lanes]),
        ],
    )
    stats[13:14, :] = total(fold(work.dq[...].astype(F32)))
    stats[14:15, :] = total(fold(work.dkv[1].astype(F32)))
    wait_rows(weights, plan, sems, range(4, 8))
    work.de[...] = dot_nn(work.dq[...], work.wq[...])
    work.need("x")
    norm_back_rows(work.x, g, work.de, work.mod, info, 3, work.out, stats)
    work.flush("out")


def self_back_kernel(info, work, weights):
    rows = weights[0].shape[0] // 4
    sems = work.sems
    plan = [(s, 3 * rows, rows, work.wo.at[pl.ds(s * rows, rows)]) for s in range(4)]
    start_rows(weights, info[0], plan, sems)
    work.stats[...] = work.early[...]
    stats = work.stats.at[pl.ds(0, 24)]
    work.need("g", "branch")
    gate_back(work.g, work.mod, info, 2, work.branch, work.gb, stats)
    work.flush("gb")
    share = work.g.shape[0]
    blocks = share // UNIT
    marks = key_marks([info[1 + b] for b in range(2 * blocks)])
    wait_rows(weights, plan, sems, range(4))
    work.d_mixed[...] = dot_nt(work.gb[...], work.wo[...]).astype(BF)
    work.need("mixed", "rest", "q", "kv_own", "kv_sib", "lse")
    width = work.q.shape[1]
    head = lax.broadcasted_iota(jnp.int32, (16, width), 0)
    lane = lax.broadcasted_iota(jnp.int32, (16, width), 1)
    first = head * HEAD_WIDTH
    pick = jnp.where((lane >= first) & (lane < first + HEAD_WIDTH), 1.0, 0.0)
    for block in range(blocks):
        span = pl.ds(block * UNIT, UNIT)
        whole = work.mixed[span, :].astype(F32) + work.rest[span, :].astype(F32)
        work.inner[:, span] = lax.dot_general(
            pick,
            whole * work.d_mixed[span, :].astype(F32),
            (((1,), (1,)), ((), ())),
            precision=lax.Precision.HIGHEST,
            preferred_element_type=F32,
        )

    def both(which, lanes):
        return jnp.concatenate([work.kv_own[which, :, lanes], work.kv_sib[which, :, lanes]], axis=0)

    def step(pair, carry):
        lanes = pair_lanes(pair)
        keys = both(0, lanes)
        values = both(1, lanes)
        marked = jnp.concatenate([keys, marks], axis=1)
        turned = turned_halves(keys)
        lefts, grads, probs_low, scores_low = [], [], [], []
        for block in range(blocks):
            span = pl.ds(block * UNIT, UNIT)
            q_pair = work.q[span, lanes]
            d_pair = work.d_mixed[span, lanes]
            ends = query_marks(info[1 + block])
            for half in range(2):
                left = (head_half(q_pair, half) * HEAD_WIDTH**-0.5).astype(BF)
                grad = head_half(d_pair, half).astype(BF)
                logs = work.lse[pl.ds(2 * pair + half, 1), span]
                probs = jnp.exp(dot_nt(marked, jnp.concatenate([left, ends], axis=1)) - logs)
                d_probs = dot_nt(values, grad)
                inner = work.inner[pl.ds(2 * pair + half, 1), span]
                lefts.append(left)
                grads.append(grad)
                probs_low.append(probs.astype(BF))
                scores_low.append((probs * (d_probs - inner)).astype(BF))
            grad_q = dot_nn(turned, jnp.concatenate(scores_low[-2:], axis=0))
            work.dq[span, lanes] = (grad_q.T * HEAD_WIDTH**-0.5).astype(BF)
        grad_v = dot_nn(jnp.concatenate(probs_low, axis=1), jnp.concatenate(grads, axis=0))
        grad_k = dot_nn(jnp.concatenate(scores_low, axis=1), jnp.concatenate(lefts, axis=0))
        for which, grad in ((0, grad_k.astype(BF)), (1, grad_v.astype(BF))):
            work.dkv_own[which, :, lanes] = grad[:share]
            work.dkv_give[which, :, lanes] = grad[share:]
        return carry

    lax.fori_loop(0, work.q.shape[1] // LANES, step, 0)
    work.flush("dkv_give")
    work.flush("dkv_own")
    work.flush("dq")


def sum_keys_values(info, work, dkv):
    work.need("dkv_own", "dkv_sib")
    for which in range(2):
        dkv[which] = (
            work.dkv_own[which].astype(F32) + work.dkv_sib[which].astype(F32)
        ).astype(BF)
    work.need("entry")
    lanes = chip_lanes(info, dkv.shape[2])
    entry = work.entry[...].T
    pair_grads(info, work, [(entry, dkv[0, :, lanes]), (entry, dkv[1, :, lanes])])


def kv_grads_kernel(info, work, weights):
    sum_keys_values(info, work, work.dkv)
    work.flush("dkv")


def qkv_back_kernel(info, work, weights):
    rows = weights[0].shape[0] // 4
    sems = work.sems
    plan = plan_of((work.wq, work.wk, work.wv), 0, rows)
    start_rows(weights, info[0], plan, sems)
    work.stats[...] = work.early[...]
    stats = work.stats.at[pl.ds(0, 24)]
    if work.has("send"):
        sum_keys_values(info, work, work.dkv)
    else:
        work.need("dkv")
    work.need("dq")
    stats[13:14, :] = total(fold(work.dq[...].astype(F32)))
    stats[14:15, :] = total(fold(work.dkv[1].astype(F32)))
    wait_rows(weights, plan, sems, range(0, 12))
    work.de[...] = (
        dot_nn(work.dq[...], work.wq[...])
        + dot_nn(work.dkv[0], work.wk[...])
        + dot_nn(work.dkv[1], work.wv[...])
    )
    work.need("x", "g")
    low = work.low if work.has("low") else None
    norm_back_rows(work.x, work.g, work.de, work.mod, info, 0, work.out, stats, low)
    work.flush("out")
    if low is not None:
        work.flush("low")


def merge_kernel(info, *refs, spots, after):
    chains = len(spots)
    ins, outs = refs[: 4 * chains], refs[4 * chains + after :]
    for chain, (result, column) in enumerate(spots):
        for side in range(2):
            received, kept = ins[4 * chain + 2 * side], ins[4 * chain + 2 * side + 1]
            out = outs[2 * result + side]
            lanes = pl.ds(column, received.shape[2])
            out[:, :, lanes] = (received[...].astype(F32) + kept[...].astype(F32)).astype(BF)


def gate(arrays, after):
    count = len(arrays)
    return pl.pallas_call(
        lambda *refs: None,
        out_shape=[shape(*a.shape, dtype=a.dtype) for a in arrays],
        in_specs=[ANY] * (count + len(after)),
        out_specs=[ANY] * count,
        input_output_aliases={i: i for i in range(count)},
        cost_estimate=lasting(0.5),
        name="gate",
    )(*arrays, *after)


def pack_kernel(info, *refs, groups, whole, after):
    count = sum(len(members) for _, members in groups)
    sources, rest = refs[:count], refs[count + after :]
    (in_sems, out_sems), rest = rest[-2:], rest[:-2]
    count = len(groups) + sum(whole)
    outs, held = list(rest[:count]), rest[count:]
    owns = [outs.pop(0) if one else None for one in whole]
    spots = []
    at = 0
    for index, (layer, members) in enumerate(groups):
        rows = held[index].shape[0]
        piece_rows = rows // 4
        for quarter in range(4):
            row = quarter * piece_rows
            source = sources[at + quarter * len(members) // 4]
            src = source.at[layer, pl.ds(row % source.shape[1], piece_rows)]
            spots.append((index, quarter, held[index].at[pl.ds(row, piece_rows)], src))
        at += len(members)

    def arriving(place):
        _, _, spot, src = spots[place]
        return pltpu.make_async_copy(src, spot, in_sems.at[place])

    def leaving(index, which):
        if which == 2:
            return pltpu.make_async_copy(held[index], owns[index], out_sems.at[2 * index])
        rows = outs[index].shape[0]
        src = held[index].at[pl.ds(which * rows, rows)]
        return pltpu.make_async_copy(src, outs[index], out_sems.at[2 * index + 1])

    def by_parity(act):
        for parity in range(2):

            @pl.when(info[0] % 2 == parity)
            def _(parity=parity):
                act(parity)

    for place in range(len(spots)):
        arriving(place).start()
    for index in range(len(groups)):
        for quarter in range(4):
            arriving(4 * index + quarter).wait()
        by_parity(lambda parity: leaving(index, parity).start())
        if whole[index]:
            leaving(index, 2).start()
    for index in range(len(groups)):
        by_parity(lambda parity: leaving(index, parity).wait())
        if whole[index]:
            leaving(index, 2).wait()


def mod_kernel(condition, mod, mod_bias, q, v, cq, cv, up, out):
    narrow, units, columns = q.shape[1], up.shape[1], mod.shape[1]
    out[...] = jnp.zeros(out.shape, F32)
    for layer in range(LAYERS):
        row = pl.ds(layer, 1)
        out[layer, 0:SLOTS, 0:columns] = dot_nt(condition[...], mod[layer]) + mod_bias[
            row, :
        ].astype(F32)
        out[layer, 4:5, 0:units] = up[row, :].astype(F32)
        out[layer, 5:6, 0:narrow] = q[row, :].astype(F32)
        out[layer, 6:7, 0:narrow] = v[row, :].astype(F32)
        out[layer, 7:8, 0:narrow] = cq[row, :].astype(F32)
        out[layer, 4:5, 1024 : 1024 + narrow] = cv[row, :].astype(F32)


def assemble_kernel(info, *refs, narrow, units, columns):
    parts, (mods, narrows, ups) = refs[:4], refs[4:]
    narrows[...] = jnp.zeros(narrows.shape, F32)
    for rank in range(4):

        @pl.when(info[5] == rank)
        def _(rank=rank):
            for shard in range(4):
                part = parts[shard ^ rank]
                for layer in range(LAYERS):
                    mods[layer, :, shard * columns : (shard + 1) * columns] = part[
                        layer, 0:SLOTS, 0:columns
                    ]
                    ups[layer, :, shard * units : (shard + 1) * units] = part[layer, 4:5, 0:units]
                    at = slice(shard * narrow, (shard + 1) * narrow)
                    for row, source in ((0, 5), (2, 6), (3, 7)):
                        narrows[layer, row : row + 1, at] = part[
                            layer, source : source + 1, 0:narrow
                        ]
                    narrows[layer, 5:6, at] = part[layer, 4:5, 1024 : 1024 + narrow]


def collect_kernel(info, *refs, narrow, units, columns):
    stats, condition, out = refs[: 2 * LAYERS], refs[2 * LAYERS], refs[2 * LAYERS + 1]
    sums = refs[2 * LAYERS + 2]
    width = stats[0].shape[1]
    work = out
    out = refs[2 * LAYERS + 3]
    out[...] = jnp.zeros(out.shape, F32)
    for layer in range(LAYERS):
        sums[...] = stats[2 * layer][...] + stats[2 * layer + 1][...]
        base = 8 * layer
        out[base + 4 : base + 5, width : 2 * width] = sums[60:61, :]
        out[base + 5 : base + 6, 0:width] = sums[12:13, :]
        out[base + 5 : base + 6, width : 2 * width] = sums[36:37, :]
        for index in range(2):
            out[base + 6 + index : base + 7 + index, 512 : 512 + width] = condition[
                2 * layer + index : 2 * layer + index + 1, :
            ].astype(F32)
        for rank in range(4):

            @pl.when(info[5] == rank)
            def _(rank=rank, base=base):
                first = rank * columns
                for index in range(9):
                    low = max(first, index * width)
                    high = min(first + columns, (index + 1) * width)
                    if low < high:
                        row = (index // 3) * 24 + (index % 3) * 4
                        out[base : base + 4, low - first : high - first] = sums[
                            row : row + 4, low - index * width : high - index * width
                        ]
                out[base + 4 : base + 5, 0:units] = sums[61 + rank : 62 + rank, :]
                own = slice(rank * narrow, (rank + 1) * narrow)
                out[base + 6 : base + 7, 0:narrow] = sums[13:14, own]
                out[base + 6 : base + 7, 256 : 256 + narrow] = sums[14:15, own]
                out[base + 7 : base + 8, 0:narrow] = sums[37:38, own]
                out[base + 7 : base + 8, 256 : 256 + narrow] = sums[38:39, own]
    work[...] = out[...].astype(BF)


def spread_kernel(info, gathered, grad, bias_grad, q, v, cq, cv, up, o1, o2, o3, rows, conditions):
    count = gathered.shape[0]
    columns, part = grad.shape[2], grad.shape[1]
    width, narrow, units = conditions.shape[1], q.shape[1], up.shape[1]
    shift = lax.rem(width - info[8] * part, width)
    for index in range(count):
        for slot in range(SLOTS):
            row = 8 * (slot // 2) + 6 + slot % 2
            conditions[SLOTS * index + slot : SLOTS * index + slot + 1, :] = gathered[
                index ^ info[8], row : row + 1, 512 : 512 + width
            ].astype(F32)
    turned = pltpu.roll(conditions[...], shift, 1)[:, :part].T
    for layer in range(LAYERS):
        base = 8 * layer
        sums = jnp.zeros((8, gathered.shape[2]), F32)
        for index in range(count):
            values = gathered[index ^ info[8]].astype(F32)[base : base + 8]
            sums += values
            rows[SLOTS * index : SLOTS * (index + 1), :] = values[0:SLOTS, 0:columns]
        grad[layer] = jnp.dot(
            turned, rows[...], precision=lax.Precision.HIGHEST, preferred_element_type=F32
        )
        at = slice(layer, layer + 1)
        bias_grad[at, :] = jnp.sum(sums[0:SLOTS, 0:columns], axis=0, keepdims=True)
        up[at, :] = sums[4:5, 0:units]
        q[at, :] = sums[6:7, 0:narrow]
        v[at, :] = sums[6:7, 256 : 256 + narrow]
        cq[at, :] = sums[7:8, 0:narrow]
        cv[at, :] = sums[7:8, 256 : 256 + narrow]
        for out, row, lane in ((o1, 5, 0), (o2, 5, width), (o3, 4, width)):
            own = jnp.broadcast_to(sums[row : row + 1, lane : lane + width], (8, width))
            out[at, :] = pltpu.roll(own, shift, 1)[0:1, :part]


def finish_kernel(*refs, wide, spots):
    parts, outs = refs[: 2 * len(spots)], refs[2 * len(spots) :]
    step = 3 * LANES
    for chain, (at, places) in enumerate(spots):
        values = parts[2 * chain][0].astype(F32) + parts[2 * chain + 1][0].astype(F32)
        for layer, pair in places:
            if wide:
                width = outs[0].shape[2]
                for out in outs:
                    out[layer] = values[:, at : at + width]
                    at += width
                continue
            both = values[:, at : at + step]
            at += step
            first = jnp.concatenate(
                [both[:, :LANES], both[:, 2 * LANES : 2 * LANES + HEAD_WIDTH]], axis=1
            )
            second = jnp.concatenate(
                [both[:, LANES : 2 * LANES], both[:, 2 * LANES + HEAD_WIDTH :]], axis=1
            )
            for out, matrix in zip(outs[2 * pair : 2 * pair + 2], (first, second)):
                out[layer] = matrix if out.shape[1:] == matrix.shape else matrix.T


def join_kernel(info, rows, other, out):
    share = rows.shape[0]
    for core in range(2):

        @pl.when(info[5] % 2 == core)
        def _(core=core):
            out[pl.ds(core * share, share), :] = rows[...]
            out[pl.ds((1 - core) * share, share), :] = other[...]


def tensor_hop(values, step):
    return lax.ppermute(values, "tensor", [(i, i ^ step) for i in range(4)])


def dp_hop(values, step):
    size = lax.axis_size("dp")
    return lax.ppermute(values, "dp", [(i, i ^ step) for i in range(size)])


def time_features(moments, width):
    half = width // 2
    rates = jnp.exp(-math.log(10000.0) * jnp.arange(half, dtype=F32) / half)
    angles = moments.astype(F32)[:, None] * rates[None, :]
    return jnp.concatenate([jnp.cos(angles), jnp.sin(angles)], axis=1)


def shards(
    tokens,
    text,
    timesteps,
    item_frames,
    cotangent,
    self_query,
    self_query_bias,
    self_key,
    self_value,
    self_value_bias,
    self_output,
    self_output_bias,
    cross_query,
    cross_query_bias,
    cross_key,
    cross_value,
    cross_value_bias,
    cross_output,
    cross_output_bias,
    hidden_up,
    hidden_up_bias,
    hidden_down,
    hidden_down_bias,
    modulation,
    modulation_bias,
):
    frames, width = tokens.shape
    words = text.shape[1]
    columns = modulation.shape[2]
    narrow = self_query.shape[2]
    units = hidden_up.shape[2]
    rank = lax.axis_index("tensor")
    me = lax.axis_index("dp")
    size = lax.axis_size("dp")
    core = rank % 2
    share = frames // 2
    blocks = share // UNIT
    unit = width // size
    turn = lambda values: jnp.swapaxes(values, 1, 2)

    order = jnp.arange(SLOTS, dtype=jnp.int32)
    ends = jnp.sum(jnp.where(order[:, None] <= order[None, :], item_frames[:, None], 0), axis=0)
    turned = (jnp.arange(frames // UNIT, dtype=jnp.int32) + core * blocks) % (2 * blocks)
    slots = jnp.sum((turned[:, None] * UNIT >= ends[None, :]).astype(jnp.int32), axis=1)
    places = jnp.stack([rank, rank // 2, rank ^ 1, me]).astype(jnp.int32)
    info = jnp.concatenate([(rank * 2 + me % 2)[None].astype(jnp.int32), slots, places])

    def pack(members, whole, after=()):
        rows = [sum(a.shape[1] for a in some) for _, some in members]
        outs = [shape(r, width, dtype=BF) for r, one in zip(rows, whole) if one]
        outs += [shape(r // 2, width, dtype=BF) for r in rows]
        arrays = [a for _, some in members for a in some]
        results = pl.pallas_call(
            partial(
                pack_kernel,
                groups=[(layer, [None] * len(some)) for layer, some in members],
                whole=whole,
                after=len(after),
            ),
            out_shape=outs,
            in_specs=[SMALL] + [ANY] * (len(arrays) + len(after)),
            out_specs=[ANY] * len(outs),
            scratch_shapes=[
                *[pltpu.VMEM((r, width), BF) for r in rows],
                pltpu.SemaphoreType.DMA((4 * len(members),)),
                pltpu.SemaphoreType.DMA((2 * len(members),)),
            ],
            compiler_params=pltpu.CompilerParams(vmem_limit_bytes=VMEM_BYTES),
            cost_estimate=lasting(1.0),
            name="pack_weights",
        )(info, *arrays, *after)
        return list(results[: sum(whole)]), list(results[sum(whole) :])

    selfs = [turn(self_query), turn(self_key), turn(self_value), self_output]
    crosses = [turn(cross_query), turn(cross_key), turn(cross_value), cross_output]
    own0, first0 = pack([(0, selfs)], [True])


    condition = jax.nn.silu(time_features(timesteps, width)).astype(BF)
    mine = plain(
        mod_kernel,
        "mod_rows",
        None,
        [
            condition,
            turn(modulation),
            modulation_bias,
            self_query_bias,
            self_value_bias,
            cross_query_bias,
            cross_value_bias,
            hidden_up_bias,
        ],
        [shape(LAYERS, 8, -(-columns // LANES) * LANES)],
    )
    own1, first1 = pack(
        [(0, crosses), (1, selfs), (1, crosses), (1, [hidden_up]), (1, [hidden_down])],
        [True, True, True, False, False],
        [mine],
    )
    firsts, owns = first0 + first1, own0 + own1
    others = [tensor_hop(mine, 1), tensor_hop(mine, 2)]
    others.append(tensor_hop(others[0], 2))
    out_biases = [
        b.reshape(LAYERS, 1, width) for b in (self_output_bias, cross_output_bias, hidden_down_bias)
    ]

    count = len(firsts)
    along_x, along_y, over_x, over_y, sibs = [[None] * count for _ in range(5)]

    def leave(index):
        along_x[index] = tensor_hop(firsts[index], 2)

    def swap(index):
        sibs[index] = tensor_hop(owns[index], 1)

    def go_on(index):
        along_y[index] = dp_hop(along_x[index], 1)
        over_x[index] = tensor_hop(along_x[index], 1)

    def end(index):
        over_y[index] = tensor_hop(along_y[index], 1)

    def weights_of(index):
        return [
            owns[index],
            sibs[index],
            along_x[index],
            along_y[index],
            over_x[index],
            over_y[index],
        ]

    def open_gate(after, leaving=(), at_x=(), at_y=(), settled=()):
        places = [(firsts, i) for i in leaving]
        places += [(along_x, i) for i in at_x] + [(along_y, i) for i in at_y] + list(settled)
        opened = gate([values[i] for values, i in places], after)
        for (values, i), array in zip(places, opened):
            values[i] = array
        for i in leaving:
            leave(i)
        for i in at_x:
            go_on(i)
        for i in at_y:
            end(i)
        return list(opened)

    leave(0)
    swap(0)
    open_gate([mine], [], [0])
    open_gate([*others, along_x[0]], [1])
    swap(1)
    go_on(1)
    owns += [hidden_up, hidden_down]
    sibs[4:6] = tensor_hop(hidden_up, 1), tensor_hop(hidden_down, 1)
    mods, narrow_biases, up_biases = plain(
        partial(assemble_kernel, narrow=narrow, units=units, columns=columns),
        "mod_all",
        info,
        [mine, *others],
        [
            shape(LAYERS, SLOTS, 4 * columns),
            shape(LAYERS, 8, 4 * narrow),
            shape(LAYERS, 1, 4 * units),
        ],
        after=[along_x[1]],
    )
    open_gate([mods], [], [], [0])

    text_rows = jnp.pad(text, ((0, 0), (0, LANES - words), (0, 0))).reshape(-1, width)
    whole = pltpu.VMEM((width, width), BF)
    four = pltpu.VMEM((4, width, units), BF)
    two = pltpu.VMEM((2, width, units), BF)
    floats = pltpu.VMEM((share, width), F32)
    lows = pltpu.VMEM((share, width), BF)
    sems = lambda n: pltpu.SemaphoreType.DMA((n,))
    frame_low = shape(share, width, dtype=BF)
    frame_high = shape(share, width)
    frame_wide = shape(share, 4 * units, dtype=BF)
    frame_chip = shape(share, 2 * units, dtype=BF)
    two_low = shape(2, share, width, dtype=BF)
    two_text = shape(2, SLOTS * LANES, width, dtype=BF)
    logs = shape(16, share)
    log_work = pltpu.VMEM((share, LANES), F32)
    stat_shape = shape(72, width)

    kept = []
    for layer in range(LAYERS):
        first = 2 * layer
        mod = (mods, (layer,))
        biases = (narrow_biases, (layer,))
        common = dict(w=pltpu.VMEM((2, width, width), BF), sems=sems(8))
        if layer == 0:
            entry1, kv, x = run(
                kv_kernel,
                "self_kv",
                info,
                {},
                dict(mod=mod, biases=biases),
                weights_of(first) + [tokens],
                dict(entry=frame_low, kv=two_low, x=frame_high),
                {},
                common | dict(rows=lows, row_sems=sems(1)),
                [along_x[1], sibs[1], sibs[4], sibs[5]],
                3.0,
            )
        else:
            entry1, kv, x, branch3 = run(
                kv_kernel,
                "residual_kv",
                info,
                dict(part=part, other=tensor_hop(part, 2), below=kept[-1]["x2"]),
                dict(
                    mod=mod,
                    mod_below=(mods, (layer - 1,)),
                    bias=(out_biases[2], (layer - 1,)),
                    biases=biases,
                ),
                weights_of(first),
                dict(entry=frame_low, kv=two_low, x=frame_high, branch=frame_low),
                {},
                common | dict(sum=floats),
                opened,
                3.0,
            )
            kept[-1]["branch3"] = branch3
        kv_sib = tensor_hop(kv, 1)
        opened = (
            open_gate([entry1], [2, 3, 4])
            if layer == 0
            else open_gate([entry1], [5], [], [], [(over_x, 3), (sibs, 3)])
        )
        if layer == 0:
            end(1)
        (q,) = run(
            q_kernel,
            "query",
            info,
            dict(entry=entry1),
            dict(biases=biases),
            weights_of(first),
            dict(q=frame_low),
            {},
            dict(w=whole, sems=sems(4)),
            [],
            15.0,
        )
        if layer == 0:
            x1, mixed1, rest1, lse1, branch1, x2, entry2, cq, ckv, mixed2, lse2, branch2 = run(
                lambda info, work, w: attention_kernel(info, work, w, words),
                "self_cross",
                info,
                dict(q=q, kv_own=kv, kv_sib=kv_sib, x=x, text=text_rows),
                dict(
                    mod=mod,
                    biases=biases,
                    self_bias=(out_biases[0], (layer,)),
                    cross_bias=(out_biases[1], (layer,)),
                ),
                weights_of(first) + weights_of(first + 1),
                dict(
                    x1=frame_high,
                    mixed1=frame_low,
                    rest=frame_low,
                    lse1=logs,
                    branch1=frame_low,
                    out=frame_high,
                    entry=frame_low,
                    cq=frame_low,
                    ckv=two_text,
                    mixed2=frame_low,
                    lse2=logs,
                    branch2=frame_low,
                ),
                {},
                dict(
                    wq=whole,
                    wk=whole,
                    wv=whole,
                    wo=whole,
                    cross_wo=whole,
                    logs=log_work,
                    sum=floats,
                    sems=sems(4),
                    csems=sems(16),
                ),
                opened,
                14.0,
            )
            opened = open_gate([x2], [], [2, 3])
            swap(2)
            swap(3)
        else:
            x1, mixed1, rest1, lse1, branch1 = run(
                self_kernel,
                "self",
                info,
                dict(q=q, kv_own=kv, kv_sib=kv_sib, x=x),
                dict(mod=mod, bias=(out_biases[0], (layer,))),
                weights_of(first),
                dict(out=frame_high, mixed=frame_low, rest=frame_low, lse=logs, branch=frame_low),
                {},
                dict(wo=whole, logs=log_work, sum=floats, sems=sems(4)),
                opened,
                8.0,
            )
            opened = open_gate([x1], [], [5], [3, 4], [(over_x, 4)])
            x2, entry2, cq, ckv, mixed2, lse2, branch2 = run(
                partial(cross_kernel, words=words),
                "cross",
                info,
                dict(x=x1, text=text_rows),
                dict(mod=mod, biases=biases, bias=(out_biases[1], (layer,))),
                weights_of(first + 1),
                dict(
                    out=frame_high,
                    entry=frame_low,
                    q=frame_low,
                    kv=two_text,
                    mixed=frame_low,
                    lse=logs,
                    branch=frame_low,
                ),
                {},
                dict(
                    wq=whole, wk=whole, wv=whole, wo=whole, logs=log_work, sum=floats, sems=sems(16)
                ),
                opened,
                6.0,
            )
            opened = open_gate([x2], [], [], [5], [(over_x, 5), (over_y, 4)])
        if layer == 0:
            part, entry3, active, slope = run(
                lambda info, work, w: hidden_kernel(info, work, w, 0),
                "ff_part",
                info,
                dict(x=x2),
                dict(mod=mod, up_bias=(up_biases, (layer,))),
                [hidden_up, sibs[4], hidden_down, sibs[5]],
                dict(part=frame_low, entry=frame_low, active=frame_chip, slope=frame_chip),
                {},
                dict(
                    up=two, down=two, before=floats, sum=floats, sems=sems(2), down_sems=sems(2)
                ),
                opened,
                5.0,
            )
            opened = open_gate([part], [], [4], [2], [(over_x, 2), (sibs, 2)])
            x3 = branch3 = None
        else:
            x3 = branch3 = active = slope = entry3 = None
        kept.append(
            dict(
                x=x,
                entry1=entry1,
                q=q,
                kv=kv,
                kv_sib=kv_sib,
                mixed1=mixed1,
                rest1=rest1,
                lse1=lse1,
                branch1=branch1,
                x1=x1,
                entry2=entry2,
                cq=cq,
                ckv=ckv,
                mixed2=mixed2,
                lse2=lse2,
                branch2=branch2,
                x2=x2,
                entry3=entry3,
                active=active,
                slope=slope,
                branch3=branch3,
            )
        )
        x = x3
    last_gate = opened

    def join(rows, *after):
        return plain(
            join_kernel,
            "join_rows",
            info,
            [rows, tensor_hop(rows, 1)],
            [shape(2 * share, width, dtype=BF)],
            after=after,
        )


    chains = {}

    def start(name, send, keep):
        view = (size, unit, send.shape[1])
        chains[name] = (tensor_hop(send, 1).reshape(view), keep.reshape(view), 0)

    def held(*names):
        return [chains[name][1] for name in names]

    def advance(names, after=(), cost=1.5):
        targets = [(n, [n]) if isinstance(n, str) else n for n in names]
        targets = [t for t in targets if 2 ** chains[t[1][0]][2] < size]
        if not targets:
            return
        ins, in_specs, outs, out_specs, spots = [], [], [], [], []
        for result, (_, parts) in enumerate(targets):
            column = 0
            for name in parts:
                received, kept_part, bit = chains[name]
                blocks_left, rows, wide = received.shape
                spots.append((result, column))
                column += wide
                for side in range(2):

                    def at(i, info, bit=bit, side=side):
                        return (0, ((info[8] >> bit) & 1) ^ side, 0, 0)

                    for part in (received, kept_part):
                        ins.append(part.reshape(blocks_left // 2, 2, rows, wide))
                        in_specs.append(pl.BlockSpec((blocks_left // 2, None, rows, wide), at))
            for side in range(2):
                outs.append(shape(blocks_left // 2, rows, column, dtype=BF))
                out_specs.append(
                    pl.BlockSpec((blocks_left // 2, rows, column), lambda i, info: (0, 0, 0))
                )
        results = pl.pallas_call(
            partial(merge_kernel, spots=spots, after=len(after)),
            grid_spec=pltpu.PrefetchScalarGridSpec(
                num_scalar_prefetch=1,
                grid=(1,),
                in_specs=in_specs + [ANY] * len(after),
                out_specs=out_specs,
            ),
            out_shape=outs,
            compiler_params=pltpu.CompilerParams(vmem_limit_bytes=VMEM_BYTES),
            cost_estimate=lasting(cost),
            name="merge_grads",
        )(info, *ins, *after)
        for index, (name, parts) in enumerate(targets):
            bit = chains[parts[0]][2]
            hold, give = results[2 * index : 2 * index + 2]
            for part in parts:
                del chains[part]
            chains[name] = (dp_hop(give, 2**bit), hold, bit + 1)

    sums = []
    last = LAYERS - 1
    for layer in reversed(range(LAYERS)):
        first = 2 * layer
        k = kept[layer]
        mod = (mods, (layer,))
        above = layer + 1
        f_name, c_name, a_name, s_name = [f"{kind}{layer}" for kind in "fcas"]
        n_name = f"n{above}"

        def grads_out(members):
            return dict.fromkeys(SIDES, shape(width, members * narrow, dtype=BF))

        older = []
        if layer < last:
            older = [f"f{above}", n_name]
            more = held(*older)
        if layer == last:
            f_send, f_keep, low, c_send, c_keep, g, stats = run(
                lambda info, work, w: hidden_cross_kernel(info, work, w, words),
                "ff_cross_back",
                info,
                dict(
                    x2=k["x2"],
                    branch2=k["branch2"],
                    q=k["cq"],
                    kv=k["ckv"],
                    lse=k["lse2"],
                    entry2=k["entry2"],
                    text=text_rows,
                    mixed=k["mixed2"],
                    x1=k["x1"],
                ),
                dict(mod=mod, up_bias=(up_biases, (layer,)), bias=(out_biases[2], (layer,))),
                weights_of(4) + weights_of(5) + [cotangent] + weights_of(first + 1),
                {f"f_{name}": shape(width, 2 * units, dtype=BF) for name in SIDES}
                | dict(low=frame_low)
                | {f"c_{name}": shape(width, 4 * narrow, dtype=BF) for name in SIDES}
                | dict(out=frame_high),
                dict(stats=stat_shape),
                dict(
                    up=four,
                    down=four,
                    g=floats,
                    g_mid=floats,
                    rows=lows,
                    row_sems=sems(1),
                    gb=lows,
                    entry3=lows,
                    branch3=lows,
                    active=pltpu.VMEM((share, 4 * units), BF),
                    slope=pltpu.VMEM((share, 4 * units), BF),
                    d_before=pltpu.VMEM((share, 4 * units), BF),
                    before=floats,
                    sum=floats,
                    sems=sems(8),
                    down_sems=sems(8),
                    wq=whole,
                    wo=whole,
                    dkv=pltpu.VMEM(two_text.shape, BF),
                    dkv_sum=pltpu.VMEM(two_text.shape, F32),
                    csems=sems(8),
                ),
                last_gate,
                10.0,
            )
            start(f_name, f_send, f_keep)
            start(c_name, c_send, c_keep)
        else:
            part, gb, d_before, stats = run(
                lambda info, work, w: hidden_back_kernel(info, work, w, 0),
                "ff_back",
                info,
                dict(g=g, branch=k["branch3"], slope=k["slope"]),
                dict(mod=mod),
                [hidden_up, sibs[4], hidden_down, sibs[5]],
                dict(part=frame_low, gb=frame_low, d_before=frame_chip),
                dict(stats=stat_shape),
                dict(
                    up=two, down=two, before=floats, de=floats, sems=sems(2), down_sems=sems(2)
                ),
                more,
                5.0,
            )
            other = tensor_hop(part, 2)
            send, keep = run(
                hidden_grads_kernel,
                "ff_grads",
                info,
                dict(entry=k["entry3"], d_before=d_before, gb=gb, active=k["active"]),
                {},
                [],
                dict.fromkeys(SIDES, shape(width, 2 * units, dtype=BF)),
                {},
                {},
                [gb],
                1.0,
            )
            start(f_name, send, keep)
            output = join(low, gb)
            advance(older, held(f_name), 0.5)
            extra = dict(part=part, other=other, above=k["x2"])
            scratch = dict(g_mid=floats)
        if layer < last:
            send, keep, g, stats = run(
                partial(cross_back_kernel, words=words),
                "cross_back",
                info,
                dict(
                    g=g,
                    branch=k["branch2"],
                    q=k["cq"],
                    kv=k["ckv"],
                    lse=k["lse2"],
                    entry=k["entry2"],
                    text=text_rows,
                    mixed=k["mixed2"],
                    x=k["x1"],
                    **extra,
                ),
                dict(mod=mod, early=(stats, ())),
                weights_of(first + 1),
                grads_out(4) | dict(out=frame_high),
                dict(stats=stat_shape),
                dict(
                    wq=whole,
                    wo=whole,
                    gb=lows,
                    dq=lows,
                    dkv=pltpu.VMEM(two_text.shape, BF),
                    d_mixed=lows,
                    de=floats,
                    dkv_sum=pltpu.VMEM(two_text.shape, F32),
                    sems=sems(8),
                    **scratch,
                ),
                held(f_name, *older) + [output],
                60.0,
            )
            start(c_name, send, keep)
            advance([f_name, n_name], [g, chains[f"f{above}"][0]])
        gb1, dq, dkv_own, dkv_give, stats = run(
            self_back_kernel,
            "self_back",
            info,
            dict(
                g=g,
                branch=k["branch1"],
                mixed=k["mixed1"],
                rest=k["rest1"],
                q=k["q"],
                kv_own=k["kv"],
                kv_sib=k["kv_sib"],
                lse=k["lse1"],
            ),
            dict(mod=mod, early=(stats, ())),
            weights_of(first),
            dict(gb=frame_low, dq=frame_low, dkv_own=two_low, dkv_give=two_low),
            dict(stats=stat_shape),
            dict(wo=whole, d_mixed=lows, inner=pltpu.VMEM((16, share), F32), sems=sems(4)),
            held(f_name, c_name, *([n_name] if layer < last else [])),
            13.0,
        )
        dkv_sib = tensor_hop(dkv_give, 1)
        if layer == last:
            advance([f_name], [dq])
        else:
            advance([f_name, c_name], [dq, chains[n_name][0]])
        send, keep = run(
            query_output_kernel,
            "qo_grads",
            info,
            dict(entry=k["entry1"], gb=gb1, dq=dq, mixed=k["mixed1"]),
            {},
            [],
            grads_out(2),
            {},
            {},
            held(f_name, c_name),
            60.0,
        )
        start(a_name, send, keep)
        arriving = dict(dkv_own=dkv_own, dkv_sib=dkv_sib, entry=k["entry1"])
        if layer == 0:
            send, keep, dkv = run(
                kv_grads_kernel,
                "kv_grads",
                info,
                arriving,
                {},
                [],
                grads_out(2) | dict(dkv=two_low),
                {},
                {},
                held(a_name),
                4.0,
            )
            start(s_name, send, keep)
            rest = f"t{layer}"
            advance([f_name, c_name, (rest, [a_name, s_name])], held(s_name))
            arriving = dict(dkv=dkv)
        results = run(
            qkv_back_kernel,
            "qkv_back",
            info,
            arriving | dict(dq=dq, x=k["x"], g=g),
            dict(mod=mod, early=(stats, ())),
            weights_of(first),
            (dict(low=frame_low) if layer == 0 else grads_out(2)) | dict(out=frame_high),
            dict(stats=stat_shape),
            dict(wq=whole, wk=whole, wv=whole, de=floats, sems=sems(12))
            | (dict(dkv=pltpu.VMEM(two_low.shape, BF)) if layer else {}),
            held(f_name, c_name, rest if layer == 0 else a_name),
            6.0,
        )
        g, stats = results[-2:]
        if layer:
            start(s_name, *results[:2])
        if layer:
            advance([f_name, (f"n{layer}", [c_name, a_name, s_name])], [g])
        else:
            to_rest = [g, chains[f_name][0]]
        sums = [stats, tensor_hop(stats, 1)] + sums
    vectors = plain(
        partial(collect_kernel, narrow=narrow, units=units, columns=columns),
        "collect",
        info,
        [*sums, condition],
        [shape(16, mine.shape[2], dtype=BF)],
        [pltpu.VMEM(stat_shape.shape, F32), pltpu.VMEM((16, mine.shape[2]), F32)],
    )
    advance(["c0", "t0"], to_rest + [vectors])
    gathered, hop = vectors[None], size // 2

    def gather_sums():
        nonlocal gathered, hop
        if hop:
            both = jnp.stack([gathered, dp_hop(gathered, hop)], axis=1)
            gathered = both.reshape(-1, *vectors.shape)
            hop //= 2

    low = results[0]
    (low,) = gate([low], held("t0"))
    input_grad = join(low)

    def parts_of(*names):
        return [part.reshape(1, unit, -1) for name in names for part in chains[name][:2]]

    up_grad, down_grad = plain(
        partial(finish_kernel, wide=True, spots=[(0, [(0, 0)]), (0, [(1, 0)])]),
        "wide",
        None,
        parts_of("f0", "f1"),
        [shape(LAYERS, unit, units)] * 2,
    )
    ready = [input_grad, up_grad, chains["c0"][0]]
    while any(2 ** chain[2] < size for chain in chains.values()):
        gather_sums()
        advance(list(chains), held("t0") + [gathered] + ready)
    while hop:
        gather_sums()
    straight, across = shape(LAYERS, unit, narrow), shape(LAYERS, narrow, unit)
    spots = [(0, [(1, 0), (1, 1), (1, 2), (1, 3)])]
    spots += [(0, [(0, 0), (0, 1)]), (0, [(0, 2), (0, 3)])]
    cq_grad, ck_grad, cv_grad, co_grad, q_grad, o_grad, k_grad, v_grad = plain(
        partial(finish_kernel, wide=False, spots=spots),
        "narrow",
        None,
        parts_of("n1", "c0", "t0"),
        [straight, straight, straight, across, straight, across, straight, straight],
    )
    small = plain(
        spread_kernel,
        "spread",
        info,
        [gathered],
        [shape(LAYERS, unit, columns), shape(LAYERS, columns)]
        + [shape(LAYERS, narrow)] * 4
        + [shape(LAYERS, units)]
        + [shape(LAYERS, unit)] * 3,
        [pltpu.VMEM((SLOTS * size, columns), F32), pltpu.VMEM((SLOTS * size, width), F32)],
    )
    mod_grad, mod_bias_grad, q_sum, v_sum, cq_sum, cv_sum, up_sum, o1, o2, o3 = small
    return (
        output,
        input_grad,
        q_grad,
        q_sum,
        k_grad,
        v_grad,
        v_sum,
        o_grad,
        o1,
        cq_grad,
        cq_sum,
        ck_grad,
        cv_grad,
        cv_sum,
        co_grad,
        o2,
        up_grad,
        up_sum,
        turn(down_grad),
        o3,
        mod_grad,
        mod_bias_grad,
    )


def solution(mesh):
    dp, tensor = "dp", "tensor"
    columns, vector = P(None, None, tensor), P(None, tensor)
    matrix, turned, spread = P(None, dp, tensor), P(None, tensor, dp), P(None, dp)
    placed = (
        P(dp, None),
        P(dp, None, None),
        P(dp),
        P(dp),
        P(dp, None),
        columns,
        vector,
        columns,
        columns,
        vector,
        P(None, tensor, None),
        P(),
        columns,
        vector,
        columns,
        columns,
        vector,
        P(None, tensor, None),
        P(),
        columns,
        vector,
        P(None, tensor, None),
        P(),
        columns,
        vector,
    )
    results = (
        P(dp, None),
        P(dp, None),
        matrix,
        vector,
        matrix,
        matrix,
        vector,
        turned,
        spread,
        matrix,
        vector,
        matrix,
        matrix,
        vector,
        turned,
        spread,
        matrix,
        vector,
        turned,
        spread,
        matrix,
        vector,
    )
    return jax.shard_map(
        shards, mesh=mesh, in_specs=placed, out_specs=results, check_vma=False
    )
```
